32 devices in a mesh: ctx: 16 (over z, y, core), fsdp: 2 (over x).
Axes of the slice: x: 2, y: 2, z: 4, core: 2. Of those that a mesh axis runs over, the one named last changes fastest.
Arguments:
- tokens: bfloat16 [2, 4096, 1024], P('fsdp', 'ctx'), may hold values from -6 to 6
- qkv_weight: bfloat16 [1024, 2048], P('fsdp'), may hold values from -0.1875 to 0.1875
- out_weight: bfloat16 [1024, 1024], P('fsdp'), may hold values from -1.5 to 1.5
- gate_up_weight: bfloat16 [1024, 2, 4608], P('fsdp'), may hold values from -0.1875 to 0.1875
- down_weight: bfloat16 [4608, 1024], P('fsdp'), may hold values from -0.1875 to 0.1875
- attn_gain: bfloat16 [1024], P('fsdp'), may hold values from 0.25 to 1.75
- ffn_gain: bfloat16 [1024], P('fsdp'), may hold values from 0.25 to 1.75
- query_gain: bfloat16 [64], P('fsdp'), may hold values from 0.796875 to 2
- key_gain: bfloat16 [64], P('fsdp'), may hold values from 0.796875 to 2
- seq_lengths: int32 [2, 3], P('fsdp'), may hold values from 1024 to 2048, as said below
- block_order: int32 [2, 32], P('fsdp'), may hold values from 0 to 31, as said below
- cotangent: bfloat16 [2, 4096, 1024], P('fsdp', 'ctx'), may hold values from -6 to 6
Outputs:
- output: bfloat16 [2, 4096, 1024], P('fsdp', 'ctx')
- input_grad: float32 [2, 4096, 1024], P('fsdp', 'ctx')
- grad_qkv: float32 [1024, 2048], P('fsdp')
- grad_out: float32 [1024, 1024], P('fsdp')
- grad_gate_up: float32 [1024, 2, 4608], P('fsdp')
- grad_down: float32 [4608, 1024], P('fsdp')
- grad_attn_gain: float32 [1024], P('fsdp')
- grad_ffn_gain: float32 [1024], P('fsdp')
- grad_query_gain: float32 [64], P('fsdp')
- grad_key_gain: float32 [64], P('fsdp')
The draws below stay inside these ranges and needn't reach their ends.
Inputs may be any that keep to these rules, and one draw needn't show every extreme that they name: `seq_lengths`: the 3 lengths of a group add up to 4096; one of them is exactly 2048 and one is exactly 1024. `block_order`: each row is a permutation of the numbers 0 to 31.
All inputs are finite; a program needn't handle non-finite values.
Results may differ from the reference program's by a relative error of at most 0.03.
Values may be sent and summed in bfloat16 or wider, within the bound.
No kernel may reach another device: no remote copies, remote signals or barrier semaphores. Data moves between devices by JAX's collectives and lax.ppermute only.
A program may use at most 256 MiB of HBM per device.

```python
import jax
import jax.numpy as jnp
from jax import lax

D = 1024
HEADS = 16
KV_HEADS = 8
HD = 64
FF = 4608
BLK = 128
MINLEN = 1024
NBLK = 32
GROUP_TOK = 4096
GROUPS = 2
NSEQ = 3


def group_draw(key):
    extra = GROUP_TOK // 2 - (NSEQ - 1) * MINLEN
    drawn = jax.random.randint(jax.random.fold_in(key, 1), (NSEQ - 3,), 0, extra + 1).astype(jnp.int32)
    cuts = jnp.sort(jnp.concatenate([jnp.zeros((1,), jnp.int32), drawn])).astype(jnp.int32)
    edges = jnp.concatenate([jnp.zeros((1,), jnp.int32), cuts, jnp.full((1,), extra, jnp.int32)])
    shorter = (MINLEN + edges[1:] - edges[:-1]).astype(jnp.int32)
    shuffle = jax.random.permutation(jax.random.fold_in(key, 4), NSEQ - 1).astype(jnp.int32)
    shorter = shorter[shuffle]
    longest = jax.random.randint(jax.random.fold_in(key, 2), (), 0, NSEQ).astype(jnp.int32)
    places = jnp.arange(NSEQ, dtype=jnp.int32)
    picked = jnp.clip(jnp.where(places > longest, places - 1, places), 0, NSEQ - 2)
    lengths = jnp.where(places == longest, GROUP_TOK // 2, shorter[picked]).astype(jnp.int32)
    return (lengths, longest)


def lengths_for(key):
    return group_draw(key)[0]


def order_for(key):
    lengths, longest = group_draw(key)
    places = jnp.arange(NSEQ, dtype=jnp.int32)
    begin = jnp.sum(jnp.where(places < longest, lengths, 0)).astype(jnp.int32)
    finish = begin + GROUP_TOK // 2
    first_full = (begin + BLK - 1) // BLK
    last_full = finish // BLK - 1
    ranking = jax.random.permutation(jax.random.fold_in(key, 3), NBLK).astype(jnp.int32)
    ranking = ranking.at[first_full].set(-1).at[last_full].set(NBLK)
    return jnp.argsort(ranking, stable=True).astype(jnp.int32)


def group_keys(key):
    base = jax.random.fold_in(key, 11)
    indices = jnp.arange(GROUPS, dtype=jnp.int32)
    return jax.vmap(partial_fold(base))(indices)


def partial_fold(base):

    def folded(index):
        return jax.random.fold_in(base, index)
    return folded


def draw_seq_lengths(key, part):
    return jax.vmap(lengths_for)(group_keys(key))


def draw_block_order(key, part):
    return jax.vmap(order_for)(group_keys(key))


def block_scale(rng, extent, shards, least, high):
    gain, own = 1.0, jax.random.fold_in(rng, 6)
    for dim, blocks in shards:
        heights = jnp.exp(jax.random.uniform(jax.random.fold_in(own, dim), (blocks,), jnp.float32, least / len(shards), high / len(shards)))
        gain = gain * jnp.repeat(heights, extent[dim] // blocks).reshape([-1 if axis == dim else 1 for axis in range(len(extent))])
    return gain


def gaussian(own_key, dims, scale, limit, split=(), kind=jnp.bfloat16):
    values = jax.random.normal(own_key, dims, jnp.float32) * scale
    if len(split) > 0:
        values = block_scale(own_key, dims, split, -0.22, 0.18) * values
    return jnp.clip(values, min=-limit, max=limit).astype(kind)


def setup_inputs(seed: int = 0) -> dict:
    key_list = jax.random.split(jax.random.key(seed), 13)
    tokens = gaussian(key_list[0], (GROUPS, GROUP_TOK, D), 1.0, 6.0, ((0, 2), (1, 16)))
    qkv_weight = gaussian(key_list[1], (D, (HEADS + 2 * KV_HEADS) * HD), D ** -0.5, 0.1875, ((0, 2),))
    out_weight = gaussian(key_list[2], (HEADS * HD, D), (D // 64) ** -0.5, 1.5, ((0, 2),))
    gate_up_weight = gaussian(key_list[3], (D, 2, FF), D ** -0.5, 0.1875, ((0, 2),))
    down_weight = gaussian(key_list[4], (FF, D), (FF // 4) ** -0.5, 0.1875, ((0, 2),))
    attn_gain = jnp.clip(1.0 + 0.15 * jax.random.normal(key_list[5], (D,), jnp.float32), 0.25, 1.75).astype(jnp.bfloat16)
    ffn_gain = jnp.clip(1.0 + 0.15 * jax.random.normal(key_list[6], (D,), jnp.float32), 0.25, 1.75).astype(jnp.bfloat16)
    query_gain = jnp.clip(0.796875 + 1.203125 * jax.random.uniform(key_list[7], (HD,), jnp.float32) ** block_scale(key_list[7], (HD,), ((0, 2),), -0.2, 0.2), 0.796875, 2.0).astype(jnp.bfloat16)
    key_gain = jnp.clip(0.796875 + 1.203125 * jax.random.uniform(key_list[8], (HD,), jnp.float32) ** block_scale(key_list[8], (HD,), ((0, 2),), -0.2, 0.2), 0.796875, 2.0).astype(jnp.bfloat16)
    seq_lengths = draw_seq_lengths(jax.random.fold_in(key_list[12], 71), 0)
    block_order = draw_block_order(jax.random.fold_in(key_list[12], 71), 0)
    cotangent = gaussian(key_list[11], (GROUPS, GROUP_TOK, D), 1.0, 6.0, ((0, 2), (1, 16)))
    return {"tokens": tokens, "qkv_weight": qkv_weight, "out_weight": out_weight, "gate_up_weight": gate_up_weight, "down_weight": down_weight, "attn_gain": attn_gain, "ffn_gain": ffn_gain, "query_gain": query_gain, "key_gain": key_gain, "seq_lengths": seq_lengths, "block_order": block_order, "cotangent": cotangent}


EPSILON = 1e-05
ROPE_BASE = 1000000.0
NEGATIVE = -1e+30
HIGHEST = lax.Precision.HIGHEST

@jax.custom_vjp
def low(v):
    return lax.optimization_barrier(v.astype(jnp.bfloat16)).astype(jnp.float32)

@jax.custom_vjp
def low_back(v):
    return v

def low_keep(v):
    return (low(v), None)

def low_pass(kept, grad):
    return (grad,)

def back_keep(v):
    return (v, None)

def back_low(kept, grad):
    return (low(grad),)
low.defvjp(low_keep, low_pass)
low_back.defvjp(back_keep, back_low)

def rms_scale(values):
    return lax.rsqrt(lax.optimization_barrier(jnp.mean(values * values, axis=-1, keepdims=True)) + EPSILON)

def rotate_half(values):
    half = values.shape[-1] // 2
    return jnp.concatenate([-values[..., half:], values[..., :half]], axis=-1)

def slot_info(order, lengths):
    slots = jnp.arange(GROUP_TOK, dtype=jnp.int32)
    packed = (order[slots // BLK] * BLK + slots % BLK).astype(jnp.int32)
    ends = jnp.cumsum(lengths).astype(jnp.int32)
    past = packed[:, None] >= ends[None, :]
    segment = lax.optimization_barrier(jnp.sum(past.astype(jnp.int32), axis=1)).astype(jnp.int32)
    local = (packed - lax.optimization_barrier(jnp.sum(jnp.where(past, lengths[None, :], 0), axis=1))).astype(jnp.int32)
    return (packed, segment, local)

def group_forward(weights, inputs, lengths, order):
    w_qkv, w_out, w_gate_up, w_down, gain_attn, gain_ffn, gain_query, gain_key = weights
    packed, segment, local = slot_info(order, lengths)
    per_group = HEADS // KV_HEADS
    frequency = ROPE_BASE ** (-2.0 * jnp.arange(HD // 2, dtype=jnp.float32) / HD)
    angle = local.astype(jnp.float32)[:, None] * frequency[None, :]
    cosine = jnp.concatenate([jnp.cos(angle), jnp.cos(angle)], axis=-1)[:, None, :]
    sine_table = jnp.concatenate([jnp.sin(angle), jnp.sin(angle)], axis=-1)[:, None, :]
    normed = low(inputs * rms_scale(inputs) * gain_attn)
    qkv = low_back(jnp.dot(normed, w_qkv, precision=HIGHEST))
    q_width = HEADS * HD
    kv_width = KV_HEADS * HD
    q_raw = qkv[:, :q_width].reshape(GROUP_TOK, HEADS, HD)
    k_raw = qkv[:, q_width:q_width + kv_width].reshape(GROUP_TOK, KV_HEADS, HD)
    values_all = low(qkv[:, q_width + kv_width:].reshape(GROUP_TOK, KV_HEADS, HD))
    q_normed = q_raw * rms_scale(q_raw) * gain_query
    k_normed = k_raw * rms_scale(k_raw) * gain_key
    queries = low(q_normed * cosine + rotate_half(q_normed) * sine_table)
    keys_all = low(k_normed * cosine + rotate_half(k_normed) * sine_table)
    queries = queries.reshape(GROUP_TOK, KV_HEADS, per_group, HD)
    rows_block = min(512, GROUP_TOK)
    blocks = GROUP_TOK // rows_block

    def attend(block):
        q_block, pos_block, seg_block = block
        scores = jnp.einsum('qhgd,khd->hgqk', q_block, keys_all, precision=HIGHEST)
        scores = low_back(scores) * HD ** (-0.5)
        allowed = (seg_block[:, None] == segment[None, :]) & (packed[None, :] <= pos_block[:, None])
        scores = jnp.where(allowed[None, None], scores, NEGATIVE)
        highest = lax.optimization_barrier(jnp.max(scores, axis=-1, keepdims=True))
        lifted = jnp.where(allowed[None, None], jnp.exp(scores - highest), 0.0)
        shares = lifted / lax.optimization_barrier(jnp.sum(lifted, axis=-1, keepdims=True))
        return jnp.einsum('hgqk,khd->qhgd', low(shares), values_all, precision=HIGHEST)
    attn = lax.map(jax.checkpoint(attend), (queries.reshape(blocks, rows_block, KV_HEADS, per_group, HD), packed.reshape(blocks, rows_block), segment.reshape(blocks, rows_block)))
    attn_in = low_back(low(attn.reshape(GROUP_TOK, q_width)))
    h_one = inputs + low_back(jnp.dot(attn_in, w_out, precision=HIGHEST))
    normed_two = low(h_one * rms_scale(h_one) * gain_ffn)
    gate_up = low_back(jnp.einsum('td,dgf->tgf', normed_two, w_gate_up, precision=HIGHEST))
    gate = gate_up[:, 0]
    upper = gate_up[:, 1]
    hidden = low(gate * jax.nn.sigmoid(gate) * upper)
    return h_one + low_back(jnp.dot(hidden, w_down, precision=HIGHEST))

def reference(tokens, qkv_weight, out_weight, gate_up_weight, down_weight, attn_gain, ffn_gain, query_gain, key_gain, seq_lengths, block_order, cotangent):

    def forward(inputs_all, w_qkv, w_out, w_gate_up, w_down, gain_attn, gain_ffn, gain_query, gain_key):
        weights = (w_qkv, w_out, w_gate_up, w_down, gain_attn, gain_ffn, gain_query, gain_key)

        def group_step(carry, pieces):
            inputs, lengths, order = pieces
            return (carry, group_forward(weights, inputs, lengths, order))
        return lax.scan(jax.checkpoint(group_step), jnp.zeros((), jnp.float32), (inputs_all, seq_lengths, block_order))[1]
    primals = (tokens.astype(jnp.float32), qkv_weight.astype(jnp.float32), out_weight.astype(jnp.float32), gate_up_weight.astype(jnp.float32), down_weight.astype(jnp.float32), attn_gain.astype(jnp.float32), ffn_gain.astype(jnp.float32), query_gain.astype(jnp.float32), key_gain.astype(jnp.float32))
    result, pullback = jax.vjp(forward, *primals)
    grads = pullback(cotangent.astype(jnp.float32))
    return (result.astype(jnp.bfloat16), grads[0], grads[1], grads[2], grads[3], grads[4], grads[5], grads[6], grads[7], grads[8])
```

```python
import functools

import jax
import jax.numpy as jnp
from jax import lax
from jax.experimental import pallas as pl
from jax.experimental.pallas import tpu as pltpu
from jax.sharding import PartitionSpec as P

HEADS = 16
KV_HEADS = 8
HD = 64
BLK = 128
TILE = 256


EPSILON = 1e-05
ROPE_BASE = 1000000.0
LOG2E = 1.4426950408889634
SCORE_SCALE = LOG2E * HD ** (-0.5)


def rms_scale(values, axis=-1):
    return lax.rsqrt(jnp.mean(values * values, axis=axis, keepdims=True) + EPSILON)


def norm_back(grad_normed, inputs, scale, gain, axis=-1):
    scaled = grad_normed * gain
    grad_in = scale * scaled - inputs * scale * scale * scale * jnp.mean(
        scaled * inputs, axis=axis, keepdims=True
    )
    return (grad_in, grad_normed * inputs * scale)


def rope(values, cosine, sine):
    half = HD // 2
    first, second = values[:, :half], values[:, half:]
    return jnp.concatenate([first * cosine - second * sine, second * cosine + first * sine], axis=1)


def rope_back(values, cosine, sine):
    half = HD // 2
    first, second = values[:, :half], values[:, half:]
    return jnp.concatenate([first * cosine + second * sine, second * cosine - first * sine], axis=1)


def starts_of(packed, lengths_row):
    ends = jnp.cumsum(lengths_row)
    past = packed[:, None] >= ends[None, :]
    return jnp.sum(jnp.where(past, lengths_row[None, :], 0), axis=1)


def block_tables(order, lengths_row):
    count = order.shape[0]
    rank = jnp.sum((order[None, :] < order[:, None]).astype(jnp.int32), axis=1)
    hit = rank[None, :] == jnp.arange(count, dtype=jnp.int32)[:, None]
    slot = jnp.sum(jnp.where(hit, jnp.arange(count, dtype=jnp.int32)[None, :], 0), axis=1)
    block = jnp.sum(jnp.where(hit, order[None, :], 0), axis=1)
    place = (block[:, None] * BLK + jnp.arange(BLK, dtype=jnp.int32)[None, :]).reshape(-1)
    return (slot, place, starts_of(place, lengths_row))


def attend_kernel(
    q_slot, kv_slot, first, last, qkv_ref, place_ref, start_ref,
    out_ref, q_ref, qt_ref, k_ref, kt_ref, v_ref, ot_ref, total_ref, vt_ref
):
    per_device = qkv_ref.shape[2] // BLK
    kv_blocks = k_ref.shape[0] // BLK
    q_blocks = q_ref.shape[0] // BLK

    def piece(slot, lower):
        return qkv_ref[
            slot // per_device,
            lower : lower + HD,
            pl.ds(pl.multiple_of((slot % per_device) * BLK, BLK), BLK),
        ]

    for i in range(kv_blocks):
        here = slice(i * BLK, (i + 1) * BLK)
        keys = piece(kv_slot[i], HD)
        kt_ref[:, here] = keys
        k_ref[here, :] = keys.T
        values = piece(kv_slot[i], 2 * HD)
        vt_ref[:, here] = values
        v_ref[here, :] = values.T
    for i in range(q_blocks):
        here = slice(i * BLK, (i + 1) * BLK)
        queries = piece(q_slot[i], 0)
        qt_ref[:, here] = queries
        q_ref[here, :] = queries.T
    if q_blocks < kv_blocks:
        out_ref[...] = jnp.zeros_like(out_ref)

    def tile(i, carry):
        rows = pl.ds(pl.multiple_of(i * TILE, TILE), TILE)
        queries = qt_ref[:, rows]
        place = place_ref[:, rows]
        start = start_ref[:, rows]

        def step(j, state):
            total, summed = state
            at = pl.multiple_of(j * TILE, TILE)
            scores = jnp.dot(
                k_ref[pl.ds(at, TILE), :], queries, preferred_element_type=jnp.float32
            )
            key_place = lax.broadcasted_iota(jnp.int32, (TILE, TILE), 0) + at
            allowed = (key_place <= place) & (key_place >= start)
            lifted = jnp.where(allowed, jnp.exp2(scores * SCORE_SCALE), 0.0)
            total = total + jnp.sum(lifted, axis=0, keepdims=True)
            summed = summed + jnp.dot(
                vt_ref[:, pl.ds(at, TILE)],
                lifted.astype(jnp.bfloat16),
                preferred_element_type=jnp.float32,
            )
            return (total, summed)

        total, summed = lax.fori_loop(
            first[i],
            last[i],
            step,
            (jnp.zeros((1, TILE), jnp.float32), jnp.zeros((HD, TILE), jnp.float32)),
        )
        attn = summed / total
        ot_ref[:, rows] = attn
        total_ref[:, rows] = jnp.log(total) * LOG2E
        rounded = attn.astype(jnp.bfloat16)
        for part in range(TILE // BLK):
            slot = q_slot[i * (TILE // BLK) + part]
            out_ref[
                slot // per_device,
                :,
                pl.ds(pl.multiple_of((slot % per_device) * BLK, BLK), BLK),
            ] = rounded[:, part * BLK : (part + 1) * BLK]
        return carry

    lax.fori_loop(0, q_blocks * BLK // TILE, tile, 0)


def attend_back_kernel(
    q_slot, kv_slot, first, last, d_ref, place_ref, start_ref,
    q_ref, qt_ref, k_ref, kt_ref, v_ref, ot_ref, total_ref,
    out_ref, dt_ref, do_ref, dk_ref, dv_ref
):
    per_device = d_ref.shape[2] // BLK
    kv_blocks = k_ref.shape[0] // BLK
    q_blocks = q_ref.shape[0] // BLK

    def lanes(slot):
        return pl.ds(pl.multiple_of((slot % per_device) * BLK, BLK), BLK)

    for i in range(q_blocks):
        here = slice(i * BLK, (i + 1) * BLK)
        slot = q_slot[i]
        grads = d_ref[slot // per_device, :, lanes(slot)]
        dt_ref[:, here] = grads
        do_ref[here, :] = grads.T
    dk_ref[...] = jnp.zeros_like(dk_ref)
    dv_ref[...] = jnp.zeros_like(dv_ref)
    if q_blocks < kv_blocks:
        out_ref[...] = jnp.zeros_like(out_ref)

    def tile(i, carry):
        rows = pl.ds(pl.multiple_of(i * TILE, TILE), TILE)
        queries = qt_ref[:, rows]
        grads = dt_ref[:, rows]
        place = place_ref[:, rows]
        start = start_ref[:, rows]
        delta = jnp.sum(grads.astype(jnp.float32) * ot_ref[:, rows], axis=0, keepdims=True)
        total = total_ref[:, rows]

        def step(j, d_query):
            at = pl.multiple_of(j * TILE, TILE)
            here = pl.ds(at, TILE)
            scores = jnp.dot(k_ref[here, :], queries, preferred_element_type=jnp.float32)
            key_place = lax.broadcasted_iota(jnp.int32, (TILE, TILE), 0) + at
            allowed = (key_place <= place) & (key_place >= start)
            shares = jnp.where(allowed, jnp.exp2(scores * SCORE_SCALE - total), 0.0)
            d_shares = jnp.dot(v_ref[here, :], grads, preferred_element_type=jnp.float32)
            d_scores = (shares * (d_shares - delta)).astype(jnp.bfloat16)
            dv_ref[here, :] += jnp.dot(
                shares.astype(jnp.bfloat16), do_ref[rows, :], preferred_element_type=jnp.float32
            )
            dk_ref[here, :] += jnp.dot(
                d_scores, q_ref[rows, :], preferred_element_type=jnp.float32
            )
            return d_query + jnp.dot(
                kt_ref[:, here], d_scores, preferred_element_type=jnp.float32
            )

        d_query = lax.fori_loop(first[i], last[i], step, jnp.zeros((HD, TILE), jnp.float32))
        rounded = (d_query * HD ** (-0.5)).astype(jnp.bfloat16)
        for part in range(TILE // BLK):
            slot = q_slot[i * (TILE // BLK) + part]
            out_ref[slot // per_device, 0:HD, lanes(slot)] = rounded[
                :, part * BLK : (part + 1) * BLK
            ]
        return carry

    lax.fori_loop(0, q_blocks * BLK // TILE, tile, 0)
    for i in range(kv_blocks):
        here = slice(i * BLK, (i + 1) * BLK)
        slot = kv_slot[i]
        out_ref[slot // per_device, HD : 2 * HD, lanes(slot)] = (
            (dk_ref[here, :] * HD ** (-0.5)).T.astype(jnp.bfloat16)
        )
        out_ref[slot // per_device, 2 * HD : 3 * HD, lanes(slot)] = (
            dv_ref[here, :].T.astype(jnp.bfloat16)
        )


def kernel_call(kernel, tables, arrays, outs, scratch):
    smem = pl.BlockSpec(memory_space=pltpu.SMEM)
    vmem = pl.BlockSpec(memory_space=pltpu.VMEM)
    return pl.pallas_call(
        kernel,
        out_shape=outs,
        in_specs=[smem] * len(tables) + [vmem] * len(arrays),
        out_specs=[vmem] * len(outs),
        scratch_shapes=scratch,
        compiler_params=pltpu.CompilerParams(vmem_limit_bytes=48 * 1024 * 1024),
    )(*tables, *arrays)


def on_device(
    tokens,
    qkv_weight,
    out_weight,
    gate_up_weight,
    down_weight,
    attn_gain,
    ffn_gain,
    query_gain,
    key_gain,
    seq_lengths,
    block_order,
    cotangent,
):
    inputs = tokens[0].astype(jnp.float32)
    rows_here = inputs.shape[0]
    ctx_size = lax.axis_size("ctx")
    ctx_index = lax.axis_index("ctx")
    per_group = HEADS // KV_HEADS
    q_width = HEADS * HD
    kv_width = KV_HEADS * HD
    order_row = block_order[0]
    lengths_row = seq_lengths[0]
    slots = jnp.arange(rows_here, dtype=jnp.int32) // BLK + ctx_index * (rows_here // BLK)
    table = slots[:, None] == jnp.arange(order_row.shape[0], dtype=jnp.int32)[None, :]
    packed = (
        jnp.sum(jnp.where(table, order_row[None, :], 0), axis=1) * BLK
        + jnp.arange(rows_here, dtype=jnp.int32) % BLK
    )
    local = packed - starts_of(packed, lengths_row)
    frequency = ROPE_BASE ** (-2.0 * jnp.arange(HD // 2, dtype=jnp.float32) / HD)
    angle = frequency[:, None] * local.astype(jnp.float32)[None, :]
    cosine = jnp.cos(angle)[None]
    sine = jnp.sin(angle)[None]
    bf16, f32 = jnp.bfloat16, jnp.float32
    parts = ctx_size // HEADS
    part = ctx_index // HEADS
    part_blocks = HEADS * rows_here // BLK
    q_order = lax.dynamic_slice_in_dim(order_row, part * part_blocks, part_blocks)
    q_slot, q_place, q_start = block_tables(q_order, lengths_row)
    q_slot = q_slot + part * part_blocks
    kv_slot, _, _ = block_tables(order_row, lengths_row)
    first = jnp.min(q_start.reshape(-1, TILE), axis=1) // TILE
    last = jnp.max(q_place.reshape(-1, TILE), axis=1) // TILE + 1
    tables = (q_slot, kv_slot, first, last)
    q_rows, kv_rows = part_blocks * BLK, order_row.shape[0] * BLK

    def fetch_attention():
        return (
            lax.all_gather(qkv_weight, "fsdp", axis=0, tiled=True),
            lax.all_gather(out_weight, "fsdp", axis=0, tiled=True),
            lax.all_gather(attn_gain, "fsdp", axis=0, tiled=True),
            lax.all_gather(ffn_gain, "fsdp", axis=0, tiled=True),
            lax.all_gather(query_gain, "fsdp", axis=0, tiled=True),
            lax.all_gather(key_gain, "fsdp", axis=0, tiled=True),
        )

    w_qkv, w_out, gain_attn, gain_ffn, gain_query, gain_key = fetch_attention()
    gain_attn = gain_attn.astype(jnp.float32)
    gain_ffn = gain_ffn.astype(jnp.float32)
    gain_query = gain_query.astype(jnp.float32)
    gain_key = gain_key.astype(jnp.float32)
    scale_one = rms_scale(inputs)
    normed = (inputs * scale_one * gain_attn).astype(jnp.bfloat16)
    projected = lax.dot_general(
        w_qkv, normed, (((0,), (1,)), ((), ())), preferred_element_type=f32
    )
    q_raw = projected[:q_width].reshape(HEADS, HD, rows_here)
    k_raw = projected[q_width : q_width + kv_width].reshape(KV_HEADS, HD, rows_here)
    values_here = projected[q_width + kv_width :].reshape(KV_HEADS, HD, rows_here).astype(bf16)
    q_scale = rms_scale(q_raw, 1)
    k_scale = rms_scale(k_raw, 1)
    column_query, column_key = gain_query[:, None], gain_key[:, None]
    queries = rope(q_raw * q_scale * column_query, cosine, sine).astype(bf16)
    keys_here = rope(k_raw * k_scale * column_key, cosine, sine).astype(bf16)
    sent = jnp.concatenate(
        [queries, jnp.repeat(keys_here, per_group, 0), jnp.repeat(values_here, per_group, 0)], axis=1
    )
    sent = jnp.concatenate([sent] * parts, axis=0)
    got = lax.all_to_all(sent, "ctx", 0, 0, tiled=True)
    q_place, q_start = q_place[None], q_start[None]
    shape = jax.ShapeDtypeStruct
    attn_sent, *held = kernel_call(
        attend_kernel,
        tables,
        (got, q_place, q_start),
        [
            shape((ctx_size, HD, rows_here), bf16),
            shape((q_rows, HD), bf16),
            shape((HD, q_rows), bf16),
            shape((kv_rows, HD), bf16),
            shape((HD, kv_rows), bf16),
            shape((kv_rows, HD), bf16),
            shape((HD, q_rows), f32),
            shape((1, q_rows), f32),
        ],
        [pltpu.VMEM((HD, kv_rows), bf16)],
    )
    attn_in = lax.dynamic_slice_in_dim(
        lax.all_to_all(attn_sent, "ctx", 0, 0, tiled=True), part * HEADS, HEADS
    ).reshape(q_width, rows_here)
    h_one = inputs + lax.dot_general(
        attn_in, w_out, (((0,), (0,)), ((), ())), preferred_element_type=f32
    )
    scale_two = rms_scale(h_one)
    normed_two = (h_one * scale_two * gain_ffn).astype(jnp.bfloat16)
    columns = normed_two
    gate_up = jnp.einsum(
        "tr,rgf->tgf",
        columns,
        lax.all_gather(gate_up_weight, "fsdp", axis=0, tiled=True),
        preferred_element_type=jnp.float32,
    )
    gate = gate_up[:, 0]
    upper = gate_up[:, 1]
    sigma = jax.nn.sigmoid(gate)
    hidden = (gate * sigma * upper).astype(jnp.bfloat16)
    columns = hidden
    ffn_out = jnp.dot(
        columns,
        lax.all_gather(down_weight, "fsdp", axis=0, tiled=True),
        preferred_element_type=jnp.float32,
    )
    output = (h_one + ffn_out).astype(jnp.bfloat16)
    d_out = cotangent[0].astype(jnp.float32)
    d_ffn = d_out.astype(jnp.bfloat16)
    d_hidden = lax.dot_general(
        d_ffn,
        lax.all_gather(down_weight, "fsdp", axis=0, tiled=True),
        (((1,), (1,)), ((), ())),
        preferred_element_type=jnp.float32,
    )
    d_gate = d_hidden * upper * sigma * (1.0 + gate * (1.0 - sigma))
    d_upper = d_hidden * gate * sigma
    d_gate_up = jnp.stack([d_gate, d_upper], axis=1).astype(jnp.bfloat16)
    d_normed_two = jnp.einsum(
        "tgf,rgf->tr",
        d_gate_up,
        lax.all_gather(gate_up_weight, "fsdp", axis=0, tiled=True),
        preferred_element_type=jnp.float32,
    )
    columns = normed_two
    grad_gate_up = lax.psum_scatter(
        jnp.einsum("tr,tgf->rgf", columns, d_gate_up, preferred_element_type=jnp.float32).astype(
            jnp.bfloat16
        ),
        "fsdp",
        scatter_dimension=0,
        tiled=True,
    )
    columns = hidden
    grad_down = lax.psum_scatter(
        lax.dot_general(
            columns, d_ffn, (((0,), (0,)), ((), ())), preferred_element_type=jnp.float32
        ).astype(jnp.bfloat16),
        "fsdp",
        scatter_dimension=0,
        tiled=True,
    )
    d_norm_two, ffn_gain_term = norm_back(d_normed_two, h_one, scale_two, gain_ffn)
    d_h_one = d_out + d_norm_two
    d_attn = d_h_one.astype(jnp.bfloat16)
    grad_out_here = jnp.dot(attn_in, d_attn, preferred_element_type=f32)
    d_heads = lax.dot_general(
        w_out, d_attn, (((1,), (1,)), ((), ())), preferred_element_type=f32
    ).astype(bf16)
    d_heads = jnp.concatenate([d_heads.reshape(HEADS, HD, rows_here)] * parts, axis=0)
    d_got = lax.all_to_all(d_heads, "ctx", 0, 0, tiled=True)
    (d_sent,) = kernel_call(
        attend_back_kernel,
        tables,
        (d_got, q_place, q_start, *held),
        [shape((ctx_size, 3 * HD, rows_here), bf16)],
        [
            pltpu.VMEM((HD, q_rows), bf16),
            pltpu.VMEM((q_rows, HD), bf16),
            pltpu.VMEM((kv_rows, HD), f32),
            pltpu.VMEM((kv_rows, HD), f32),
        ],
    )
    d_back = lax.all_to_all(d_sent, "ctx", 0, 0, tiled=True)
    d_query = lax.dynamic_slice_in_dim(d_back[:, :HD], part * HEADS, HEADS).astype(f32)
    d_key_value = jnp.sum(
        d_back[:, HD:].reshape(parts, KV_HEADS, per_group, 2 * HD, rows_here).astype(f32),
        axis=(0, 2),
    )
    dq_normed = rope_back(d_query, cosine, sine)
    dk_normed = rope_back(d_key_value[:, :HD], cosine, sine)
    dq_raw, query_term = norm_back(dq_normed, q_raw, q_scale, column_query, 1)
    dk_raw, key_term = norm_back(dk_normed, k_raw, k_scale, column_key, 1)
    d_projected = jnp.concatenate(
        [
            dq_raw.reshape(q_width, rows_here).astype(bf16),
            dk_raw.reshape(kv_width, rows_here).astype(bf16),
            d_key_value[:, HD:].reshape(kv_width, rows_here).astype(bf16),
        ],
        axis=0,
    )
    grad_qkv_here = lax.dot_general(
        normed, d_projected, (((0,), (1,)), ((), ())), preferred_element_type=f32
    )
    d_normed = lax.dot_general(
        d_projected, w_qkv, (((0,), (1,)), ((), ())), preferred_element_type=f32
    )
    d_norm_one, attn_gain_term = norm_back(d_normed, inputs, scale_one, gain_attn)
    d_inputs = d_h_one + d_norm_one
    shard_qkv, shard_out, shard_attn_gain, shard_ffn_gain, shard_query_gain, shard_key_gain = (
        lax.psum_scatter(
            grad_qkv_here.astype(jnp.bfloat16), "fsdp", scatter_dimension=0, tiled=True
        ).astype(jnp.float32),
        lax.psum_scatter(
            grad_out_here.astype(jnp.bfloat16), "fsdp", scatter_dimension=0, tiled=True
        ).astype(jnp.float32),
        lax.psum_scatter(
            jnp.sum(attn_gain_term, axis=0).astype(jnp.bfloat16),
            "fsdp",
            scatter_dimension=0,
            tiled=True,
        ).astype(jnp.float32),
        lax.psum_scatter(
            jnp.sum(ffn_gain_term, axis=0).astype(jnp.bfloat16),
            "fsdp",
            scatter_dimension=0,
            tiled=True,
        ).astype(jnp.float32),
        lax.psum_scatter(
            jnp.sum(query_term, axis=(0, 2)).astype(jnp.bfloat16),
            "fsdp",
            scatter_dimension=0,
            tiled=True,
        ).astype(jnp.float32),
        lax.psum_scatter(
            jnp.sum(key_term, axis=(0, 2)).astype(jnp.bfloat16),
            "fsdp",
            scatter_dimension=0,
            tiled=True,
        ).astype(jnp.float32),
    )
    summed_grads = (
        lax.psum(shard_qkv.astype(jnp.bfloat16), "ctx").astype(jnp.float32),
        lax.psum(shard_out.astype(jnp.bfloat16), "ctx").astype(jnp.float32),
        lax.psum(grad_gate_up, "ctx").astype(jnp.float32),
        lax.psum(grad_down, "ctx").astype(jnp.float32),
        lax.psum(shard_attn_gain.astype(jnp.bfloat16), "ctx").astype(jnp.float32),
        lax.psum(shard_ffn_gain.astype(jnp.bfloat16), "ctx").astype(jnp.float32),
        lax.psum(shard_query_gain.astype(jnp.bfloat16), "ctx").astype(jnp.float32),
        lax.psum(shard_key_gain.astype(jnp.bfloat16), "ctx").astype(jnp.float32),
    )
    return (
        output[None],
        d_inputs[None],
        summed_grads[0],
        summed_grads[1],
        summed_grads[2],
        summed_grads[3],
        summed_grads[4],
        summed_grads[5],
        summed_grads[6],
        summed_grads[7],
    )


def solution(mesh):
    return jax.shard_map(
        on_device,
        mesh=mesh,
        in_specs=(
            P("fsdp", "ctx", None),
            P("fsdp", None),
            P("fsdp", None),
            P("fsdp", None, None),
            P("fsdp", None),
            P("fsdp"),
            P("fsdp"),
            P("fsdp"),
            P("fsdp"),
            P("fsdp", None),
            P("fsdp", None),
            P("fsdp", "ctx", None),
        ),
        out_specs=(
            P("fsdp", "ctx", None),
            P("fsdp", "ctx", None),
            P("fsdp", None),
            P("fsdp", None),
            P("fsdp", None, None),
            P("fsdp", None),
            P("fsdp"),
            P("fsdp"),
            P("fsdp"),
            P("fsdp"),
        ),
        check_vma=False,
    )
```

```python
import functools

import jax
import jax.numpy as jnp
from jax import lax
from jax.experimental import pallas as pl
from jax.experimental.pallas import tpu as pltpu
from jax.sharding import PartitionSpec as P

HEADS = 16
KV_HEADS = 8
HD = 64
BLK = 128
TILE = 256
CHUNKS = 2


EPSILON = 1e-05
ROPE_BASE = 1000000.0
LOG2E = 1.4426950408889634
SCORE_SCALE = LOG2E * HD ** (-0.5)


def rms_scale(values, axis=-1):
    return lax.rsqrt(jnp.mean(values * values, axis=axis, keepdims=True) + EPSILON)


def norm_back(grad_normed, inputs, scale, gain, axis=-1):
    scaled = grad_normed * gain
    grad_in = scale * scaled - inputs * scale * scale * scale * jnp.mean(
        scaled * inputs, axis=axis, keepdims=True
    )
    return (grad_in, grad_normed * inputs * scale)


def rope(values, cosine, sine):
    half = HD // 2
    first, second = values[:, :half], values[:, half:]
    return jnp.concatenate([first * cosine - second * sine, second * cosine + first * sine], axis=1)


def rope_back(values, cosine, sine):
    half = HD // 2
    first, second = values[:, :half], values[:, half:]
    return jnp.concatenate([first * cosine + second * sine, second * cosine - first * sine], axis=1)


def starts_of(packed, lengths_row):
    ends = jnp.cumsum(lengths_row)
    past = packed[:, None] >= ends[None, :]
    return jnp.sum(jnp.where(past, lengths_row[None, :], 0), axis=1)


def block_tables(order, lengths_row):
    count = order.shape[0]
    rank = jnp.sum((order[None, :] < order[:, None]).astype(jnp.int32), axis=1)
    hit = rank[None, :] == jnp.arange(count, dtype=jnp.int32)[:, None]
    slot = jnp.sum(jnp.where(hit, jnp.arange(count, dtype=jnp.int32)[None, :], 0), axis=1)
    block = jnp.sum(jnp.where(hit, order[None, :], 0), axis=1)
    place = (block[:, None] * BLK + jnp.arange(BLK, dtype=jnp.int32)[None, :]).reshape(-1)
    return (slot, place, starts_of(place, lengths_row))


def attend_kernel(
    q_slot, kv_slot, first, last, qkv_ref, place_ref, start_ref,
    out_ref, q_ref, qt_ref, k_ref, kt_ref, v_ref, ot_ref, total_ref, vt_ref
):
    per_device = qkv_ref.shape[2] // BLK
    kv_blocks = k_ref.shape[0] // BLK
    q_blocks = q_ref.shape[0] // BLK

    def piece(slot, lower):
        return qkv_ref[
            slot // per_device,
            lower : lower + HD,
            pl.ds(pl.multiple_of((slot % per_device) * BLK, BLK), BLK),
        ]

    for i in range(kv_blocks):
        here = slice(i * BLK, (i + 1) * BLK)
        keys = piece(kv_slot[i], HD)
        kt_ref[:, here] = keys
        k_ref[here, :] = keys.T
        values = piece(kv_slot[i], 2 * HD)
        vt_ref[:, here] = values
        v_ref[here, :] = values.T
    for i in range(q_blocks):
        here = slice(i * BLK, (i + 1) * BLK)
        queries = piece(q_slot[i], 0)
        qt_ref[:, here] = queries
        q_ref[here, :] = queries.T
    if q_blocks < kv_blocks:
        out_ref[...] = jnp.zeros_like(out_ref)

    def tile(i, carry):
        rows = pl.ds(pl.multiple_of(i * TILE, TILE), TILE)
        queries = qt_ref[:, rows]
        place = place_ref[:, rows]
        start = start_ref[:, rows]

        def step(j, state):
            total, summed = state
            at = pl.multiple_of(j * TILE, TILE)
            scores = jnp.dot(
                k_ref[pl.ds(at, TILE), :], queries, preferred_element_type=jnp.float32
            )
            key_place = lax.broadcasted_iota(jnp.int32, (TILE, TILE), 0) + at
            allowed = (key_place <= place) & (key_place >= start)
            lifted = jnp.where(allowed, jnp.exp2(scores * SCORE_SCALE), 0.0)
            total = total + jnp.sum(lifted, axis=0, keepdims=True)
            summed = summed + jnp.dot(
                vt_ref[:, pl.ds(at, TILE)],
                lifted.astype(jnp.bfloat16),
                preferred_element_type=jnp.float32,
            )
            return (total, summed)

        total, summed = lax.fori_loop(
            first[i],
            last[i],
            step,
            (jnp.zeros((1, TILE), jnp.float32), jnp.zeros((HD, TILE), jnp.float32)),
        )
        attn = summed / total
        ot_ref[:, rows] = attn
        total_ref[:, rows] = jnp.log(total) * LOG2E
        rounded = attn.astype(jnp.bfloat16)
        for part in range(TILE // BLK):
            slot = q_slot[i * (TILE // BLK) + part]
            out_ref[
                slot // per_device,
                :,
                pl.ds(pl.multiple_of((slot % per_device) * BLK, BLK), BLK),
            ] = rounded[:, part * BLK : (part + 1) * BLK]
        return carry

    lax.fori_loop(0, q_blocks * BLK // TILE, tile, 0)


def attend_back_kernel(
    q_slot, kv_slot, first, last, d_ref, place_ref, start_ref,
    q_ref, qt_ref, k_ref, kt_ref, v_ref, ot_ref, total_ref,
    out_ref, dt_ref, do_ref, dk_ref, dv_ref
):
    per_device = d_ref.shape[2] // BLK
    kv_blocks = k_ref.shape[0] // BLK
    q_blocks = q_ref.shape[0] // BLK

    def lanes(slot):
        return pl.ds(pl.multiple_of((slot % per_device) * BLK, BLK), BLK)

    for i in range(q_blocks):
        here = slice(i * BLK, (i + 1) * BLK)
        slot = q_slot[i]
        grads = d_ref[slot // per_device, :, lanes(slot)]
        dt_ref[:, here] = grads
        do_ref[here, :] = grads.T
    dk_ref[...] = jnp.zeros_like(dk_ref)
    dv_ref[...] = jnp.zeros_like(dv_ref)
    if q_blocks < kv_blocks:
        out_ref[...] = jnp.zeros_like(out_ref)

    def tile(i, carry):
        rows = pl.ds(pl.multiple_of(i * TILE, TILE), TILE)
        queries = qt_ref[:, rows]
        grads = dt_ref[:, rows]
        place = place_ref[:, rows]
        start = start_ref[:, rows]
        delta = jnp.sum(grads.astype(jnp.float32) * ot_ref[:, rows], axis=0, keepdims=True)
        total = total_ref[:, rows]

        def step(j, d_query):
            at = pl.multiple_of(j * TILE, TILE)
            here = pl.ds(at, TILE)
            scores = jnp.dot(k_ref[here, :], queries, preferred_element_type=jnp.float32)
            key_place = lax.broadcasted_iota(jnp.int32, (TILE, TILE), 0) + at
            allowed = (key_place <= place) & (key_place >= start)
            shares = jnp.where(allowed, jnp.exp2(scores * SCORE_SCALE - total), 0.0)
            d_shares = jnp.dot(v_ref[here, :], grads, preferred_element_type=jnp.float32)
            d_scores = (shares * (d_shares - delta)).astype(jnp.bfloat16)
            dv_ref[here, :] += jnp.dot(
                shares.astype(jnp.bfloat16), do_ref[rows, :], preferred_element_type=jnp.float32
            )
            dk_ref[here, :] += jnp.dot(
                d_scores, q_ref[rows, :], preferred_element_type=jnp.float32
            )
            return d_query + jnp.dot(
                kt_ref[:, here], d_scores, preferred_element_type=jnp.float32
            )

        d_query = lax.fori_loop(first[i], last[i], step, jnp.zeros((HD, TILE), jnp.float32))
        rounded = (d_query * HD ** (-0.5)).astype(jnp.bfloat16)
        for part in range(TILE // BLK):
            slot = q_slot[i * (TILE // BLK) + part]
            out_ref[slot // per_device, 0:HD, lanes(slot)] = rounded[
                :, part * BLK : (part + 1) * BLK
            ]
        return carry

    lax.fori_loop(0, q_blocks * BLK // TILE, tile, 0)
    for i in range(kv_blocks):
        here = slice(i * BLK, (i + 1) * BLK)
        slot = kv_slot[i]
        out_ref[slot // per_device, HD : 2 * HD, lanes(slot)] = (
            (dk_ref[here, :] * HD ** (-0.5)).T.astype(jnp.bfloat16)
        )
        out_ref[slot // per_device, 2 * HD : 3 * HD, lanes(slot)] = (
            dv_ref[here, :].T.astype(jnp.bfloat16)
        )


def kernel_call(kernel, tables, arrays, outs, scratch):
    smem = pl.BlockSpec(memory_space=pltpu.SMEM)
    vmem = pl.BlockSpec(memory_space=pltpu.VMEM)
    return pl.pallas_call(
        kernel,
        out_shape=outs,
        in_specs=[smem] * len(tables) + [vmem] * len(arrays),
        out_specs=[vmem] * len(outs),
        scratch_shapes=scratch,
        compiler_params=pltpu.CompilerParams(vmem_limit_bytes=48 * 1024 * 1024),
    )(*tables, *arrays)


class Links:
    def __init__(self, ctx_size):
        self.depth = ctx_size // 4
        index = lax.axis_index("ctx")
        self.core = index % 2
        self.y = (index // 2) % 2
        self.side = lax.axis_index("fsdp")
        self.half = ((index // 4 + 1) // 2) % 2

    def route(self, place):
        pairs = []
        for z in range(self.depth):
            for y in range(2):
                for core in range(2):
                    to_z, to_y, to_core = place(z, y, core)
                    pairs.append(((z * 2 + y) * 2 + core, (to_z * 2 + to_y) * 2 + to_core))
        return pairs

    def over_core(self, value):
        return lax.ppermute(value, "ctx", self.route(lambda z, y, c: (z, y, 1 - c)))

    def over_y(self, value):
        return lax.ppermute(value, "ctx", self.route(lambda z, y, c: (z, 1 - y, c)))

    def over_z(self, value):
        return lax.ppermute(value, "ctx", self.route(lambda z, y, c: (z ^ 1, y, c)))

    def mirror_z(self, value):
        return lax.ppermute(value, "ctx", self.route(lambda z, y, c: (self.depth - 1 - z, y, c)))

    def over_x(self, value):
        return lax.ppermute(value, "fsdp", [(0, 1), (1, 0)])

    def gather_plane(self, value):
        pair = jnp.stack([value, self.over_y(value)])
        other = self.over_core(pair)
        return jnp.stack([pair[0], other[0], pair[1], other[1]])

    def sum_depth(self, value):
        halves = value.reshape(2, value.shape[0] // 2, value.shape[1])
        mine = pick(halves, self.half, 0)
        part = add(mine, self.over_z(pick(halves, 1 - self.half, 0)))
        full = add(part, self.mirror_z(part))
        return jnp.stack([full, self.over_z(full)])

    def spread_plane(self, value):
        beside = self.over_y(value)
        return (value, beside, self.over_core(value), self.over_core(beside))


def pick(value, index, axis):
    return lax.dynamic_index_in_dim(value, index, axis, keepdims=False)


def add(left, right):
    return (left.astype(jnp.float32) + right.astype(jnp.float32)).astype(jnp.bfloat16)


def place_gate_up_kernel(here, *refs):
    out_ref = refs[-1]
    half, core, y = here[0], here[1], here[2]
    wide = refs[0].shape[2]
    for chunk in range(len(refs) // 4):
        mine, beside, across, diagonal = (r[0] for r in refs[4 * chunk : 4 * chunk + 4])
        for kind in range(2):
            for column in range(2):
                value = jnp.where(
                    core == kind,
                    jnp.where(y == column, mine, beside),
                    jnp.where(y == column, across, diagonal),
                )
                at = (2 * chunk + column) * wide
                out_ref[:, kind, at : at + wide] = value.astype(jnp.float32)


def place_gate_up(here, chunks):
    _, rows, wide = chunks[0][0].shape
    step = 32
    flat = [array for chunk in chunks for array in chunk]

    def piece(i, here):
        return ((i // (rows // step)) ^ here[0], i % (rows // step), 0)

    return pl.pallas_call(
        place_gate_up_kernel,
        grid_spec=pltpu.PrefetchScalarGridSpec(
            num_scalar_prefetch=1,
            grid=(2 * rows // step,),
            in_specs=[pl.BlockSpec((1, step, wide), piece)] * len(flat),
            out_specs=pl.BlockSpec((step, 2, 2 * wide * len(chunks)), lambda i, here: (i, 0, 0)),
        ),
        out_shape=jax.ShapeDtypeStruct((2 * rows, 2, 2 * wide * len(chunks)), jnp.float32),
        compiler_params=pltpu.CompilerParams(vmem_limit_bytes=40 * 1024 * 1024),
    )(here, *flat)


def place_pieces(here, pieces, cuts, by_rows):
    _, rows, _ = pieces[0].shape

    def kernel(here, *refs):
        s = pl.program_id(0)
        for a in range(4):

            @pl.when(s // 2 == a)
            def _(a=a):
                at = 0
                for out_ref in refs[4:]:
                    wide = out_ref.shape[1]
                    out_ref[...] = refs[a][0, :, at : at + wide].astype(jnp.float32)
                    at += wide

    def source(a):
        return lambda s, here: (jnp.clip(s - 2 * a, 0, 1), 0, 0)

    def target(s, here):
        half = (s % 2) ^ here[0]
        core = (s // 4) ^ here[1]
        y = ((s // 2) % 2) ^ here[2]
        if by_rows:
            return ((core * 2 + y) * 2 + half, 0)
        return (half, core * 2 + y)

    across, along = (1, 8) if by_rows else (4, 2)
    return pl.pallas_call(
        kernel,
        grid_spec=pltpu.PrefetchScalarGridSpec(
            num_scalar_prefetch=1,
            grid=(8,),
            in_specs=[pl.BlockSpec((1, rows, sum(cuts)), source(a)) for a in range(4)],
            out_specs=[pl.BlockSpec((rows, wide), target) for wide in cuts],
        ),
        out_shape=[
            jax.ShapeDtypeStruct((rows * along, wide * across), jnp.float32) for wide in cuts
        ],
        compiler_params=pltpu.CompilerParams(vmem_limit_bytes=40 * 1024 * 1024),
    )(here, *pieces)


def contract(left, right, axes):
    return lax.dot_general(
        left, right, ((axes[:1], axes[1:]), ((), ())), preferred_element_type=jnp.float32
    )


def side_sum(links, both):
    got = links.over_x(both(1 - links.side).astype(jnp.bfloat16))
    return (both(links.side) + got.astype(jnp.float32)).astype(jnp.bfloat16)


def wide_grads(links, rows_plane, kinds):
    stacked = jnp.stack(kinds)
    tokens, columns = kinds[0].shape
    mine = pick(stacked, links.core, 0)
    pair = jnp.stack([mine, links.over_core(pick(stacked, 1 - links.core, 0))])
    pair = pair.reshape(2 * tokens, 2, columns // 2)
    kept = pick(pair, links.y, 1)
    got = links.over_y(pick(pair, 1 - links.y, 1))
    terms = jnp.concatenate([kept, got])
    rows = rows_plane.shape[1] // 2

    def both(side):
        return contract(
            lax.dynamic_slice_in_dim(rows_plane, side * rows, rows, 1), terms, (0, 0)
        )

    return links.spread_plane(links.sum_depth(side_sum(links, both)))


def exchange_plane(links, value):
    mine = pick(value, links.core, 0)
    across = links.over_core(pick(value, 1 - links.core, 0))
    pair = jnp.stack([mine, across])
    got = links.over_y(pick(pair, 1 - links.y, 1))
    kept = pick(pair, links.y, 1)
    return (kept[0], kept[1], got[0], got[1])


def on_device(
    tokens,
    qkv_weight,
    out_weight,
    gate_up_weight,
    down_weight,
    attn_gain,
    ffn_gain,
    query_gain,
    key_gain,
    seq_lengths,
    block_order,
    cotangent,
):
    inputs = tokens[0].astype(jnp.float32)
    rows_here = inputs.shape[0]
    ctx_size = lax.axis_size("ctx")
    ctx_index = lax.axis_index("ctx")
    fast = lax.axis_size("fsdp") == 2 and ctx_size == 16
    per_group = HEADS // KV_HEADS
    q_width = HEADS * HD
    kv_width = KV_HEADS * HD
    order_row = block_order[0]
    lengths_row = seq_lengths[0]
    slots = jnp.arange(rows_here, dtype=jnp.int32) // BLK + ctx_index * (rows_here // BLK)
    table = slots[:, None] == jnp.arange(order_row.shape[0], dtype=jnp.int32)[None, :]
    packed = (
        jnp.sum(jnp.where(table, order_row[None, :], 0), axis=1) * BLK
        + jnp.arange(rows_here, dtype=jnp.int32) % BLK
    )
    local = packed - starts_of(packed, lengths_row)
    frequency = ROPE_BASE ** (-2.0 * jnp.arange(HD // 2, dtype=jnp.float32) / HD)
    angle = frequency[:, None] * local.astype(jnp.float32)[None, :]
    cosine = jnp.cos(angle)[None]
    sine = jnp.sin(angle)[None]
    bf16, f32 = jnp.bfloat16, jnp.float32
    parts = ctx_size // HEADS
    part = ctx_index // HEADS
    part_blocks = HEADS * rows_here // BLK
    q_order = lax.dynamic_slice_in_dim(order_row, part * part_blocks, part_blocks)
    q_slot, q_place, q_start = block_tables(q_order, lengths_row)
    q_slot = q_slot + part * part_blocks
    kv_slot, _, _ = block_tables(order_row, lengths_row)
    first = jnp.min(q_start.reshape(-1, TILE), axis=1) // TILE
    last = jnp.max(q_place.reshape(-1, TILE), axis=1) // TILE + 1
    tables = (q_slot, kv_slot, first, last)
    q_rows, kv_rows = part_blocks * BLK, order_row.shape[0] * BLK

    def fetch_attention():
        return (
            lax.all_gather(qkv_weight, "fsdp", axis=0, tiled=True),
            lax.all_gather(out_weight, "fsdp", axis=0, tiled=True),
            lax.all_gather(attn_gain, "fsdp", axis=0, tiled=True),
            lax.all_gather(ffn_gain, "fsdp", axis=0, tiled=True),
            lax.all_gather(query_gain, "fsdp", axis=0, tiled=True),
            lax.all_gather(key_gain, "fsdp", axis=0, tiled=True),
        )

    w_qkv, w_out, gain_attn, gain_ffn, gain_query, gain_key = fetch_attention()
    gain_attn = gain_attn.astype(jnp.float32)
    gain_ffn = gain_ffn.astype(jnp.float32)
    gain_query = gain_query.astype(jnp.float32)
    gain_key = gain_key.astype(jnp.float32)
    scale_one = rms_scale(inputs)
    normed = (inputs * scale_one * gain_attn).astype(jnp.bfloat16)
    projected = lax.dot_general(
        w_qkv, normed, (((0,), (1,)), ((), ())), preferred_element_type=f32
    )
    q_raw = projected[:q_width].reshape(HEADS, HD, rows_here)
    k_raw = projected[q_width : q_width + kv_width].reshape(KV_HEADS, HD, rows_here)
    values_here = projected[q_width + kv_width :].reshape(KV_HEADS, HD, rows_here).astype(bf16)
    q_scale = rms_scale(q_raw, 1)
    k_scale = rms_scale(k_raw, 1)
    column_query, column_key = gain_query[:, None], gain_key[:, None]
    queries = rope(q_raw * q_scale * column_query, cosine, sine).astype(bf16)
    keys_here = rope(k_raw * k_scale * column_key, cosine, sine).astype(bf16)
    sent = jnp.concatenate(
        [queries, jnp.repeat(keys_here, per_group, 0), jnp.repeat(values_here, per_group, 0)], axis=1
    )
    sent = jnp.concatenate([sent] * parts, axis=0)
    got = lax.all_to_all(sent, "ctx", 0, 0, tiled=True)
    q_place, q_start = q_place[None], q_start[None]
    shape = jax.ShapeDtypeStruct
    attn_sent, *held = kernel_call(
        attend_kernel,
        tables,
        (got, q_place, q_start),
        [
            shape((ctx_size, HD, rows_here), bf16),
            shape((q_rows, HD), bf16),
            shape((HD, q_rows), bf16),
            shape((kv_rows, HD), bf16),
            shape((HD, kv_rows), bf16),
            shape((kv_rows, HD), bf16),
            shape((HD, q_rows), f32),
            shape((1, q_rows), f32),
        ],
        [pltpu.VMEM((HD, kv_rows), bf16)],
    )
    attn_in = lax.dynamic_slice_in_dim(
        lax.all_to_all(attn_sent, "ctx", 0, 0, tiled=True), part * HEADS, HEADS
    ).reshape(q_width, rows_here)
    h_one = inputs + lax.dot_general(
        attn_in, w_out, (((0,), (0,)), ((), ())), preferred_element_type=f32
    )
    scale_two = rms_scale(h_one)
    normed_two = (h_one * scale_two * gain_ffn).astype(jnp.bfloat16)
    columns = normed_two
    gate_up = jnp.einsum(
        "tr,rgf->tgf",
        columns,
        lax.all_gather(gate_up_weight, "fsdp", axis=0, tiled=True),
        preferred_element_type=jnp.float32,
    )
    gate = gate_up[:, 0]
    upper = gate_up[:, 1]
    sigma = jax.nn.sigmoid(gate)
    hidden = (gate * sigma * upper).astype(jnp.bfloat16)
    columns = hidden
    ffn_out = jnp.dot(
        columns,
        lax.all_gather(down_weight, "fsdp", axis=0, tiled=True),
        preferred_element_type=jnp.float32,
    )
    output = (h_one + ffn_out).astype(jnp.bfloat16)
    d_out = cotangent[0].astype(jnp.float32)
    d_ffn = d_out.astype(jnp.bfloat16)
    d_hidden = lax.dot_general(
        d_ffn,
        lax.all_gather(down_weight, "fsdp", axis=0, tiled=True),
        (((1,), (1,)), ((), ())),
        preferred_element_type=jnp.float32,
    )
    d_gate = d_hidden * upper * sigma * (1.0 + gate * (1.0 - sigma))
    d_upper = d_hidden * gate * sigma
    d_gate_up = jnp.stack([d_gate, d_upper], axis=1).astype(jnp.bfloat16)
    d_normed_two = jnp.einsum(
        "tgf,rgf->tr",
        d_gate_up,
        lax.all_gather(gate_up_weight, "fsdp", axis=0, tiled=True),
        preferred_element_type=jnp.float32,
    )
    columns = normed_two
    if fast:
        links = Links(ctx_size)
        here = jnp.stack([links.half, links.core, links.y])
        normed_plane = links.gather_plane(normed).reshape(4 * rows_here, -1)
        attn_plane = links.gather_plane(attn_in)
        attn_plane = jnp.concatenate(list(attn_plane), axis=1)
        two_plane = links.gather_plane(normed_two).reshape(4 * rows_here, -1)
        ffn_plane = links.gather_plane(d_ffn).reshape(4 * rows_here, -1)
        ff_width = hidden.shape[1]
        chunk = ff_width // CHUNKS
        gate_up_pieces = [
            wide_grads(
                links, two_plane, [d_gate_up[:, j, i * chunk : (i + 1) * chunk] for j in range(2)]
            )
            for i in range(CHUNKS)
        ]
        grad_gate_up = place_gate_up(here, gate_up_pieces)
        hidden_t = hidden.T.reshape(2, 2, 2, ff_width // 8, rows_here)
        hidden_t = jnp.transpose(hidden_t, (1, 2, 0, 3, 4))
        hidden_plane = jnp.concatenate(exchange_plane(links, hidden_t), axis=-1)
        down_pieces = links.spread_plane(
            links.sum_depth(
                side_sum(
                    links, lambda side: contract(pick(hidden_plane, side, 0), ffn_plane, (1, 0))
                )
            )
        )
        (grad_down,) = place_pieces(here, down_pieces, (d_ffn.shape[1],), True)
    else:
        grad_gate_up = lax.psum_scatter(
            jnp.einsum("tr,tgf->rgf", columns, d_gate_up, preferred_element_type=jnp.float32).astype(
                jnp.bfloat16
            ),
            "fsdp",
            scatter_dimension=0,
            tiled=True,
        )
        columns = hidden
        grad_down = lax.psum_scatter(
            lax.dot_general(
                columns, d_ffn, (((0,), (0,)), ((), ())), preferred_element_type=jnp.float32
            ).astype(jnp.bfloat16),
            "fsdp",
            scatter_dimension=0,
            tiled=True,
        )
    d_norm_two, ffn_gain_term = norm_back(d_normed_two, h_one, scale_two, gain_ffn)
    d_h_one = d_out + d_norm_two
    d_attn = d_h_one.astype(jnp.bfloat16)
    d_heads = lax.dot_general(
        w_out, d_attn, (((1,), (1,)), ((), ())), preferred_element_type=f32
    ).astype(bf16)
    d_heads = jnp.concatenate([d_heads.reshape(HEADS, HD, rows_here)] * parts, axis=0)
    d_got = lax.all_to_all(d_heads, "ctx", 0, 0, tiled=True)
    (d_sent,) = kernel_call(
        attend_back_kernel,
        tables,
        (d_got, q_place, q_start, *held),
        [shape((ctx_size, 3 * HD, rows_here), bf16)],
        [
            pltpu.VMEM((HD, q_rows), bf16),
            pltpu.VMEM((q_rows, HD), bf16),
            pltpu.VMEM((kv_rows, HD), f32),
            pltpu.VMEM((kv_rows, HD), f32),
        ],
    )
    d_back = lax.all_to_all(d_sent, "ctx", 0, 0, tiled=True)
    d_query = lax.dynamic_slice_in_dim(d_back[:, :HD], part * HEADS, HEADS).astype(f32)
    d_key_value = jnp.sum(
        d_back[:, HD:].reshape(parts, KV_HEADS, per_group, 2 * HD, rows_here).astype(f32),
        axis=(0, 2),
    )
    dq_normed = rope_back(d_query, cosine, sine)
    dk_normed = rope_back(d_key_value[:, :HD], cosine, sine)
    dq_raw, query_term = norm_back(dq_normed, q_raw, q_scale, column_query, 1)
    dk_raw, key_term = norm_back(dk_normed, k_raw, k_scale, column_key, 1)
    d_projected = jnp.concatenate(
        [
            dq_raw.reshape(q_width, rows_here).astype(bf16),
            dk_raw.reshape(kv_width, rows_here).astype(bf16),
            d_key_value[:, HD:].reshape(kv_width, rows_here).astype(bf16),
        ],
        axis=0,
    )
    d_normed = lax.dot_general(
        d_projected, w_qkv, (((0,), (1,)), ((), ())), preferred_element_type=f32
    )
    d_norm_one, attn_gain_term = norm_back(d_normed, inputs, scale_one, gain_attn)
    d_inputs = d_h_one + d_norm_one
    gains = jnp.concatenate(
        [
            jnp.sum(attn_gain_term, axis=0),
            jnp.sum(ffn_gain_term, axis=0),
            jnp.sum(query_term, axis=(0, 2)),
            jnp.sum(key_term, axis=(0, 2)),
        ]
    )
    gains = lax.psum(gains, ("ctx", "fsdp"))
    gain_grads = []
    at = 0
    for gain in (attn_gain, ffn_gain, query_gain, key_gain):
        size = gain.shape[0]
        gain_grads.append(
            lax.dynamic_slice_in_dim(gains, at + lax.axis_index("fsdp") * size, size)
        )
        at += size * lax.axis_size("fsdp")
    if fast:
        projected_plane = jnp.concatenate(
            exchange_plane(links, d_projected.reshape(2, 2, -1, rows_here)), axis=1
        )
        attn_columns = jnp.transpose(d_attn.reshape(rows_here, 2, 2, -1), (1, 2, 0, 3))
        out_plane = jnp.concatenate(exchange_plane(links, attn_columns), axis=0)
        rows = normed_plane.shape[1] // 2

        def both(side):
            return jnp.concatenate(
                [
                    contract(
                        lax.dynamic_slice_in_dim(normed_plane, side * rows, rows, 1),
                        projected_plane,
                        (0, 1),
                    ),
                    contract(
                        lax.dynamic_slice_in_dim(attn_plane, side * rows, rows, 0),
                        out_plane,
                        (1, 0),
                    ),
                ],
                axis=1,
            )

        pieces = links.spread_plane(links.sum_depth(side_sum(links, both)))
        grad_qkv, grad_out = place_pieces(
            here, pieces, (projected_plane.shape[0], out_plane.shape[1]), False
        )
    else:
        grad_qkv, grad_out = (
            lax.psum_scatter(grad.astype(bf16), "fsdp", scatter_dimension=0, tiled=True)
            for grad in (contract(normed, d_projected, (0, 1)), jnp.dot(attn_in, d_attn, preferred_element_type=f32))
        )
        grad_qkv, grad_out, grad_gate_up, grad_down = (
            lax.psum(grad, "ctx").astype(f32)
            for grad in (grad_qkv, grad_out, grad_gate_up, grad_down)
        )
    return (
        output[None],
        d_inputs[None],
        grad_qkv,
        grad_out,
        grad_gate_up,
        grad_down,
        *gain_grads,
    )


def solution(mesh):
    return jax.shard_map(
        on_device,
        mesh=mesh,
        in_specs=(
            P("fsdp", "ctx", None),
            P("fsdp", None),
            P("fsdp", None),
            P("fsdp", None, None),
            P("fsdp", None),
            P("fsdp"),
            P("fsdp"),
            P("fsdp"),
            P("fsdp"),
            P("fsdp", None),
            P("fsdp", None),
            P("fsdp", "ctx", None),
        ),
        out_specs=(
            P("fsdp", "ctx", None),
            P("fsdp", "ctx", None),
            P("fsdp", None),
            P("fsdp", None),
            P("fsdp", None, None),
            P("fsdp", None),
            P("fsdp"),
            P("fsdp"),
            P("fsdp"),
            P("fsdp"),
        ),
        check_vma=False,
    )
```

```python
import functools

import jax
import jax.numpy as jnp
from jax import lax
from jax.experimental import pallas as pl
from jax.experimental.pallas import tpu as pltpu
from jax.sharding import PartitionSpec as P

HEADS = 16
KV_HEADS = 8
HD = 64
BLK = 128
TILE = 256
CHUNKS = 2


EPSILON = 1e-05
ROPE_BASE = 1000000.0
LOG2E = 1.4426950408889634
SCORE_SCALE = LOG2E * HD ** (-0.5)


def rms_scale(values, axis=-1):
    return lax.rsqrt(jnp.mean(values * values, axis=axis, keepdims=True) + EPSILON)


def norm_back(grad_normed, inputs, scale, gain, axis=-1):
    scaled = grad_normed * gain
    grad_in = scale * scaled - inputs * scale * scale * scale * jnp.mean(
        scaled * inputs, axis=axis, keepdims=True
    )
    return (grad_in, grad_normed * inputs * scale)


def rope(values, cosine, sine):
    half = HD // 2
    first, second = values[:, :half], values[:, half:]
    return jnp.concatenate([first * cosine - second * sine, second * cosine + first * sine], axis=1)


def rope_back(values, cosine, sine):
    half = HD // 2
    first, second = values[:, :half], values[:, half:]
    return jnp.concatenate([first * cosine + second * sine, second * cosine - first * sine], axis=1)


def starts_of(packed, lengths_row):
    ends = jnp.cumsum(lengths_row)
    past = packed[:, None] >= ends[None, :]
    return jnp.sum(jnp.where(past, lengths_row[None, :], 0), axis=1)


def block_tables(order, lengths_row):
    count = order.shape[0]
    rank = jnp.sum((order[None, :] < order[:, None]).astype(jnp.int32), axis=1)
    hit = rank[None, :] == jnp.arange(count, dtype=jnp.int32)[:, None]
    slot = jnp.sum(jnp.where(hit, jnp.arange(count, dtype=jnp.int32)[None, :], 0), axis=1)
    block = jnp.sum(jnp.where(hit, order[None, :], 0), axis=1)
    place = (block[:, None] * BLK + jnp.arange(BLK, dtype=jnp.int32)[None, :]).reshape(-1)
    return (slot, place, starts_of(place, lengths_row))


def attend_kernel(
    q_slot, kv_slot, first, last, qkv_ref, place_ref, start_ref,
    out_ref, q_ref, qt_ref, k_ref, kt_ref, v_ref, ot_ref, total_ref, vt_ref
):
    per_device = qkv_ref.shape[2] // BLK
    kv_blocks = k_ref.shape[0] // BLK
    q_blocks = q_ref.shape[0] // BLK

    def piece(slot, lower):
        return qkv_ref[
            slot // per_device,
            lower : lower + HD,
            pl.ds(pl.multiple_of((slot % per_device) * BLK, BLK), BLK),
        ]

    for i in range(kv_blocks):
        here = slice(i * BLK, (i + 1) * BLK)
        keys = piece(kv_slot[i], HD)
        kt_ref[:, here] = keys
        k_ref[here, :] = keys.T
        values = piece(kv_slot[i], 2 * HD)
        vt_ref[:, here] = values
        v_ref[here, :] = values.T
    for i in range(q_blocks):
        here = slice(i * BLK, (i + 1) * BLK)
        queries = piece(q_slot[i], 0)
        qt_ref[:, here] = queries
        q_ref[here, :] = queries.T
    if q_blocks < kv_blocks:
        out_ref[...] = jnp.zeros_like(out_ref)

    def tile(i, carry):
        rows = pl.ds(pl.multiple_of(i * TILE, TILE), TILE)
        queries = qt_ref[:, rows]
        place = place_ref[:, rows]
        start = start_ref[:, rows]

        def step(j, state):
            total, summed = state
            at = pl.multiple_of(j * TILE, TILE)
            scores = jnp.dot(
                k_ref[pl.ds(at, TILE), :], queries, preferred_element_type=jnp.float32
            )
            key_place = lax.broadcasted_iota(jnp.int32, (TILE, TILE), 0) + at
            allowed = (key_place <= place) & (key_place >= start)
            lifted = jnp.where(allowed, jnp.exp2(scores * SCORE_SCALE), 0.0)
            total = total + jnp.sum(lifted, axis=0, keepdims=True)
            summed = summed + jnp.dot(
                vt_ref[:, pl.ds(at, TILE)],
                lifted.astype(jnp.bfloat16),
                preferred_element_type=jnp.float32,
            )
            return (total, summed)

        total, summed = lax.fori_loop(
            first[i],
            last[i],
            step,
            (jnp.zeros((1, TILE), jnp.float32), jnp.zeros((HD, TILE), jnp.float32)),
        )
        attn = summed / total
        ot_ref[:, rows] = attn
        total_ref[:, rows] = jnp.log(total) * LOG2E
        rounded = attn.astype(jnp.bfloat16)
        for part in range(TILE // BLK):
            slot = q_slot[i * (TILE // BLK) + part]
            out_ref[
                slot // per_device,
                :,
                pl.ds(pl.multiple_of((slot % per_device) * BLK, BLK), BLK),
            ] = rounded[:, part * BLK : (part + 1) * BLK]
        return carry

    lax.fori_loop(0, q_blocks * BLK // TILE, tile, 0)


def attend_back_kernel(
    q_slot, kv_slot, first, last, d_ref, place_ref, start_ref,
    q_ref, qt_ref, k_ref, kt_ref, v_ref, ot_ref, total_ref,
    out_ref, dt_ref, do_ref, dk_ref, dv_ref
):
    per_device = d_ref.shape[2] // BLK
    kv_blocks = k_ref.shape[0] // BLK
    q_blocks = q_ref.shape[0] // BLK

    def lanes(slot):
        return pl.ds(pl.multiple_of((slot % per_device) * BLK, BLK), BLK)

    for i in range(q_blocks):
        here = slice(i * BLK, (i + 1) * BLK)
        slot = q_slot[i]
        grads = d_ref[slot // per_device, :, lanes(slot)]
        dt_ref[:, here] = grads
        do_ref[here, :] = grads.T
    dk_ref[...] = jnp.zeros_like(dk_ref)
    dv_ref[...] = jnp.zeros_like(dv_ref)
    if q_blocks < kv_blocks:
        out_ref[...] = jnp.zeros_like(out_ref)

    def tile(i, carry):
        rows = pl.ds(pl.multiple_of(i * TILE, TILE), TILE)
        queries = qt_ref[:, rows]
        grads = dt_ref[:, rows]
        place = place_ref[:, rows]
        start = start_ref[:, rows]
        delta = jnp.sum(grads.astype(jnp.float32) * ot_ref[:, rows], axis=0, keepdims=True)
        total = total_ref[:, rows]

        def step(j, d_query):
            at = pl.multiple_of(j * TILE, TILE)
            here = pl.ds(at, TILE)
            scores = jnp.dot(k_ref[here, :], queries, preferred_element_type=jnp.float32)
            key_place = lax.broadcasted_iota(jnp.int32, (TILE, TILE), 0) + at
            allowed = (key_place <= place) & (key_place >= start)
            shares = jnp.where(allowed, jnp.exp2(scores * SCORE_SCALE - total), 0.0)
            d_shares = jnp.dot(v_ref[here, :], grads, preferred_element_type=jnp.float32)
            d_scores = (shares * (d_shares - delta)).astype(jnp.bfloat16)
            dv_ref[here, :] += jnp.dot(
                shares.astype(jnp.bfloat16), do_ref[rows, :], preferred_element_type=jnp.float32
            )
            dk_ref[here, :] += jnp.dot(
                d_scores, q_ref[rows, :], preferred_element_type=jnp.float32
            )
            return d_query + jnp.dot(
                kt_ref[:, here], d_scores, preferred_element_type=jnp.float32
            )

        d_query = lax.fori_loop(first[i], last[i], step, jnp.zeros((HD, TILE), jnp.float32))
        rounded = (d_query * HD ** (-0.5)).astype(jnp.bfloat16)
        for part in range(TILE // BLK):
            slot = q_slot[i * (TILE // BLK) + part]
            out_ref[slot // per_device, 0:HD, lanes(slot)] = rounded[
                :, part * BLK : (part + 1) * BLK
            ]
        return carry

    lax.fori_loop(0, q_blocks * BLK // TILE, tile, 0)
    for i in range(kv_blocks):
        here = slice(i * BLK, (i + 1) * BLK)
        slot = kv_slot[i]
        out_ref[slot // per_device, HD : 2 * HD, lanes(slot)] = (
            (dk_ref[here, :] * HD ** (-0.5)).T.astype(jnp.bfloat16)
        )
        out_ref[slot // per_device, 2 * HD : 3 * HD, lanes(slot)] = (
            dv_ref[here, :].T.astype(jnp.bfloat16)
        )


def kernel_call(kernel, tables, arrays, outs, scratch):
    smem = pl.BlockSpec(memory_space=pltpu.SMEM)
    vmem = pl.BlockSpec(memory_space=pltpu.VMEM)
    return pl.pallas_call(
        kernel,
        out_shape=outs,
        in_specs=[smem] * len(tables) + [vmem] * len(arrays),
        out_specs=[vmem] * len(outs),
        scratch_shapes=scratch,
        compiler_params=pltpu.CompilerParams(vmem_limit_bytes=48 * 1024 * 1024),
    )(*tables, *arrays)


class Links:
    def __init__(self, ctx_size):
        self.depth = ctx_size // 4
        index = lax.axis_index("ctx")
        self.core = index % 2
        self.y = (index // 2) % 2
        self.side = lax.axis_index("fsdp")
        self.half = ((index // 4 + 1) // 2) % 2
        self.quarter = index % 2 * 2 + self.y
        self.here = jnp.stack([self.half, self.core, self.y, self.side]).astype(jnp.int32)

    def route(self, place):
        pairs = []
        for z in range(self.depth):
            for y in range(2):
                for core in range(2):
                    to_z, to_y, to_core = place(z, y, core)
                    pairs.append(((z * 2 + y) * 2 + core, (to_z * 2 + to_y) * 2 + to_core))
        return pairs

    def over_core(self, value):
        return lax.ppermute(value, "ctx", self.route(lambda z, y, c: (z, y, 1 - c)))

    def over_y(self, value):
        return lax.ppermute(value, "ctx", self.route(lambda z, y, c: (z, 1 - y, c)))

    def over_z(self, value):
        return lax.ppermute(value, "ctx", self.route(lambda z, y, c: (z ^ 1, y, c)))

    def mirror_z(self, value):
        return lax.ppermute(value, "ctx", self.route(lambda z, y, c: (self.depth - 1 - z, y, c)))

    def over_x(self, value):
        return lax.ppermute(value, "fsdp", [(0, 1), (1, 0)])

    def spread_plane(self, value):
        across = self.over_core(value)
        beside = self.over_y(value)
        return (value, across, beside, self.over_core(beside))

    def deal_plane(self, keep, keep_far, give, give_far):
        got, got_far = self.over_core(give), self.over_core(give_far)
        return (keep, got, self.over_y(keep_far), self.over_y(got_far))

    def sum_depth(self, kept, got):
        rows = kept.shape[0] // 2

        def half(index):
            return add(
                lax.dynamic_slice_in_dim(kept, index * rows, rows),
                lax.dynamic_slice_in_dim(got, index * rows, rows),
            )

        given = self.over_z(half(1 - self.half))
        part = add(half(self.half), given)
        full = add(part, self.mirror_z(part))
        return (full, self.over_z(full))

    def reduce(self, sent, kept):
        return [self.spread_plane(v) for v in self.sum_depth(kept, self.over_x(sent))]

    def total(self, value):
        for swap in (self.over_core, self.over_y, self.over_x, self.over_z, self.mirror_z):
            value = value + swap(value)
        return value


def pick(value, index, axis):
    return lax.dynamic_index_in_dim(value, index, axis, keepdims=False)


def add(left, right):
    return (left.astype(jnp.float32) + right.astype(jnp.float32)).astype(jnp.bfloat16)


def after(value, *others):
    return lax.optimization_barrier((value, *others))[0]


def contract(left, right, axes):
    return lax.dot_general(
        left, right, ((axes[:1], axes[1:]), ((), ())), preferred_element_type=jnp.float32
    )


PARAMS = pltpu.CompilerParams(vmem_limit_bytes=56 * 1024 * 1024)


def call_with_here(kernel, here, grid, arrays, specs, outs, out_specs, scratch=(), aliases=None):
    return pl.pallas_call(
        kernel,
        grid_spec=pltpu.PrefetchScalarGridSpec(
            num_scalar_prefetch=1,
            grid=grid,
            in_specs=specs,
            out_specs=out_specs,
            scratch_shapes=list(scratch),
        ),
        out_shape=outs,
        input_output_aliases=aliases or {},
        compiler_params=PARAMS,
    )(here, *arrays)


def whole(array):
    rank = len(array.shape)
    return pl.BlockSpec(array.shape, lambda i, here: (0,) * rank)


def place_rows(here, own, pieces):
    rows, columns = own.shape
    part = rows // 4

    def kernel(here, own_ref, *refs):
        out_ref = refs[-1]
        s = pl.program_id(0)

        @pl.when(s < 4)
        def _():
            out_ref[...] = own_ref[...]

        for p in range(4):

            @pl.when(s == 4 + p)
            def _(p=p):
                out_ref[...] = refs[p][...]

    def target(s, here):
        p = s - 4
        other = (1 - here[3]) * 4 + ((p % 2) ^ here[1]) * 2 + ((p // 2) ^ here[2])
        return (jnp.where(s < 4, here[3] * 4 + s, other), 0)

    (out,) = call_with_here(
        kernel,
        here,
        (8,),
        [own, *pieces],
        [pl.BlockSpec((part, columns), lambda s, here: (jnp.minimum(s, 3), 0))]
        + [whole(p) for p in pieces],
        [jax.ShapeDtypeStruct((2 * rows, columns), own.dtype)],
        [pl.BlockSpec((part, columns), target)],
    )
    return out


def ffn_kernel(chunk, here, *refs):
    two_ref, d_ref, own_ref = refs[:3]
    gate_pieces, down_ref, down_pieces = refs[3:7], refs[7], refs[8:12]
    before_out, before_two = refs[12:14]
    keep, give, hidden_keep, hidden_give = refs[14:16], refs[16:18], refs[18:20], refs[20:22]
    out_ref, d_two_ref = refs[22:24]
    weight, down, hidden_t = refs[24:27]
    core, y, side = here[1], here[2], here[3]
    t = pl.program_id(0)
    f32, bf16 = jnp.float32, jnp.bfloat16
    own_rows = own_ref.shape[1]
    part = own_rows // 4

    @pl.when(t == 0)
    def _():
        out_ref[...] = before_out[...]
        d_two_ref[...] = before_two[...]

    def quarter(p):
        return ((p % 2) ^ core) * 2 + ((p // 2) ^ y)

    weight[:, pl.ds(pl.multiple_of(side * own_rows, own_rows), own_rows), :] = own_ref[...]
    for p in range(4):
        at = pl.multiple_of((1 - side) * own_rows + quarter(p) * part, part)
        weight[:, pl.ds(at, part), :] = gate_pieces[p][...]

    @pl.when(side == chunk)
    def _():
        down[...] = down_ref[...]

    @pl.when(side != chunk)
    def _():
        for p in range(4):
            wide = down_pieces[p].shape[1]
            at = pl.multiple_of(quarter(p) * wide, wide)
            down[:, pl.ds(at, wide)] = down_pieces[p][...]

    two = two_ref[...]
    d_ffn = d_ref[...]
    tile = own_ref.shape[2]
    first = (tile // 2) // 256 * 256
    for begin, end in ((0, first), (first, tile)):
        at = slice(begin, end)
        gate = jnp.dot(two, weight[0, :, at], preferred_element_type=f32)
        upper = jnp.dot(two, weight[1, :, at], preferred_element_type=f32)
        d_hidden = contract(d_ffn, down[at, :], (1, 1))
        sigma = jax.nn.sigmoid(gate)
        silu = gate * sigma
        hidden = (silu * upper).astype(bf16)
        d_gate = (d_hidden * upper * sigma * (1.0 + gate * (1.0 - sigma))).astype(bf16)
        d_upper = (d_hidden * silu).astype(bf16)
        out_ref[...] += jnp.dot(hidden, down[at, :], preferred_element_type=f32)
        d_two_ref[...] += contract(d_gate, weight[0, :, at], (1, 1)) + contract(
            d_upper, weight[1, :, at], (1, 1)
        )
        hidden_t[at, :] = hidden.T
        mine = jnp.where(core == 0, d_gate, d_upper)
        other = jnp.where(core == 0, d_upper, d_gate)
        for far in range(2):

            @pl.when((t == y) == (far == 0))
            def _(far=far):
                keep[far][:, at] = mine
                give[far][:, at] = other

    share = tile // 2
    for far in range(2):
        at = pl.multiple_of((y ^ far) * share, share)

        @pl.when(t == core)
        def _(far=far, at=at):
            hidden_keep[far][...] = hidden_t[pl.ds(at, share), :]

        @pl.when(t != core)
        def _(far=far, at=at):
            hidden_give[far][...] = hidden_t[pl.ds(at, share), :]


def ffn(here, chunk, two, d_ffn, own, pieces, down, down_pieces, before):
    tokens, width = two.shape
    tile = own.shape[2] // 4
    share = tile // 2
    shape = jax.ShapeDtypeStruct
    f32, bf16 = jnp.float32, jnp.bfloat16
    outs = (
        [shape((tokens, tile), bf16)] * 4
        + [shape((share, tokens), bf16)] * 4
        + [shape((tokens, width), f32)] * 2
    )

    def own_down(t, here):
        return (jnp.where(here[3] == chunk, t, 0), 0)

    def other_down(t, here):
        return (jnp.where(here[3] == chunk, 0, t), 0)

    specs = (
        [whole(two), whole(d_ffn)]
        + [pl.BlockSpec((2, own.shape[1], tile), lambda t, here: (0, 0, 2 * chunk + t))]
        + [pl.BlockSpec((2, own.shape[1] // 4, tile), lambda t, here: (0, 0, t))] * 4
        + [pl.BlockSpec((tile, width), own_down)]
        + [pl.BlockSpec((tile, width // 4), other_down)] * 4
        + [whole(before[0]), whole(before[1])]
    )
    got = call_with_here(
        functools.partial(ffn_kernel, chunk),
        here,
        (2,),
        [two, d_ffn, own, *pieces, down, *down_pieces, *before],
        specs,
        outs,
        [whole(o) for o in outs],
        [
            pltpu.VMEM((2, width, tile), bf16),
            pltpu.VMEM((tile, width), bf16),
            pltpu.VMEM((tile, tokens), bf16),
        ],
    )
    return got[:4], got[4:8], got[8:]


def wide_product_kernel(here, *refs):
    planes, terms = refs[:4], refs[4:8]
    sent, kept, left, right = refs[8:]
    tokens = planes[0].shape[0]
    for i in range(4):
        left[:, i * tokens : (i + 1) * tokens] = planes[i][...].T
        right[i * tokens : (i + 1) * tokens, :] = terms[i][...]
    side = here[3]
    rows = kept.shape[0]
    step = 256
    for at in range(0, rows, step):
        for owner, out_ref in ((1 - side, sent), (side, kept)):
            place = pl.multiple_of(owner * rows + at, step)
            out_ref[at : at + step, :] = jnp.dot(
                left[pl.ds(place, step), :], right[...], preferred_element_type=jnp.float32
            ).astype(out_ref.dtype)


def wide_products(here, planes, terms):
    tokens, rows = planes[0].shape
    columns = terms[0].shape[1]
    outs = [
        jax.ShapeDtypeStruct((rows // 2, columns), jnp.bfloat16),
        jax.ShapeDtypeStruct((rows // 2, columns), jnp.float32),
    ]
    arrays = [*planes, *terms]
    return call_with_here(
        wide_product_kernel,
        here,
        (1,),
        arrays,
        [whole(a) for a in arrays],
        outs,
        [whole(o) for o in outs],
        [
            pltpu.VMEM((rows, 4 * tokens), jnp.bfloat16),
            pltpu.VMEM((4 * tokens, columns), jnp.bfloat16),
        ],
    )


def down_product_kernel(here, *refs):
    planes, terms = refs[:4], (refs[4:8], refs[8:12])
    sent, kept, left, right = refs[12:]
    tokens = planes[0].shape[0]
    for i in range(4):
        right[i * tokens : (i + 1) * tokens, :] = planes[i][...]
    for chunk in range(2):
        for i in range(4):
            left[:, i * tokens : (i + 1) * tokens] = terms[chunk][i][...]
        product = jnp.dot(left[...], right[...], preferred_element_type=jnp.float32)

        @pl.when(here[3] == chunk)
        def _(product=product):
            kept[...] = product

        @pl.when(here[3] != chunk)
        def _(product=product):
            sent[...] = product.astype(sent.dtype)


def down_products(here, planes, first, second):
    tokens, columns = planes[0].shape
    rows = first[0].shape[0]
    outs = [
        jax.ShapeDtypeStruct((rows, columns), jnp.bfloat16),
        jax.ShapeDtypeStruct((rows, columns), jnp.float32),
    ]
    arrays = [*planes, *first, *second]
    return call_with_here(
        down_product_kernel,
        here,
        (1,),
        arrays,
        [whole(a) for a in arrays],
        outs,
        [whole(o) for o in outs],
        [
            pltpu.VMEM((rows, 4 * tokens), jnp.bfloat16),
            pltpu.VMEM((4 * tokens, columns), jnp.bfloat16),
        ],
    )


def attention_product_kernel(here, *refs):
    normed, projected, attn, d_attn = refs[:4], refs[4:8], refs[8:12], refs[12:16]
    sent, kept, left, right, left_out, right_out = refs[16:]
    tokens = normed[0].shape[0]
    for i in range(4):
        at = slice(i * tokens, (i + 1) * tokens)
        left[:, at] = normed[i][...].T
        right[at, :] = projected[i][...].T
        left_out[:, at] = attn[i][...]
        right_out[at, :] = d_attn[i][...]
    rows = kept.shape[0]
    cut = right.shape[1]
    for owner, out_ref in ((1 - here[3], sent), (here[3], kept)):
        at = pl.ds(pl.multiple_of(owner * rows, rows), rows)
        out_ref[:, :cut] = jnp.dot(
            left[at, :], right[...], preferred_element_type=jnp.float32
        ).astype(out_ref.dtype)
        out_ref[:, cut:] = jnp.dot(
            left_out[at, :], right_out[...], preferred_element_type=jnp.float32
        ).astype(out_ref.dtype)


def attention_products(here, normed, projected, attn, d_attn):
    tokens, rows = normed[0].shape
    cut, rest = projected[0].shape[0], d_attn[0].shape[1]
    outs = [
        jax.ShapeDtypeStruct((rows // 2, cut + rest), jnp.bfloat16),
        jax.ShapeDtypeStruct((rows // 2, cut + rest), jnp.float32),
    ]
    arrays = [*normed, *projected, *attn, *d_attn]
    return call_with_here(
        attention_product_kernel,
        here,
        (1,),
        arrays,
        [whole(a) for a in arrays],
        outs,
        [whole(o) for o in outs],
        [
            pltpu.VMEM((rows, 4 * tokens), jnp.bfloat16),
            pltpu.VMEM((4 * tokens, cut), jnp.bfloat16),
            pltpu.VMEM((rows, 4 * tokens), jnp.bfloat16),
            pltpu.VMEM((4 * tokens, rest), jnp.bfloat16),
        ],
    )


def place_gate_up_kernel(blocks, here, *refs):
    out_ref = refs[-1]
    pieces = refs[:8]
    wide = pieces[0].shape[1]
    far_half = (pl.program_id(0) // blocks) ^ here[0]
    for case in range(8):
        half, core, y = case // 4, case // 2 % 2, case % 2

        @pl.when((far_half == half) & (here[1] == core) & (here[2] == y))
        def _(half=half, core=core, y=y):
            for kind in range(2):
                for column in range(2):
                    value = pieces[half * 4 + (y ^ column) * 2 + (core ^ kind)][...]
                    out_ref[:, kind, column * wide : (column + 1) * wide] = value.astype(
                        jnp.float32
                    )


def place_gate_up(here, chunk, pieces, before):
    rows, wide = pieces[0][0].shape
    step = 64
    blocks = rows // step

    def source(half):
        return lambda i, here: (jnp.clip(i - blocks * (here[0] ^ half), 0, blocks - 1), 0)

    arrays = [v for plane in pieces for v in plane]
    specs = [pl.BlockSpec((step, wide), source(n // 4)) for n in range(8)]
    aliases = {}
    if before is not None:
        arrays.append(before)
        specs.append(pl.BlockSpec(memory_space=pl.ANY))
        aliases = {9: 0}
    (out,) = call_with_here(
        functools.partial(place_gate_up_kernel, blocks),
        here,
        (2 * blocks,),
        arrays,
        specs,
        [jax.ShapeDtypeStruct((2 * rows, 2, 2 * wide * CHUNKS), jnp.float32)],
        [pl.BlockSpec((step, 2, 2 * wide), lambda i, here: (i, 0, chunk))],
        aliases=aliases,
    )
    return out


def place_pieces(here, pieces, cuts, by_rows):
    rows = pieces[0][0].shape[0]
    flat = [v for plane in pieces for v in plane]

    def kernel(here, *refs):
        for s in range(8):

            @pl.when(pl.program_id(0) == s)
            def _(s=s):
                at = 0
                for out_ref in refs[8:]:
                    wide = out_ref.shape[1]
                    out_ref[...] = refs[s][:, at : at + wide].astype(jnp.float32)
                    at += wide

    def target(s, here):
        half = (s // 4) ^ here[0]
        y = ((s // 2) % 2) ^ here[2]
        core = (s % 2) ^ here[1]
        if by_rows:
            return ((core * 2 + y) * 2 + half, 0)
        return (half, core * 2 + y)

    across, along = (1, 8) if by_rows else (4, 2)
    return call_with_here(
        kernel,
        here,
        (8,),
        flat,
        [whole(v) for v in flat],
        [jax.ShapeDtypeStruct((rows * along, wide * across), jnp.float32) for wide in cuts],
        [pl.BlockSpec((rows, wide), target) for wide in cuts],
    )


def on_block(
    tokens,
    qkv_weight,
    out_weight,
    gate_up_weight,
    down_weight,
    attn_gain,
    ffn_gain,
    query_gain,
    key_gain,
    seq_lengths,
    block_order,
    cotangent,
):
    inputs = tokens[0].astype(jnp.float32)
    rows_here = inputs.shape[0]
    ctx_size = lax.axis_size("ctx")
    ctx_index = lax.axis_index("ctx")
    per_group = HEADS // KV_HEADS
    q_width = HEADS * HD
    kv_width = KV_HEADS * HD
    order_row = block_order[0]
    lengths_row = seq_lengths[0]
    slots = jnp.arange(rows_here, dtype=jnp.int32) // BLK + ctx_index * (rows_here // BLK)
    table = slots[:, None] == jnp.arange(order_row.shape[0], dtype=jnp.int32)[None, :]
    packed = (
        jnp.sum(jnp.where(table, order_row[None, :], 0), axis=1) * BLK
        + jnp.arange(rows_here, dtype=jnp.int32) % BLK
    )
    local = packed - starts_of(packed, lengths_row)
    frequency = ROPE_BASE ** (-2.0 * jnp.arange(HD // 2, dtype=jnp.float32) / HD)
    angle = frequency[:, None] * local.astype(jnp.float32)[None, :]
    cosine = jnp.cos(angle)[None]
    sine = jnp.sin(angle)[None]
    bf16, f32 = jnp.bfloat16, jnp.float32
    parts = ctx_size // HEADS
    part = ctx_index // HEADS
    part_blocks = HEADS * rows_here // BLK
    q_order = lax.dynamic_slice_in_dim(order_row, part * part_blocks, part_blocks)
    q_slot, q_place, q_start = block_tables(q_order, lengths_row)
    q_slot = q_slot + part * part_blocks
    kv_slot, _, _ = block_tables(order_row, lengths_row)
    first = jnp.min(q_start.reshape(-1, TILE), axis=1) // TILE
    last = jnp.max(q_place.reshape(-1, TILE), axis=1) // TILE + 1
    tables = (q_slot, kv_slot, first, last)
    q_rows, kv_rows = part_blocks * BLK, order_row.shape[0] * BLK

    links = Links(ctx_size)
    here = links.here
    width = inputs.shape[1]
    rows = qkv_weight.shape[0]
    part_rows = rows // 4

    def quarter_rows(weight):
        return lax.dynamic_slice_in_dim(weight, links.quarter * part_rows, part_rows)

    gains_here = jnp.concatenate([attn_gain, ffn_gain, query_gain, key_gain])
    gains_there = links.over_x(gains_here)

    def gain_of(at, size):
        mine, other = gains_here[at : at + size], gains_there[at : at + size]
        return jnp.where(
            links.side == 0, jnp.concatenate([mine, other]), jnp.concatenate([other, mine])
        ).astype(f32)

    gain_attn = gain_of(0, rows)
    gain_ffn = gain_of(rows, rows)
    gain_query = gain_of(2 * rows, HD // 2)
    gain_key = gain_of(2 * rows + HD // 2, HD // 2)
    qkv_there = links.over_x(quarter_rows(qkv_weight))
    qkv_pieces = links.spread_plane(qkv_there)
    gate_up = jnp.transpose(gate_up_weight, (1, 0, 2))
    ff_chunk = gate_up.shape[2] // CHUNKS
    out_there = links.over_x(after(quarter_rows(out_weight), qkv_there))

    def gate_up_piece(chunk):
        return lax.dynamic_slice(
            gate_up, (0, links.quarter * part_rows, chunk * ff_chunk), (2, part_rows, ff_chunk)
        )

    first_there = links.over_x(after(gate_up_piece(0), qkv_there))
    down_there = links.over_x(
        after(
            lax.dynamic_slice_in_dim(down_weight, links.quarter * (width // 4), width // 4, 1),
            out_there,
        )
    )
    second_there = links.over_x(after(gate_up_piece(1), first_there))
    out_pieces = links.spread_plane(out_there)
    gate_up_pieces = [links.spread_plane(first_there), links.spread_plane(second_there)]
    down_pieces = links.spread_plane(down_there)
    w_out = place_rows(here, out_weight, out_pieces)
    scale_one = rms_scale(inputs)
    normed = (inputs * scale_one * gain_attn).astype(jnp.bfloat16)
    w_qkv = place_rows(here, qkv_weight, qkv_pieces)
    projected = lax.dot_general(
        w_qkv, normed, (((0,), (1,)), ((), ())), preferred_element_type=f32
    )
    q_raw = projected[:q_width].reshape(HEADS, HD, rows_here)
    k_raw = projected[q_width : q_width + kv_width].reshape(KV_HEADS, HD, rows_here)
    values_here = projected[q_width + kv_width :].reshape(KV_HEADS, HD, rows_here).astype(bf16)
    q_scale = rms_scale(q_raw, 1)
    k_scale = rms_scale(k_raw, 1)
    column_query, column_key = gain_query[:, None], gain_key[:, None]
    queries = rope(q_raw * q_scale * column_query, cosine, sine).astype(bf16)
    keys_here = rope(k_raw * k_scale * column_key, cosine, sine).astype(bf16)
    sent = jnp.concatenate(
        [queries, jnp.repeat(keys_here, per_group, 0), jnp.repeat(values_here, per_group, 0)], axis=1
    )
    sent = jnp.concatenate([sent] * parts, axis=0)
    got = lax.all_to_all(sent, "ctx", 0, 0, tiled=True)
    q_place, q_start = q_place[None], q_start[None]
    shape = jax.ShapeDtypeStruct
    attn_sent, *held = kernel_call(
        attend_kernel,
        tables,
        (got, q_place, q_start),
        [
            shape((ctx_size, HD, rows_here), bf16),
            shape((q_rows, HD), bf16),
            shape((HD, q_rows), bf16),
            shape((kv_rows, HD), bf16),
            shape((HD, kv_rows), bf16),
            shape((kv_rows, HD), bf16),
            shape((HD, q_rows), f32),
            shape((1, q_rows), f32),
        ],
        [pltpu.VMEM((HD, kv_rows), bf16)],
    )
    attn_in = lax.dynamic_slice_in_dim(
        lax.all_to_all(attn_sent, "ctx", 0, 0, tiled=True), part * HEADS, HEADS
    ).reshape(q_width, rows_here)
    normed_plane = links.spread_plane(after(normed, got))
    d_ffn = cotangent[0]
    ffn_plane = links.spread_plane(after(d_ffn, got))
    attn_plane = links.spread_plane(attn_in)
    h_one = inputs + contract(attn_in, w_out, (0, 0))
    scale_two = rms_scale(h_one)
    normed_two = (h_one * scale_two * gain_ffn).astype(bf16)
    two_plane = links.spread_plane(normed_two)
    sums = [h_one, jnp.zeros_like(h_one)]
    products, hidden_plane = [], []
    for chunk in range(CHUNKS):
        d_wide, hidden, sums = ffn(
            here, chunk, normed_two, d_ffn, gate_up, gate_up_pieces[chunk],
            down_weight, down_pieces, sums,
        )
        products.append(wide_products(here, two_plane, links.deal_plane(*d_wide)))
        hidden_plane.append(links.deal_plane(*hidden))
    output = sums[0].astype(bf16)
    d_norm_two, ffn_gain_term = norm_back(sums[1], h_one, scale_two, gain_ffn)
    d_h_one = d_ffn.astype(f32) + d_norm_two
    d_attn = d_h_one.astype(bf16)
    d_heads = lax.dot_general(
        w_out, d_attn, (((1,), (1,)), ((), ())), preferred_element_type=f32
    ).astype(bf16)
    d_heads = jnp.concatenate([d_heads.reshape(HEADS, HD, rows_here)] * parts, axis=0)
    d_got = lax.all_to_all(d_heads, "ctx", 0, 0, tiled=True)
    (d_sent,) = kernel_call(
        attend_back_kernel,
        tables,
        (d_got, q_place, q_start, *held),
        [shape((ctx_size, 3 * HD, rows_here), bf16)],
        [
            pltpu.VMEM((HD, q_rows), bf16),
            pltpu.VMEM((q_rows, HD), bf16),
            pltpu.VMEM((kv_rows, HD), f32),
            pltpu.VMEM((kv_rows, HD), f32),
        ],
    )
    d_back = lax.all_to_all(d_sent, "ctx", 0, 0, tiled=True)
    d_query = lax.dynamic_slice_in_dim(d_back[:, :HD], part * HEADS, HEADS).astype(f32)
    d_key_value = jnp.sum(
        d_back[:, HD:].reshape(parts, KV_HEADS, per_group, 2 * HD, rows_here).astype(f32),
        axis=(0, 2),
    )
    dq_normed = rope_back(d_query, cosine, sine)
    dk_normed = rope_back(d_key_value[:, :HD], cosine, sine)
    dq_raw, query_term = norm_back(dq_normed, q_raw, q_scale, column_query, 1)
    dk_raw, key_term = norm_back(dk_normed, k_raw, k_scale, column_key, 1)
    d_projected = jnp.concatenate(
        [
            dq_raw.reshape(q_width, rows_here).astype(bf16),
            dk_raw.reshape(kv_width, rows_here).astype(bf16),
            d_key_value[:, HD:].reshape(kv_width, rows_here).astype(bf16),
        ],
        axis=0,
    )
    d_normed = contract(d_projected, w_qkv, (0, 1))
    d_norm_one, attn_gain_term = norm_back(d_normed, inputs, scale_one, gain_attn)
    d_inputs = d_h_one + d_norm_one
    grad_gate_up = None
    for chunk in range(CHUNKS):
        grad_gate_up = place_gate_up(here, chunk, links.reduce(*products[chunk]), grad_gate_up)
    (grad_down,) = place_pieces(
        here, links.reduce(*down_products(here, ffn_plane, *hidden_plane)), (width,), True
    )

    def deal(value, size, axis):
        def share(core, y):
            return lax.dynamic_slice_in_dim(value, (core * 2 + y) * size, size, axis)

        return links.deal_plane(
            share(links.core, links.y),
            share(links.core, 1 - links.y),
            share(1 - links.core, links.y),
            share(1 - links.core, 1 - links.y),
        )

    attention_terms = attention_products(
        here,
        normed_plane,
        deal(d_projected, d_projected.shape[0] // 4, 0),
        attn_plane,
        deal(d_attn, width // 4, 1),
    )
    grad_qkv, grad_out = place_pieces(
        here, links.reduce(*attention_terms), (d_projected.shape[0] // 4, width // 4), False
    )
    gain_terms = jnp.concatenate(
        [
            jnp.sum(attn_gain_term, axis=0),
            jnp.sum(ffn_gain_term, axis=0),
            jnp.sum(query_term, axis=(0, 2)),
            jnp.sum(key_term, axis=(0, 2)),
        ]
    )
    gain_sums = links.total(gain_terms.reshape(-1, 128)).reshape(-1)
    gain_grads = []
    at = 0
    for gain in (attn_gain, ffn_gain, query_gain, key_gain):
        size = gain.shape[0]
        gain_grads.append(lax.dynamic_slice_in_dim(gain_sums, at + links.side * size, size))
        at += 2 * size
    return (
        output[None],
        d_inputs[None],
        grad_qkv,
        grad_out,
        grad_gate_up,
        grad_down,
        *gain_grads,
    )


def on_device(
    tokens,
    qkv_weight,
    out_weight,
    gate_up_weight,
    down_weight,
    attn_gain,
    ffn_gain,
    query_gain,
    key_gain,
    seq_lengths,
    block_order,
    cotangent,
):
    inputs = tokens[0].astype(jnp.float32)
    rows_here = inputs.shape[0]
    ctx_size = lax.axis_size("ctx")
    ctx_index = lax.axis_index("ctx")
    per_group = HEADS // KV_HEADS
    q_width = HEADS * HD
    kv_width = KV_HEADS * HD
    order_row = block_order[0]
    lengths_row = seq_lengths[0]
    slots = jnp.arange(rows_here, dtype=jnp.int32) // BLK + ctx_index * (rows_here // BLK)
    table = slots[:, None] == jnp.arange(order_row.shape[0], dtype=jnp.int32)[None, :]
    packed = (
        jnp.sum(jnp.where(table, order_row[None, :], 0), axis=1) * BLK
        + jnp.arange(rows_here, dtype=jnp.int32) % BLK
    )
    local = packed - starts_of(packed, lengths_row)
    frequency = ROPE_BASE ** (-2.0 * jnp.arange(HD // 2, dtype=jnp.float32) / HD)
    angle = frequency[:, None] * local.astype(jnp.float32)[None, :]
    cosine = jnp.cos(angle)[None]
    sine = jnp.sin(angle)[None]
    bf16, f32 = jnp.bfloat16, jnp.float32
    parts = ctx_size // HEADS
    part = ctx_index // HEADS
    part_blocks = HEADS * rows_here // BLK
    q_order = lax.dynamic_slice_in_dim(order_row, part * part_blocks, part_blocks)
    q_slot, q_place, q_start = block_tables(q_order, lengths_row)
    q_slot = q_slot + part * part_blocks
    kv_slot, _, _ = block_tables(order_row, lengths_row)
    first = jnp.min(q_start.reshape(-1, TILE), axis=1) // TILE
    last = jnp.max(q_place.reshape(-1, TILE), axis=1) // TILE + 1
    tables = (q_slot, kv_slot, first, last)
    q_rows, kv_rows = part_blocks * BLK, order_row.shape[0] * BLK

    def fetch_attention():
        return (
            lax.all_gather(qkv_weight, "fsdp", axis=0, tiled=True),
            lax.all_gather(out_weight, "fsdp", axis=0, tiled=True),
            lax.all_gather(attn_gain, "fsdp", axis=0, tiled=True),
            lax.all_gather(ffn_gain, "fsdp", axis=0, tiled=True),
            lax.all_gather(query_gain, "fsdp", axis=0, tiled=True),
            lax.all_gather(key_gain, "fsdp", axis=0, tiled=True),
        )

    w_qkv, w_out, gain_attn, gain_ffn, gain_query, gain_key = fetch_attention()
    gain_attn = gain_attn.astype(jnp.float32)
    gain_ffn = gain_ffn.astype(jnp.float32)
    gain_query = gain_query.astype(jnp.float32)
    gain_key = gain_key.astype(jnp.float32)
    scale_one = rms_scale(inputs)
    normed = (inputs * scale_one * gain_attn).astype(jnp.bfloat16)
    projected = lax.dot_general(
        w_qkv, normed, (((0,), (1,)), ((), ())), preferred_element_type=f32
    )
    q_raw = projected[:q_width].reshape(HEADS, HD, rows_here)
    k_raw = projected[q_width : q_width + kv_width].reshape(KV_HEADS, HD, rows_here)
    values_here = projected[q_width + kv_width :].reshape(KV_HEADS, HD, rows_here).astype(bf16)
    q_scale = rms_scale(q_raw, 1)
    k_scale = rms_scale(k_raw, 1)
    column_query, column_key = gain_query[:, None], gain_key[:, None]
    queries = rope(q_raw * q_scale * column_query, cosine, sine).astype(bf16)
    keys_here = rope(k_raw * k_scale * column_key, cosine, sine).astype(bf16)
    sent = jnp.concatenate(
        [queries, jnp.repeat(keys_here, per_group, 0), jnp.repeat(values_here, per_group, 0)], axis=1
    )
    sent = jnp.concatenate([sent] * parts, axis=0)
    got = lax.all_to_all(sent, "ctx", 0, 0, tiled=True)
    q_place, q_start = q_place[None], q_start[None]
    shape = jax.ShapeDtypeStruct
    attn_sent, *held = kernel_call(
        attend_kernel,
        tables,
        (got, q_place, q_start),
        [
            shape((ctx_size, HD, rows_here), bf16),
            shape((q_rows, HD), bf16),
            shape((HD, q_rows), bf16),
            shape((kv_rows, HD), bf16),
            shape((HD, kv_rows), bf16),
            shape((kv_rows, HD), bf16),
            shape((HD, q_rows), f32),
            shape((1, q_rows), f32),
        ],
        [pltpu.VMEM((HD, kv_rows), bf16)],
    )
    attn_in = lax.dynamic_slice_in_dim(
        lax.all_to_all(attn_sent, "ctx", 0, 0, tiled=True), part * HEADS, HEADS
    ).reshape(q_width, rows_here)
    h_one = inputs + lax.dot_general(
        attn_in, w_out, (((0,), (0,)), ((), ())), preferred_element_type=f32
    )
    scale_two = rms_scale(h_one)
    normed_two = (h_one * scale_two * gain_ffn).astype(jnp.bfloat16)
    columns = normed_two
    gate_up = jnp.einsum(
        "tr,rgf->tgf",
        columns,
        lax.all_gather(gate_up_weight, "fsdp", axis=0, tiled=True),
        preferred_element_type=jnp.float32,
    )
    gate = gate_up[:, 0]
    upper = gate_up[:, 1]
    sigma = jax.nn.sigmoid(gate)
    hidden = (gate * sigma * upper).astype(jnp.bfloat16)
    columns = hidden
    ffn_out = jnp.dot(
        columns,
        lax.all_gather(down_weight, "fsdp", axis=0, tiled=True),
        preferred_element_type=jnp.float32,
    )
    output = (h_one + ffn_out).astype(jnp.bfloat16)
    d_out = cotangent[0].astype(jnp.float32)
    d_ffn = d_out.astype(jnp.bfloat16)
    d_hidden = lax.dot_general(
        d_ffn,
        lax.all_gather(down_weight, "fsdp", axis=0, tiled=True),
        (((1,), (1,)), ((), ())),
        preferred_element_type=jnp.float32,
    )
    d_gate = d_hidden * upper * sigma * (1.0 + gate * (1.0 - sigma))
    d_upper = d_hidden * gate * sigma
    d_gate_up = jnp.stack([d_gate, d_upper], axis=1).astype(jnp.bfloat16)
    d_normed_two = jnp.einsum(
        "tgf,rgf->tr",
        d_gate_up,
        lax.all_gather(gate_up_weight, "fsdp", axis=0, tiled=True),
        preferred_element_type=jnp.float32,
    )
    columns = normed_two
    grad_gate_up = lax.psum_scatter(
        jnp.einsum("tr,tgf->rgf", columns, d_gate_up, preferred_element_type=jnp.float32).astype(
            jnp.bfloat16
        ),
        "fsdp",
        scatter_dimension=0,
        tiled=True,
    )
    columns = hidden
    grad_down = lax.psum_scatter(
        lax.dot_general(
            columns, d_ffn, (((0,), (0,)), ((), ())), preferred_element_type=jnp.float32
        ).astype(jnp.bfloat16),
        "fsdp",
        scatter_dimension=0,
        tiled=True,
    )
    d_norm_two, ffn_gain_term = norm_back(d_normed_two, h_one, scale_two, gain_ffn)
    d_h_one = d_out + d_norm_two
    d_attn = d_h_one.astype(jnp.bfloat16)
    grad_out_here = jnp.dot(attn_in, d_attn, preferred_element_type=f32)
    d_heads = lax.dot_general(
        w_out, d_attn, (((1,), (1,)), ((), ())), preferred_element_type=f32
    ).astype(bf16)
    d_heads = jnp.concatenate([d_heads.reshape(HEADS, HD, rows_here)] * parts, axis=0)
    d_got = lax.all_to_all(d_heads, "ctx", 0, 0, tiled=True)
    (d_sent,) = kernel_call(
        attend_back_kernel,
        tables,
        (d_got, q_place, q_start, *held),
        [shape((ctx_size, 3 * HD, rows_here), bf16)],
        [
            pltpu.VMEM((HD, q_rows), bf16),
            pltpu.VMEM((q_rows, HD), bf16),
            pltpu.VMEM((kv_rows, HD), f32),
            pltpu.VMEM((kv_rows, HD), f32),
        ],
    )
    d_back = lax.all_to_all(d_sent, "ctx", 0, 0, tiled=True)
    d_query = lax.dynamic_slice_in_dim(d_back[:, :HD], part * HEADS, HEADS).astype(f32)
    d_key_value = jnp.sum(
        d_back[:, HD:].reshape(parts, KV_HEADS, per_group, 2 * HD, rows_here).astype(f32),
        axis=(0, 2),
    )
    dq_normed = rope_back(d_query, cosine, sine)
    dk_normed = rope_back(d_key_value[:, :HD], cosine, sine)
    dq_raw, query_term = norm_back(dq_normed, q_raw, q_scale, column_query, 1)
    dk_raw, key_term = norm_back(dk_normed, k_raw, k_scale, column_key, 1)
    d_projected = jnp.concatenate(
        [
            dq_raw.reshape(q_width, rows_here).astype(bf16),
            dk_raw.reshape(kv_width, rows_here).astype(bf16),
            d_key_value[:, HD:].reshape(kv_width, rows_here).astype(bf16),
        ],
        axis=0,
    )
    grad_qkv_here = lax.dot_general(
        normed, d_projected, (((0,), (1,)), ((), ())), preferred_element_type=f32
    )
    d_normed = lax.dot_general(
        d_projected, w_qkv, (((0,), (1,)), ((), ())), preferred_element_type=f32
    )
    d_norm_one, attn_gain_term = norm_back(d_normed, inputs, scale_one, gain_attn)
    d_inputs = d_h_one + d_norm_one
    shard_qkv, shard_out, shard_attn_gain, shard_ffn_gain, shard_query_gain, shard_key_gain = (
        lax.psum_scatter(
            grad_qkv_here.astype(jnp.bfloat16), "fsdp", scatter_dimension=0, tiled=True
        ).astype(jnp.float32),
        lax.psum_scatter(
            grad_out_here.astype(jnp.bfloat16), "fsdp", scatter_dimension=0, tiled=True
        ).astype(jnp.float32),
        lax.psum_scatter(
            jnp.sum(attn_gain_term, axis=0).astype(jnp.bfloat16),
            "fsdp",
            scatter_dimension=0,
            tiled=True,
        ).astype(jnp.float32),
        lax.psum_scatter(
            jnp.sum(ffn_gain_term, axis=0).astype(jnp.bfloat16),
            "fsdp",
            scatter_dimension=0,
            tiled=True,
        ).astype(jnp.float32),
        lax.psum_scatter(
            jnp.sum(query_term, axis=(0, 2)).astype(jnp.bfloat16),
            "fsdp",
            scatter_dimension=0,
            tiled=True,
        ).astype(jnp.float32),
        lax.psum_scatter(
            jnp.sum(key_term, axis=(0, 2)).astype(jnp.bfloat16),
            "fsdp",
            scatter_dimension=0,
            tiled=True,
        ).astype(jnp.float32),
    )
    summed_grads = (
        lax.psum(shard_qkv.astype(jnp.bfloat16), "ctx").astype(jnp.float32),
        lax.psum(shard_out.astype(jnp.bfloat16), "ctx").astype(jnp.float32),
        lax.psum(grad_gate_up, "ctx").astype(jnp.float32),
        lax.psum(grad_down, "ctx").astype(jnp.float32),
        lax.psum(shard_attn_gain.astype(jnp.bfloat16), "ctx").astype(jnp.float32),
        lax.psum(shard_ffn_gain.astype(jnp.bfloat16), "ctx").astype(jnp.float32),
        lax.psum(shard_query_gain.astype(jnp.bfloat16), "ctx").astype(jnp.float32),
        lax.psum(shard_key_gain.astype(jnp.bfloat16), "ctx").astype(jnp.float32),
    )
    return (
        output[None],
        d_inputs[None],
        summed_grads[0],
        summed_grads[1],
        summed_grads[2],
        summed_grads[3],
        summed_grads[4],
        summed_grads[5],
        summed_grads[6],
        summed_grads[7],
    )


def solution(mesh):
    block = mesh.shape["fsdp"] == 2 and mesh.shape["ctx"] == 16
    return jax.shard_map(
        on_block if block else on_device,
        mesh=mesh,
        in_specs=(
            P("fsdp", "ctx", None),
            P("fsdp", None),
            P("fsdp", None),
            P("fsdp", None, None),
            P("fsdp", None),
            P("fsdp"),
            P("fsdp"),
            P("fsdp"),
            P("fsdp"),
            P("fsdp", None),
            P("fsdp", None),
            P("fsdp", "ctx", None),
        ),
        out_specs=(
            P("fsdp", "ctx", None),
            P("fsdp", "ctx", None),
            P("fsdp", None),
            P("fsdp", None),
            P("fsdp", None, None),
            P("fsdp", None),
            P("fsdp"),
            P("fsdp"),
            P("fsdp"),
            P("fsdp"),
        ),
        check_vma=False,
    )
```

```python
import functools

import jax
import jax.numpy as jnp
from jax import lax
from jax.experimental import pallas as pl
from jax.experimental.pallas import tpu as pltpu
from jax.sharding import PartitionSpec as P

HEADS = 16
KV_HEADS = 8
HD = 64
BLK = 128
TILE = 256
CHUNKS = 2


EPSILON = 1e-05
ROPE_BASE = 1000000.0
LOG2E = 1.4426950408889634
SCORE_SCALE = LOG2E * HD ** (-0.5)


def rms_scale(values, axis=-1):
    return lax.rsqrt(jnp.mean(values * values, axis=axis, keepdims=True) + EPSILON)


def norm_back(grad_normed, inputs, scale, gain, axis=-1):
    scaled = grad_normed * gain
    grad_in = scale * scaled - inputs * scale * scale * scale * jnp.mean(
        scaled * inputs, axis=axis, keepdims=True
    )
    return (grad_in, grad_normed * inputs * scale)


def rope(values, cosine, sine):
    half = HD // 2
    first, second = values[:, :half], values[:, half:]
    return jnp.concatenate([first * cosine - second * sine, second * cosine + first * sine], axis=1)


def rope_back(values, cosine, sine):
    half = HD // 2
    first, second = values[:, :half], values[:, half:]
    return jnp.concatenate([first * cosine + second * sine, second * cosine - first * sine], axis=1)


def starts_of(packed, lengths_row):
    ends = jnp.cumsum(lengths_row)
    past = packed[:, None] >= ends[None, :]
    return jnp.sum(jnp.where(past, lengths_row[None, :], 0), axis=1)


def block_tables(order, lengths_row):
    count = order.shape[0]
    rank = jnp.sum((order[None, :] < order[:, None]).astype(jnp.int32), axis=1)
    hit = rank[None, :] == jnp.arange(count, dtype=jnp.int32)[:, None]
    slot = jnp.sum(jnp.where(hit, jnp.arange(count, dtype=jnp.int32)[None, :], 0), axis=1)
    block = jnp.sum(jnp.where(hit, order[None, :], 0), axis=1)
    place = (block[:, None] * BLK + jnp.arange(BLK, dtype=jnp.int32)[None, :]).reshape(-1)
    return (slot, place, starts_of(place, lengths_row))


def attend_kernel(
    q_slot, kv_slot, first, last, qkv_ref, place_ref, start_ref,
    out_ref, q_ref, qt_ref, k_ref, kt_ref, v_ref, ot_ref, total_ref, vt_ref
):
    per_device = qkv_ref.shape[2] // BLK
    kv_blocks = k_ref.shape[0] // BLK
    q_blocks = q_ref.shape[0] // BLK

    def piece(slot, lower):
        return qkv_ref[
            slot // per_device,
            lower : lower + HD,
            pl.ds(pl.multiple_of((slot % per_device) * BLK, BLK), BLK),
        ]

    for i in range(kv_blocks):
        here = slice(i * BLK, (i + 1) * BLK)
        keys = piece(kv_slot[i], HD)
        kt_ref[:, here] = keys
        k_ref[here, :] = keys.T
        values = piece(kv_slot[i], 2 * HD)
        vt_ref[:, here] = values
        v_ref[here, :] = values.T
    for i in range(q_blocks):
        here = slice(i * BLK, (i + 1) * BLK)
        queries = piece(q_slot[i], 0)
        qt_ref[:, here] = queries
        q_ref[here, :] = queries.T
    if q_blocks < kv_blocks:
        out_ref[...] = jnp.zeros_like(out_ref)

    def tile(i, carry):
        rows = pl.ds(pl.multiple_of(i * TILE, TILE), TILE)
        queries = qt_ref[:, rows]
        place = place_ref[:, rows]
        start = start_ref[:, rows]

        def step(j, state):
            total, summed = state
            at = pl.multiple_of(j * TILE, TILE)
            scores = jnp.dot(
                k_ref[pl.ds(at, TILE), :], queries, preferred_element_type=jnp.float32
            )
            key_place = lax.broadcasted_iota(jnp.int32, (TILE, TILE), 0) + at
            allowed = (key_place <= place) & (key_place >= start)
            lifted = jnp.where(allowed, jnp.exp2(scores * SCORE_SCALE), 0.0)
            total = total + jnp.sum(lifted, axis=0, keepdims=True)
            summed = summed + jnp.dot(
                vt_ref[:, pl.ds(at, TILE)],
                lifted.astype(jnp.bfloat16),
                preferred_element_type=jnp.float32,
            )
            return (total, summed)

        total, summed = lax.fori_loop(
            first[i],
            last[i],
            step,
            (jnp.zeros((1, TILE), jnp.float32), jnp.zeros((HD, TILE), jnp.float32)),
        )
        attn = summed / total
        ot_ref[:, rows] = attn
        total_ref[:, rows] = jnp.log(total) * LOG2E
        rounded = attn.astype(jnp.bfloat16)
        for part in range(TILE // BLK):
            slot = q_slot[i * (TILE // BLK) + part]
            out_ref[
                slot // per_device,
                :,
                pl.ds(pl.multiple_of((slot % per_device) * BLK, BLK), BLK),
            ] = rounded[:, part * BLK : (part + 1) * BLK]
        return carry

    lax.fori_loop(0, q_blocks * BLK // TILE, tile, 0)


def attend_back_kernel(
    q_slot, kv_slot, first, last, d_ref, place_ref, start_ref,
    q_ref, qt_ref, k_ref, kt_ref, v_ref, ot_ref, total_ref,
    out_ref, dt_ref, do_ref, dk_ref, dv_ref
):
    per_device = d_ref.shape[2] // BLK
    kv_blocks = k_ref.shape[0] // BLK
    q_blocks = q_ref.shape[0] // BLK

    def lanes(slot):
        return pl.ds(pl.multiple_of((slot % per_device) * BLK, BLK), BLK)

    for i in range(q_blocks):
        here = slice(i * BLK, (i + 1) * BLK)
        slot = q_slot[i]
        grads = d_ref[slot // per_device, :, lanes(slot)]
        dt_ref[:, here] = grads
        do_ref[here, :] = grads.T
    dk_ref[...] = jnp.zeros_like(dk_ref)
    dv_ref[...] = jnp.zeros_like(dv_ref)
    if q_blocks < kv_blocks:
        out_ref[...] = jnp.zeros_like(out_ref)

    def tile(i, carry):
        rows = pl.ds(pl.multiple_of(i * TILE, TILE), TILE)
        queries = qt_ref[:, rows]
        grads = dt_ref[:, rows]
        place = place_ref[:, rows]
        start = start_ref[:, rows]
        delta = jnp.sum(grads.astype(jnp.float32) * ot_ref[:, rows], axis=0, keepdims=True)
        total = total_ref[:, rows]

        def step(j, d_query):
            at = pl.multiple_of(j * TILE, TILE)
            here = pl.ds(at, TILE)
            scores = jnp.dot(k_ref[here, :], queries, preferred_element_type=jnp.float32)
            key_place = lax.broadcasted_iota(jnp.int32, (TILE, TILE), 0) + at
            allowed = (key_place <= place) & (key_place >= start)
            shares = jnp.where(allowed, jnp.exp2(scores * SCORE_SCALE - total), 0.0)
            d_shares = jnp.dot(v_ref[here, :], grads, preferred_element_type=jnp.float32)
            d_scores = (shares * (d_shares - delta)).astype(jnp.bfloat16)
            dv_ref[here, :] += jnp.dot(
                shares.astype(jnp.bfloat16), do_ref[rows, :], preferred_element_type=jnp.float32
            )
            dk_ref[here, :] += jnp.dot(
                d_scores, q_ref[rows, :], preferred_element_type=jnp.float32
            )
            return d_query + jnp.dot(
                kt_ref[:, here], d_scores, preferred_element_type=jnp.float32
            )

        d_query = lax.fori_loop(first[i], last[i], step, jnp.zeros((HD, TILE), jnp.float32))
        rounded = (d_query * HD ** (-0.5)).astype(jnp.bfloat16)
        for part in range(TILE // BLK):
            slot = q_slot[i * (TILE // BLK) + part]
            out_ref[slot // per_device, 0:HD, lanes(slot)] = rounded[
                :, part * BLK : (part + 1) * BLK
            ]
        return carry

    lax.fori_loop(0, q_blocks * BLK // TILE, tile, 0)
    for i in range(kv_blocks):
        here = slice(i * BLK, (i + 1) * BLK)
        slot = kv_slot[i]
        out_ref[slot // per_device, HD : 2 * HD, lanes(slot)] = (
            (dk_ref[here, :] * HD ** (-0.5)).T.astype(jnp.bfloat16)
        )
        out_ref[slot // per_device, 2 * HD : 3 * HD, lanes(slot)] = (
            dv_ref[here, :].T.astype(jnp.bfloat16)
        )


def kernel_call(kernel, tables, arrays, outs, scratch):
    smem = pl.BlockSpec(memory_space=pltpu.SMEM)
    vmem = pl.BlockSpec(memory_space=pltpu.VMEM)
    return pl.pallas_call(
        kernel,
        out_shape=outs,
        in_specs=[smem] * len(tables) + [vmem] * len(arrays),
        out_specs=[vmem] * len(outs),
        scratch_shapes=scratch,
        compiler_params=pltpu.CompilerParams(vmem_limit_bytes=48 * 1024 * 1024),
        cost_estimate=pl.CostEstimate(
            flops=1, bytes_accessed=24 * 3_000_000, transcendentals=0
        ),
    )(*tables, *arrays)


class Links:
    def __init__(self, ctx_size):
        self.depth = ctx_size // 4
        index = lax.axis_index("ctx")
        self.core = index % 2
        self.y = (index // 2) % 2
        self.side = lax.axis_index("fsdp")
        self.half = ((index // 4 + 1) // 2) % 2
        self.quarter = index % 2 * 2 + self.y
        self.here = jnp.stack([self.half, self.core, self.y, self.side]).astype(jnp.int32)

    def route(self, place):
        pairs = []
        for z in range(self.depth):
            for y in range(2):
                for core in range(2):
                    to_z, to_y, to_core = place(z, y, core)
                    pairs.append(((z * 2 + y) * 2 + core, (to_z * 2 + to_y) * 2 + to_core))
        return pairs

    def over_core(self, value):
        return lax.ppermute(value, "ctx", self.route(lambda z, y, c: (z, y, 1 - c)))

    def over_y(self, value):
        return lax.ppermute(value, "ctx", self.route(lambda z, y, c: (z, 1 - y, c)))

    def over_z(self, value):
        return lax.ppermute(value, "ctx", self.route(lambda z, y, c: (z ^ 1, y, c)))

    def mirror_z(self, value):
        return lax.ppermute(value, "ctx", self.route(lambda z, y, c: (self.depth - 1 - z, y, c)))

    def over_x(self, value):
        return lax.ppermute(value, "fsdp", [(0, 1), (1, 0)])

    def spread_plane(self, value):
        across = self.over_core(value)
        beside = self.over_y(value)
        return (value, across, beside, self.over_core(beside))

    def deal_plane(self, keep, keep_far, give, give_far):
        got, got_far = self.over_core(give), self.over_core(give_far)
        return (keep, got, self.over_y(keep_far), self.over_y(got_far))

    def sum_depth(self, kept, got):
        rows = kept.shape[0] // 2

        def half(index):
            return add(
                lax.dynamic_slice_in_dim(kept, index * rows, rows),
                lax.dynamic_slice_in_dim(got, index * rows, rows),
            )

        given = self.over_z(half(1 - self.half))
        part = add(half(self.half), given)
        full = add(part, self.mirror_z(part))
        return (full, self.over_z(full))

    def reduce(self, sent, kept):
        return [self.spread_plane(v) for v in self.sum_depth(kept, self.over_x(sent))]

    def total(self, value):
        for swap in (self.over_core, self.over_y, self.over_x, self.over_z, self.mirror_z):
            value = value + swap(value)
        return value


def pick(value, index, axis):
    return lax.dynamic_index_in_dim(value, index, axis, keepdims=False)


def add(left, right):
    return (left.astype(jnp.float32) + right.astype(jnp.float32)).astype(jnp.bfloat16)


def after(value, *others):
    return lax.optimization_barrier((value, *others))[0]


def contract(left, right, axes):
    return lax.dot_general(
        left, right, ((axes[:1], axes[1:]), ((), ())), preferred_element_type=jnp.float32
    )


PARAMS = pltpu.CompilerParams(vmem_limit_bytes=56 * 1024 * 1024)


def cost(micros):
    return pl.CostEstimate(flops=1, bytes_accessed=micros * 3_000_000, transcendentals=0)


def call_with_here(
    kernel, here, grid, arrays, specs, outs, out_specs, scratch=(), aliases=None, micros=5
):
    return pl.pallas_call(
        kernel,
        grid_spec=pltpu.PrefetchScalarGridSpec(
            num_scalar_prefetch=1,
            grid=grid,
            in_specs=specs,
            out_specs=out_specs,
            scratch_shapes=list(scratch),
        ),
        out_shape=outs,
        input_output_aliases=aliases or {},
        compiler_params=PARAMS,
        cost_estimate=cost(micros),
    )(here, *arrays)


def whole(array):
    rank = len(array.shape)
    return pl.BlockSpec(array.shape, lambda i, here: (0,) * rank)


def project_kernel(here, *refs):
    x_ref, gain_ref, own_ref = refs[:3]
    pieces, q_gain, k_gain, cos_ref, sin_ref = refs[3:7], refs[7], refs[8], refs[9], refs[10]
    sent, weight, q_ref, k_ref, q_scale, k_scale, normed_ref, scale_ref = refs[11:]
    core, y, side = here[1], here[2], here[3]
    rows = own_ref.shape[0]
    part = rows // 4
    f32, bf16 = jnp.float32, jnp.bfloat16
    weight[pl.ds(pl.multiple_of(side * rows, rows), rows), :] = own_ref[...]
    for p in range(4):
        at = (1 - side) * rows + (((p % 2) ^ core) * 2 + ((p // 2) ^ y)) * part
        weight[pl.ds(pl.multiple_of(at, part), part), :] = pieces[p][...]
    x = x_ref[...].astype(f32)
    scale = rms_scale(x)
    scale_ref[...] = scale
    normed = (x * scale * gain_ref[...]).astype(bf16)
    normed_ref[...] = normed
    cosine, sine = cos_ref[...], sin_ref[...]
    half = HD // 2

    def turned(raw, gain, raw_ref, kept_scale, head):
        raw_ref[head * HD : (head + 1) * HD, :] = raw
        scale = rms_scale(raw, 0)
        kept_scale[head : head + 1, :] = scale
        value = raw * scale * gain
        first, second = value[:half], value[half:]
        return jnp.concatenate(
            [first * cosine - second * sine, second * cosine + first * sine], axis=0
        ).astype(bf16)

    per_group = HEADS // KV_HEADS
    for at in range(0, weight.shape[1], 2 * BLK):
        block = jnp.dot(normed, weight[:, at : at + 2 * BLK], preferred_element_type=f32)
        turned_block = block.T
        for n in range(2 * BLK // HD):
            head = at // HD + n
            raw = turned_block[n * HD : (n + 1) * HD, :]
            if head < HEADS:
                sent[head, 0:HD, :] = turned(raw, q_gain[...], q_ref, q_scale, head)
                continue
            head -= HEADS
            if head < KV_HEADS:
                value, row = turned(raw, k_gain[...], k_ref, k_scale, head), HD
            else:
                value, row, head = raw.astype(bf16), 2 * HD, head - KV_HEADS
            for copy in range(per_group):
                sent[head * per_group + copy, row : row + HD, :] = value


def project(here, x, gain, own, pieces, q_gain, k_gain, cosine, sine):
    tokens, width = x.shape
    f32, bf16 = jnp.float32, jnp.bfloat16
    shape = jax.ShapeDtypeStruct
    arrays = [x, gain, own, *pieces, q_gain, k_gain, cosine, sine]
    outs = [
        shape((HEADS, 3 * HD, tokens), bf16),
        shape((width, own.shape[1]), bf16),
        shape((HEADS * HD, tokens), f32),
        shape((KV_HEADS * HD, tokens), f32),
        shape((HEADS, tokens), f32),
        shape((KV_HEADS, tokens), f32),
        shape((tokens, width), bf16),
        shape((tokens, 1), f32),
    ]
    return call_with_here(
        project_kernel, here, (1,), arrays, [whole(a) for a in arrays], outs,
        [whole(o) for o in outs], micros=8,
    )


def place_rows(here, own, pieces):
    rows, columns = own.shape
    part = rows // 4

    def kernel(here, own_ref, *refs):
        out_ref = refs[-1]
        s = pl.program_id(0)

        @pl.when(s < 4)
        def _():
            out_ref[...] = own_ref[...]

        for p in range(4):

            @pl.when(s == 4 + p)
            def _(p=p):
                out_ref[...] = refs[p][...]

    def target(s, here):
        p = s - 4
        other = (1 - here[3]) * 4 + ((p % 2) ^ here[1]) * 2 + ((p // 2) ^ here[2])
        return (jnp.where(s < 4, here[3] * 4 + s, other), 0)

    (out,) = call_with_here(
        kernel,
        here,
        (8,),
        [own, *pieces],
        [pl.BlockSpec((part, columns), lambda s, here: (jnp.minimum(s, 3), 0))]
        + [whole(p) for p in pieces],
        [jax.ShapeDtypeStruct((2 * rows, columns), own.dtype)],
        [pl.BlockSpec((part, columns), target)],
    )
    return out


def ffn_kernel(chunk, here, *refs):
    two_ref, d_ref, own_ref = refs[:3]
    gate_pieces, down_ref, down_pieces = refs[3:7], refs[7], refs[8:12]
    before_out, before_two = refs[12:14]
    keep, give, hidden_keep, hidden_give = refs[14:16], refs[16:18], refs[18:20], refs[20:22]
    out_ref, d_two_ref = refs[22:24]
    weight, down, hidden_t = refs[24:27]
    core, y, side = here[1], here[2], here[3]
    t = pl.program_id(0)
    f32, bf16 = jnp.float32, jnp.bfloat16
    own_rows = own_ref.shape[1]
    part = own_rows // 4

    @pl.when(t == 0)
    def _():
        out_ref[...] = before_out[...]
        d_two_ref[...] = before_two[...]

    def quarter(p):
        return ((p % 2) ^ core) * 2 + ((p // 2) ^ y)

    weight[:, pl.ds(pl.multiple_of(side * own_rows, own_rows), own_rows), :] = own_ref[...]
    for p in range(4):
        at = pl.multiple_of((1 - side) * own_rows + quarter(p) * part, part)
        weight[:, pl.ds(at, part), :] = gate_pieces[p][...]

    @pl.when(side == chunk)
    def _():
        down[...] = down_ref[...]

    @pl.when(side != chunk)
    def _():
        for p in range(4):
            wide = down_pieces[p].shape[1]
            at = pl.multiple_of(quarter(p) * wide, wide)
            down[:, pl.ds(at, wide)] = down_pieces[p][...]

    two = two_ref[...]
    d_ffn = d_ref[...]
    tile = own_ref.shape[2]
    first = (tile // 2) // 256 * 256
    for begin, end in ((0, first), (first, tile)):
        at = slice(begin, end)
        gate = jnp.dot(two, weight[0, :, at], preferred_element_type=f32)
        upper = jnp.dot(two, weight[1, :, at], preferred_element_type=f32)
        d_hidden = contract(d_ffn, down[at, :], (1, 1))
        sigma = jax.nn.sigmoid(gate)
        silu = gate * sigma
        hidden = (silu * upper).astype(bf16)
        d_gate = (d_hidden * upper * sigma * (1.0 + gate * (1.0 - sigma))).astype(bf16)
        d_upper = (d_hidden * silu).astype(bf16)
        out_ref[...] += jnp.dot(hidden, down[at, :], preferred_element_type=f32)
        d_two_ref[...] += contract(d_gate, weight[0, :, at], (1, 1)) + contract(
            d_upper, weight[1, :, at], (1, 1)
        )
        hidden_t[at, :] = hidden.T
        mine = jnp.where(core == 0, d_gate, d_upper)
        other = jnp.where(core == 0, d_upper, d_gate)
        for far in range(2):

            @pl.when((t == y) == (far == 0))
            def _(far=far):
                keep[far][:, at] = mine
                give[far][:, at] = other

    share = tile // 2
    for far in range(2):
        at = pl.multiple_of((y ^ far) * share, share)

        @pl.when(t == core)
        def _(far=far, at=at):
            hidden_keep[far][...] = hidden_t[pl.ds(at, share), :]

        @pl.when(t != core)
        def _(far=far, at=at):
            hidden_give[far][...] = hidden_t[pl.ds(at, share), :]


def ffn(here, chunk, two, d_ffn, own, pieces, down, down_pieces, before):
    tokens, width = two.shape
    tile = own.shape[2] // 4
    share = tile // 2
    shape = jax.ShapeDtypeStruct
    f32, bf16 = jnp.float32, jnp.bfloat16
    outs = (
        [shape((tokens, tile), bf16)] * 4
        + [shape((share, tokens), bf16)] * 4
        + [shape((tokens, width), f32)] * 2
    )

    def own_down(t, here):
        return (jnp.where(here[3] == chunk, t, 0), 0)

    def other_down(t, here):
        return (jnp.where(here[3] == chunk, 0, t), 0)

    specs = (
        [whole(two), whole(d_ffn)]
        + [pl.BlockSpec((2, own.shape[1], tile), lambda t, here: (0, 0, 2 * chunk + t))]
        + [pl.BlockSpec((2, own.shape[1] // 4, tile), lambda t, here: (0, 0, t))] * 4
        + [pl.BlockSpec((tile, width), own_down)]
        + [pl.BlockSpec((tile, width // 4), other_down)] * 4
        + [whole(before[0]), whole(before[1])]
    )
    got = call_with_here(
        functools.partial(ffn_kernel, chunk),
        here,
        (2,),
        [two, d_ffn, own, *pieces, down, *down_pieces, *before],
        specs,
        outs,
        [whole(o) for o in outs],
        [
            pltpu.VMEM((2, width, tile), bf16),
            pltpu.VMEM((tile, width), bf16),
            pltpu.VMEM((tile, tokens), bf16),
        ],
    )
    return got[:4], got[4:8], got[8:]


def wide_product_kernel(here, *refs):
    planes, terms = refs[:4], refs[4:8]
    sent, kept, left, right = refs[8:]
    tokens = planes[0].shape[0]
    for i in range(4):
        left[:, i * tokens : (i + 1) * tokens] = planes[i][...].T
        right[i * tokens : (i + 1) * tokens, :] = terms[i][...]
    side = here[3]
    rows = kept.shape[0]
    step = 256
    for at in range(0, rows, step):
        for owner, out_ref in ((1 - side, sent), (side, kept)):
            place = pl.multiple_of(owner * rows + at, step)
            out_ref[at : at + step, :] = jnp.dot(
                left[pl.ds(place, step), :], right[...], preferred_element_type=jnp.float32
            ).astype(out_ref.dtype)


def wide_products(here, planes, terms):
    tokens, rows = planes[0].shape
    columns = terms[0].shape[1]
    outs = [
        jax.ShapeDtypeStruct((rows // 2, columns), jnp.bfloat16),
        jax.ShapeDtypeStruct((rows // 2, columns), jnp.float32),
    ]
    arrays = [*planes, *terms]
    return call_with_here(
        wide_product_kernel,
        here,
        (1,),
        arrays,
        [whole(a) for a in arrays],
        outs,
        [whole(o) for o in outs],
        [
            pltpu.VMEM((rows, 4 * tokens), jnp.bfloat16),
            pltpu.VMEM((4 * tokens, columns), jnp.bfloat16),
        ],
    )


def down_product_kernel(here, *refs):
    planes, terms = refs[:4], (refs[4:8], refs[8:12])
    sent, kept, left, right = refs[12:]
    tokens = planes[0].shape[0]
    for i in range(4):
        right[i * tokens : (i + 1) * tokens, :] = planes[i][...]
    for chunk in range(2):
        for i in range(4):
            left[:, i * tokens : (i + 1) * tokens] = terms[chunk][i][...]
        product = jnp.dot(left[...], right[...], preferred_element_type=jnp.float32)

        @pl.when(here[3] == chunk)
        def _(product=product):
            kept[...] = product

        @pl.when(here[3] != chunk)
        def _(product=product):
            sent[...] = product.astype(sent.dtype)


def down_products(here, planes, first, second):
    tokens, columns = planes[0].shape
    rows = first[0].shape[0]
    outs = [
        jax.ShapeDtypeStruct((rows, columns), jnp.bfloat16),
        jax.ShapeDtypeStruct((rows, columns), jnp.float32),
    ]
    arrays = [*planes, *first, *second]
    return call_with_here(
        down_product_kernel,
        here,
        (1,),
        arrays,
        [whole(a) for a in arrays],
        outs,
        [whole(o) for o in outs],
        [
            pltpu.VMEM((rows, 4 * tokens), jnp.bfloat16),
            pltpu.VMEM((4 * tokens, columns), jnp.bfloat16),
        ],
    )


def attention_product_kernel(here, *refs):
    normed, projected, attn, d_attn = refs[:4], refs[4:8], refs[8:12], refs[12:16]
    sent, kept, left, right, left_out, right_out = refs[16:]
    tokens = normed[0].shape[0]
    for i in range(4):
        at = slice(i * tokens, (i + 1) * tokens)
        left[:, at] = normed[i][...].T
        right[at, :] = projected[i][...].T
        left_out[:, at] = attn[i][...]
        right_out[at, :] = d_attn[i][...]
    rows = kept.shape[0]
    cut = right.shape[1]
    for owner, out_ref in ((1 - here[3], sent), (here[3], kept)):
        at = pl.ds(pl.multiple_of(owner * rows, rows), rows)
        out_ref[:, :cut] = jnp.dot(
            left[at, :], right[...], preferred_element_type=jnp.float32
        ).astype(out_ref.dtype)
        out_ref[:, cut:] = jnp.dot(
            left_out[at, :], right_out[...], preferred_element_type=jnp.float32
        ).astype(out_ref.dtype)


def attention_products(here, normed, projected, attn, d_attn):
    tokens, rows = normed[0].shape
    cut, rest = projected[0].shape[0], d_attn[0].shape[1]
    outs = [
        jax.ShapeDtypeStruct((rows // 2, cut + rest), jnp.bfloat16),
        jax.ShapeDtypeStruct((rows // 2, cut + rest), jnp.float32),
    ]
    arrays = [*normed, *projected, *attn, *d_attn]
    return call_with_here(
        attention_product_kernel,
        here,
        (1,),
        arrays,
        [whole(a) for a in arrays],
        outs,
        [whole(o) for o in outs],
        [
            pltpu.VMEM((rows, 4 * tokens), jnp.bfloat16),
            pltpu.VMEM((4 * tokens, cut), jnp.bfloat16),
            pltpu.VMEM((rows, 4 * tokens), jnp.bfloat16),
            pltpu.VMEM((4 * tokens, rest), jnp.bfloat16),
        ],
    )


def place_gate_up_kernel(blocks, here, *refs):
    out_ref = refs[-1]
    pieces = refs[:8]
    wide = pieces[0].shape[1]
    far_half = (pl.program_id(0) // blocks) ^ here[0]
    for case in range(8):
        half, core, y = case // 4, case // 2 % 2, case % 2

        @pl.when((far_half == half) & (here[1] == core) & (here[2] == y))
        def _(half=half, core=core, y=y):
            for kind in range(2):
                for column in range(2):
                    value = pieces[half * 4 + (y ^ column) * 2 + (core ^ kind)][...]
                    out_ref[:, kind, column * wide : (column + 1) * wide] = value.astype(
                        jnp.float32
                    )


def place_gate_up(here, chunk, pieces, before):
    rows, wide = pieces[0][0].shape
    step = 64
    blocks = rows // step

    def source(half):
        return lambda i, here: (jnp.clip(i - blocks * (here[0] ^ half), 0, blocks - 1), 0)

    arrays = [v for plane in pieces for v in plane]
    specs = [pl.BlockSpec((step, wide), source(n // 4)) for n in range(8)]
    aliases = {}
    if before is not None:
        arrays.append(before)
        specs.append(pl.BlockSpec(memory_space=pl.ANY))
        aliases = {9: 0}
    (out,) = call_with_here(
        functools.partial(place_gate_up_kernel, blocks),
        here,
        (2 * blocks,),
        arrays,
        specs,
        [jax.ShapeDtypeStruct((2 * rows, 2, 2 * wide * CHUNKS), jnp.float32)],
        [pl.BlockSpec((step, 2, 2 * wide), lambda i, here: (i, 0, chunk))],
        aliases=aliases,
        micros=10,
    )
    return out


def place_pieces(here, pieces, cuts, by_rows):
    rows = pieces[0][0].shape[0]
    flat = [v for plane in pieces for v in plane]

    def kernel(here, *refs):
        for s in range(8):

            @pl.when(pl.program_id(0) == s)
            def _(s=s):
                at = 0
                for out_ref in refs[8:]:
                    wide = out_ref.shape[1]
                    out_ref[...] = refs[s][:, at : at + wide].astype(jnp.float32)
                    at += wide

    def target(s, here):
        half = (s // 4) ^ here[0]
        y = ((s // 2) % 2) ^ here[2]
        core = (s % 2) ^ here[1]
        if by_rows:
            return ((core * 2 + y) * 2 + half, 0)
        return (half, core * 2 + y)

    across, along = (1, 8) if by_rows else (4, 2)
    return call_with_here(
        kernel,
        here,
        (8,),
        flat,
        [whole(v) for v in flat],
        [jax.ShapeDtypeStruct((rows * along, wide * across), jnp.float32) for wide in cuts],
        [pl.BlockSpec((rows, wide), target) for wide in cuts],
    )


def on_block(
    tokens,
    qkv_weight,
    out_weight,
    gate_up_weight,
    down_weight,
    attn_gain,
    ffn_gain,
    query_gain,
    key_gain,
    seq_lengths,
    block_order,
    cotangent,
):
    inputs = tokens[0].astype(jnp.float32)
    rows_here = inputs.shape[0]
    ctx_size = lax.axis_size("ctx")
    ctx_index = lax.axis_index("ctx")
    per_group = HEADS // KV_HEADS
    q_width = HEADS * HD
    kv_width = KV_HEADS * HD
    order_row = block_order[0]
    lengths_row = seq_lengths[0]
    slots = jnp.arange(rows_here, dtype=jnp.int32) // BLK + ctx_index * (rows_here // BLK)
    table = slots[:, None] == jnp.arange(order_row.shape[0], dtype=jnp.int32)[None, :]
    packed = (
        jnp.sum(jnp.where(table, order_row[None, :], 0), axis=1) * BLK
        + jnp.arange(rows_here, dtype=jnp.int32) % BLK
    )
    local = packed - starts_of(packed, lengths_row)
    frequency = ROPE_BASE ** (-2.0 * jnp.arange(HD // 2, dtype=jnp.float32) / HD)
    angle = frequency[:, None] * local.astype(jnp.float32)[None, :]
    cosine = jnp.cos(angle)[None]
    sine = jnp.sin(angle)[None]
    bf16, f32 = jnp.bfloat16, jnp.float32
    parts = ctx_size // HEADS
    part = ctx_index // HEADS
    part_blocks = HEADS * rows_here // BLK
    q_order = lax.dynamic_slice_in_dim(order_row, part * part_blocks, part_blocks)
    q_slot, q_place, q_start = block_tables(q_order, lengths_row)
    q_slot = q_slot + part * part_blocks
    kv_slot, _, _ = block_tables(order_row, lengths_row)
    first = jnp.min(q_start.reshape(-1, TILE), axis=1) // TILE
    last = jnp.max(q_place.reshape(-1, TILE), axis=1) // TILE + 1
    tables = (q_slot, kv_slot, first, last)
    q_rows, kv_rows = part_blocks * BLK, order_row.shape[0] * BLK

    links = Links(ctx_size)
    here = links.here
    width = inputs.shape[1]
    rows = qkv_weight.shape[0]
    part_rows = rows // 4

    def quarter_rows(weight):
        return lax.dynamic_slice_in_dim(weight, links.quarter * part_rows, part_rows)

    gains_here = jnp.concatenate([attn_gain, ffn_gain, query_gain, key_gain])
    gains_there = links.over_x(gains_here)

    def gain_of(at, size):
        mine, other = gains_here[at : at + size], gains_there[at : at + size]
        return jnp.where(
            links.side == 0, jnp.concatenate([mine, other]), jnp.concatenate([other, mine])
        ).astype(f32)

    gain_attn = gain_of(0, rows)
    gain_ffn = gain_of(rows, rows)
    gain_query = gain_of(2 * rows, HD // 2)
    gain_key = gain_of(2 * rows + HD // 2, HD // 2)
    ff_chunk = gate_up_weight.shape[2] // CHUNKS

    def gate_up_piece(chunk):
        return jnp.transpose(
            lax.dynamic_slice(
                gate_up_weight,
                (links.quarter * part_rows, 0, chunk * ff_chunk),
                (part_rows, 2, ff_chunk),
            ),
            (1, 0, 2),
        )

    qkv_there = links.over_x(quarter_rows(qkv_weight))
    out_piece = quarter_rows(out_weight)
    first_piece, second_piece = gate_up_piece(0), gate_up_piece(1)
    down_piece = lax.dynamic_slice_in_dim(
        down_weight, links.quarter * (width // 4), width // 4, 1
    )
    d_ffn = cotangent[0]
    qkv_there = after(qkv_there, out_piece, first_piece, second_piece, down_piece)
    out_there = links.over_x(after(out_piece, qkv_there))
    first_there = links.over_x(after(first_piece, qkv_there))
    gate_up = jnp.transpose(after(gate_up_weight, qkv_there), (1, 0, 2))
    qkv_beside = links.over_y(qkv_there)
    qkv_pieces = (
        qkv_there,
        links.over_core(qkv_there),
        qkv_beside,
        links.over_core(after(qkv_beside, gate_up)),
    )
    ffn_plane = links.spread_plane(after(d_ffn, qkv_beside))
    tokens_here = tokens[0]
    sent, w_qkv, q_raw, k_raw, q_scale, k_scale, normed, scale_one = project(
        here, tokens_here, gain_attn[None], qkv_weight, qkv_pieces,
        gain_query[:, None], gain_key[:, None], cosine[0], sine[0],
    )
    q_raw = q_raw.reshape(HEADS, HD, rows_here)
    k_raw = k_raw.reshape(KV_HEADS, HD, rows_here)
    q_scale, k_scale = q_scale[:, None], k_scale[:, None]
    column_query, column_key = gain_query[:, None], gain_key[:, None]
    got = lax.all_to_all(sent, "ctx", 0, 0, tiled=True)
    out_there = after(out_there, sent)
    first_there = after(first_there, sent)
    down_there = links.over_x(after(down_piece, first_there))
    first_beside = links.over_y(first_there)
    out_beside = links.over_y(out_there)
    normed_plane = links.spread_plane(after(normed, sent))
    second_there = links.over_x(after(second_piece, down_there))
    down_beside = links.over_y(down_there)
    got = after(got, down_there)
    q_place, q_start = q_place[None], q_start[None]
    shape = jax.ShapeDtypeStruct
    attn_sent, *held = kernel_call(
        attend_kernel,
        tables,
        (got, q_place, q_start),
        [
            shape((ctx_size, HD, rows_here), bf16),
            shape((q_rows, HD), bf16),
            shape((HD, q_rows), bf16),
            shape((kv_rows, HD), bf16),
            shape((HD, kv_rows), bf16),
            shape((kv_rows, HD), bf16),
            shape((HD, q_rows), f32),
            shape((1, q_rows), f32),
        ],
        [pltpu.VMEM((HD, kv_rows), bf16)],
    )
    attn_in = lax.dynamic_slice_in_dim(
        lax.all_to_all(attn_sent, "ctx", 0, 0, tiled=True), part * HEADS, HEADS
    ).reshape(q_width, rows_here)
    second_there = after(second_there, attn_sent)

    def spread(there, beside):
        return (there, links.over_core(there), beside, links.over_core(after(beside, attn_sent)))

    out_pieces = spread(out_there, out_beside)
    w_out = place_rows(here, out_weight, out_pieces)
    gate_up_pieces = [spread(first_there, first_beside), links.spread_plane(second_there)]
    down_pieces = spread(down_there, down_beside)
    attn_plane = links.spread_plane(attn_in)
    h_one = inputs + contract(attn_in, w_out, (0, 0))
    scale_two = rms_scale(h_one)
    normed_two = (h_one * scale_two * gain_ffn).astype(bf16)
    two_plane = links.spread_plane(normed_two)
    sums = [h_one, jnp.zeros_like(h_one)]
    wide_shares, hidden_plane = [], []
    for chunk in range(CHUNKS):
        d_wide, hidden, sums = ffn(
            here, chunk, normed_two, d_ffn, gate_up, gate_up_pieces[chunk],
            down_weight, down_pieces, sums,
        )
        shares = links.deal_plane(*d_wide)
        if chunk == 0:
            sums = [after(sums[0], shares[1]), sums[1]]
        wide_shares.append(shares)
        hidden_plane.append(links.deal_plane(*hidden))
    output = sums[0].astype(bf16)
    d_norm_two, ffn_gain_term = norm_back(sums[1], h_one, scale_two, gain_ffn)
    d_h_one = d_ffn.astype(f32) + d_norm_two
    d_attn = d_h_one.astype(bf16)
    d_heads = lax.dot_general(
        w_out, d_attn, (((1,), (1,)), ((), ())), preferred_element_type=f32
    ).astype(bf16)
    d_heads = jnp.concatenate([d_heads.reshape(HEADS, HD, rows_here)] * parts, axis=0)
    d_got = lax.all_to_all(d_heads, "ctx", 0, 0, tiled=True)
    first_shares = [after(v, d_heads) for v in wide_shares[0]]
    first_products = wide_products(here, two_plane, first_shares)
    d_got = after(d_got, first_products[0])
    (d_sent,) = kernel_call(
        attend_back_kernel,
        tables,
        (d_got, q_place, q_start, *held),
        [shape((ctx_size, 3 * HD, rows_here), bf16)],
        [
            pltpu.VMEM((HD, q_rows), bf16),
            pltpu.VMEM((q_rows, HD), bf16),
            pltpu.VMEM((kv_rows, HD), f32),
            pltpu.VMEM((kv_rows, HD), f32),
        ],
    )
    d_back = lax.all_to_all(d_sent, "ctx", 0, 0, tiled=True)
    second_shares = [after(v, d_sent) for v in wide_shares[1]]
    products = [first_products, wide_products(here, two_plane, second_shares)]
    d_query = lax.dynamic_slice_in_dim(d_back[:, :HD], part * HEADS, HEADS).astype(f32)
    d_key_value = jnp.sum(
        d_back[:, HD:].reshape(parts, KV_HEADS, per_group, 2 * HD, rows_here).astype(f32),
        axis=(0, 2),
    )
    dq_normed = rope_back(d_query, cosine, sine)
    dk_normed = rope_back(d_key_value[:, :HD], cosine, sine)
    dq_raw, query_term = norm_back(dq_normed, q_raw, q_scale, column_query, 1)
    dk_raw, key_term = norm_back(dk_normed, k_raw, k_scale, column_key, 1)
    d_projected = jnp.concatenate(
        [
            dq_raw.reshape(q_width, rows_here).astype(bf16),
            dk_raw.reshape(kv_width, rows_here).astype(bf16),
            d_key_value[:, HD:].reshape(kv_width, rows_here).astype(bf16),
        ],
        axis=0,
    )
    d_normed = contract(d_projected, w_qkv, (0, 1))
    d_norm_one, attn_gain_term = norm_back(d_normed, inputs, scale_one, gain_attn)
    d_inputs = d_h_one + d_norm_one
    grad_gate_up = None
    for chunk in range(CHUNKS):
        grad_gate_up = place_gate_up(here, chunk, links.reduce(*products[chunk]), grad_gate_up)
    (grad_down,) = place_pieces(
        here, links.reduce(*down_products(here, ffn_plane, *hidden_plane)), (width,), True
    )

    def deal(value, size, axis):
        def share(core, y):
            return lax.dynamic_slice_in_dim(value, (core * 2 + y) * size, size, axis)

        return links.deal_plane(
            share(links.core, links.y),
            share(links.core, 1 - links.y),
            share(1 - links.core, links.y),
            share(1 - links.core, 1 - links.y),
        )

    attention_terms = attention_products(
        here,
        normed_plane,
        deal(d_projected, d_projected.shape[0] // 4, 0),
        attn_plane,
        deal(d_attn, width // 4, 1),
    )
    grad_qkv, grad_out = place_pieces(
        here, links.reduce(*attention_terms), (d_projected.shape[0] // 4, width // 4), False
    )
    gain_terms = jnp.concatenate(
        [
            jnp.sum(attn_gain_term, axis=0),
            jnp.sum(ffn_gain_term, axis=0),
            jnp.sum(query_term, axis=(0, 2)),
            jnp.sum(key_term, axis=(0, 2)),
        ]
    )
    gain_sums = links.total(gain_terms.reshape(-1, 128)).reshape(-1)
    gain_grads = []
    at = 0
    for gain in (attn_gain, ffn_gain, query_gain, key_gain):
        size = gain.shape[0]
        gain_grads.append(lax.dynamic_slice_in_dim(gain_sums, at + links.side * size, size))
        at += 2 * size
    return (
        output[None],
        d_inputs[None],
        grad_qkv,
        grad_out,
        grad_gate_up,
        grad_down,
        *gain_grads,
    )


def on_device(
    tokens,
    qkv_weight,
    out_weight,
    gate_up_weight,
    down_weight,
    attn_gain,
    ffn_gain,
    query_gain,
    key_gain,
    seq_lengths,
    block_order,
    cotangent,
):
    inputs = tokens[0].astype(jnp.float32)
    rows_here = inputs.shape[0]
    ctx_size = lax.axis_size("ctx")
    ctx_index = lax.axis_index("ctx")
    per_group = HEADS // KV_HEADS
    q_width = HEADS * HD
    kv_width = KV_HEADS * HD
    order_row = block_order[0]
    lengths_row = seq_lengths[0]
    slots = jnp.arange(rows_here, dtype=jnp.int32) // BLK + ctx_index * (rows_here // BLK)
    table = slots[:, None] == jnp.arange(order_row.shape[0], dtype=jnp.int32)[None, :]
    packed = (
        jnp.sum(jnp.where(table, order_row[None, :], 0), axis=1) * BLK
        + jnp.arange(rows_here, dtype=jnp.int32) % BLK
    )
    local = packed - starts_of(packed, lengths_row)
    frequency = ROPE_BASE ** (-2.0 * jnp.arange(HD // 2, dtype=jnp.float32) / HD)
    angle = frequency[:, None] * local.astype(jnp.float32)[None, :]
    cosine = jnp.cos(angle)[None]
    sine = jnp.sin(angle)[None]
    bf16, f32 = jnp.bfloat16, jnp.float32
    parts = ctx_size // HEADS
    part = ctx_index // HEADS
    part_blocks = HEADS * rows_here // BLK
    q_order = lax.dynamic_slice_in_dim(order_row, part * part_blocks, part_blocks)
    q_slot, q_place, q_start = block_tables(q_order, lengths_row)
    q_slot = q_slot + part * part_blocks
    kv_slot, _, _ = block_tables(order_row, lengths_row)
    first = jnp.min(q_start.reshape(-1, TILE), axis=1) // TILE
    last = jnp.max(q_place.reshape(-1, TILE), axis=1) // TILE + 1
    tables = (q_slot, kv_slot, first, last)
    q_rows, kv_rows = part_blocks * BLK, order_row.shape[0] * BLK

    def fetch_attention():
        return (
            lax.all_gather(qkv_weight, "fsdp", axis=0, tiled=True),
            lax.all_gather(out_weight, "fsdp", axis=0, tiled=True),
            lax.all_gather(attn_gain, "fsdp", axis=0, tiled=True),
            lax.all_gather(ffn_gain, "fsdp", axis=0, tiled=True),
            lax.all_gather(query_gain, "fsdp", axis=0, tiled=True),
            lax.all_gather(key_gain, "fsdp", axis=0, tiled=True),
        )

    w_qkv, w_out, gain_attn, gain_ffn, gain_query, gain_key = fetch_attention()
    gain_attn = gain_attn.astype(jnp.float32)
    gain_ffn = gain_ffn.astype(jnp.float32)
    gain_query = gain_query.astype(jnp.float32)
    gain_key = gain_key.astype(jnp.float32)
    scale_one = rms_scale(inputs)
    normed = (inputs * scale_one * gain_attn).astype(jnp.bfloat16)
    projected = lax.dot_general(
        w_qkv, normed, (((0,), (1,)), ((), ())), preferred_element_type=f32
    )
    q_raw = projected[:q_width].reshape(HEADS, HD, rows_here)
    k_raw = projected[q_width : q_width + kv_width].reshape(KV_HEADS, HD, rows_here)
    values_here = projected[q_width + kv_width :].reshape(KV_HEADS, HD, rows_here).astype(bf16)
    q_scale = rms_scale(q_raw, 1)
    k_scale = rms_scale(k_raw, 1)
    column_query, column_key = gain_query[:, None], gain_key[:, None]
    queries = rope(q_raw * q_scale * column_query, cosine, sine).astype(bf16)
    keys_here = rope(k_raw * k_scale * column_key, cosine, sine).astype(bf16)
    sent = jnp.concatenate(
        [queries, jnp.repeat(keys_here, per_group, 0), jnp.repeat(values_here, per_group, 0)], axis=1
    )
    sent = jnp.concatenate([sent] * parts, axis=0)
    got = lax.all_to_all(sent, "ctx", 0, 0, tiled=True)
    q_place, q_start = q_place[None], q_start[None]
    shape = jax.ShapeDtypeStruct
    attn_sent, *held = kernel_call(
        attend_kernel,
        tables,
        (got, q_place, q_start),
        [
            shape((ctx_size, HD, rows_here), bf16),
            shape((q_rows, HD), bf16),
            shape((HD, q_rows), bf16),
            shape((kv_rows, HD), bf16),
            shape((HD, kv_rows), bf16),
            shape((kv_rows, HD), bf16),
            shape((HD, q_rows), f32),
            shape((1, q_rows), f32),
        ],
        [pltpu.VMEM((HD, kv_rows), bf16)],
    )
    attn_in = lax.dynamic_slice_in_dim(
        lax.all_to_all(attn_sent, "ctx", 0, 0, tiled=True), part * HEADS, HEADS
    ).reshape(q_width, rows_here)
    h_one = inputs + lax.dot_general(
        attn_in, w_out, (((0,), (0,)), ((), ())), preferred_element_type=f32
    )
    scale_two = rms_scale(h_one)
    normed_two = (h_one * scale_two * gain_ffn).astype(jnp.bfloat16)
    columns = normed_two
    gate_up = jnp.einsum(
        "tr,rgf->tgf",
        columns,
        lax.all_gather(gate_up_weight, "fsdp", axis=0, tiled=True),
        preferred_element_type=jnp.float32,
    )
    gate = gate_up[:, 0]
    upper = gate_up[:, 1]
    sigma = jax.nn.sigmoid(gate)
    hidden = (gate * sigma * upper).astype(jnp.bfloat16)
    columns = hidden
    ffn_out = jnp.dot(
        columns,
        lax.all_gather(down_weight, "fsdp", axis=0, tiled=True),
        preferred_element_type=jnp.float32,
    )
    output = (h_one + ffn_out).astype(jnp.bfloat16)
    d_out = cotangent[0].astype(jnp.float32)
    d_ffn = d_out.astype(jnp.bfloat16)
    d_hidden = lax.dot_general(
        d_ffn,
        lax.all_gather(down_weight, "fsdp", axis=0, tiled=True),
        (((1,), (1,)), ((), ())),
        preferred_element_type=jnp.float32,
    )
    d_gate = d_hidden * upper * sigma * (1.0 + gate * (1.0 - sigma))
    d_upper = d_hidden * gate * sigma
    d_gate_up = jnp.stack([d_gate, d_upper], axis=1).astype(jnp.bfloat16)
    d_normed_two = jnp.einsum(
        "tgf,rgf->tr",
        d_gate_up,
        lax.all_gather(gate_up_weight, "fsdp", axis=0, tiled=True),
        preferred_element_type=jnp.float32,
    )
    columns = normed_two
    grad_gate_up = lax.psum_scatter(
        jnp.einsum("tr,tgf->rgf", columns, d_gate_up, preferred_element_type=jnp.float32).astype(
            jnp.bfloat16
        ),
        "fsdp",
        scatter_dimension=0,
        tiled=True,
    )
    columns = hidden
    grad_down = lax.psum_scatter(
        lax.dot_general(
            columns, d_ffn, (((0,), (0,)), ((), ())), preferred_element_type=jnp.float32
        ).astype(jnp.bfloat16),
        "fsdp",
        scatter_dimension=0,
        tiled=True,
    )
    d_norm_two, ffn_gain_term = norm_back(d_normed_two, h_one, scale_two, gain_ffn)
    d_h_one = d_out + d_norm_two
    d_attn = d_h_one.astype(jnp.bfloat16)
    grad_out_here = jnp.dot(attn_in, d_attn, preferred_element_type=f32)
    d_heads = lax.dot_general(
        w_out, d_attn, (((1,), (1,)), ((), ())), preferred_element_type=f32
    ).astype(bf16)
    d_heads = jnp.concatenate([d_heads.reshape(HEADS, HD, rows_here)] * parts, axis=0)
    d_got = lax.all_to_all(d_heads, "ctx", 0, 0, tiled=True)
    (d_sent,) = kernel_call(
        attend_back_kernel,
        tables,
        (d_got, q_place, q_start, *held),
        [shape((ctx_size, 3 * HD, rows_here), bf16)],
        [
            pltpu.VMEM((HD, q_rows), bf16),
            pltpu.VMEM((q_rows, HD), bf16),
            pltpu.VMEM((kv_rows, HD), f32),
            pltpu.VMEM((kv_rows, HD), f32),
        ],
    )
    d_back = lax.all_to_all(d_sent, "ctx", 0, 0, tiled=True)
    d_query = lax.dynamic_slice_in_dim(d_back[:, :HD], part * HEADS, HEADS).astype(f32)
    d_key_value = jnp.sum(
        d_back[:, HD:].reshape(parts, KV_HEADS, per_group, 2 * HD, rows_here).astype(f32),
        axis=(0, 2),
    )
    dq_normed = rope_back(d_query, cosine, sine)
    dk_normed = rope_back(d_key_value[:, :HD], cosine, sine)
    dq_raw, query_term = norm_back(dq_normed, q_raw, q_scale, column_query, 1)
    dk_raw, key_term = norm_back(dk_normed, k_raw, k_scale, column_key, 1)
    d_projected = jnp.concatenate(
        [
            dq_raw.reshape(q_width, rows_here).astype(bf16),
            dk_raw.reshape(kv_width, rows_here).astype(bf16),
            d_key_value[:, HD:].reshape(kv_width, rows_here).astype(bf16),
        ],
        axis=0,
    )
    grad_qkv_here = lax.dot_general(
        normed, d_projected, (((0,), (1,)), ((), ())), preferred_element_type=f32
    )
    d_normed = lax.dot_general(
        d_projected, w_qkv, (((0,), (1,)), ((), ())), preferred_element_type=f32
    )
    d_norm_one, attn_gain_term = norm_back(d_normed, inputs, scale_one, gain_attn)
    d_inputs = d_h_one + d_norm_one
    shard_qkv, shard_out, shard_attn_gain, shard_ffn_gain, shard_query_gain, shard_key_gain = (
        lax.psum_scatter(
            grad_qkv_here.astype(jnp.bfloat16), "fsdp", scatter_dimension=0, tiled=True
        ).astype(jnp.float32),
        lax.psum_scatter(
            grad_out_here.astype(jnp.bfloat16), "fsdp", scatter_dimension=0, tiled=True
        ).astype(jnp.float32),
        lax.psum_scatter(
            jnp.sum(attn_gain_term, axis=0).astype(jnp.bfloat16),
            "fsdp",
            scatter_dimension=0,
            tiled=True,
        ).astype(jnp.float32),
        lax.psum_scatter(
            jnp.sum(ffn_gain_term, axis=0).astype(jnp.bfloat16),
            "fsdp",
            scatter_dimension=0,
            tiled=True,
        ).astype(jnp.float32),
        lax.psum_scatter(
            jnp.sum(query_term, axis=(0, 2)).astype(jnp.bfloat16),
            "fsdp",
            scatter_dimension=0,
            tiled=True,
        ).astype(jnp.float32),
        lax.psum_scatter(
            jnp.sum(key_term, axis=(0, 2)).astype(jnp.bfloat16),
            "fsdp",
            scatter_dimension=0,
            tiled=True,
        ).astype(jnp.float32),
    )
    summed_grads = (
        lax.psum(shard_qkv.astype(jnp.bfloat16), "ctx").astype(jnp.float32),
        lax.psum(shard_out.astype(jnp.bfloat16), "ctx").astype(jnp.float32),
        lax.psum(grad_gate_up, "ctx").astype(jnp.float32),
        lax.psum(grad_down, "ctx").astype(jnp.float32),
        lax.psum(shard_attn_gain.astype(jnp.bfloat16), "ctx").astype(jnp.float32),
        lax.psum(shard_ffn_gain.astype(jnp.bfloat16), "ctx").astype(jnp.float32),
        lax.psum(shard_query_gain.astype(jnp.bfloat16), "ctx").astype(jnp.float32),
        lax.psum(shard_key_gain.astype(jnp.bfloat16), "ctx").astype(jnp.float32),
    )
    return (
        output[None],
        d_inputs[None],
        summed_grads[0],
        summed_grads[1],
        summed_grads[2],
        summed_grads[3],
        summed_grads[4],
        summed_grads[5],
        summed_grads[6],
        summed_grads[7],
    )


def solution(mesh):
    block = mesh.shape["fsdp"] == 2 and mesh.shape["ctx"] == 16
    return jax.shard_map(
        on_block if block else on_device,
        mesh=mesh,
        in_specs=(
            P("fsdp", "ctx", None),
            P("fsdp", None),
            P("fsdp", None),
            P("fsdp", None, None),
            P("fsdp", None),
            P("fsdp"),
            P("fsdp"),
            P("fsdp"),
            P("fsdp"),
            P("fsdp", None),
            P("fsdp", None),
            P("fsdp", "ctx", None),
        ),
        out_specs=(
            P("fsdp", "ctx", None),
            P("fsdp", "ctx", None),
            P("fsdp", None),
            P("fsdp", None),
            P("fsdp", None, None),
            P("fsdp", None),
            P("fsdp"),
            P("fsdp"),
            P("fsdp"),
            P("fsdp"),
        ),
        check_vma=False,
    )
```

```python
import functools

import jax
import jax.numpy as jnp
from jax import lax
from jax.experimental import pallas as pl
from jax.experimental.pallas import tpu as pltpu
from jax.sharding import PartitionSpec as P

HEADS = 16
KV_HEADS = 8
HD = 64
BLK = 128
TILE = 256
CHUNKS = 2


EPSILON = 1e-05
ROPE_BASE = 1000000.0
LOG2E = 1.4426950408889634
SCORE_SCALE = LOG2E * HD ** (-0.5)


def rms_scale(values, axis=-1):
    return lax.rsqrt(jnp.mean(values * values, axis=axis, keepdims=True) + EPSILON)


def norm_back(grad_normed, inputs, scale, gain, axis=-1):
    scaled = grad_normed * gain
    grad_in = scale * scaled - inputs * scale * scale * scale * jnp.mean(
        scaled * inputs, axis=axis, keepdims=True
    )
    return (grad_in, grad_normed * inputs * scale)


def rope(values, cosine, sine):
    half = HD // 2
    first, second = values[:, :half], values[:, half:]
    return jnp.concatenate([first * cosine - second * sine, second * cosine + first * sine], axis=1)


def rope_back(values, cosine, sine):
    half = HD // 2
    first, second = values[:, :half], values[:, half:]
    return jnp.concatenate([first * cosine + second * sine, second * cosine - first * sine], axis=1)


def starts_of(packed, lengths_row):
    ends = jnp.cumsum(lengths_row)
    past = packed[:, None] >= ends[None, :]
    return jnp.sum(jnp.where(past, lengths_row[None, :], 0), axis=1)


def block_tables(order, lengths_row):
    count = order.shape[0]
    rank = jnp.sum((order[None, :] < order[:, None]).astype(jnp.int32), axis=1)
    hit = rank[None, :] == jnp.arange(count, dtype=jnp.int32)[:, None]
    slot = jnp.sum(jnp.where(hit, jnp.arange(count, dtype=jnp.int32)[None, :], 0), axis=1)
    block = jnp.sum(jnp.where(hit, order[None, :], 0), axis=1)
    place = (block[:, None] * BLK + jnp.arange(BLK, dtype=jnp.int32)[None, :]).reshape(-1)
    return (slot, place, starts_of(place, lengths_row))


def attend_kernel(
    q_slot, kv_slot, first, last, qkv_ref, place_ref, start_ref,
    out_ref, q_ref, qt_ref, k_ref, kt_ref, v_ref, ot_ref, total_ref, vt_ref
):
    per_device = qkv_ref.shape[2] // BLK
    kv_blocks = k_ref.shape[0] // BLK
    q_blocks = q_ref.shape[0] // BLK

    def piece(slot, lower):
        return qkv_ref[
            slot // per_device,
            lower : lower + HD,
            pl.ds(pl.multiple_of((slot % per_device) * BLK, BLK), BLK),
        ]

    for i in range(kv_blocks):
        here = slice(i * BLK, (i + 1) * BLK)
        keys = piece(kv_slot[i], HD)
        kt_ref[:, here] = keys
        k_ref[here, :] = keys.T
        values = piece(kv_slot[i], 2 * HD)
        vt_ref[:, here] = values
        v_ref[here, :] = values.T
    for i in range(q_blocks):
        here = slice(i * BLK, (i + 1) * BLK)
        queries = piece(q_slot[i], 0)
        qt_ref[:, here] = queries
        q_ref[here, :] = queries.T
    if q_blocks < kv_blocks:
        out_ref[...] = jnp.zeros_like(out_ref)

    def tile(i, carry):
        rows = pl.ds(pl.multiple_of(i * TILE, TILE), TILE)
        queries = qt_ref[:, rows]
        place = place_ref[:, rows]
        start = start_ref[:, rows]

        def step(j, state):
            total, summed = state
            at = pl.multiple_of(j * TILE, TILE)
            scores = jnp.dot(
                k_ref[pl.ds(at, TILE), :], queries, preferred_element_type=jnp.float32
            )
            key_place = lax.broadcasted_iota(jnp.int32, (TILE, TILE), 0) + at
            allowed = (key_place <= place) & (key_place >= start)
            lifted = jnp.where(allowed, jnp.exp2(scores * SCORE_SCALE), 0.0)
            total = total + jnp.sum(lifted, axis=0, keepdims=True)
            summed = summed + jnp.dot(
                vt_ref[:, pl.ds(at, TILE)],
                lifted.astype(jnp.bfloat16),
                preferred_element_type=jnp.float32,
            )
            return (total, summed)

        total, summed = lax.fori_loop(
            first[i],
            last[i],
            step,
            (jnp.zeros((1, TILE), jnp.float32), jnp.zeros((HD, TILE), jnp.float32)),
        )
        attn = summed / total
        ot_ref[:, rows] = attn
        total_ref[:, rows] = jnp.log(total) * LOG2E
        rounded = attn.astype(jnp.bfloat16)
        for part in range(TILE // BLK):
            slot = q_slot[i * (TILE // BLK) + part]
            out_ref[
                slot // per_device,
                :,
                pl.ds(pl.multiple_of((slot % per_device) * BLK, BLK), BLK),
            ] = rounded[:, part * BLK : (part + 1) * BLK]
        return carry

    lax.fori_loop(0, q_blocks * BLK // TILE, tile, 0)


def attend_back_kernel(
    q_slot, kv_slot, first, last, d_ref, place_ref, start_ref,
    q_ref, qt_ref, k_ref, kt_ref, v_ref, ot_ref, total_ref,
    out_ref, dt_ref, do_ref, dk_ref, dv_ref
):
    per_device = d_ref.shape[2] // BLK
    kv_blocks = k_ref.shape[0] // BLK
    q_blocks = q_ref.shape[0] // BLK

    def lanes(slot):
        return pl.ds(pl.multiple_of((slot % per_device) * BLK, BLK), BLK)

    for i in range(q_blocks):
        here = slice(i * BLK, (i + 1) * BLK)
        slot = q_slot[i]
        grads = d_ref[slot // per_device, :, lanes(slot)]
        dt_ref[:, here] = grads
        do_ref[here, :] = grads.T
    dk_ref[...] = jnp.zeros_like(dk_ref)
    dv_ref[...] = jnp.zeros_like(dv_ref)
    if q_blocks < kv_blocks:
        out_ref[...] = jnp.zeros_like(out_ref)

    def tile(i, carry):
        rows = pl.ds(pl.multiple_of(i * TILE, TILE), TILE)
        queries = qt_ref[:, rows]
        grads = dt_ref[:, rows]
        place = place_ref[:, rows]
        start = start_ref[:, rows]
        delta = jnp.sum(grads.astype(jnp.float32) * ot_ref[:, rows], axis=0, keepdims=True)
        total = total_ref[:, rows]

        def step(j, d_query):
            at = pl.multiple_of(j * TILE, TILE)
            here = pl.ds(at, TILE)
            scores = jnp.dot(k_ref[here, :], queries, preferred_element_type=jnp.float32)
            key_place = lax.broadcasted_iota(jnp.int32, (TILE, TILE), 0) + at
            allowed = (key_place <= place) & (key_place >= start)
            shares = jnp.where(allowed, jnp.exp2(scores * SCORE_SCALE - total), 0.0)
            d_shares = jnp.dot(v_ref[here, :], grads, preferred_element_type=jnp.float32)
            d_scores = (shares * (d_shares - delta)).astype(jnp.bfloat16)
            dv_ref[here, :] += jnp.dot(
                shares.astype(jnp.bfloat16), do_ref[rows, :], preferred_element_type=jnp.float32
            )
            dk_ref[here, :] += jnp.dot(
                d_scores, q_ref[rows, :], preferred_element_type=jnp.float32
            )
            return d_query + jnp.dot(
                kt_ref[:, here], d_scores, preferred_element_type=jnp.float32
            )

        d_query = lax.fori_loop(first[i], last[i], step, jnp.zeros((HD, TILE), jnp.float32))
        rounded = (d_query * HD ** (-0.5)).astype(jnp.bfloat16)
        for part in range(TILE // BLK):
            slot = q_slot[i * (TILE // BLK) + part]
            out_ref[slot // per_device, 0:HD, lanes(slot)] = rounded[
                :, part * BLK : (part + 1) * BLK
            ]
        return carry

    lax.fori_loop(0, q_blocks * BLK // TILE, tile, 0)
    for i in range(kv_blocks):
        here = slice(i * BLK, (i + 1) * BLK)
        slot = kv_slot[i]
        out_ref[slot // per_device, HD : 2 * HD, lanes(slot)] = (
            (dk_ref[here, :] * HD ** (-0.5)).T.astype(jnp.bfloat16)
        )
        out_ref[slot // per_device, 2 * HD : 3 * HD, lanes(slot)] = (
            dv_ref[here, :].T.astype(jnp.bfloat16)
        )


def kernel_call(kernel, tables, arrays, outs, scratch):
    smem = pl.BlockSpec(memory_space=pltpu.SMEM)
    vmem = pl.BlockSpec(memory_space=pltpu.VMEM)
    return pl.pallas_call(
        kernel,
        out_shape=outs,
        in_specs=[smem] * len(tables) + [vmem] * len(arrays),
        out_specs=[vmem] * len(outs),
        scratch_shapes=scratch,
        compiler_params=pltpu.CompilerParams(vmem_limit_bytes=48 * 1024 * 1024),
        cost_estimate=pl.CostEstimate(
            flops=1, bytes_accessed=24 * 3_000_000, transcendentals=0
        ),
    )(*tables, *arrays)


class Links:
    def __init__(self, ctx_size):
        self.depth = ctx_size // 4
        index = lax.axis_index("ctx")
        self.core = index % 2
        self.y = (index // 2) % 2
        self.side = lax.axis_index("fsdp")
        self.half = ((index // 4 + 1) // 2) % 2
        self.quarter = index % 2 * 2 + self.y
        self.here = jnp.stack([self.half, self.core, self.y, self.side]).astype(jnp.int32)

    def route(self, place):
        pairs = []
        for z in range(self.depth):
            for y in range(2):
                for core in range(2):
                    to_z, to_y, to_core = place(z, y, core)
                    pairs.append(((z * 2 + y) * 2 + core, (to_z * 2 + to_y) * 2 + to_core))
        return pairs

    def over_core(self, value):
        return lax.ppermute(value, "ctx", self.route(lambda z, y, c: (z, y, 1 - c)))

    def over_y(self, value):
        return lax.ppermute(value, "ctx", self.route(lambda z, y, c: (z, 1 - y, c)))

    def over_z(self, value):
        return lax.ppermute(value, "ctx", self.route(lambda z, y, c: (z ^ 1, y, c)))

    def mirror_z(self, value):
        return lax.ppermute(value, "ctx", self.route(lambda z, y, c: (self.depth - 1 - z, y, c)))

    def over_x(self, value):
        return lax.ppermute(value, "fsdp", [(0, 1), (1, 0)])

    def spread_plane(self, value):
        across = self.over_core(value)
        beside = self.over_y(value)
        return (value, across, beside, self.over_core(beside))

    def deal_plane(self, near, give, far):
        beside = self.over_y(far)
        return (near, self.over_core(give), beside, self.over_core(beside))

    def sum_depth(self, kept, got):
        def half(index):
            return add(pick(kept, index, 0), pick(got, index, 0))

        given = self.over_z(half(1 - self.half))
        part = add(half(self.half), given)
        full = add(part, self.mirror_z(part))
        return jnp.stack([full, self.over_z(full)])

    def reduce(self, sent, kept):
        return self.spread_plane(self.sum_depth(kept, self.over_x(sent)))


def pick(value, index, axis):
    return lax.dynamic_index_in_dim(value, index, axis, keepdims=False)


def add(left, right):
    return (left.astype(jnp.float32) + right.astype(jnp.float32)).astype(jnp.bfloat16)


def after(value, *others):
    return lax.optimization_barrier((value, *others))[0]


def contract(left, right, axes):
    return lax.dot_general(
        left, right, ((axes[:1], axes[1:]), ((), ())), preferred_element_type=jnp.float32
    )


PARAMS = pltpu.CompilerParams(vmem_limit_bytes=56 * 1024 * 1024)


def cost(micros):
    return pl.CostEstimate(flops=1, bytes_accessed=micros * 3_000_000, transcendentals=0)


def call_with_here(
    kernel, here, grid, arrays, specs, outs, out_specs, scratch=(), aliases=None, micros=5
):
    return pl.pallas_call(
        kernel,
        grid_spec=pltpu.PrefetchScalarGridSpec(
            num_scalar_prefetch=1,
            grid=grid,
            in_specs=specs,
            out_specs=out_specs,
            scratch_shapes=list(scratch),
        ),
        out_shape=outs,
        input_output_aliases=aliases or {},
        compiler_params=PARAMS,
        cost_estimate=cost(micros),
    )(here, *arrays)


def whole(array):
    rank = len(array.shape)
    return pl.BlockSpec(array.shape, lambda i, here: (0,) * rank)


def project_kernel(here, *refs):
    x_ref, gain_ref, own_ref = refs[:3]
    pieces, q_gain, k_gain, cos_ref, sin_ref = refs[3:7], refs[7], refs[8], refs[9], refs[10]
    d_ref = refs[11]
    sent, weight, q_ref, k_ref, q_scale, k_scale, early_ref, scale_ref = refs[12:]
    core, y, side = here[1], here[2], here[3]
    rows = own_ref.shape[0]
    part = rows // 4
    f32, bf16 = jnp.float32, jnp.bfloat16
    weight[pl.ds(pl.multiple_of(side * rows, rows), rows), :] = own_ref[...]
    for p in range(4):
        at = (1 - side) * rows + (((p % 2) ^ core) * 2 + ((p // 2) ^ y)) * part
        weight[pl.ds(pl.multiple_of(at, part), part), :] = pieces[p][...]
    x = x_ref[...].astype(f32)
    scale = rms_scale(x)
    scale_ref[...] = scale
    normed = (x * scale * gain_ref[...]).astype(bf16)
    early_ref[0] = d_ref[...]
    early_ref[1] = normed
    cosine, sine = cos_ref[...], sin_ref[...]
    half = HD // 2

    def turned(raw, gain, raw_ref, kept_scale, head):
        raw_ref[head * HD : (head + 1) * HD, :] = raw
        scale = rms_scale(raw, 0)
        kept_scale[head : head + 1, :] = scale
        value = raw * scale * gain
        first, second = value[:half], value[half:]
        return jnp.concatenate(
            [first * cosine - second * sine, second * cosine + first * sine], axis=0
        ).astype(bf16)

    per_group = HEADS // KV_HEADS
    for at in range(0, weight.shape[1], 2 * BLK):
        block = jnp.dot(normed, weight[:, at : at + 2 * BLK], preferred_element_type=f32)
        turned_block = block.T
        for n in range(2 * BLK // HD):
            head = at // HD + n
            raw = turned_block[n * HD : (n + 1) * HD, :]
            if head < HEADS:
                sent[head, 0:HD, :] = turned(raw, q_gain[...], q_ref, q_scale, head)
                continue
            head -= HEADS
            if head < KV_HEADS:
                value, row = turned(raw, k_gain[...], k_ref, k_scale, head), HD
            else:
                value, row, head = raw.astype(bf16), 2 * HD, head - KV_HEADS
            for copy in range(per_group):
                sent[head * per_group + copy, row : row + HD, :] = value


def project(here, x, gain, own, pieces, q_gain, k_gain, cosine, sine, d_ffn):
    tokens, width = x.shape
    f32, bf16 = jnp.float32, jnp.bfloat16
    shape = jax.ShapeDtypeStruct
    arrays = [x, gain, own, *pieces, q_gain, k_gain, cosine, sine, d_ffn]
    outs = [
        shape((HEADS, 3 * HD, tokens), bf16),
        shape((width, own.shape[1]), bf16),
        shape((HEADS * HD, tokens), f32),
        shape((KV_HEADS * HD, tokens), f32),
        shape((HEADS, tokens), f32),
        shape((KV_HEADS, tokens), f32),
        shape((2, tokens, width), bf16),
        shape((tokens, 1), f32),
    ]
    return call_with_here(
        project_kernel, here, (1,), arrays, [whole(a) for a in arrays], outs,
        [whole(o) for o in outs], micros=8,
    )


def layer(array, index):
    return pl.BlockSpec((1, *array.shape[1:]), lambda i, here: (index, 0, 0))


def attend_out_kernel(here, *refs):
    attn_ref, x_ref, gain_ref, own_ref = refs[:4]
    pieces = refs[4:12]
    weight, h_ref, scale_ref, late_ref = refs[12:]
    core, y, side = here[1], here[2], here[3]
    rows = own_ref.shape[0]
    part = rows // 4
    weight[pl.ds(pl.multiple_of(side * rows, rows), rows), :] = own_ref[...]
    for p in range(4):
        at = (1 - side) * rows + (((p % 2) ^ core) * 2 + ((p // 2) ^ y)) * part
        for n in range(2):
            piece = pieces[2 * p + n]
            wide = piece.shape[1]
            weight[pl.ds(pl.multiple_of(at, part), part), n * wide : (n + 1) * wide] = piece[...]
    attn = attn_ref[...].T
    late_ref[0] = attn
    h_one = x_ref[...].astype(jnp.float32) + jnp.dot(
        attn, weight[...], preferred_element_type=jnp.float32
    )
    scale = rms_scale(h_one)
    h_ref[...] = h_one
    scale_ref[...] = scale
    late_ref[1] = (h_one * scale * gain_ref[...]).astype(jnp.bfloat16)


def attend_out(here, attn, x, gain, own, pieces):
    tokens, width = x.shape
    f32, bf16 = jnp.float32, jnp.bfloat16
    shape = jax.ShapeDtypeStruct
    part = own.shape[0] // 4
    half = width // 2
    first = pieces[0].shape[1] // half - 2
    arrays = [attn, x, gain, own]
    specs = [whole(a) for a in arrays]
    for piece in pieces:
        for n in range(2):
            arrays.append(piece)
            specs.append(pl.BlockSpec((part, half), lambda i, here, n=n: (0, first + n)))
    outs = [
        shape((width, width), bf16),
        shape((tokens, width), f32),
        shape((tokens, 1), f32),
        shape((2, tokens, width), bf16),
    ]
    return call_with_here(
        attend_out_kernel, here, (1,), arrays, specs, outs, [whole(o) for o in outs], micros=5
    )


def ffn_kernel(chunk, here, *refs):
    two_ref, d_ref, own_ref = refs[:3]
    gate_pieces, up_pieces, down_ref, down_pieces = refs[3:7], refs[7:11], refs[11], refs[12:16]
    before_out, before_two = refs[16:18]
    near, give, far, out_ref, d_two_ref = refs[18:23]
    weight, down, hidden_rows = refs[23:26]
    core, y, side = here[1], here[2], here[3]
    t = pl.program_id(0)
    f32, bf16 = jnp.float32, jnp.bfloat16
    own_rows = own_ref.shape[1]
    part = own_rows // 4

    @pl.when(t == 0)
    def _():
        out_ref[...] = before_out[...]
        d_two_ref[...] = before_two[...]

    def quarter(p):
        return ((p % 2) ^ core) * 2 + ((p // 2) ^ y)

    weight[:, pl.ds(pl.multiple_of(side * own_rows, own_rows), own_rows), :] = own_ref[...]
    for p in range(4):
        at = pl.multiple_of((1 - side) * own_rows + quarter(p) * part, part)
        weight[0, pl.ds(at, part), :] = gate_pieces[p][...]
        weight[1, pl.ds(at, part), :] = up_pieces[p][...]

    @pl.when(side == chunk)
    def _():
        down[...] = down_ref[...]

    @pl.when(side != chunk)
    def _():
        for p in range(4):
            wide = down_pieces[p].shape[1]
            at = pl.multiple_of(quarter(p) * wide, wide)
            down[:, pl.ds(at, wide)] = down_pieces[p][...]

    two = two_ref[0]
    d_ffn = d_ref[...]
    tile = own_ref.shape[2]
    first = (tile // 2) // 256 * 256
    for begin, end in ((0, first), (first, tile)):
        at = slice(begin, end)
        gate = jnp.dot(two, weight[0, :, at], preferred_element_type=f32)
        upper = jnp.dot(two, weight[1, :, at], preferred_element_type=f32)
        d_hidden = contract(d_ffn, down[at, :], (1, 1))
        sigma = jax.nn.sigmoid(gate)
        silu = gate * sigma
        hidden = (silu * upper).astype(bf16)
        d_gate = (d_hidden * upper * sigma * (1.0 + gate * (1.0 - sigma))).astype(bf16)
        d_upper = (d_hidden * silu).astype(bf16)
        out_ref[...] += jnp.dot(hidden, down[at, :], preferred_element_type=f32)
        d_two_ref[...] += contract(d_gate, weight[0, :, at], (1, 1)) + contract(
            d_upper, weight[1, :, at], (1, 1)
        )
        hidden_rows[:, at] = hidden
        mine = jnp.where(core == 0, d_gate, d_upper)
        other = jnp.where(core == 0, d_upper, d_gate)

        @pl.when(t == y)
        def _(mine=mine, other=other, at=at):
            near[:, at] = mine
            give[:, at] = other

        @pl.when(t != y)
        def _(mine=mine, other=other, at=at):
            far[0, :, at] = mine
            far[1, :, at] = other

    share = tile // 2
    lower, upper = hidden_rows[:, :share], hidden_rows[:, share:]
    close = jnp.where(y == 0, lower, upper)
    distant = jnp.where(y == 0, upper, lower)
    at = slice(tile, tile + share)

    @pl.when(t == core)
    def _():
        near[:, at] = close
        far[0, :, at] = distant

    @pl.when(t != core)
    def _():
        give[:, at] = close
        far[1, :, at] = distant


def ffn(here, chunk, late, d_ffn, own, pieces, down, down_pieces, before):
    _, tokens, width = late.shape
    tile = own.shape[2] // 4
    padded = (tile + tile // 2 + BLK - 1) // BLK * BLK
    shape = jax.ShapeDtypeStruct
    f32, bf16 = jnp.float32, jnp.bfloat16
    outs = [shape((tokens, padded), bf16)] * 2 + [shape((2, tokens, padded), bf16)]
    outs += [shape((tokens, width), f32)] * 2

    def own_down(t, here):
        return (jnp.where(here[3] == chunk, t, 0), 0)

    def other_down(t, here):
        return (jnp.where(here[3] == chunk, 0, t), 0)

    part = own.shape[1] // 4
    specs = (
        [layer(late, 1), whole(d_ffn)]
        + [pl.BlockSpec((2, own.shape[1], tile), lambda t, here: (0, 0, 2 * chunk + t))]
        + [pl.BlockSpec((part, tile), lambda t, here: (0, t))] * 4
        + [pl.BlockSpec((part, tile), lambda t, here: (0, 2 + t))] * 4
        + [pl.BlockSpec((tile, width), own_down)]
        + [pl.BlockSpec((tile, width // 4), other_down)] * 4
        + [whole(before[0]), whole(before[1])]
    )
    got = call_with_here(
        functools.partial(ffn_kernel, chunk),
        here,
        (2,),
        [late, d_ffn, own, *pieces, *pieces, down, *down_pieces, *before],
        specs,
        outs,
        [whole(o) for o in outs],
        [
            pltpu.VMEM((2, width, tile), bf16),
            pltpu.VMEM((tile, width), bf16),
            pltpu.VMEM((tokens, tile), bf16),
        ],
        micros=20,
    )
    return got[:3], got[3:]


def dealt(shares):
    return list(shares), [whole(shares[0]), whole(shares[1]), layer(shares[2], 0), layer(shares[3], 1)]


def flat(ref):
    return ref[...] if len(ref.shape) == 2 else ref[0]


def wide_product_kernel(here, *refs):
    planes, terms = refs[:4], refs[4:8]
    sent, kept, left, right = refs[8:]
    tokens = planes[0].shape[1]
    columns = right.shape[1]
    for i in range(4):
        left[:, i * tokens : (i + 1) * tokens] = planes[i][0].T
        right[i * tokens : (i + 1) * tokens, :] = flat(terms[i])[:, :columns]
    side = here[3]
    _, step, _ = kept.shape
    for half in range(2):
        for owner, out_ref in ((1 - side, sent), (side, kept)):
            place = pl.multiple_of(owner * 2 * step + half * step, step)
            out_ref[half] = jnp.dot(
                left[pl.ds(place, step), :], right[...], preferred_element_type=jnp.float32
            ).astype(out_ref.dtype)


def wide_products(here, late_plane, shares, columns):
    _, tokens, rows = late_plane[0].shape
    outs = [
        jax.ShapeDtypeStruct((2, rows // 4, columns), jnp.bfloat16),
        jax.ShapeDtypeStruct((2, rows // 4, columns), jnp.float32),
    ]
    arrays, specs = dealt(shares)
    return call_with_here(
        wide_product_kernel,
        here,
        (1,),
        [*late_plane, *arrays],
        [layer(a, 1) for a in late_plane] + specs,
        outs,
        [whole(o) for o in outs],
        [
            pltpu.VMEM((rows, 4 * tokens), jnp.bfloat16),
            pltpu.VMEM((4 * tokens, columns), jnp.bfloat16),
        ],
        micros=8,
    )


def down_product_kernel(here, *refs):
    planes, terms = refs[:4], (refs[4:8], refs[8:12])
    sent, kept, left, right = refs[12:]
    tokens = planes[0].shape[1]
    rows = left.shape[0]
    for i in range(4):
        right[i * tokens : (i + 1) * tokens, :] = planes[i][0]
    for chunk in range(2):
        for i in range(4):
            share = flat(terms[chunk][i])
            at = share.shape[1] // BLK * BLK - (rows + BLK - 1) // BLK * BLK
            left[:, i * tokens : (i + 1) * tokens] = share[:, at : at + rows].T
        for half in range(2):
            product = jnp.dot(
                left[half * rows // 2 : (half + 1) * rows // 2, :],
                right[...],
                preferred_element_type=jnp.float32,
            )

            @pl.when(here[3] == chunk)
            def _(product=product, half=half):
                kept[half] = product

            @pl.when(here[3] != chunk)
            def _(product=product, half=half):
                sent[half] = product.astype(sent.dtype)


def down_products(here, early_plane, first, second, rows):
    _, tokens, columns = early_plane[0].shape
    outs = [
        jax.ShapeDtypeStruct((2, rows // 2, columns), jnp.bfloat16),
        jax.ShapeDtypeStruct((2, rows // 2, columns), jnp.float32),
    ]
    first, first_specs = dealt(first)
    second, second_specs = dealt(second)
    return call_with_here(
        down_product_kernel,
        here,
        (1,),
        [*early_plane, *first, *second],
        [layer(a, 0) for a in early_plane] + first_specs + second_specs,
        outs,
        [whole(o) for o in outs],
        [
            pltpu.VMEM((rows, 4 * tokens), jnp.bfloat16),
            pltpu.VMEM((4 * tokens, columns), jnp.bfloat16),
        ],
        micros=8,
    )


GAIN_ROWS = 16


def attention_back_kernel(here, *refs):
    d_ref, q_ref, k_ref, q_scale, k_scale, q_gain, k_gain, cos_ref, sin_ref = refs[:9]
    weight, x_ref, scale_ref, gain_ref, d_h_ref, d_attn_ref = refs[9:15]
    near, give, far, d_x_ref, gains_ref = refs[15:20]
    turned, natural = refs[20:]
    f32, bf16 = jnp.float32, jnp.bfloat16
    core, y = here[1], here[2]
    cosine, sine = cos_ref[...], sin_ref[...]
    half = HD // 2
    per_group = HEADS // KV_HEADS
    tokens = x_ref.shape[0]

    def back(grad, raw, scale, gain):
        first, second = grad[:half], grad[half:]
        normed = jnp.concatenate(
            [first * cosine + second * sine, second * cosine - first * sine], axis=0
        )
        return norm_back(normed, raw, scale, gain, 0)

    q_term = jnp.zeros((HD, tokens), f32)
    k_term = jnp.zeros((HD, tokens), f32)
    for head in range(HEADS):
        at = slice(head * HD, (head + 1) * HD)
        grad, term = back(
            d_ref[head, :HD, :].astype(f32), q_ref[at, :], q_scale[head : head + 1, :], q_gain[...]
        )
        turned[at, :] = grad.astype(bf16)
        q_term = q_term + term
    for head in range(KV_HEADS):
        at = slice(head * HD, (head + 1) * HD)
        both = d_ref[head * per_group, HD:, :].astype(f32)
        for other in range(1, per_group):
            both = both + d_ref[head * per_group + other, HD:, :].astype(f32)
        grad, term = back(both[:HD], k_ref[at, :], k_scale[head : head + 1, :], k_gain[...])
        place = HEADS * HD + head * HD
        turned[place : place + HD, :] = grad.astype(bf16)
        k_term = k_term + term
        place += KV_HEADS * HD
        turned[place : place + HD, :] = both[HD:].astype(bf16)
    rows = turned.shape[0] // 4
    columns = d_attn_ref.shape[1] // 4
    shares = (
        (near, None, core, y), (give, None, 1 - core, y), (far, 0, core, 1 - y), (far, 1, 1 - core, 1 - y),
    )
    for out_ref, index, to_core, to_y in shares:
        share = to_core * 2 + to_y
        first = turned[pl.ds(pl.multiple_of(share * rows, rows), rows), :]
        second = d_attn_ref[:, pl.ds(pl.multiple_of(share * columns, columns), columns)]
        if index is None:
            out_ref[:rows, :] = first
            out_ref[rows:, :] = second
        else:
            out_ref[index, :rows, :] = first
            out_ref[index, rows:, :] = second
    for at in range(0, turned.shape[0], 256):
        natural[:, at : at + 256] = turned[at : at + 256, :].T
    d_normed = contract(natural[...], weight[...], (1, 1))
    x = x_ref[...].astype(f32)
    d_norm, gain_term = norm_back(d_normed, x, scale_ref[...], gain_ref[...])
    d_x_ref[...] = d_h_ref[...] + d_norm
    gains_ref[...] = jnp.zeros_like(gains_ref)
    gains_ref[0:1, :] = jnp.sum(gain_term, axis=0, keepdims=True)
    gains_ref[1:2, 0:HD] = jnp.sum(q_term.T, axis=0, keepdims=True)
    gains_ref[2:3, 0:HD] = jnp.sum(k_term.T, axis=0, keepdims=True)


def attention_back(here, arrays):
    f32, bf16 = jnp.float32, jnp.bfloat16
    shape = jax.ShapeDtypeStruct
    weight, x = arrays[9], arrays[10]
    tokens, width = x.shape
    rows = weight.shape[1] // 4 + tokens
    assert width // 4 == tokens
    outs = [
        shape((rows, tokens), bf16),
        shape((rows, tokens), bf16),
        shape((2, rows, tokens), bf16),
        shape((tokens, width), f32),
        shape((8, width), f32),
    ]
    return call_with_here(
        attention_back_kernel, here, (1,), arrays, [whole(a) for a in arrays], outs,
        [whole(o) for o in outs],
        [pltpu.VMEM((weight.shape[1], tokens), bf16), pltpu.VMEM((tokens, weight.shape[1]), bf16)],
        micros=12,
    )


def attention_product_kernel(here, *refs):
    normed, attn, terms, gains_ref, ffn_gain_ref = refs[:4], refs[4:8], refs[8:12], refs[12], refs[13]
    sent, kept, left, right, left_out, right_out = refs[14:]
    tokens = normed[0].shape[1]
    cut = right.shape[1]
    for i in range(4):
        at = slice(i * tokens, (i + 1) * tokens)
        left[:, at] = normed[i][0].T
        left_out[:, at] = attn[i][0].T
        share = flat(terms[i])
        right[at, :] = share[:cut].T
        right_out[at, :] = share[cut:]
    step = left.shape[0] // 4
    for owner, out_ref in ((1 - here[3], sent), (here[3], kept)):
        for half in range(2):
            at = pl.ds(pl.multiple_of(owner * 2 * step + half * step, step), step)
            out_ref[half, :step, :cut] = jnp.dot(
                left[at, :], right[...], preferred_element_type=jnp.float32
            ).astype(out_ref.dtype)
            out_ref[half, :step, cut:] = jnp.dot(
                left_out[at, :], right_out[...], preferred_element_type=jnp.float32
            ).astype(out_ref.dtype)
        rows = gains_ref.shape[1] // 2
        mine = pl.ds(pl.multiple_of(owner * rows, rows), rows)
        wide = out_ref.shape[2] - rows
        block = jnp.concatenate(
            [
                jnp.concatenate([gains_ref[0:1, mine], gains_ref[1:2, 0:wide]], axis=1),
                jnp.concatenate([ffn_gain_ref[:, mine], gains_ref[2:3, 0:wide]], axis=1),
                jnp.zeros((GAIN_ROWS - 2, out_ref.shape[2]), jnp.float32),
            ],
            axis=0,
        )
        out_ref[0, step:, :] = block.astype(out_ref.dtype)
        out_ref[1, step:, :] = jnp.zeros((GAIN_ROWS, out_ref.shape[2]), out_ref.dtype)


def attention_products(here, early_plane, late_plane, shares, gains, ffn_gain):
    _, tokens, width = early_plane[0].shape
    cut = shares[0].shape[0] - tokens
    shape = (2, width // 4 + GAIN_ROWS, cut + tokens)
    outs = [jax.ShapeDtypeStruct(shape, jnp.bfloat16), jax.ShapeDtypeStruct(shape, jnp.float32)]
    arrays, specs = dealt(shares)
    return call_with_here(
        attention_product_kernel,
        here,
        (1,),
        [*early_plane, *late_plane, *arrays, gains, ffn_gain],
        [layer(a, 1) for a in early_plane]
        + [layer(a, 0) for a in late_plane]
        + specs
        + [whole(gains), whole(ffn_gain)],
        outs,
        [whole(o) for o in outs],
        [
            pltpu.VMEM((width, 4 * tokens), jnp.bfloat16),
            pltpu.VMEM((4 * tokens, cut), jnp.bfloat16),
            pltpu.VMEM((width, 4 * tokens), jnp.bfloat16),
            pltpu.VMEM((4 * tokens, tokens), jnp.bfloat16),
        ],
        micros=8,
    )


def place_gate_up_kernel(here, *refs):
    mine, across, beside, diagonal, out_ref = *refs[:4], refs[-1]
    pieces = (mine, across, beside, diagonal)
    wide = mine.shape[2]
    for case in range(4):
        core, y = case // 2, case % 2

        @pl.when((here[1] == core) & (here[2] == y))
        def _(core=core, y=y):
            for kind in range(2):
                for column in range(2):
                    value = pieces[(y ^ column) * 2 + (core ^ kind)][0]
                    out_ref[:, kind, column * wide : (column + 1) * wide] = value.astype(
                        jnp.float32
                    )


def place_gate_up(here, chunk, pieces, before):
    _, rows, wide = pieces[0].shape
    step = 64
    blocks = rows // step

    def source(i, here):
        return ((i // blocks) ^ here[0], i % blocks, 0)

    arrays = list(pieces)
    specs = [pl.BlockSpec((1, step, wide), source)] * 4
    aliases = {}
    if before is not None:
        arrays.append(before)
        specs.append(pl.BlockSpec(memory_space=pl.ANY))
        aliases = {5: 0}
    (out,) = call_with_here(
        place_gate_up_kernel,
        here,
        (2 * blocks,),
        arrays,
        specs,
        [jax.ShapeDtypeStruct((2 * rows, 2, 2 * wide * CHUNKS), jnp.float32)],
        [pl.BlockSpec((step, 2, 2 * wide), lambda i, here: (i, 0, chunk))],
        aliases=aliases,
        micros=10,
    )
    return out


def place_down(here, pieces):
    _, rows, columns = pieces[0].shape

    def kernel(here, *refs):
        for s in range(8):

            @pl.when(pl.program_id(0) == s)
            def _(s=s):
                refs[4][...] = refs[s % 4][s // 4].astype(jnp.float32)

    def target(s, here):
        half = (s // 4) ^ here[0]
        y = ((s // 2) % 2) ^ here[2]
        core = (s % 2) ^ here[1]
        return ((core * 2 + y) * 2 + half, 0)

    (out,) = call_with_here(
        kernel,
        here,
        (8,),
        list(pieces),
        [whole(v) for v in pieces],
        [jax.ShapeDtypeStruct((rows * 8, columns), jnp.float32)],
        [pl.BlockSpec((rows, columns), target)],
    )
    return out


def place_attention(here, pieces, cut):
    _, rows, columns = pieces[0].shape
    rows -= GAIN_ROWS

    def kernel(here, *refs):
        qkv_ref, out_ref, gains_ref = refs[4:]
        for s in range(8):

            @pl.when(pl.program_id(0) == s)
            def _(s=s):
                value = refs[s % 4][s // 4]
                qkv_ref[...] = value[:rows, :cut].astype(jnp.float32)
                out_ref[...] = value[:rows, cut:].astype(jnp.float32)
                gains = value[rows:].astype(jnp.float32)
                gains_ref[...] = gains if s == 0 else gains_ref[...] + gains

    def target(s, here):
        half = (s // 4) ^ here[0]
        return (half, ((s % 2) ^ here[1]) * 2 + (((s // 2) % 2) ^ here[2]))

    shape = jax.ShapeDtypeStruct
    f32 = jnp.float32
    gain_shape = (GAIN_ROWS, columns)
    return call_with_here(
        kernel,
        here,
        (8,),
        list(pieces),
        [whole(v) for v in pieces],
        [
            shape((2 * rows, 4 * cut), f32),
            shape((2 * rows, 4 * (columns - cut)), f32),
            shape(gain_shape, f32),
        ],
        [
            pl.BlockSpec((rows, cut), target),
            pl.BlockSpec((rows, columns - cut), target),
            pl.BlockSpec(gain_shape, lambda s, here: (0, 0)),
        ],
    )


def on_block(
    tokens,
    qkv_weight,
    out_weight,
    gate_up_weight,
    down_weight,
    attn_gain,
    ffn_gain,
    query_gain,
    key_gain,
    seq_lengths,
    block_order,
    cotangent,
):
    inputs = tokens[0].astype(jnp.float32)
    rows_here = inputs.shape[0]
    ctx_size = lax.axis_size("ctx")
    ctx_index = lax.axis_index("ctx")
    per_group = HEADS // KV_HEADS
    q_width = HEADS * HD
    kv_width = KV_HEADS * HD
    order_row = block_order[0]
    lengths_row = seq_lengths[0]
    slots = jnp.arange(rows_here, dtype=jnp.int32) // BLK + ctx_index * (rows_here // BLK)
    table = slots[:, None] == jnp.arange(order_row.shape[0], dtype=jnp.int32)[None, :]
    packed = (
        jnp.sum(jnp.where(table, order_row[None, :], 0), axis=1) * BLK
        + jnp.arange(rows_here, dtype=jnp.int32) % BLK
    )
    local = packed - starts_of(packed, lengths_row)
    frequency = ROPE_BASE ** (-2.0 * jnp.arange(HD // 2, dtype=jnp.float32) / HD)
    angle = frequency[:, None] * local.astype(jnp.float32)[None, :]
    cosine = jnp.cos(angle)[None]
    sine = jnp.sin(angle)[None]
    bf16, f32 = jnp.bfloat16, jnp.float32
    parts = ctx_size // HEADS
    part = ctx_index // HEADS
    part_blocks = HEADS * rows_here // BLK
    q_order = lax.dynamic_slice_in_dim(order_row, part * part_blocks, part_blocks)
    q_slot, q_place, q_start = block_tables(q_order, lengths_row)
    q_slot = q_slot + part * part_blocks
    kv_slot, _, _ = block_tables(order_row, lengths_row)
    first = jnp.min(q_start.reshape(-1, TILE), axis=1) // TILE
    last = jnp.max(q_place.reshape(-1, TILE), axis=1) // TILE + 1
    tables = (q_slot, kv_slot, first, last)
    q_rows, kv_rows = part_blocks * BLK, order_row.shape[0] * BLK

    links = Links(ctx_size)
    here = links.here
    width = inputs.shape[1]
    rows = qkv_weight.shape[0]
    part_rows = rows // 4

    def quarter_rows(weight):
        return lax.dynamic_slice_in_dim(weight, links.quarter * part_rows, part_rows)

    gains_here = jnp.concatenate([attn_gain, ffn_gain, query_gain, key_gain])
    gains_there = links.over_x(gains_here)

    def gain_of(at, size):
        mine, other = gains_here[at : at + size], gains_there[at : at + size]
        return jnp.where(
            links.side == 0, jnp.concatenate([mine, other]), jnp.concatenate([other, mine])
        ).astype(f32)

    gain_attn = gain_of(0, rows)
    gain_ffn = gain_of(rows, rows)
    gain_query = gain_of(2 * rows, HD // 2)
    gain_key = gain_of(2 * rows + HD // 2, HD // 2)
    ff_chunk = gate_up_weight.shape[2] // CHUNKS

    def gate_up_piece(chunk):
        piece = lax.dynamic_slice(
            gate_up_weight,
            (links.quarter * part_rows, 0, chunk * ff_chunk),
            (part_rows, 2, ff_chunk),
        )
        return [piece[:, 0], piece[:, 1]]

    qkv_there = links.over_x(quarter_rows(qkv_weight))
    first_piece = jnp.concatenate([*gate_up_piece(0), quarter_rows(out_weight)], axis=1)
    second_piece = jnp.concatenate(gate_up_piece(1), axis=1)
    down_piece = lax.dynamic_slice_in_dim(
        down_weight, links.quarter * (width // 4), width // 4, 1
    )
    d_ffn = cotangent[0]
    tokens_here = tokens[0]
    qkv_there = after(qkv_there, first_piece)
    first_there = links.over_x(after(first_piece, qkv_there))
    gate_up = jnp.transpose(after(gate_up_weight, qkv_there), (1, 0, 2))
    qkv_beside = links.over_y(qkv_there)
    qkv_pieces = (
        qkv_there,
        links.over_core(qkv_there),
        qkv_beside,
        links.over_core(after(qkv_beside, gate_up)),
    )
    sent, w_qkv, q_raw, k_raw, q_scale, k_scale, early, scale_one = project(
        here, tokens_here, gain_attn[None], qkv_weight, qkv_pieces,
        gain_query[:, None], gain_key[:, None], cosine[0], sine[0], d_ffn,
    )
    got = lax.all_to_all(sent, "ctx", 0, 0, tiled=True)
    early_beside = links.over_y(early)
    first_there = after(first_there, sent)
    down_there = links.over_x(after(down_piece, first_there))
    first_beside = links.over_y(first_there)
    second_there = links.over_x(after(second_piece, down_there))
    down_beside = links.over_y(down_there)
    got = after(got, down_there)
    q_place, q_start = q_place[None], q_start[None]
    shape = jax.ShapeDtypeStruct
    attn_sent, *held = kernel_call(
        attend_kernel,
        tables,
        (got, q_place, q_start),
        [
            shape((ctx_size, HD, rows_here), bf16),
            shape((q_rows, HD), bf16),
            shape((HD, q_rows), bf16),
            shape((kv_rows, HD), bf16),
            shape((HD, kv_rows), bf16),
            shape((kv_rows, HD), bf16),
            shape((HD, q_rows), f32),
            shape((1, q_rows), f32),
        ],
        [pltpu.VMEM((HD, kv_rows), bf16)],
    )
    attn_in = lax.dynamic_slice_in_dim(
        lax.all_to_all(attn_sent, "ctx", 0, 0, tiled=True), part * HEADS, HEADS
    ).reshape(q_width, rows_here)
    second_there = after(second_there, attn_sent)

    def spread(there, beside):
        there, beside = after(there, attn_sent), after(beside, attn_sent)
        return (there, links.over_core(there), beside, links.over_core(beside))

    first_pieces = spread(first_there, first_beside)
    down_pieces = spread(down_there, down_beside)
    second_pieces = links.spread_plane(second_there)
    w_out, h_one, scale_two, late = attend_out(
        here, attn_in, tokens_here, gain_ffn[None], out_weight, first_pieces
    )
    late_plane = links.spread_plane(late)
    sums = [h_one, jnp.zeros_like(h_one)]
    shares = []
    for chunk, pieces in enumerate((first_pieces, second_pieces)):
        dealt_here, sums = ffn(
            here, chunk, late, d_ffn, gate_up, pieces, down_weight, down_pieces, sums
        )
        shares.append(links.deal_plane(*dealt_here))
        if chunk == 0:
            early = after(early, sums[0])
            early_plane = (
                early, links.over_core(early), early_beside,
                links.over_core(after(early_beside, sums[0])),
            )
    columns = ff_chunk // 2
    output = sums[0].astype(bf16)
    d_norm_two, ffn_gain_term = norm_back(sums[1], h_one, scale_two, gain_ffn)
    d_h_one = d_ffn.astype(f32) + d_norm_two
    d_attn = d_h_one.astype(bf16)
    d_heads = lax.dot_general(
        w_out, d_attn, (((1,), (1,)), ((), ())), preferred_element_type=f32
    ).astype(bf16)
    d_heads = jnp.concatenate([d_heads.reshape(HEADS, HD, rows_here)] * parts, axis=0)
    d_got = lax.all_to_all(d_heads, "ctx", 0, 0, tiled=True)
    first_shares = [after(v, d_heads) for v in shares[0]]
    first_products = wide_products(here, late_plane, first_shares, columns)
    d_got = after(d_got, first_products[0])
    (d_sent,) = kernel_call(
        attend_back_kernel,
        tables,
        (d_got, q_place, q_start, *held),
        [shape((ctx_size, 3 * HD, rows_here), bf16)],
        [
            pltpu.VMEM((HD, q_rows), bf16),
            pltpu.VMEM((q_rows, HD), bf16),
            pltpu.VMEM((kv_rows, HD), f32),
            pltpu.VMEM((kv_rows, HD), f32),
        ],
    )
    d_back = lax.all_to_all(d_sent, "ctx", 0, 0, tiled=True)
    second_shares = [after(v, d_sent) for v in shares[1]]
    second_products = wide_products(here, late_plane, second_shares, columns)
    *d_shares, d_inputs, gain_sums = attention_back(
        here,
        [
            d_back, q_raw, k_raw, q_scale, k_scale, gain_query[:, None], gain_key[:, None],
            cosine[0], sine[0], w_qkv, tokens_here, scale_one, gain_attn[None], d_h_one, d_attn,
        ],
    )
    grad_gate_up = None
    for chunk, products in enumerate((first_products, second_products)):
        grad_gate_up = place_gate_up(here, chunk, links.reduce(*products), grad_gate_up)
    grad_down = place_down(
        here, links.reduce(*down_products(here, early_plane, *shares, columns // 2))
    )
    attention_terms = attention_products(
        here, early_plane, late_plane, links.deal_plane(*d_shares), gain_sums,
        jnp.sum(ffn_gain_term, axis=0, keepdims=True),
    )
    cut = qkv_weight.shape[1] // 4
    grad_qkv, grad_out, gain_sums = place_attention(here, links.reduce(*attention_terms), cut)
    at = links.side * (HD // 2)
    gain_grads = [
        gain_sums[0, :rows],
        gain_sums[1, :rows],
        lax.dynamic_slice_in_dim(gain_sums[0, rows : rows + HD], at, HD // 2),
        lax.dynamic_slice_in_dim(gain_sums[1, rows : rows + HD], at, HD // 2),
    ]
    return (
        output[None],
        d_inputs[None],
        grad_qkv,
        grad_out,
        grad_gate_up,
        grad_down,
        *gain_grads,
    )


def on_device(
    tokens,
    qkv_weight,
    out_weight,
    gate_up_weight,
    down_weight,
    attn_gain,
    ffn_gain,
    query_gain,
    key_gain,
    seq_lengths,
    block_order,
    cotangent,
):
    inputs = tokens[0].astype(jnp.float32)
    rows_here = inputs.shape[0]
    ctx_size = lax.axis_size("ctx")
    ctx_index = lax.axis_index("ctx")
    per_group = HEADS // KV_HEADS
    q_width = HEADS * HD
    kv_width = KV_HEADS * HD
    order_row = block_order[0]
    lengths_row = seq_lengths[0]
    slots = jnp.arange(rows_here, dtype=jnp.int32) // BLK + ctx_index * (rows_here // BLK)
    table = slots[:, None] == jnp.arange(order_row.shape[0], dtype=jnp.int32)[None, :]
    packed = (
        jnp.sum(jnp.where(table, order_row[None, :], 0), axis=1) * BLK
        + jnp.arange(rows_here, dtype=jnp.int32) % BLK
    )
    local = packed - starts_of(packed, lengths_row)
    frequency = ROPE_BASE ** (-2.0 * jnp.arange(HD // 2, dtype=jnp.float32) / HD)
    angle = frequency[:, None] * local.astype(jnp.float32)[None, :]
    cosine = jnp.cos(angle)[None]
    sine = jnp.sin(angle)[None]
    bf16, f32 = jnp.bfloat16, jnp.float32
    parts = ctx_size // HEADS
    part = ctx_index // HEADS
    part_blocks = HEADS * rows_here // BLK
    q_order = lax.dynamic_slice_in_dim(order_row, part * part_blocks, part_blocks)
    q_slot, q_place, q_start = block_tables(q_order, lengths_row)
    q_slot = q_slot + part * part_blocks
    kv_slot, _, _ = block_tables(order_row, lengths_row)
    first = jnp.min(q_start.reshape(-1, TILE), axis=1) // TILE
    last = jnp.max(q_place.reshape(-1, TILE), axis=1) // TILE + 1
    tables = (q_slot, kv_slot, first, last)
    q_rows, kv_rows = part_blocks * BLK, order_row.shape[0] * BLK

    def fetch_attention():
        return (
            lax.all_gather(qkv_weight, "fsdp", axis=0, tiled=True),
            lax.all_gather(out_weight, "fsdp", axis=0, tiled=True),
            lax.all_gather(attn_gain, "fsdp", axis=0, tiled=True),
            lax.all_gather(ffn_gain, "fsdp", axis=0, tiled=True),
            lax.all_gather(query_gain, "fsdp", axis=0, tiled=True),
            lax.all_gather(key_gain, "fsdp", axis=0, tiled=True),
        )

    w_qkv, w_out, gain_attn, gain_ffn, gain_query, gain_key = fetch_attention()
    gain_attn = gain_attn.astype(jnp.float32)
    gain_ffn = gain_ffn.astype(jnp.float32)
    gain_query = gain_query.astype(jnp.float32)
    gain_key = gain_key.astype(jnp.float32)
    scale_one = rms_scale(inputs)
    normed = (inputs * scale_one * gain_attn).astype(jnp.bfloat16)
    projected = lax.dot_general(
        w_qkv, normed, (((0,), (1,)), ((), ())), preferred_element_type=f32
    )
    q_raw = projected[:q_width].reshape(HEADS, HD, rows_here)
    k_raw = projected[q_width : q_width + kv_width].reshape(KV_HEADS, HD, rows_here)
    values_here = projected[q_width + kv_width :].reshape(KV_HEADS, HD, rows_here).astype(bf16)
    q_scale = rms_scale(q_raw, 1)
    k_scale = rms_scale(k_raw, 1)
    column_query, column_key = gain_query[:, None], gain_key[:, None]
    queries = rope(q_raw * q_scale * column_query, cosine, sine).astype(bf16)
    keys_here = rope(k_raw * k_scale * column_key, cosine, sine).astype(bf16)
    sent = jnp.concatenate(
        [queries, jnp.repeat(keys_here, per_group, 0), jnp.repeat(values_here, per_group, 0)], axis=1
    )
    sent = jnp.concatenate([sent] * parts, axis=0)
    got = lax.all_to_all(sent, "ctx", 0, 0, tiled=True)
    q_place, q_start = q_place[None], q_start[None]
    shape = jax.ShapeDtypeStruct
    attn_sent, *held = kernel_call(
        attend_kernel,
        tables,
        (got, q_place, q_start),
        [
            shape((ctx_size, HD, rows_here), bf16),
            shape((q_rows, HD), bf16),
            shape((HD, q_rows), bf16),
            shape((kv_rows, HD), bf16),
            shape((HD, kv_rows), bf16),
            shape((kv_rows, HD), bf16),
            shape((HD, q_rows), f32),
            shape((1, q_rows), f32),
        ],
        [pltpu.VMEM((HD, kv_rows), bf16)],
    )
    attn_in = lax.dynamic_slice_in_dim(
        lax.all_to_all(attn_sent, "ctx", 0, 0, tiled=True), part * HEADS, HEADS
    ).reshape(q_width, rows_here)
    h_one = inputs + lax.dot_general(
        attn_in, w_out, (((0,), (0,)), ((), ())), preferred_element_type=f32
    )
    scale_two = rms_scale(h_one)
    normed_two = (h_one * scale_two * gain_ffn).astype(jnp.bfloat16)
    columns = normed_two
    gate_up = jnp.einsum(
        "tr,rgf->tgf",
        columns,
        lax.all_gather(gate_up_weight, "fsdp", axis=0, tiled=True),
        preferred_element_type=jnp.float32,
    )
    gate = gate_up[:, 0]
    upper = gate_up[:, 1]
    sigma = jax.nn.sigmoid(gate)
    hidden = (gate * sigma * upper).astype(jnp.bfloat16)
    columns = hidden
    ffn_out = jnp.dot(
        columns,
        lax.all_gather(down_weight, "fsdp", axis=0, tiled=True),
        preferred_element_type=jnp.float32,
    )
    output = (h_one + ffn_out).astype(jnp.bfloat16)
    d_out = cotangent[0].astype(jnp.float32)
    d_ffn = d_out.astype(jnp.bfloat16)
    d_hidden = lax.dot_general(
        d_ffn,
        lax.all_gather(down_weight, "fsdp", axis=0, tiled=True),
        (((1,), (1,)), ((), ())),
        preferred_element_type=jnp.float32,
    )
    d_gate = d_hidden * upper * sigma * (1.0 + gate * (1.0 - sigma))
    d_upper = d_hidden * gate * sigma
    d_gate_up = jnp.stack([d_gate, d_upper], axis=1).astype(jnp.bfloat16)
    d_normed_two = jnp.einsum(
        "tgf,rgf->tr",
        d_gate_up,
        lax.all_gather(gate_up_weight, "fsdp", axis=0, tiled=True),
        preferred_element_type=jnp.float32,
    )
    columns = normed_two
    grad_gate_up = lax.psum_scatter(
        jnp.einsum("tr,tgf->rgf", columns, d_gate_up, preferred_element_type=jnp.float32).astype(
            jnp.bfloat16
        ),
        "fsdp",
        scatter_dimension=0,
        tiled=True,
    )
    columns = hidden
    grad_down = lax.psum_scatter(
        lax.dot_general(
            columns, d_ffn, (((0,), (0,)), ((), ())), preferred_element_type=jnp.float32
        ).astype(jnp.bfloat16),
        "fsdp",
        scatter_dimension=0,
        tiled=True,
    )
    d_norm_two, ffn_gain_term = norm_back(d_normed_two, h_one, scale_two, gain_ffn)
    d_h_one = d_out + d_norm_two
    d_attn = d_h_one.astype(jnp.bfloat16)
    grad_out_here = jnp.dot(attn_in, d_attn, preferred_element_type=f32)
    d_heads = lax.dot_general(
        w_out, d_attn, (((1,), (1,)), ((), ())), preferred_element_type=f32
    ).astype(bf16)
    d_heads = jnp.concatenate([d_heads.reshape(HEADS, HD, rows_here)] * parts, axis=0)
    d_got = lax.all_to_all(d_heads, "ctx", 0, 0, tiled=True)
    (d_sent,) = kernel_call(
        attend_back_kernel,
        tables,
        (d_got, q_place, q_start, *held),
        [shape((ctx_size, 3 * HD, rows_here), bf16)],
        [
            pltpu.VMEM((HD, q_rows), bf16),
            pltpu.VMEM((q_rows, HD), bf16),
            pltpu.VMEM((kv_rows, HD), f32),
            pltpu.VMEM((kv_rows, HD), f32),
        ],
    )
    d_back = lax.all_to_all(d_sent, "ctx", 0, 0, tiled=True)
    d_query = lax.dynamic_slice_in_dim(d_back[:, :HD], part * HEADS, HEADS).astype(f32)
    d_key_value = jnp.sum(
        d_back[:, HD:].reshape(parts, KV_HEADS, per_group, 2 * HD, rows_here).astype(f32),
        axis=(0, 2),
    )
    dq_normed = rope_back(d_query, cosine, sine)
    dk_normed = rope_back(d_key_value[:, :HD], cosine, sine)
    dq_raw, query_term = norm_back(dq_normed, q_raw, q_scale, column_query, 1)
    dk_raw, key_term = norm_back(dk_normed, k_raw, k_scale, column_key, 1)
    d_projected = jnp.concatenate(
        [
            dq_raw.reshape(q_width, rows_here).astype(bf16),
            dk_raw.reshape(kv_width, rows_here).astype(bf16),
            d_key_value[:, HD:].reshape(kv_width, rows_here).astype(bf16),
        ],
        axis=0,
    )
    grad_qkv_here = lax.dot_general(
        normed, d_projected, (((0,), (1,)), ((), ())), preferred_element_type=f32
    )
    d_normed = lax.dot_general(
        d_projected, w_qkv, (((0,), (1,)), ((), ())), preferred_element_type=f32
    )
    d_norm_one, attn_gain_term = norm_back(d_normed, inputs, scale_one, gain_attn)
    d_inputs = d_h_one + d_norm_one
    shard_qkv, shard_out, shard_attn_gain, shard_ffn_gain, shard_query_gain, shard_key_gain = (
        lax.psum_scatter(
            grad_qkv_here.astype(jnp.bfloat16), "fsdp", scatter_dimension=0, tiled=True
        ).astype(jnp.float32),
        lax.psum_scatter(
            grad_out_here.astype(jnp.bfloat16), "fsdp", scatter_dimension=0, tiled=True
        ).astype(jnp.float32),
        lax.psum_scatter(
            jnp.sum(attn_gain_term, axis=0).astype(jnp.bfloat16),
            "fsdp",
            scatter_dimension=0,
            tiled=True,
        ).astype(jnp.float32),
        lax.psum_scatter(
            jnp.sum(ffn_gain_term, axis=0).astype(jnp.bfloat16),
            "fsdp",
            scatter_dimension=0,
            tiled=True,
        ).astype(jnp.float32),
        lax.psum_scatter(
            jnp.sum(query_term, axis=(0, 2)).astype(jnp.bfloat16),
            "fsdp",
            scatter_dimension=0,
            tiled=True,
        ).astype(jnp.float32),
        lax.psum_scatter(
            jnp.sum(key_term, axis=(0, 2)).astype(jnp.bfloat16),
            "fsdp",
            scatter_dimension=0,
            tiled=True,
        ).astype(jnp.float32),
    )
    summed_grads = (
        lax.psum(shard_qkv.astype(jnp.bfloat16), "ctx").astype(jnp.float32),
        lax.psum(shard_out.astype(jnp.bfloat16), "ctx").astype(jnp.float32),
        lax.psum(grad_gate_up, "ctx").astype(jnp.float32),
        lax.psum(grad_down, "ctx").astype(jnp.float32),
        lax.psum(shard_attn_gain.astype(jnp.bfloat16), "ctx").astype(jnp.float32),
        lax.psum(shard_ffn_gain.astype(jnp.bfloat16), "ctx").astype(jnp.float32),
        lax.psum(shard_query_gain.astype(jnp.bfloat16), "ctx").astype(jnp.float32),
        lax.psum(shard_key_gain.astype(jnp.bfloat16), "ctx").astype(jnp.float32),
    )
    return (
        output[None],
        d_inputs[None],
        summed_grads[0],
        summed_grads[1],
        summed_grads[2],
        summed_grads[3],
        summed_grads[4],
        summed_grads[5],
        summed_grads[6],
        summed_grads[7],
    )


def solution(mesh):
    block = mesh.shape["fsdp"] == 2 and mesh.shape["ctx"] == 16
    return jax.shard_map(
        on_block if block else on_device,
        mesh=mesh,
        in_specs=(
            P("fsdp", "ctx", None),
            P("fsdp", None),
            P("fsdp", None),
            P("fsdp", None, None),
            P("fsdp", None),
            P("fsdp"),
            P("fsdp"),
            P("fsdp"),
            P("fsdp"),
            P("fsdp", None),
            P("fsdp", None),
            P("fsdp", "ctx", None),
        ),
        out_specs=(
            P("fsdp", "ctx", None),
            P("fsdp", "ctx", None),
            P("fsdp", None),
            P("fsdp", None),
            P("fsdp", None, None),
            P("fsdp", None),
            P("fsdp"),
            P("fsdp"),
            P("fsdp"),
            P("fsdp"),
        ),
        check_vma=False,
    )
```

```python
import functools

import jax
import jax.numpy as jnp
from jax import lax
from jax.experimental import pallas as pl
from jax.experimental.pallas import tpu as pltpu
from jax.sharding import PartitionSpec as P

HEADS = 16
KV_HEADS = 8
HD = 64
BLK = 128
TILE = 256
CHUNKS = 2
PROJECT = 0
ATTEND = 0
OUT = 0
FFN = (0, 0)
ATTEND_BACK = 25


EPSILON = 1e-05
ROPE_BASE = 1000000.0
LOG2E = 1.4426950408889634
SCORE_SCALE = LOG2E * HD ** (-0.5)


def rms_scale(values, axis=-1):
    return lax.rsqrt(jnp.mean(values * values, axis=axis, keepdims=True) + EPSILON)


def norm_back(grad_normed, inputs, scale, gain, axis=-1):
    scaled = grad_normed * gain
    grad_in = scale * scaled - inputs * scale * scale * scale * jnp.mean(
        scaled * inputs, axis=axis, keepdims=True
    )
    return (grad_in, grad_normed * inputs * scale)


def rope(values, cosine, sine):
    half = HD // 2
    first, second = values[:, :half], values[:, half:]
    return jnp.concatenate([first * cosine - second * sine, second * cosine + first * sine], axis=1)


def rope_back(values, cosine, sine):
    half = HD // 2
    first, second = values[:, :half], values[:, half:]
    return jnp.concatenate([first * cosine + second * sine, second * cosine - first * sine], axis=1)


def starts_of(packed, lengths_row):
    ends = jnp.cumsum(lengths_row)
    past = packed[:, None] >= ends[None, :]
    return jnp.sum(jnp.where(past, lengths_row[None, :], 0), axis=1)


def block_tables(order, lengths_row):
    count = order.shape[0]
    rank = jnp.sum((order[None, :] < order[:, None]).astype(jnp.int32), axis=1)
    hit = rank[None, :] == jnp.arange(count, dtype=jnp.int32)[:, None]
    slot = jnp.sum(jnp.where(hit, jnp.arange(count, dtype=jnp.int32)[None, :], 0), axis=1)
    block = jnp.sum(jnp.where(hit, order[None, :], 0), axis=1)
    place = (block[:, None] * BLK + jnp.arange(BLK, dtype=jnp.int32)[None, :]).reshape(-1)
    return (slot, place, starts_of(place, lengths_row))


def attend_kernel(
    q_slot, kv_slot, first, last, qkv_ref, place_ref, start_ref,
    out_ref, q_ref, qt_ref, k_ref, kt_ref, v_ref, ot_ref, total_ref, vt_ref
):
    per_device = qkv_ref.shape[2] // BLK
    kv_blocks = k_ref.shape[0] // BLK
    q_blocks = q_ref.shape[0] // BLK

    def piece(slot, lower):
        return qkv_ref[
            slot // per_device,
            lower : lower + HD,
            pl.ds(pl.multiple_of((slot % per_device) * BLK, BLK), BLK),
        ]

    for i in range(kv_blocks):
        here = slice(i * BLK, (i + 1) * BLK)
        keys = piece(kv_slot[i], HD)
        kt_ref[:, here] = keys
        k_ref[here, :] = keys.T
        values = piece(kv_slot[i], 2 * HD)
        vt_ref[:, here] = values
        v_ref[here, :] = values.T
    for i in range(q_blocks):
        here = slice(i * BLK, (i + 1) * BLK)
        queries = piece(q_slot[i], 0)
        qt_ref[:, here] = queries
        q_ref[here, :] = queries.T
    if q_blocks < kv_blocks:
        out_ref[...] = jnp.zeros_like(out_ref)

    def tile(i, carry):
        rows = pl.ds(pl.multiple_of(i * TILE, TILE), TILE)
        queries = qt_ref[:, rows]
        place = place_ref[:, rows]
        start = start_ref[:, rows]

        def step(j, state):
            total, summed = state
            at = pl.multiple_of(j * TILE, TILE)
            scores = jnp.dot(
                k_ref[pl.ds(at, TILE), :], queries, preferred_element_type=jnp.float32
            )
            key_place = lax.broadcasted_iota(jnp.int32, (TILE, TILE), 0) + at
            allowed = (key_place <= place) & (key_place >= start)
            lifted = jnp.where(allowed, jnp.exp2(scores * SCORE_SCALE), 0.0)
            total = total + jnp.sum(lifted, axis=0, keepdims=True)
            summed = summed + jnp.dot(
                vt_ref[:, pl.ds(at, TILE)],
                lifted.astype(jnp.bfloat16),
                preferred_element_type=jnp.float32,
            )
            return (total, summed)

        total, summed = lax.fori_loop(
            first[i],
            last[i],
            step,
            (jnp.zeros((1, TILE), jnp.float32), jnp.zeros((HD, TILE), jnp.float32)),
        )
        attn = summed / total
        ot_ref[:, rows] = attn
        total_ref[:, rows] = jnp.log(total) * LOG2E
        rounded = attn.astype(jnp.bfloat16)
        for part in range(TILE // BLK):
            slot = q_slot[i * (TILE // BLK) + part]
            out_ref[
                slot // per_device,
                :,
                pl.ds(pl.multiple_of((slot % per_device) * BLK, BLK), BLK),
            ] = rounded[:, part * BLK : (part + 1) * BLK]
        return carry

    lax.fori_loop(0, q_blocks * BLK // TILE, tile, 0)


def attend_back_kernel(
    q_slot, kv_slot, first, last, d_ref, place_ref, start_ref,
    q_ref, qt_ref, k_ref, kt_ref, v_ref, ot_ref, total_ref,
    out_ref, dt_ref, do_ref, dk_ref, dv_ref
):
    per_device = d_ref.shape[2] // BLK
    kv_blocks = k_ref.shape[0] // BLK
    q_blocks = q_ref.shape[0] // BLK

    def lanes(slot):
        return pl.ds(pl.multiple_of((slot % per_device) * BLK, BLK), BLK)

    for i in range(q_blocks):
        here = slice(i * BLK, (i + 1) * BLK)
        slot = q_slot[i]
        grads = d_ref[slot // per_device, :, lanes(slot)]
        dt_ref[:, here] = grads
        do_ref[here, :] = grads.T
    dk_ref[...] = jnp.zeros_like(dk_ref)
    dv_ref[...] = jnp.zeros_like(dv_ref)
    if q_blocks < kv_blocks:
        out_ref[...] = jnp.zeros_like(out_ref)

    def tile(i, carry):
        rows = pl.ds(pl.multiple_of(i * TILE, TILE), TILE)
        queries = qt_ref[:, rows]
        grads = dt_ref[:, rows]
        place = place_ref[:, rows]
        start = start_ref[:, rows]
        delta = jnp.sum(grads.astype(jnp.float32) * ot_ref[:, rows], axis=0, keepdims=True)
        total = total_ref[:, rows]

        def step(j, d_query):
            at = pl.multiple_of(j * TILE, TILE)
            here = pl.ds(at, TILE)
            scores = jnp.dot(k_ref[here, :], queries, preferred_element_type=jnp.float32)
            key_place = lax.broadcasted_iota(jnp.int32, (TILE, TILE), 0) + at
            allowed = (key_place <= place) & (key_place >= start)
            shares = jnp.where(allowed, jnp.exp2(scores * SCORE_SCALE - total), 0.0)
            d_shares = jnp.dot(v_ref[here, :], grads, preferred_element_type=jnp.float32)
            d_scores = (shares * (d_shares - delta)).astype(jnp.bfloat16)
            dv_ref[here, :] += jnp.dot(
                shares.astype(jnp.bfloat16), do_ref[rows, :], preferred_element_type=jnp.float32
            )
            dk_ref[here, :] += jnp.dot(
                d_scores, q_ref[rows, :], preferred_element_type=jnp.float32
            )
            return d_query + jnp.dot(
                kt_ref[:, here], d_scores, preferred_element_type=jnp.float32
            )

        d_query = lax.fori_loop(first[i], last[i], step, jnp.zeros((HD, TILE), jnp.float32))
        rounded = (d_query * HD ** (-0.5)).astype(jnp.bfloat16)
        for part in range(TILE // BLK):
            slot = q_slot[i * (TILE // BLK) + part]
            out_ref[slot // per_device, 0:HD, lanes(slot)] = rounded[
                :, part * BLK : (part + 1) * BLK
            ]
        return carry

    lax.fori_loop(0, q_blocks * BLK // TILE, tile, 0)
    for i in range(kv_blocks):
        here = slice(i * BLK, (i + 1) * BLK)
        slot = kv_slot[i]
        out_ref[slot // per_device, HD : 2 * HD, lanes(slot)] = (
            (dk_ref[here, :] * HD ** (-0.5)).T.astype(jnp.bfloat16)
        )
        out_ref[slot // per_device, 2 * HD : 3 * HD, lanes(slot)] = (
            dv_ref[here, :].T.astype(jnp.bfloat16)
        )


def cost(micros):
    return pl.CostEstimate(
        flops=1 + micros * 1_000_000_000, bytes_accessed=1, transcendentals=0
    )


def kernel_call(kernel, tables, arrays, outs, scratch, micros):
    smem = pl.BlockSpec(memory_space=pltpu.SMEM)
    vmem = pl.BlockSpec(memory_space=pltpu.VMEM)
    return pl.pallas_call(
        kernel,
        out_shape=outs,
        in_specs=[smem] * len(tables) + [vmem] * len(arrays),
        out_specs=[vmem] * len(outs),
        scratch_shapes=scratch,
        compiler_params=pltpu.CompilerParams(vmem_limit_bytes=48 * 1024 * 1024),
        cost_estimate=cost(micros),
    )(*tables, *arrays)


class Links:
    def __init__(self, ctx_size):
        self.depth = ctx_size // 4
        index = lax.axis_index("ctx")
        self.core = index % 2
        self.y = (index // 2) % 2
        self.side = lax.axis_index("fsdp")
        self.half = ((index // 4 + 1) // 2) % 2
        self.quarter = index % 2 * 2 + self.y
        self.here = jnp.stack([self.half, self.core, self.y, self.side]).astype(jnp.int32)

    def route(self, place):
        pairs = []
        for z in range(self.depth):
            for y in range(2):
                for core in range(2):
                    to_z, to_y, to_core = place(z, y, core)
                    pairs.append(((z * 2 + y) * 2 + core, (to_z * 2 + to_y) * 2 + to_core))
        return pairs

    def over_core(self, value):
        return lax.ppermute(value, "ctx", self.route(lambda z, y, c: (z, y, 1 - c)))

    def over_y(self, value):
        return lax.ppermute(value, "ctx", self.route(lambda z, y, c: (z, 1 - y, c)))

    def over_z(self, value):
        return lax.ppermute(value, "ctx", self.route(lambda z, y, c: (z ^ 1, y, c)))

    def mirror_z(self, value):
        return lax.ppermute(value, "ctx", self.route(lambda z, y, c: (self.depth - 1 - z, y, c)))

    def over_x(self, value):
        return lax.ppermute(value, "fsdp", [(0, 1), (1, 0)])

    def spread_plane(self, value):
        across = self.over_core(value)
        beside = self.over_y(value)
        return (value, across, beside, self.over_core(beside))

    def deal_plane(self, near, far, give, give_far):
        got, got_far = self.over_core(give), self.over_core(give_far)
        return (near, got, self.over_y(far), self.over_y(got_far))

    def sum_depth(self, kept, got):
        def half(index):
            return add(pick(kept, index, 0), pick(got, index, 0))

        given = self.over_z(half(1 - self.half))
        part = add(half(self.half), given)
        full = add(part, self.mirror_z(part))
        return jnp.stack([full, self.over_z(full)])

    def reduce(self, got, kept):
        return self.spread_plane(self.sum_depth(kept, got))


def pick(value, index, axis):
    return lax.dynamic_index_in_dim(value, index, axis, keepdims=False)


def add(left, right):
    return (left.astype(jnp.float32) + right.astype(jnp.float32)).astype(jnp.bfloat16)


def after(value, *others):
    return lax.optimization_barrier((value, *others))[0]


def contract(left, right, axes):
    return lax.dot_general(
        left, right, ((axes[:1], axes[1:]), ((), ())), preferred_element_type=jnp.float32
    )


PARAMS = pltpu.CompilerParams(vmem_limit_bytes=56 * 1024 * 1024)


def call_with_here(
    kernel, here, grid, arrays, specs, outs, out_specs, scratch=(), aliases=None, micros=5
):
    return pl.pallas_call(
        kernel,
        grid_spec=pltpu.PrefetchScalarGridSpec(
            num_scalar_prefetch=1,
            grid=grid,
            in_specs=specs,
            out_specs=out_specs,
            scratch_shapes=list(scratch),
        ),
        out_shape=outs,
        input_output_aliases=aliases or {},
        compiler_params=PARAMS,
        cost_estimate=cost(micros),
    )(here, *arrays)


def whole(array):
    rank = len(array.shape)
    return pl.BlockSpec(array.shape, lambda i, here: (0,) * rank)


def project_kernel(here, *refs):
    x_ref, gain_ref, own_ref = refs[:3]
    pieces, q_gain, k_gain, cos_ref, sin_ref = refs[3:7], refs[7], refs[8], refs[9], refs[10]
    d_ref = refs[11]
    sent, weight, q_ref, k_ref, q_scale, k_scale, early_ref, scale_ref = refs[12:]
    core, y, side = here[1], here[2], here[3]
    rows = own_ref.shape[0]
    part = rows // 4
    f32, bf16 = jnp.float32, jnp.bfloat16
    weight[pl.ds(pl.multiple_of(side * rows, rows), rows), :] = own_ref[...]
    for p in range(4):
        at = (1 - side) * rows + (((p % 2) ^ core) * 2 + ((p // 2) ^ y)) * part
        weight[pl.ds(pl.multiple_of(at, part), part), :] = pieces[p][...]
    x = x_ref[...].astype(f32)
    scale = rms_scale(x)
    scale_ref[...] = scale
    normed = (x * scale * gain_ref[...]).astype(bf16)
    early_ref[0] = d_ref[...]
    early_ref[1] = normed
    cosine, sine = cos_ref[...], sin_ref[...]
    half = HD // 2

    def turned(raw, gain, raw_ref, kept_scale, head):
        raw_ref[head * HD : (head + 1) * HD, :] = raw
        scale = rms_scale(raw, 0)
        kept_scale[head : head + 1, :] = scale
        value = raw * scale * gain
        first, second = value[:half], value[half:]
        return jnp.concatenate(
            [first * cosine - second * sine, second * cosine + first * sine], axis=0
        ).astype(bf16)

    per_group = HEADS // KV_HEADS
    for at in range(0, weight.shape[1], 2 * BLK):
        block = jnp.dot(normed, weight[:, at : at + 2 * BLK], preferred_element_type=f32)
        turned_block = block.T
        for n in range(2 * BLK // HD):
            head = at // HD + n
            raw = turned_block[n * HD : (n + 1) * HD, :]
            if head < HEADS:
                sent[head, 0:HD, :] = turned(raw, q_gain[...], q_ref, q_scale, head)
                continue
            head -= HEADS
            if head < KV_HEADS:
                value, row = turned(raw, k_gain[...], k_ref, k_scale, head), HD
            else:
                value, row, head = raw.astype(bf16), 2 * HD, head - KV_HEADS
            for copy in range(per_group):
                sent[head * per_group + copy, row : row + HD, :] = value


def project(here, x, gain, own, pieces, q_gain, k_gain, cosine, sine, d_ffn):
    tokens, width = x.shape
    f32, bf16 = jnp.float32, jnp.bfloat16
    shape = jax.ShapeDtypeStruct
    arrays = [x, gain, own, *pieces, q_gain, k_gain, cosine, sine, d_ffn]
    outs = [
        shape((HEADS, 3 * HD, tokens), bf16),
        shape((width, own.shape[1]), bf16),
        shape((HEADS * HD, tokens), f32),
        shape((KV_HEADS * HD, tokens), f32),
        shape((HEADS, tokens), f32),
        shape((KV_HEADS, tokens), f32),
        shape((2, tokens, width), bf16),
        shape((tokens, 1), f32),
    ]
    return call_with_here(
        project_kernel, here, (1,), arrays, [whole(a) for a in arrays], outs,
        [whole(o) for o in outs], micros=PROJECT,
    )


def layer(array, index):
    return pl.BlockSpec((1, *array.shape[1:]), lambda i, here: (index, 0, 0))


def attend_out_kernel(here, *refs):
    attn_ref, x_ref, gain_ref, own_ref = refs[:4]
    pieces = refs[4:12]
    weight, h_ref, scale_ref, two_ref, two_t_ref = refs[12:]
    core, y, side = here[1], here[2], here[3]
    rows = own_ref.shape[0]
    part = rows // 4
    weight[pl.ds(pl.multiple_of(side * rows, rows), rows), :] = own_ref[...]
    for p in range(4):
        at = (1 - side) * rows + (((p % 2) ^ core) * 2 + ((p // 2) ^ y)) * part
        for n in range(2):
            piece = pieces[2 * p + n]
            wide = piece.shape[1]
            weight[pl.ds(pl.multiple_of(at, part), part), n * wide : (n + 1) * wide] = piece[...]
    attn = attn_ref[...].T
    h_one = x_ref[...].astype(jnp.float32) + jnp.dot(
        attn, weight[...], preferred_element_type=jnp.float32
    )
    scale = rms_scale(h_one)
    h_ref[...] = h_one
    scale_ref[...] = scale
    two = (h_one * scale * gain_ref[...]).astype(jnp.bfloat16)
    two_ref[...] = two
    two_t_ref[...] = two.T


def attend_out(here, attn, x, gain, own, pieces):
    tokens, width = x.shape
    f32, bf16 = jnp.float32, jnp.bfloat16
    shape = jax.ShapeDtypeStruct
    part = own.shape[0] // 4
    half = width // 2
    first = pieces[0].shape[1] // half - 2
    arrays = [attn, x, gain, own]
    specs = [whole(a) for a in arrays]
    for piece in pieces:
        for n in range(2):
            arrays.append(piece)
            specs.append(pl.BlockSpec((part, half), lambda i, here, n=n: (0, first + n)))
    outs = [
        shape((width, width), bf16),
        shape((tokens, width), f32),
        shape((tokens, 1), f32),
        shape((tokens, width), bf16),
        shape((width, tokens), bf16),
    ]
    return call_with_here(
        attend_out_kernel, here, (1,), arrays, specs, outs, [whole(o) for o in outs], micros=OUT
    )


def ffn_kernel(chunk, here, *refs):
    two_ref, d_ref, own_ref = refs[:3]
    pieces, down_ref, down_pieces = refs[3:7], refs[7], refs[8:12]
    if chunk == 0:
        before_refs, refs = refs[12:13], refs[13:]
        near, far, give, give_far, out_ref, d_two_ref = refs[:6]
        refs = refs[6:]
    else:
        before_refs, gain_ref, refs = refs[12:17], refs[17], refs[18:]
        near, far, give, give_far = refs[:4]
        out_ref, d_h_ref, d_attn_ref, heads_ref, gain_term_ref = refs[4:9]
        refs = refs[9:]
    weight, down, hidden_rows, out_sum, two_sum = refs[:5]
    held, weight_sem, down_sem, before_sem = refs[5:-3], refs[-3], refs[-2], refs[-1]
    core, y, side = here[1], here[2], here[3]
    f32, bf16 = jnp.float32, jnp.bfloat16
    own_rows, columns = own_ref.shape[1], own_ref.shape[2] // CHUNKS
    part = own_rows // 4
    tile = columns // FFN_TILES
    half = columns // 2

    def quarter(p):
        return ((p % 2) ^ core) * 2 + ((p // 2) ^ y)

    def copies(n):
        at = slice(n * tile, (n + 1) * tile)
        mine = pl.ds(pl.multiple_of(side * own_rows, own_rows), own_rows)
        found = [
            pltpu.make_async_copy(
                own_ref.at[:, :, chunk * columns + n * tile : chunk * columns + (n + 1) * tile],
                weight.at[:, mine, at],
                weight_sem.at[n, 0],
            )
        ]
        for p in range(4):
            rows = pl.ds(pl.multiple_of((1 - side) * own_rows + quarter(p) * part, part), part)
            for kind in range(2):
                begin = kind * columns + n * tile
                found.append(
                    pltpu.make_async_copy(
                        pieces[p].at[:, begin : begin + tile],
                        weight.at[kind, rows, at],
                        weight_sem.at[n, 1 + 2 * p + kind],
                    )
                )
        return found

    def own_down(n):
        at = slice(n * tile, (n + 1) * tile)
        return [pltpu.make_async_copy(down_ref.at[at, :], down.at[at, :], down_sem.at[n, 0])]

    def other_down(n):
        at = slice(n * tile, (n + 1) * tile)
        found = []
        for p in range(4):
            wide = down_pieces[p].shape[1]
            lanes = pl.ds(pl.multiple_of(quarter(p) * wide, wide), wide)
            found.append(
                pltpu.make_async_copy(
                    down_pieces[p].at[at, :], down.at[at, lanes], down_sem.at[n, p]
                )
            )
        return found

    def each(action, n):
        for copy in copies(n):
            action(copy)

        @pl.when(side == chunk)
        def _():
            for copy in own_down(n):
                action(copy)

        @pl.when(side != chunk)
        def _():
            for copy in other_down(n):
                action(copy)

    before = [
        pltpu.make_async_copy(ref, held[n], before_sem.at[n]) for n, ref in enumerate(before_refs)
    ]
    for n in range(FFN_TILES):
        each(lambda copy: copy.start(), n)
    for copy in before:
        copy.start()
    two = two_ref[...]
    d_ffn = d_ref[...]
    for n in range(FFN_TILES):
        each(lambda copy: copy.wait(), n)
        at = slice(n * tile, (n + 1) * tile)
        gate = jnp.dot(two, weight[0, :, at], preferred_element_type=f32)
        upper = jnp.dot(two, weight[1, :, at], preferred_element_type=f32)
        d_hidden = contract(d_ffn, down[at, :], (1, 1))
        sigma = jax.nn.sigmoid(gate)
        silu = gate * sigma
        hidden = (silu * upper).astype(bf16)
        d_gate = (d_hidden * upper * sigma * (1.0 + gate * (1.0 - sigma))).astype(bf16)
        d_upper = (d_hidden * silu).astype(bf16)
        out_term = jnp.dot(hidden, down[at, :], preferred_element_type=f32)
        two_term = contract(d_gate, weight[0, :, at], (1, 1)) + contract(
            d_upper, weight[1, :, at], (1, 1)
        )
        out_sum[...] = out_term if n == 0 else out_sum[...] + out_term
        two_sum[...] = two_term if n == 0 else two_sum[...] + two_term
        hidden_rows[:, at] = hidden
        mine = jnp.where(core == 0, d_gate, d_upper)
        other = jnp.where(core == 0, d_upper, d_gate)
        for column in range(2):
            begin, end = max(n * tile, column * half), min((n + 1) * tile, (column + 1) * half)
            if begin >= end:
                continue
            source = slice(begin - n * tile, end - n * tile)
            target = slice(begin - column * half, end - column * half)
            first, second = mine[:, source], other[:, source]

            @pl.when(y == column)
            def _(first=first, second=second, target=target):
                near[:, target] = first
                give[:, target] = second

            @pl.when(y != column)
            def _(first=first, second=second, target=target):
                far[:, target] = first
                give_far[:, target] = second

    share = half // 2
    target = slice(half, half + share)
    for owner in range(2):
        lower = hidden_rows[:, owner * half : owner * half + share]
        upper = hidden_rows[:, owner * half + share : (owner + 1) * half]
        close = jnp.where(y == 0, lower, upper)
        distant = jnp.where(y == 0, upper, lower)

        @pl.when(core == owner)
        def _(close=close, distant=distant):
            near[:, target] = close
            far[:, target] = distant

        @pl.when(core != owner)
        def _(close=close, distant=distant):
            give[:, target] = close
            give_far[:, target] = distant

    for copy in before:
        copy.wait()
    if chunk == 0:
        out_ref[...] = held[0][...] + out_sum[...]
        d_two_ref[...] = two_sum[...]
    else:
        out_before, two_before, h_one, scale, w_out = held
        out_ref[...] = (out_before[...] + out_sum[...]).astype(bf16)
        d_norm, gain_term = norm_back(
            two_before[...] + two_sum[...], h_one[...], scale[...], gain_ref[...]
        )
        gain_term_ref[...] = jnp.sum(gain_term, axis=0, keepdims=True)
        d_h_one = d_ffn.astype(f32) + d_norm
        d_h_ref[...] = d_h_one
        d_attn = d_h_one.astype(bf16)
        d_attn_ref[...] = d_attn
        heads_ref[...] = contract(w_out[...], d_attn, (1, 1)).astype(bf16)


FFN_TILES = 3


def ffn(here, chunk, two, d_ffn, own, pieces, down, down_pieces, before, gain=None):
    tokens, width = two.shape
    columns = own.shape[2] // CHUNKS
    padded = (columns // 2 + columns // 4 + BLK - 1) // BLK * BLK
    shape = jax.ShapeDtypeStruct
    f32, bf16 = jnp.float32, jnp.bfloat16
    outs = [shape((tokens, padded), bf16)] * 4
    if chunk == 0:
        outs += [shape((tokens, width), f32)] * 2
    else:
        outs += [
            shape((tokens, width), bf16),
            shape((tokens, width), f32),
            shape((tokens, width), bf16),
            shape((width, tokens), bf16),
            shape((1, width), f32),
        ]
    far_away = pl.BlockSpec(memory_space=pl.ANY)
    arrays = [two, d_ffn, own, *pieces, down, *down_pieces, *before]
    specs = [whole(two), whole(d_ffn)] + [far_away] * (len(arrays) - 2)
    if gain is not None:
        arrays.append(gain)
        specs.append(whole(gain))
    got = call_with_here(
        functools.partial(ffn_kernel, chunk),
        here,
        (1,),
        arrays,
        specs,
        outs,
        [whole(o) for o in outs],
        [
            pltpu.VMEM((2, width, columns), bf16),
            pltpu.VMEM((columns, width), bf16),
            pltpu.VMEM((tokens, columns), bf16),
            pltpu.VMEM((tokens, width), f32),
            pltpu.VMEM((tokens, width), f32),
        ]
        + [pltpu.VMEM(v.shape, v.dtype) for v in before]
        + [
            pltpu.SemaphoreType.DMA((FFN_TILES, 9)),
            pltpu.SemaphoreType.DMA((FFN_TILES, 4)),
            pltpu.SemaphoreType.DMA((len(before),)),
        ],
        micros=FFN[chunk],
    )
    return got[:4], got[4:]


def wide_product_kernel(here, *refs):
    planes, terms = refs[:4], refs[4:8]
    sent, kept, left, right = refs[8:]
    tokens = planes[0].shape[1]
    columns = right.shape[1]
    for i in range(4):
        left[:, i * tokens : (i + 1) * tokens] = planes[i][...]
        right[i * tokens : (i + 1) * tokens, :] = terms[i][:, :columns]
    side = here[3]
    _, step, _ = kept.shape
    for half in range(2):
        for owner, out_ref in ((1 - side, sent), (side, kept)):
            place = pl.multiple_of(owner * 2 * step + half * step, step)
            out_ref[half] = jnp.dot(
                left[pl.ds(place, step), :], right[...], preferred_element_type=jnp.float32
            ).astype(out_ref.dtype)


def wide_products(here, two_plane, shares, columns):
    rows, tokens = two_plane[0].shape
    outs = [
        jax.ShapeDtypeStruct((2, rows // 4, columns), jnp.bfloat16),
        jax.ShapeDtypeStruct((2, rows // 4, columns), jnp.float32),
    ]
    arrays = [*two_plane, *shares]
    return call_with_here(
        wide_product_kernel,
        here,
        (1,),
        arrays,
        [whole(a) for a in two_plane]
        + [pl.BlockSpec((tokens, columns), lambda i, here: (0, 0))] * 4,
        outs,
        [whole(o) for o in outs],
        [
            pltpu.VMEM((rows, 4 * tokens), jnp.bfloat16),
            pltpu.VMEM((4 * tokens, columns), jnp.bfloat16),
        ],
        micros=8,
    )


def down_product_kernel(here, *refs):
    planes, terms = refs[:4], (refs[4:8], refs[8:12])
    sent, kept, left, right = refs[12:]
    tokens = planes[0].shape[1]
    rows = left.shape[0]
    for i in range(4):
        right[i * tokens : (i + 1) * tokens, :] = planes[i][0]
    for chunk in range(2):
        for i in range(4):
            share = terms[chunk][i]
            at = share.shape[1] // BLK * BLK - (rows + BLK - 1) // BLK * BLK
            left[:, i * tokens : (i + 1) * tokens] = share[:, at : at + rows].T
        for half in range(2):
            product = jnp.dot(
                left[half * rows // 2 : (half + 1) * rows // 2, :],
                right[...],
                preferred_element_type=jnp.float32,
            )

            @pl.when(here[3] == chunk)
            def _(product=product, half=half):
                kept[half] = product

            @pl.when(here[3] != chunk)
            def _(product=product, half=half):
                sent[half] = product.astype(sent.dtype)


def down_products(here, early_plane, first, second, rows):
    _, tokens, columns = early_plane[0].shape
    outs = [
        jax.ShapeDtypeStruct((2, rows // 2, columns), jnp.bfloat16),
        jax.ShapeDtypeStruct((2, rows // 2, columns), jnp.float32),
    ]
    return call_with_here(
        down_product_kernel,
        here,
        (1,),
        [*early_plane, *first, *second],
        [layer(a, 0) for a in early_plane] + [whole(a) for a in (*first, *second)],
        outs,
        [whole(o) for o in outs],
        [
            pltpu.VMEM((rows, 4 * tokens), jnp.bfloat16),
            pltpu.VMEM((4 * tokens, columns), jnp.bfloat16),
        ],
        micros=8,
    )


GAIN_ROWS = 16


def attention_back_kernel(here, *refs):
    d_ref, q_ref, k_ref, q_scale, k_scale, q_gain, k_gain, cos_ref, sin_ref = refs[:9]
    weight, x_ref, scale_ref, gain_ref, d_h_ref, d_attn_ref = refs[9:15]
    near, far, give, give_far, d_x_ref, gains_ref = refs[15:21]
    turned, natural = refs[21:]
    f32, bf16 = jnp.float32, jnp.bfloat16
    core, y = here[1], here[2]
    cosine, sine = cos_ref[...], sin_ref[...]
    half = HD // 2
    per_group = HEADS // KV_HEADS
    tokens = x_ref.shape[0]

    def back(grad, raw, scale, gain):
        first, second = grad[:half], grad[half:]
        normed = jnp.concatenate(
            [first * cosine + second * sine, second * cosine - first * sine], axis=0
        )
        return norm_back(normed, raw, scale, gain, 0)

    q_term = jnp.zeros((HD, tokens), f32)
    k_term = jnp.zeros((HD, tokens), f32)
    for head in range(HEADS):
        at = slice(head * HD, (head + 1) * HD)
        grad, term = back(
            d_ref[head, :HD, :].astype(f32), q_ref[at, :], q_scale[head : head + 1, :], q_gain[...]
        )
        turned[at, :] = grad.astype(bf16)
        q_term = q_term + term
    for head in range(KV_HEADS):
        at = slice(head * HD, (head + 1) * HD)
        both = d_ref[head * per_group, HD:, :].astype(f32)
        for other in range(1, per_group):
            both = both + d_ref[head * per_group + other, HD:, :].astype(f32)
        grad, term = back(both[:HD], k_ref[at, :], k_scale[head : head + 1, :], k_gain[...])
        place = HEADS * HD + head * HD
        turned[place : place + HD, :] = grad.astype(bf16)
        k_term = k_term + term
        place += KV_HEADS * HD
        turned[place : place + HD, :] = both[HD:].astype(bf16)
    rows = turned.shape[0] // 4
    columns = d_attn_ref.shape[1] // 4
    shares = ((near, core, y), (far, core, 1 - y), (give, 1 - core, y), (give_far, 1 - core, 1 - y))
    for out_ref, to_core, to_y in shares:
        share = to_core * 2 + to_y
        out_ref[:rows, :] = turned[pl.ds(pl.multiple_of(share * rows, rows), rows), :]
        out_ref[rows:, :] = d_attn_ref[:, pl.ds(pl.multiple_of(share * columns, columns), columns)]
    for at in range(0, turned.shape[0], 256):
        natural[:, at : at + 256] = turned[at : at + 256, :].T
    d_normed = contract(natural[...], weight[...], (1, 1))
    x = x_ref[...].astype(f32)
    d_norm, gain_term = norm_back(d_normed, x, scale_ref[...], gain_ref[...])
    d_x_ref[...] = d_h_ref[...] + d_norm
    gains_ref[...] = jnp.zeros_like(gains_ref)
    gains_ref[0:1, :] = jnp.sum(gain_term, axis=0, keepdims=True)
    gains_ref[1:2, 0:HD] = jnp.sum(q_term.T, axis=0, keepdims=True)
    gains_ref[2:3, 0:HD] = jnp.sum(k_term.T, axis=0, keepdims=True)


def attention_back(here, arrays):
    f32, bf16 = jnp.float32, jnp.bfloat16
    shape = jax.ShapeDtypeStruct
    weight, x = arrays[9], arrays[10]
    tokens, width = x.shape
    rows = weight.shape[1] // 4 + tokens
    assert width // 4 == tokens
    outs = [
        *[shape((rows, tokens), bf16)] * 4,
        shape((tokens, width), f32),
        shape((8, width), f32),
    ]
    return call_with_here(
        attention_back_kernel, here, (1,), arrays, [whole(a) for a in arrays], outs,
        [whole(o) for o in outs],
        [pltpu.VMEM((weight.shape[1], tokens), bf16), pltpu.VMEM((tokens, weight.shape[1]), bf16)],
        micros=12,
    )


def attention_product_kernel(here, *refs):
    normed, attn, terms, gains_ref, ffn_gain_ref = refs[:4], refs[4:8], refs[8:12], refs[12], refs[13]
    sent, kept, left, right, left_out, right_out = refs[14:]
    tokens = normed[0].shape[1]
    cut = right.shape[1]
    for i in range(4):
        at = slice(i * tokens, (i + 1) * tokens)
        left[:, at] = normed[i][0].T
        left_out[:, at] = attn[i][...]
        share = terms[i]
        right[at, :] = share[:cut].T
        right_out[at, :] = share[cut:]
    step = left.shape[0] // 4
    for owner, out_ref in ((1 - here[3], sent), (here[3], kept)):
        for half in range(2):
            at = pl.ds(pl.multiple_of(owner * 2 * step + half * step, step), step)
            out_ref[half, :step, :cut] = jnp.dot(
                left[at, :], right[...], preferred_element_type=jnp.float32
            ).astype(out_ref.dtype)
            out_ref[half, :step, cut:] = jnp.dot(
                left_out[at, :], right_out[...], preferred_element_type=jnp.float32
            ).astype(out_ref.dtype)
        rows = gains_ref.shape[1] // 2
        mine = pl.ds(pl.multiple_of(owner * rows, rows), rows)
        wide = out_ref.shape[2] - rows
        block = jnp.concatenate(
            [
                jnp.concatenate([gains_ref[0:1, mine], gains_ref[1:2, 0:wide]], axis=1),
                jnp.concatenate([ffn_gain_ref[:, mine], gains_ref[2:3, 0:wide]], axis=1),
                jnp.zeros((GAIN_ROWS - 2, out_ref.shape[2]), jnp.float32),
            ],
            axis=0,
        )
        out_ref[0, step:, :] = block.astype(out_ref.dtype)
        out_ref[1, step:, :] = jnp.zeros((GAIN_ROWS, out_ref.shape[2]), out_ref.dtype)


def attention_products(here, early_plane, attn_plane, shares, gains, ffn_gain):
    _, tokens, width = early_plane[0].shape
    cut = shares[0].shape[0] - tokens
    shape = (2, width // 4 + GAIN_ROWS, cut + tokens)
    outs = [jax.ShapeDtypeStruct(shape, jnp.bfloat16), jax.ShapeDtypeStruct(shape, jnp.float32)]
    return call_with_here(
        attention_product_kernel,
        here,
        (1,),
        [*early_plane, *attn_plane, *shares, gains, ffn_gain],
        [layer(a, 1) for a in early_plane]
        + [whole(a) for a in (*attn_plane, *shares, gains, ffn_gain)],
        outs,
        [whole(o) for o in outs],
        [
            pltpu.VMEM((width, 4 * tokens), jnp.bfloat16),
            pltpu.VMEM((4 * tokens, cut), jnp.bfloat16),
            pltpu.VMEM((width, 4 * tokens), jnp.bfloat16),
            pltpu.VMEM((4 * tokens, tokens), jnp.bfloat16),
        ],
        micros=8,
    )


def place_gate_up_kernel(here, *refs):
    mine, across, beside, diagonal, out_ref = *refs[:4], refs[-1]
    pieces = (mine, across, beside, diagonal)
    wide = mine.shape[2]
    for case in range(4):
        core, y = case // 2, case % 2

        @pl.when((here[1] == core) & (here[2] == y))
        def _(core=core, y=y):
            for kind in range(2):
                for column in range(2):
                    value = pieces[(y ^ column) * 2 + (core ^ kind)][0]
                    out_ref[:, kind, column * wide : (column + 1) * wide] = value.astype(
                        jnp.float32
                    )


def place_gate_up(here, chunk, pieces, before):
    _, rows, wide = pieces[0].shape
    step = 64
    blocks = rows // step

    def source(i, here):
        return ((i // blocks) ^ here[0], i % blocks, 0)

    arrays = list(pieces)
    specs = [pl.BlockSpec((1, step, wide), source)] * 4
    aliases = {}
    if before is not None:
        arrays.append(before)
        specs.append(pl.BlockSpec(memory_space=pl.ANY))
        aliases = {5: 0}
    (out,) = call_with_here(
        place_gate_up_kernel,
        here,
        (2 * blocks,),
        arrays,
        specs,
        [jax.ShapeDtypeStruct((2 * rows, 2, 2 * wide * CHUNKS), jnp.float32)],
        [pl.BlockSpec((step, 2, 2 * wide), lambda i, here: (i, 0, chunk))],
        aliases=aliases,
        micros=10,
    )
    return out


def place_down(here, pieces):
    _, rows, columns = pieces[0].shape

    def kernel(here, *refs):
        for s in range(8):

            @pl.when(pl.program_id(0) == s)
            def _(s=s):
                refs[4][...] = refs[s % 4][s // 4].astype(jnp.float32)

    def target(s, here):
        half = (s // 4) ^ here[0]
        y = ((s // 2) % 2) ^ here[2]
        core = (s % 2) ^ here[1]
        return ((core * 2 + y) * 2 + half, 0)

    (out,) = call_with_here(
        kernel,
        here,
        (8,),
        list(pieces),
        [whole(v) for v in pieces],
        [jax.ShapeDtypeStruct((rows * 8, columns), jnp.float32)],
        [pl.BlockSpec((rows, columns), target)],
    )
    return out


def place_attention(here, pieces, cut):
    _, rows, columns = pieces[0].shape
    rows -= GAIN_ROWS

    def kernel(here, *refs):
        qkv_ref, out_ref, gains_ref = refs[4:]
        for s in range(8):

            @pl.when(pl.program_id(0) == s)
            def _(s=s):
                value = refs[s % 4][s // 4]
                qkv_ref[...] = value[:rows, :cut].astype(jnp.float32)
                out_ref[...] = value[:rows, cut:].astype(jnp.float32)
                gains = value[rows:].astype(jnp.float32)
                gains_ref[...] = gains if s == 0 else gains_ref[...] + gains

    def target(s, here):
        half = (s // 4) ^ here[0]
        return (half, ((s % 2) ^ here[1]) * 2 + (((s // 2) % 2) ^ here[2]))

    shape = jax.ShapeDtypeStruct
    f32 = jnp.float32
    gain_shape = (GAIN_ROWS, columns)
    return call_with_here(
        kernel,
        here,
        (8,),
        list(pieces),
        [whole(v) for v in pieces],
        [
            shape((2 * rows, 4 * cut), f32),
            shape((2 * rows, 4 * (columns - cut)), f32),
            shape(gain_shape, f32),
        ],
        [
            pl.BlockSpec((rows, cut), target),
            pl.BlockSpec((rows, columns - cut), target),
            pl.BlockSpec(gain_shape, lambda s, here: (0, 0)),
        ],
    )


def on_block(
    tokens,
    qkv_weight,
    out_weight,
    gate_up_weight,
    down_weight,
    attn_gain,
    ffn_gain,
    query_gain,
    key_gain,
    seq_lengths,
    block_order,
    cotangent,
):
    inputs = tokens[0].astype(jnp.float32)
    rows_here = inputs.shape[0]
    ctx_size = lax.axis_size("ctx")
    ctx_index = lax.axis_index("ctx")
    per_group = HEADS // KV_HEADS
    q_width = HEADS * HD
    kv_width = KV_HEADS * HD
    order_row = block_order[0]
    lengths_row = seq_lengths[0]
    slots = jnp.arange(rows_here, dtype=jnp.int32) // BLK + ctx_index * (rows_here // BLK)
    table = slots[:, None] == jnp.arange(order_row.shape[0], dtype=jnp.int32)[None, :]
    packed = (
        jnp.sum(jnp.where(table, order_row[None, :], 0), axis=1) * BLK
        + jnp.arange(rows_here, dtype=jnp.int32) % BLK
    )
    local = packed - starts_of(packed, lengths_row)
    frequency = ROPE_BASE ** (-2.0 * jnp.arange(HD // 2, dtype=jnp.float32) / HD)
    angle = frequency[:, None] * local.astype(jnp.float32)[None, :]
    cosine = jnp.cos(angle)[None]
    sine = jnp.sin(angle)[None]
    bf16, f32 = jnp.bfloat16, jnp.float32
    parts = ctx_size // HEADS
    part = ctx_index // HEADS
    part_blocks = HEADS * rows_here // BLK
    q_order = lax.dynamic_slice_in_dim(order_row, part * part_blocks, part_blocks)
    q_slot, q_place, q_start = block_tables(q_order, lengths_row)
    q_slot = q_slot + part * part_blocks
    kv_slot, _, _ = block_tables(order_row, lengths_row)
    first = jnp.min(q_start.reshape(-1, TILE), axis=1) // TILE
    last = jnp.max(q_place.reshape(-1, TILE), axis=1) // TILE + 1
    tables = (q_slot, kv_slot, first, last)
    q_rows, kv_rows = part_blocks * BLK, order_row.shape[0] * BLK

    links = Links(ctx_size)
    here = links.here
    width = inputs.shape[1]
    rows = qkv_weight.shape[0]
    part_rows = rows // 4

    def quarter_rows(weight):
        return lax.dynamic_slice_in_dim(weight, links.quarter * part_rows, part_rows)

    qkv_piece = quarter_rows(qkv_weight)
    gains_here = jnp.concatenate([after(attn_gain, qkv_piece), ffn_gain, query_gain, key_gain])
    gains_there = links.over_x(gains_here)

    def gain_of(at, size):
        mine, other = gains_here[at : at + size], gains_there[at : at + size]
        return jnp.where(
            links.side == 0, jnp.concatenate([mine, other]), jnp.concatenate([other, mine])
        ).astype(f32)

    gain_attn = gain_of(0, rows)
    gain_ffn = gain_of(rows, rows)
    gain_query = gain_of(2 * rows, HD // 2)
    gain_key = gain_of(2 * rows + HD // 2, HD // 2)
    ff_chunk = gate_up_weight.shape[2] // CHUNKS

    def gate_up_piece(chunk):
        piece = lax.dynamic_slice(
            gate_up_weight,
            (links.quarter * part_rows, 0, chunk * ff_chunk),
            (part_rows, 2, ff_chunk),
        )
        return [piece[:, 0], piece[:, 1]]

    qkv_there = links.over_x(qkv_piece)
    first_piece = jnp.concatenate([*gate_up_piece(0), quarter_rows(out_weight)], axis=1)
    second_piece = jnp.concatenate(gate_up_piece(1), axis=1)
    down_piece = lax.dynamic_slice_in_dim(
        down_weight, links.quarter * (width // 4), width // 4, 1
    )
    d_ffn = cotangent[0]
    tokens_here = tokens[0]
    qkv_there = after(qkv_there, first_piece)
    first_there = links.over_x(after(first_piece, qkv_there))
    gate_up = jnp.transpose(after(gate_up_weight, qkv_there), (1, 0, 2))
    qkv_beside = links.over_y(qkv_there)
    qkv_pieces = (
        qkv_there,
        links.over_core(qkv_there),
        qkv_beside,
        links.over_core(after(qkv_beside, gate_up)),
    )
    sent, w_qkv, q_raw, k_raw, q_scale, k_scale, early, scale_one = project(
        here, tokens_here, gain_attn[None], qkv_weight, qkv_pieces,
        gain_query[:, None], gain_key[:, None], cosine[0], sine[0], d_ffn,
    )
    got = lax.all_to_all(sent, "ctx", 0, 0, tiled=True)
    early_beside = links.over_y(early)
    first_there = after(first_there, sent)
    down_there = links.over_x(after(down_piece, first_there))
    first_beside = links.over_y(first_there)
    second_there = links.over_x(after(second_piece, down_there))
    down_beside = links.over_y(down_there)
    got = after(got, down_there)
    q_place, q_start = q_place[None], q_start[None]
    shape = jax.ShapeDtypeStruct
    attn_sent, *held = kernel_call(
        attend_kernel,
        tables,
        (got, q_place, q_start),
        [
            shape((ctx_size, HD, rows_here), bf16),
            shape((q_rows, HD), bf16),
            shape((HD, q_rows), bf16),
            shape((kv_rows, HD), bf16),
            shape((HD, kv_rows), bf16),
            shape((kv_rows, HD), bf16),
            shape((HD, q_rows), f32),
            shape((1, q_rows), f32),
        ],
        [pltpu.VMEM((HD, kv_rows), bf16)],
        ATTEND,
    )
    attn_in = lax.dynamic_slice_in_dim(
        lax.all_to_all(attn_sent, "ctx", 0, 0, tiled=True), part * HEADS, HEADS
    ).reshape(q_width, rows_here)
    second_there = after(second_there, attn_sent)

    def spread(there, beside, time):
        there, beside = after(there, time), after(beside, time)
        return (there, links.over_core(there), beside, links.over_core(beside))

    first_pieces = spread(first_there, first_beside, attn_sent)
    down_pieces = spread(down_there, down_beside, attn_in)
    second_pieces = links.spread_plane(second_there)
    w_out, h_one, scale_two, two, two_t = attend_out(
        here, after(attn_in, early_beside), tokens_here, gain_ffn[None], out_weight, first_pieces
    )
    attn_beside = links.over_y(attn_in)
    two_beside = links.over_y(two_t)
    dealt_here, (out_sum, two_sum) = ffn(
        here, 0, two, d_ffn, gate_up, first_pieces, down_weight, down_pieces, [h_one]
    )
    two_plane = (two_t, links.over_core(two_t), two_beside, links.over_core(two_beside))
    near, far, give, give_far = dealt_here
    got_far = links.over_core(give_far)
    first_shares = (near, links.over_core(give), links.over_y(far), links.over_y(got_far))
    out_sum = after(out_sum, got_far)
    dealt_here, (output, d_h_one, d_attn, d_heads, ffn_gain_term) = ffn(
        here, 1, two, d_ffn, gate_up, second_pieces, down_weight, down_pieces,
        [out_sum, two_sum, h_one, scale_two, w_out], gain_ffn[None],
    )
    second_shares = links.deal_plane(*dealt_here)

    def plane(value, beside, time):
        value, beside = after(value, time), after(beside, time)
        return (value, links.over_core(value), beside, links.over_core(beside))

    columns = ff_chunk // 2
    d_heads = d_heads.reshape(HEADS, HD, rows_here)
    d_got = lax.all_to_all(d_heads, "ctx", 0, 0, tiled=True)
    first_products = wide_products(
        here, two_plane, [after(v, d_heads) for v in first_shares], columns
    )
    d_got = after(d_got, first_products[0])
    (d_sent,) = kernel_call(
        attend_back_kernel,
        tables,
        (d_got, q_place, q_start, *held),
        [shape((ctx_size, 3 * HD, rows_here), bf16)],
        [
            pltpu.VMEM((HD, q_rows), bf16),
            pltpu.VMEM((q_rows, HD), bf16),
            pltpu.VMEM((kv_rows, HD), f32),
            pltpu.VMEM((kv_rows, HD), f32),
        ],
        ATTEND_BACK,
    )
    first_got = links.over_x(first_products[0])
    d_sent = after(d_sent, first_got)
    d_back = lax.all_to_all(d_sent, "ctx", 0, 0, tiled=True)
    second_products = wide_products(
        here, two_plane, [after(v, d_sent) for v in second_shares], columns
    )
    early_plane = plane(early, early_beside, d_sent)
    attn_plane = plane(attn_in, attn_beside, d_sent)
    down_terms = down_products(
        here, early_plane, first_shares, second_shares, columns // 2
    )
    second_got = links.over_x(after(second_products[0], first_got))
    down_got = links.over_x(after(down_terms[0], second_got))
    *d_shares, d_inputs, gain_sums = attention_back(
        here,
        [
            d_back, q_raw, k_raw, q_scale, k_scale, gain_query[:, None], gain_key[:, None],
            cosine[0], sine[0], w_qkv, tokens_here, scale_one, gain_attn[None], d_h_one, d_attn,
        ],
    )
    grad_gate_up = None
    for chunk, (got, kept) in enumerate(
        ((first_got, first_products[1]), (second_got, second_products[1]))
    ):
        grad_gate_up = place_gate_up(here, chunk, links.reduce(got, kept), grad_gate_up)
    grad_down = place_down(here, links.reduce(down_got, down_terms[1]))
    attention_terms = attention_products(
        here, early_plane, attn_plane, links.deal_plane(*d_shares), gain_sums, ffn_gain_term
    )
    cut = qkv_weight.shape[1] // 4
    grad_qkv, grad_out, gain_sums = place_attention(
        here, links.reduce(links.over_x(attention_terms[0]), attention_terms[1]), cut
    )
    at = links.side * (HD // 2)
    gain_grads = [
        gain_sums[0, :rows],
        gain_sums[1, :rows],
        lax.dynamic_slice_in_dim(gain_sums[0, rows : rows + HD], at, HD // 2),
        lax.dynamic_slice_in_dim(gain_sums[1, rows : rows + HD], at, HD // 2),
    ]
    return (
        output[None],
        d_inputs[None],
        grad_qkv,
        grad_out,
        grad_gate_up,
        grad_down,
        *gain_grads,
    )


def on_device(
    tokens,
    qkv_weight,
    out_weight,
    gate_up_weight,
    down_weight,
    attn_gain,
    ffn_gain,
    query_gain,
    key_gain,
    seq_lengths,
    block_order,
    cotangent,
):
    inputs = tokens[0].astype(jnp.float32)
    rows_here = inputs.shape[0]
    ctx_size = lax.axis_size("ctx")
    ctx_index = lax.axis_index("ctx")
    per_group = HEADS // KV_HEADS
    q_width = HEADS * HD
    kv_width = KV_HEADS * HD
    order_row = block_order[0]
    lengths_row = seq_lengths[0]
    slots = jnp.arange(rows_here, dtype=jnp.int32) // BLK + ctx_index * (rows_here // BLK)
    table = slots[:, None] == jnp.arange(order_row.shape[0], dtype=jnp.int32)[None, :]
    packed = (
        jnp.sum(jnp.where(table, order_row[None, :], 0), axis=1) * BLK
        + jnp.arange(rows_here, dtype=jnp.int32) % BLK
    )
    local = packed - starts_of(packed, lengths_row)
    frequency = ROPE_BASE ** (-2.0 * jnp.arange(HD // 2, dtype=jnp.float32) / HD)
    angle = frequency[:, None] * local.astype(jnp.float32)[None, :]
    cosine = jnp.cos(angle)[None]
    sine = jnp.sin(angle)[None]
    bf16, f32 = jnp.bfloat16, jnp.float32
    parts = ctx_size // HEADS
    part = ctx_index // HEADS
    part_blocks = HEADS * rows_here // BLK
    q_order = lax.dynamic_slice_in_dim(order_row, part * part_blocks, part_blocks)
    q_slot, q_place, q_start = block_tables(q_order, lengths_row)
    q_slot = q_slot + part * part_blocks
    kv_slot, _, _ = block_tables(order_row, lengths_row)
    first = jnp.min(q_start.reshape(-1, TILE), axis=1) // TILE
    last = jnp.max(q_place.reshape(-1, TILE), axis=1) // TILE + 1
    tables = (q_slot, kv_slot, first, last)
    q_rows, kv_rows = part_blocks * BLK, order_row.shape[0] * BLK

    def fetch_attention():
        return (
            lax.all_gather(qkv_weight, "fsdp", axis=0, tiled=True),
            lax.all_gather(out_weight, "fsdp", axis=0, tiled=True),
            lax.all_gather(attn_gain, "fsdp", axis=0, tiled=True),
            lax.all_gather(ffn_gain, "fsdp", axis=0, tiled=True),
            lax.all_gather(query_gain, "fsdp", axis=0, tiled=True),
            lax.all_gather(key_gain, "fsdp", axis=0, tiled=True),
        )

    w_qkv, w_out, gain_attn, gain_ffn, gain_query, gain_key = fetch_attention()
    gain_attn = gain_attn.astype(jnp.float32)
    gain_ffn = gain_ffn.astype(jnp.float32)
    gain_query = gain_query.astype(jnp.float32)
    gain_key = gain_key.astype(jnp.float32)
    scale_one = rms_scale(inputs)
    normed = (inputs * scale_one * gain_attn).astype(jnp.bfloat16)
    projected = lax.dot_general(
        w_qkv, normed, (((0,), (1,)), ((), ())), preferred_element_type=f32
    )
    q_raw = projected[:q_width].reshape(HEADS, HD, rows_here)
    k_raw = projected[q_width : q_width + kv_width].reshape(KV_HEADS, HD, rows_here)
    values_here = projected[q_width + kv_width :].reshape(KV_HEADS, HD, rows_here).astype(bf16)
    q_scale = rms_scale(q_raw, 1)
    k_scale = rms_scale(k_raw, 1)
    column_query, column_key = gain_query[:, None], gain_key[:, None]
    queries = rope(q_raw * q_scale * column_query, cosine, sine).astype(bf16)
    keys_here = rope(k_raw * k_scale * column_key, cosine, sine).astype(bf16)
    sent = jnp.concatenate(
        [queries, jnp.repeat(keys_here, per_group, 0), jnp.repeat(values_here, per_group, 0)], axis=1
    )
    sent = jnp.concatenate([sent] * parts, axis=0)
    got = lax.all_to_all(sent, "ctx", 0, 0, tiled=True)
    q_place, q_start = q_place[None], q_start[None]
    shape = jax.ShapeDtypeStruct
    attn_sent, *held = kernel_call(
        attend_kernel,
        tables,
        (got, q_place, q_start),
        [
            shape((ctx_size, HD, rows_here), bf16),
            shape((q_rows, HD), bf16),
            shape((HD, q_rows), bf16),
            shape((kv_rows, HD), bf16),
            shape((HD, kv_rows), bf16),
            shape((kv_rows, HD), bf16),
            shape((HD, q_rows), f32),
            shape((1, q_rows), f32),
        ],
        [pltpu.VMEM((HD, kv_rows), bf16)],
        ATTEND,
    )
    attn_in = lax.dynamic_slice_in_dim(
        lax.all_to_all(attn_sent, "ctx", 0, 0, tiled=True), part * HEADS, HEADS
    ).reshape(q_width, rows_here)
    h_one = inputs + lax.dot_general(
        attn_in, w_out, (((0,), (0,)), ((), ())), preferred_element_type=f32
    )
    scale_two = rms_scale(h_one)
    normed_two = (h_one * scale_two * gain_ffn).astype(jnp.bfloat16)
    columns = normed_two
    gate_up = jnp.einsum(
        "tr,rgf->tgf",
        columns,
        lax.all_gather(gate_up_weight, "fsdp", axis=0, tiled=True),
        preferred_element_type=jnp.float32,
    )
    gate = gate_up[:, 0]
    upper = gate_up[:, 1]
    sigma = jax.nn.sigmoid(gate)
    hidden = (gate * sigma * upper).astype(jnp.bfloat16)
    columns = hidden
    ffn_out = jnp.dot(
        columns,
        lax.all_gather(down_weight, "fsdp", axis=0, tiled=True),
        preferred_element_type=jnp.float32,
    )
    output = (h_one + ffn_out).astype(jnp.bfloat16)
    d_out = cotangent[0].astype(jnp.float32)
    d_ffn = d_out.astype(jnp.bfloat16)
    d_hidden = lax.dot_general(
        d_ffn,
        lax.all_gather(down_weight, "fsdp", axis=0, tiled=True),
        (((1,), (1,)), ((), ())),
        preferred_element_type=jnp.float32,
    )
    d_gate = d_hidden * upper * sigma * (1.0 + gate * (1.0 - sigma))
    d_upper = d_hidden * gate * sigma
    d_gate_up = jnp.stack([d_gate, d_upper], axis=1).astype(jnp.bfloat16)
    d_normed_two = jnp.einsum(
        "tgf,rgf->tr",
        d_gate_up,
        lax.all_gather(gate_up_weight, "fsdp", axis=0, tiled=True),
        preferred_element_type=jnp.float32,
    )
    columns = normed_two
    grad_gate_up = lax.psum_scatter(
        jnp.einsum("tr,tgf->rgf", columns, d_gate_up, preferred_element_type=jnp.float32).astype(
            jnp.bfloat16
        ),
        "fsdp",
        scatter_dimension=0,
        tiled=True,
    )
    columns = hidden
    grad_down = lax.psum_scatter(
        lax.dot_general(
            columns, d_ffn, (((0,), (0,)), ((), ())), preferred_element_type=jnp.float32
        ).astype(jnp.bfloat16),
        "fsdp",
        scatter_dimension=0,
        tiled=True,
    )
    d_norm_two, ffn_gain_term = norm_back(d_normed_two, h_one, scale_two, gain_ffn)
    d_h_one = d_out + d_norm_two
    d_attn = d_h_one.astype(jnp.bfloat16)
    grad_out_here = jnp.dot(attn_in, d_attn, preferred_element_type=f32)
    d_heads = lax.dot_general(
        w_out, d_attn, (((1,), (1,)), ((), ())), preferred_element_type=f32
    ).astype(bf16)
    d_heads = jnp.concatenate([d_heads.reshape(HEADS, HD, rows_here)] * parts, axis=0)
    d_got = lax.all_to_all(d_heads, "ctx", 0, 0, tiled=True)
    (d_sent,) = kernel_call(
        attend_back_kernel,
        tables,
        (d_got, q_place, q_start, *held),
        [shape((ctx_size, 3 * HD, rows_here), bf16)],
        [
            pltpu.VMEM((HD, q_rows), bf16),
            pltpu.VMEM((q_rows, HD), bf16),
            pltpu.VMEM((kv_rows, HD), f32),
            pltpu.VMEM((kv_rows, HD), f32),
        ],
        ATTEND_BACK,
    )
    d_back = lax.all_to_all(d_sent, "ctx", 0, 0, tiled=True)
    d_query = lax.dynamic_slice_in_dim(d_back[:, :HD], part * HEADS, HEADS).astype(f32)
    d_key_value = jnp.sum(
        d_back[:, HD:].reshape(parts, KV_HEADS, per_group, 2 * HD, rows_here).astype(f32),
        axis=(0, 2),
    )
    dq_normed = rope_back(d_query, cosine, sine)
    dk_normed = rope_back(d_key_value[:, :HD], cosine, sine)
    dq_raw, query_term = norm_back(dq_normed, q_raw, q_scale, column_query, 1)
    dk_raw, key_term = norm_back(dk_normed, k_raw, k_scale, column_key, 1)
    d_projected = jnp.concatenate(
        [
            dq_raw.reshape(q_width, rows_here).astype(bf16),
            dk_raw.reshape(kv_width, rows_here).astype(bf16),
            d_key_value[:, HD:].reshape(kv_width, rows_here).astype(bf16),
        ],
        axis=0,
    )
    grad_qkv_here = lax.dot_general(
        normed, d_projected, (((0,), (1,)), ((), ())), preferred_element_type=f32
    )
    d_normed = lax.dot_general(
        d_projected, w_qkv, (((0,), (1,)), ((), ())), preferred_element_type=f32
    )
    d_norm_one, attn_gain_term = norm_back(d_normed, inputs, scale_one, gain_attn)
    d_inputs = d_h_one + d_norm_one
    shard_qkv, shard_out, shard_attn_gain, shard_ffn_gain, shard_query_gain, shard_key_gain = (
        lax.psum_scatter(
            grad_qkv_here.astype(jnp.bfloat16), "fsdp", scatter_dimension=0, tiled=True
        ).astype(jnp.float32),
        lax.psum_scatter(
            grad_out_here.astype(jnp.bfloat16), "fsdp", scatter_dimension=0, tiled=True
        ).astype(jnp.float32),
        lax.psum_scatter(
            jnp.sum(attn_gain_term, axis=0).astype(jnp.bfloat16),
            "fsdp",
            scatter_dimension=0,
            tiled=True,
        ).astype(jnp.float32),
        lax.psum_scatter(
            jnp.sum(ffn_gain_term, axis=0).astype(jnp.bfloat16),
            "fsdp",
            scatter_dimension=0,
            tiled=True,
        ).astype(jnp.float32),
        lax.psum_scatter(
            jnp.sum(query_term, axis=(0, 2)).astype(jnp.bfloat16),
            "fsdp",
            scatter_dimension=0,
            tiled=True,
        ).astype(jnp.float32),
        lax.psum_scatter(
            jnp.sum(key_term, axis=(0, 2)).astype(jnp.bfloat16),
            "fsdp",
            scatter_dimension=0,
            tiled=True,
        ).astype(jnp.float32),
    )
    summed_grads = (
        lax.psum(shard_qkv.astype(jnp.bfloat16), "ctx").astype(jnp.float32),
        lax.psum(shard_out.astype(jnp.bfloat16), "ctx").astype(jnp.float32),
        lax.psum(grad_gate_up, "ctx").astype(jnp.float32),
        lax.psum(grad_down, "ctx").astype(jnp.float32),
        lax.psum(shard_attn_gain.astype(jnp.bfloat16), "ctx").astype(jnp.float32),
        lax.psum(shard_ffn_gain.astype(jnp.bfloat16), "ctx").astype(jnp.float32),
        lax.psum(shard_query_gain.astype(jnp.bfloat16), "ctx").astype(jnp.float32),
        lax.psum(shard_key_gain.astype(jnp.bfloat16), "ctx").astype(jnp.float32),
    )
    return (
        output[None],
        d_inputs[None],
        summed_grads[0],
        summed_grads[1],
        summed_grads[2],
        summed_grads[3],
        summed_grads[4],
        summed_grads[5],
        summed_grads[6],
        summed_grads[7],
    )


def solution(mesh):
    block = mesh.shape["fsdp"] == 2 and mesh.shape["ctx"] == 16
    return jax.shard_map(
        on_block if block else on_device,
        mesh=mesh,
        in_specs=(
            P("fsdp", "ctx", None),
            P("fsdp", None),
            P("fsdp", None),
            P("fsdp", None, None),
            P("fsdp", None),
            P("fsdp"),
            P("fsdp"),
            P("fsdp"),
            P("fsdp"),
            P("fsdp", None),
            P("fsdp", None),
            P("fsdp", "ctx", None),
        ),
        out_specs=(
            P("fsdp", "ctx", None),
            P("fsdp", "ctx", None),
            P("fsdp", None),
            P("fsdp", None),
            P("fsdp", None, None),
            P("fsdp", None),
            P("fsdp"),
            P("fsdp"),
            P("fsdp"),
            P("fsdp"),
        ),
        check_vma=False,
    )
```

```python
import functools

import jax
import jax.numpy as jnp
from jax import lax
from jax.experimental import pallas as pl
from jax.experimental.pallas import tpu as pltpu
from jax.sharding import PartitionSpec as P

HEADS = 16
KV_HEADS = 8
HD = 64
BLK = 128
TILE = 256
CHUNKS = 2
PROJECT = 0
ATTEND = 22
OUT = 0
FFN = (0, 0)
ATTEND_BACK = 25


EPSILON = 1e-05
ROPE_BASE = 1000000.0
LOG2E = 1.4426950408889634
SCORE_SCALE = LOG2E * HD ** (-0.5)


def rms_scale(values, axis=-1):
    return lax.rsqrt(jnp.mean(values * values, axis=axis, keepdims=True) + EPSILON)


def norm_back(grad_normed, inputs, scale, gain, axis=-1):
    scaled = grad_normed * gain
    grad_in = scale * scaled - inputs * scale * scale * scale * jnp.mean(
        scaled * inputs, axis=axis, keepdims=True
    )
    return (grad_in, grad_normed * inputs * scale)


def rope(values, cosine, sine):
    half = HD // 2
    first, second = values[:, :half], values[:, half:]
    return jnp.concatenate([first * cosine - second * sine, second * cosine + first * sine], axis=1)


def rope_back(values, cosine, sine):
    half = HD // 2
    first, second = values[:, :half], values[:, half:]
    return jnp.concatenate([first * cosine + second * sine, second * cosine - first * sine], axis=1)


def starts_of(packed, lengths_row):
    ends = jnp.cumsum(lengths_row)
    past = packed[:, None] >= ends[None, :]
    return jnp.sum(jnp.where(past, lengths_row[None, :], 0), axis=1)


def block_tables(order, lengths_row):
    count = order.shape[0]
    rank = jnp.sum((order[None, :] < order[:, None]).astype(jnp.int32), axis=1)
    hit = rank[None, :] == jnp.arange(count, dtype=jnp.int32)[:, None]
    slot = jnp.sum(jnp.where(hit, jnp.arange(count, dtype=jnp.int32)[None, :], 0), axis=1)
    block = jnp.sum(jnp.where(hit, order[None, :], 0), axis=1)
    place = (block[:, None] * BLK + jnp.arange(BLK, dtype=jnp.int32)[None, :]).reshape(-1)
    return (slot, place, starts_of(place, lengths_row))


def attend_kernel(
    q_slot, kv_slot, first, last, qkv_ref, place_ref, start_ref,
    out_ref, q_ref, qt_ref, k_ref, kt_ref, v_ref, ot_ref, total_ref, vt_ref
):
    per_device = qkv_ref.shape[2] // BLK
    kv_blocks = k_ref.shape[0] // BLK
    q_blocks = q_ref.shape[0] // BLK

    def piece(slot, lower):
        return qkv_ref[
            slot // per_device,
            lower : lower + HD,
            pl.ds(pl.multiple_of((slot % per_device) * BLK, BLK), BLK),
        ]

    for i in range(kv_blocks):
        here = slice(i * BLK, (i + 1) * BLK)
        keys = piece(kv_slot[i], HD)
        kt_ref[:, here] = keys
        k_ref[here, :] = keys.T
        values = piece(kv_slot[i], 2 * HD)
        vt_ref[:, here] = values
        v_ref[here, :] = values.T
    for i in range(q_blocks):
        here = slice(i * BLK, (i + 1) * BLK)
        queries = piece(q_slot[i], 0)
        qt_ref[:, here] = queries
        q_ref[here, :] = queries.T
    if q_blocks < kv_blocks:
        out_ref[...] = jnp.zeros_like(out_ref)

    def tile(i, carry):
        rows = pl.ds(pl.multiple_of(i * TILE, TILE), TILE)
        queries = qt_ref[:, rows]
        place = place_ref[:, rows]
        start = start_ref[:, rows]

        def step(j, state):
            total, summed = state
            at = pl.multiple_of(j * TILE, TILE)
            scores = jnp.dot(
                k_ref[pl.ds(at, TILE), :], queries, preferred_element_type=jnp.float32
            )
            key_place = lax.broadcasted_iota(jnp.int32, (TILE, TILE), 0) + at
            allowed = (key_place <= place) & (key_place >= start)
            lifted = jnp.where(allowed, jnp.exp2(scores * SCORE_SCALE), 0.0)
            total = total + jnp.sum(lifted, axis=0, keepdims=True)
            summed = summed + jnp.dot(
                vt_ref[:, pl.ds(at, TILE)],
                lifted.astype(jnp.bfloat16),
                preferred_element_type=jnp.float32,
            )
            return (total, summed)

        total, summed = lax.fori_loop(
            first[i],
            last[i],
            step,
            (jnp.zeros((1, TILE), jnp.float32), jnp.zeros((HD, TILE), jnp.float32)),
        )
        attn = summed / total
        ot_ref[:, rows] = attn
        total_ref[:, rows] = jnp.log(total) * LOG2E
        rounded = attn.astype(jnp.bfloat16)
        for part in range(TILE // BLK):
            slot = q_slot[i * (TILE // BLK) + part]
            out_ref[
                slot // per_device,
                :,
                pl.ds(pl.multiple_of((slot % per_device) * BLK, BLK), BLK),
            ] = rounded[:, part * BLK : (part + 1) * BLK]
        return carry

    lax.fori_loop(0, q_blocks * BLK // TILE, tile, 0)


def attend_back_kernel(
    q_slot, kv_slot, first, last, d_ref, place_ref, start_ref,
    q_ref, qt_ref, k_ref, kt_ref, v_ref, ot_ref, total_ref,
    out_ref, dt_ref, do_ref, dk_ref, dv_ref
):
    per_device = d_ref.shape[2] // BLK
    kv_blocks = k_ref.shape[0] // BLK
    q_blocks = q_ref.shape[0] // BLK

    def lanes(slot):
        return pl.ds(pl.multiple_of((slot % per_device) * BLK, BLK), BLK)

    for i in range(q_blocks):
        here = slice(i * BLK, (i + 1) * BLK)
        slot = q_slot[i]
        grads = d_ref[slot // per_device, :, lanes(slot)]
        dt_ref[:, here] = grads
        do_ref[here, :] = grads.T
    dk_ref[...] = jnp.zeros_like(dk_ref)
    dv_ref[...] = jnp.zeros_like(dv_ref)
    if q_blocks < kv_blocks:
        out_ref[...] = jnp.zeros_like(out_ref)

    def tile(i, carry):
        rows = pl.ds(pl.multiple_of(i * TILE, TILE), TILE)
        queries = qt_ref[:, rows]
        grads = dt_ref[:, rows]
        place = place_ref[:, rows]
        start = start_ref[:, rows]
        delta = jnp.sum(grads.astype(jnp.float32) * ot_ref[:, rows], axis=0, keepdims=True)
        total = total_ref[:, rows]

        def step(j, d_query):
            at = pl.multiple_of(j * TILE, TILE)
            here = pl.ds(at, TILE)
            scores = jnp.dot(k_ref[here, :], queries, preferred_element_type=jnp.float32)
            key_place = lax.broadcasted_iota(jnp.int32, (TILE, TILE), 0) + at
            allowed = (key_place <= place) & (key_place >= start)
            shares = jnp.where(allowed, jnp.exp2(scores * SCORE_SCALE - total), 0.0)
            d_shares = jnp.dot(v_ref[here, :], grads, preferred_element_type=jnp.float32)
            d_scores = (shares * (d_shares - delta)).astype(jnp.bfloat16)
            dv_ref[here, :] += jnp.dot(
                shares.astype(jnp.bfloat16), do_ref[rows, :], preferred_element_type=jnp.float32
            )
            dk_ref[here, :] += jnp.dot(
                d_scores, q_ref[rows, :], preferred_element_type=jnp.float32
            )
            return d_query + jnp.dot(
                kt_ref[:, here], d_scores, preferred_element_type=jnp.float32
            )

        d_query = lax.fori_loop(first[i], last[i], step, jnp.zeros((HD, TILE), jnp.float32))
        rounded = (d_query * HD ** (-0.5)).astype(jnp.bfloat16)
        for part in range(TILE // BLK):
            slot = q_slot[i * (TILE // BLK) + part]
            out_ref[slot // per_device, 0:HD, lanes(slot)] = rounded[
                :, part * BLK : (part + 1) * BLK
            ]
        return carry

    lax.fori_loop(0, q_blocks * BLK // TILE, tile, 0)
    for i in range(kv_blocks):
        here = slice(i * BLK, (i + 1) * BLK)
        slot = kv_slot[i]
        out_ref[slot // per_device, HD : 2 * HD, lanes(slot)] = (
            (dk_ref[here, :] * HD ** (-0.5)).T.astype(jnp.bfloat16)
        )
        out_ref[slot // per_device, 2 * HD : 3 * HD, lanes(slot)] = (
            dv_ref[here, :].T.astype(jnp.bfloat16)
        )


def cost(micros):
    return pl.CostEstimate(
        flops=1 + micros * 1_000_000_000, bytes_accessed=1, transcendentals=0
    )


def kernel_call(kernel, tables, arrays, outs, scratch, micros):
    smem = pl.BlockSpec(memory_space=pltpu.SMEM)
    vmem = pl.BlockSpec(memory_space=pltpu.VMEM)
    return pl.pallas_call(
        kernel,
        out_shape=outs,
        in_specs=[smem] * len(tables) + [vmem] * len(arrays),
        out_specs=[vmem] * len(outs),
        scratch_shapes=scratch,
        compiler_params=pltpu.CompilerParams(vmem_limit_bytes=48 * 1024 * 1024),
        cost_estimate=cost(micros),
    )(*tables, *arrays)


class Links:
    def __init__(self, ctx_size):
        self.depth = ctx_size // 4
        index = lax.axis_index("ctx")
        self.core = index % 2
        self.y = (index // 2) % 2
        self.side = lax.axis_index("fsdp")
        self.half = ((index // 4 + 1) // 2) % 2
        self.quarter = index % 2 * 2 + self.y
        self.here = jnp.stack([self.half, self.core, self.y, self.side]).astype(jnp.int32)

    def route(self, place):
        pairs = []
        for z in range(self.depth):
            for y in range(2):
                for core in range(2):
                    to_z, to_y, to_core = place(z, y, core)
                    pairs.append(((z * 2 + y) * 2 + core, (to_z * 2 + to_y) * 2 + to_core))
        return pairs

    def over_core(self, value):
        return lax.ppermute(value, "ctx", self.route(lambda z, y, c: (z, y, 1 - c)))

    def over_y(self, value):
        return lax.ppermute(value, "ctx", self.route(lambda z, y, c: (z, 1 - y, c)))

    def over_z(self, value):
        return lax.ppermute(value, "ctx", self.route(lambda z, y, c: (z ^ 1, y, c)))

    def mirror_z(self, value):
        return lax.ppermute(value, "ctx", self.route(lambda z, y, c: (self.depth - 1 - z, y, c)))

    def over_x(self, value):
        return lax.ppermute(value, "fsdp", [(0, 1), (1, 0)])

    def spread_plane(self, value):
        across = self.over_core(value)
        beside = self.over_y(value)
        return (value, across, beside, self.over_core(beside))

    def deal_plane(self, near, far, give, give_far):
        got, got_far = self.over_core(give), self.over_core(give_far)
        return (near, got, self.over_y(far), self.over_y(got_far))

    def sum_depth(self, kept, got, time=None):
        def half(index):
            return add(pick(kept, index, 0), pick(got, index, 0))

        given = self.over_z(half(1 - self.half))
        part = add(half(self.half), given)
        other = self.mirror_z(part)
        full = add(part, other if time is None else after(other, time))
        return jnp.stack([full, self.over_z(full)])


def pick(value, index, axis):
    return lax.dynamic_index_in_dim(value, index, axis, keepdims=False)


def add(left, right):
    return (left.astype(jnp.float32) + right.astype(jnp.float32)).astype(jnp.bfloat16)


def after(value, *others):
    return lax.optimization_barrier((value, *others))[0]


def contract(left, right, axes):
    return lax.dot_general(
        left, right, ((axes[:1], axes[1:]), ((), ())), preferred_element_type=jnp.float32
    )


PARAMS = pltpu.CompilerParams(vmem_limit_bytes=56 * 1024 * 1024)


def call_with_here(
    kernel, here, grid, arrays, specs, outs, out_specs, scratch=(), aliases=None, micros=5
):
    return pl.pallas_call(
        kernel,
        grid_spec=pltpu.PrefetchScalarGridSpec(
            num_scalar_prefetch=1,
            grid=grid,
            in_specs=specs,
            out_specs=out_specs,
            scratch_shapes=list(scratch),
        ),
        out_shape=outs,
        input_output_aliases=aliases or {},
        compiler_params=PARAMS,
        cost_estimate=cost(micros),
    )(here, *arrays)


def whole(array):
    rank = len(array.shape)
    return pl.BlockSpec(array.shape, lambda i, here: (0,) * rank)


def project_kernel(here, *refs):
    x_ref, gain_ref, own_ref = refs[:3]
    pieces, q_gain, k_gain, cos_ref, sin_ref = refs[3:7], refs[7], refs[8], refs[9], refs[10]
    sent, weight, q_ref, k_ref, q_scale, k_scale, normed_ref, scale_ref = refs[11:]
    core, y, side = here[1], here[2], here[3]
    rows = own_ref.shape[0]
    part = rows // 4
    f32, bf16 = jnp.float32, jnp.bfloat16
    weight[pl.ds(pl.multiple_of(side * rows, rows), rows), :] = own_ref[...]
    for p in range(4):
        at = (1 - side) * rows + (((p % 2) ^ core) * 2 + ((p // 2) ^ y)) * part
        weight[pl.ds(pl.multiple_of(at, part), part), :] = pieces[p][...]
    x = x_ref[...].astype(f32)
    scale = rms_scale(x)
    scale_ref[...] = scale
    normed = (x * scale * gain_ref[...]).astype(bf16)
    normed_ref[...] = normed.T
    cosine, sine = cos_ref[...], sin_ref[...]
    half = HD // 2

    def turned(raw, gain, raw_ref, kept_scale, head):
        raw_ref[head * HD : (head + 1) * HD, :] = raw
        scale = rms_scale(raw, 0)
        kept_scale[head : head + 1, :] = scale
        value = raw * scale * gain
        first, second = value[:half], value[half:]
        return jnp.concatenate(
            [first * cosine - second * sine, second * cosine + first * sine], axis=0
        ).astype(bf16)

    per_group = HEADS // KV_HEADS
    for at in range(0, weight.shape[1], 2 * BLK):
        block = jnp.dot(normed, weight[:, at : at + 2 * BLK], preferred_element_type=f32)
        turned_block = block.T
        for n in range(2 * BLK // HD):
            head = at // HD + n
            raw = turned_block[n * HD : (n + 1) * HD, :]
            if head < HEADS:
                sent[head, 0:HD, :] = turned(raw, q_gain[...], q_ref, q_scale, head)
                continue
            head -= HEADS
            if head < KV_HEADS:
                value, row = turned(raw, k_gain[...], k_ref, k_scale, head), HD
            else:
                value, row, head = raw.astype(bf16), 2 * HD, head - KV_HEADS
            for copy in range(per_group):
                sent[head * per_group + copy, row : row + HD, :] = value


def project(here, x, gain, own, pieces, q_gain, k_gain, cosine, sine):
    tokens, width = x.shape
    f32, bf16 = jnp.float32, jnp.bfloat16
    shape = jax.ShapeDtypeStruct
    arrays = [x, gain, own, *pieces, q_gain, k_gain, cosine, sine]
    outs = [
        shape((HEADS, 3 * HD, tokens), bf16),
        shape((width, own.shape[1]), bf16),
        shape((HEADS * HD, tokens), f32),
        shape((KV_HEADS * HD, tokens), f32),
        shape((HEADS, tokens), f32),
        shape((KV_HEADS, tokens), f32),
        shape((width, tokens), bf16),
        shape((tokens, 1), f32),
    ]
    return call_with_here(
        project_kernel, here, (1,), arrays, [whole(a) for a in arrays], outs,
        [whole(o) for o in outs], micros=PROJECT,
    )


def layer(array, index):
    return pl.BlockSpec((1, *array.shape[1:]), lambda i, here: (index, 0, 0))


def attend_out_kernel(here, *refs):
    attn_ref, x_ref, gain_ref, own_ref = refs[:4]
    pieces = refs[4:20]
    weight, h_ref, scale_ref, two_ref, two_t_ref = refs[20:]
    core, y, side = here[1], here[2], here[3]
    rows = own_ref.shape[0]
    part = rows // 4
    weight[pl.ds(pl.multiple_of(side * rows, rows), rows), :] = own_ref[...]
    for p in range(4):
        at = (1 - side) * rows + (((p % 2) ^ core) * 2 + ((p // 2) ^ y)) * part
        for n in range(4):
            piece = pieces[4 * p + n]
            wide = piece.shape[1]
            weight[pl.ds(pl.multiple_of(at, part), part), n * wide : (n + 1) * wide] = piece[...]
    attn = attn_ref[...].T
    h_one = x_ref[...].astype(jnp.float32) + jnp.dot(
        attn, weight[...], preferred_element_type=jnp.float32
    )
    scale = rms_scale(h_one)
    h_ref[...] = h_one
    scale_ref[...] = scale
    two = (h_one * scale * gain_ref[...]).astype(jnp.bfloat16)
    two_ref[...] = two
    two_t_ref[...] = two.T


def attend_out(here, attn, x, gain, own, pieces):
    tokens, width = x.shape
    f32, bf16 = jnp.float32, jnp.bfloat16
    shape = jax.ShapeDtypeStruct
    part = own.shape[0] // 4
    cuts = 4
    part_width = width // cuts
    first = pieces[0].shape[1] // part_width - cuts
    arrays = [attn, x, gain, own]
    specs = [whole(a) for a in arrays]
    for piece in pieces:
        for n in range(cuts):
            arrays.append(piece)
            specs.append(pl.BlockSpec((part, part_width), lambda i, here, n=n: (0, first + n)))
    outs = [
        shape((width, width), bf16),
        shape((tokens, width), f32),
        shape((tokens, 1), f32),
        shape((tokens, width), bf16),
        shape((width, tokens), bf16),
    ]
    return call_with_here(
        attend_out_kernel, here, (1,), arrays, specs, outs, [whole(o) for o in outs], micros=OUT
    )


def ffn_kernel(chunk, here, *refs):
    two_ref, d_ref, own_ref = refs[:3]
    pieces, down_ref, down_pieces = (refs[3:7], refs[7:11]), refs[11], refs[12:16]
    refs = refs[4:]
    if chunk == 0:
        before_refs, refs = refs[12:13], refs[13:]
        near, far, give, give_far, out_ref, d_two_ref = refs[:6]
        refs = refs[6:]
    else:
        before_refs, gain_ref, refs = refs[12:17], refs[17], refs[18:]
        near, far, give, give_far = refs[:4]
        out_ref, d_h_ref, d_attn_ref, heads_ref, gain_term_ref = refs[4:9]
        refs = refs[9:]
    weight, down, hidden_rows, out_sum, two_sum = refs[:5]
    held, weight_sem, down_sem, before_sem = refs[5:-3], refs[-3], refs[-2], refs[-1]
    core, y, side = here[1], here[2], here[3]
    f32, bf16 = jnp.float32, jnp.bfloat16
    own_rows, columns = own_ref.shape[1], own_ref.shape[2] // CHUNKS
    part = own_rows // 4
    tile = columns // FFN_TILES
    half = columns // 2

    def quarter(p):
        return ((p % 2) ^ core) * 2 + ((p // 2) ^ y)

    def copies(n):
        at = slice(n * tile, (n + 1) * tile)
        mine = pl.ds(pl.multiple_of(side * own_rows, own_rows), own_rows)
        found = [
            pltpu.make_async_copy(
                own_ref.at[:, :, chunk * columns + n * tile : chunk * columns + (n + 1) * tile],
                weight.at[:, mine, at],
                weight_sem.at[n, 0],
            )
        ]
        for p in range(4):
            rows = pl.ds(pl.multiple_of((1 - side) * own_rows + quarter(p) * part, part), part)
            for kind in range(2):
                begin = n * tile + (columns if kind == 1 and chunk == 1 else 0)
                found.append(
                    pltpu.make_async_copy(
                        pieces[kind][p].at[:, begin : begin + tile],
                        weight.at[kind, rows, at],
                        weight_sem.at[n, 1 + 2 * p + kind],
                    )
                )
        return found

    def own_down(n):
        at = slice(n * tile, (n + 1) * tile)
        return [pltpu.make_async_copy(down_ref.at[at, :], down.at[at, :], down_sem.at[n, 0])]

    def other_down(n):
        at = slice(n * tile, (n + 1) * tile)
        found = []
        for p in range(4):
            wide = down_pieces[p].shape[1]
            lanes = pl.ds(pl.multiple_of(quarter(p) * wide, wide), wide)
            found.append(
                pltpu.make_async_copy(
                    down_pieces[p].at[at, :], down.at[at, lanes], down_sem.at[n, p]
                )
            )
        return found

    def each(action, n):
        for copy in copies(n):
            action(copy)

        @pl.when(side == chunk)
        def _():
            for copy in own_down(n):
                action(copy)

        @pl.when(side != chunk)
        def _():
            for copy in other_down(n):
                action(copy)

    before = [
        pltpu.make_async_copy(ref, held[n], before_sem.at[n]) for n, ref in enumerate(before_refs)
    ]
    for n in range(FFN_TILES):
        each(lambda copy: copy.start(), n)
    for copy in before:
        copy.start()
    two = two_ref[...]
    d_ffn = d_ref[...]
    for n in range(FFN_TILES):
        each(lambda copy: copy.wait(), n)
        at = slice(n * tile, (n + 1) * tile)
        gate = jnp.dot(two, weight[0, :, at], preferred_element_type=f32)
        upper = jnp.dot(two, weight[1, :, at], preferred_element_type=f32)
        d_hidden = contract(d_ffn, down[at, :], (1, 1))
        sigma = jax.nn.sigmoid(gate)
        silu = gate * sigma
        hidden = (silu * upper).astype(bf16)
        d_gate = (d_hidden * upper * sigma * (1.0 + gate * (1.0 - sigma))).astype(bf16)
        d_upper = (d_hidden * silu).astype(bf16)
        out_term = jnp.dot(hidden, down[at, :], preferred_element_type=f32)
        two_term = contract(d_gate, weight[0, :, at], (1, 1)) + contract(
            d_upper, weight[1, :, at], (1, 1)
        )
        out_sum[...] = out_term if n == 0 else out_sum[...] + out_term
        two_sum[...] = two_term if n == 0 else two_sum[...] + two_term
        hidden_rows[:, at] = hidden
        mine = jnp.where(core == 0, d_gate, d_upper)
        other = jnp.where(core == 0, d_upper, d_gate)
        for column in range(2):
            begin, end = max(n * tile, column * half), min((n + 1) * tile, (column + 1) * half)
            if begin >= end:
                continue
            source = slice(begin - n * tile, end - n * tile)
            target = slice(begin - column * half, end - column * half)
            first, second = mine[:, source], other[:, source]

            @pl.when(y == column)
            def _(first=first, second=second, target=target):
                near[:, target] = first
                give[:, target] = second

            @pl.when(y != column)
            def _(first=first, second=second, target=target):
                far[:, target] = first
                give_far[:, target] = second

    share = half // 2
    target = slice(half, half + share)
    for owner in range(2):
        lower = hidden_rows[:, owner * half : owner * half + share]
        upper = hidden_rows[:, owner * half + share : (owner + 1) * half]
        close = jnp.where(y == 0, lower, upper)
        distant = jnp.where(y == 0, upper, lower)

        @pl.when(core == owner)
        def _(close=close, distant=distant):
            near[:, target] = close
            far[:, target] = distant

        @pl.when(core != owner)
        def _(close=close, distant=distant):
            give[:, target] = close
            give_far[:, target] = distant

    for copy in before:
        copy.wait()
    if chunk == 0:
        out_ref[...] = held[0][...] + out_sum[...]
        d_two_ref[...] = two_sum[...]
    else:
        out_before, two_before, h_one, scale, w_out = held
        out_ref[...] = (out_before[...] + out_sum[...]).astype(bf16)
        d_norm, gain_term = norm_back(
            two_before[...] + two_sum[...], h_one[...], scale[...], gain_ref[...]
        )
        gain_term_ref[...] = jnp.sum(gain_term, axis=0, keepdims=True)
        d_h_one = d_ffn.astype(f32) + d_norm
        d_h_ref[...] = d_h_one
        d_attn = d_h_one.astype(bf16)
        d_attn_ref[...] = d_attn
        heads_ref[...] = contract(w_out[...], d_attn, (1, 1)).astype(bf16)


FFN_TILES = 3


def ffn(here, chunk, two, d_ffn, own, pieces, down, down_pieces, before, gain=None):
    tokens, width = two.shape
    columns = own.shape[2] // CHUNKS
    padded = (columns // 2 + columns // 4 + BLK - 1) // BLK * BLK
    shape = jax.ShapeDtypeStruct
    f32, bf16 = jnp.float32, jnp.bfloat16
    outs = [shape((tokens, padded), bf16)] * 4
    if chunk == 0:
        outs += [shape((tokens, width), f32)] * 2
    else:
        outs += [
            shape((tokens, width), bf16),
            shape((tokens, width), f32),
            shape((tokens, width), bf16),
            shape((width, tokens), bf16),
            shape((1, width), f32),
        ]
    far_away = pl.BlockSpec(memory_space=pl.ANY)
    arrays = [two, d_ffn, own, *pieces[0], *pieces[1], down, *down_pieces, *before]
    specs = [whole(two), whole(d_ffn)] + [far_away] * (len(arrays) - 2)
    if gain is not None:
        arrays.append(gain)
        specs.append(whole(gain))
    got = call_with_here(
        functools.partial(ffn_kernel, chunk),
        here,
        (1,),
        arrays,
        specs,
        outs,
        [whole(o) for o in outs],
        [
            pltpu.VMEM((2, width, columns), bf16),
            pltpu.VMEM((columns, width), bf16),
            pltpu.VMEM((tokens, columns), bf16),
            pltpu.VMEM((tokens, width), f32),
            pltpu.VMEM((tokens, width), f32),
        ]
        + [pltpu.VMEM(v.shape, v.dtype) for v in before]
        + [
            pltpu.SemaphoreType.DMA((FFN_TILES, 9)),
            pltpu.SemaphoreType.DMA((FFN_TILES, 4)),
            pltpu.SemaphoreType.DMA((len(before),)),
        ],
        micros=FFN[chunk],
    )
    return got[:4], got[4:]


def wide_product_kernel(here, *refs):
    planes, terms = refs[:4], refs[4:8]
    sent, kept, left, right = refs[8:]
    tokens = planes[0].shape[1]
    columns = right.shape[1]
    for i in range(4):
        left[:, i * tokens : (i + 1) * tokens] = planes[i][...]
        right[i * tokens : (i + 1) * tokens, :] = terms[i][:, :columns]
    side = here[3]
    _, step, _ = kept.shape
    for half in range(2):
        for owner, out_ref in ((1 - side, sent), (side, kept)):
            place = pl.multiple_of(owner * 2 * step + half * step, step)
            out_ref[half] = jnp.dot(
                left[pl.ds(place, step), :], right[...], preferred_element_type=jnp.float32
            ).astype(out_ref.dtype)


def wide_products(here, two_plane, shares, columns):
    rows, tokens = two_plane[0].shape
    outs = [
        jax.ShapeDtypeStruct((2, rows // 4, columns), jnp.bfloat16),
        jax.ShapeDtypeStruct((2, rows // 4, columns), jnp.float32),
    ]
    arrays = [*two_plane, *shares]
    return call_with_here(
        wide_product_kernel,
        here,
        (1,),
        arrays,
        [whole(a) for a in two_plane]
        + [pl.BlockSpec((tokens, columns), lambda i, here: (0, 0))] * 4,
        outs,
        [whole(o) for o in outs],
        [
            pltpu.VMEM((rows, 4 * tokens), jnp.bfloat16),
            pltpu.VMEM((4 * tokens, columns), jnp.bfloat16),
        ],
        micros=8,
    )


def down_product_kernel(here, *refs):
    planes, terms = refs[:4], (refs[4:8], refs[8:12])
    sent, kept, left, right = refs[12:]
    tokens = planes[0].shape[0]
    rows = left.shape[0]
    for i in range(4):
        right[i * tokens : (i + 1) * tokens, :] = planes[i][...]
    for chunk in range(2):
        for i in range(4):
            share = terms[chunk][i]
            at = share.shape[1] // BLK * BLK - (rows + BLK - 1) // BLK * BLK
            left[:, i * tokens : (i + 1) * tokens] = share[:, at : at + rows].T
        for half in range(2):
            product = jnp.dot(
                left[half * rows // 2 : (half + 1) * rows // 2, :],
                right[...],
                preferred_element_type=jnp.float32,
            )

            @pl.when(here[3] == chunk)
            def _(product=product, half=half):
                kept[half] = product

            @pl.when(here[3] != chunk)
            def _(product=product, half=half):
                sent[half] = product.astype(sent.dtype)


def down_products(here, d_plane, first, second, rows):
    tokens, columns = d_plane[0].shape
    outs = [
        jax.ShapeDtypeStruct((2, rows // 2, columns), jnp.bfloat16),
        jax.ShapeDtypeStruct((2, rows // 2, columns), jnp.float32),
    ]
    return call_with_here(
        down_product_kernel,
        here,
        (1,),
        [*d_plane, *first, *second],
        [whole(a) for a in (*d_plane, *first, *second)],
        outs,
        [whole(o) for o in outs],
        [
            pltpu.VMEM((rows, 4 * tokens), jnp.bfloat16),
            pltpu.VMEM((4 * tokens, columns), jnp.bfloat16),
        ],
        micros=8,
    )


GAIN_ROWS = 16


def attention_back_kernel(here, *refs):
    d_ref, q_ref, k_ref, q_scale, k_scale, q_gain, k_gain, cos_ref, sin_ref = refs[:9]
    weight, x_ref, scale_ref, gain_ref, d_h_ref, d_attn_ref = refs[9:15]
    near, far, give, give_far, d_x_ref, gains_ref = refs[15:21]
    turned, natural = refs[21:]
    f32, bf16 = jnp.float32, jnp.bfloat16
    core, y = here[1], here[2]
    cosine, sine = cos_ref[...], sin_ref[...]
    half = HD // 2
    per_group = HEADS // KV_HEADS
    tokens = x_ref.shape[0]

    def back(grad, raw, scale, gain):
        first, second = grad[:half], grad[half:]
        normed = jnp.concatenate(
            [first * cosine + second * sine, second * cosine - first * sine], axis=0
        )
        return norm_back(normed, raw, scale, gain, 0)

    q_term = jnp.zeros((HD, tokens), f32)
    k_term = jnp.zeros((HD, tokens), f32)
    for head in range(HEADS):
        at = slice(head * HD, (head + 1) * HD)
        grad, term = back(
            d_ref[head, :HD, :].astype(f32), q_ref[at, :], q_scale[head : head + 1, :], q_gain[...]
        )
        turned[at, :] = grad.astype(bf16)
        q_term = q_term + term
    for head in range(KV_HEADS):
        at = slice(head * HD, (head + 1) * HD)
        both = d_ref[head * per_group, HD:, :].astype(f32)
        for other in range(1, per_group):
            both = both + d_ref[head * per_group + other, HD:, :].astype(f32)
        grad, term = back(both[:HD], k_ref[at, :], k_scale[head : head + 1, :], k_gain[...])
        place = HEADS * HD + head * HD
        turned[place : place + HD, :] = grad.astype(bf16)
        k_term = k_term + term
        place += KV_HEADS * HD
        turned[place : place + HD, :] = both[HD:].astype(bf16)
    rows = turned.shape[0] // 4
    columns = d_attn_ref.shape[1] // 4
    shares = ((near, core, y), (far, core, 1 - y), (give, 1 - core, y), (give_far, 1 - core, 1 - y))
    for out_ref, to_core, to_y in shares:
        share = to_core * 2 + to_y
        out_ref[:rows, :] = turned[pl.ds(pl.multiple_of(share * rows, rows), rows), :]
        out_ref[rows:, :] = d_attn_ref[:, pl.ds(pl.multiple_of(share * columns, columns), columns)]
    for at in range(0, turned.shape[0], 256):
        natural[:, at : at + 256] = turned[at : at + 256, :].T
    d_normed = contract(natural[...], weight[...], (1, 1))
    x = x_ref[...].astype(f32)
    d_norm, gain_term = norm_back(d_normed, x, scale_ref[...], gain_ref[...])
    d_x_ref[...] = d_h_ref[...] + d_norm
    gains_ref[...] = jnp.zeros_like(gains_ref)
    gains_ref[0:1, :] = jnp.sum(gain_term, axis=0, keepdims=True)
    gains_ref[1:2, 0:HD] = jnp.sum(q_term.T, axis=0, keepdims=True)
    gains_ref[2:3, 0:HD] = jnp.sum(k_term.T, axis=0, keepdims=True)


def attention_back(here, arrays):
    f32, bf16 = jnp.float32, jnp.bfloat16
    shape = jax.ShapeDtypeStruct
    weight, x = arrays[9], arrays[10]
    tokens, width = x.shape
    rows = weight.shape[1] // 4 + tokens
    assert width // 4 == tokens
    outs = [
        *[shape((rows, tokens), bf16)] * 4,
        shape((tokens, width), f32),
        shape((8, width), f32),
    ]
    return call_with_here(
        attention_back_kernel, here, (1,), arrays, [whole(a) for a in arrays], outs,
        [whole(o) for o in outs],
        [pltpu.VMEM((weight.shape[1], tokens), bf16), pltpu.VMEM((tokens, weight.shape[1]), bf16)],
        micros=12,
    )


def attention_product_kernel(here, *refs):
    planes, terms, gains_ref, ffn_gain_ref = refs[:4], refs[4:8], refs[8], refs[9]
    sent, kept, left, right, left_out, right_out = refs[10:]
    tokens = planes[0].shape[2]
    cut = right.shape[1]
    for i in range(4):
        at = slice(i * tokens, (i + 1) * tokens)
        left[:, at] = planes[i][0]
        left_out[:, at] = planes[i][1]
        share = terms[i]
        right[at, :] = share[:cut].T
        right_out[at, :] = share[cut:]
    step = left.shape[0] // 4
    for owner, out_ref in ((1 - here[3], sent), (here[3], kept)):
        for half in range(2):
            at = pl.ds(pl.multiple_of(owner * 2 * step + half * step, step), step)
            out_ref[half, :step, :cut] = jnp.dot(
                left[at, :], right[...], preferred_element_type=jnp.float32
            ).astype(out_ref.dtype)
            out_ref[half, :step, cut:] = jnp.dot(
                left_out[at, :], right_out[...], preferred_element_type=jnp.float32
            ).astype(out_ref.dtype)
        rows = gains_ref.shape[1] // 2
        mine = pl.ds(pl.multiple_of(owner * rows, rows), rows)
        wide = out_ref.shape[2] - rows
        block = jnp.concatenate(
            [
                jnp.concatenate([gains_ref[0:1, mine], gains_ref[1:2, 0:wide]], axis=1),
                jnp.concatenate([ffn_gain_ref[:, mine], gains_ref[2:3, 0:wide]], axis=1),
                jnp.zeros((GAIN_ROWS - 2, out_ref.shape[2]), jnp.float32),
            ],
            axis=0,
        )
        out_ref[0, step:, :] = block.astype(out_ref.dtype)
        out_ref[1, step:, :] = jnp.zeros((GAIN_ROWS, out_ref.shape[2]), out_ref.dtype)


def attention_products(here, pair_plane, shares, gains, ffn_gain):
    _, width, tokens = pair_plane[0].shape
    cut = shares[0].shape[0] - tokens
    shape = (2, width // 4 + GAIN_ROWS, cut + tokens)
    outs = [jax.ShapeDtypeStruct(shape, jnp.bfloat16), jax.ShapeDtypeStruct(shape, jnp.float32)]
    return call_with_here(
        attention_product_kernel,
        here,
        (1,),
        [*pair_plane, *shares, gains, ffn_gain],
        [whole(a) for a in (*pair_plane, *shares, gains, ffn_gain)],
        outs,
        [whole(o) for o in outs],
        [
            pltpu.VMEM((width, 4 * tokens), jnp.bfloat16),
            pltpu.VMEM((4 * tokens, cut), jnp.bfloat16),
            pltpu.VMEM((width, 4 * tokens), jnp.bfloat16),
            pltpu.VMEM((4 * tokens, tokens), jnp.bfloat16),
        ],
        micros=8,
    )


def place_gate_up_kernel(here, *refs):
    mine, across, beside, diagonal, out_ref = *refs[:4], refs[-1]
    pieces = (mine, across, beside, diagonal)
    wide = mine.shape[2]
    for case in range(4):
        core, y = case // 2, case % 2

        @pl.when((here[1] == core) & (here[2] == y))
        def _(core=core, y=y):
            for kind in range(2):
                for column in range(2):
                    value = pieces[(y ^ column) * 2 + (core ^ kind)][0]
                    out_ref[:, kind, column * wide : (column + 1) * wide] = value.astype(
                        jnp.float32
                    )


def place_gate_up(here, chunk, pieces, before):
    _, rows, wide = pieces[0].shape
    step = 64
    blocks = rows // step

    def source(i, here):
        return ((i // blocks) ^ here[0], i % blocks, 0)

    arrays = list(pieces)
    specs = [pl.BlockSpec((1, step, wide), source)] * 4
    aliases = {}
    if before is not None:
        arrays.append(before)
        specs.append(pl.BlockSpec(memory_space=pl.ANY))
        aliases = {5: 0}
    (out,) = call_with_here(
        place_gate_up_kernel,
        here,
        (2 * blocks,),
        arrays,
        specs,
        [jax.ShapeDtypeStruct((2 * rows, 2, 2 * wide * CHUNKS), jnp.float32)],
        [pl.BlockSpec((step, 2, 2 * wide), lambda i, here: (i, 0, chunk))],
        aliases=aliases,
        micros=10,
    )
    return out


def place_down(here, pieces):
    _, rows, columns = pieces[0].shape

    def kernel(here, *refs):
        for s in range(8):

            @pl.when(pl.program_id(0) == s)
            def _(s=s):
                refs[4][...] = refs[s % 4][s // 4].astype(jnp.float32)

    def target(s, here):
        half = (s // 4) ^ here[0]
        y = ((s // 2) % 2) ^ here[2]
        core = (s % 2) ^ here[1]
        return ((core * 2 + y) * 2 + half, 0)

    (out,) = call_with_here(
        kernel,
        here,
        (8,),
        list(pieces),
        [whole(v) for v in pieces],
        [jax.ShapeDtypeStruct((rows * 8, columns), jnp.float32)],
        [pl.BlockSpec((rows, columns), target)],
    )
    return out


def place_attention(here, pieces, cut):
    _, rows, columns = pieces[0].shape
    rows -= GAIN_ROWS

    def kernel(here, *refs):
        qkv_ref, out_ref, gains_ref = refs[4:]
        for s in range(8):

            @pl.when(pl.program_id(0) == s)
            def _(s=s):
                value = refs[s % 4][s // 4]
                qkv_ref[...] = value[:rows, :cut].astype(jnp.float32)
                out_ref[...] = value[:rows, cut:].astype(jnp.float32)
                gains = value[rows:].astype(jnp.float32)
                gains_ref[...] = gains if s == 0 else gains_ref[...] + gains

    def target(s, here):
        half = (s // 4) ^ here[0]
        return (half, ((s % 2) ^ here[1]) * 2 + (((s // 2) % 2) ^ here[2]))

    shape = jax.ShapeDtypeStruct
    f32 = jnp.float32
    gain_shape = (GAIN_ROWS, columns)
    return call_with_here(
        kernel,
        here,
        (8,),
        list(pieces),
        [whole(v) for v in pieces],
        [
            shape((2 * rows, 4 * cut), f32),
            shape((2 * rows, 4 * (columns - cut)), f32),
            shape(gain_shape, f32),
        ],
        [
            pl.BlockSpec((rows, cut), target),
            pl.BlockSpec((rows, columns - cut), target),
            pl.BlockSpec(gain_shape, lambda s, here: (0, 0)),
        ],
    )


def on_block(
    tokens,
    qkv_weight,
    out_weight,
    gate_up_weight,
    down_weight,
    attn_gain,
    ffn_gain,
    query_gain,
    key_gain,
    seq_lengths,
    block_order,
    cotangent,
):
    inputs = tokens[0].astype(jnp.float32)
    rows_here = inputs.shape[0]
    ctx_size = lax.axis_size("ctx")
    ctx_index = lax.axis_index("ctx")
    per_group = HEADS // KV_HEADS
    q_width = HEADS * HD
    kv_width = KV_HEADS * HD
    order_row = block_order[0]
    lengths_row = seq_lengths[0]
    slots = jnp.arange(rows_here, dtype=jnp.int32) // BLK + ctx_index * (rows_here // BLK)
    table = slots[:, None] == jnp.arange(order_row.shape[0], dtype=jnp.int32)[None, :]
    packed = (
        jnp.sum(jnp.where(table, order_row[None, :], 0), axis=1) * BLK
        + jnp.arange(rows_here, dtype=jnp.int32) % BLK
    )
    local = packed - starts_of(packed, lengths_row)
    frequency = ROPE_BASE ** (-2.0 * jnp.arange(HD // 2, dtype=jnp.float32) / HD)
    angle = frequency[:, None] * local.astype(jnp.float32)[None, :]
    cosine = jnp.cos(angle)[None]
    sine = jnp.sin(angle)[None]
    bf16, f32 = jnp.bfloat16, jnp.float32
    parts = ctx_size // HEADS
    part = ctx_index // HEADS
    part_blocks = HEADS * rows_here // BLK
    q_order = lax.dynamic_slice_in_dim(order_row, part * part_blocks, part_blocks)
    q_slot, q_place, q_start = block_tables(q_order, lengths_row)
    q_slot = q_slot + part * part_blocks
    kv_slot, _, _ = block_tables(order_row, lengths_row)
    first = jnp.min(q_start.reshape(-1, TILE), axis=1) // TILE
    last = jnp.max(q_place.reshape(-1, TILE), axis=1) // TILE + 1
    tables = (q_slot, kv_slot, first, last)
    q_rows, kv_rows = part_blocks * BLK, order_row.shape[0] * BLK

    links = Links(ctx_size)
    here = links.here
    width = inputs.shape[1]
    rows = qkv_weight.shape[0]
    part_rows = rows // 4

    def quarter_rows(weight):
        return lax.dynamic_slice_in_dim(weight, links.quarter * part_rows, part_rows)

    qkv_piece = quarter_rows(qkv_weight)
    gains_here = jnp.concatenate([after(attn_gain, qkv_piece), ffn_gain, query_gain, key_gain])
    gains_there = links.over_x(gains_here)

    def gain_of(at, size):
        mine, other = gains_here[at : at + size], gains_there[at : at + size]
        return jnp.where(
            links.side == 0, jnp.concatenate([mine, other]), jnp.concatenate([other, mine])
        ).astype(f32)

    gain_attn = gain_of(0, rows)
    gain_ffn = gain_of(rows, rows)
    gain_query = gain_of(2 * rows, HD // 2)
    gain_key = gain_of(2 * rows + HD // 2, HD // 2)
    ff_chunk = gate_up_weight.shape[2] // CHUNKS

    def gate_up_piece(chunk):
        piece = lax.dynamic_slice(
            gate_up_weight,
            (links.quarter * part_rows, 0, chunk * ff_chunk),
            (part_rows, 2, ff_chunk),
        )
        return [piece[:, 0], piece[:, 1]]

    qkv_there = links.over_x(qkv_piece)
    first_gate, first_up = gate_up_piece(0)
    first_piece = jnp.concatenate([first_gate, quarter_rows(out_weight)], axis=1)
    second_gate, second_up = gate_up_piece(1)
    second_piece = jnp.concatenate([second_gate, second_up], axis=1)
    down_piece = lax.dynamic_slice_in_dim(
        down_weight, links.quarter * (width // 4), width // 4, 1
    )
    d_ffn = cotangent[0]
    d_beside = links.over_y(d_ffn)
    tokens_here = tokens[0]
    qkv_there = after(qkv_there, first_piece, d_beside)
    first_there = links.over_x(after(first_piece, qkv_there))
    up_there = links.over_x(after(first_up, first_there))
    qkv_pieces = links.spread_plane(qkv_there)
    sent, w_qkv, q_raw, k_raw, q_scale, k_scale, normed, scale_one = project(
        here, after(tokens_here, first_there), gain_attn[None], qkv_weight, qkv_pieces,
        gain_query[:, None], gain_key[:, None], cosine[0], sine[0],
    )
    got = lax.all_to_all(sent, "ctx", 0, 0, tiled=True)
    gate_up = jnp.transpose(after(gate_up_weight, sent), (1, 0, 2))
    up_there = after(up_there, sent)
    down_there = links.over_x(after(down_piece, up_there))
    first_beside = links.over_y(first_there)
    up_beside = links.over_y(up_there)
    second_there = links.over_x(after(second_piece, down_there))
    down_beside = links.over_y(down_there)
    got = after(got, down_there, gate_up)
    q_place, q_start = q_place[None], q_start[None]
    shape = jax.ShapeDtypeStruct
    attn_sent, *held = kernel_call(
        attend_kernel,
        tables,
        (got, q_place, q_start),
        [
            shape((ctx_size, HD, rows_here), bf16),
            shape((q_rows, HD), bf16),
            shape((HD, q_rows), bf16),
            shape((kv_rows, HD), bf16),
            shape((HD, kv_rows), bf16),
            shape((kv_rows, HD), bf16),
            shape((HD, q_rows), f32),
            shape((1, q_rows), f32),
        ],
        [pltpu.VMEM((HD, kv_rows), bf16)],
        ATTEND,
    )
    attn_sent = after(attn_sent, up_beside)
    attn_in = lax.dynamic_slice_in_dim(
        lax.all_to_all(attn_sent, "ctx", 0, 0, tiled=True), part * HEADS, HEADS
    ).reshape(q_width, rows_here)
    second_there = after(second_there, attn_sent)

    def spread(there, beside, time):
        there, beside = after(there, time), after(beside, time)
        return (there, links.over_core(there), beside, links.over_core(beside))

    first_pieces = spread(first_there, first_beside, attn_sent)
    up_pieces = spread(up_there, up_beside, attn_in)
    down_pieces = spread(down_there, down_beside, attn_in)
    second_pieces = links.spread_plane(second_there)
    w_out, h_one, scale_two, two, two_t = attend_out(
        here, attn_in, tokens_here, gain_ffn[None], out_weight, first_pieces
    )
    d_plane = spread(d_ffn, d_beside, attn_sent)
    two = after(two, d_plane[1], d_plane[3])
    two_beside = links.over_y(two_t)
    dealt_here, (out_sum, two_sum) = ffn(
        here, 0, two, d_ffn, gate_up, (first_pieces, up_pieces), down_weight, down_pieces, [h_one]
    )
    near, far, give, give_far = dealt_here
    got_far = links.over_core(give_far)
    first_shares = (near, links.over_core(give), links.over_y(far), links.over_y(got_far))
    out_sum = after(out_sum, got_far)
    dealt_here, (output, d_h_one, d_attn, d_heads, ffn_gain_term) = ffn(
        here, 1, two, d_ffn, gate_up, (second_pieces, second_pieces), down_weight, down_pieces,
        [out_sum, two_sum, h_one, scale_two, w_out], gain_ffn[None],
    )
    second_shares = links.deal_plane(*dealt_here)

    def plane(value, beside, time):
        value, beside = after(value, time), after(beside, time)
        return (value, links.over_core(value), beside, links.over_core(beside))

    two_plane = plane(two_t, two_beside, d_heads)
    columns = ff_chunk // 2
    d_heads = d_heads.reshape(HEADS, HD, rows_here)
    pair = jnp.stack([after(normed, d_heads), attn_in])
    d_got = lax.all_to_all(d_heads, "ctx", 0, 0, tiled=True)
    first_products = wide_products(
        here, two_plane, [after(v, d_heads) for v in first_shares], columns
    )
    d_got = after(d_got, first_products[0], pair)
    (d_sent,) = kernel_call(
        attend_back_kernel,
        tables,
        (d_got, q_place, q_start, *held),
        [shape((ctx_size, 3 * HD, rows_here), bf16)],
        [
            pltpu.VMEM((HD, q_rows), bf16),
            pltpu.VMEM((q_rows, HD), bf16),
            pltpu.VMEM((kv_rows, HD), f32),
            pltpu.VMEM((kv_rows, HD), f32),
        ],
        ATTEND_BACK,
    )
    first_got = links.over_x(first_products[0])
    d_sent = after(d_sent, first_got, *second_shares[2:])
    d_back = lax.all_to_all(d_sent, "ctx", 0, 0, tiled=True)
    second_products = wide_products(
        here, two_plane, [after(v, d_sent) for v in second_shares], columns
    )
    down_terms = down_products(
        here, d_plane, first_shares, second_shares, columns // 2
    )
    second_got = links.over_x(after(second_products[0], first_got))
    *d_shares, d_inputs, gain_sums = attention_back(
        here,
        [
            d_back, q_raw, k_raw, q_scale, k_scale, gain_query[:, None], gain_key[:, None],
            cosine[0], sine[0], w_qkv, tokens_here, scale_one, gain_attn[None], d_h_one, d_attn,
        ],
    )
    second_got = after(second_got, d_shares[0])
    down_got = links.over_x(after(down_terms[0], second_got))
    pair_plane = plane(pair, links.over_y(after(pair, d_sent)), d_shares[0])
    first_pair = links.sum_depth(first_products[1], first_got, d_shares[0])
    second_pair = links.sum_depth(second_products[1], second_got)
    down_pair = links.sum_depth(down_terms[1], down_got)
    grad_gate_up = place_gate_up(here, 0, links.spread_plane(first_pair), None)
    second_spread = links.spread_plane(second_pair)
    down_spread = links.spread_plane(after(down_pair, grad_gate_up))
    attention_terms = attention_products(
        here, pair_plane, links.deal_plane(*d_shares), gain_sums, ffn_gain_term
    )
    cut = qkv_weight.shape[1] // 4
    attention_pair = links.sum_depth(attention_terms[1], links.over_x(attention_terms[0]))
    grad_gate_up = place_gate_up(here, 1, second_spread, grad_gate_up)
    attention_spread = links.spread_plane(after(attention_pair, grad_gate_up))
    grad_down = place_down(here, down_spread)
    grad_qkv, grad_out, gain_sums = place_attention(here, attention_spread, cut)
    at = links.side * (HD // 2)
    gain_grads = [
        gain_sums[0, :rows],
        gain_sums[1, :rows],
        lax.dynamic_slice_in_dim(gain_sums[0, rows : rows + HD], at, HD // 2),
        lax.dynamic_slice_in_dim(gain_sums[1, rows : rows + HD], at, HD // 2),
    ]
    return (
        output[None],
        d_inputs[None],
        grad_qkv,
        grad_out,
        grad_gate_up,
        grad_down,
        *gain_grads,
    )


def on_device(
    tokens,
    qkv_weight,
    out_weight,
    gate_up_weight,
    down_weight,
    attn_gain,
    ffn_gain,
    query_gain,
    key_gain,
    seq_lengths,
    block_order,
    cotangent,
):
    inputs = tokens[0].astype(jnp.float32)
    rows_here = inputs.shape[0]
    ctx_size = lax.axis_size("ctx")
    ctx_index = lax.axis_index("ctx")
    per_group = HEADS // KV_HEADS
    q_width = HEADS * HD
    kv_width = KV_HEADS * HD
    order_row = block_order[0]
    lengths_row = seq_lengths[0]
    slots = jnp.arange(rows_here, dtype=jnp.int32) // BLK + ctx_index * (rows_here // BLK)
    table = slots[:, None] == jnp.arange(order_row.shape[0], dtype=jnp.int32)[None, :]
    packed = (
        jnp.sum(jnp.where(table, order_row[None, :], 0), axis=1) * BLK
        + jnp.arange(rows_here, dtype=jnp.int32) % BLK
    )
    local = packed - starts_of(packed, lengths_row)
    frequency = ROPE_BASE ** (-2.0 * jnp.arange(HD // 2, dtype=jnp.float32) / HD)
    angle = frequency[:, None] * local.astype(jnp.float32)[None, :]
    cosine = jnp.cos(angle)[None]
    sine = jnp.sin(angle)[None]
    bf16, f32 = jnp.bfloat16, jnp.float32
    parts = ctx_size // HEADS
    part = ctx_index // HEADS
    part_blocks = HEADS * rows_here // BLK
    q_order = lax.dynamic_slice_in_dim(order_row, part * part_blocks, part_blocks)
    q_slot, q_place, q_start = block_tables(q_order, lengths_row)
    q_slot = q_slot + part * part_blocks
    kv_slot, _, _ = block_tables(order_row, lengths_row)
    first = jnp.min(q_start.reshape(-1, TILE), axis=1) // TILE
    last = jnp.max(q_place.reshape(-1, TILE), axis=1) // TILE + 1
    tables = (q_slot, kv_slot, first, last)
    q_rows, kv_rows = part_blocks * BLK, order_row.shape[0] * BLK

    def fetch_attention():
        return (
            lax.all_gather(qkv_weight, "fsdp", axis=0, tiled=True),
            lax.all_gather(out_weight, "fsdp", axis=0, tiled=True),
            lax.all_gather(attn_gain, "fsdp", axis=0, tiled=True),
            lax.all_gather(ffn_gain, "fsdp", axis=0, tiled=True),
            lax.all_gather(query_gain, "fsdp", axis=0, tiled=True),
            lax.all_gather(key_gain, "fsdp", axis=0, tiled=True),
        )

    w_qkv, w_out, gain_attn, gain_ffn, gain_query, gain_key = fetch_attention()
    gain_attn = gain_attn.astype(jnp.float32)
    gain_ffn = gain_ffn.astype(jnp.float32)
    gain_query = gain_query.astype(jnp.float32)
    gain_key = gain_key.astype(jnp.float32)
    scale_one = rms_scale(inputs)
    normed = (inputs * scale_one * gain_attn).astype(jnp.bfloat16)
    projected = lax.dot_general(
        w_qkv, normed, (((0,), (1,)), ((), ())), preferred_element_type=f32
    )
    q_raw = projected[:q_width].reshape(HEADS, HD, rows_here)
    k_raw = projected[q_width : q_width + kv_width].reshape(KV_HEADS, HD, rows_here)
    values_here = projected[q_width + kv_width :].reshape(KV_HEADS, HD, rows_here).astype(bf16)
    q_scale = rms_scale(q_raw, 1)
    k_scale = rms_scale(k_raw, 1)
    column_query, column_key = gain_query[:, None], gain_key[:, None]
    queries = rope(q_raw * q_scale * column_query, cosine, sine).astype(bf16)
    keys_here = rope(k_raw * k_scale * column_key, cosine, sine).astype(bf16)
    sent = jnp.concatenate(
        [queries, jnp.repeat(keys_here, per_group, 0), jnp.repeat(values_here, per_group, 0)], axis=1
    )
    sent = jnp.concatenate([sent] * parts, axis=0)
    got = lax.all_to_all(sent, "ctx", 0, 0, tiled=True)
    q_place, q_start = q_place[None], q_start[None]
    shape = jax.ShapeDtypeStruct
    attn_sent, *held = kernel_call(
        attend_kernel,
        tables,
        (got, q_place, q_start),
        [
            shape((ctx_size, HD, rows_here), bf16),
            shape((q_rows, HD), bf16),
            shape((HD, q_rows), bf16),
            shape((kv_rows, HD), bf16),
            shape((HD, kv_rows), bf16),
            shape((kv_rows, HD), bf16),
            shape((HD, q_rows), f32),
            shape((1, q_rows), f32),
        ],
        [pltpu.VMEM((HD, kv_rows), bf16)],
        ATTEND,
    )
    attn_in = lax.dynamic_slice_in_dim(
        lax.all_to_all(attn_sent, "ctx", 0, 0, tiled=True), part * HEADS, HEADS
    ).reshape(q_width, rows_here)
    h_one = inputs + lax.dot_general(
        attn_in, w_out, (((0,), (0,)), ((), ())), preferred_element_type=f32
    )
    scale_two = rms_scale(h_one)
    normed_two = (h_one * scale_two * gain_ffn).astype(jnp.bfloat16)
    columns = normed_two
    gate_up = jnp.einsum(
        "tr,rgf->tgf",
        columns,
        lax.all_gather(gate_up_weight, "fsdp", axis=0, tiled=True),
        preferred_element_type=jnp.float32,
    )
    gate = gate_up[:, 0]
    upper = gate_up[:, 1]
    sigma = jax.nn.sigmoid(gate)
    hidden = (gate * sigma * upper).astype(jnp.bfloat16)
    columns = hidden
    ffn_out = jnp.dot(
        columns,
        lax.all_gather(down_weight, "fsdp", axis=0, tiled=True),
        preferred_element_type=jnp.float32,
    )
    output = (h_one + ffn_out).astype(jnp.bfloat16)
    d_out = cotangent[0].astype(jnp.float32)
    d_ffn = d_out.astype(jnp.bfloat16)
    d_hidden = lax.dot_general(
        d_ffn,
        lax.all_gather(down_weight, "fsdp", axis=0, tiled=True),
        (((1,), (1,)), ((), ())),
        preferred_element_type=jnp.float32,
    )
    d_gate = d_hidden * upper * sigma * (1.0 + gate * (1.0 - sigma))
    d_upper = d_hidden * gate * sigma
    d_gate_up = jnp.stack([d_gate, d_upper], axis=1).astype(jnp.bfloat16)
    d_normed_two = jnp.einsum(
        "tgf,rgf->tr",
        d_gate_up,
        lax.all_gather(gate_up_weight, "fsdp", axis=0, tiled=True),
        preferred_element_type=jnp.float32,
    )
    columns = normed_two
    grad_gate_up = lax.psum_scatter(
        jnp.einsum("tr,tgf->rgf", columns, d_gate_up, preferred_element_type=jnp.float32).astype(
            jnp.bfloat16
        ),
        "fsdp",
        scatter_dimension=0,
        tiled=True,
    )
    columns = hidden
    grad_down = lax.psum_scatter(
        lax.dot_general(
            columns, d_ffn, (((0,), (0,)), ((), ())), preferred_element_type=jnp.float32
        ).astype(jnp.bfloat16),
        "fsdp",
        scatter_dimension=0,
        tiled=True,
    )
    d_norm_two, ffn_gain_term = norm_back(d_normed_two, h_one, scale_two, gain_ffn)
    d_h_one = d_out + d_norm_two
    d_attn = d_h_one.astype(jnp.bfloat16)
    grad_out_here = jnp.dot(attn_in, d_attn, preferred_element_type=f32)
    d_heads = lax.dot_general(
        w_out, d_attn, (((1,), (1,)), ((), ())), preferred_element_type=f32
    ).astype(bf16)
    d_heads = jnp.concatenate([d_heads.reshape(HEADS, HD, rows_here)] * parts, axis=0)
    d_got = lax.all_to_all(d_heads, "ctx", 0, 0, tiled=True)
    (d_sent,) = kernel_call(
        attend_back_kernel,
        tables,
        (d_got, q_place, q_start, *held),
        [shape((ctx_size, 3 * HD, rows_here), bf16)],
        [
            pltpu.VMEM((HD, q_rows), bf16),
            pltpu.VMEM((q_rows, HD), bf16),
            pltpu.VMEM((kv_rows, HD), f32),
            pltpu.VMEM((kv_rows, HD), f32),
        ],
        ATTEND_BACK,
    )
    d_back = lax.all_to_all(d_sent, "ctx", 0, 0, tiled=True)
    d_query = lax.dynamic_slice_in_dim(d_back[:, :HD], part * HEADS, HEADS).astype(f32)
    d_key_value = jnp.sum(
        d_back[:, HD:].reshape(parts, KV_HEADS, per_group, 2 * HD, rows_here).astype(f32),
        axis=(0, 2),
    )
    dq_normed = rope_back(d_query, cosine, sine)
    dk_normed = rope_back(d_key_value[:, :HD], cosine, sine)
    dq_raw, query_term = norm_back(dq_normed, q_raw, q_scale, column_query, 1)
    dk_raw, key_term = norm_back(dk_normed, k_raw, k_scale, column_key, 1)
    d_projected = jnp.concatenate(
        [
            dq_raw.reshape(q_width, rows_here).astype(bf16),
            dk_raw.reshape(kv_width, rows_here).astype(bf16),
            d_key_value[:, HD:].reshape(kv_width, rows_here).astype(bf16),
        ],
        axis=0,
    )
    grad_qkv_here = lax.dot_general(
        normed, d_projected, (((0,), (1,)), ((), ())), preferred_element_type=f32
    )
    d_normed = lax.dot_general(
        d_projected, w_qkv, (((0,), (1,)), ((), ())), preferred_element_type=f32
    )
    d_norm_one, attn_gain_term = norm_back(d_normed, inputs, scale_one, gain_attn)
    d_inputs = d_h_one + d_norm_one
    shard_qkv, shard_out, shard_attn_gain, shard_ffn_gain, shard_query_gain, shard_key_gain = (
        lax.psum_scatter(
            grad_qkv_here.astype(jnp.bfloat16), "fsdp", scatter_dimension=0, tiled=True
        ).astype(jnp.float32),
        lax.psum_scatter(
            grad_out_here.astype(jnp.bfloat16), "fsdp", scatter_dimension=0, tiled=True
        ).astype(jnp.float32),
        lax.psum_scatter(
            jnp.sum(attn_gain_term, axis=0).astype(jnp.bfloat16),
            "fsdp",
            scatter_dimension=0,
            tiled=True,
        ).astype(jnp.float32),
        lax.psum_scatter(
            jnp.sum(ffn_gain_term, axis=0).astype(jnp.bfloat16),
            "fsdp",
            scatter_dimension=0,
            tiled=True,
        ).astype(jnp.float32),
        lax.psum_scatter(
            jnp.sum(query_term, axis=(0, 2)).astype(jnp.bfloat16),
            "fsdp",
            scatter_dimension=0,
            tiled=True,
        ).astype(jnp.float32),
        lax.psum_scatter(
            jnp.sum(key_term, axis=(0, 2)).astype(jnp.bfloat16),
            "fsdp",
            scatter_dimension=0,
            tiled=True,
        ).astype(jnp.float32),
    )
    summed_grads = (
        lax.psum(shard_qkv.astype(jnp.bfloat16), "ctx").astype(jnp.float32),
        lax.psum(shard_out.astype(jnp.bfloat16), "ctx").astype(jnp.float32),
        lax.psum(grad_gate_up, "ctx").astype(jnp.float32),
        lax.psum(grad_down, "ctx").astype(jnp.float32),
        lax.psum(shard_attn_gain.astype(jnp.bfloat16), "ctx").astype(jnp.float32),
        lax.psum(shard_ffn_gain.astype(jnp.bfloat16), "ctx").astype(jnp.float32),
        lax.psum(shard_query_gain.astype(jnp.bfloat16), "ctx").astype(jnp.float32),
        lax.psum(shard_key_gain.astype(jnp.bfloat16), "ctx").astype(jnp.float32),
    )
    return (
        output[None],
        d_inputs[None],
        summed_grads[0],
        summed_grads[1],
        summed_grads[2],
        summed_grads[3],
        summed_grads[4],
        summed_grads[5],
        summed_grads[6],
        summed_grads[7],
    )


def solution(mesh):
    block = mesh.shape["fsdp"] == 2 and mesh.shape["ctx"] == 16
    return jax.shard_map(
        on_block if block else on_device,
        mesh=mesh,
        in_specs=(
            P("fsdp", "ctx", None),
            P("fsdp", None),
            P("fsdp", None),
            P("fsdp", None, None),
            P("fsdp", None),
            P("fsdp"),
            P("fsdp"),
            P("fsdp"),
            P("fsdp"),
            P("fsdp", None),
            P("fsdp", None),
            P("fsdp", "ctx", None),
        ),
        out_specs=(
            P("fsdp", "ctx", None),
            P("fsdp", "ctx", None),
            P("fsdp", None),
            P("fsdp", None),
            P("fsdp", None, None),
            P("fsdp", None),
            P("fsdp"),
            P("fsdp"),
            P("fsdp"),
            P("fsdp"),
        ),
        check_vma=False,
    )
```

```python
import functools

import jax
import jax.numpy as jnp
from jax import lax
from jax.experimental import pallas as pl
from jax.experimental.pallas import tpu as pltpu
from jax.sharding import PartitionSpec as P

HEADS = 16
KV_HEADS = 8
HD = 64
BLK = 128
TILE = 256
CHUNKS = 2
PROJECT = 0
ATTEND = 22
OUT = 0
FFN = (15, 18)
ATTEND_BACK = 25


EPSILON = 1e-05
ROPE_BASE = 1000000.0
LOG2E = 1.4426950408889634
SCORE_SCALE = LOG2E * HD ** (-0.5)


def rms_scale(values, axis=-1):
    return lax.rsqrt(jnp.mean(values * values, axis=axis, keepdims=True) + EPSILON)


def norm_back(grad_normed, inputs, scale, gain, axis=-1):
    scaled = grad_normed * gain
    grad_in = scale * scaled - inputs * scale * scale * scale * jnp.mean(
        scaled * inputs, axis=axis, keepdims=True
    )
    return (grad_in, grad_normed * inputs * scale)


def rope(values, cosine, sine):
    half = HD // 2
    first, second = values[:, :half], values[:, half:]
    return jnp.concatenate([first * cosine - second * sine, second * cosine + first * sine], axis=1)


def rope_back(values, cosine, sine):
    half = HD // 2
    first, second = values[:, :half], values[:, half:]
    return jnp.concatenate([first * cosine + second * sine, second * cosine - first * sine], axis=1)


def starts_of(packed, lengths_row):
    ends = jnp.cumsum(lengths_row)
    past = packed[:, None] >= ends[None, :]
    return jnp.sum(jnp.where(past, lengths_row[None, :], 0), axis=1)


def block_tables(order, lengths_row):
    count = order.shape[0]
    rank = jnp.sum((order[None, :] < order[:, None]).astype(jnp.int32), axis=1)
    hit = rank[None, :] == jnp.arange(count, dtype=jnp.int32)[:, None]
    slot = jnp.sum(jnp.where(hit, jnp.arange(count, dtype=jnp.int32)[None, :], 0), axis=1)
    block = jnp.sum(jnp.where(hit, order[None, :], 0), axis=1)
    place = (block[:, None] * BLK + jnp.arange(BLK, dtype=jnp.int32)[None, :]).reshape(-1)
    return (slot, place, starts_of(place, lengths_row))


def attend_kernel(
    q_slot, kv_slot, first, last, qkv_ref, place_ref, start_ref,
    out_ref, q_ref, qt_ref, k_ref, kt_ref, v_ref, ot_ref, total_ref, vt_ref
):
    per_device = qkv_ref.shape[2] // BLK
    kv_blocks = k_ref.shape[0] // BLK
    q_blocks = q_ref.shape[0] // BLK

    def piece(slot, lower):
        return qkv_ref[
            slot // per_device,
            lower : lower + HD,
            pl.ds(pl.multiple_of((slot % per_device) * BLK, BLK), BLK),
        ]

    for i in range(kv_blocks):
        here = slice(i * BLK, (i + 1) * BLK)
        keys = piece(kv_slot[i], HD)
        kt_ref[:, here] = keys
        k_ref[here, :] = keys.T
        values = piece(kv_slot[i], 2 * HD)
        vt_ref[:, here] = values
        v_ref[here, :] = values.T
    for i in range(q_blocks):
        here = slice(i * BLK, (i + 1) * BLK)
        queries = piece(q_slot[i], 0)
        qt_ref[:, here] = queries
        q_ref[here, :] = queries.T
    if q_blocks < kv_blocks:
        out_ref[...] = jnp.zeros_like(out_ref)

    def tile(i, carry):
        rows = pl.ds(pl.multiple_of(i * TILE, TILE), TILE)
        queries = qt_ref[:, rows]
        place = place_ref[:, rows]
        start = start_ref[:, rows]

        def step(j, state):
            total, summed = state
            at = pl.multiple_of(j * TILE, TILE)
            scores = jnp.dot(
                k_ref[pl.ds(at, TILE), :], queries, preferred_element_type=jnp.float32
            )
            key_place = lax.broadcasted_iota(jnp.int32, (TILE, TILE), 0) + at
            allowed = (key_place <= place) & (key_place >= start)
            lifted = jnp.where(allowed, jnp.exp2(scores * SCORE_SCALE), 0.0)
            total = total + jnp.sum(lifted, axis=0, keepdims=True)
            summed = summed + jnp.dot(
                vt_ref[:, pl.ds(at, TILE)],
                lifted.astype(jnp.bfloat16),
                preferred_element_type=jnp.float32,
            )
            return (total, summed)

        total, summed = lax.fori_loop(
            first[i],
            last[i],
            step,
            (jnp.zeros((1, TILE), jnp.float32), jnp.zeros((HD, TILE), jnp.float32)),
        )
        attn = summed / total
        ot_ref[:, rows] = attn
        total_ref[:, rows] = jnp.log(total) * LOG2E
        rounded = attn.astype(jnp.bfloat16)
        for part in range(TILE // BLK):
            slot = q_slot[i * (TILE // BLK) + part]
            out_ref[
                slot // per_device,
                :,
                pl.ds(pl.multiple_of((slot % per_device) * BLK, BLK), BLK),
            ] = rounded[:, part * BLK : (part + 1) * BLK]
        return carry

    lax.fori_loop(0, q_blocks * BLK // TILE, tile, 0)


def attend_back_kernel(
    q_slot, kv_slot, first, last, d_ref, place_ref, start_ref,
    q_ref, qt_ref, k_ref, kt_ref, v_ref, ot_ref, total_ref,
    out_ref, dt_ref, do_ref, dk_ref, dv_ref
):
    per_device = d_ref.shape[2] // BLK
    kv_blocks = k_ref.shape[0] // BLK
    q_blocks = q_ref.shape[0] // BLK

    def lanes(slot):
        return pl.ds(pl.multiple_of((slot % per_device) * BLK, BLK), BLK)

    for i in range(q_blocks):
        here = slice(i * BLK, (i + 1) * BLK)
        slot = q_slot[i]
        grads = d_ref[slot // per_device, :, lanes(slot)]
        dt_ref[:, here] = grads
        do_ref[here, :] = grads.T
    dk_ref[...] = jnp.zeros_like(dk_ref)
    dv_ref[...] = jnp.zeros_like(dv_ref)
    if q_blocks < kv_blocks:
        out_ref[...] = jnp.zeros_like(out_ref)

    def tile(i, carry):
        rows = pl.ds(pl.multiple_of(i * TILE, TILE), TILE)
        queries = qt_ref[:, rows]
        grads = dt_ref[:, rows]
        place = place_ref[:, rows]
        start = start_ref[:, rows]
        delta = jnp.sum(grads.astype(jnp.float32) * ot_ref[:, rows], axis=0, keepdims=True)
        total = total_ref[:, rows]

        def step(j, d_query):
            at = pl.multiple_of(j * TILE, TILE)
            here = pl.ds(at, TILE)
            scores = jnp.dot(k_ref[here, :], queries, preferred_element_type=jnp.float32)
            key_place = lax.broadcasted_iota(jnp.int32, (TILE, TILE), 0) + at
            allowed = (key_place <= place) & (key_place >= start)
            shares = jnp.where(allowed, jnp.exp2(scores * SCORE_SCALE - total), 0.0)
            d_shares = jnp.dot(v_ref[here, :], grads, preferred_element_type=jnp.float32)
            d_scores = (shares * (d_shares - delta)).astype(jnp.bfloat16)
            dv_ref[here, :] += jnp.dot(
                shares.astype(jnp.bfloat16), do_ref[rows, :], preferred_element_type=jnp.float32
            )
            dk_ref[here, :] += jnp.dot(
                d_scores, q_ref[rows, :], preferred_element_type=jnp.float32
            )
            return d_query + jnp.dot(
                kt_ref[:, here], d_scores, preferred_element_type=jnp.float32
            )

        d_query = lax.fori_loop(first[i], last[i], step, jnp.zeros((HD, TILE), jnp.float32))
        rounded = (d_query * HD ** (-0.5)).astype(jnp.bfloat16)
        for part in range(TILE // BLK):
            slot = q_slot[i * (TILE // BLK) + part]
            out_ref[slot // per_device, 0:HD, lanes(slot)] = rounded[
                :, part * BLK : (part + 1) * BLK
            ]
        return carry

    lax.fori_loop(0, q_blocks * BLK // TILE, tile, 0)
    for i in range(kv_blocks):
        here = slice(i * BLK, (i + 1) * BLK)
        slot = kv_slot[i]
        out_ref[slot // per_device, HD : 2 * HD, lanes(slot)] = (
            (dk_ref[here, :] * HD ** (-0.5)).T.astype(jnp.bfloat16)
        )
        out_ref[slot // per_device, 2 * HD : 3 * HD, lanes(slot)] = (
            dv_ref[here, :].T.astype(jnp.bfloat16)
        )


def cost(micros):
    return pl.CostEstimate(
        flops=1 + micros * 1_000_000_000, bytes_accessed=1, transcendentals=0
    )


def kernel_call(kernel, tables, arrays, outs, scratch, micros):
    smem = pl.BlockSpec(memory_space=pltpu.SMEM)
    vmem = pl.BlockSpec(memory_space=pltpu.VMEM)
    return pl.pallas_call(
        kernel,
        out_shape=outs,
        in_specs=[smem] * len(tables) + [vmem] * len(arrays),
        out_specs=[vmem] * len(outs),
        scratch_shapes=scratch,
        compiler_params=pltpu.CompilerParams(vmem_limit_bytes=48 * 1024 * 1024),
        cost_estimate=cost(micros),
    )(*tables, *arrays)


class Links:
    def __init__(self, ctx_size):
        self.depth = ctx_size // 4
        index = lax.axis_index("ctx")
        self.core = index % 2
        self.y = (index // 2) % 2
        self.side = lax.axis_index("fsdp")
        self.half = ((index // 4 + 1) // 2) % 2
        self.quarter = index % 2 * 2 + self.y
        self.here = jnp.stack([self.half, self.core, self.y, self.side]).astype(jnp.int32)

    def route(self, place):
        pairs = []
        for z in range(self.depth):
            for y in range(2):
                for core in range(2):
                    to_z, to_y, to_core = place(z, y, core)
                    pairs.append(((z * 2 + y) * 2 + core, (to_z * 2 + to_y) * 2 + to_core))
        return pairs

    def over_core(self, value):
        return lax.ppermute(value, "ctx", self.route(lambda z, y, c: (z, y, 1 - c)))

    def over_y(self, value):
        return lax.ppermute(value, "ctx", self.route(lambda z, y, c: (z, 1 - y, c)))

    def over_z(self, value):
        return lax.ppermute(value, "ctx", self.route(lambda z, y, c: (z ^ 1, y, c)))

    def mirror_z(self, value):
        return lax.ppermute(value, "ctx", self.route(lambda z, y, c: (self.depth - 1 - z, y, c)))

    def over_x(self, value):
        return lax.ppermute(value, "fsdp", [(0, 1), (1, 0)])

    def to_side(self, value, side):
        return lax.ppermute(value, "fsdp", [(1 - side, side)])

    def spread_plane(self, value):
        across = self.over_core(value)
        beside = self.over_y(value)
        return (value, across, beside, self.over_core(beside))

    def deal_plane(self, near, far, give, give_far):
        got, got_far = self.over_core(give), self.over_core(give_far)
        return (near, got, self.over_y(far), self.over_y(got_far))

    def sum_depth(self, kept, got, time=None):
        def half(index):
            return add(pick(kept, index, 0), pick(got, index, 0))

        given = self.over_z(half(1 - self.half))
        part = add(half(self.half), given)
        other = self.mirror_z(part)
        full = add(part, other if time is None else after(other, time))
        return jnp.stack([full, self.over_z(full)])


def pick(value, index, axis):
    return lax.dynamic_index_in_dim(value, index, axis, keepdims=False)


def add(left, right):
    return (left.astype(jnp.float32) + right.astype(jnp.float32)).astype(jnp.bfloat16)


def after(value, *others):
    return lax.optimization_barrier((value, *others))[0]


def contract(left, right, axes):
    return lax.dot_general(
        left, right, ((axes[:1], axes[1:]), ((), ())), preferred_element_type=jnp.float32
    )


PARAMS = pltpu.CompilerParams(vmem_limit_bytes=56 * 1024 * 1024)


def call_with_here(
    kernel, here, grid, arrays, specs, outs, out_specs, scratch=(), aliases=None, micros=5
):
    return pl.pallas_call(
        kernel,
        grid_spec=pltpu.PrefetchScalarGridSpec(
            num_scalar_prefetch=1,
            grid=grid,
            in_specs=specs,
            out_specs=out_specs,
            scratch_shapes=list(scratch),
        ),
        out_shape=outs,
        input_output_aliases=aliases or {},
        compiler_params=PARAMS,
        cost_estimate=cost(micros),
    )(here, *arrays)


def whole(array):
    rank = len(array.shape)
    return pl.BlockSpec(array.shape, lambda i, here: (0,) * rank)


def project_kernel(here, *refs):
    x_ref, gain_ref, own_ref = refs[:3]
    pieces, q_gain, k_gain, cos_ref, sin_ref = refs[3:7], refs[7], refs[8], refs[9], refs[10]
    sent, weight, q_ref, k_ref, q_scale, k_scale, normed_ref, scale_ref = refs[11:]
    core, y, side = here[1], here[2], here[3]
    rows = own_ref.shape[0]
    part = rows // 4
    f32, bf16 = jnp.float32, jnp.bfloat16
    weight[pl.ds(pl.multiple_of(side * rows, rows), rows), :] = own_ref[...]
    for p in range(4):
        at = (1 - side) * rows + (((p % 2) ^ core) * 2 + ((p // 2) ^ y)) * part
        weight[pl.ds(pl.multiple_of(at, part), part), :] = pieces[p][...]
    x = x_ref[...].astype(f32)
    scale = rms_scale(x)
    scale_ref[...] = scale
    normed = (x * scale * gain_ref[...]).astype(bf16)
    normed_ref[...] = normed.T
    cosine, sine = cos_ref[...], sin_ref[...]
    half = HD // 2

    def turned(raw, gain, raw_ref, kept_scale, head):
        raw_ref[head * HD : (head + 1) * HD, :] = raw
        scale = rms_scale(raw, 0)
        kept_scale[head : head + 1, :] = scale
        value = raw * scale * gain
        first, second = value[:half], value[half:]
        return jnp.concatenate(
            [first * cosine - second * sine, second * cosine + first * sine], axis=0
        ).astype(bf16)

    per_group = HEADS // KV_HEADS
    for at in range(0, weight.shape[1], 2 * BLK):
        block = jnp.dot(normed, weight[:, at : at + 2 * BLK], preferred_element_type=f32)
        turned_block = block.T
        for n in range(2 * BLK // HD):
            head = at // HD + n
            raw = turned_block[n * HD : (n + 1) * HD, :]
            if head < HEADS:
                sent[head, 0:HD, :] = turned(raw, q_gain[...], q_ref, q_scale, head)
                continue
            head -= HEADS
            if head < KV_HEADS:
                value, row = turned(raw, k_gain[...], k_ref, k_scale, head), HD
            else:
                value, row, head = raw.astype(bf16), 2 * HD, head - KV_HEADS
            for copy in range(per_group):
                sent[head * per_group + copy, row : row + HD, :] = value


def project(here, x, gain, own, pieces, q_gain, k_gain, cosine, sine):
    tokens, width = x.shape
    f32, bf16 = jnp.float32, jnp.bfloat16
    shape = jax.ShapeDtypeStruct
    arrays = [x, gain, own, *pieces, q_gain, k_gain, cosine, sine]
    outs = [
        shape((HEADS, 3 * HD, tokens), bf16),
        shape((width, own.shape[1]), bf16),
        shape((HEADS * HD, tokens), f32),
        shape((KV_HEADS * HD, tokens), f32),
        shape((HEADS, tokens), f32),
        shape((KV_HEADS, tokens), f32),
        shape((width, tokens), bf16),
        shape((tokens, 1), f32),
    ]
    return call_with_here(
        project_kernel, here, (1,), arrays, [whole(a) for a in arrays], outs,
        [whole(o) for o in outs], micros=PROJECT,
    )


def layer(array, index):
    return pl.BlockSpec((1, *array.shape[1:]), lambda i, here: (index, 0, 0))


def attend_out_kernel(here, *refs):
    attn_ref, x_ref, gain_ref, own_ref = refs[:4]
    pieces = refs[4:20]
    weight, h_ref, scale_ref, two_ref, two_t_ref = refs[20:]
    core, y, side = here[1], here[2], here[3]
    rows = own_ref.shape[0]
    part = rows // 4
    weight[pl.ds(pl.multiple_of(side * rows, rows), rows), :] = own_ref[...]
    for p in range(4):
        at = (1 - side) * rows + (((p % 2) ^ core) * 2 + ((p // 2) ^ y)) * part
        for n in range(4):
            piece = pieces[4 * p + n]
            wide = piece.shape[1]
            weight[pl.ds(pl.multiple_of(at, part), part), n * wide : (n + 1) * wide] = piece[...]
    attn = attn_ref[...].T
    h_one = x_ref[...].astype(jnp.float32) + jnp.dot(
        attn, weight[...], preferred_element_type=jnp.float32
    )
    scale = rms_scale(h_one)
    h_ref[...] = h_one
    scale_ref[...] = scale
    two = (h_one * scale * gain_ref[...]).astype(jnp.bfloat16)
    two_ref[...] = two
    two_t_ref[...] = two.T


def attend_out(here, attn, x, gain, own, pieces):
    tokens, width = x.shape
    f32, bf16 = jnp.float32, jnp.bfloat16
    shape = jax.ShapeDtypeStruct
    part = own.shape[0] // 4
    cuts = 4
    part_width = width // cuts
    first = pieces[0].shape[1] // part_width - cuts
    arrays = [attn, x, gain, own]
    specs = [whole(a) for a in arrays]
    for piece in pieces:
        for n in range(cuts):
            arrays.append(piece)
            specs.append(pl.BlockSpec((part, part_width), lambda i, here, n=n: (0, first + n)))
    outs = [
        shape((width, width), bf16),
        shape((tokens, width), f32),
        shape((tokens, 1), f32),
        shape((tokens, width), bf16),
        shape((width, tokens), bf16),
    ]
    return call_with_here(
        attend_out_kernel, here, (1,), arrays, specs, outs, [whole(o) for o in outs], micros=OUT
    )


def ffn_kernel(chunk, here, *refs):
    two_ref, d_ref, own_ref = refs[:3]
    pieces, down_ref, down_pieces = (refs[3:7], refs[7:11]), refs[11], refs[12:16]
    refs = refs[4:]
    if chunk == 0:
        before_refs, refs = refs[12:13], refs[13:]
        near, far, give, give_far, hidden_ref, out_ref, d_two_ref = refs[:7]
        refs = refs[7:]
    else:
        before_refs, gain_ref, refs = refs[12:17], refs[17], refs[18:]
        near, far, give, give_far, hidden_ref = refs[:5]
        out_ref, d_h_ref, d_attn_ref, heads_ref, gain_term_ref = refs[5:10]
        refs = refs[10:]
    weight, down, hidden_rows, out_sum, two_sum = refs[:5]
    held, weight_sem, down_sem, before_sem = refs[5:-3], refs[-3], refs[-2], refs[-1]
    core, y, side = here[1], here[2], here[3]
    f32, bf16 = jnp.float32, jnp.bfloat16
    own_rows, columns = own_ref.shape[1], own_ref.shape[2] // CHUNKS
    part = own_rows // 4
    tile = columns // FFN_TILES
    half = columns // 2

    def quarter(p):
        return ((p % 2) ^ core) * 2 + ((p // 2) ^ y)

    def copies(n):
        at = slice(n * tile, (n + 1) * tile)
        mine = pl.ds(pl.multiple_of(side * own_rows, own_rows), own_rows)
        found = [
            pltpu.make_async_copy(
                own_ref.at[:, :, chunk * columns + n * tile : chunk * columns + (n + 1) * tile],
                weight.at[:, mine, at],
                weight_sem.at[n, 0],
            )
        ]
        for p in range(4):
            rows = pl.ds(pl.multiple_of((1 - side) * own_rows + quarter(p) * part, part), part)
            for kind in range(2):
                begin = n * tile + (columns if kind == 1 and chunk == 1 else 0)
                found.append(
                    pltpu.make_async_copy(
                        pieces[kind][p].at[:, begin : begin + tile],
                        weight.at[kind, rows, at],
                        weight_sem.at[n, 1 + 2 * p + kind],
                    )
                )
        return found

    def own_down(n):
        at = slice(n * tile, (n + 1) * tile)
        return [pltpu.make_async_copy(down_ref.at[at, :], down.at[at, :], down_sem.at[n, 0])]

    def other_down(n):
        at = slice(n * tile, (n + 1) * tile)
        found = []
        for p in range(4):
            wide = down_pieces[p].shape[1]
            lanes = pl.ds(pl.multiple_of(quarter(p) * wide, wide), wide)
            found.append(
                pltpu.make_async_copy(
                    down_pieces[p].at[at, :], down.at[at, lanes], down_sem.at[n, p]
                )
            )
        return found

    def each(action, n):
        for copy in copies(n):
            action(copy)

        @pl.when(side == chunk)
        def _():
            for copy in own_down(n):
                action(copy)

        @pl.when(side != chunk)
        def _():
            for copy in other_down(n):
                action(copy)

    before = [
        pltpu.make_async_copy(ref, held[n], before_sem.at[n]) for n, ref in enumerate(before_refs)
    ]
    for n in range(FFN_TILES):
        each(lambda copy: copy.start(), n)
    for copy in before:
        copy.start()
    two = two_ref[...]
    d_ffn = d_ref[...]
    for n in range(FFN_TILES):
        each(lambda copy: copy.wait(), n)
        at = slice(n * tile, (n + 1) * tile)
        gate = jnp.dot(two, weight[0, :, at], preferred_element_type=f32)
        upper = jnp.dot(two, weight[1, :, at], preferred_element_type=f32)
        d_hidden = contract(d_ffn, down[at, :], (1, 1))
        sigma = jax.nn.sigmoid(gate)
        silu = gate * sigma
        hidden = (silu * upper).astype(bf16)
        d_gate = (d_hidden * upper * sigma * (1.0 + gate * (1.0 - sigma))).astype(bf16)
        d_upper = (d_hidden * silu).astype(bf16)
        out_term = jnp.dot(hidden, down[at, :], preferred_element_type=f32)
        two_term = contract(d_gate, weight[0, :, at], (1, 1)) + contract(
            d_upper, weight[1, :, at], (1, 1)
        )
        out_sum[...] = out_term if n == 0 else out_sum[...] + out_term
        two_sum[...] = two_term if n == 0 else two_sum[...] + two_term
        hidden_rows[:, at] = hidden
        mine = jnp.where(core == 0, d_gate, d_upper)
        other = jnp.where(core == 0, d_upper, d_gate)
        for column in range(2):
            begin, end = max(n * tile, column * half), min((n + 1) * tile, (column + 1) * half)
            if begin >= end:
                continue
            source = slice(begin - n * tile, end - n * tile)
            target = slice(begin - column * half, end - column * half)
            first, second = mine[:, source], other[:, source]

            @pl.when(y == column)
            def _(first=first, second=second, target=target):
                near[:, target] = first
                give[:, target] = second

            @pl.when(y != column)
            def _(first=first, second=second, target=target):
                far[:, target] = first
                give_far[:, target] = second

    lower, upper = hidden_rows[:, :half], hidden_rows[:, half:]
    hidden_ref[0] = jnp.where(core == 0, lower, upper)
    hidden_ref[1] = jnp.where(core == 0, upper, lower)
    for copy in before:
        copy.wait()
    if chunk == 0:
        out_ref[...] = held[0][...] + out_sum[...]
        d_two_ref[...] = two_sum[...]
    else:
        out_before, two_before, h_one, scale, w_out = held
        out_ref[...] = (out_before[...] + out_sum[...]).astype(bf16)
        d_norm, gain_term = norm_back(
            two_before[...] + two_sum[...], h_one[...], scale[...], gain_ref[...]
        )
        gain_term_ref[...] = jnp.sum(gain_term, axis=0, keepdims=True)
        d_h_one = d_ffn.astype(f32) + d_norm
        d_h_ref[...] = d_h_one
        d_attn = d_h_one.astype(bf16)
        d_attn_ref[...] = d_attn
        heads_ref[...] = contract(w_out[...], d_attn, (1, 1)).astype(bf16)


FFN_TILES = 3


def ffn(here, chunk, two, d_ffn, own, pieces, down, down_pieces, before, gain=None):
    tokens, width = two.shape
    columns = own.shape[2] // CHUNKS
    shape = jax.ShapeDtypeStruct
    f32, bf16 = jnp.float32, jnp.bfloat16
    outs = [shape((tokens, columns // 2), bf16)] * 4 + [shape((2, tokens, columns // 2), bf16)]
    if chunk == 0:
        outs += [shape((tokens, width), f32)] * 2
    else:
        outs += [
            shape((tokens, width), bf16),
            shape((tokens, width), f32),
            shape((tokens, width), bf16),
            shape((width, tokens), bf16),
            shape((1, width), f32),
        ]
    far_away = pl.BlockSpec(memory_space=pl.ANY)
    arrays = [two, d_ffn, own, *pieces[0], *pieces[1], down, *down_pieces, *before]
    specs = [whole(two), whole(d_ffn)] + [far_away] * (len(arrays) - 2)
    if gain is not None:
        arrays.append(gain)
        specs.append(whole(gain))
    got = call_with_here(
        functools.partial(ffn_kernel, chunk),
        here,
        (1,),
        arrays,
        specs,
        outs,
        [whole(o) for o in outs],
        [
            pltpu.VMEM((2, width, columns), bf16),
            pltpu.VMEM((columns, width), bf16),
            pltpu.VMEM((tokens, columns), bf16),
            pltpu.VMEM((tokens, width), f32),
            pltpu.VMEM((tokens, width), f32),
        ]
        + [pltpu.VMEM(v.shape, v.dtype) for v in before]
        + [
            pltpu.SemaphoreType.DMA((FFN_TILES, 9)),
            pltpu.SemaphoreType.DMA((FFN_TILES, 4)),
            pltpu.SemaphoreType.DMA((len(before),)),
        ],
        micros=FFN[chunk],
    )
    return got[:4], got[4], got[5:]


def wide_product_kernel(here, *refs):
    planes, terms = refs[:4], refs[4:8]
    sent, kept, left, right = refs[8:]
    tokens = planes[0].shape[1]
    for i in range(4):
        left[:, i * tokens : (i + 1) * tokens] = planes[i][...]
        right[i * tokens : (i + 1) * tokens, :] = terms[i][...]
    side = here[3]
    _, step, _ = kept.shape
    for half in range(2):
        for owner, out_ref in ((1 - side, sent), (side, kept)):
            place = pl.multiple_of(owner * 2 * step + half * step, step)
            out_ref[half] = jnp.dot(
                left[pl.ds(place, step), :], right[...], preferred_element_type=jnp.float32
            ).astype(out_ref.dtype)


def wide_products(here, two_plane, shares, columns):
    rows, tokens = two_plane[0].shape
    outs = [
        jax.ShapeDtypeStruct((2, rows // 4, columns), jnp.bfloat16),
        jax.ShapeDtypeStruct((2, rows // 4, columns), jnp.float32),
    ]
    arrays = [*two_plane, *shares]
    return call_with_here(
        wide_product_kernel,
        here,
        (1,),
        arrays,
        [whole(a) for a in two_plane]
        + [pl.BlockSpec((tokens, columns), lambda i, here: (0, 0))] * 4,
        outs,
        [whole(o) for o in outs],
        [
            pltpu.VMEM((rows, 4 * tokens), jnp.bfloat16),
            pltpu.VMEM((4 * tokens, columns), jnp.bfloat16),
        ],
        micros=8,
    )


def down_product_kernel(here, *refs):
    planes, terms = refs[:4], (refs[4:8], refs[8:12])
    sent, kept, left, right = refs[12:]
    tokens = planes[0].shape[0]
    for i in range(4):
        right[i * tokens : (i + 1) * tokens, :] = planes[i][...]
    for chunk in range(2):

        @pl.when(here[3] == chunk)
        def _(chunk=chunk):
            for i in range(4):
                left[:, i * tokens : (i + 1) * tokens] = terms[chunk][i][0].T

    _, step, _ = kept.shape
    for half in range(2):
        for owner, out_ref in ((1 - here[2], sent), (here[2], kept)):
            place = pl.multiple_of(owner * 2 * step + half * step, step)
            out_ref[half] = jnp.dot(
                left[pl.ds(place, step), :], right[...], preferred_element_type=jnp.float32
            ).astype(out_ref.dtype)


def down_products(here, d_plane, first, second):
    tokens, columns = d_plane[0].shape
    rows = first[0].shape[2]
    outs = [
        jax.ShapeDtypeStruct((2, rows // 4, columns), jnp.bfloat16),
        jax.ShapeDtypeStruct((2, rows // 4, columns), jnp.float32),
    ]
    return call_with_here(
        down_product_kernel,
        here,
        (1,),
        [*d_plane, *first, *second],
        [whole(a) for a in d_plane] + [layer(a, i % 2) for i, a in enumerate((*first, *second))],
        outs,
        [whole(o) for o in outs],
        [
            pltpu.VMEM((rows, 4 * tokens), jnp.bfloat16),
            pltpu.VMEM((4 * tokens, columns), jnp.bfloat16),
        ],
        micros=8,
    )


GAIN_ROWS = 16


def attention_back_kernel(here, *refs):
    d_ref, q_ref, k_ref, q_scale, k_scale, q_gain, k_gain, cos_ref, sin_ref = refs[:9]
    weight, x_ref, scale_ref, gain_ref, d_h_ref, d_attn_ref = refs[9:15]
    near, far, give, give_far, d_x_ref, gains_ref = refs[15:21]
    turned, natural = refs[21:]
    f32, bf16 = jnp.float32, jnp.bfloat16
    core, y = here[1], here[2]
    cosine, sine = cos_ref[...], sin_ref[...]
    half = HD // 2
    per_group = HEADS // KV_HEADS
    tokens = x_ref.shape[0]

    def back(grad, raw, scale, gain):
        first, second = grad[:half], grad[half:]
        normed = jnp.concatenate(
            [first * cosine + second * sine, second * cosine - first * sine], axis=0
        )
        return norm_back(normed, raw, scale, gain, 0)

    q_term = jnp.zeros((HD, tokens), f32)
    k_term = jnp.zeros((HD, tokens), f32)
    for head in range(HEADS):
        at = slice(head * HD, (head + 1) * HD)
        grad, term = back(
            d_ref[head, :HD, :].astype(f32), q_ref[at, :], q_scale[head : head + 1, :], q_gain[...]
        )
        turned[at, :] = grad.astype(bf16)
        q_term = q_term + term
    for head in range(KV_HEADS):
        at = slice(head * HD, (head + 1) * HD)
        both = d_ref[head * per_group, HD:, :].astype(f32)
        for other in range(1, per_group):
            both = both + d_ref[head * per_group + other, HD:, :].astype(f32)
        grad, term = back(both[:HD], k_ref[at, :], k_scale[head : head + 1, :], k_gain[...])
        place = HEADS * HD + head * HD
        turned[place : place + HD, :] = grad.astype(bf16)
        k_term = k_term + term
        place += KV_HEADS * HD
        turned[place : place + HD, :] = both[HD:].astype(bf16)
    rows = turned.shape[0] // 4
    columns = d_attn_ref.shape[1] // 4
    shares = ((near, core, y), (far, core, 1 - y), (give, 1 - core, y), (give_far, 1 - core, 1 - y))
    for out_ref, to_core, to_y in shares:
        share = to_core * 2 + to_y
        out_ref[:rows, :] = turned[pl.ds(pl.multiple_of(share * rows, rows), rows), :]
        out_ref[rows:, :] = d_attn_ref[:, pl.ds(pl.multiple_of(share * columns, columns), columns)]
    for at in range(0, turned.shape[0], 256):
        natural[:, at : at + 256] = turned[at : at + 256, :].T
    d_normed = contract(natural[...], weight[...], (1, 1))
    x = x_ref[...].astype(f32)
    d_norm, gain_term = norm_back(d_normed, x, scale_ref[...], gain_ref[...])
    d_x_ref[...] = d_h_ref[...] + d_norm
    gains_ref[...] = jnp.zeros_like(gains_ref)
    gains_ref[0:1, :] = jnp.sum(gain_term, axis=0, keepdims=True)
    gains_ref[1:2, 0:HD] = jnp.sum(q_term.T, axis=0, keepdims=True)
    gains_ref[2:3, 0:HD] = jnp.sum(k_term.T, axis=0, keepdims=True)


def attention_back(here, arrays):
    f32, bf16 = jnp.float32, jnp.bfloat16
    shape = jax.ShapeDtypeStruct
    weight, x = arrays[9], arrays[10]
    tokens, width = x.shape
    rows = weight.shape[1] // 4 + tokens
    assert width // 4 == tokens
    outs = [
        *[shape((rows, tokens), bf16)] * 4,
        shape((tokens, width), f32),
        shape((8, width), f32),
    ]
    return call_with_here(
        attention_back_kernel, here, (1,), arrays, [whole(a) for a in arrays], outs,
        [whole(o) for o in outs],
        [pltpu.VMEM((weight.shape[1], tokens), bf16), pltpu.VMEM((tokens, weight.shape[1]), bf16)],
        micros=12,
    )


def attention_product_kernel(here, *refs):
    planes, terms, gains_ref, ffn_gain_ref = refs[:4], refs[4:8], refs[8], refs[9]
    sent, kept, left, right, left_out, right_out = refs[10:]
    tokens = planes[0].shape[2]
    cut = right.shape[1]
    for i in range(4):
        at = slice(i * tokens, (i + 1) * tokens)
        left[:, at] = planes[i][0]
        left_out[:, at] = planes[i][1]
        share = terms[i]
        right[at, :] = share[:cut].T
        right_out[at, :] = share[cut:]
    step = left.shape[0] // 4
    for owner, out_ref in ((1 - here[3], sent), (here[3], kept)):
        for half in range(2):
            at = pl.ds(pl.multiple_of(owner * 2 * step + half * step, step), step)
            out_ref[half, :step, :cut] = jnp.dot(
                left[at, :], right[...], preferred_element_type=jnp.float32
            ).astype(out_ref.dtype)
            out_ref[half, :step, cut:] = jnp.dot(
                left_out[at, :], right_out[...], preferred_element_type=jnp.float32
            ).astype(out_ref.dtype)
        rows = gains_ref.shape[1] // 2
        mine = pl.ds(pl.multiple_of(owner * rows, rows), rows)
        wide = out_ref.shape[2] - rows
        block = jnp.concatenate(
            [
                jnp.concatenate([gains_ref[0:1, mine], gains_ref[1:2, 0:wide]], axis=1),
                jnp.concatenate([ffn_gain_ref[:, mine], gains_ref[2:3, 0:wide]], axis=1),
                jnp.zeros((GAIN_ROWS - 2, out_ref.shape[2]), jnp.float32),
            ],
            axis=0,
        )
        out_ref[0, step:, :] = block.astype(out_ref.dtype)
        out_ref[1, step:, :] = jnp.zeros((GAIN_ROWS, out_ref.shape[2]), out_ref.dtype)


def attention_products(here, pair_plane, shares, gains, ffn_gain):
    _, width, tokens = pair_plane[0].shape
    cut = shares[0].shape[0] - tokens
    shape = (2, width // 4 + GAIN_ROWS, cut + tokens)
    outs = [jax.ShapeDtypeStruct(shape, jnp.bfloat16), jax.ShapeDtypeStruct(shape, jnp.float32)]
    return call_with_here(
        attention_product_kernel,
        here,
        (1,),
        [*pair_plane, *shares, gains, ffn_gain],
        [whole(a) for a in (*pair_plane, *shares, gains, ffn_gain)],
        outs,
        [whole(o) for o in outs],
        [
            pltpu.VMEM((width, 4 * tokens), jnp.bfloat16),
            pltpu.VMEM((4 * tokens, cut), jnp.bfloat16),
            pltpu.VMEM((width, 4 * tokens), jnp.bfloat16),
            pltpu.VMEM((4 * tokens, tokens), jnp.bfloat16),
        ],
        micros=8,
    )


def place_gate_up_kernel(here, *refs):
    mine, across, beside, diagonal, out_ref = *refs[:4], refs[-1]
    pieces = (mine, across, beside, diagonal)
    wide = mine.shape[2]
    for case in range(4):
        core, y = case // 2, case % 2

        @pl.when((here[1] == core) & (here[2] == y))
        def _(core=core, y=y):
            for kind in range(2):
                for column in range(2):
                    value = pieces[(y ^ column) * 2 + (core ^ kind)][0]
                    out_ref[:, kind, column * wide : (column + 1) * wide] = value.astype(
                        jnp.float32
                    )


def place_gate_up(here, chunk, pieces, before):
    _, rows, wide = pieces[0].shape
    step = 64
    blocks = rows // step

    def source(i, here):
        return ((i // blocks) ^ here[0], i % blocks, 0)

    arrays = list(pieces)
    specs = [pl.BlockSpec((1, step, wide), source)] * 4
    aliases = {}
    if before is not None:
        arrays.append(before)
        specs.append(pl.BlockSpec(memory_space=pl.ANY))
        aliases = {5: 0}
    (out,) = call_with_here(
        place_gate_up_kernel,
        here,
        (2 * blocks,),
        arrays,
        specs,
        [jax.ShapeDtypeStruct((2 * rows, 2, 2 * wide * CHUNKS), jnp.float32)],
        [pl.BlockSpec((step, 2, 2 * wide), lambda i, here: (i, 0, chunk))],
        aliases=aliases,
        micros=10,
    )
    return out


def place_down(here, pieces):
    _, rows, columns = pieces[0].shape

    def kernel(here, *refs):
        for s in range(8):

            @pl.when(pl.program_id(0) == s)
            def _(s=s):
                refs[4][...] = refs[s % 4][s // 4].astype(jnp.float32)

    def target(s, here):
        half = (s // 4) ^ here[0]
        y = ((s // 2) % 2) ^ here[2]
        core = (s % 2) ^ here[1]
        return ((core * 2 + y) * 2 + half, 0)

    (out,) = call_with_here(
        kernel,
        here,
        (8,),
        list(pieces),
        [whole(v) for v in pieces],
        [jax.ShapeDtypeStruct((rows * 8, columns), jnp.float32)],
        [pl.BlockSpec((rows, columns), target)],
    )
    return out


def place_attention(here, pieces, cut):
    _, rows, columns = pieces[0].shape
    rows -= GAIN_ROWS

    def kernel(here, *refs):
        qkv_ref, out_ref, gains_ref = refs[4:]
        for s in range(8):

            @pl.when(pl.program_id(0) == s)
            def _(s=s):
                value = refs[s % 4][s // 4]
                qkv_ref[...] = value[:rows, :cut].astype(jnp.float32)
                out_ref[...] = value[:rows, cut:].astype(jnp.float32)
                gains = value[rows:].astype(jnp.float32)
                gains_ref[...] = gains if s == 0 else gains_ref[...] + gains

    def target(s, here):
        half = (s // 4) ^ here[0]
        return (half, ((s % 2) ^ here[1]) * 2 + (((s // 2) % 2) ^ here[2]))

    shape = jax.ShapeDtypeStruct
    f32 = jnp.float32
    gain_shape = (GAIN_ROWS, columns)
    return call_with_here(
        kernel,
        here,
        (8,),
        list(pieces),
        [whole(v) for v in pieces],
        [
            shape((2 * rows, 4 * cut), f32),
            shape((2 * rows, 4 * (columns - cut)), f32),
            shape(gain_shape, f32),
        ],
        [
            pl.BlockSpec((rows, cut), target),
            pl.BlockSpec((rows, columns - cut), target),
            pl.BlockSpec(gain_shape, lambda s, here: (0, 0)),
        ],
    )


def on_block(
    tokens,
    qkv_weight,
    out_weight,
    gate_up_weight,
    down_weight,
    attn_gain,
    ffn_gain,
    query_gain,
    key_gain,
    seq_lengths,
    block_order,
    cotangent,
):
    inputs = tokens[0].astype(jnp.float32)
    rows_here = inputs.shape[0]
    ctx_size = lax.axis_size("ctx")
    ctx_index = lax.axis_index("ctx")
    per_group = HEADS // KV_HEADS
    q_width = HEADS * HD
    kv_width = KV_HEADS * HD
    order_row = block_order[0]
    lengths_row = seq_lengths[0]
    slots = jnp.arange(rows_here, dtype=jnp.int32) // BLK + ctx_index * (rows_here // BLK)
    table = slots[:, None] == jnp.arange(order_row.shape[0], dtype=jnp.int32)[None, :]
    packed = (
        jnp.sum(jnp.where(table, order_row[None, :], 0), axis=1) * BLK
        + jnp.arange(rows_here, dtype=jnp.int32) % BLK
    )
    local = packed - starts_of(packed, lengths_row)
    frequency = ROPE_BASE ** (-2.0 * jnp.arange(HD // 2, dtype=jnp.float32) / HD)
    angle = frequency[:, None] * local.astype(jnp.float32)[None, :]
    cosine = jnp.cos(angle)[None]
    sine = jnp.sin(angle)[None]
    bf16, f32 = jnp.bfloat16, jnp.float32
    parts = ctx_size // HEADS
    part = ctx_index // HEADS
    part_blocks = HEADS * rows_here // BLK
    q_order = lax.dynamic_slice_in_dim(order_row, part * part_blocks, part_blocks)
    q_slot, q_place, q_start = block_tables(q_order, lengths_row)
    q_slot = q_slot + part * part_blocks
    kv_slot, _, _ = block_tables(order_row, lengths_row)
    first = jnp.min(q_start.reshape(-1, TILE), axis=1) // TILE
    last = jnp.max(q_place.reshape(-1, TILE), axis=1) // TILE + 1
    tables = (q_slot, kv_slot, first, last)
    q_rows, kv_rows = part_blocks * BLK, order_row.shape[0] * BLK

    links = Links(ctx_size)
    here = links.here
    width = inputs.shape[1]
    rows = qkv_weight.shape[0]
    part_rows = rows // 4

    def quarter_rows(weight):
        return lax.dynamic_slice_in_dim(weight, links.quarter * part_rows, part_rows)

    qkv_piece = quarter_rows(qkv_weight)
    gains_here = jnp.concatenate([after(attn_gain, qkv_piece), ffn_gain, query_gain, key_gain])
    gains_there = links.over_x(gains_here)

    def gain_of(at, size):
        mine, other = gains_here[at : at + size], gains_there[at : at + size]
        return jnp.where(
            links.side == 0, jnp.concatenate([mine, other]), jnp.concatenate([other, mine])
        ).astype(f32)

    gain_attn = gain_of(0, rows)
    gain_ffn = gain_of(rows, rows)
    gain_query = gain_of(2 * rows, HD // 2)
    gain_key = gain_of(2 * rows + HD // 2, HD // 2)
    ff_chunk = gate_up_weight.shape[2] // CHUNKS

    def gate_up_piece(chunk):
        piece = lax.dynamic_slice(
            gate_up_weight,
            (links.quarter * part_rows, 0, chunk * ff_chunk),
            (part_rows, 2, ff_chunk),
        )
        return [piece[:, 0], piece[:, 1]]

    qkv_there = links.over_x(qkv_piece)
    first_gate, first_up = gate_up_piece(0)
    first_piece = jnp.concatenate([first_gate, quarter_rows(out_weight)], axis=1)
    second_gate, second_up = gate_up_piece(1)
    second_piece = jnp.concatenate([second_gate, second_up], axis=1)
    down_piece = lax.dynamic_slice_in_dim(
        down_weight, links.quarter * (width // 4), width // 4, 1
    )
    d_ffn = cotangent[0]
    tokens_here = tokens[0]
    qkv_there = after(qkv_there, first_piece)
    first_there = links.over_x(after(first_piece, qkv_piece))
    up_there = links.over_x(after(first_up, first_there))
    qkv_pieces = links.spread_plane(qkv_there)
    sent, w_qkv, q_raw, k_raw, q_scale, k_scale, normed, scale_one = project(
        here, after(tokens_here, first_there, first_up), gain_attn[None], qkv_weight, qkv_pieces,
        gain_query[:, None], gain_key[:, None], cosine[0], sine[0],
    )
    got = lax.all_to_all(sent, "ctx", 0, 0, tiled=True)
    gate_up = jnp.transpose(after(gate_up_weight, sent), (1, 0, 2))
    up_there = after(up_there, sent)
    down_there = links.over_x(after(down_piece, up_there))
    first_beside = links.over_y(first_there)
    up_beside = links.over_y(up_there)
    second_there = links.over_x(after(second_piece, down_there))
    down_beside = links.over_y(down_there)
    got = after(got, down_there, gate_up)
    q_place, q_start = q_place[None], q_start[None]
    shape = jax.ShapeDtypeStruct
    attn_sent, *held = kernel_call(
        attend_kernel,
        tables,
        (got, q_place, q_start),
        [
            shape((ctx_size, HD, rows_here), bf16),
            shape((q_rows, HD), bf16),
            shape((HD, q_rows), bf16),
            shape((kv_rows, HD), bf16),
            shape((HD, kv_rows), bf16),
            shape((kv_rows, HD), bf16),
            shape((HD, q_rows), f32),
            shape((1, q_rows), f32),
        ],
        [pltpu.VMEM((HD, kv_rows), bf16)],
        ATTEND,
    )
    attn_sent = after(attn_sent, up_beside)
    attn_in = lax.dynamic_slice_in_dim(
        lax.all_to_all(attn_sent, "ctx", 0, 0, tiled=True), part * HEADS, HEADS
    ).reshape(q_width, rows_here)
    second_there = after(second_there, attn_sent)

    def spread(there, beside, time):
        there, beside = after(there, time), after(beside, time)
        return (there, links.over_core(there), beside, links.over_core(beside))

    first_pieces = spread(first_there, first_beside, attn_sent)
    up_pieces = spread(up_there, up_beside, attn_in)
    down_pieces = spread(down_there, down_beside, attn_in)
    second_pieces = links.spread_plane(second_there)
    w_out, h_one, scale_two, two, two_t = attend_out(
        here, attn_in, tokens_here, gain_ffn[None], out_weight, first_pieces
    )
    two_beside = links.over_y(two_t)
    dealt_here, first_hidden, (out_sum, two_sum) = ffn(
        here, 0, two, d_ffn, gate_up, (first_pieces, up_pieces), down_weight, down_pieces, [h_one]
    )
    near, far, give, give_far = dealt_here
    got_far = links.over_core(give_far)
    first_shares = (near, links.over_core(give), links.over_y(far), links.over_y(got_far))
    out_sum = after(out_sum, got_far)
    dealt_here, second_hidden, (output, d_h_one, d_attn, d_heads, ffn_gain_term) = ffn(
        here, 1, two, d_ffn, gate_up, (second_pieces, second_pieces), down_weight, down_pieces,
        [out_sum, two_sum, h_one, scale_two, w_out], gain_ffn[None],
    )
    second_shares = links.deal_plane(*dealt_here)

    def plane(value, beside, time):
        value, beside = after(value, time), after(beside, time)
        return (value, links.over_core(value), beside, links.over_core(beside))

    columns = ff_chunk // 2
    d_there = links.over_x(after(d_ffn, attn_sent))
    first_hidden_there = links.to_side(first_hidden, 0)
    second_hidden_there = links.to_side(second_hidden, 1)
    d_heads = after(d_heads, two_beside, first_shares[2], first_hidden_there).reshape(HEADS, HD, rows_here)
    pair = jnp.stack([after(normed, d_heads), attn_in])
    d_got = lax.all_to_all(d_heads, "ctx", 0, 0, tiled=True)
    two_plane = plane(two_t, two_beside, d_got)
    first_products = wide_products(here, two_plane, first_shares, columns)
    d_got = after(d_got, first_products[0], pair, second_hidden_there, d_there)
    (d_sent,) = kernel_call(
        attend_back_kernel,
        tables,
        (d_got, q_place, q_start, *held),
        [shape((ctx_size, 3 * HD, rows_here), bf16)],
        [
            pltpu.VMEM((HD, q_rows), bf16),
            pltpu.VMEM((q_rows, HD), bf16),
            pltpu.VMEM((kv_rows, HD), f32),
            pltpu.VMEM((kv_rows, HD), f32),
        ],
        ATTEND_BACK,
    )
    first_got = links.over_x(first_products[0])
    d_sent = after(d_sent, first_got, *second_shares[2:])
    d_back = lax.all_to_all(d_sent, "ctx", 0, 0, tiled=True)
    second_products = wide_products(
        here, two_plane, [after(v, d_sent) for v in second_shares], columns
    )
    def hidden_plane(hidden, there):
        return (hidden, links.over_core(after(hidden, d_sent)), there, links.over_core(there))

    d_plane = (d_ffn, links.over_core(after(d_ffn, d_got)), d_there, links.over_core(d_there))
    down_terms = down_products(
        here, d_plane,
        hidden_plane(first_hidden, first_hidden_there),
        hidden_plane(second_hidden, second_hidden_there),
    )
    second_got = links.over_x(after(second_products[0], first_got))
    *d_shares, d_inputs, gain_sums = attention_back(
        here,
        [
            d_back, q_raw, k_raw, q_scale, k_scale, gain_query[:, None], gain_key[:, None],
            cosine[0], sine[0], w_qkv, tokens_here, scale_one, gain_attn[None], d_h_one, d_attn,
        ],
    )
    near, far, give, give_far = d_shares
    got, got_far = links.over_core(give), links.over_core(give_far)
    attention_shares = (near, got, links.over_y(far), links.over_y(got_far))
    second_got = after(second_got, got_far)
    down_got = after(links.over_y(down_terms[0]), got_far)
    pair_plane = plane(pair, links.over_y(after(pair, d_sent)), d_shares[0])
    first_pair = links.sum_depth(first_products[1], after(first_got, d_back), got_far)
    second_pair = links.sum_depth(second_products[1], second_got)
    down_pair = links.sum_depth(down_terms[1], down_got)
    first_placed = place_gate_up(here, 0, links.spread_plane(first_pair), None)
    second_spread = links.spread_plane(second_pair)
    down_spread = links.spread_plane(down_pair)
    attention_terms = attention_products(
        here, pair_plane, attention_shares, gain_sums, ffn_gain_term
    )
    cut = qkv_weight.shape[1] // 4
    attention_pair = links.sum_depth(attention_terms[1], links.over_x(attention_terms[0]))
    grad_gate_up = place_gate_up(here, 1, second_spread, first_placed)
    grad_down = place_down(here, down_spread)
    beside = after(links.over_y(attention_pair), first_placed, grad_down)
    attention_spread = (
        attention_pair, links.over_core(attention_pair), beside, links.over_core(beside)
    )
    grad_qkv, grad_out, gain_sums = place_attention(here, attention_spread, cut)
    at = links.side * (HD // 2)
    gain_grads = [
        gain_sums[0, :rows],
        gain_sums[1, :rows],
        lax.dynamic_slice_in_dim(gain_sums[0, rows : rows + HD], at, HD // 2),
        lax.dynamic_slice_in_dim(gain_sums[1, rows : rows + HD], at, HD // 2),
    ]
    return (
        output[None],
        d_inputs[None],
        grad_qkv,
        grad_out,
        grad_gate_up,
        grad_down,
        *gain_grads,
    )


def on_device(
    tokens,
    qkv_weight,
    out_weight,
    gate_up_weight,
    down_weight,
    attn_gain,
    ffn_gain,
    query_gain,
    key_gain,
    seq_lengths,
    block_order,
    cotangent,
):
    inputs = tokens[0].astype(jnp.float32)
    rows_here = inputs.shape[0]
    ctx_size = lax.axis_size("ctx")
    ctx_index = lax.axis_index("ctx")
    per_group = HEADS // KV_HEADS
    q_width = HEADS * HD
    kv_width = KV_HEADS * HD
    order_row = block_order[0]
    lengths_row = seq_lengths[0]
    slots = jnp.arange(rows_here, dtype=jnp.int32) // BLK + ctx_index * (rows_here // BLK)
    table = slots[:, None] == jnp.arange(order_row.shape[0], dtype=jnp.int32)[None, :]
    packed = (
        jnp.sum(jnp.where(table, order_row[None, :], 0), axis=1) * BLK
        + jnp.arange(rows_here, dtype=jnp.int32) % BLK
    )
    local = packed - starts_of(packed, lengths_row)
    frequency = ROPE_BASE ** (-2.0 * jnp.arange(HD // 2, dtype=jnp.float32) / HD)
    angle = frequency[:, None] * local.astype(jnp.float32)[None, :]
    cosine = jnp.cos(angle)[None]
    sine = jnp.sin(angle)[None]
    bf16, f32 = jnp.bfloat16, jnp.float32
    parts = ctx_size // HEADS
    part = ctx_index // HEADS
    part_blocks = HEADS * rows_here // BLK
    q_order = lax.dynamic_slice_in_dim(order_row, part * part_blocks, part_blocks)
    q_slot, q_place, q_start = block_tables(q_order, lengths_row)
    q_slot = q_slot + part * part_blocks
    kv_slot, _, _ = block_tables(order_row, lengths_row)
    first = jnp.min(q_start.reshape(-1, TILE), axis=1) // TILE
    last = jnp.max(q_place.reshape(-1, TILE), axis=1) // TILE + 1
    tables = (q_slot, kv_slot, first, last)
    q_rows, kv_rows = part_blocks * BLK, order_row.shape[0] * BLK

    def fetch_attention():
        return (
            lax.all_gather(qkv_weight, "fsdp", axis=0, tiled=True),
            lax.all_gather(out_weight, "fsdp", axis=0, tiled=True),
            lax.all_gather(attn_gain, "fsdp", axis=0, tiled=True),
            lax.all_gather(ffn_gain, "fsdp", axis=0, tiled=True),
            lax.all_gather(query_gain, "fsdp", axis=0, tiled=True),
            lax.all_gather(key_gain, "fsdp", axis=0, tiled=True),
        )

    w_qkv, w_out, gain_attn, gain_ffn, gain_query, gain_key = fetch_attention()
    gain_attn = gain_attn.astype(jnp.float32)
    gain_ffn = gain_ffn.astype(jnp.float32)
    gain_query = gain_query.astype(jnp.float32)
    gain_key = gain_key.astype(jnp.float32)
    scale_one = rms_scale(inputs)
    normed = (inputs * scale_one * gain_attn).astype(jnp.bfloat16)
    projected = lax.dot_general(
        w_qkv, normed, (((0,), (1,)), ((), ())), preferred_element_type=f32
    )
    q_raw = projected[:q_width].reshape(HEADS, HD, rows_here)
    k_raw = projected[q_width : q_width + kv_width].reshape(KV_HEADS, HD, rows_here)
    values_here = projected[q_width + kv_width :].reshape(KV_HEADS, HD, rows_here).astype(bf16)
    q_scale = rms_scale(q_raw, 1)
    k_scale = rms_scale(k_raw, 1)
    column_query, column_key = gain_query[:, None], gain_key[:, None]
    queries = rope(q_raw * q_scale * column_query, cosine, sine).astype(bf16)
    keys_here = rope(k_raw * k_scale * column_key, cosine, sine).astype(bf16)
    sent = jnp.concatenate(
        [queries, jnp.repeat(keys_here, per_group, 0), jnp.repeat(values_here, per_group, 0)], axis=1
    )
    sent = jnp.concatenate([sent] * parts, axis=0)
    got = lax.all_to_all(sent, "ctx", 0, 0, tiled=True)
    q_place, q_start = q_place[None], q_start[None]
    shape = jax.ShapeDtypeStruct
    attn_sent, *held = kernel_call(
        attend_kernel,
        tables,
        (got, q_place, q_start),
        [
            shape((ctx_size, HD, rows_here), bf16),
            shape((q_rows, HD), bf16),
            shape((HD, q_rows), bf16),
            shape((kv_rows, HD), bf16),
            shape((HD, kv_rows), bf16),
            shape((kv_rows, HD), bf16),
            shape((HD, q_rows), f32),
            shape((1, q_rows), f32),
        ],
        [pltpu.VMEM((HD, kv_rows), bf16)],
        ATTEND,
    )
    attn_in = lax.dynamic_slice_in_dim(
        lax.all_to_all(attn_sent, "ctx", 0, 0, tiled=True), part * HEADS, HEADS
    ).reshape(q_width, rows_here)
    h_one = inputs + lax.dot_general(
        attn_in, w_out, (((0,), (0,)), ((), ())), preferred_element_type=f32
    )
    scale_two = rms_scale(h_one)
    normed_two = (h_one * scale_two * gain_ffn).astype(jnp.bfloat16)
    columns = normed_two
    gate_up = jnp.einsum(
        "tr,rgf->tgf",
        columns,
        lax.all_gather(gate_up_weight, "fsdp", axis=0, tiled=True),
        preferred_element_type=jnp.float32,
    )
    gate = gate_up[:, 0]
    upper = gate_up[:, 1]
    sigma = jax.nn.sigmoid(gate)
    hidden = (gate * sigma * upper).astype(jnp.bfloat16)
    columns = hidden
    ffn_out = jnp.dot(
        columns,
        lax.all_gather(down_weight, "fsdp", axis=0, tiled=True),
        preferred_element_type=jnp.float32,
    )
    output = (h_one + ffn_out).astype(jnp.bfloat16)
    d_out = cotangent[0].astype(jnp.float32)
    d_ffn = d_out.astype(jnp.bfloat16)
    d_hidden = lax.dot_general(
        d_ffn,
        lax.all_gather(down_weight, "fsdp", axis=0, tiled=True),
        (((1,), (1,)), ((), ())),
        preferred_element_type=jnp.float32,
    )
    d_gate = d_hidden * upper * sigma * (1.0 + gate * (1.0 - sigma))
    d_upper = d_hidden * gate * sigma
    d_gate_up = jnp.stack([d_gate, d_upper], axis=1).astype(jnp.bfloat16)
    d_normed_two = jnp.einsum(
        "tgf,rgf->tr",
        d_gate_up,
        lax.all_gather(gate_up_weight, "fsdp", axis=0, tiled=True),
        preferred_element_type=jnp.float32,
    )
    columns = normed_two
    grad_gate_up = lax.psum_scatter(
        jnp.einsum("tr,tgf->rgf", columns, d_gate_up, preferred_element_type=jnp.float32).astype(
            jnp.bfloat16
        ),
        "fsdp",
        scatter_dimension=0,
        tiled=True,
    )
    columns = hidden
    grad_down = lax.psum_scatter(
        lax.dot_general(
            columns, d_ffn, (((0,), (0,)), ((), ())), preferred_element_type=jnp.float32
        ).astype(jnp.bfloat16),
        "fsdp",
        scatter_dimension=0,
        tiled=True,
    )
    d_norm_two, ffn_gain_term = norm_back(d_normed_two, h_one, scale_two, gain_ffn)
    d_h_one = d_out + d_norm_two
    d_attn = d_h_one.astype(jnp.bfloat16)
    grad_out_here = jnp.dot(attn_in, d_attn, preferred_element_type=f32)
    d_heads = lax.dot_general(
        w_out, d_attn, (((1,), (1,)), ((), ())), preferred_element_type=f32
    ).astype(bf16)
    d_heads = jnp.concatenate([d_heads.reshape(HEADS, HD, rows_here)] * parts, axis=0)
    d_got = lax.all_to_all(d_heads, "ctx", 0, 0, tiled=True)
    (d_sent,) = kernel_call(
        attend_back_kernel,
        tables,
        (d_got, q_place, q_start, *held),
        [shape((ctx_size, 3 * HD, rows_here), bf16)],
        [
            pltpu.VMEM((HD, q_rows), bf16),
            pltpu.VMEM((q_rows, HD), bf16),
            pltpu.VMEM((kv_rows, HD), f32),
            pltpu.VMEM((kv_rows, HD), f32),
        ],
        ATTEND_BACK,
    )
    d_back = lax.all_to_all(d_sent, "ctx", 0, 0, tiled=True)
    d_query = lax.dynamic_slice_in_dim(d_back[:, :HD], part * HEADS, HEADS).astype(f32)
    d_key_value = jnp.sum(
        d_back[:, HD:].reshape(parts, KV_HEADS, per_group, 2 * HD, rows_here).astype(f32),
        axis=(0, 2),
    )
    dq_normed = rope_back(d_query, cosine, sine)
    dk_normed = rope_back(d_key_value[:, :HD], cosine, sine)
    dq_raw, query_term = norm_back(dq_normed, q_raw, q_scale, column_query, 1)
    dk_raw, key_term = norm_back(dk_normed, k_raw, k_scale, column_key, 1)
    d_projected = jnp.concatenate(
        [
            dq_raw.reshape(q_width, rows_here).astype(bf16),
            dk_raw.reshape(kv_width, rows_here).astype(bf16),
            d_key_value[:, HD:].reshape(kv_width, rows_here).astype(bf16),
        ],
        axis=0,
    )
    grad_qkv_here = lax.dot_general(
        normed, d_projected, (((0,), (1,)), ((), ())), preferred_element_type=f32
    )
    d_normed = lax.dot_general(
        d_projected, w_qkv, (((0,), (1,)), ((), ())), preferred_element_type=f32
    )
    d_norm_one, attn_gain_term = norm_back(d_normed, inputs, scale_one, gain_attn)
    d_inputs = d_h_one + d_norm_one
    shard_qkv, shard_out, shard_attn_gain, shard_ffn_gain, shard_query_gain, shard_key_gain = (
        lax.psum_scatter(
            grad_qkv_here.astype(jnp.bfloat16), "fsdp", scatter_dimension=0, tiled=True
        ).astype(jnp.float32),
        lax.psum_scatter(
            grad_out_here.astype(jnp.bfloat16), "fsdp", scatter_dimension=0, tiled=True
        ).astype(jnp.float32),
        lax.psum_scatter(
            jnp.sum(attn_gain_term, axis=0).astype(jnp.bfloat16),
            "fsdp",
            scatter_dimension=0,
            tiled=True,
        ).astype(jnp.float32),
        lax.psum_scatter(
            jnp.sum(ffn_gain_term, axis=0).astype(jnp.bfloat16),
            "fsdp",
            scatter_dimension=0,
            tiled=True,
        ).astype(jnp.float32),
        lax.psum_scatter(
            jnp.sum(query_term, axis=(0, 2)).astype(jnp.bfloat16),
            "fsdp",
            scatter_dimension=0,
            tiled=True,
        ).astype(jnp.float32),
        lax.psum_scatter(
            jnp.sum(key_term, axis=(0, 2)).astype(jnp.bfloat16),
            "fsdp",
            scatter_dimension=0,
            tiled=True,
        ).astype(jnp.float32),
    )
    summed_grads = (
        lax.psum(shard_qkv.astype(jnp.bfloat16), "ctx").astype(jnp.float32),
        lax.psum(shard_out.astype(jnp.bfloat16), "ctx").astype(jnp.float32),
        lax.psum(grad_gate_up, "ctx").astype(jnp.float32),
        lax.psum(grad_down, "ctx").astype(jnp.float32),
        lax.psum(shard_attn_gain.astype(jnp.bfloat16), "ctx").astype(jnp.float32),
        lax.psum(shard_ffn_gain.astype(jnp.bfloat16), "ctx").astype(jnp.float32),
        lax.psum(shard_query_gain.astype(jnp.bfloat16), "ctx").astype(jnp.float32),
        lax.psum(shard_key_gain.astype(jnp.bfloat16), "ctx").astype(jnp.float32),
    )
    return (
        output[None],
        d_inputs[None],
        summed_grads[0],
        summed_grads[1],
        summed_grads[2],
        summed_grads[3],
        summed_grads[4],
        summed_grads[5],
        summed_grads[6],
        summed_grads[7],
    )


def solution(mesh):
    block = mesh.shape["fsdp"] == 2 and mesh.shape["ctx"] == 16
    return jax.shard_map(
        on_block if block else on_device,
        mesh=mesh,
        in_specs=(
            P("fsdp", "ctx", None),
            P("fsdp", None),
            P("fsdp", None),
            P("fsdp", None, None),
            P("fsdp", None),
            P("fsdp"),
            P("fsdp"),
            P("fsdp"),
            P("fsdp"),
            P("fsdp", None),
            P("fsdp", None),
            P("fsdp", "ctx", None),
        ),
        out_specs=(
            P("fsdp", "ctx", None),
            P("fsdp", "ctx", None),
            P("fsdp", None),
            P("fsdp", None),
            P("fsdp", None, None),
            P("fsdp", None),
            P("fsdp"),
            P("fsdp"),
            P("fsdp"),
            P("fsdp"),
        ),
        check_vma=False,
    )
```

```python
import functools

import jax
import jax.numpy as jnp
from jax import lax
from jax.experimental import pallas as pl
from jax.experimental.pallas import tpu as pltpu
from jax.sharding import PartitionSpec as P

HEADS = 16
KV_HEADS = 8
HD = 64
BLK = 128
TILE = 256
CHUNKS = 2
PROJECT = 0
ATTEND = 22
OUT = 5
FFN = (15, 18)
ATTEND_BACK = 25


EPSILON = 1e-05
ROPE_BASE = 1000000.0
LOG2E = 1.4426950408889634
SCORE_SCALE = LOG2E * HD ** (-0.5)


def rms_scale(values, axis=-1):
    return lax.rsqrt(jnp.mean(values * values, axis=axis, keepdims=True) + EPSILON)


def norm_back(grad_normed, inputs, scale, gain, axis=-1):
    scaled = grad_normed * gain
    grad_in = scale * scaled - inputs * scale * scale * scale * jnp.mean(
        scaled * inputs, axis=axis, keepdims=True
    )
    return (grad_in, grad_normed * inputs * scale)


def rope(values, cosine, sine):
    half = HD // 2
    first, second = values[:, :half], values[:, half:]
    return jnp.concatenate([first * cosine - second * sine, second * cosine + first * sine], axis=1)


def rope_back(values, cosine, sine):
    half = HD // 2
    first, second = values[:, :half], values[:, half:]
    return jnp.concatenate([first * cosine + second * sine, second * cosine - first * sine], axis=1)


def starts_of(packed, lengths_row):
    ends = jnp.cumsum(lengths_row)
    past = packed[:, None] >= ends[None, :]
    return jnp.sum(jnp.where(past, lengths_row[None, :], 0), axis=1)


def block_tables(order, lengths_row):
    count = order.shape[0]
    rank = jnp.sum((order[None, :] < order[:, None]).astype(jnp.int32), axis=1)
    hit = rank[None, :] == jnp.arange(count, dtype=jnp.int32)[:, None]
    slot = jnp.sum(jnp.where(hit, jnp.arange(count, dtype=jnp.int32)[None, :], 0), axis=1)
    block = jnp.sum(jnp.where(hit, order[None, :], 0), axis=1)
    place = (block[:, None] * BLK + jnp.arange(BLK, dtype=jnp.int32)[None, :]).reshape(-1)
    return (slot, place, starts_of(place, lengths_row))


def attend_kernel(
    q_slot, kv_slot, first, last, qkv_ref, place_ref, start_ref,
    out_ref, q_ref, qt_ref, k_ref, kt_ref, v_ref, ot_ref, total_ref, vt_ref
):
    per_device = qkv_ref.shape[2] // BLK
    kv_blocks = k_ref.shape[0] // BLK
    q_blocks = q_ref.shape[0] // BLK

    def piece(slot, lower):
        return qkv_ref[
            slot // per_device,
            lower : lower + HD,
            pl.ds(pl.multiple_of((slot % per_device) * BLK, BLK), BLK),
        ]

    for i in range(kv_blocks):
        here = slice(i * BLK, (i + 1) * BLK)
        keys = piece(kv_slot[i], HD)
        kt_ref[:, here] = keys
        k_ref[here, :] = keys.T
        values = piece(kv_slot[i], 2 * HD)
        vt_ref[:, here] = values
        v_ref[here, :] = values.T
    for i in range(q_blocks):
        here = slice(i * BLK, (i + 1) * BLK)
        queries = piece(q_slot[i], 0)
        qt_ref[:, here] = queries
        q_ref[here, :] = queries.T
    if q_blocks < kv_blocks:
        out_ref[...] = jnp.zeros_like(out_ref)

    def tile(i, carry):
        rows = pl.ds(pl.multiple_of(i * TILE, TILE), TILE)
        queries = qt_ref[:, rows]
        place = place_ref[:, rows]
        start = start_ref[:, rows]

        def step(j, state):
            total, summed = state
            at = pl.multiple_of(j * TILE, TILE)
            scores = jnp.dot(
                k_ref[pl.ds(at, TILE), :], queries, preferred_element_type=jnp.float32
            )
            key_place = lax.broadcasted_iota(jnp.int32, (TILE, TILE), 0) + at
            allowed = (key_place <= place) & (key_place >= start)
            lifted = jnp.where(allowed, jnp.exp2(scores * SCORE_SCALE), 0.0)
            total = total + jnp.sum(lifted, axis=0, keepdims=True)
            summed = summed + jnp.dot(
                vt_ref[:, pl.ds(at, TILE)],
                lifted.astype(jnp.bfloat16),
                preferred_element_type=jnp.float32,
            )
            return (total, summed)

        total, summed = lax.fori_loop(
            first[i],
            last[i],
            step,
            (jnp.zeros((1, TILE), jnp.float32), jnp.zeros((HD, TILE), jnp.float32)),
        )
        attn = summed / total
        ot_ref[:, rows] = attn
        total_ref[:, rows] = jnp.log(total) * LOG2E
        rounded = attn.astype(jnp.bfloat16)
        for part in range(TILE // BLK):
            slot = q_slot[i * (TILE // BLK) + part]
            out_ref[
                slot // per_device,
                :,
                pl.ds(pl.multiple_of((slot % per_device) * BLK, BLK), BLK),
            ] = rounded[:, part * BLK : (part + 1) * BLK]
        return carry

    lax.fori_loop(0, q_blocks * BLK // TILE, tile, 0)


def attend_back_kernel(
    q_slot, kv_slot, first, last, d_ref, place_ref, start_ref,
    q_ref, qt_ref, k_ref, kt_ref, v_ref, ot_ref, total_ref,
    out_ref, dt_ref, do_ref, dk_ref, dv_ref
):
    per_device = d_ref.shape[2] // BLK
    kv_blocks = k_ref.shape[0] // BLK
    q_blocks = q_ref.shape[0] // BLK

    def lanes(slot):
        return pl.ds(pl.multiple_of((slot % per_device) * BLK, BLK), BLK)

    for i in range(q_blocks):
        here = slice(i * BLK, (i + 1) * BLK)
        slot = q_slot[i]
        grads = d_ref[slot // per_device, :, lanes(slot)]
        dt_ref[:, here] = grads
        do_ref[here, :] = grads.T
    dk_ref[...] = jnp.zeros_like(dk_ref)
    dv_ref[...] = jnp.zeros_like(dv_ref)
    if q_blocks < kv_blocks:
        out_ref[...] = jnp.zeros_like(out_ref)

    def tile(i, carry):
        rows = pl.ds(pl.multiple_of(i * TILE, TILE), TILE)
        queries = qt_ref[:, rows]
        grads = dt_ref[:, rows]
        place = place_ref[:, rows]
        start = start_ref[:, rows]
        delta = jnp.sum(grads.astype(jnp.float32) * ot_ref[:, rows], axis=0, keepdims=True)
        total = total_ref[:, rows]

        def step(j, d_query):
            at = pl.multiple_of(j * TILE, TILE)
            here = pl.ds(at, TILE)
            scores = jnp.dot(k_ref[here, :], queries, preferred_element_type=jnp.float32)
            key_place = lax.broadcasted_iota(jnp.int32, (TILE, TILE), 0) + at
            allowed = (key_place <= place) & (key_place >= start)
            shares = jnp.where(allowed, jnp.exp2(scores * SCORE_SCALE - total), 0.0)
            d_shares = jnp.dot(v_ref[here, :], grads, preferred_element_type=jnp.float32)
            d_scores = (shares * (d_shares - delta)).astype(jnp.bfloat16)
            dv_ref[here, :] += jnp.dot(
                shares.astype(jnp.bfloat16), do_ref[rows, :], preferred_element_type=jnp.float32
            )
            dk_ref[here, :] += jnp.dot(
                d_scores, q_ref[rows, :], preferred_element_type=jnp.float32
            )
            return d_query + jnp.dot(
                kt_ref[:, here], d_scores, preferred_element_type=jnp.float32
            )

        d_query = lax.fori_loop(first[i], last[i], step, jnp.zeros((HD, TILE), jnp.float32))
        rounded = (d_query * HD ** (-0.5)).astype(jnp.bfloat16)
        for part in range(TILE // BLK):
            slot = q_slot[i * (TILE // BLK) + part]
            out_ref[slot // per_device, 0:HD, lanes(slot)] = rounded[
                :, part * BLK : (part + 1) * BLK
            ]
        return carry

    lax.fori_loop(0, q_blocks * BLK // TILE, tile, 0)
    for i in range(kv_blocks):
        here = slice(i * BLK, (i + 1) * BLK)
        slot = kv_slot[i]
        out_ref[slot // per_device, HD : 2 * HD, lanes(slot)] = (
            (dk_ref[here, :] * HD ** (-0.5)).T.astype(jnp.bfloat16)
        )
        out_ref[slot // per_device, 2 * HD : 3 * HD, lanes(slot)] = (
            dv_ref[here, :].T.astype(jnp.bfloat16)
        )


def cost(micros):
    return pl.CostEstimate(
        flops=1 + micros * 1_000_000_000, bytes_accessed=1, transcendentals=0
    )


def kernel_call(kernel, tables, arrays, outs, scratch, micros):
    smem = pl.BlockSpec(memory_space=pltpu.SMEM)
    vmem = pl.BlockSpec(memory_space=pltpu.VMEM)
    return pl.pallas_call(
        kernel,
        out_shape=outs,
        in_specs=[smem] * len(tables) + [vmem] * len(arrays),
        out_specs=[vmem] * len(outs),
        scratch_shapes=scratch,
        compiler_params=pltpu.CompilerParams(vmem_limit_bytes=48 * 1024 * 1024),
        cost_estimate=cost(micros),
    )(*tables, *arrays)


class Links:
    def __init__(self, ctx_size):
        self.depth = ctx_size // 4
        index = lax.axis_index("ctx")
        self.core = index % 2
        self.y = (index // 2) % 2
        self.side = lax.axis_index("fsdp")
        self.half = index // 4 % 2
        self.quarter = index % 2 * 2 + self.y
        self.here = jnp.stack([self.half, self.core, self.y, self.side]).astype(jnp.int32)

    def route(self, place):
        pairs = []
        for z in range(self.depth):
            for y in range(2):
                for core in range(2):
                    to_z, to_y, to_core = place(z, y, core)
                    pairs.append(((z * 2 + y) * 2 + core, (to_z * 2 + to_y) * 2 + to_core))
        return pairs

    def over_core(self, value):
        return lax.ppermute(value, "ctx", self.route(lambda z, y, c: (z, y, 1 - c)))

    def over_y(self, value):
        return lax.ppermute(value, "ctx", self.route(lambda z, y, c: (z, 1 - y, c)))

    def over_z(self, value):
        return lax.ppermute(value, "ctx", self.route(lambda z, y, c: (z ^ 1, y, c)))

    def over_two_z(self, value):
        return lax.ppermute(value, "ctx", self.route(lambda z, y, c: (z ^ 2, y, c)))

    def over_x(self, value):
        return lax.ppermute(value, "fsdp", [(0, 1), (1, 0)])

    def to_side(self, value, side):
        return lax.ppermute(value, "fsdp", [(1 - side, side)])

    def spread_plane(self, value):
        across = self.over_core(value)
        beside = self.over_y(value)
        return (value, across, beside, self.over_core(beside))

    def deal_plane(self, near, far, give, give_far):
        got, got_far = self.over_core(give), self.over_core(give_far)
        return (near, got, self.over_y(far), self.over_y(got_far))

    def sum_depth(self, kept, got, time=None):
        def half(index):
            return add(pick(kept, index, 0), pick(got, index, 0))

        given = self.over_z(half(1 - self.half))
        if time is not None:
            given = after(given, time)
        part = add(half(self.half), given)
        full = add(part, self.over_two_z(part))
        return jnp.stack([full, self.over_z(full)])


def pick(value, index, axis):
    return lax.dynamic_index_in_dim(value, index, axis, keepdims=False)


def add(left, right):
    return (left.astype(jnp.float32) + right.astype(jnp.float32)).astype(jnp.bfloat16)


def after(value, *others):
    return lax.optimization_barrier((value, *others))[0]


def contract(left, right, axes):
    return lax.dot_general(
        left, right, ((axes[:1], axes[1:]), ((), ())), preferred_element_type=jnp.float32
    )


PARAMS = pltpu.CompilerParams(vmem_limit_bytes=56 * 1024 * 1024)


def call_with_here(
    kernel, here, grid, arrays, specs, outs, out_specs, scratch=(), aliases=None, micros=5
):
    return pl.pallas_call(
        kernel,
        grid_spec=pltpu.PrefetchScalarGridSpec(
            num_scalar_prefetch=1,
            grid=grid,
            in_specs=specs,
            out_specs=out_specs,
            scratch_shapes=list(scratch),
        ),
        out_shape=outs,
        input_output_aliases=aliases or {},
        compiler_params=PARAMS,
        cost_estimate=cost(micros),
    )(here, *arrays)


def whole(array):
    rank = len(array.shape)
    return pl.BlockSpec(array.shape, lambda i, here: (0,) * rank)


def project_kernel(here, *refs):
    x_ref, gain_ref, own_ref = refs[:3]
    pieces, q_gain, k_gain, cos_ref, sin_ref = refs[3:7], refs[7], refs[8], refs[9], refs[10]
    sent, weight, q_ref, k_ref, q_scale, k_scale, normed_ref, scale_ref = refs[11:]
    core, y, side = here[1], here[2], here[3]
    rows = own_ref.shape[0]
    part = rows // 4
    f32, bf16 = jnp.float32, jnp.bfloat16
    weight[pl.ds(pl.multiple_of(side * rows, rows), rows), :] = own_ref[...]
    for p in range(4):
        at = (1 - side) * rows + (((p % 2) ^ core) * 2 + ((p // 2) ^ y)) * part
        weight[pl.ds(pl.multiple_of(at, part), part), :] = pieces[p][...]
    x = x_ref[...].astype(f32)
    scale = rms_scale(x)
    scale_ref[...] = scale
    normed = (x * scale * gain_ref[...]).astype(bf16)
    normed_ref[...] = normed.T
    cosine, sine = cos_ref[...], sin_ref[...]
    half = HD // 2

    def turned(raw, gain, raw_ref, kept_scale, head):
        raw_ref[head * HD : (head + 1) * HD, :] = raw
        scale = rms_scale(raw, 0)
        kept_scale[head : head + 1, :] = scale
        value = raw * scale * gain
        first, second = value[:half], value[half:]
        return jnp.concatenate(
            [first * cosine - second * sine, second * cosine + first * sine], axis=0
        ).astype(bf16)

    per_group = HEADS // KV_HEADS
    for at in range(0, weight.shape[1], 2 * BLK):
        block = jnp.dot(normed, weight[:, at : at + 2 * BLK], preferred_element_type=f32)
        turned_block = block.T
        for n in range(2 * BLK // HD):
            head = at // HD + n
            raw = turned_block[n * HD : (n + 1) * HD, :]
            if head < HEADS:
                sent[head, 0:HD, :] = turned(raw, q_gain[...], q_ref, q_scale, head)
                continue
            head -= HEADS
            if head < KV_HEADS:
                value, row = turned(raw, k_gain[...], k_ref, k_scale, head), HD
            else:
                value, row, head = raw.astype(bf16), 2 * HD, head - KV_HEADS
            for copy in range(per_group):
                sent[head * per_group + copy, row : row + HD, :] = value


def project(here, x, gain, own, pieces, q_gain, k_gain, cosine, sine):
    tokens, width = x.shape
    f32, bf16 = jnp.float32, jnp.bfloat16
    shape = jax.ShapeDtypeStruct
    arrays = [x, gain, own, *pieces, q_gain, k_gain, cosine, sine]
    outs = [
        shape((HEADS, 3 * HD, tokens), bf16),
        shape((width, own.shape[1]), bf16),
        shape((HEADS * HD, tokens), f32),
        shape((KV_HEADS * HD, tokens), f32),
        shape((HEADS, tokens), f32),
        shape((KV_HEADS, tokens), f32),
        shape((width, tokens), bf16),
        shape((tokens, 1), f32),
    ]
    return call_with_here(
        project_kernel, here, (1,), arrays, [whole(a) for a in arrays], outs,
        [whole(o) for o in outs], micros=PROJECT,
    )


def layer(array, index):
    return pl.BlockSpec((1, *array.shape[1:]), lambda i, here: (index, 0, 0))


def attend_out_kernel(here, *refs):
    attn_ref, x_ref, gain_ref, own_ref = refs[:4]
    pieces = refs[4:20]
    weight, h_ref, scale_ref, two_ref, two_t_ref = refs[20:]
    core, y, side = here[1], here[2], here[3]
    rows = own_ref.shape[0]
    part = rows // 4
    weight[pl.ds(pl.multiple_of(side * rows, rows), rows), :] = own_ref[...]
    for p in range(4):
        at = (1 - side) * rows + (((p % 2) ^ core) * 2 + ((p // 2) ^ y)) * part
        for n in range(4):
            piece = pieces[4 * p + n]
            wide = piece.shape[1]
            weight[pl.ds(pl.multiple_of(at, part), part), n * wide : (n + 1) * wide] = piece[...]
    attn = attn_ref[...].T
    h_one = x_ref[...].astype(jnp.float32) + jnp.dot(
        attn, weight[...], preferred_element_type=jnp.float32
    )
    scale = rms_scale(h_one)
    h_ref[...] = h_one
    scale_ref[...] = scale
    two = (h_one * scale * gain_ref[...]).astype(jnp.bfloat16)
    two_ref[...] = two
    two_t_ref[...] = two.T


def attend_out(here, attn, x, gain, own, pieces):
    tokens, width = x.shape
    f32, bf16 = jnp.float32, jnp.bfloat16
    shape = jax.ShapeDtypeStruct
    part = own.shape[0] // 4
    cuts = 4
    part_width = width // cuts
    first = pieces[0].shape[1] // part_width - cuts
    arrays = [attn, x, gain, own]
    specs = [whole(a) for a in arrays]
    for piece in pieces:
        for n in range(cuts):
            arrays.append(piece)
            specs.append(pl.BlockSpec((part, part_width), lambda i, here, n=n: (0, first + n)))
    outs = [
        shape((width, width), bf16),
        shape((tokens, width), f32),
        shape((tokens, 1), f32),
        shape((tokens, width), bf16),
        shape((width, tokens), bf16),
    ]
    return call_with_here(
        attend_out_kernel, here, (1,), arrays, specs, outs, [whole(o) for o in outs], micros=OUT
    )


def ffn_kernel(chunk, here, *refs):
    two_ref, d_ref, own_ref = refs[:3]
    pieces, down_ref, down_pieces = (refs[3:7], refs[7:11]), refs[11], refs[12:16]
    refs = refs[4:]
    if chunk == 0:
        before_refs, refs = refs[12:13], refs[13:]
        near, far, give, give_far, hidden_ref, out_ref, d_two_ref = refs[:7]
        refs = refs[7:]
    else:
        before_refs, gain_ref, refs = refs[12:17], refs[17], refs[18:]
        near, far, give, give_far, hidden_ref = refs[:5]
        out_ref, d_h_ref, d_attn_ref, heads_ref, gain_term_ref = refs[5:10]
        refs = refs[10:]
    weight, down, hidden_rows, out_sum, two_sum = refs[:5]
    held, weight_sem, down_sem, before_sem = refs[5:-3], refs[-3], refs[-2], refs[-1]
    core, y, side = here[1], here[2], here[3]
    f32, bf16 = jnp.float32, jnp.bfloat16
    own_rows, columns = own_ref.shape[1], own_ref.shape[2] // CHUNKS
    part = own_rows // 4
    tile = columns // FFN_TILES
    half = columns // 2

    def quarter(p):
        return ((p % 2) ^ core) * 2 + ((p // 2) ^ y)

    def copies(n):
        at = slice(n * tile, (n + 1) * tile)
        mine = pl.ds(pl.multiple_of(side * own_rows, own_rows), own_rows)
        found = [
            pltpu.make_async_copy(
                own_ref.at[:, :, chunk * columns + n * tile : chunk * columns + (n + 1) * tile],
                weight.at[:, mine, at],
                weight_sem.at[n, 0],
            )
        ]
        for p in range(4):
            rows = pl.ds(pl.multiple_of((1 - side) * own_rows + quarter(p) * part, part), part)
            for kind in range(2):
                begin = n * tile + (columns if kind == 1 and chunk == 1 else 0)
                found.append(
                    pltpu.make_async_copy(
                        pieces[kind][p].at[:, begin : begin + tile],
                        weight.at[kind, rows, at],
                        weight_sem.at[n, 1 + 2 * p + kind],
                    )
                )
        return found

    def own_down(n):
        at = slice(n * tile, (n + 1) * tile)
        return [pltpu.make_async_copy(down_ref.at[at, :], down.at[at, :], down_sem.at[n, 0])]

    def other_down(n):
        at = slice(n * tile, (n + 1) * tile)
        found = []
        for p in range(4):
            wide = down_pieces[p].shape[1]
            lanes = pl.ds(pl.multiple_of(quarter(p) * wide, wide), wide)
            found.append(
                pltpu.make_async_copy(
                    down_pieces[p].at[at, :], down.at[at, lanes], down_sem.at[n, p]
                )
            )
        return found

    def each(action, n):
        for copy in copies(n):
            action(copy)

        @pl.when(side == chunk)
        def _():
            for copy in own_down(n):
                action(copy)

        @pl.when(side != chunk)
        def _():
            for copy in other_down(n):
                action(copy)

    before = [
        pltpu.make_async_copy(ref, held[n], before_sem.at[n]) for n, ref in enumerate(before_refs)
    ]
    for n in range(FFN_TILES):
        each(lambda copy: copy.start(), n)
    for copy in before:
        copy.start()
    two = two_ref[...]
    d_ffn = d_ref[...]
    for n in range(FFN_TILES):
        each(lambda copy: copy.wait(), n)
        at = slice(n * tile, (n + 1) * tile)
        gate = jnp.dot(two, weight[0, :, at], preferred_element_type=f32)
        upper = jnp.dot(two, weight[1, :, at], preferred_element_type=f32)
        d_hidden = contract(d_ffn, down[at, :], (1, 1))
        sigma = jax.nn.sigmoid(gate)
        silu = gate * sigma
        hidden = (silu * upper).astype(bf16)
        d_gate = (d_hidden * upper * sigma * (1.0 + gate * (1.0 - sigma))).astype(bf16)
        d_upper = (d_hidden * silu).astype(bf16)
        out_term = jnp.dot(hidden, down[at, :], preferred_element_type=f32)
        two_term = contract(d_gate, weight[0, :, at], (1, 1)) + contract(
            d_upper, weight[1, :, at], (1, 1)
        )
        out_sum[...] = out_term if n == 0 else out_sum[...] + out_term
        two_sum[...] = two_term if n == 0 else two_sum[...] + two_term
        hidden_rows[:, at] = hidden
        mine = jnp.where(core == 0, d_gate, d_upper)
        other = jnp.where(core == 0, d_upper, d_gate)
        for column in range(2):
            begin, end = max(n * tile, column * half), min((n + 1) * tile, (column + 1) * half)
            if begin >= end:
                continue
            source = slice(begin - n * tile, end - n * tile)
            target = slice(begin - column * half, end - column * half)
            first, second = mine[:, source], other[:, source]

            @pl.when(y == column)
            def _(first=first, second=second, target=target):
                near[:, target] = first
                give[:, target] = second

            @pl.when(y != column)
            def _(first=first, second=second, target=target):
                far[:, target] = first
                give_far[:, target] = second

    lower, upper = hidden_rows[:, :half], hidden_rows[:, half:]
    hidden_ref[0] = jnp.where(core == 0, lower, upper)
    hidden_ref[1] = jnp.where(core == 0, upper, lower)
    for copy in before:
        copy.wait()
    if chunk == 0:
        out_ref[...] = held[0][...] + out_sum[...]
        d_two_ref[...] = two_sum[...]
    else:
        out_before, two_before, h_one, scale, w_out = held
        out_ref[...] = (out_before[...] + out_sum[...]).astype(bf16)
        d_norm, gain_term = norm_back(
            two_before[...] + two_sum[...], h_one[...], scale[...], gain_ref[...]
        )
        gain_term_ref[...] = jnp.sum(gain_term, axis=0, keepdims=True)
        d_h_one = d_ffn.astype(f32) + d_norm
        d_h_ref[...] = d_h_one
        d_attn = d_h_one.astype(bf16)
        d_attn_ref[...] = d_attn
        heads_ref[...] = contract(w_out[...], d_attn, (1, 1)).astype(bf16)


FFN_TILES = 3


def ffn(here, chunk, two, d_ffn, own, pieces, down, down_pieces, before, gain=None):
    tokens, width = two.shape
    columns = own.shape[2] // CHUNKS
    shape = jax.ShapeDtypeStruct
    f32, bf16 = jnp.float32, jnp.bfloat16
    outs = [shape((tokens, columns // 2), bf16)] * 4 + [shape((2, tokens, columns // 2), bf16)]
    if chunk == 0:
        outs += [shape((tokens, width), f32)] * 2
    else:
        outs += [
            shape((tokens, width), bf16),
            shape((tokens, width), f32),
            shape((tokens, width), bf16),
            shape((width, tokens), bf16),
            shape((1, width), f32),
        ]
    far_away = pl.BlockSpec(memory_space=pl.ANY)
    arrays = [two, d_ffn, own, *pieces[0], *pieces[1], down, *down_pieces, *before]
    specs = [whole(two), whole(d_ffn)] + [far_away] * (len(arrays) - 2)
    if gain is not None:
        arrays.append(gain)
        specs.append(whole(gain))
    got = call_with_here(
        functools.partial(ffn_kernel, chunk),
        here,
        (1,),
        arrays,
        specs,
        outs,
        [whole(o) for o in outs],
        [
            pltpu.VMEM((2, width, columns), bf16),
            pltpu.VMEM((columns, width), bf16),
            pltpu.VMEM((tokens, columns), bf16),
            pltpu.VMEM((tokens, width), f32),
            pltpu.VMEM((tokens, width), f32),
        ]
        + [pltpu.VMEM(v.shape, v.dtype) for v in before]
        + [
            pltpu.SemaphoreType.DMA((FFN_TILES, 9)),
            pltpu.SemaphoreType.DMA((FFN_TILES, 4)),
            pltpu.SemaphoreType.DMA((len(before),)),
        ],
        micros=FFN[chunk],
    )
    return got[:4], got[4], got[5:]


def wide_product_kernel(here, *refs):
    planes, terms = refs[:4], refs[4:8]
    sent, kept, left, right = refs[8:]
    tokens = planes[0].shape[1]
    for i in range(4):
        left[:, i * tokens : (i + 1) * tokens] = planes[i][...]
        right[i * tokens : (i + 1) * tokens, :] = terms[i][...]
    side = here[3]
    _, step, _ = kept.shape
    for half in range(2):
        for owner, out_ref in ((1 - side, sent), (side, kept)):
            place = pl.multiple_of(owner * 2 * step + half * step, step)
            out_ref[half] = jnp.dot(
                left[pl.ds(place, step), :], right[...], preferred_element_type=jnp.float32
            ).astype(out_ref.dtype)


def wide_products(here, two_plane, shares, columns):
    rows, tokens = two_plane[0].shape
    outs = [
        jax.ShapeDtypeStruct((2, rows // 4, columns), jnp.bfloat16),
        jax.ShapeDtypeStruct((2, rows // 4, columns), jnp.float32),
    ]
    arrays = [*two_plane, *shares]
    return call_with_here(
        wide_product_kernel,
        here,
        (1,),
        arrays,
        [whole(a) for a in two_plane]
        + [pl.BlockSpec((tokens, columns), lambda i, here: (0, 0))] * 4,
        outs,
        [whole(o) for o in outs],
        [
            pltpu.VMEM((rows, 4 * tokens), jnp.bfloat16),
            pltpu.VMEM((4 * tokens, columns), jnp.bfloat16),
        ],
        micros=8,
    )


def down_product_kernel(here, *refs):
    planes, terms = refs[:4], (refs[4:8], refs[8:12])
    sent, kept, left, right = refs[12:]
    tokens = planes[0].shape[0]
    for i in range(4):
        right[i * tokens : (i + 1) * tokens, :] = planes[i][...]
    for chunk in range(2):

        @pl.when(here[3] == chunk)
        def _(chunk=chunk):
            for i in range(4):
                left[:, i * tokens : (i + 1) * tokens] = terms[chunk][i][0].T

    _, step, _ = kept.shape
    for half in range(2):
        for owner, out_ref in ((1 - here[2], sent), (here[2], kept)):
            place = pl.multiple_of(owner * 2 * step + half * step, step)
            out_ref[half] = jnp.dot(
                left[pl.ds(place, step), :], right[...], preferred_element_type=jnp.float32
            ).astype(out_ref.dtype)


def down_products(here, d_plane, first, second):
    tokens, columns = d_plane[0].shape
    rows = first[0].shape[2]
    outs = [
        jax.ShapeDtypeStruct((2, rows // 4, columns), jnp.bfloat16),
        jax.ShapeDtypeStruct((2, rows // 4, columns), jnp.float32),
    ]
    return call_with_here(
        down_product_kernel,
        here,
        (1,),
        [*d_plane, *first, *second],
        [whole(a) for a in d_plane] + [layer(a, i % 2) for i, a in enumerate((*first, *second))],
        outs,
        [whole(o) for o in outs],
        [
            pltpu.VMEM((rows, 4 * tokens), jnp.bfloat16),
            pltpu.VMEM((4 * tokens, columns), jnp.bfloat16),
        ],
        micros=8,
    )


GAIN_ROWS = 16


def attention_back_kernel(here, *refs):
    d_ref, q_ref, k_ref, q_scale, k_scale, q_gain, k_gain, cos_ref, sin_ref = refs[:9]
    weight, x_ref, scale_ref, gain_ref, d_h_ref, d_attn_ref = refs[9:15]
    near, far, give, give_far, d_x_ref, gains_ref = refs[15:21]
    turned, natural = refs[21:]
    f32, bf16 = jnp.float32, jnp.bfloat16
    core, y = here[1], here[2]
    cosine, sine = cos_ref[...], sin_ref[...]
    half = HD // 2
    per_group = HEADS // KV_HEADS
    tokens = x_ref.shape[0]

    def back(grad, raw, scale, gain):
        first, second = grad[:half], grad[half:]
        normed = jnp.concatenate(
            [first * cosine + second * sine, second * cosine - first * sine], axis=0
        )
        return norm_back(normed, raw, scale, gain, 0)

    q_term = jnp.zeros((HD, tokens), f32)
    k_term = jnp.zeros((HD, tokens), f32)
    for head in range(HEADS):
        at = slice(head * HD, (head + 1) * HD)
        grad, term = back(
            d_ref[head, :HD, :].astype(f32), q_ref[at, :], q_scale[head : head + 1, :], q_gain[...]
        )
        turned[at, :] = grad.astype(bf16)
        q_term = q_term + term
    for head in range(KV_HEADS):
        at = slice(head * HD, (head + 1) * HD)
        both = d_ref[head * per_group, HD:, :].astype(f32)
        for other in range(1, per_group):
            both = both + d_ref[head * per_group + other, HD:, :].astype(f32)
        grad, term = back(both[:HD], k_ref[at, :], k_scale[head : head + 1, :], k_gain[...])
        place = HEADS * HD + head * HD
        turned[place : place + HD, :] = grad.astype(bf16)
        k_term = k_term + term
        place += KV_HEADS * HD
        turned[place : place + HD, :] = both[HD:].astype(bf16)
    rows = turned.shape[0] // 4
    columns = d_attn_ref.shape[1] // 4
    shares = ((near, core, y), (far, core, 1 - y), (give, 1 - core, y), (give_far, 1 - core, 1 - y))
    for out_ref, to_core, to_y in shares:
        share = to_core * 2 + to_y
        out_ref[:rows, :] = turned[pl.ds(pl.multiple_of(share * rows, rows), rows), :]
        out_ref[rows:, :] = d_attn_ref[:, pl.ds(pl.multiple_of(share * columns, columns), columns)]
    for at in range(0, turned.shape[0], 256):
        natural[:, at : at + 256] = turned[at : at + 256, :].T
    d_normed = contract(natural[...], weight[...], (1, 1))
    x = x_ref[...].astype(f32)
    d_norm, gain_term = norm_back(d_normed, x, scale_ref[...], gain_ref[...])
    d_x_ref[...] = d_h_ref[...] + d_norm
    gains_ref[...] = jnp.zeros_like(gains_ref)
    gains_ref[0:1, :] = jnp.sum(gain_term, axis=0, keepdims=True)
    gains_ref[1:2, 0:HD] = jnp.sum(q_term.T, axis=0, keepdims=True)
    gains_ref[2:3, 0:HD] = jnp.sum(k_term.T, axis=0, keepdims=True)


def attention_back(here, arrays):
    f32, bf16 = jnp.float32, jnp.bfloat16
    shape = jax.ShapeDtypeStruct
    weight, x = arrays[9], arrays[10]
    tokens, width = x.shape
    rows = weight.shape[1] // 4 + tokens
    assert width // 4 == tokens
    outs = [
        *[shape((rows, tokens), bf16)] * 4,
        shape((tokens, width), f32),
        shape((8, width), f32),
    ]
    return call_with_here(
        attention_back_kernel, here, (1,), arrays, [whole(a) for a in arrays], outs,
        [whole(o) for o in outs],
        [pltpu.VMEM((weight.shape[1], tokens), bf16), pltpu.VMEM((tokens, weight.shape[1]), bf16)],
        micros=12,
    )


def attention_product_kernel(here, *refs):
    planes, terms, gains_ref, ffn_gain_ref = refs[:4], refs[4:8], refs[8], refs[9]
    sent, kept, left, right, left_out, right_out = refs[10:]
    tokens = planes[0].shape[2]
    cut = right.shape[1]
    for i in range(4):
        at = slice(i * tokens, (i + 1) * tokens)
        left[:, at] = planes[i][0]
        left_out[:, at] = planes[i][1]
        share = terms[i]
        right[at, :] = share[:cut].T
        right_out[at, :] = share[cut:]
    step = left.shape[0] // 4
    for owner, out_ref in ((1 - here[3], sent), (here[3], kept)):
        for half in range(2):
            at = pl.ds(pl.multiple_of(owner * 2 * step + half * step, step), step)
            out_ref[half, :step, :cut] = jnp.dot(
                left[at, :], right[...], preferred_element_type=jnp.float32
            ).astype(out_ref.dtype)
            out_ref[half, :step, cut:] = jnp.dot(
                left_out[at, :], right_out[...], preferred_element_type=jnp.float32
            ).astype(out_ref.dtype)
        rows = gains_ref.shape[1] // 2
        mine = pl.ds(pl.multiple_of(owner * rows, rows), rows)
        wide = out_ref.shape[2] - rows
        block = jnp.concatenate(
            [
                jnp.concatenate([gains_ref[0:1, mine], gains_ref[1:2, 0:wide]], axis=1),
                jnp.concatenate([ffn_gain_ref[:, mine], gains_ref[2:3, 0:wide]], axis=1),
                jnp.zeros((GAIN_ROWS - 2, out_ref.shape[2]), jnp.float32),
            ],
            axis=0,
        )
        out_ref[0, step:, :] = block.astype(out_ref.dtype)
        out_ref[1, step:, :] = jnp.zeros((GAIN_ROWS, out_ref.shape[2]), out_ref.dtype)


def attention_products(here, pair_plane, shares, gains, ffn_gain):
    _, width, tokens = pair_plane[0].shape
    cut = shares[0].shape[0] - tokens
    shape = (2, width // 4 + GAIN_ROWS, cut + tokens)
    outs = [jax.ShapeDtypeStruct(shape, jnp.bfloat16), jax.ShapeDtypeStruct(shape, jnp.float32)]
    return call_with_here(
        attention_product_kernel,
        here,
        (1,),
        [*pair_plane, *shares, gains, ffn_gain],
        [whole(a) for a in (*pair_plane, *shares, gains, ffn_gain)],
        outs,
        [whole(o) for o in outs],
        [
            pltpu.VMEM((width, 4 * tokens), jnp.bfloat16),
            pltpu.VMEM((4 * tokens, cut), jnp.bfloat16),
            pltpu.VMEM((width, 4 * tokens), jnp.bfloat16),
            pltpu.VMEM((4 * tokens, tokens), jnp.bfloat16),
        ],
        micros=8,
    )


def place_gate_up_kernel(here, *refs):
    mine, across, beside, diagonal, out_ref = *refs[:4], refs[-1]
    pieces = (mine, across, beside, diagonal)
    wide = mine.shape[2]
    for case in range(4):
        core, y = case // 2, case % 2

        @pl.when((here[1] == core) & (here[2] == y))
        def _(core=core, y=y):
            for kind in range(2):
                for column in range(2):
                    value = pieces[(y ^ column) * 2 + (core ^ kind)][0]
                    out_ref[:, kind, column * wide : (column + 1) * wide] = value.astype(
                        jnp.float32
                    )


def place_gate_up(here, chunk, pieces, before):
    _, rows, wide = pieces[0].shape
    step = 64
    blocks = rows // step

    def source(i, here):
        return ((i // blocks) ^ here[0], i % blocks, 0)

    arrays = list(pieces)
    specs = [pl.BlockSpec((1, step, wide), source)] * 4
    aliases = {}
    if before is not None:
        arrays.append(before)
        specs.append(pl.BlockSpec(memory_space=pl.ANY))
        aliases = {5: 0}
    (out,) = call_with_here(
        place_gate_up_kernel,
        here,
        (2 * blocks,),
        arrays,
        specs,
        [jax.ShapeDtypeStruct((2 * rows, 2, 2 * wide * CHUNKS), jnp.float32)],
        [pl.BlockSpec((step, 2, 2 * wide), lambda i, here: (i, 0, chunk))],
        aliases=aliases,
        micros=10,
    )
    return out


def place_down(here, pieces):
    _, rows, columns = pieces[0].shape

    def kernel(here, *refs):
        for s in range(8):

            @pl.when(pl.program_id(0) == s)
            def _(s=s):
                refs[4][...] = refs[s % 4][s // 4].astype(jnp.float32)

    def target(s, here):
        half = (s // 4) ^ here[0]
        y = ((s // 2) % 2) ^ here[2]
        core = (s % 2) ^ here[1]
        return ((core * 2 + y) * 2 + half, 0)

    (out,) = call_with_here(
        kernel,
        here,
        (8,),
        list(pieces),
        [whole(v) for v in pieces],
        [jax.ShapeDtypeStruct((rows * 8, columns), jnp.float32)],
        [pl.BlockSpec((rows, columns), target)],
    )
    return out


def place_attention(here, pieces, cut):
    _, rows, columns = pieces[0].shape
    rows -= GAIN_ROWS

    def kernel(here, *refs):
        qkv_ref, out_ref, gains_ref = refs[4:]
        for s in range(8):

            @pl.when(pl.program_id(0) == s)
            def _(s=s):
                value = refs[s % 4][s // 4]
                qkv_ref[...] = value[:rows, :cut].astype(jnp.float32)
                out_ref[...] = value[:rows, cut:].astype(jnp.float32)
                gains = value[rows:].astype(jnp.float32)
                gains_ref[...] = gains if s == 0 else gains_ref[...] + gains

    def target(s, here):
        half = (s // 4) ^ here[0]
        return (half, ((s % 2) ^ here[1]) * 2 + (((s // 2) % 2) ^ here[2]))

    shape = jax.ShapeDtypeStruct
    f32 = jnp.float32
    gain_shape = (GAIN_ROWS, columns)
    return call_with_here(
        kernel,
        here,
        (8,),
        list(pieces),
        [whole(v) for v in pieces],
        [
            shape((2 * rows, 4 * cut), f32),
            shape((2 * rows, 4 * (columns - cut)), f32),
            shape(gain_shape, f32),
        ],
        [
            pl.BlockSpec((rows, cut), target),
            pl.BlockSpec((rows, columns - cut), target),
            pl.BlockSpec(gain_shape, lambda s, here: (0, 0)),
        ],
    )


def on_block(
    tokens,
    qkv_weight,
    out_weight,
    gate_up_weight,
    down_weight,
    attn_gain,
    ffn_gain,
    query_gain,
    key_gain,
    seq_lengths,
    block_order,
    cotangent,
):
    inputs = tokens[0].astype(jnp.float32)
    rows_here = inputs.shape[0]
    ctx_size = lax.axis_size("ctx")
    ctx_index = lax.axis_index("ctx")
    per_group = HEADS // KV_HEADS
    q_width = HEADS * HD
    kv_width = KV_HEADS * HD
    order_row = block_order[0]
    lengths_row = seq_lengths[0]
    slots = jnp.arange(rows_here, dtype=jnp.int32) // BLK + ctx_index * (rows_here // BLK)
    table = slots[:, None] == jnp.arange(order_row.shape[0], dtype=jnp.int32)[None, :]
    packed = (
        jnp.sum(jnp.where(table, order_row[None, :], 0), axis=1) * BLK
        + jnp.arange(rows_here, dtype=jnp.int32) % BLK
    )
    local = packed - starts_of(packed, lengths_row)
    frequency = ROPE_BASE ** (-2.0 * jnp.arange(HD // 2, dtype=jnp.float32) / HD)
    angle = frequency[:, None] * local.astype(jnp.float32)[None, :]
    cosine = jnp.cos(angle)[None]
    sine = jnp.sin(angle)[None]
    bf16, f32 = jnp.bfloat16, jnp.float32
    parts = ctx_size // HEADS
    part = ctx_index // HEADS
    part_blocks = HEADS * rows_here // BLK
    q_order = lax.dynamic_slice_in_dim(order_row, part * part_blocks, part_blocks)
    q_slot, q_place, q_start = block_tables(q_order, lengths_row)
    q_slot = q_slot + part * part_blocks
    kv_slot, _, _ = block_tables(order_row, lengths_row)
    first = jnp.min(q_start.reshape(-1, TILE), axis=1) // TILE
    last = jnp.max(q_place.reshape(-1, TILE), axis=1) // TILE + 1
    tables = (q_slot, kv_slot, first, last)
    q_rows, kv_rows = part_blocks * BLK, order_row.shape[0] * BLK

    links = Links(ctx_size)
    here = links.here
    width = inputs.shape[1]
    rows = qkv_weight.shape[0]
    part_rows = rows // 4

    def quarter_rows(weight):
        return lax.dynamic_slice_in_dim(weight, links.quarter * part_rows, part_rows)

    qkv_piece = quarter_rows(qkv_weight)
    gains_here = jnp.concatenate([after(attn_gain, qkv_piece), ffn_gain, query_gain, key_gain])
    gains_there = links.over_x(gains_here)

    def gain_of(at, size):
        mine, other = gains_here[at : at + size], gains_there[at : at + size]
        return jnp.where(
            links.side == 0, jnp.concatenate([mine, other]), jnp.concatenate([other, mine])
        ).astype(f32)

    gain_attn = gain_of(0, rows)
    gain_ffn = gain_of(rows, rows)
    gain_query = gain_of(2 * rows, HD // 2)
    gain_key = gain_of(2 * rows + HD // 2, HD // 2)
    ff_chunk = gate_up_weight.shape[2] // CHUNKS

    def gate_up_piece(chunk):
        piece = lax.dynamic_slice(
            gate_up_weight,
            (links.quarter * part_rows, 0, chunk * ff_chunk),
            (part_rows, 2, ff_chunk),
        )
        return [piece[:, 0], piece[:, 1]]

    qkv_there = links.over_x(qkv_piece)
    first_gate, first_up = gate_up_piece(0)
    first_piece = first_gate
    up_piece = jnp.concatenate([first_up, quarter_rows(out_weight)], axis=1)
    second_gate, second_up = gate_up_piece(1)
    second_piece = jnp.concatenate([second_gate, second_up], axis=1)
    down_piece = lax.dynamic_slice_in_dim(
        down_weight, links.quarter * (width // 4), width // 4, 1
    )
    d_ffn = cotangent[0]
    tokens_here = tokens[0]
    qkv_there = after(qkv_there, first_piece, up_piece)
    first_there = links.over_x(after(first_piece, qkv_there))
    up_there = links.over_x(after(up_piece, first_there))
    qkv_pieces = links.spread_plane(qkv_there)
    sent, w_qkv, q_raw, k_raw, q_scale, k_scale, normed, scale_one = project(
        here, after(tokens_here, first_there), gain_attn[None], qkv_weight, qkv_pieces,
        gain_query[:, None], gain_key[:, None], cosine[0], sine[0],
    )
    got = lax.all_to_all(sent, "ctx", 0, 0, tiled=True)
    gate_up = jnp.transpose(after(gate_up_weight, sent), (1, 0, 2))
    up_there = after(up_there, sent)
    d_there = links.over_x(after(d_ffn, up_there))
    down_there = links.over_x(after(down_piece, up_there))
    first_beside = links.over_y(first_there)
    up_beside = links.over_y(up_there)
    second_there = links.over_x(after(second_piece, down_there))
    down_beside = links.over_y(down_there)
    got = after(got, d_there, gate_up)
    q_place, q_start = q_place[None], q_start[None]
    shape = jax.ShapeDtypeStruct
    attn_sent, *held = kernel_call(
        attend_kernel,
        tables,
        (got, q_place, q_start),
        [
            shape((ctx_size, HD, rows_here), bf16),
            shape((q_rows, HD), bf16),
            shape((HD, q_rows), bf16),
            shape((kv_rows, HD), bf16),
            shape((HD, kv_rows), bf16),
            shape((kv_rows, HD), bf16),
            shape((HD, q_rows), f32),
            shape((1, q_rows), f32),
        ],
        [pltpu.VMEM((HD, kv_rows), bf16)],
        ATTEND,
    )
    attn_sent = after(attn_sent, up_beside, first_beside)
    attn_in = lax.dynamic_slice_in_dim(
        lax.all_to_all(attn_sent, "ctx", 0, 0, tiled=True), part * HEADS, HEADS
    ).reshape(q_width, rows_here)
    second_there = after(second_there, attn_sent)

    def spread(there, beside, time):
        there, beside = after(there, time), after(beside, time)
        return (there, links.over_core(there), beside, links.over_core(beside))

    first_pieces = spread(first_there, first_beside, attn_in)
    up_pieces = spread(up_there, up_beside, attn_sent)
    down_pieces = spread(down_there, down_beside, attn_in)
    second_beside = links.over_y(second_there)
    w_out, h_one, scale_two, two, two_t = attend_out(
        here, attn_in, tokens_here, gain_ffn[None], out_weight, up_pieces
    )
    two_beside = links.over_y(two_t)
    dealt_here, first_hidden, (out_sum, two_sum) = ffn(
        here, 0, two, d_ffn, gate_up, (first_pieces, up_pieces), down_weight, down_pieces, [h_one]
    )
    second_beside = after(second_beside, out_sum)
    second_pieces = (
        second_there, links.over_core(second_there), second_beside, links.over_core(second_beside)
    )
    near, far, give, give_far = dealt_here
    got_far = links.over_core(give_far)
    first_shares = (near, links.over_core(give), links.over_y(far), links.over_y(got_far))
    out_sum = after(out_sum, got_far)
    dealt_here, second_hidden, (output, d_h_one, d_attn, d_heads, ffn_gain_term) = ffn(
        here, 1, two, d_ffn, gate_up, (second_pieces, second_pieces), down_weight, down_pieces,
        [out_sum, two_sum, h_one, scale_two, w_out], gain_ffn[None],
    )
    second_shares = links.deal_plane(*dealt_here)

    def plane(value, beside, time):
        value, beside = after(value, time), after(beside, time)
        return (value, links.over_core(value), beside, links.over_core(beside))

    columns = ff_chunk // 2
    first_hidden_there = links.to_side(first_hidden, 0)
    second_hidden_there = links.to_side(second_hidden, 1)
    d_heads = after(d_heads, two_beside, first_shares[2], first_hidden_there).reshape(HEADS, HD, rows_here)
    pair = jnp.stack([after(normed, d_heads), attn_in])
    d_got = lax.all_to_all(d_heads, "ctx", 0, 0, tiled=True)
    two_plane = plane(two_t, two_beside, d_got)
    first_products = wide_products(here, two_plane, first_shares, columns)
    d_plane = (d_ffn, links.over_core(after(d_ffn, attn_sent)), d_there, links.over_core(d_there))
    first_across, first_diagonal = (
        links.over_core(after(first_hidden, d_heads)), links.over_core(first_hidden_there)
    )
    second_across = links.over_core(second_hidden)
    d_got = after(
        d_got, first_products[0], pair, second_hidden_there,
        d_plane[1], d_plane[3], first_across, first_diagonal, second_across,
    )
    (d_sent,) = kernel_call(
        attend_back_kernel,
        tables,
        (d_got, q_place, q_start, *held),
        [shape((ctx_size, 3 * HD, rows_here), bf16)],
        [
            pltpu.VMEM((HD, q_rows), bf16),
            pltpu.VMEM((q_rows, HD), bf16),
            pltpu.VMEM((kv_rows, HD), f32),
            pltpu.VMEM((kv_rows, HD), f32),
        ],
        ATTEND_BACK,
    )
    first_got = links.over_x(first_products[0])
    d_sent = after(d_sent, first_got, *second_shares[2:])
    d_back = lax.all_to_all(d_sent, "ctx", 0, 0, tiled=True)
    second_products = wide_products(
        here, two_plane, [after(v, d_sent) for v in second_shares], columns
    )
    down_terms = down_products(
        here, d_plane,
        (first_hidden, first_across, first_hidden_there, first_diagonal),
        (second_hidden, second_across, second_hidden_there, links.over_core(second_hidden_there)),
    )
    pair_beside = links.over_y(after(pair, d_sent))
    d_back = after(d_back, down_terms[0], pair_beside, second_products[0])
    *d_shares, d_inputs, gain_sums = attention_back(
        here,
        [
            d_back, q_raw, k_raw, q_scale, k_scale, gain_query[:, None], gain_key[:, None],
            cosine[0], sine[0], w_qkv, tokens_here, scale_one, gain_attn[None], d_h_one, d_attn,
        ],
    )
    near, far, give, give_far = d_shares
    got, got_far = links.over_core(give), links.over_core(give_far)
    second_got = links.over_x(after(second_products[0], first_got))
    attention_shares = (
        near, got, links.over_y(after(far, second_got)), links.over_y(got_far)
    )
    second_got = after(second_got, got_far)
    down_got = links.over_y(after(down_terms[0], *attention_shares[2:]))
    pair_plane = plane(pair, pair_beside, d_shares[0])
    attention_terms = attention_products(
        here, pair_plane, attention_shares, gain_sums, ffn_gain_term
    )
    attention_got = links.over_x(attention_terms[0])
    down_got = after(down_got, attention_got)
    first_pair = links.sum_depth(first_products[1], after(first_got, d_back), got_far)
    second_pair = links.sum_depth(second_products[1], second_got)
    down_pair = links.sum_depth(down_terms[1], down_got)
    first_placed = place_gate_up(here, 0, links.spread_plane(first_pair), None)
    second_spread = links.spread_plane(after(second_pair, first_placed))
    down_spread = links.spread_plane(down_pair)
    cut = qkv_weight.shape[1] // 4
    attention_pair = links.sum_depth(attention_terms[1], attention_got)
    grad_gate_up = place_gate_up(here, 1, second_spread, first_placed)
    grad_down = place_down(here, down_spread)
    beside = after(links.over_y(attention_pair), first_placed, grad_down)
    attention_spread = (
        attention_pair, links.over_core(attention_pair), beside, links.over_core(beside)
    )
    grad_qkv, grad_out, gain_sums = place_attention(here, attention_spread, cut)
    at = links.side * (HD // 2)
    gain_grads = [
        gain_sums[0, :rows],
        gain_sums[1, :rows],
        lax.dynamic_slice_in_dim(gain_sums[0, rows : rows + HD], at, HD // 2),
        lax.dynamic_slice_in_dim(gain_sums[1, rows : rows + HD], at, HD // 2),
    ]
    return (
        output[None],
        d_inputs[None],
        grad_qkv,
        grad_out,
        grad_gate_up,
        grad_down,
        *gain_grads,
    )


def on_device(
    tokens,
    qkv_weight,
    out_weight,
    gate_up_weight,
    down_weight,
    attn_gain,
    ffn_gain,
    query_gain,
    key_gain,
    seq_lengths,
    block_order,
    cotangent,
):
    inputs = tokens[0].astype(jnp.float32)
    rows_here = inputs.shape[0]
    ctx_size = lax.axis_size("ctx")
    ctx_index = lax.axis_index("ctx")
    per_group = HEADS // KV_HEADS
    q_width = HEADS * HD
    kv_width = KV_HEADS * HD
    order_row = block_order[0]
    lengths_row = seq_lengths[0]
    slots = jnp.arange(rows_here, dtype=jnp.int32) // BLK + ctx_index * (rows_here // BLK)
    table = slots[:, None] == jnp.arange(order_row.shape[0], dtype=jnp.int32)[None, :]
    packed = (
        jnp.sum(jnp.where(table, order_row[None, :], 0), axis=1) * BLK
        + jnp.arange(rows_here, dtype=jnp.int32) % BLK
    )
    local = packed - starts_of(packed, lengths_row)
    frequency = ROPE_BASE ** (-2.0 * jnp.arange(HD // 2, dtype=jnp.float32) / HD)
    angle = frequency[:, None] * local.astype(jnp.float32)[None, :]
    cosine = jnp.cos(angle)[None]
    sine = jnp.sin(angle)[None]
    bf16, f32 = jnp.bfloat16, jnp.float32
    parts = ctx_size // HEADS
    part = ctx_index // HEADS
    part_blocks = HEADS * rows_here // BLK
    q_order = lax.dynamic_slice_in_dim(order_row, part * part_blocks, part_blocks)
    q_slot, q_place, q_start = block_tables(q_order, lengths_row)
    q_slot = q_slot + part * part_blocks
    kv_slot, _, _ = block_tables(order_row, lengths_row)
    first = jnp.min(q_start.reshape(-1, TILE), axis=1) // TILE
    last = jnp.max(q_place.reshape(-1, TILE), axis=1) // TILE + 1
    tables = (q_slot, kv_slot, first, last)
    q_rows, kv_rows = part_blocks * BLK, order_row.shape[0] * BLK

    def fetch_attention():
        return (
            lax.all_gather(qkv_weight, "fsdp", axis=0, tiled=True),
            lax.all_gather(out_weight, "fsdp", axis=0, tiled=True),
            lax.all_gather(attn_gain, "fsdp", axis=0, tiled=True),
            lax.all_gather(ffn_gain, "fsdp", axis=0, tiled=True),
            lax.all_gather(query_gain, "fsdp", axis=0, tiled=True),
            lax.all_gather(key_gain, "fsdp", axis=0, tiled=True),
        )

    w_qkv, w_out, gain_attn, gain_ffn, gain_query, gain_key = fetch_attention()
    gain_attn = gain_attn.astype(jnp.float32)
    gain_ffn = gain_ffn.astype(jnp.float32)
    gain_query = gain_query.astype(jnp.float32)
    gain_key = gain_key.astype(jnp.float32)
    scale_one = rms_scale(inputs)
    normed = (inputs * scale_one * gain_attn).astype(jnp.bfloat16)
    projected = lax.dot_general(
        w_qkv, normed, (((0,), (1,)), ((), ())), preferred_element_type=f32
    )
    q_raw = projected[:q_width].reshape(HEADS, HD, rows_here)
    k_raw = projected[q_width : q_width + kv_width].reshape(KV_HEADS, HD, rows_here)
    values_here = projected[q_width + kv_width :].reshape(KV_HEADS, HD, rows_here).astype(bf16)
    q_scale = rms_scale(q_raw, 1)
    k_scale = rms_scale(k_raw, 1)
    column_query, column_key = gain_query[:, None], gain_key[:, None]
    queries = rope(q_raw * q_scale * column_query, cosine, sine).astype(bf16)
    keys_here = rope(k_raw * k_scale * column_key, cosine, sine).astype(bf16)
    sent = jnp.concatenate(
        [queries, jnp.repeat(keys_here, per_group, 0), jnp.repeat(values_here, per_group, 0)], axis=1
    )
    sent = jnp.concatenate([sent] * parts, axis=0)
    got = lax.all_to_all(sent, "ctx", 0, 0, tiled=True)
    q_place, q_start = q_place[None], q_start[None]
    shape = jax.ShapeDtypeStruct
    attn_sent, *held = kernel_call(
        attend_kernel,
        tables,
        (got, q_place, q_start),
        [
            shape((ctx_size, HD, rows_here), bf16),
            shape((q_rows, HD), bf16),
            shape((HD, q_rows), bf16),
            shape((kv_rows, HD), bf16),
            shape((HD, kv_rows), bf16),
            shape((kv_rows, HD), bf16),
            shape((HD, q_rows), f32),
            shape((1, q_rows), f32),
        ],
        [pltpu.VMEM((HD, kv_rows), bf16)],
        ATTEND,
    )
    attn_in = lax.dynamic_slice_in_dim(
        lax.all_to_all(attn_sent, "ctx", 0, 0, tiled=True), part * HEADS, HEADS
    ).reshape(q_width, rows_here)
    h_one = inputs + lax.dot_general(
        attn_in, w_out, (((0,), (0,)), ((), ())), preferred_element_type=f32
    )
    scale_two = rms_scale(h_one)
    normed_two = (h_one * scale_two * gain_ffn).astype(jnp.bfloat16)
    columns = normed_two
    gate_up = jnp.einsum(
        "tr,rgf->tgf",
        columns,
        lax.all_gather(gate_up_weight, "fsdp", axis=0, tiled=True),
        preferred_element_type=jnp.float32,
    )
    gate = gate_up[:, 0]
    upper = gate_up[:, 1]
    sigma = jax.nn.sigmoid(gate)
    hidden = (gate * sigma * upper).astype(jnp.bfloat16)
    columns = hidden
    ffn_out = jnp.dot(
        columns,
        lax.all_gather(down_weight, "fsdp", axis=0, tiled=True),
        preferred_element_type=jnp.float32,
    )
    output = (h_one + ffn_out).astype(jnp.bfloat16)
    d_out = cotangent[0].astype(jnp.float32)
    d_ffn = d_out.astype(jnp.bfloat16)
    d_hidden = lax.dot_general(
        d_ffn,
        lax.all_gather(down_weight, "fsdp", axis=0, tiled=True),
        (((1,), (1,)), ((), ())),
        preferred_element_type=jnp.float32,
    )
    d_gate = d_hidden * upper * sigma * (1.0 + gate * (1.0 - sigma))
    d_upper = d_hidden * gate * sigma
    d_gate_up = jnp.stack([d_gate, d_upper], axis=1).astype(jnp.bfloat16)
    d_normed_two = jnp.einsum(
        "tgf,rgf->tr",
        d_gate_up,
        lax.all_gather(gate_up_weight, "fsdp", axis=0, tiled=True),
        preferred_element_type=jnp.float32,
    )
    columns = normed_two
    grad_gate_up = lax.psum_scatter(
        jnp.einsum("tr,tgf->rgf", columns, d_gate_up, preferred_element_type=jnp.float32).astype(
            jnp.bfloat16
        ),
        "fsdp",
        scatter_dimension=0,
        tiled=True,
    )
    columns = hidden
    grad_down = lax.psum_scatter(
        lax.dot_general(
            columns, d_ffn, (((0,), (0,)), ((), ())), preferred_element_type=jnp.float32
        ).astype(jnp.bfloat16),
        "fsdp",
        scatter_dimension=0,
        tiled=True,
    )
    d_norm_two, ffn_gain_term = norm_back(d_normed_two, h_one, scale_two, gain_ffn)
    d_h_one = d_out + d_norm_two
    d_attn = d_h_one.astype(jnp.bfloat16)
    grad_out_here = jnp.dot(attn_in, d_attn, preferred_element_type=f32)
    d_heads = lax.dot_general(
        w_out, d_attn, (((1,), (1,)), ((), ())), preferred_element_type=f32
    ).astype(bf16)
    d_heads = jnp.concatenate([d_heads.reshape(HEADS, HD, rows_here)] * parts, axis=0)
    d_got = lax.all_to_all(d_heads, "ctx", 0, 0, tiled=True)
    (d_sent,) = kernel_call(
        attend_back_kernel,
        tables,
        (d_got, q_place, q_start, *held),
        [shape((ctx_size, 3 * HD, rows_here), bf16)],
        [
            pltpu.VMEM((HD, q_rows), bf16),
            pltpu.VMEM((q_rows, HD), bf16),
            pltpu.VMEM((kv_rows, HD), f32),
            pltpu.VMEM((kv_rows, HD), f32),
        ],
        ATTEND_BACK,
    )
    d_back = lax.all_to_all(d_sent, "ctx", 0, 0, tiled=True)
    d_query = lax.dynamic_slice_in_dim(d_back[:, :HD], part * HEADS, HEADS).astype(f32)
    d_key_value = jnp.sum(
        d_back[:, HD:].reshape(parts, KV_HEADS, per_group, 2 * HD, rows_here).astype(f32),
        axis=(0, 2),
    )
    dq_normed = rope_back(d_query, cosine, sine)
    dk_normed = rope_back(d_key_value[:, :HD], cosine, sine)
    dq_raw, query_term = norm_back(dq_normed, q_raw, q_scale, column_query, 1)
    dk_raw, key_term = norm_back(dk_normed, k_raw, k_scale, column_key, 1)
    d_projected = jnp.concatenate(
        [
            dq_raw.reshape(q_width, rows_here).astype(bf16),
            dk_raw.reshape(kv_width, rows_here).astype(bf16),
            d_key_value[:, HD:].reshape(kv_width, rows_here).astype(bf16),
        ],
        axis=0,
    )
    grad_qkv_here = lax.dot_general(
        normed, d_projected, (((0,), (1,)), ((), ())), preferred_element_type=f32
    )
    d_normed = lax.dot_general(
        d_projected, w_qkv, (((0,), (1,)), ((), ())), preferred_element_type=f32
    )
    d_norm_one, attn_gain_term = norm_back(d_normed, inputs, scale_one, gain_attn)
    d_inputs = d_h_one + d_norm_one
    shard_qkv, shard_out, shard_attn_gain, shard_ffn_gain, shard_query_gain, shard_key_gain = (
        lax.psum_scatter(
            grad_qkv_here.astype(jnp.bfloat16), "fsdp", scatter_dimension=0, tiled=True
        ).astype(jnp.float32),
        lax.psum_scatter(
            grad_out_here.astype(jnp.bfloat16), "fsdp", scatter_dimension=0, tiled=True
        ).astype(jnp.float32),
        lax.psum_scatter(
            jnp.sum(attn_gain_term, axis=0).astype(jnp.bfloat16),
            "fsdp",
            scatter_dimension=0,
            tiled=True,
        ).astype(jnp.float32),
        lax.psum_scatter(
            jnp.sum(ffn_gain_term, axis=0).astype(jnp.bfloat16),
            "fsdp",
            scatter_dimension=0,
            tiled=True,
        ).astype(jnp.float32),
        lax.psum_scatter(
            jnp.sum(query_term, axis=(0, 2)).astype(jnp.bfloat16),
            "fsdp",
            scatter_dimension=0,
            tiled=True,
        ).astype(jnp.float32),
        lax.psum_scatter(
            jnp.sum(key_term, axis=(0, 2)).astype(jnp.bfloat16),
            "fsdp",
            scatter_dimension=0,
            tiled=True,
        ).astype(jnp.float32),
    )
    summed_grads = (
        lax.psum(shard_qkv.astype(jnp.bfloat16), "ctx").astype(jnp.float32),
        lax.psum(shard_out.astype(jnp.bfloat16), "ctx").astype(jnp.float32),
        lax.psum(grad_gate_up, "ctx").astype(jnp.float32),
        lax.psum(grad_down, "ctx").astype(jnp.float32),
        lax.psum(shard_attn_gain.astype(jnp.bfloat16), "ctx").astype(jnp.float32),
        lax.psum(shard_ffn_gain.astype(jnp.bfloat16), "ctx").astype(jnp.float32),
        lax.psum(shard_query_gain.astype(jnp.bfloat16), "ctx").astype(jnp.float32),
        lax.psum(shard_key_gain.astype(jnp.bfloat16), "ctx").astype(jnp.float32),
    )
    return (
        output[None],
        d_inputs[None],
        summed_grads[0],
        summed_grads[1],
        summed_grads[2],
        summed_grads[3],
        summed_grads[4],
        summed_grads[5],
        summed_grads[6],
        summed_grads[7],
    )


def solution(mesh):
    block = mesh.shape["fsdp"] == 2 and mesh.shape["ctx"] == 16
    return jax.shard_map(
        on_block if block else on_device,
        mesh=mesh,
        in_specs=(
            P("fsdp", "ctx", None),
            P("fsdp", None),
            P("fsdp", None),
            P("fsdp", None, None),
            P("fsdp", None),
            P("fsdp"),
            P("fsdp"),
            P("fsdp"),
            P("fsdp"),
            P("fsdp", None),
            P("fsdp", None),
            P("fsdp", "ctx", None),
        ),
        out_specs=(
            P("fsdp", "ctx", None),
            P("fsdp", "ctx", None),
            P("fsdp", None),
            P("fsdp", None),
            P("fsdp", None, None),
            P("fsdp", None),
            P("fsdp"),
            P("fsdp"),
            P("fsdp"),
            P("fsdp"),
        ),
        check_vma=False,
    )
```

```python
import functools

import jax
import jax.numpy as jnp
from jax import lax
from jax.experimental import pallas as pl
from jax.experimental.pallas import tpu as pltpu
from jax.sharding import PartitionSpec as P

HEADS = 16
KV_HEADS = 8
HD = 64
BLK = 128
TILE = 256
CHUNKS = 2
PROJECT = 0
ATTEND = 0
OUT = 0
FFN = (0, 0)
ATTEND_BACK = 25


EPSILON = 1e-05
ROPE_BASE = 1000000.0
LOG2E = 1.4426950408889634
SCORE_SCALE = LOG2E * HD ** (-0.5)


def rms_scale(values, axis=-1):
    return lax.rsqrt(jnp.mean(values * values, axis=axis, keepdims=True) + EPSILON)


def norm_back(grad_normed, inputs, scale, gain, axis=-1):
    scaled = grad_normed * gain
    grad_in = scale * scaled - inputs * scale * scale * scale * jnp.mean(
        scaled * inputs, axis=axis, keepdims=True
    )
    return (grad_in, grad_normed * inputs * scale)


def rope(values, cosine, sine):
    half = HD // 2
    first, second = values[:, :half], values[:, half:]
    return jnp.concatenate([first * cosine - second * sine, second * cosine + first * sine], axis=1)


def rope_back(values, cosine, sine):
    half = HD // 2
    first, second = values[:, :half], values[:, half:]
    return jnp.concatenate([first * cosine + second * sine, second * cosine - first * sine], axis=1)


def starts_of(packed, lengths_row):
    ends = jnp.cumsum(lengths_row)
    past = packed[:, None] >= ends[None, :]
    return jnp.sum(jnp.where(past, lengths_row[None, :], 0), axis=1)


def block_tables(order, lengths_row):
    count = order.shape[0]
    rank = jnp.sum((order[None, :] < order[:, None]).astype(jnp.int32), axis=1)
    hit = rank[None, :] == jnp.arange(count, dtype=jnp.int32)[:, None]
    slot = jnp.sum(jnp.where(hit, jnp.arange(count, dtype=jnp.int32)[None, :], 0), axis=1)
    block = jnp.sum(jnp.where(hit, order[None, :], 0), axis=1)
    place = (block[:, None] * BLK + jnp.arange(BLK, dtype=jnp.int32)[None, :]).reshape(-1)
    return (slot, place, starts_of(place, lengths_row))


def attend_kernel(
    q_slot, kv_slot, first, last, qkv_ref, place_ref, start_ref,
    out_ref, q_ref, qt_ref, k_ref, kt_ref, v_ref, ot_ref, total_ref, vt_ref
):
    per_device = qkv_ref.shape[2] // BLK
    kv_blocks = k_ref.shape[0] // BLK
    q_blocks = q_ref.shape[0] // BLK

    def piece(slot, lower):
        return qkv_ref[
            slot // per_device,
            lower : lower + HD,
            pl.ds(pl.multiple_of((slot % per_device) * BLK, BLK), BLK),
        ]

    for i in range(kv_blocks):
        here = slice(i * BLK, (i + 1) * BLK)
        keys = piece(kv_slot[i], HD)
        kt_ref[:, here] = keys
        k_ref[here, :] = keys.T
        values = piece(kv_slot[i], 2 * HD)
        vt_ref[:, here] = values
        v_ref[here, :] = values.T
    for i in range(q_blocks):
        here = slice(i * BLK, (i + 1) * BLK)
        queries = piece(q_slot[i], 0)
        qt_ref[:, here] = queries
        q_ref[here, :] = queries.T
    if q_blocks < kv_blocks:
        out_ref[...] = jnp.zeros_like(out_ref)

    def tile(i, carry):
        rows = pl.ds(pl.multiple_of(i * TILE, TILE), TILE)
        queries = qt_ref[:, rows]
        place = place_ref[:, rows]
        start = start_ref[:, rows]

        def step(j, state):
            total, summed = state
            at = pl.multiple_of(j * TILE, TILE)
            scores = jnp.dot(
                k_ref[pl.ds(at, TILE), :], queries, preferred_element_type=jnp.float32
            )
            key_place = lax.broadcasted_iota(jnp.int32, (TILE, TILE), 0) + at
            allowed = (key_place <= place) & (key_place >= start)
            lifted = jnp.where(allowed, jnp.exp2(scores * SCORE_SCALE), 0.0)
            total = total + jnp.sum(lifted, axis=0, keepdims=True)
            summed = summed + jnp.dot(
                vt_ref[:, pl.ds(at, TILE)],
                lifted.astype(jnp.bfloat16),
                preferred_element_type=jnp.float32,
            )
            return (total, summed)

        total, summed = lax.fori_loop(
            first[i],
            last[i],
            step,
            (jnp.zeros((1, TILE), jnp.float32), jnp.zeros((HD, TILE), jnp.float32)),
        )
        attn = summed / total
        ot_ref[:, rows] = attn
        total_ref[:, rows] = jnp.log(total) * LOG2E
        rounded = attn.astype(jnp.bfloat16)
        for part in range(TILE // BLK):
            slot = q_slot[i * (TILE // BLK) + part]
            out_ref[
                slot // per_device,
                :,
                pl.ds(pl.multiple_of((slot % per_device) * BLK, BLK), BLK),
            ] = rounded[:, part * BLK : (part + 1) * BLK]
        return carry

    lax.fori_loop(0, q_blocks * BLK // TILE, tile, 0)


def attend_back_kernel(
    q_slot, kv_slot, first, last, d_ref, place_ref, start_ref,
    q_ref, qt_ref, k_ref, kt_ref, v_ref, ot_ref, total_ref,
    out_ref, dt_ref, do_ref, dk_ref, dv_ref
):
    per_device = d_ref.shape[2] // BLK
    kv_blocks = k_ref.shape[0] // BLK
    q_blocks = q_ref.shape[0] // BLK

    def lanes(slot):
        return pl.ds(pl.multiple_of((slot % per_device) * BLK, BLK), BLK)

    for i in range(q_blocks):
        here = slice(i * BLK, (i + 1) * BLK)
        slot = q_slot[i]
        grads = d_ref[slot // per_device, :, lanes(slot)]
        dt_ref[:, here] = grads
        do_ref[here, :] = grads.T
    dk_ref[...] = jnp.zeros_like(dk_ref)
    dv_ref[...] = jnp.zeros_like(dv_ref)
    if q_blocks < kv_blocks:
        out_ref[...] = jnp.zeros_like(out_ref)

    def tile(i, carry):
        rows = pl.ds(pl.multiple_of(i * TILE, TILE), TILE)
        queries = qt_ref[:, rows]
        grads = dt_ref[:, rows]
        place = place_ref[:, rows]
        start = start_ref[:, rows]
        delta = jnp.sum(grads.astype(jnp.float32) * ot_ref[:, rows], axis=0, keepdims=True)
        total = total_ref[:, rows]

        def step(j, d_query):
            at = pl.multiple_of(j * TILE, TILE)
            here = pl.ds(at, TILE)
            scores = jnp.dot(k_ref[here, :], queries, preferred_element_type=jnp.float32)
            key_place = lax.broadcasted_iota(jnp.int32, (TILE, TILE), 0) + at
            allowed = (key_place <= place) & (key_place >= start)
            shares = jnp.where(allowed, jnp.exp2(scores * SCORE_SCALE - total), 0.0)
            d_shares = jnp.dot(v_ref[here, :], grads, preferred_element_type=jnp.float32)
            d_scores = (shares * (d_shares - delta)).astype(jnp.bfloat16)
            dv_ref[here, :] += jnp.dot(
                shares.astype(jnp.bfloat16), do_ref[rows, :], preferred_element_type=jnp.float32
            )
            dk_ref[here, :] += jnp.dot(
                d_scores, q_ref[rows, :], preferred_element_type=jnp.float32
            )
            return d_query + jnp.dot(
                kt_ref[:, here], d_scores, preferred_element_type=jnp.float32
            )

        d_query = lax.fori_loop(first[i], last[i], step, jnp.zeros((HD, TILE), jnp.float32))
        rounded = (d_query * HD ** (-0.5)).astype(jnp.bfloat16)
        for part in range(TILE // BLK):
            slot = q_slot[i * (TILE // BLK) + part]
            out_ref[slot // per_device, 0:HD, lanes(slot)] = rounded[
                :, part * BLK : (part + 1) * BLK
            ]
        return carry

    lax.fori_loop(0, q_blocks * BLK // TILE, tile, 0)
    for i in range(kv_blocks):
        here = slice(i * BLK, (i + 1) * BLK)
        slot = kv_slot[i]
        out_ref[slot // per_device, HD : 2 * HD, lanes(slot)] = (
            (dk_ref[here, :] * HD ** (-0.5)).T.astype(jnp.bfloat16)
        )
        out_ref[slot // per_device, 2 * HD : 3 * HD, lanes(slot)] = (
            dv_ref[here, :].T.astype(jnp.bfloat16)
        )


def cost(micros):
    return pl.CostEstimate(
        flops=1 + micros * 1_000_000_000, bytes_accessed=1, transcendentals=0
    )


def kernel_call(kernel, tables, arrays, outs, scratch, micros):
    smem = pl.BlockSpec(memory_space=pltpu.SMEM)
    vmem = pl.BlockSpec(memory_space=pltpu.VMEM)
    return pl.pallas_call(
        kernel,
        out_shape=outs,
        in_specs=[smem] * len(tables) + [vmem] * len(arrays),
        out_specs=[vmem] * len(outs),
        scratch_shapes=scratch,
        compiler_params=pltpu.CompilerParams(vmem_limit_bytes=48 * 1024 * 1024),
        cost_estimate=cost(micros),
    )(*tables, *arrays)


class Links:
    def __init__(self, ctx_size):
        self.depth = ctx_size // 4
        index = lax.axis_index("ctx")
        self.core = index % 2
        self.y = (index // 2) % 2
        self.side = lax.axis_index("fsdp")
        self.half = index // 4 % 2
        self.quarter = index % 2 * 2 + self.y
        self.here = jnp.stack([self.half, self.core, self.y, self.side]).astype(jnp.int32)

    def route(self, place):
        pairs = []
        for z in range(self.depth):
            for y in range(2):
                for core in range(2):
                    to_z, to_y, to_core = place(z, y, core)
                    pairs.append(((z * 2 + y) * 2 + core, (to_z * 2 + to_y) * 2 + to_core))
        return pairs

    def over_core(self, value):
        return lax.ppermute(value, "ctx", self.route(lambda z, y, c: (z, y, 1 - c)))

    def over_y(self, value):
        return lax.ppermute(value, "ctx", self.route(lambda z, y, c: (z, 1 - y, c)))

    def over_z(self, value):
        return lax.ppermute(value, "ctx", self.route(lambda z, y, c: (z ^ 1, y, c)))

    def over_two_z(self, value):
        return lax.ppermute(value, "ctx", self.route(lambda z, y, c: (z ^ 2, y, c)))

    def over_x(self, value):
        return lax.ppermute(value, "fsdp", [(0, 1), (1, 0)])

    def spread_plane(self, value):
        across = self.over_core(value)
        beside = self.over_y(value)
        return (value, across, beside, self.over_core(beside))

    def deal_plane(self, near, far, give, give_far):
        got, got_far = self.over_core(give), self.over_core(give_far)
        return (near, got, self.over_y(far), self.over_y(got_far))

    def sum_depth(self, kept, got, time=None):
        def half(index):
            return add(pick(kept, index, 0), pick(got, index, 0))

        given = self.over_z(half(1 - self.half))
        part = add(half(self.half), given)
        full = add(part, self.over_two_z(part))
        other = self.over_z(full)
        return jnp.stack([full, other if time is None else after(other, time)])


def pick(value, index, axis):
    return lax.dynamic_index_in_dim(value, index, axis, keepdims=False)


def add(left, right):
    return (left.astype(jnp.float32) + right.astype(jnp.float32)).astype(jnp.bfloat16)


def after(value, *others):
    return lax.optimization_barrier((value, *others))[0]


def contract(left, right, axes):
    return lax.dot_general(
        left, right, ((axes[:1], axes[1:]), ((), ())), preferred_element_type=jnp.float32
    )


PARAMS = pltpu.CompilerParams(vmem_limit_bytes=56 * 1024 * 1024)


def call_with_here(
    kernel, here, grid, arrays, specs, outs, out_specs, scratch=(), aliases=None, micros=5
):
    return pl.pallas_call(
        kernel,
        grid_spec=pltpu.PrefetchScalarGridSpec(
            num_scalar_prefetch=1,
            grid=grid,
            in_specs=specs,
            out_specs=out_specs,
            scratch_shapes=list(scratch),
        ),
        out_shape=outs,
        input_output_aliases=aliases or {},
        compiler_params=PARAMS,
        cost_estimate=cost(micros),
    )(here, *arrays)


def whole(array):
    rank = len(array.shape)
    return pl.BlockSpec(array.shape, lambda i, here: (0,) * rank)


def project_kernel(here, *refs):
    x_ref, gain_ref, own_ref = refs[:3]
    pieces, q_gain, k_gain, cos_ref, sin_ref = refs[3:7], refs[7], refs[8], refs[9], refs[10]
    sent, weight, q_ref, k_ref, q_scale, k_scale, normed_ref, scale_ref = refs[11:]
    core, y, side = here[1], here[2], here[3]
    rows = own_ref.shape[0]
    part = rows // 4
    f32, bf16 = jnp.float32, jnp.bfloat16
    weight[pl.ds(pl.multiple_of(side * rows, rows), rows), :] = own_ref[...]
    for p in range(4):
        at = (1 - side) * rows + (((p % 2) ^ core) * 2 + ((p // 2) ^ y)) * part
        weight[pl.ds(pl.multiple_of(at, part), part), :] = pieces[p][...]
    x = x_ref[...].astype(f32)
    scale = rms_scale(x)
    scale_ref[...] = scale
    normed = (x * scale * gain_ref[...]).astype(bf16)
    normed_ref[...] = normed.T
    cosine, sine = cos_ref[...], sin_ref[...]
    half = HD // 2

    def turned(raw, gain, raw_ref, kept_scale, head):
        raw_ref[head * HD : (head + 1) * HD, :] = raw
        scale = rms_scale(raw, 0)
        kept_scale[head : head + 1, :] = scale
        value = raw * scale * gain
        first, second = value[:half], value[half:]
        return jnp.concatenate(
            [first * cosine - second * sine, second * cosine + first * sine], axis=0
        ).astype(bf16)

    per_group = HEADS // KV_HEADS
    for at in range(0, weight.shape[1], 2 * BLK):
        block = jnp.dot(normed, weight[:, at : at + 2 * BLK], preferred_element_type=f32)
        turned_block = block.T
        for n in range(2 * BLK // HD):
            head = at // HD + n
            raw = turned_block[n * HD : (n + 1) * HD, :]
            if head < HEADS:
                sent[head, 0:HD, :] = turned(raw, q_gain[...], q_ref, q_scale, head)
                continue
            head -= HEADS
            if head < KV_HEADS:
                value, row = turned(raw, k_gain[...], k_ref, k_scale, head), HD
            else:
                value, row, head = raw.astype(bf16), 2 * HD, head - KV_HEADS
            for copy in range(per_group):
                sent[head * per_group + copy, row : row + HD, :] = value


def project(here, x, gain, own, pieces, q_gain, k_gain, cosine, sine):
    tokens, width = x.shape
    f32, bf16 = jnp.float32, jnp.bfloat16
    shape = jax.ShapeDtypeStruct
    arrays = [x, gain, own, *pieces, q_gain, k_gain, cosine, sine]
    outs = [
        shape((HEADS, 3 * HD, tokens), bf16),
        shape((width, own.shape[1]), bf16),
        shape((HEADS * HD, tokens), f32),
        shape((KV_HEADS * HD, tokens), f32),
        shape((HEADS, tokens), f32),
        shape((KV_HEADS, tokens), f32),
        shape((width, tokens), bf16),
        shape((tokens, 1), f32),
    ]
    return call_with_here(
        project_kernel, here, (1,), arrays, [whole(a) for a in arrays], outs,
        [whole(o) for o in outs], micros=PROJECT,
    )


def layer(array, index):
    return pl.BlockSpec((1, *array.shape[1:]), lambda i, here: (index, 0, 0))


def attend_out_kernel(here, *refs):
    attn_ref, x_ref, gain_ref, own_ref = refs[:4]
    pieces = refs[4:12]
    weight, h_ref, scale_ref, two_ref, two_t_ref = refs[12:]
    core, y, side = here[1], here[2], here[3]
    rows = own_ref.shape[0]
    part = rows // 4
    weight[pl.ds(pl.multiple_of(side * rows, rows), rows), :] = own_ref[...]
    for p in range(4):
        at = (1 - side) * rows + (((p % 2) ^ core) * 2 + ((p // 2) ^ y)) * part
        for n in range(2):
            piece = pieces[2 * p + n]
            wide = piece.shape[1]
            weight[pl.ds(pl.multiple_of(at, part), part), n * wide : (n + 1) * wide] = piece[...]
    attn = attn_ref[...].T
    h_one = x_ref[...].astype(jnp.float32) + jnp.dot(
        attn, weight[...], preferred_element_type=jnp.float32
    )
    scale = rms_scale(h_one)
    h_ref[...] = h_one
    scale_ref[...] = scale
    two = (h_one * scale * gain_ref[...]).astype(jnp.bfloat16)
    two_ref[...] = two
    two_t_ref[...] = two.T


def attend_out(here, attn, x, gain, own, pieces):
    tokens, width = x.shape
    f32, bf16 = jnp.float32, jnp.bfloat16
    shape = jax.ShapeDtypeStruct
    part = own.shape[0] // 4
    half = width // 2
    first = pieces[0].shape[1] // half - 2
    arrays = [attn, x, gain, own]
    specs = [whole(a) for a in arrays]
    for piece in pieces:
        for n in range(2):
            arrays.append(piece)
            specs.append(pl.BlockSpec((part, half), lambda i, here, n=n: (0, first + n)))
    outs = [
        shape((width, width), bf16),
        shape((tokens, width), f32),
        shape((tokens, 1), f32),
        shape((tokens, width), bf16),
        shape((width, tokens), bf16),
    ]
    return call_with_here(
        attend_out_kernel, here, (1,), arrays, specs, outs, [whole(o) for o in outs], micros=OUT
    )


def ffn_kernel(chunk, here, *refs):
    two_ref, d_ref, own_ref = refs[:3]
    pieces, down_ref, down_pieces = refs[3:7], refs[7], refs[8:12]
    if chunk == 0:
        before_refs, refs = refs[12:13], refs[13:]
        near, far, give, give_far, out_ref, d_two_ref = refs[:6]
        refs = refs[6:]
    else:
        before_refs, gain_ref, refs = refs[12:17], refs[17], refs[18:]
        near, far, give, give_far = refs[:4]
        out_ref, d_h_ref, d_attn_ref, heads_ref, gain_term_ref = refs[4:9]
        refs = refs[9:]
    weight, down, hidden_rows, out_sum, two_sum = refs[:5]
    held, weight_sem, down_sem, before_sem = refs[5:-3], refs[-3], refs[-2], refs[-1]
    core, y, side = here[1], here[2], here[3]
    f32, bf16 = jnp.float32, jnp.bfloat16
    own_rows, columns = own_ref.shape[1], own_ref.shape[2] // CHUNKS
    part = own_rows // 4
    tile = columns // FFN_TILES
    half = columns // 2

    def quarter(p):
        return ((p % 2) ^ core) * 2 + ((p // 2) ^ y)

    def copies(n):
        at = slice(n * tile, (n + 1) * tile)
        mine = pl.ds(pl.multiple_of(side * own_rows, own_rows), own_rows)
        found = [
            pltpu.make_async_copy(
                own_ref.at[:, :, chunk * columns + n * tile : chunk * columns + (n + 1) * tile],
                weight.at[:, mine, at],
                weight_sem.at[n, 0],
            )
        ]
        for p in range(4):
            rows = pl.ds(pl.multiple_of((1 - side) * own_rows + quarter(p) * part, part), part)
            for kind in range(2):
                begin = kind * columns + n * tile
                found.append(
                    pltpu.make_async_copy(
                        pieces[p].at[:, begin : begin + tile],
                        weight.at[kind, rows, at],
                        weight_sem.at[n, 1 + 2 * p + kind],
                    )
                )
        return found

    def own_down(n):
        at = slice(n * tile, (n + 1) * tile)
        return [pltpu.make_async_copy(down_ref.at[at, :], down.at[at, :], down_sem.at[n, 0])]

    def other_down(n):
        at = slice(n * tile, (n + 1) * tile)
        found = []
        for p in range(4):
            wide = down_pieces[p].shape[1]
            lanes = pl.ds(pl.multiple_of(quarter(p) * wide, wide), wide)
            found.append(
                pltpu.make_async_copy(
                    down_pieces[p].at[at, :], down.at[at, lanes], down_sem.at[n, p]
                )
            )
        return found

    def each(action, n):
        for copy in copies(n):
            action(copy)

        @pl.when(side == chunk)
        def _():
            for copy in own_down(n):
                action(copy)

        @pl.when(side != chunk)
        def _():
            for copy in other_down(n):
                action(copy)

    before = [
        pltpu.make_async_copy(ref, held[n], before_sem.at[n]) for n, ref in enumerate(before_refs)
    ]
    for n in range(FFN_TILES):
        each(lambda copy: copy.start(), n)
    for copy in before:
        copy.start()
    two = two_ref[...]
    d_ffn = d_ref[...]
    for n in range(FFN_TILES):
        each(lambda copy: copy.wait(), n)
        at = slice(n * tile, (n + 1) * tile)
        gate = jnp.dot(two, weight[0, :, at], preferred_element_type=f32)
        upper = jnp.dot(two, weight[1, :, at], preferred_element_type=f32)
        d_hidden = contract(d_ffn, down[at, :], (1, 1))
        sigma = jax.nn.sigmoid(gate)
        silu = gate * sigma
        hidden = (silu * upper).astype(bf16)
        d_gate = (d_hidden * upper * sigma * (1.0 + gate * (1.0 - sigma))).astype(bf16)
        d_upper = (d_hidden * silu).astype(bf16)
        out_term = jnp.dot(hidden, down[at, :], preferred_element_type=f32)
        two_term = contract(d_gate, weight[0, :, at], (1, 1)) + contract(
            d_upper, weight[1, :, at], (1, 1)
        )
        out_sum[...] = out_term if n == 0 else out_sum[...] + out_term
        two_sum[...] = two_term if n == 0 else two_sum[...] + two_term
        hidden_rows[:, at] = hidden
        mine = jnp.where(core == 0, d_gate, d_upper)
        other = jnp.where(core == 0, d_upper, d_gate)
        for column in range(2):
            begin, end = max(n * tile, column * half), min((n + 1) * tile, (column + 1) * half)
            if begin >= end:
                continue
            source = slice(begin - n * tile, end - n * tile)
            target = slice(begin - column * half, end - column * half)
            first, second = mine[:, source], other[:, source]

            @pl.when(y == column)
            def _(first=first, second=second, target=target):
                near[:, target] = first
                give[:, target] = second

            @pl.when(y != column)
            def _(first=first, second=second, target=target):
                far[:, target] = first
                give_far[:, target] = second

    share = half // 2
    target = slice(half, half + share)
    for owner in range(2):
        lower = hidden_rows[:, owner * half : owner * half + share]
        upper = hidden_rows[:, owner * half + share : (owner + 1) * half]
        close = jnp.where(y == 0, lower, upper)
        distant = jnp.where(y == 0, upper, lower)

        @pl.when(core == owner)
        def _(close=close, distant=distant):
            near[:, target] = close
            far[:, target] = distant

        @pl.when(core != owner)
        def _(close=close, distant=distant):
            give[:, target] = close
            give_far[:, target] = distant

    for copy in before:
        copy.wait()
    if chunk == 0:
        out_ref[...] = held[0][...] + out_sum[...]
        d_two_ref[...] = two_sum[...]
    else:
        out_before, two_before, h_one, scale, w_out = held
        out_ref[...] = (out_before[...] + out_sum[...]).astype(bf16)
        d_norm, gain_term = norm_back(
            two_before[...] + two_sum[...], h_one[...], scale[...], gain_ref[...]
        )
        gain_term_ref[...] = jnp.sum(gain_term, axis=0, keepdims=True)
        d_h_one = d_ffn.astype(f32) + d_norm
        d_h_ref[...] = d_h_one
        d_attn = d_h_one.astype(bf16)
        d_attn_ref[...] = d_attn
        heads_ref[...] = contract(w_out[...], d_attn, (1, 1)).astype(bf16)


FFN_TILES = 3


def ffn(here, chunk, two, d_ffn, own, pieces, down, down_pieces, before, gain=None):
    tokens, width = two.shape
    columns = own.shape[2] // CHUNKS
    padded = (columns // 2 + columns // 4 + BLK - 1) // BLK * BLK
    shape = jax.ShapeDtypeStruct
    f32, bf16 = jnp.float32, jnp.bfloat16
    outs = [shape((tokens, padded), bf16)] * 4
    if chunk == 0:
        outs += [shape((tokens, width), f32)] * 2
    else:
        outs += [
            shape((tokens, width), bf16),
            shape((tokens, width), f32),
            shape((tokens, width), bf16),
            shape((width, tokens), bf16),
            shape((1, width), f32),
        ]
    far_away = pl.BlockSpec(memory_space=pl.ANY)
    arrays = [two, d_ffn, own, *pieces, down, *down_pieces, *before]
    specs = [whole(two), whole(d_ffn)] + [far_away] * (len(arrays) - 2)
    if gain is not None:
        arrays.append(gain)
        specs.append(whole(gain))
    got = call_with_here(
        functools.partial(ffn_kernel, chunk),
        here,
        (1,),
        arrays,
        specs,
        outs,
        [whole(o) for o in outs],
        [
            pltpu.VMEM((2, width, columns), bf16),
            pltpu.VMEM((columns, width), bf16),
            pltpu.VMEM((tokens, columns), bf16),
            pltpu.VMEM((tokens, width), f32),
            pltpu.VMEM((tokens, width), f32),
        ]
        + [pltpu.VMEM(v.shape, v.dtype) for v in before]
        + [
            pltpu.SemaphoreType.DMA((FFN_TILES, 9)),
            pltpu.SemaphoreType.DMA((FFN_TILES, 4)),
            pltpu.SemaphoreType.DMA((len(before),)),
        ],
        micros=FFN[chunk],
    )
    return got[:4], got[4:]


def wide_product_kernel(here, *refs):
    planes, terms = refs[:4], refs[4:8]
    sent, kept, left, right = refs[8:]
    tokens = planes[0].shape[1]
    columns = right.shape[1]
    for i in range(4):
        left[:, i * tokens : (i + 1) * tokens] = planes[i][...]
        right[i * tokens : (i + 1) * tokens, :] = terms[i][:, :columns]
    side = here[3]
    _, step, _ = kept.shape
    for half in range(2):
        for owner, out_ref in ((1 - side, sent), (side, kept)):
            place = pl.multiple_of(owner * 2 * step + half * step, step)
            out_ref[half] = jnp.dot(
                left[pl.ds(place, step), :], right[...], preferred_element_type=jnp.float32
            ).astype(out_ref.dtype)


def wide_products(here, two_plane, shares, columns):
    rows, tokens = two_plane[0].shape
    outs = [
        jax.ShapeDtypeStruct((2, rows // 4, columns), jnp.bfloat16),
        jax.ShapeDtypeStruct((2, rows // 4, columns), jnp.float32),
    ]
    arrays = [*two_plane, *shares]
    return call_with_here(
        wide_product_kernel,
        here,
        (1,),
        arrays,
        [whole(a) for a in two_plane]
        + [pl.BlockSpec((tokens, columns), lambda i, here: (0, 0))] * 4,
        outs,
        [whole(o) for o in outs],
        [
            pltpu.VMEM((rows, 4 * tokens), jnp.bfloat16),
            pltpu.VMEM((4 * tokens, columns), jnp.bfloat16),
        ],
        micros=3,
    )


def down_product_kernel(here, *refs):
    planes, terms = refs[:4], (refs[4:8], refs[8:12])
    sent, kept, left, right = refs[12:]
    tokens = planes[0].shape[0]
    rows = left.shape[0]
    for i in range(4):
        right[i * tokens : (i + 1) * tokens, :] = planes[i][...]
    for chunk in range(2):
        for i in range(4):
            share = terms[chunk][i]
            at = share.shape[1] // BLK * BLK - (rows + BLK - 1) // BLK * BLK
            left[:, i * tokens : (i + 1) * tokens] = share[:, at : at + rows].T
        for half in range(2):
            product = jnp.dot(
                left[half * rows // 2 : (half + 1) * rows // 2, :],
                right[...],
                preferred_element_type=jnp.float32,
            )

            @pl.when(here[3] == chunk)
            def _(product=product, half=half):
                kept[half] = product

            @pl.when(here[3] != chunk)
            def _(product=product, half=half):
                sent[half] = product.astype(sent.dtype)


def down_products(here, d_plane, first, second, rows):
    tokens, columns = d_plane[0].shape
    outs = [
        jax.ShapeDtypeStruct((2, rows // 2, columns), jnp.bfloat16),
        jax.ShapeDtypeStruct((2, rows // 2, columns), jnp.float32),
    ]
    return call_with_here(
        down_product_kernel,
        here,
        (1,),
        [*d_plane, *first, *second],
        [whole(a) for a in (*d_plane, *first, *second)],
        outs,
        [whole(o) for o in outs],
        [
            pltpu.VMEM((rows, 4 * tokens), jnp.bfloat16),
            pltpu.VMEM((4 * tokens, columns), jnp.bfloat16),
        ],
        micros=3,
    )


GAIN_ROWS = 16


def attention_back_kernel(here, *refs):
    d_ref, q_ref, k_ref, q_scale, k_scale, q_gain, k_gain, cos_ref, sin_ref = refs[:9]
    weight, x_ref, scale_ref, gain_ref, d_h_ref, d_attn_ref = refs[9:15]
    near, far, give, give_far, d_x_ref, gains_ref = refs[15:21]
    turned, natural = refs[21:]
    f32, bf16 = jnp.float32, jnp.bfloat16
    core, y = here[1], here[2]
    cosine, sine = cos_ref[...], sin_ref[...]
    half = HD // 2
    per_group = HEADS // KV_HEADS
    tokens = x_ref.shape[0]

    def back(grad, raw, scale, gain):
        first, second = grad[:half], grad[half:]
        normed = jnp.concatenate(
            [first * cosine + second * sine, second * cosine - first * sine], axis=0
        )
        return norm_back(normed, raw, scale, gain, 0)

    q_term = jnp.zeros((HD, tokens), f32)
    k_term = jnp.zeros((HD, tokens), f32)
    for head in range(HEADS):
        at = slice(head * HD, (head + 1) * HD)
        grad, term = back(
            d_ref[head, :HD, :].astype(f32), q_ref[at, :], q_scale[head : head + 1, :], q_gain[...]
        )
        turned[at, :] = grad.astype(bf16)
        q_term = q_term + term
    for head in range(KV_HEADS):
        at = slice(head * HD, (head + 1) * HD)
        both = d_ref[head * per_group, HD:, :].astype(f32)
        for other in range(1, per_group):
            both = both + d_ref[head * per_group + other, HD:, :].astype(f32)
        grad, term = back(both[:HD], k_ref[at, :], k_scale[head : head + 1, :], k_gain[...])
        place = HEADS * HD + head * HD
        turned[place : place + HD, :] = grad.astype(bf16)
        k_term = k_term + term
        place += KV_HEADS * HD
        turned[place : place + HD, :] = both[HD:].astype(bf16)
    rows = turned.shape[0] // 4
    columns = d_attn_ref.shape[1] // 4
    shares = ((near, core, y), (far, core, 1 - y), (give, 1 - core, y), (give_far, 1 - core, 1 - y))
    for out_ref, to_core, to_y in shares:
        share = to_core * 2 + to_y
        out_ref[:rows, :] = turned[pl.ds(pl.multiple_of(share * rows, rows), rows), :]
        out_ref[rows:, :] = d_attn_ref[:, pl.ds(pl.multiple_of(share * columns, columns), columns)]
    for at in range(0, turned.shape[0], 256):
        natural[:, at : at + 256] = turned[at : at + 256, :].T
    d_normed = contract(natural[...], weight[...], (1, 1))
    x = x_ref[...].astype(f32)
    d_norm, gain_term = norm_back(d_normed, x, scale_ref[...], gain_ref[...])
    d_x_ref[...] = d_h_ref[...] + d_norm
    gains_ref[...] = jnp.zeros_like(gains_ref)
    gains_ref[0:1, :] = jnp.sum(gain_term, axis=0, keepdims=True)
    gains_ref[1:2, 0:HD] = jnp.sum(q_term.T, axis=0, keepdims=True)
    gains_ref[2:3, 0:HD] = jnp.sum(k_term.T, axis=0, keepdims=True)


def attention_back(here, arrays):
    f32, bf16 = jnp.float32, jnp.bfloat16
    shape = jax.ShapeDtypeStruct
    weight, x = arrays[9], arrays[10]
    tokens, width = x.shape
    rows = weight.shape[1] // 4 + tokens
    assert width // 4 == tokens
    outs = [
        *[shape((rows, tokens), bf16)] * 4,
        shape((tokens, width), f32),
        shape((8, width), f32),
    ]
    return call_with_here(
        attention_back_kernel, here, (1,), arrays, [whole(a) for a in arrays], outs,
        [whole(o) for o in outs],
        [pltpu.VMEM((weight.shape[1], tokens), bf16), pltpu.VMEM((tokens, weight.shape[1]), bf16)],
        micros=12,
    )


def attention_product_kernel(here, *refs):
    planes, terms, gains_ref, ffn_gain_ref = refs[:4], refs[4:8], refs[8], refs[9]
    sent, kept, left, right, left_out, right_out = refs[10:]
    tokens = planes[0].shape[2]
    cut = right.shape[1]
    for i in range(4):
        at = slice(i * tokens, (i + 1) * tokens)
        left[:, at] = planes[i][0]
        left_out[:, at] = planes[i][1]
        share = terms[i]
        right[at, :] = share[:cut].T
        right_out[at, :] = share[cut:]
    step = left.shape[0] // 4
    for owner, out_ref in ((1 - here[3], sent), (here[3], kept)):
        for half in range(2):
            at = pl.ds(pl.multiple_of(owner * 2 * step + half * step, step), step)
            out_ref[half, :step, :cut] = jnp.dot(
                left[at, :], right[...], preferred_element_type=jnp.float32
            ).astype(out_ref.dtype)
            out_ref[half, :step, cut:] = jnp.dot(
                left_out[at, :], right_out[...], preferred_element_type=jnp.float32
            ).astype(out_ref.dtype)
        rows = gains_ref.shape[1] // 2
        mine = pl.ds(pl.multiple_of(owner * rows, rows), rows)
        wide = out_ref.shape[2] - rows
        block = jnp.concatenate(
            [
                jnp.concatenate([gains_ref[0:1, mine], gains_ref[1:2, 0:wide]], axis=1),
                jnp.concatenate([ffn_gain_ref[:, mine], gains_ref[2:3, 0:wide]], axis=1),
                jnp.zeros((GAIN_ROWS - 2, out_ref.shape[2]), jnp.float32),
            ],
            axis=0,
        )
        out_ref[0, step:, :] = block.astype(out_ref.dtype)
        out_ref[1, step:, :] = jnp.zeros((GAIN_ROWS, out_ref.shape[2]), out_ref.dtype)


def attention_products(here, pair_plane, shares, gains, ffn_gain):
    _, width, tokens = pair_plane[0].shape
    cut = shares[0].shape[0] - tokens
    shape = (2, width // 4 + GAIN_ROWS, cut + tokens)
    outs = [jax.ShapeDtypeStruct(shape, jnp.bfloat16), jax.ShapeDtypeStruct(shape, jnp.float32)]
    return call_with_here(
        attention_product_kernel,
        here,
        (1,),
        [*pair_plane, *shares, gains, ffn_gain],
        [whole(a) for a in (*pair_plane, *shares, gains, ffn_gain)],
        outs,
        [whole(o) for o in outs],
        [
            pltpu.VMEM((width, 4 * tokens), jnp.bfloat16),
            pltpu.VMEM((4 * tokens, cut), jnp.bfloat16),
            pltpu.VMEM((width, 4 * tokens), jnp.bfloat16),
            pltpu.VMEM((4 * tokens, tokens), jnp.bfloat16),
        ],
        micros=3,
    )


def place_gate_up_kernel(here, *refs):
    mine, across, beside, diagonal, out_ref = *refs[:4], refs[-1]
    pieces = (mine, across, beside, diagonal)
    wide = mine.shape[2]
    for case in range(4):
        core, y = case // 2, case % 2

        @pl.when((here[1] == core) & (here[2] == y))
        def _(core=core, y=y):
            for kind in range(2):
                for column in range(2):
                    value = pieces[(y ^ column) * 2 + (core ^ kind)][0]
                    out_ref[:, kind, column * wide : (column + 1) * wide] = value.astype(
                        jnp.float32
                    )


def place_gate_up(here, chunk, pieces, before):
    _, rows, wide = pieces[0].shape
    step = 64
    blocks = rows // step

    def source(i, here):
        return ((i // blocks) ^ here[0], i % blocks, 0)

    arrays = list(pieces)
    specs = [pl.BlockSpec((1, step, wide), source)] * 4
    aliases = {}
    if before is not None:
        arrays.append(before)
        specs.append(pl.BlockSpec(memory_space=pl.ANY))
        aliases = {5: 0}
    (out,) = call_with_here(
        place_gate_up_kernel,
        here,
        (2 * blocks,),
        arrays,
        specs,
        [jax.ShapeDtypeStruct((2 * rows, 2, 2 * wide * CHUNKS), jnp.float32)],
        [pl.BlockSpec((step, 2, 2 * wide), lambda i, here: (i, 0, chunk))],
        aliases=aliases,
        micros=10,
    )
    return out


def place_down(here, pieces):
    _, rows, columns = pieces[0].shape

    def kernel(here, *refs):
        for s in range(8):

            @pl.when(pl.program_id(0) == s)
            def _(s=s):
                refs[4][...] = refs[s % 4][s // 4].astype(jnp.float32)

    def target(s, here):
        half = (s // 4) ^ here[0]
        y = ((s // 2) % 2) ^ here[2]
        core = (s % 2) ^ here[1]
        return ((core * 2 + y) * 2 + half, 0)

    (out,) = call_with_here(
        kernel,
        here,
        (8,),
        list(pieces),
        [whole(v) for v in pieces],
        [jax.ShapeDtypeStruct((rows * 8, columns), jnp.float32)],
        [pl.BlockSpec((rows, columns), target)],
    )
    return out


def place_attention(here, pieces, cut):
    _, rows, columns = pieces[0].shape
    rows -= GAIN_ROWS

    def kernel(here, *refs):
        qkv_ref, out_ref, gains_ref = refs[4:]
        for s in range(8):

            @pl.when(pl.program_id(0) == s)
            def _(s=s):
                value = refs[s % 4][s // 4]
                qkv_ref[...] = value[:rows, :cut].astype(jnp.float32)
                out_ref[...] = value[:rows, cut:].astype(jnp.float32)
                gains = value[rows:].astype(jnp.float32)
                gains_ref[...] = gains if s == 0 else gains_ref[...] + gains

    def target(s, here):
        half = (s // 4) ^ here[0]
        return (half, ((s % 2) ^ here[1]) * 2 + (((s // 2) % 2) ^ here[2]))

    shape = jax.ShapeDtypeStruct
    f32 = jnp.float32
    gain_shape = (GAIN_ROWS, columns)
    return call_with_here(
        kernel,
        here,
        (8,),
        list(pieces),
        [whole(v) for v in pieces],
        [
            shape((2 * rows, 4 * cut), f32),
            shape((2 * rows, 4 * (columns - cut)), f32),
            shape(gain_shape, f32),
        ],
        [
            pl.BlockSpec((rows, cut), target),
            pl.BlockSpec((rows, columns - cut), target),
            pl.BlockSpec(gain_shape, lambda s, here: (0, 0)),
        ],
    )


def on_block(
    tokens,
    qkv_weight,
    out_weight,
    gate_up_weight,
    down_weight,
    attn_gain,
    ffn_gain,
    query_gain,
    key_gain,
    seq_lengths,
    block_order,
    cotangent,
):
    inputs = tokens[0].astype(jnp.float32)
    rows_here = inputs.shape[0]
    ctx_size = lax.axis_size("ctx")
    ctx_index = lax.axis_index("ctx")
    per_group = HEADS // KV_HEADS
    q_width = HEADS * HD
    kv_width = KV_HEADS * HD
    order_row = block_order[0]
    lengths_row = seq_lengths[0]
    slots = jnp.arange(rows_here, dtype=jnp.int32) // BLK + ctx_index * (rows_here // BLK)
    table = slots[:, None] == jnp.arange(order_row.shape[0], dtype=jnp.int32)[None, :]
    packed = (
        jnp.sum(jnp.where(table, order_row[None, :], 0), axis=1) * BLK
        + jnp.arange(rows_here, dtype=jnp.int32) % BLK
    )
    local = packed - starts_of(packed, lengths_row)
    frequency = ROPE_BASE ** (-2.0 * jnp.arange(HD // 2, dtype=jnp.float32) / HD)
    angle = frequency[:, None] * local.astype(jnp.float32)[None, :]
    cosine = jnp.cos(angle)[None]
    sine = jnp.sin(angle)[None]
    bf16, f32 = jnp.bfloat16, jnp.float32
    parts = ctx_size // HEADS
    part = ctx_index // HEADS
    part_blocks = HEADS * rows_here // BLK
    q_order = lax.dynamic_slice_in_dim(order_row, part * part_blocks, part_blocks)
    q_slot, q_place, q_start = block_tables(q_order, lengths_row)
    q_slot = q_slot + part * part_blocks
    kv_slot, _, _ = block_tables(order_row, lengths_row)
    first = jnp.min(q_start.reshape(-1, TILE), axis=1) // TILE
    last = jnp.max(q_place.reshape(-1, TILE), axis=1) // TILE + 1
    tables = (q_slot, kv_slot, first, last)
    q_rows, kv_rows = part_blocks * BLK, order_row.shape[0] * BLK

    links = Links(ctx_size)
    here = links.here
    width = inputs.shape[1]
    rows = qkv_weight.shape[0]
    part_rows = rows // 4

    def quarter_rows(weight):
        return lax.dynamic_slice_in_dim(weight, links.quarter * part_rows, part_rows)

    qkv_piece = quarter_rows(qkv_weight)
    gains_here = jnp.concatenate([after(attn_gain, qkv_piece), ffn_gain, query_gain, key_gain])
    gains_there = links.over_x(gains_here)

    def gain_of(at, size):
        mine, other = gains_here[at : at + size], gains_there[at : at + size]
        return jnp.where(
            links.side == 0, jnp.concatenate([mine, other]), jnp.concatenate([other, mine])
        ).astype(f32)

    gain_attn = gain_of(0, rows)
    gain_ffn = gain_of(rows, rows)
    gain_query = gain_of(2 * rows, HD // 2)
    gain_key = gain_of(2 * rows + HD // 2, HD // 2)
    ff_chunk = gate_up_weight.shape[2] // CHUNKS

    def gate_up_piece(chunk):
        piece = lax.dynamic_slice(
            gate_up_weight,
            (links.quarter * part_rows, 0, chunk * ff_chunk),
            (part_rows, 2, ff_chunk),
        )
        return [piece[:, 0], piece[:, 1]]

    qkv_there = links.over_x(qkv_piece)
    first_piece = jnp.concatenate([*gate_up_piece(0), quarter_rows(out_weight)], axis=1)
    second_piece = jnp.concatenate(gate_up_piece(1), axis=1)
    down_piece = lax.dynamic_slice_in_dim(
        down_weight, links.quarter * (width // 4), width // 4, 1
    )
    d_ffn = cotangent[0]
    tokens_here = tokens[0]
    qkv_there = after(qkv_there, first_piece)
    first_there = links.over_x(after(first_piece, qkv_there))
    gate_up = jnp.transpose(after(gate_up_weight, qkv_there), (1, 0, 2))
    qkv_beside = links.over_y(qkv_there)
    qkv_pieces = (
        qkv_there,
        links.over_core(qkv_there),
        qkv_beside,
        links.over_core(after(qkv_beside, gate_up)),
    )
    sent, w_qkv, q_raw, k_raw, q_scale, k_scale, normed, scale_one = project(
        here, tokens_here, gain_attn[None], qkv_weight, qkv_pieces,
        gain_query[:, None], gain_key[:, None], cosine[0], sine[0],
    )
    got = lax.all_to_all(sent, "ctx", 0, 0, tiled=True)
    d_beside = links.over_y(after(d_ffn, sent))
    first_there = after(first_there, sent)
    down_there = links.over_x(after(down_piece, first_there))
    first_beside = links.over_y(first_there)
    got = after(got, d_beside)
    q_place, q_start = q_place[None], q_start[None]
    shape = jax.ShapeDtypeStruct
    attn_sent, *held = kernel_call(
        attend_kernel,
        tables,
        (got, q_place, q_start),
        [
            shape((ctx_size, HD, rows_here), bf16),
            shape((q_rows, HD), bf16),
            shape((HD, q_rows), bf16),
            shape((kv_rows, HD), bf16),
            shape((HD, kv_rows), bf16),
            shape((kv_rows, HD), bf16),
            shape((HD, q_rows), f32),
            shape((1, q_rows), f32),
        ],
        [pltpu.VMEM((HD, kv_rows), bf16)],
        ATTEND,
    )
    attn_in = lax.dynamic_slice_in_dim(
        lax.all_to_all(attn_sent, "ctx", 0, 0, tiled=True), part * HEADS, HEADS
    ).reshape(q_width, rows_here)
    down_there = after(down_there, attn_sent)
    second_there = links.over_x(after(second_piece, down_there))
    down_beside = links.over_y(down_there)

    def spread(there, beside, time):
        there, beside = after(there, time), after(beside, time)
        return (there, links.over_core(there), beside, links.over_core(beside))

    first_pieces = spread(first_there, first_beside, attn_sent)
    down_pieces = spread(down_there, down_beside, attn_in)
    second_beside = links.over_y(second_there)
    w_out, h_one, scale_two, two, two_t = attend_out(
        here, attn_in, tokens_here, gain_ffn[None], out_weight, first_pieces
    )
    two_beside = links.over_y(two_t)
    dealt_here, (out_sum, two_sum) = ffn(
        here, 0, two, d_ffn, gate_up, first_pieces, down_weight, down_pieces, [h_one]
    )
    second_beside = after(second_beside, out_sum)
    second_pieces = (
        second_there, links.over_core(second_there), second_beside, links.over_core(second_beside)
    )
    near, far, give, give_far = dealt_here
    got_far = links.over_core(give_far)
    first_shares = (near, links.over_core(give), links.over_y(far), links.over_y(got_far))
    out_sum = after(out_sum, got_far)
    dealt_here, (output, d_h_one, d_attn, d_heads, ffn_gain_term) = ffn(
        here, 1, two, d_ffn, gate_up, second_pieces, down_weight, down_pieces,
        [out_sum, two_sum, h_one, scale_two, w_out], gain_ffn[None],
    )
    second_shares = links.deal_plane(*dealt_here)

    def plane(value, beside, time):
        value, beside = after(value, time), after(beside, time)
        return (value, links.over_core(value), beside, links.over_core(beside))

    columns = ff_chunk // 2
    d_heads = d_heads.reshape(HEADS, HD, rows_here)
    d_got = lax.all_to_all(d_heads, "ctx", 0, 0, tiled=True)
    pair = jnp.stack([after(normed, d_heads), attn_in])
    two_plane = plane(two_t, two_beside, pair)
    first_products = wide_products(
        here, two_plane, [after(v, d_heads) for v in first_shares], columns
    )
    d_got = after(d_got, first_products[0])
    (d_sent,) = kernel_call(
        attend_back_kernel,
        tables,
        (d_got, q_place, q_start, *held),
        [shape((ctx_size, 3 * HD, rows_here), bf16)],
        [
            pltpu.VMEM((HD, q_rows), bf16),
            pltpu.VMEM((q_rows, HD), bf16),
            pltpu.VMEM((kv_rows, HD), f32),
            pltpu.VMEM((kv_rows, HD), f32),
        ],
        ATTEND_BACK,
    )
    first_got = links.over_x(first_products[0])
    d_sent = after(d_sent, first_got)
    d_back = lax.all_to_all(d_sent, "ctx", 0, 0, tiled=True)
    d_plane = plane(d_ffn, d_beside, d_sent)
    second_products = wide_products(
        here, two_plane, [after(v, d_plane[1]) for v in second_shares], columns
    )
    down_terms = down_products(
        here, d_plane, first_shares, second_shares, columns // 2
    )
    second_got = links.over_x(after(second_products[0], first_got))
    *d_shares, d_inputs, gain_sums = attention_back(
        here,
        [
            d_back, q_raw, k_raw, q_scale, k_scale, gain_query[:, None], gain_key[:, None],
            cosine[0], sine[0], w_qkv, tokens_here, scale_one, gain_attn[None], d_h_one, d_attn,
        ],
    )
    near, far, give, give_far = d_shares
    got, got_far = links.over_core(give), links.over_core(give_far)
    attention_shares = (near, got, links.over_y(far), links.over_y(got_far))
    down_got = links.over_x(after(down_terms[0], second_got))
    pair_plane = plane(pair, links.over_y(after(pair, d_sent)), d_shares[0])
    attention_terms = attention_products(
        here, pair_plane, attention_shares, gain_sums, ffn_gain_term
    )
    first_pair = links.sum_depth(first_products[1], first_got, got_far)
    second_pair = links.sum_depth(second_products[1], second_got)
    down_pair = links.sum_depth(down_terms[1], after(down_got, got_far))
    attention_pair = links.sum_depth(attention_terms[1], links.over_x(attention_terms[0]))
    first_placed = place_gate_up(here, 0, links.spread_plane(first_pair), None)
    grad_gate_up = place_gate_up(here, 1, links.spread_plane(second_pair), first_placed)

    def spread_after(value, time):
        beside = after(links.over_y(value), time)
        return (value, links.over_core(value), beside, links.over_core(beside))

    grad_down = place_down(here, spread_after(down_pair, first_placed))
    cut = qkv_weight.shape[1] // 4
    grad_qkv, grad_out, gain_sums = place_attention(
        here, spread_after(attention_pair, grad_gate_up), cut
    )
    at = links.side * (HD // 2)
    gain_grads = [
        gain_sums[0, :rows],
        gain_sums[1, :rows],
        lax.dynamic_slice_in_dim(gain_sums[0, rows : rows + HD], at, HD // 2),
        lax.dynamic_slice_in_dim(gain_sums[1, rows : rows + HD], at, HD // 2),
    ]
    return (
        output[None],
        d_inputs[None],
        grad_qkv,
        grad_out,
        grad_gate_up,
        grad_down,
        *gain_grads,
    )


def on_device(
    tokens,
    qkv_weight,
    out_weight,
    gate_up_weight,
    down_weight,
    attn_gain,
    ffn_gain,
    query_gain,
    key_gain,
    seq_lengths,
    block_order,
    cotangent,
):
    inputs = tokens[0].astype(jnp.float32)
    rows_here = inputs.shape[0]
    ctx_size = lax.axis_size("ctx")
    ctx_index = lax.axis_index("ctx")
    per_group = HEADS // KV_HEADS
    q_width = HEADS * HD
    kv_width = KV_HEADS * HD
    order_row = block_order[0]
    lengths_row = seq_lengths[0]
    slots = jnp.arange(rows_here, dtype=jnp.int32) // BLK + ctx_index * (rows_here // BLK)
    table = slots[:, None] == jnp.arange(order_row.shape[0], dtype=jnp.int32)[None, :]
    packed = (
        jnp.sum(jnp.where(table, order_row[None, :], 0), axis=1) * BLK
        + jnp.arange(rows_here, dtype=jnp.int32) % BLK
    )
    local = packed - starts_of(packed, lengths_row)
    frequency = ROPE_BASE ** (-2.0 * jnp.arange(HD // 2, dtype=jnp.float32) / HD)
    angle = frequency[:, None] * local.astype(jnp.float32)[None, :]
    cosine = jnp.cos(angle)[None]
    sine = jnp.sin(angle)[None]
    bf16, f32 = jnp.bfloat16, jnp.float32
    parts = ctx_size // HEADS
    part = ctx_index // HEADS
    part_blocks = HEADS * rows_here // BLK
    q_order = lax.dynamic_slice_in_dim(order_row, part * part_blocks, part_blocks)
    q_slot, q_place, q_start = block_tables(q_order, lengths_row)
    q_slot = q_slot + part * part_blocks
    kv_slot, _, _ = block_tables(order_row, lengths_row)
    first = jnp.min(q_start.reshape(-1, TILE), axis=1) // TILE
    last = jnp.max(q_place.reshape(-1, TILE), axis=1) // TILE + 1
    tables = (q_slot, kv_slot, first, last)
    q_rows, kv_rows = part_blocks * BLK, order_row.shape[0] * BLK

    def fetch_attention():
        return (
            lax.all_gather(qkv_weight, "fsdp", axis=0, tiled=True),
            lax.all_gather(out_weight, "fsdp", axis=0, tiled=True),
            lax.all_gather(attn_gain, "fsdp", axis=0, tiled=True),
            lax.all_gather(ffn_gain, "fsdp", axis=0, tiled=True),
            lax.all_gather(query_gain, "fsdp", axis=0, tiled=True),
            lax.all_gather(key_gain, "fsdp", axis=0, tiled=True),
        )

    w_qkv, w_out, gain_attn, gain_ffn, gain_query, gain_key = fetch_attention()
    gain_attn = gain_attn.astype(jnp.float32)
    gain_ffn = gain_ffn.astype(jnp.float32)
    gain_query = gain_query.astype(jnp.float32)
    gain_key = gain_key.astype(jnp.float32)
    scale_one = rms_scale(inputs)
    normed = (inputs * scale_one * gain_attn).astype(jnp.bfloat16)
    projected = lax.dot_general(
        w_qkv, normed, (((0,), (1,)), ((), ())), preferred_element_type=f32
    )
    q_raw = projected[:q_width].reshape(HEADS, HD, rows_here)
    k_raw = projected[q_width : q_width + kv_width].reshape(KV_HEADS, HD, rows_here)
    values_here = projected[q_width + kv_width :].reshape(KV_HEADS, HD, rows_here).astype(bf16)
    q_scale = rms_scale(q_raw, 1)
    k_scale = rms_scale(k_raw, 1)
    column_query, column_key = gain_query[:, None], gain_key[:, None]
    queries = rope(q_raw * q_scale * column_query, cosine, sine).astype(bf16)
    keys_here = rope(k_raw * k_scale * column_key, cosine, sine).astype(bf16)
    sent = jnp.concatenate(
        [queries, jnp.repeat(keys_here, per_group, 0), jnp.repeat(values_here, per_group, 0)], axis=1
    )
    sent = jnp.concatenate([sent] * parts, axis=0)
    got = lax.all_to_all(sent, "ctx", 0, 0, tiled=True)
    q_place, q_start = q_place[None], q_start[None]
    shape = jax.ShapeDtypeStruct
    attn_sent, *held = kernel_call(
        attend_kernel,
        tables,
        (got, q_place, q_start),
        [
            shape((ctx_size, HD, rows_here), bf16),
            shape((q_rows, HD), bf16),
            shape((HD, q_rows), bf16),
            shape((kv_rows, HD), bf16),
            shape((HD, kv_rows), bf16),
            shape((kv_rows, HD), bf16),
            shape((HD, q_rows), f32),
            shape((1, q_rows), f32),
        ],
        [pltpu.VMEM((HD, kv_rows), bf16)],
        ATTEND,
    )
    attn_in = lax.dynamic_slice_in_dim(
        lax.all_to_all(attn_sent, "ctx", 0, 0, tiled=True), part * HEADS, HEADS
    ).reshape(q_width, rows_here)
    h_one = inputs + lax.dot_general(
        attn_in, w_out, (((0,), (0,)), ((), ())), preferred_element_type=f32
    )
    scale_two = rms_scale(h_one)
    normed_two = (h_one * scale_two * gain_ffn).astype(jnp.bfloat16)
    columns = normed_two
    gate_up = jnp.einsum(
        "tr,rgf->tgf",
        columns,
        lax.all_gather(gate_up_weight, "fsdp", axis=0, tiled=True),
        preferred_element_type=jnp.float32,
    )
    gate = gate_up[:, 0]
    upper = gate_up[:, 1]
    sigma = jax.nn.sigmoid(gate)
    hidden = (gate * sigma * upper).astype(jnp.bfloat16)
    columns = hidden
    ffn_out = jnp.dot(
        columns,
        lax.all_gather(down_weight, "fsdp", axis=0, tiled=True),
        preferred_element_type=jnp.float32,
    )
    output = (h_one + ffn_out).astype(jnp.bfloat16)
    d_out = cotangent[0].astype(jnp.float32)
    d_ffn = d_out.astype(jnp.bfloat16)
    d_hidden = lax.dot_general(
        d_ffn,
        lax.all_gather(down_weight, "fsdp", axis=0, tiled=True),
        (((1,), (1,)), ((), ())),
        preferred_element_type=jnp.float32,
    )
    d_gate = d_hidden * upper * sigma * (1.0 + gate * (1.0 - sigma))
    d_upper = d_hidden * gate * sigma
    d_gate_up = jnp.stack([d_gate, d_upper], axis=1).astype(jnp.bfloat16)
    d_normed_two = jnp.einsum(
        "tgf,rgf->tr",
        d_gate_up,
        lax.all_gather(gate_up_weight, "fsdp", axis=0, tiled=True),
        preferred_element_type=jnp.float32,
    )
    columns = normed_two
    grad_gate_up = lax.psum_scatter(
        jnp.einsum("tr,tgf->rgf", columns, d_gate_up, preferred_element_type=jnp.float32).astype(
            jnp.bfloat16
        ),
        "fsdp",
        scatter_dimension=0,
        tiled=True,
    )
    columns = hidden
    grad_down = lax.psum_scatter(
        lax.dot_general(
            columns, d_ffn, (((0,), (0,)), ((), ())), preferred_element_type=jnp.float32
        ).astype(jnp.bfloat16),
        "fsdp",
        scatter_dimension=0,
        tiled=True,
    )
    d_norm_two, ffn_gain_term = norm_back(d_normed_two, h_one, scale_two, gain_ffn)
    d_h_one = d_out + d_norm_two
    d_attn = d_h_one.astype(jnp.bfloat16)
    grad_out_here = jnp.dot(attn_in, d_attn, preferred_element_type=f32)
    d_heads = lax.dot_general(
        w_out, d_attn, (((1,), (1,)), ((), ())), preferred_element_type=f32
    ).astype(bf16)
    d_heads = jnp.concatenate([d_heads.reshape(HEADS, HD, rows_here)] * parts, axis=0)
    d_got = lax.all_to_all(d_heads, "ctx", 0, 0, tiled=True)
    (d_sent,) = kernel_call(
        attend_back_kernel,
        tables,
        (d_got, q_place, q_start, *held),
        [shape((ctx_size, 3 * HD, rows_here), bf16)],
        [
            pltpu.VMEM((HD, q_rows), bf16),
            pltpu.VMEM((q_rows, HD), bf16),
            pltpu.VMEM((kv_rows, HD), f32),
            pltpu.VMEM((kv_rows, HD), f32),
        ],
        ATTEND_BACK,
    )
    d_back = lax.all_to_all(d_sent, "ctx", 0, 0, tiled=True)
    d_query = lax.dynamic_slice_in_dim(d_back[:, :HD], part * HEADS, HEADS).astype(f32)
    d_key_value = jnp.sum(
        d_back[:, HD:].reshape(parts, KV_HEADS, per_group, 2 * HD, rows_here).astype(f32),
        axis=(0, 2),
    )
    dq_normed = rope_back(d_query, cosine, sine)
    dk_normed = rope_back(d_key_value[:, :HD], cosine, sine)
    dq_raw, query_term = norm_back(dq_normed, q_raw, q_scale, column_query, 1)
    dk_raw, key_term = norm_back(dk_normed, k_raw, k_scale, column_key, 1)
    d_projected = jnp.concatenate(
        [
            dq_raw.reshape(q_width, rows_here).astype(bf16),
            dk_raw.reshape(kv_width, rows_here).astype(bf16),
            d_key_value[:, HD:].reshape(kv_width, rows_here).astype(bf16),
        ],
        axis=0,
    )
    grad_qkv_here = lax.dot_general(
        normed, d_projected, (((0,), (1,)), ((), ())), preferred_element_type=f32
    )
    d_normed = lax.dot_general(
        d_projected, w_qkv, (((0,), (1,)), ((), ())), preferred_element_type=f32
    )
    d_norm_one, attn_gain_term = norm_back(d_normed, inputs, scale_one, gain_attn)
    d_inputs = d_h_one + d_norm_one
    shard_qkv, shard_out, shard_attn_gain, shard_ffn_gain, shard_query_gain, shard_key_gain = (
        lax.psum_scatter(
            grad_qkv_here.astype(jnp.bfloat16), "fsdp", scatter_dimension=0, tiled=True
        ).astype(jnp.float32),
        lax.psum_scatter(
            grad_out_here.astype(jnp.bfloat16), "fsdp", scatter_dimension=0, tiled=True
        ).astype(jnp.float32),
        lax.psum_scatter(
            jnp.sum(attn_gain_term, axis=0).astype(jnp.bfloat16),
            "fsdp",
            scatter_dimension=0,
            tiled=True,
        ).astype(jnp.float32),
        lax.psum_scatter(
            jnp.sum(ffn_gain_term, axis=0).astype(jnp.bfloat16),
            "fsdp",
            scatter_dimension=0,
            tiled=True,
        ).astype(jnp.float32),
        lax.psum_scatter(
            jnp.sum(query_term, axis=(0, 2)).astype(jnp.bfloat16),
            "fsdp",
            scatter_dimension=0,
            tiled=True,
        ).astype(jnp.float32),
        lax.psum_scatter(
            jnp.sum(key_term, axis=(0, 2)).astype(jnp.bfloat16),
            "fsdp",
            scatter_dimension=0,
            tiled=True,
        ).astype(jnp.float32),
    )
    summed_grads = (
        lax.psum(shard_qkv.astype(jnp.bfloat16), "ctx").astype(jnp.float32),
        lax.psum(shard_out.astype(jnp.bfloat16), "ctx").astype(jnp.float32),
        lax.psum(grad_gate_up, "ctx").astype(jnp.float32),
        lax.psum(grad_down, "ctx").astype(jnp.float32),
        lax.psum(shard_attn_gain.astype(jnp.bfloat16), "ctx").astype(jnp.float32),
        lax.psum(shard_ffn_gain.astype(jnp.bfloat16), "ctx").astype(jnp.float32),
        lax.psum(shard_query_gain.astype(jnp.bfloat16), "ctx").astype(jnp.float32),
        lax.psum(shard_key_gain.astype(jnp.bfloat16), "ctx").astype(jnp.float32),
    )
    return (
        output[None],
        d_inputs[None],
        summed_grads[0],
        summed_grads[1],
        summed_grads[2],
        summed_grads[3],
        summed_grads[4],
        summed_grads[5],
        summed_grads[6],
        summed_grads[7],
    )


def solution(mesh):
    block = mesh.shape["fsdp"] == 2 and mesh.shape["ctx"] == 16
    return jax.shard_map(
        on_block if block else on_device,
        mesh=mesh,
        in_specs=(
            P("fsdp", "ctx", None),
            P("fsdp", None),
            P("fsdp", None),
            P("fsdp", None, None),
            P("fsdp", None),
            P("fsdp"),
            P("fsdp"),
            P("fsdp"),
            P("fsdp"),
            P("fsdp", None),
            P("fsdp", None),
            P("fsdp", "ctx", None),
        ),
        out_specs=(
            P("fsdp", "ctx", None),
            P("fsdp", "ctx", None),
            P("fsdp", None),
            P("fsdp", None),
            P("fsdp", None, None),
            P("fsdp", None),
            P("fsdp"),
            P("fsdp"),
            P("fsdp"),
            P("fsdp"),
        ),
        check_vma=False,
    )
```

```python
import functools

import jax
import jax.numpy as jnp
from jax import lax
from jax.experimental import pallas as pl
from jax.experimental.pallas import tpu as pltpu
from jax.sharding import PartitionSpec as P

HEADS = 16
KV_HEADS = 8
HD = 64
BLK = 128
TILE = 256
CHUNKS = 2
PROJECT = 0
ATTEND = 0
OUT = 0
FFN = (0, 0)
ATTEND_BACK = 25


EPSILON = 1e-05
ROPE_BASE = 1000000.0
LOG2E = 1.4426950408889634
SCORE_SCALE = LOG2E * HD ** (-0.5)


def rms_scale(values, axis=-1):
    return lax.rsqrt(jnp.mean(values * values, axis=axis, keepdims=True) + EPSILON)


def norm_back(grad_normed, inputs, scale, gain, axis=-1):
    scaled = grad_normed * gain
    grad_in = scale * scaled - inputs * scale * scale * scale * jnp.mean(
        scaled * inputs, axis=axis, keepdims=True
    )
    return (grad_in, grad_normed * inputs * scale)


def rope(values, cosine, sine):
    half = HD // 2
    first, second = values[:, :half], values[:, half:]
    return jnp.concatenate([first * cosine - second * sine, second * cosine + first * sine], axis=1)


def rope_back(values, cosine, sine):
    half = HD // 2
    first, second = values[:, :half], values[:, half:]
    return jnp.concatenate([first * cosine + second * sine, second * cosine - first * sine], axis=1)


def starts_of(packed, lengths_row):
    ends = jnp.cumsum(lengths_row)
    past = packed[:, None] >= ends[None, :]
    return jnp.sum(jnp.where(past, lengths_row[None, :], 0), axis=1)


def block_tables(order, lengths_row):
    count = order.shape[0]
    rank = jnp.sum((order[None, :] < order[:, None]).astype(jnp.int32), axis=1)
    hit = rank[None, :] == jnp.arange(count, dtype=jnp.int32)[:, None]
    slot = jnp.sum(jnp.where(hit, jnp.arange(count, dtype=jnp.int32)[None, :], 0), axis=1)
    block = jnp.sum(jnp.where(hit, order[None, :], 0), axis=1)
    place = (block[:, None] * BLK + jnp.arange(BLK, dtype=jnp.int32)[None, :]).reshape(-1)
    return (slot, place, starts_of(place, lengths_row))


def attend_kernel(
    q_slot, kv_slot, first, last, qkv_ref, place_ref, start_ref,
    out_ref, q_ref, qt_ref, k_ref, kt_ref, v_ref, ot_ref, total_ref, vt_ref
):
    per_device = qkv_ref.shape[2] // BLK
    kv_blocks = k_ref.shape[0] // BLK
    q_blocks = q_ref.shape[0] // BLK

    def piece(slot, lower):
        return qkv_ref[
            slot // per_device,
            lower : lower + HD,
            pl.ds(pl.multiple_of((slot % per_device) * BLK, BLK), BLK),
        ]

    for i in range(kv_blocks):
        here = slice(i * BLK, (i + 1) * BLK)
        keys = piece(kv_slot[i], HD)
        kt_ref[:, here] = keys
        k_ref[here, :] = keys.T
        values = piece(kv_slot[i], 2 * HD)
        vt_ref[:, here] = values
        v_ref[here, :] = values.T
    for i in range(q_blocks):
        here = slice(i * BLK, (i + 1) * BLK)
        queries = piece(q_slot[i], 0)
        qt_ref[:, here] = queries
        q_ref[here, :] = queries.T
    if q_blocks < kv_blocks:
        out_ref[...] = jnp.zeros_like(out_ref)

    def tile(i, carry):
        rows = pl.ds(pl.multiple_of(i * TILE, TILE), TILE)
        queries = qt_ref[:, rows]
        place = place_ref[:, rows]
        start = start_ref[:, rows]

        def step(j, state):
            total, summed = state
            at = pl.multiple_of(j * TILE, TILE)
            scores = jnp.dot(
                k_ref[pl.ds(at, TILE), :], queries, preferred_element_type=jnp.float32
            )
            key_place = lax.broadcasted_iota(jnp.int32, (TILE, TILE), 0) + at
            allowed = (key_place <= place) & (key_place >= start)
            lifted = jnp.where(allowed, jnp.exp2(scores * SCORE_SCALE), 0.0)
            total = total + jnp.sum(lifted, axis=0, keepdims=True)
            summed = summed + jnp.dot(
                vt_ref[:, pl.ds(at, TILE)],
                lifted.astype(jnp.bfloat16),
                preferred_element_type=jnp.float32,
            )
            return (total, summed)

        total, summed = lax.fori_loop(
            first[i],
            last[i],
            step,
            (jnp.zeros((1, TILE), jnp.float32), jnp.zeros((HD, TILE), jnp.float32)),
        )
        attn = summed / total
        ot_ref[:, rows] = attn
        total_ref[:, rows] = jnp.log(total) * LOG2E
        rounded = attn.astype(jnp.bfloat16)
        for part in range(TILE // BLK):
            slot = q_slot[i * (TILE // BLK) + part]
            out_ref[
                slot // per_device,
                :,
                pl.ds(pl.multiple_of((slot % per_device) * BLK, BLK), BLK),
            ] = rounded[:, part * BLK : (part + 1) * BLK]
        return carry

    lax.fori_loop(0, q_blocks * BLK // TILE, tile, 0)


def attend_back_kernel(
    q_slot, kv_slot, first, last, d_ref, place_ref, start_ref,
    q_ref, qt_ref, k_ref, kt_ref, v_ref, ot_ref, total_ref,
    out_ref, dt_ref, do_ref, dk_ref, dv_ref
):
    per_device = d_ref.shape[2] // BLK
    kv_blocks = k_ref.shape[0] // BLK
    q_blocks = q_ref.shape[0] // BLK

    def lanes(slot):
        return pl.ds(pl.multiple_of((slot % per_device) * BLK, BLK), BLK)

    for i in range(q_blocks):
        here = slice(i * BLK, (i + 1) * BLK)
        slot = q_slot[i]
        grads = d_ref[slot // per_device, :, lanes(slot)]
        dt_ref[:, here] = grads
        do_ref[here, :] = grads.T
    dk_ref[...] = jnp.zeros_like(dk_ref)
    dv_ref[...] = jnp.zeros_like(dv_ref)
    if q_blocks < kv_blocks:
        out_ref[...] = jnp.zeros_like(out_ref)

    def tile(i, carry):
        rows = pl.ds(pl.multiple_of(i * TILE, TILE), TILE)
        queries = qt_ref[:, rows]
        grads = dt_ref[:, rows]
        place = place_ref[:, rows]
        start = start_ref[:, rows]
        delta = jnp.sum(grads.astype(jnp.float32) * ot_ref[:, rows], axis=0, keepdims=True)
        total = total_ref[:, rows]

        def step(j, d_query):
            at = pl.multiple_of(j * TILE, TILE)
            here = pl.ds(at, TILE)
            scores = jnp.dot(k_ref[here, :], queries, preferred_element_type=jnp.float32)
            key_place = lax.broadcasted_iota(jnp.int32, (TILE, TILE), 0) + at
            allowed = (key_place <= place) & (key_place >= start)
            shares = jnp.where(allowed, jnp.exp2(scores * SCORE_SCALE - total), 0.0)
            d_shares = jnp.dot(v_ref[here, :], grads, preferred_element_type=jnp.float32)
            d_scores = (shares * (d_shares - delta)).astype(jnp.bfloat16)
            dv_ref[here, :] += jnp.dot(
                shares.astype(jnp.bfloat16), do_ref[rows, :], preferred_element_type=jnp.float32
            )
            dk_ref[here, :] += jnp.dot(
                d_scores, q_ref[rows, :], preferred_element_type=jnp.float32
            )
            return d_query + jnp.dot(
                kt_ref[:, here], d_scores, preferred_element_type=jnp.float32
            )

        d_query = lax.fori_loop(first[i], last[i], step, jnp.zeros((HD, TILE), jnp.float32))
        rounded = (d_query * HD ** (-0.5)).astype(jnp.bfloat16)
        for part in range(TILE // BLK):
            slot = q_slot[i * (TILE // BLK) + part]
            out_ref[slot // per_device, 0:HD, lanes(slot)] = rounded[
                :, part * BLK : (part + 1) * BLK
            ]
        return carry

    lax.fori_loop(0, q_blocks * BLK // TILE, tile, 0)
    for i in range(kv_blocks):
        here = slice(i * BLK, (i + 1) * BLK)
        slot = kv_slot[i]
        out_ref[slot // per_device, HD : 2 * HD, lanes(slot)] = (
            (dk_ref[here, :] * HD ** (-0.5)).T.astype(jnp.bfloat16)
        )
        out_ref[slot // per_device, 2 * HD : 3 * HD, lanes(slot)] = (
            dv_ref[here, :].T.astype(jnp.bfloat16)
        )


def cost(micros):
    return pl.CostEstimate(
        flops=1 + micros * 1_000_000_000, bytes_accessed=1, transcendentals=0
    )


def kernel_call(kernel, tables, arrays, outs, scratch, micros):
    smem = pl.BlockSpec(memory_space=pltpu.SMEM)
    vmem = pl.BlockSpec(memory_space=pltpu.VMEM)
    return pl.pallas_call(
        kernel,
        out_shape=outs,
        in_specs=[smem] * len(tables) + [vmem] * len(arrays),
        out_specs=[vmem] * len(outs),
        scratch_shapes=scratch,
        compiler_params=pltpu.CompilerParams(vmem_limit_bytes=48 * 1024 * 1024),
        cost_estimate=cost(micros),
    )(*tables, *arrays)


class Links:
    def __init__(self, ctx_size):
        self.depth = ctx_size // 4
        index = lax.axis_index("ctx")
        self.core = index % 2
        self.y = (index // 2) % 2
        self.side = lax.axis_index("fsdp")
        self.half = index // 4 % 2
        self.quarter = index % 2 * 2 + self.y
        self.here = jnp.stack([self.half, self.core, self.y, self.side]).astype(jnp.int32)

    def route(self, place):
        pairs = []
        for z in range(self.depth):
            for y in range(2):
                for core in range(2):
                    to_z, to_y, to_core = place(z, y, core)
                    pairs.append(((z * 2 + y) * 2 + core, (to_z * 2 + to_y) * 2 + to_core))
        return pairs

    def over_core(self, value):
        return lax.ppermute(value, "ctx", self.route(lambda z, y, c: (z, y, 1 - c)))

    def over_y(self, value):
        return lax.ppermute(value, "ctx", self.route(lambda z, y, c: (z, 1 - y, c)))

    def over_z(self, value):
        return lax.ppermute(value, "ctx", self.route(lambda z, y, c: (z ^ 1, y, c)))

    def over_two_z(self, value):
        return lax.ppermute(value, "ctx", self.route(lambda z, y, c: (z ^ 2, y, c)))

    def over_x(self, value):
        return lax.ppermute(value, "fsdp", [(0, 1), (1, 0)])

    def spread_plane(self, value):
        across = self.over_core(value)
        beside = self.over_y(value)
        return (value, across, beside, self.over_core(beside))

    def deal_plane(self, near, far, give, give_far):
        got, got_far = self.over_core(give), self.over_core(give_far)
        return (near, got, self.over_y(far), self.over_y(got_far))

    def sum_depth(self, kept, got, time=None):
        def half(index):
            return add(pick(kept, index, 0), pick(got, index, 0))

        given = self.over_z(half(1 - self.half))
        part = add(half(self.half), given)
        other = self.over_two_z(part)
        full = add(part, other if time is None else after(other, time))
        return jnp.stack([full, self.over_z(full)])


def pick(value, index, axis):
    return lax.dynamic_index_in_dim(value, index, axis, keepdims=False)


def add(left, right):
    return (left.astype(jnp.float32) + right.astype(jnp.float32)).astype(jnp.bfloat16)


def after(value, *others):
    return lax.optimization_barrier((value, *others))[0]


def contract(left, right, axes):
    return lax.dot_general(
        left, right, ((axes[:1], axes[1:]), ((), ())), preferred_element_type=jnp.float32
    )


PARAMS = pltpu.CompilerParams(vmem_limit_bytes=56 * 1024 * 1024)


def call_with_here(
    kernel, here, grid, arrays, specs, outs, out_specs, scratch=(), aliases=None, micros=5
):
    return pl.pallas_call(
        kernel,
        grid_spec=pltpu.PrefetchScalarGridSpec(
            num_scalar_prefetch=1,
            grid=grid,
            in_specs=specs,
            out_specs=out_specs,
            scratch_shapes=list(scratch),
        ),
        out_shape=outs,
        input_output_aliases=aliases or {},
        compiler_params=PARAMS,
        cost_estimate=cost(micros),
    )(here, *arrays)


def whole(array):
    rank = len(array.shape)
    return pl.BlockSpec(array.shape, lambda i, here: (0,) * rank)


def project_kernel(here, *refs):
    x_ref, gain_ref, own_ref = refs[:3]
    pieces, q_gain, k_gain, cos_ref, sin_ref = refs[3:7], refs[7], refs[8], refs[9], refs[10]
    sent, weight, q_ref, k_ref, q_scale, k_scale, normed_ref, scale_ref = refs[11:]
    core, y, side = here[1], here[2], here[3]
    rows = own_ref.shape[0]
    part = rows // 4
    f32, bf16 = jnp.float32, jnp.bfloat16
    weight[pl.ds(pl.multiple_of(side * rows, rows), rows), :] = own_ref[...]
    for p in range(4):
        at = (1 - side) * rows + (((p % 2) ^ core) * 2 + ((p // 2) ^ y)) * part
        weight[pl.ds(pl.multiple_of(at, part), part), :] = pieces[p][...]
    x = x_ref[...].astype(f32)
    scale = rms_scale(x)
    scale_ref[...] = scale
    normed = (x * scale * gain_ref[...]).astype(bf16)
    normed_ref[...] = normed.T
    cosine, sine = cos_ref[...], sin_ref[...]
    half = HD // 2

    def turned(raw, gain, raw_ref, kept_scale, head):
        raw_ref[head * HD : (head + 1) * HD, :] = raw
        scale = rms_scale(raw, 0)
        kept_scale[head : head + 1, :] = scale
        value = raw * scale * gain
        first, second = value[:half], value[half:]
        return jnp.concatenate(
            [first * cosine - second * sine, second * cosine + first * sine], axis=0
        ).astype(bf16)

    per_group = HEADS // KV_HEADS
    for at in range(0, weight.shape[1], 2 * BLK):
        block = jnp.dot(normed, weight[:, at : at + 2 * BLK], preferred_element_type=f32)
        turned_block = block.T
        for n in range(2 * BLK // HD):
            head = at // HD + n
            raw = turned_block[n * HD : (n + 1) * HD, :]
            if head < HEADS:
                sent[head, 0:HD, :] = turned(raw, q_gain[...], q_ref, q_scale, head)
                continue
            head -= HEADS
            if head < KV_HEADS:
                value, row = turned(raw, k_gain[...], k_ref, k_scale, head), HD
            else:
                value, row, head = raw.astype(bf16), 2 * HD, head - KV_HEADS
            for copy in range(per_group):
                sent[head * per_group + copy, row : row + HD, :] = value


def project(here, x, gain, own, pieces, q_gain, k_gain, cosine, sine):
    tokens, width = x.shape
    f32, bf16 = jnp.float32, jnp.bfloat16
    shape = jax.ShapeDtypeStruct
    arrays = [x, gain, own, *pieces, q_gain, k_gain, cosine, sine]
    outs = [
        shape((HEADS, 3 * HD, tokens), bf16),
        shape((width, own.shape[1]), bf16),
        shape((HEADS * HD, tokens), f32),
        shape((KV_HEADS * HD, tokens), f32),
        shape((HEADS, tokens), f32),
        shape((KV_HEADS, tokens), f32),
        shape((width, tokens), bf16),
        shape((tokens, 1), f32),
    ]
    return call_with_here(
        project_kernel, here, (1,), arrays, [whole(a) for a in arrays], outs,
        [whole(o) for o in outs], micros=PROJECT,
    )


def layer(array, index):
    return pl.BlockSpec((1, *array.shape[1:]), lambda i, here: (index, 0, 0))


def attend_out_kernel(here, *refs):
    attn_ref, x_ref, gain_ref, own_ref = refs[:4]
    pieces = refs[4:12]
    weight, h_ref, scale_ref, two_ref, two_t_ref = refs[12:]
    core, y, side = here[1], here[2], here[3]
    rows = own_ref.shape[0]
    part = rows // 4
    weight[pl.ds(pl.multiple_of(side * rows, rows), rows), :] = own_ref[...]
    for p in range(4):
        at = (1 - side) * rows + (((p % 2) ^ core) * 2 + ((p // 2) ^ y)) * part
        for n in range(2):
            piece = pieces[2 * p + n]
            wide = piece.shape[1]
            weight[pl.ds(pl.multiple_of(at, part), part), n * wide : (n + 1) * wide] = piece[...]
    attn = attn_ref[...].T
    h_one = x_ref[...].astype(jnp.float32) + jnp.dot(
        attn, weight[...], preferred_element_type=jnp.float32
    )
    scale = rms_scale(h_one)
    h_ref[...] = h_one
    scale_ref[...] = scale
    two = (h_one * scale * gain_ref[...]).astype(jnp.bfloat16)
    two_ref[...] = two
    two_t_ref[...] = two.T


def attend_out(here, attn, x, gain, own, pieces):
    tokens, width = x.shape
    f32, bf16 = jnp.float32, jnp.bfloat16
    shape = jax.ShapeDtypeStruct
    part = own.shape[0] // 4
    half = width // 2
    first = pieces[0].shape[1] // half - 2
    arrays = [attn, x, gain, own]
    specs = [whole(a) for a in arrays]
    for piece in pieces:
        for n in range(2):
            arrays.append(piece)
            specs.append(pl.BlockSpec((part, half), lambda i, here, n=n: (0, first + n)))
    outs = [
        shape((width, width), bf16),
        shape((tokens, width), f32),
        shape((tokens, 1), f32),
        shape((tokens, width), bf16),
        shape((width, tokens), bf16),
    ]
    return call_with_here(
        attend_out_kernel, here, (1,), arrays, specs, outs, [whole(o) for o in outs], micros=OUT
    )


def ffn_kernel(chunk, here, *refs):
    two_ref, d_ref, own_ref = refs[:3]
    pieces, down_ref, down_pieces = refs[3:7], refs[7], refs[8:12]
    if chunk == 0:
        before_refs, refs = refs[12:13], refs[13:]
        near, far, give, give_far, out_ref, d_two_ref = refs[:6]
        refs = refs[6:]
    else:
        before_refs, gain_ref, refs = refs[12:17], refs[17], refs[18:]
        near, far, give, give_far = refs[:4]
        out_ref, d_h_ref, d_attn_ref, heads_ref, gain_term_ref = refs[4:9]
        refs = refs[9:]
    weight, down, hidden_rows, out_sum, two_sum = refs[:5]
    held, weight_sem, down_sem, before_sem = refs[5:-3], refs[-3], refs[-2], refs[-1]
    core, y, side = here[1], here[2], here[3]
    f32, bf16 = jnp.float32, jnp.bfloat16
    own_rows, columns = own_ref.shape[1], own_ref.shape[2] // CHUNKS
    part = own_rows // 4
    tile = columns // FFN_TILES
    half = columns // 2

    def quarter(p):
        return ((p % 2) ^ core) * 2 + ((p // 2) ^ y)

    def copies(n):
        at = slice(n * tile, (n + 1) * tile)
        mine = pl.ds(pl.multiple_of(side * own_rows, own_rows), own_rows)
        found = [
            pltpu.make_async_copy(
                own_ref.at[:, :, chunk * columns + n * tile : chunk * columns + (n + 1) * tile],
                weight.at[:, mine, at],
                weight_sem.at[n, 0],
            )
        ]
        for p in range(4):
            rows = pl.ds(pl.multiple_of((1 - side) * own_rows + quarter(p) * part, part), part)
            for kind in range(2):
                begin = kind * columns + n * tile
                found.append(
                    pltpu.make_async_copy(
                        pieces[p].at[:, begin : begin + tile],
                        weight.at[kind, rows, at],
                        weight_sem.at[n, 1 + 2 * p + kind],
                    )
                )
        return found

    def own_down(n):
        at = slice(n * tile, (n + 1) * tile)
        return [pltpu.make_async_copy(down_ref.at[at, :], down.at[at, :], down_sem.at[n, 0])]

    def other_down(n):
        at = slice(n * tile, (n + 1) * tile)
        found = []
        for p in range(4):
            wide = down_pieces[p].shape[1]
            lanes = pl.ds(pl.multiple_of(quarter(p) * wide, wide), wide)
            found.append(
                pltpu.make_async_copy(
                    down_pieces[p].at[at, :], down.at[at, lanes], down_sem.at[n, p]
                )
            )
        return found

    def each(action, n):
        for copy in copies(n):
            action(copy)

        @pl.when(side == chunk)
        def _():
            for copy in own_down(n):
                action(copy)

        @pl.when(side != chunk)
        def _():
            for copy in other_down(n):
                action(copy)

    before = [
        pltpu.make_async_copy(ref, held[n], before_sem.at[n]) for n, ref in enumerate(before_refs)
    ]
    for n in range(FFN_TILES):
        each(lambda copy: copy.start(), n)
    for copy in before:
        copy.start()
    two = two_ref[...]
    d_ffn = d_ref[...]
    for n in range(FFN_TILES):
        each(lambda copy: copy.wait(), n)
        at = slice(n * tile, (n + 1) * tile)
        gate = jnp.dot(two, weight[0, :, at], preferred_element_type=f32)
        upper = jnp.dot(two, weight[1, :, at], preferred_element_type=f32)
        d_hidden = contract(d_ffn, down[at, :], (1, 1))
        sigma = jax.nn.sigmoid(gate)
        silu = gate * sigma
        hidden = (silu * upper).astype(bf16)
        d_gate = (d_hidden * upper * sigma * (1.0 + gate * (1.0 - sigma))).astype(bf16)
        d_upper = (d_hidden * silu).astype(bf16)
        out_term = jnp.dot(hidden, down[at, :], preferred_element_type=f32)
        two_term = contract(d_gate, weight[0, :, at], (1, 1)) + contract(
            d_upper, weight[1, :, at], (1, 1)
        )
        out_sum[...] = out_term if n == 0 else out_sum[...] + out_term
        two_sum[...] = two_term if n == 0 else two_sum[...] + two_term
        hidden_rows[:, at] = hidden
        mine = jnp.where(core == 0, d_gate, d_upper)
        other = jnp.where(core == 0, d_upper, d_gate)
        for column in range(2):
            begin, end = max(n * tile, column * half), min((n + 1) * tile, (column + 1) * half)
            if begin >= end:
                continue
            source = slice(begin - n * tile, end - n * tile)
            target = slice(begin - column * half, end - column * half)
            first, second = mine[:, source], other[:, source]

            @pl.when(y == column)
            def _(first=first, second=second, target=target):
                near[:, target] = first
                give[:, target] = second

            @pl.when(y != column)
            def _(first=first, second=second, target=target):
                far[:, target] = first
                give_far[:, target] = second

    share = half // 2
    target = slice(half, half + share)
    for owner in range(2):
        lower = hidden_rows[:, owner * half : owner * half + share]
        upper = hidden_rows[:, owner * half + share : (owner + 1) * half]
        close = jnp.where(y == 0, lower, upper)
        distant = jnp.where(y == 0, upper, lower)

        @pl.when(core == owner)
        def _(close=close, distant=distant):
            near[:, target] = close
            far[:, target] = distant

        @pl.when(core != owner)
        def _(close=close, distant=distant):
            give[:, target] = close
            give_far[:, target] = distant

    for copy in before:
        copy.wait()
    if chunk == 0:
        out_ref[...] = held[0][...] + out_sum[...]
        d_two_ref[...] = two_sum[...]
    else:
        out_before, two_before, h_one, scale, w_out = held
        out_ref[...] = (out_before[...] + out_sum[...]).astype(bf16)
        d_norm, gain_term = norm_back(
            two_before[...] + two_sum[...], h_one[...], scale[...], gain_ref[...]
        )
        gain_term_ref[...] = jnp.sum(gain_term, axis=0, keepdims=True)
        d_h_one = d_ffn.astype(f32) + d_norm
        d_h_ref[...] = d_h_one
        d_attn = d_h_one.astype(bf16)
        d_attn_ref[...] = d_attn
        heads_ref[...] = contract(w_out[...], d_attn, (1, 1)).astype(bf16)


FFN_TILES = 3


def ffn(here, chunk, two, d_ffn, own, pieces, down, down_pieces, before, gain=None):
    tokens, width = two.shape
    columns = own.shape[2] // CHUNKS
    padded = (columns // 2 + columns // 4 + BLK - 1) // BLK * BLK
    shape = jax.ShapeDtypeStruct
    f32, bf16 = jnp.float32, jnp.bfloat16
    outs = [shape((tokens, padded), bf16)] * 4
    if chunk == 0:
        outs += [shape((tokens, width), f32)] * 2
    else:
        outs += [
            shape((tokens, width), bf16),
            shape((tokens, width), f32),
            shape((tokens, width), bf16),
            shape((width, tokens), bf16),
            shape((1, width), f32),
        ]
    far_away = pl.BlockSpec(memory_space=pl.ANY)
    arrays = [two, d_ffn, own, *pieces, down, *down_pieces, *before]
    specs = [whole(two), whole(d_ffn)] + [far_away] * (len(arrays) - 2)
    if gain is not None:
        arrays.append(gain)
        specs.append(whole(gain))
    got = call_with_here(
        functools.partial(ffn_kernel, chunk),
        here,
        (1,),
        arrays,
        specs,
        outs,
        [whole(o) for o in outs],
        [
            pltpu.VMEM((2, width, columns), bf16),
            pltpu.VMEM((columns, width), bf16),
            pltpu.VMEM((tokens, columns), bf16),
            pltpu.VMEM((tokens, width), f32),
            pltpu.VMEM((tokens, width), f32),
        ]
        + [pltpu.VMEM(v.shape, v.dtype) for v in before]
        + [
            pltpu.SemaphoreType.DMA((FFN_TILES, 9)),
            pltpu.SemaphoreType.DMA((FFN_TILES, 4)),
            pltpu.SemaphoreType.DMA((len(before),)),
        ],
        micros=FFN[chunk],
    )
    return got[:4], got[4:]


def wide_product_kernel(here, *refs):
    planes, terms = refs[:4], refs[4:8]
    sent, kept, left, right = refs[8:]
    tokens = planes[0].shape[1]
    columns = right.shape[1]
    for i in range(4):
        left[:, i * tokens : (i + 1) * tokens] = planes[i][...]
        right[i * tokens : (i + 1) * tokens, :] = terms[i][:, :columns]
    side = here[3]
    _, step, _ = kept.shape
    for half in range(2):
        for owner, out_ref in ((1 - side, sent), (side, kept)):
            place = pl.multiple_of(owner * 2 * step + half * step, step)
            out_ref[half] = jnp.dot(
                left[pl.ds(place, step), :], right[...], preferred_element_type=jnp.float32
            ).astype(out_ref.dtype)


def wide_products(here, two_plane, shares, columns):
    rows, tokens = two_plane[0].shape
    outs = [
        jax.ShapeDtypeStruct((2, rows // 4, columns), jnp.bfloat16),
        jax.ShapeDtypeStruct((2, rows // 4, columns), jnp.float32),
    ]
    arrays = [*two_plane, *shares]
    return call_with_here(
        wide_product_kernel,
        here,
        (1,),
        arrays,
        [whole(a) for a in two_plane]
        + [pl.BlockSpec((tokens, columns), lambda i, here: (0, 0))] * 4,
        outs,
        [whole(o) for o in outs],
        [
            pltpu.VMEM((rows, 4 * tokens), jnp.bfloat16),
            pltpu.VMEM((4 * tokens, columns), jnp.bfloat16),
        ],
        micros=3,
    )


def down_product_kernel(here, *refs):
    planes, terms = refs[:4], (refs[4:8], refs[8:12])
    sent, kept, left, right = refs[12:]
    tokens = planes[0].shape[0]
    rows = left.shape[0]
    for i in range(4):
        right[i * tokens : (i + 1) * tokens, :] = planes[i][...]
    for chunk in range(2):
        for i in range(4):
            share = terms[chunk][i]
            at = share.shape[1] // BLK * BLK - (rows + BLK - 1) // BLK * BLK
            left[:, i * tokens : (i + 1) * tokens] = share[:, at : at + rows].T
        for half in range(2):
            product = jnp.dot(
                left[half * rows // 2 : (half + 1) * rows // 2, :],
                right[...],
                preferred_element_type=jnp.float32,
            )

            @pl.when(here[3] == chunk)
            def _(product=product, half=half):
                kept[half] = product

            @pl.when(here[3] != chunk)
            def _(product=product, half=half):
                sent[half] = product.astype(sent.dtype)


def down_products(here, d_plane, first, second, rows):
    tokens, columns = d_plane[0].shape
    outs = [
        jax.ShapeDtypeStruct((2, rows // 2, columns), jnp.bfloat16),
        jax.ShapeDtypeStruct((2, rows // 2, columns), jnp.float32),
    ]
    return call_with_here(
        down_product_kernel,
        here,
        (1,),
        [*d_plane, *first, *second],
        [whole(a) for a in (*d_plane, *first, *second)],
        outs,
        [whole(o) for o in outs],
        [
            pltpu.VMEM((rows, 4 * tokens), jnp.bfloat16),
            pltpu.VMEM((4 * tokens, columns), jnp.bfloat16),
        ],
        micros=3,
    )


GAIN_ROWS = 16


def attention_back_kernel(here, *refs):
    d_ref, q_ref, k_ref, q_scale, k_scale, q_gain, k_gain, cos_ref, sin_ref = refs[:9]
    weight, x_ref, scale_ref, gain_ref, d_h_ref, d_attn_ref = refs[9:15]
    near, far, give, give_far, d_x_ref, gains_ref = refs[15:21]
    turned, natural = refs[21:]
    f32, bf16 = jnp.float32, jnp.bfloat16
    core, y = here[1], here[2]
    cosine, sine = cos_ref[...], sin_ref[...]
    half = HD // 2
    per_group = HEADS // KV_HEADS
    tokens = x_ref.shape[0]

    def back(grad, raw, scale, gain):
        first, second = grad[:half], grad[half:]
        normed = jnp.concatenate(
            [first * cosine + second * sine, second * cosine - first * sine], axis=0
        )
        return norm_back(normed, raw, scale, gain, 0)

    q_term = jnp.zeros((HD, tokens), f32)
    k_term = jnp.zeros((HD, tokens), f32)
    for head in range(HEADS):
        at = slice(head * HD, (head + 1) * HD)
        grad, term = back(
            d_ref[head, :HD, :].astype(f32), q_ref[at, :], q_scale[head : head + 1, :], q_gain[...]
        )
        turned[at, :] = grad.astype(bf16)
        q_term = q_term + term
    for head in range(KV_HEADS):
        at = slice(head * HD, (head + 1) * HD)
        both = d_ref[head * per_group, HD:, :].astype(f32)
        for other in range(1, per_group):
            both = both + d_ref[head * per_group + other, HD:, :].astype(f32)
        grad, term = back(both[:HD], k_ref[at, :], k_scale[head : head + 1, :], k_gain[...])
        place = HEADS * HD + head * HD
        turned[place : place + HD, :] = grad.astype(bf16)
        k_term = k_term + term
        place += KV_HEADS * HD
        turned[place : place + HD, :] = both[HD:].astype(bf16)
    rows = turned.shape[0] // 4
    columns = d_attn_ref.shape[1] // 4
    shares = ((near, core, y), (far, core, 1 - y), (give, 1 - core, y), (give_far, 1 - core, 1 - y))
    for out_ref, to_core, to_y in shares:
        share = to_core * 2 + to_y
        out_ref[:rows, :] = turned[pl.ds(pl.multiple_of(share * rows, rows), rows), :]
        out_ref[rows:, :] = d_attn_ref[:, pl.ds(pl.multiple_of(share * columns, columns), columns)]
    for at in range(0, turned.shape[0], 256):
        natural[:, at : at + 256] = turned[at : at + 256, :].T
    d_normed = contract(natural[...], weight[...], (1, 1))
    x = x_ref[...].astype(f32)
    d_norm, gain_term = norm_back(d_normed, x, scale_ref[...], gain_ref[...])
    d_x_ref[...] = d_h_ref[...] + d_norm
    gains_ref[...] = jnp.zeros_like(gains_ref)
    gains_ref[0:1, :] = jnp.sum(gain_term, axis=0, keepdims=True)
    gains_ref[1:2, 0:HD] = jnp.sum(q_term.T, axis=0, keepdims=True)
    gains_ref[2:3, 0:HD] = jnp.sum(k_term.T, axis=0, keepdims=True)


def attention_back(here, arrays):
    f32, bf16 = jnp.float32, jnp.bfloat16
    shape = jax.ShapeDtypeStruct
    weight, x = arrays[9], arrays[10]
    tokens, width = x.shape
    rows = weight.shape[1] // 4 + tokens
    assert width // 4 == tokens
    outs = [
        *[shape((rows, tokens), bf16)] * 4,
        shape((tokens, width), f32),
        shape((8, width), f32),
    ]
    return call_with_here(
        attention_back_kernel, here, (1,), arrays, [whole(a) for a in arrays], outs,
        [whole(o) for o in outs],
        [pltpu.VMEM((weight.shape[1], tokens), bf16), pltpu.VMEM((tokens, weight.shape[1]), bf16)],
        micros=12,
    )


def attention_product_kernel(here, *refs):
    planes, terms, gains_ref, ffn_gain_ref = refs[:4], refs[4:8], refs[8], refs[9]
    sent, kept, left, right, left_out, right_out = refs[10:]
    tokens = planes[0].shape[2]
    cut = right.shape[1]
    for i in range(4):
        at = slice(i * tokens, (i + 1) * tokens)
        left[:, at] = planes[i][0]
        left_out[:, at] = planes[i][1]
        share = terms[i]
        right[at, :] = share[:cut].T
        right_out[at, :] = share[cut:]
    step = left.shape[0] // 4
    for owner, out_ref in ((1 - here[3], sent), (here[3], kept)):
        for half in range(2):
            at = pl.ds(pl.multiple_of(owner * 2 * step + half * step, step), step)
            out_ref[half, :step, :cut] = jnp.dot(
                left[at, :], right[...], preferred_element_type=jnp.float32
            ).astype(out_ref.dtype)
            out_ref[half, :step, cut:] = jnp.dot(
                left_out[at, :], right_out[...], preferred_element_type=jnp.float32
            ).astype(out_ref.dtype)
        rows = gains_ref.shape[1] // 2
        mine = pl.ds(pl.multiple_of(owner * rows, rows), rows)
        wide = out_ref.shape[2] - rows
        block = jnp.concatenate(
            [
                jnp.concatenate([gains_ref[0:1, mine], gains_ref[1:2, 0:wide]], axis=1),
                jnp.concatenate([ffn_gain_ref[:, mine], gains_ref[2:3, 0:wide]], axis=1),
                jnp.zeros((GAIN_ROWS - 2, out_ref.shape[2]), jnp.float32),
            ],
            axis=0,
        )
        out_ref[0, step:, :] = block.astype(out_ref.dtype)
        out_ref[1, step:, :] = jnp.zeros((GAIN_ROWS, out_ref.shape[2]), out_ref.dtype)


def attention_products(here, pair_plane, shares, gains, ffn_gain):
    _, width, tokens = pair_plane[0].shape
    cut = shares[0].shape[0] - tokens
    shape = (2, width // 4 + GAIN_ROWS, cut + tokens)
    outs = [jax.ShapeDtypeStruct(shape, jnp.bfloat16), jax.ShapeDtypeStruct(shape, jnp.float32)]
    return call_with_here(
        attention_product_kernel,
        here,
        (1,),
        [*pair_plane, *shares, gains, ffn_gain],
        [whole(a) for a in (*pair_plane, *shares, gains, ffn_gain)],
        outs,
        [whole(o) for o in outs],
        [
            pltpu.VMEM((width, 4 * tokens), jnp.bfloat16),
            pltpu.VMEM((4 * tokens, cut), jnp.bfloat16),
            pltpu.VMEM((width, 4 * tokens), jnp.bfloat16),
            pltpu.VMEM((4 * tokens, tokens), jnp.bfloat16),
        ],
        micros=3,
    )


def place_gate_up_kernel(here, *refs):
    mine, across, beside, diagonal, out_ref = *refs[:4], refs[-1]
    pieces = (mine, across, beside, diagonal)
    wide = mine.shape[2]
    for case in range(4):
        core, y = case // 2, case % 2

        @pl.when((here[1] == core) & (here[2] == y))
        def _(core=core, y=y):
            for kind in range(2):
                for column in range(2):
                    value = pieces[(y ^ column) * 2 + (core ^ kind)][0]
                    out_ref[:, kind, column * wide : (column + 1) * wide] = value.astype(
                        jnp.float32
                    )


def place_gate_up(here, chunk, pieces, before):
    _, rows, wide = pieces[0].shape
    step = 64
    blocks = rows // step

    def source(i, here):
        return ((i // blocks) ^ here[0], i % blocks, 0)

    arrays = list(pieces)
    specs = [pl.BlockSpec((1, step, wide), source)] * 4
    aliases = {}
    if before is not None:
        arrays.append(before)
        specs.append(pl.BlockSpec(memory_space=pl.ANY))
        aliases = {5: 0}
    (out,) = call_with_here(
        place_gate_up_kernel,
        here,
        (2 * blocks,),
        arrays,
        specs,
        [jax.ShapeDtypeStruct((2 * rows, 2, 2 * wide * CHUNKS), jnp.float32)],
        [pl.BlockSpec((step, 2, 2 * wide), lambda i, here: (i, 0, chunk))],
        aliases=aliases,
        micros=10,
    )
    return out


def place_down(here, pieces):
    _, rows, columns = pieces[0].shape

    def kernel(here, *refs):
        for s in range(8):

            @pl.when(pl.program_id(0) == s)
            def _(s=s):
                refs[4][...] = refs[s % 4][s // 4].astype(jnp.float32)

    def target(s, here):
        half = (s // 4) ^ here[0]
        y = ((s // 2) % 2) ^ here[2]
        core = (s % 2) ^ here[1]
        return ((core * 2 + y) * 2 + half, 0)

    (out,) = call_with_here(
        kernel,
        here,
        (8,),
        list(pieces),
        [whole(v) for v in pieces],
        [jax.ShapeDtypeStruct((rows * 8, columns), jnp.float32)],
        [pl.BlockSpec((rows, columns), target)],
    )
    return out


def place_attention(here, pieces, cut):
    _, rows, columns = pieces[0].shape
    rows -= GAIN_ROWS

    def kernel(here, *refs):
        qkv_ref, out_ref, gains_ref = refs[4:]
        for s in range(8):

            @pl.when(pl.program_id(0) == s)
            def _(s=s):
                value = refs[s % 4][s // 4]
                qkv_ref[...] = value[:rows, :cut].astype(jnp.float32)
                out_ref[...] = value[:rows, cut:].astype(jnp.float32)
                gains = value[rows:].astype(jnp.float32)
                gains_ref[...] = gains if s == 0 else gains_ref[...] + gains

    def target(s, here):
        half = (s // 4) ^ here[0]
        return (half, ((s % 2) ^ here[1]) * 2 + (((s // 2) % 2) ^ here[2]))

    shape = jax.ShapeDtypeStruct
    f32 = jnp.float32
    gain_shape = (GAIN_ROWS, columns)
    return call_with_here(
        kernel,
        here,
        (8,),
        list(pieces),
        [whole(v) for v in pieces],
        [
            shape((2 * rows, 4 * cut), f32),
            shape((2 * rows, 4 * (columns - cut)), f32),
            shape(gain_shape, f32),
        ],
        [
            pl.BlockSpec((rows, cut), target),
            pl.BlockSpec((rows, columns - cut), target),
            pl.BlockSpec(gain_shape, lambda s, here: (0, 0)),
        ],
    )


def on_block(
    tokens,
    qkv_weight,
    out_weight,
    gate_up_weight,
    down_weight,
    attn_gain,
    ffn_gain,
    query_gain,
    key_gain,
    seq_lengths,
    block_order,
    cotangent,
):
    inputs = tokens[0].astype(jnp.float32)
    rows_here = inputs.shape[0]
    ctx_size = lax.axis_size("ctx")
    ctx_index = lax.axis_index("ctx")
    per_group = HEADS // KV_HEADS
    q_width = HEADS * HD
    kv_width = KV_HEADS * HD
    order_row = block_order[0]
    lengths_row = seq_lengths[0]
    slots = jnp.arange(rows_here, dtype=jnp.int32) // BLK + ctx_index * (rows_here // BLK)
    table = slots[:, None] == jnp.arange(order_row.shape[0], dtype=jnp.int32)[None, :]
    packed = (
        jnp.sum(jnp.where(table, order_row[None, :], 0), axis=1) * BLK
        + jnp.arange(rows_here, dtype=jnp.int32) % BLK
    )
    local = packed - starts_of(packed, lengths_row)
    frequency = ROPE_BASE ** (-2.0 * jnp.arange(HD // 2, dtype=jnp.float32) / HD)
    angle = frequency[:, None] * local.astype(jnp.float32)[None, :]
    cosine = jnp.cos(angle)[None]
    sine = jnp.sin(angle)[None]
    bf16, f32 = jnp.bfloat16, jnp.float32
    parts = ctx_size // HEADS
    part = ctx_index // HEADS
    part_blocks = HEADS * rows_here // BLK
    q_order = lax.dynamic_slice_in_dim(order_row, part * part_blocks, part_blocks)
    q_slot, q_place, q_start = block_tables(q_order, lengths_row)
    q_slot = q_slot + part * part_blocks
    kv_slot, _, _ = block_tables(order_row, lengths_row)
    first = jnp.min(q_start.reshape(-1, TILE), axis=1) // TILE
    last = jnp.max(q_place.reshape(-1, TILE), axis=1) // TILE + 1
    tables = (q_slot, kv_slot, first, last)
    q_rows, kv_rows = part_blocks * BLK, order_row.shape[0] * BLK

    links = Links(ctx_size)
    here = links.here
    width = inputs.shape[1]
    rows = qkv_weight.shape[0]
    part_rows = rows // 4

    def quarter_rows(weight):
        return lax.dynamic_slice_in_dim(weight, links.quarter * part_rows, part_rows)

    qkv_piece = quarter_rows(qkv_weight)
    gains_here = jnp.concatenate([after(attn_gain, qkv_piece), ffn_gain, query_gain, key_gain])
    gains_there = links.over_x(gains_here)

    def gain_of(at, size):
        mine, other = gains_here[at : at + size], gains_there[at : at + size]
        return jnp.where(
            links.side == 0, jnp.concatenate([mine, other]), jnp.concatenate([other, mine])
        ).astype(f32)

    gain_attn = gain_of(0, rows)
    gain_ffn = gain_of(rows, rows)
    gain_query = gain_of(2 * rows, HD // 2)
    gain_key = gain_of(2 * rows + HD // 2, HD // 2)
    ff_chunk = gate_up_weight.shape[2] // CHUNKS

    def gate_up_piece(chunk):
        piece = lax.dynamic_slice(
            gate_up_weight,
            (links.quarter * part_rows, 0, chunk * ff_chunk),
            (part_rows, 2, ff_chunk),
        )
        return [piece[:, 0], piece[:, 1]]

    d_ffn = cotangent[0]
    d_beside = links.over_y(d_ffn)
    qkv_there = after(links.over_x(qkv_piece), d_beside)
    first_piece = jnp.concatenate([*gate_up_piece(0), quarter_rows(out_weight)], axis=1)
    second_piece = jnp.concatenate(gate_up_piece(1), axis=1)
    down_piece = lax.dynamic_slice_in_dim(
        down_weight, links.quarter * (width // 4), width // 4, 1
    )
    d_ffn = cotangent[0]
    tokens_here = tokens[0]
    qkv_there = after(qkv_there, first_piece)
    first_there = links.over_x(after(first_piece, qkv_there))
    gate_up = jnp.transpose(after(gate_up_weight, qkv_there), (1, 0, 2))
    qkv_beside = links.over_y(qkv_there)
    qkv_pieces = (
        qkv_there,
        links.over_core(qkv_there),
        qkv_beside,
        links.over_core(after(qkv_beside, gate_up)),
    )
    sent, w_qkv, q_raw, k_raw, q_scale, k_scale, normed, scale_one = project(
        here, tokens_here, gain_attn[None], qkv_weight, qkv_pieces,
        gain_query[:, None], gain_key[:, None], cosine[0], sine[0],
    )
    got = lax.all_to_all(sent, "ctx", 0, 0, tiled=True)
    first_there = after(first_there, sent)
    down_there = links.over_x(after(down_piece, first_there))
    first_beside = links.over_y(first_there)
    q_place, q_start = q_place[None], q_start[None]
    shape = jax.ShapeDtypeStruct
    attn_sent, *held = kernel_call(
        attend_kernel,
        tables,
        (got, q_place, q_start),
        [
            shape((ctx_size, HD, rows_here), bf16),
            shape((q_rows, HD), bf16),
            shape((HD, q_rows), bf16),
            shape((kv_rows, HD), bf16),
            shape((HD, kv_rows), bf16),
            shape((kv_rows, HD), bf16),
            shape((HD, q_rows), f32),
            shape((1, q_rows), f32),
        ],
        [pltpu.VMEM((HD, kv_rows), bf16)],
        ATTEND,
    )
    attn_in = lax.dynamic_slice_in_dim(
        lax.all_to_all(attn_sent, "ctx", 0, 0, tiled=True), part * HEADS, HEADS
    ).reshape(q_width, rows_here)
    down_there = after(down_there, attn_sent)
    second_there = links.over_x(after(second_piece, down_there))
    down_beside = links.over_y(down_there)

    def spread(there, beside, time):
        there, beside = after(there, time), after(beside, time)
        return (there, links.over_core(there), beside, links.over_core(beside))

    first_pieces = spread(first_there, first_beside, attn_sent)
    down_pieces = spread(down_there, down_beside, attn_in)
    second_beside = links.over_y(second_there)
    w_out, h_one, scale_two, two, two_t = attend_out(
        here, attn_in, tokens_here, gain_ffn[None], out_weight, first_pieces
    )
    two_beside = links.over_y(two_t)
    dealt_here, (out_sum, two_sum) = ffn(
        here, 0, two, d_ffn, gate_up, first_pieces, down_weight, down_pieces, [h_one]
    )
    second_beside = after(second_beside, out_sum)
    second_pieces = (
        second_there, links.over_core(second_there), second_beside, links.over_core(second_beside)
    )
    near, far, give, give_far = dealt_here
    got_far = links.over_core(give_far)
    first_shares = (near, links.over_core(give), links.over_y(far), links.over_y(got_far))
    out_sum = after(out_sum, got_far)
    dealt_here, (output, d_h_one, d_attn, d_heads, ffn_gain_term) = ffn(
        here, 1, two, d_ffn, gate_up, second_pieces, down_weight, down_pieces,
        [out_sum, two_sum, h_one, scale_two, w_out], gain_ffn[None],
    )
    second_shares = links.deal_plane(*dealt_here)

    def plane(value, beside, time):
        value, beside = after(value, time), after(beside, time)
        return (value, links.over_core(value), beside, links.over_core(beside))

    columns = ff_chunk // 2
    d_heads = d_heads.reshape(HEADS, HD, rows_here)
    d_got = lax.all_to_all(d_heads, "ctx", 0, 0, tiled=True)
    pair = jnp.stack([after(normed, d_heads), attn_in])
    two_plane = plane(two_t, two_beside, pair)
    first_products = wide_products(
        here, two_plane, [after(v, d_heads) for v in first_shares], columns
    )
    d_got = after(d_got, first_products[0])
    (d_sent,) = kernel_call(
        attend_back_kernel,
        tables,
        (d_got, q_place, q_start, *held),
        [shape((ctx_size, 3 * HD, rows_here), bf16)],
        [
            pltpu.VMEM((HD, q_rows), bf16),
            pltpu.VMEM((q_rows, HD), bf16),
            pltpu.VMEM((kv_rows, HD), f32),
            pltpu.VMEM((kv_rows, HD), f32),
        ],
        ATTEND_BACK,
    )
    first_got = links.over_x(first_products[0])
    d_sent = after(d_sent, first_got, *second_shares[2:])
    d_back = lax.all_to_all(d_sent, "ctx", 0, 0, tiled=True)
    d_plane = plane(d_ffn, d_beside, d_sent)
    second_products = wide_products(
        here, two_plane, [after(v, d_plane[1]) for v in second_shares], columns
    )
    down_terms = down_products(
        here, d_plane, first_shares, second_shares, columns // 2
    )
    second_got = links.over_x(after(second_products[0], first_got))
    *d_shares, d_inputs, gain_sums = attention_back(
        here,
        [
            d_back, q_raw, k_raw, q_scale, k_scale, gain_query[:, None], gain_key[:, None],
            cosine[0], sine[0], w_qkv, tokens_here, scale_one, gain_attn[None], d_h_one, d_attn,
        ],
    )
    second_got = after(second_got, d_shares[0])
    near, far, give, give_far = d_shares
    got, got_far = links.over_core(give), links.over_core(give_far)
    attention_shares = (near, got, links.over_y(far), links.over_y(got_far))
    down_got = links.over_x(after(down_terms[0], second_got))
    pair_plane = plane(pair, links.over_y(after(pair, d_sent)), d_shares[0])
    attention_terms = attention_products(
        here, pair_plane, attention_shares, gain_sums, ffn_gain_term
    )
    first_pair = links.sum_depth(first_products[1], first_got, attention_shares[2])
    second_pair = links.sum_depth(second_products[1], second_got, attention_shares[3])
    down_pair = links.sum_depth(down_terms[1], after(down_got, got_far))
    attention_pair = links.sum_depth(attention_terms[1], links.over_x(attention_terms[0]))
    first_placed = place_gate_up(here, 0, links.spread_plane(first_pair), None)
    grad_gate_up = place_gate_up(here, 1, links.spread_plane(second_pair), first_placed)

    def spread_after(value, time):
        beside = after(links.over_y(value), time)
        return (value, links.over_core(value), beside, links.over_core(beside))

    grad_down = place_down(here, spread_after(down_pair, first_placed))
    cut = qkv_weight.shape[1] // 4
    grad_qkv, grad_out, gain_sums = place_attention(
        here, spread_after(attention_pair, grad_gate_up), cut
    )
    at = links.side * (HD // 2)
    gain_grads = [
        gain_sums[0, :rows],
        gain_sums[1, :rows],
        lax.dynamic_slice_in_dim(gain_sums[0, rows : rows + HD], at, HD // 2),
        lax.dynamic_slice_in_dim(gain_sums[1, rows : rows + HD], at, HD // 2),
    ]
    return (
        output[None],
        d_inputs[None],
        grad_qkv,
        grad_out,
        grad_gate_up,
        grad_down,
        *gain_grads,
    )


def on_device(
    tokens,
    qkv_weight,
    out_weight,
    gate_up_weight,
    down_weight,
    attn_gain,
    ffn_gain,
    query_gain,
    key_gain,
    seq_lengths,
    block_order,
    cotangent,
):
    inputs = tokens[0].astype(jnp.float32)
    rows_here = inputs.shape[0]
    ctx_size = lax.axis_size("ctx")
    ctx_index = lax.axis_index("ctx")
    per_group = HEADS // KV_HEADS
    q_width = HEADS * HD
    kv_width = KV_HEADS * HD
    order_row = block_order[0]
    lengths_row = seq_lengths[0]
    slots = jnp.arange(rows_here, dtype=jnp.int32) // BLK + ctx_index * (rows_here // BLK)
    table = slots[:, None] == jnp.arange(order_row.shape[0], dtype=jnp.int32)[None, :]
    packed = (
        jnp.sum(jnp.where(table, order_row[None, :], 0), axis=1) * BLK
        + jnp.arange(rows_here, dtype=jnp.int32) % BLK
    )
    local = packed - starts_of(packed, lengths_row)
    frequency = ROPE_BASE ** (-2.0 * jnp.arange(HD // 2, dtype=jnp.float32) / HD)
    angle = frequency[:, None] * local.astype(jnp.float32)[None, :]
    cosine = jnp.cos(angle)[None]
    sine = jnp.sin(angle)[None]
    bf16, f32 = jnp.bfloat16, jnp.float32
    parts = ctx_size // HEADS
    part = ctx_index // HEADS
    part_blocks = HEADS * rows_here // BLK
    q_order = lax.dynamic_slice_in_dim(order_row, part * part_blocks, part_blocks)
    q_slot, q_place, q_start = block_tables(q_order, lengths_row)
    q_slot = q_slot + part * part_blocks
    kv_slot, _, _ = block_tables(order_row, lengths_row)
    first = jnp.min(q_start.reshape(-1, TILE), axis=1) // TILE
    last = jnp.max(q_place.reshape(-1, TILE), axis=1) // TILE + 1
    tables = (q_slot, kv_slot, first, last)
    q_rows, kv_rows = part_blocks * BLK, order_row.shape[0] * BLK

    def fetch_attention():
        return (
            lax.all_gather(qkv_weight, "fsdp", axis=0, tiled=True),
            lax.all_gather(out_weight, "fsdp", axis=0, tiled=True),
            lax.all_gather(attn_gain, "fsdp", axis=0, tiled=True),
            lax.all_gather(ffn_gain, "fsdp", axis=0, tiled=True),
            lax.all_gather(query_gain, "fsdp", axis=0, tiled=True),
            lax.all_gather(key_gain, "fsdp", axis=0, tiled=True),
        )

    w_qkv, w_out, gain_attn, gain_ffn, gain_query, gain_key = fetch_attention()
    gain_attn = gain_attn.astype(jnp.float32)
    gain_ffn = gain_ffn.astype(jnp.float32)
    gain_query = gain_query.astype(jnp.float32)
    gain_key = gain_key.astype(jnp.float32)
    scale_one = rms_scale(inputs)
    normed = (inputs * scale_one * gain_attn).astype(jnp.bfloat16)
    projected = lax.dot_general(
        w_qkv, normed, (((0,), (1,)), ((), ())), preferred_element_type=f32
    )
    q_raw = projected[:q_width].reshape(HEADS, HD, rows_here)
    k_raw = projected[q_width : q_width + kv_width].reshape(KV_HEADS, HD, rows_here)
    values_here = projected[q_width + kv_width :].reshape(KV_HEADS, HD, rows_here).astype(bf16)
    q_scale = rms_scale(q_raw, 1)
    k_scale = rms_scale(k_raw, 1)
    column_query, column_key = gain_query[:, None], gain_key[:, None]
    queries = rope(q_raw * q_scale * column_query, cosine, sine).astype(bf16)
    keys_here = rope(k_raw * k_scale * column_key, cosine, sine).astype(bf16)
    sent = jnp.concatenate(
        [queries, jnp.repeat(keys_here, per_group, 0), jnp.repeat(values_here, per_group, 0)], axis=1
    )
    sent = jnp.concatenate([sent] * parts, axis=0)
    got = lax.all_to_all(sent, "ctx", 0, 0, tiled=True)
    q_place, q_start = q_place[None], q_start[None]
    shape = jax.ShapeDtypeStruct
    attn_sent, *held = kernel_call(
        attend_kernel,
        tables,
        (got, q_place, q_start),
        [
            shape((ctx_size, HD, rows_here), bf16),
            shape((q_rows, HD), bf16),
            shape((HD, q_rows), bf16),
            shape((kv_rows, HD), bf16),
            shape((HD, kv_rows), bf16),
            shape((kv_rows, HD), bf16),
            shape((HD, q_rows), f32),
            shape((1, q_rows), f32),
        ],
        [pltpu.VMEM((HD, kv_rows), bf16)],
        ATTEND,
    )
    attn_in = lax.dynamic_slice_in_dim(
        lax.all_to_all(attn_sent, "ctx", 0, 0, tiled=True), part * HEADS, HEADS
    ).reshape(q_width, rows_here)
    h_one = inputs + lax.dot_general(
        attn_in, w_out, (((0,), (0,)), ((), ())), preferred_element_type=f32
    )
    scale_two = rms_scale(h_one)
    normed_two = (h_one * scale_two * gain_ffn).astype(jnp.bfloat16)
    columns = normed_two
    gate_up = jnp.einsum(
        "tr,rgf->tgf",
        columns,
        lax.all_gather(gate_up_weight, "fsdp", axis=0, tiled=True),
        preferred_element_type=jnp.float32,
    )
    gate = gate_up[:, 0]
    upper = gate_up[:, 1]
    sigma = jax.nn.sigmoid(gate)
    hidden = (gate * sigma * upper).astype(jnp.bfloat16)
    columns = hidden
    ffn_out = jnp.dot(
        columns,
        lax.all_gather(down_weight, "fsdp", axis=0, tiled=True),
        preferred_element_type=jnp.float32,
    )
    output = (h_one + ffn_out).astype(jnp.bfloat16)
    d_out = cotangent[0].astype(jnp.float32)
    d_ffn = d_out.astype(jnp.bfloat16)
    d_hidden = lax.dot_general(
        d_ffn,
        lax.all_gather(down_weight, "fsdp", axis=0, tiled=True),
        (((1,), (1,)), ((), ())),
        preferred_element_type=jnp.float32,
    )
    d_gate = d_hidden * upper * sigma * (1.0 + gate * (1.0 - sigma))
    d_upper = d_hidden * gate * sigma
    d_gate_up = jnp.stack([d_gate, d_upper], axis=1).astype(jnp.bfloat16)
    d_normed_two = jnp.einsum(
        "tgf,rgf->tr",
        d_gate_up,
        lax.all_gather(gate_up_weight, "fsdp", axis=0, tiled=True),
        preferred_element_type=jnp.float32,
    )
    columns = normed_two
    grad_gate_up = lax.psum_scatter(
        jnp.einsum("tr,tgf->rgf", columns, d_gate_up, preferred_element_type=jnp.float32).astype(
            jnp.bfloat16
        ),
        "fsdp",
        scatter_dimension=0,
        tiled=True,
    )
    columns = hidden
    grad_down = lax.psum_scatter(
        lax.dot_general(
            columns, d_ffn, (((0,), (0,)), ((), ())), preferred_element_type=jnp.float32
        ).astype(jnp.bfloat16),
        "fsdp",
        scatter_dimension=0,
        tiled=True,
    )
    d_norm_two, ffn_gain_term = norm_back(d_normed_two, h_one, scale_two, gain_ffn)
    d_h_one = d_out + d_norm_two
    d_attn = d_h_one.astype(jnp.bfloat16)
    grad_out_here = jnp.dot(attn_in, d_attn, preferred_element_type=f32)
    d_heads = lax.dot_general(
        w_out, d_attn, (((1,), (1,)), ((), ())), preferred_element_type=f32
    ).astype(bf16)
    d_heads = jnp.concatenate([d_heads.reshape(HEADS, HD, rows_here)] * parts, axis=0)
    d_got = lax.all_to_all(d_heads, "ctx", 0, 0, tiled=True)
    (d_sent,) = kernel_call(
        attend_back_kernel,
        tables,
        (d_got, q_place, q_start, *held),
        [shape((ctx_size, 3 * HD, rows_here), bf16)],
        [
            pltpu.VMEM((HD, q_rows), bf16),
            pltpu.VMEM((q_rows, HD), bf16),
            pltpu.VMEM((kv_rows, HD), f32),
            pltpu.VMEM((kv_rows, HD), f32),
        ],
        ATTEND_BACK,
    )
    d_back = lax.all_to_all(d_sent, "ctx", 0, 0, tiled=True)
    d_query = lax.dynamic_slice_in_dim(d_back[:, :HD], part * HEADS, HEADS).astype(f32)
    d_key_value = jnp.sum(
        d_back[:, HD:].reshape(parts, KV_HEADS, per_group, 2 * HD, rows_here).astype(f32),
        axis=(0, 2),
    )
    dq_normed = rope_back(d_query, cosine, sine)
    dk_normed = rope_back(d_key_value[:, :HD], cosine, sine)
    dq_raw, query_term = norm_back(dq_normed, q_raw, q_scale, column_query, 1)
    dk_raw, key_term = norm_back(dk_normed, k_raw, k_scale, column_key, 1)
    d_projected = jnp.concatenate(
        [
            dq_raw.reshape(q_width, rows_here).astype(bf16),
            dk_raw.reshape(kv_width, rows_here).astype(bf16),
            d_key_value[:, HD:].reshape(kv_width, rows_here).astype(bf16),
        ],
        axis=0,
    )
    grad_qkv_here = lax.dot_general(
        normed, d_projected, (((0,), (1,)), ((), ())), preferred_element_type=f32
    )
    d_normed = lax.dot_general(
        d_projected, w_qkv, (((0,), (1,)), ((), ())), preferred_element_type=f32
    )
    d_norm_one, attn_gain_term = norm_back(d_normed, inputs, scale_one, gain_attn)
    d_inputs = d_h_one + d_norm_one
    shard_qkv, shard_out, shard_attn_gain, shard_ffn_gain, shard_query_gain, shard_key_gain = (
        lax.psum_scatter(
            grad_qkv_here.astype(jnp.bfloat16), "fsdp", scatter_dimension=0, tiled=True
        ).astype(jnp.float32),
        lax.psum_scatter(
            grad_out_here.astype(jnp.bfloat16), "fsdp", scatter_dimension=0, tiled=True
        ).astype(jnp.float32),
        lax.psum_scatter(
            jnp.sum(attn_gain_term, axis=0).astype(jnp.bfloat16),
            "fsdp",
            scatter_dimension=0,
            tiled=True,
        ).astype(jnp.float32),
        lax.psum_scatter(
            jnp.sum(ffn_gain_term, axis=0).astype(jnp.bfloat16),
            "fsdp",
            scatter_dimension=0,
            tiled=True,
        ).astype(jnp.float32),
        lax.psum_scatter(
            jnp.sum(query_term, axis=(0, 2)).astype(jnp.bfloat16),
            "fsdp",
            scatter_dimension=0,
            tiled=True,
        ).astype(jnp.float32),
        lax.psum_scatter(
            jnp.sum(key_term, axis=(0, 2)).astype(jnp.bfloat16),
            "fsdp",
            scatter_dimension=0,
            tiled=True,
        ).astype(jnp.float32),
    )
    summed_grads = (
        lax.psum(shard_qkv.astype(jnp.bfloat16), "ctx").astype(jnp.float32),
        lax.psum(shard_out.astype(jnp.bfloat16), "ctx").astype(jnp.float32),
        lax.psum(grad_gate_up, "ctx").astype(jnp.float32),
        lax.psum(grad_down, "ctx").astype(jnp.float32),
        lax.psum(shard_attn_gain.astype(jnp.bfloat16), "ctx").astype(jnp.float32),
        lax.psum(shard_ffn_gain.astype(jnp.bfloat16), "ctx").astype(jnp.float32),
        lax.psum(shard_query_gain.astype(jnp.bfloat16), "ctx").astype(jnp.float32),
        lax.psum(shard_key_gain.astype(jnp.bfloat16), "ctx").astype(jnp.float32),
    )
    return (
        output[None],
        d_inputs[None],
        summed_grads[0],
        summed_grads[1],
        summed_grads[2],
        summed_grads[3],
        summed_grads[4],
        summed_grads[5],
        summed_grads[6],
        summed_grads[7],
    )


def solution(mesh):
    block = mesh.shape["fsdp"] == 2 and mesh.shape["ctx"] == 16
    return jax.shard_map(
        on_block if block else on_device,
        mesh=mesh,
        in_specs=(
            P("fsdp", "ctx", None),
            P("fsdp", None),
            P("fsdp", None),
            P("fsdp", None, None),
            P("fsdp", None),
            P("fsdp"),
            P("fsdp"),
            P("fsdp"),
            P("fsdp"),
            P("fsdp", None),
            P("fsdp", None),
            P("fsdp", "ctx", None),
        ),
        out_specs=(
            P("fsdp", "ctx", None),
            P("fsdp", "ctx", None),
            P("fsdp", None),
            P("fsdp", None),
            P("fsdp", None, None),
            P("fsdp", None),
            P("fsdp"),
            P("fsdp"),
            P("fsdp"),
            P("fsdp"),
        ),
        check_vma=False,
    )
```

```python
import functools

import jax
import jax.numpy as jnp
from jax import lax
from jax.experimental import pallas as pl
from jax.experimental.pallas import tpu as pltpu
from jax.sharding import PartitionSpec as P

HEADS = 16
KV_HEADS = 8
HD = 64
BLK = 128
TILE = 256
CHUNKS = 2
PROJECT = 0
ATTEND = 0
OUT = 0
FFN = (0, 0)
ATTEND_BACK = 25


EPSILON = 1e-05
ROPE_BASE = 1000000.0
LOG2E = 1.4426950408889634
SCORE_SCALE = LOG2E * HD ** (-0.5)


def rms_scale(values, axis=-1):
    return lax.rsqrt(jnp.mean(values * values, axis=axis, keepdims=True) + EPSILON)


def norm_back(grad_normed, inputs, scale, gain, axis=-1):
    scaled = grad_normed * gain
    grad_in = scale * scaled - inputs * scale * scale * scale * jnp.mean(
        scaled * inputs, axis=axis, keepdims=True
    )
    return (grad_in, grad_normed * inputs * scale)


def rope(values, cosine, sine):
    half = HD // 2
    first, second = values[:, :half], values[:, half:]
    return jnp.concatenate([first * cosine - second * sine, second * cosine + first * sine], axis=1)


def rope_back(values, cosine, sine):
    half = HD // 2
    first, second = values[:, :half], values[:, half:]
    return jnp.concatenate([first * cosine + second * sine, second * cosine - first * sine], axis=1)


def starts_of(packed, lengths_row):
    ends = jnp.cumsum(lengths_row)
    past = packed[:, None] >= ends[None, :]
    return jnp.sum(jnp.where(past, lengths_row[None, :], 0), axis=1)


def block_tables(order, lengths_row):
    count = order.shape[0]
    rank = jnp.sum((order[None, :] < order[:, None]).astype(jnp.int32), axis=1)
    hit = rank[None, :] == jnp.arange(count, dtype=jnp.int32)[:, None]
    slot = jnp.sum(jnp.where(hit, jnp.arange(count, dtype=jnp.int32)[None, :], 0), axis=1)
    block = jnp.sum(jnp.where(hit, order[None, :], 0), axis=1)
    place = (block[:, None] * BLK + jnp.arange(BLK, dtype=jnp.int32)[None, :]).reshape(-1)
    return (slot, place, starts_of(place, lengths_row))


def attend_kernel(
    q_slot, kv_slot, first, last, qkv_ref, place_ref, start_ref,
    out_ref, q_ref, qt_ref, k_ref, kt_ref, v_ref, ot_ref, total_ref, vt_ref
):
    per_device = qkv_ref.shape[2] // BLK
    kv_blocks = k_ref.shape[0] // BLK
    q_blocks = q_ref.shape[0] // BLK

    def piece(slot, lower):
        return qkv_ref[
            slot // per_device,
            lower : lower + HD,
            pl.ds(pl.multiple_of((slot % per_device) * BLK, BLK), BLK),
        ]

    for i in range(kv_blocks):
        here = slice(i * BLK, (i + 1) * BLK)
        keys = piece(kv_slot[i], HD)
        kt_ref[:, here] = keys
        k_ref[here, :] = keys.T
        values = piece(kv_slot[i], 2 * HD)
        vt_ref[:, here] = values
        v_ref[here, :] = values.T
    for i in range(q_blocks):
        here = slice(i * BLK, (i + 1) * BLK)
        queries = piece(q_slot[i], 0)
        qt_ref[:, here] = queries
        q_ref[here, :] = queries.T
    if q_blocks < kv_blocks:
        out_ref[...] = jnp.zeros_like(out_ref)

    def tile(i, carry):
        rows = pl.ds(pl.multiple_of(i * TILE, TILE), TILE)
        queries = qt_ref[:, rows]
        place = place_ref[:, rows]
        start = start_ref[:, rows]

        def step(j, state):
            total, summed = state
            at = pl.multiple_of(j * TILE, TILE)
            scores = jnp.dot(
                k_ref[pl.ds(at, TILE), :], queries, preferred_element_type=jnp.float32
            )
            key_place = lax.broadcasted_iota(jnp.int32, (TILE, TILE), 0) + at
            allowed = (key_place <= place) & (key_place >= start)
            lifted = jnp.where(allowed, jnp.exp2(scores * SCORE_SCALE), 0.0)
            total = total + jnp.sum(lifted, axis=0, keepdims=True)
            summed = summed + jnp.dot(
                vt_ref[:, pl.ds(at, TILE)],
                lifted.astype(jnp.bfloat16),
                preferred_element_type=jnp.float32,
            )
            return (total, summed)

        total, summed = lax.fori_loop(
            first[i],
            last[i],
            step,
            (jnp.zeros((1, TILE), jnp.float32), jnp.zeros((HD, TILE), jnp.float32)),
        )
        attn = summed / total
        ot_ref[:, rows] = attn
        total_ref[:, rows] = jnp.log(total) * LOG2E
        rounded = attn.astype(jnp.bfloat16)
        for part in range(TILE // BLK):
            slot = q_slot[i * (TILE // BLK) + part]
            out_ref[
                slot // per_device,
                :,
                pl.ds(pl.multiple_of((slot % per_device) * BLK, BLK), BLK),
            ] = rounded[:, part * BLK : (part + 1) * BLK]
        return carry

    lax.fori_loop(0, q_blocks * BLK // TILE, tile, 0)


def attend_back_kernel(
    q_slot, kv_slot, first, last, d_ref, place_ref, start_ref,
    q_ref, qt_ref, k_ref, kt_ref, v_ref, ot_ref, total_ref,
    out_ref, dt_ref, do_ref, dk_ref, dv_ref
):
    per_device = d_ref.shape[2] // BLK
    kv_blocks = k_ref.shape[0] // BLK
    q_blocks = q_ref.shape[0] // BLK

    def lanes(slot):
        return pl.ds(pl.multiple_of((slot % per_device) * BLK, BLK), BLK)

    for i in range(q_blocks):
        here = slice(i * BLK, (i + 1) * BLK)
        slot = q_slot[i]
        grads = d_ref[slot // per_device, :, lanes(slot)]
        dt_ref[:, here] = grads
        do_ref[here, :] = grads.T
    dk_ref[...] = jnp.zeros_like(dk_ref)
    dv_ref[...] = jnp.zeros_like(dv_ref)
    if q_blocks < kv_blocks:
        out_ref[...] = jnp.zeros_like(out_ref)

    def tile(i, carry):
        rows = pl.ds(pl.multiple_of(i * TILE, TILE), TILE)
        queries = qt_ref[:, rows]
        grads = dt_ref[:, rows]
        place = place_ref[:, rows]
        start = start_ref[:, rows]
        delta = jnp.sum(grads.astype(jnp.float32) * ot_ref[:, rows], axis=0, keepdims=True)
        total = total_ref[:, rows]

        def step(j, d_query):
            at = pl.multiple_of(j * TILE, TILE)
            here = pl.ds(at, TILE)
            scores = jnp.dot(k_ref[here, :], queries, preferred_element_type=jnp.float32)
            key_place = lax.broadcasted_iota(jnp.int32, (TILE, TILE), 0) + at
            allowed = (key_place <= place) & (key_place >= start)
            shares = jnp.where(allowed, jnp.exp2(scores * SCORE_SCALE - total), 0.0)
            d_shares = jnp.dot(v_ref[here, :], grads, preferred_element_type=jnp.float32)
            d_scores = (shares * (d_shares - delta)).astype(jnp.bfloat16)
            dv_ref[here, :] += jnp.dot(
                shares.astype(jnp.bfloat16), do_ref[rows, :], preferred_element_type=jnp.float32
            )
            dk_ref[here, :] += jnp.dot(
                d_scores, q_ref[rows, :], preferred_element_type=jnp.float32
            )
            return d_query + jnp.dot(
                kt_ref[:, here], d_scores, preferred_element_type=jnp.float32
            )

        d_query = lax.fori_loop(first[i], last[i], step, jnp.zeros((HD, TILE), jnp.float32))
        rounded = (d_query * HD ** (-0.5)).astype(jnp.bfloat16)
        for part in range(TILE // BLK):
            slot = q_slot[i * (TILE // BLK) + part]
            out_ref[slot // per_device, 0:HD, lanes(slot)] = rounded[
                :, part * BLK : (part + 1) * BLK
            ]
        return carry

    lax.fori_loop(0, q_blocks * BLK // TILE, tile, 0)
    for i in range(kv_blocks):
        here = slice(i * BLK, (i + 1) * BLK)
        slot = kv_slot[i]
        out_ref[slot // per_device, HD : 2 * HD, lanes(slot)] = (
            (dk_ref[here, :] * HD ** (-0.5)).T.astype(jnp.bfloat16)
        )
        out_ref[slot // per_device, 2 * HD : 3 * HD, lanes(slot)] = (
            dv_ref[here, :].T.astype(jnp.bfloat16)
        )


def cost(micros):
    return pl.CostEstimate(
        flops=1 + micros * 1_000_000_000, bytes_accessed=1, transcendentals=0
    )


def kernel_call(kernel, tables, arrays, outs, scratch, micros):
    smem = pl.BlockSpec(memory_space=pltpu.SMEM)
    vmem = pl.BlockSpec(memory_space=pltpu.VMEM)
    return pl.pallas_call(
        kernel,
        out_shape=outs,
        in_specs=[smem] * len(tables) + [vmem] * len(arrays),
        out_specs=[vmem] * len(outs),
        scratch_shapes=scratch,
        compiler_params=pltpu.CompilerParams(vmem_limit_bytes=48 * 1024 * 1024),
        cost_estimate=cost(micros),
    )(*tables, *arrays)


class Links:
    def __init__(self, ctx_size):
        self.depth = ctx_size // 4
        index = lax.axis_index("ctx")
        self.core = index % 2
        self.y = (index // 2) % 2
        self.side = lax.axis_index("fsdp")
        self.half = index // 4 % 2
        self.quarter = index % 2 * 2 + self.y
        self.here = jnp.stack([self.half, self.core, self.y, self.side]).astype(jnp.int32)

    def route(self, place):
        pairs = []
        for z in range(self.depth):
            for y in range(2):
                for core in range(2):
                    to_z, to_y, to_core = place(z, y, core)
                    pairs.append(((z * 2 + y) * 2 + core, (to_z * 2 + to_y) * 2 + to_core))
        return pairs

    def over_core(self, value):
        return lax.ppermute(value, "ctx", self.route(lambda z, y, c: (z, y, 1 - c)))

    def over_y(self, value):
        return lax.ppermute(value, "ctx", self.route(lambda z, y, c: (z, 1 - y, c)))

    def over_z(self, value):
        return lax.ppermute(value, "ctx", self.route(lambda z, y, c: (z ^ 1, y, c)))

    def over_two_z(self, value):
        return lax.ppermute(value, "ctx", self.route(lambda z, y, c: (z ^ 2, y, c)))

    def over_x(self, value):
        return lax.ppermute(value, "fsdp", [(0, 1), (1, 0)])

    def spread_plane(self, value):
        across = self.over_core(value)
        beside = self.over_y(value)
        return (value, across, beside, self.over_core(beside))

    def deal_plane(self, near, far, give, give_far):
        got, got_far = self.over_core(give), self.over_core(give_far)
        return (near, got, self.over_y(far), self.over_y(got_far))

    def sum_depth(self, kept, got, time=None, last=None):
        def half(index):
            return add(pick(kept, index, 0), pick(got, index, 0))

        given = self.over_z(half(1 - self.half))
        part = add(half(self.half), given)
        other = self.over_two_z(part)
        full = add(part, other if time is None else after(other, *jax.tree.leaves(time)))
        other = self.over_z(full)
        return jnp.stack([full, other if last is None else after(other, last)])


def pick(value, index, axis):
    return lax.dynamic_index_in_dim(value, index, axis, keepdims=False)


def add(left, right):
    return (left.astype(jnp.float32) + right.astype(jnp.float32)).astype(jnp.bfloat16)


def after(value, *others):
    return lax.optimization_barrier((value, *others))[0]


def contract(left, right, axes):
    return lax.dot_general(
        left, right, ((axes[:1], axes[1:]), ((), ())), preferred_element_type=jnp.float32
    )


PARAMS = pltpu.CompilerParams(vmem_limit_bytes=56 * 1024 * 1024)


def call_with_here(
    kernel, here, grid, arrays, specs, outs, out_specs, scratch=(), aliases=None, micros=5
):
    return pl.pallas_call(
        kernel,
        grid_spec=pltpu.PrefetchScalarGridSpec(
            num_scalar_prefetch=1,
            grid=grid,
            in_specs=specs,
            out_specs=out_specs,
            scratch_shapes=list(scratch),
        ),
        out_shape=outs,
        input_output_aliases=aliases or {},
        compiler_params=PARAMS,
        cost_estimate=cost(micros),
    )(here, *arrays)


def whole(array):
    rank = len(array.shape)
    return pl.BlockSpec(array.shape, lambda i, here: (0,) * rank)


def project_kernel(here, *refs):
    x_ref, gain_ref, own_ref = refs[:3]
    pieces, q_gain, k_gain, cos_ref, sin_ref = refs[3:7], refs[7], refs[8], refs[9], refs[10]
    sent, weight, q_ref, k_ref, q_scale, k_scale, normed_ref, scale_ref = refs[11:]
    core, y, side = here[1], here[2], here[3]
    rows = own_ref.shape[0]
    part = rows // 4
    f32, bf16 = jnp.float32, jnp.bfloat16
    weight[pl.ds(pl.multiple_of(side * rows, rows), rows), :] = own_ref[...]
    for p in range(4):
        at = (1 - side) * rows + (((p % 2) ^ core) * 2 + ((p // 2) ^ y)) * part
        weight[pl.ds(pl.multiple_of(at, part), part), :] = pieces[p][...]
    x = x_ref[...].astype(f32)
    scale = rms_scale(x)
    scale_ref[...] = scale
    normed = (x * scale * gain_ref[...]).astype(bf16)
    normed_ref[...] = normed.T
    cosine, sine = cos_ref[...], sin_ref[...]
    half = HD // 2

    def turned(raw, gain, raw_ref, kept_scale, head):
        raw_ref[head * HD : (head + 1) * HD, :] = raw
        scale = rms_scale(raw, 0)
        kept_scale[head : head + 1, :] = scale
        value = raw * scale * gain
        first, second = value[:half], value[half:]
        return jnp.concatenate(
            [first * cosine - second * sine, second * cosine + first * sine], axis=0
        ).astype(bf16)

    per_group = HEADS // KV_HEADS
    for at in range(0, weight.shape[1], 2 * BLK):
        block = jnp.dot(normed, weight[:, at : at + 2 * BLK], preferred_element_type=f32)
        turned_block = block.T
        for n in range(2 * BLK // HD):
            head = at // HD + n
            raw = turned_block[n * HD : (n + 1) * HD, :]
            if head < HEADS:
                sent[head, 0:HD, :] = turned(raw, q_gain[...], q_ref, q_scale, head)
                continue
            head -= HEADS
            if head < KV_HEADS:
                value, row = turned(raw, k_gain[...], k_ref, k_scale, head), HD
            else:
                value, row, head = raw.astype(bf16), 2 * HD, head - KV_HEADS
            for copy in range(per_group):
                sent[head * per_group + copy, row : row + HD, :] = value


def project(here, x, gain, own, pieces, q_gain, k_gain, cosine, sine):
    tokens, width = x.shape
    f32, bf16 = jnp.float32, jnp.bfloat16
    shape = jax.ShapeDtypeStruct
    arrays = [x, gain, own, *pieces, q_gain, k_gain, cosine, sine]
    outs = [
        shape((HEADS, 3 * HD, tokens), bf16),
        shape((width, own.shape[1]), bf16),
        shape((HEADS * HD, tokens), f32),
        shape((KV_HEADS * HD, tokens), f32),
        shape((HEADS, tokens), f32),
        shape((KV_HEADS, tokens), f32),
        shape((width, tokens), bf16),
        shape((tokens, 1), f32),
    ]
    return call_with_here(
        project_kernel, here, (1,), arrays, [whole(a) for a in arrays], outs,
        [whole(o) for o in outs], micros=PROJECT,
    )


def layer(array, index):
    return pl.BlockSpec((1, *array.shape[1:]), lambda i, here: (index, 0, 0))


def attend_out_kernel(here, *refs):
    attn_ref, x_ref, gain_ref, own_ref = refs[:4]
    pieces = refs[4:12]
    weight, h_ref, scale_ref, two_ref, two_t_ref = refs[12:]
    core, y, side = here[1], here[2], here[3]
    rows = own_ref.shape[0]
    part = rows // 4
    weight[pl.ds(pl.multiple_of(side * rows, rows), rows), :] = own_ref[...]
    for p in range(4):
        at = (1 - side) * rows + (((p % 2) ^ core) * 2 + ((p // 2) ^ y)) * part
        for n in range(2):
            piece = pieces[2 * p + n]
            wide = piece.shape[1]
            weight[pl.ds(pl.multiple_of(at, part), part), n * wide : (n + 1) * wide] = piece[...]
    attn = attn_ref[...].T
    h_one = x_ref[...].astype(jnp.float32) + jnp.dot(
        attn, weight[...], preferred_element_type=jnp.float32
    )
    scale = rms_scale(h_one)
    h_ref[...] = h_one
    scale_ref[...] = scale
    two = (h_one * scale * gain_ref[...]).astype(jnp.bfloat16)
    two_ref[...] = two
    two_t_ref[...] = two.T


def attend_out(here, attn, x, gain, own, pieces):
    tokens, width = x.shape
    f32, bf16 = jnp.float32, jnp.bfloat16
    shape = jax.ShapeDtypeStruct
    part = own.shape[0] // 4
    half = width // 2
    first = pieces[0].shape[1] // half - 2
    arrays = [attn, x, gain, own]
    specs = [whole(a) for a in arrays]
    for piece in pieces:
        for n in range(2):
            arrays.append(piece)
            specs.append(pl.BlockSpec((part, half), lambda i, here, n=n: (0, first + n)))
    outs = [
        shape((width, width), bf16),
        shape((tokens, width), f32),
        shape((tokens, 1), f32),
        shape((tokens, width), bf16),
        shape((width, tokens), bf16),
    ]
    return call_with_here(
        attend_out_kernel, here, (1,), arrays, specs, outs, [whole(o) for o in outs], micros=OUT
    )


def ffn_kernel(chunk, here, *refs):
    two_ref, d_ref, own_ref = refs[:3]
    pieces, down_ref, down_pieces = refs[3:7], refs[7], refs[8:12]
    if chunk == 0:
        before_refs, refs = refs[12:13], refs[13:]
        near, far, give, give_far, out_ref, d_two_ref = refs[:6]
        refs = refs[6:]
    else:
        before_refs, gain_ref, refs = refs[12:17], refs[17], refs[18:]
        near, far, give, give_far = refs[:4]
        out_ref, d_h_ref, d_attn_ref, heads_ref, gain_term_ref = refs[4:9]
        refs = refs[9:]
    weight, down, hidden_rows, out_sum, two_sum = refs[:5]
    held, weight_sem, down_sem, before_sem = refs[5:-3], refs[-3], refs[-2], refs[-1]
    core, y, side = here[1], here[2], here[3]
    f32, bf16 = jnp.float32, jnp.bfloat16
    own_rows, columns = own_ref.shape[1], own_ref.shape[2] // CHUNKS
    part = own_rows // 4
    tile = columns // FFN_TILES
    half = columns // 2

    def quarter(p):
        return ((p % 2) ^ core) * 2 + ((p // 2) ^ y)

    def copies(n):
        at = slice(n * tile, (n + 1) * tile)
        mine = pl.ds(pl.multiple_of(side * own_rows, own_rows), own_rows)
        found = [
            pltpu.make_async_copy(
                own_ref.at[:, :, chunk * columns + n * tile : chunk * columns + (n + 1) * tile],
                weight.at[:, mine, at],
                weight_sem.at[n, 0],
            )
        ]
        for p in range(4):
            rows = pl.ds(pl.multiple_of((1 - side) * own_rows + quarter(p) * part, part), part)
            for kind in range(2):
                begin = kind * columns + n * tile
                found.append(
                    pltpu.make_async_copy(
                        pieces[p].at[:, begin : begin + tile],
                        weight.at[kind, rows, at],
                        weight_sem.at[n, 1 + 2 * p + kind],
                    )
                )
        return found

    def own_down(n):
        at = slice(n * tile, (n + 1) * tile)
        return [pltpu.make_async_copy(down_ref.at[at, :], down.at[at, :], down_sem.at[n, 0])]

    def other_down(n):
        at = slice(n * tile, (n + 1) * tile)
        found = []
        for p in range(4):
            wide = down_pieces[p].shape[1]
            lanes = pl.ds(pl.multiple_of(quarter(p) * wide, wide), wide)
            found.append(
                pltpu.make_async_copy(
                    down_pieces[p].at[at, :], down.at[at, lanes], down_sem.at[n, p]
                )
            )
        return found

    def each(action, n):
        for copy in copies(n):
            action(copy)

        @pl.when(side == chunk)
        def _():
            for copy in own_down(n):
                action(copy)

        @pl.when(side != chunk)
        def _():
            for copy in other_down(n):
                action(copy)

    before = [
        pltpu.make_async_copy(ref, held[n], before_sem.at[n]) for n, ref in enumerate(before_refs)
    ]
    for n in range(FFN_TILES):
        each(lambda copy: copy.start(), n)
    for copy in before:
        copy.start()
    two = two_ref[...]
    d_ffn = d_ref[...]
    for n in range(FFN_TILES):
        each(lambda copy: copy.wait(), n)
        at = slice(n * tile, (n + 1) * tile)
        gate = jnp.dot(two, weight[0, :, at], preferred_element_type=f32)
        upper = jnp.dot(two, weight[1, :, at], preferred_element_type=f32)
        d_hidden = contract(d_ffn, down[at, :], (1, 1))
        sigma = jax.nn.sigmoid(gate)
        silu = gate * sigma
        hidden = (silu * upper).astype(bf16)
        d_gate = (d_hidden * upper * sigma * (1.0 + gate * (1.0 - sigma))).astype(bf16)
        d_upper = (d_hidden * silu).astype(bf16)
        out_term = jnp.dot(hidden, down[at, :], preferred_element_type=f32)
        two_term = contract(d_gate, weight[0, :, at], (1, 1)) + contract(
            d_upper, weight[1, :, at], (1, 1)
        )
        out_sum[...] = out_term if n == 0 else out_sum[...] + out_term
        two_sum[...] = two_term if n == 0 else two_sum[...] + two_term
        hidden_rows[:, at] = hidden
        mine = jnp.where(core == 0, d_gate, d_upper)
        other = jnp.where(core == 0, d_upper, d_gate)
        for column in range(2):
            begin, end = max(n * tile, column * half), min((n + 1) * tile, (column + 1) * half)
            if begin >= end:
                continue
            source = slice(begin - n * tile, end - n * tile)
            target = slice(begin - column * half, end - column * half)
            first, second = mine[:, source], other[:, source]

            @pl.when(y == column)
            def _(first=first, second=second, target=target):
                near[:, target] = first
                give[:, target] = second

            @pl.when(y != column)
            def _(first=first, second=second, target=target):
                far[:, target] = first
                give_far[:, target] = second

    share = half // 2
    target = slice(half, half + share)
    for owner in range(2):
        lower = hidden_rows[:, owner * half : owner * half + share]
        upper = hidden_rows[:, owner * half + share : (owner + 1) * half]
        close = jnp.where(y == 0, lower, upper)
        distant = jnp.where(y == 0, upper, lower)

        @pl.when(core == owner)
        def _(close=close, distant=distant):
            near[:, target] = close
            far[:, target] = distant

        @pl.when(core != owner)
        def _(close=close, distant=distant):
            give[:, target] = close
            give_far[:, target] = distant

    for copy in before:
        copy.wait()
    if chunk == 0:
        out_ref[...] = held[0][...] + out_sum[...]
        d_two_ref[...] = two_sum[...]
    else:
        out_before, two_before, h_one, scale, w_out = held
        out_ref[...] = (out_before[...] + out_sum[...]).astype(bf16)
        d_norm, gain_term = norm_back(
            two_before[...] + two_sum[...], h_one[...], scale[...], gain_ref[...]
        )
        gain_term_ref[...] = jnp.sum(gain_term, axis=0, keepdims=True)
        d_h_one = d_ffn.astype(f32) + d_norm
        d_h_ref[...] = d_h_one
        d_attn = d_h_one.astype(bf16)
        d_attn_ref[...] = d_attn
        heads_ref[...] = contract(w_out[...], d_attn, (1, 1)).astype(bf16)


FFN_TILES = 3


def ffn(here, chunk, two, d_ffn, own, pieces, down, down_pieces, before, gain=None):
    tokens, width = two.shape
    columns = own.shape[2] // CHUNKS
    padded = (columns // 2 + columns // 4 + BLK - 1) // BLK * BLK
    shape = jax.ShapeDtypeStruct
    f32, bf16 = jnp.float32, jnp.bfloat16
    outs = [shape((tokens, padded), bf16)] * 4
    if chunk == 0:
        outs += [shape((tokens, width), f32)] * 2
    else:
        outs += [
            shape((tokens, width), bf16),
            shape((tokens, width), f32),
            shape((tokens, width), bf16),
            shape((width, tokens), bf16),
            shape((1, width), f32),
        ]
    far_away = pl.BlockSpec(memory_space=pl.ANY)
    arrays = [two, d_ffn, own, *pieces, down, *down_pieces, *before]
    specs = [whole(two), whole(d_ffn)] + [far_away] * (len(arrays) - 2)
    if gain is not None:
        arrays.append(gain)
        specs.append(whole(gain))
    got = call_with_here(
        functools.partial(ffn_kernel, chunk),
        here,
        (1,),
        arrays,
        specs,
        outs,
        [whole(o) for o in outs],
        [
            pltpu.VMEM((2, width, columns), bf16),
            pltpu.VMEM((columns, width), bf16),
            pltpu.VMEM((tokens, columns), bf16),
            pltpu.VMEM((tokens, width), f32),
            pltpu.VMEM((tokens, width), f32),
        ]
        + [pltpu.VMEM(v.shape, v.dtype) for v in before]
        + [
            pltpu.SemaphoreType.DMA((FFN_TILES, 9)),
            pltpu.SemaphoreType.DMA((FFN_TILES, 4)),
            pltpu.SemaphoreType.DMA((len(before),)),
        ],
        micros=FFN[chunk],
    )
    return got[:4], got[4:]


def wide_product_kernel(here, *refs):
    planes, terms = refs[:4], refs[4:8]
    sent, kept, left, right = refs[8:]
    tokens = planes[0].shape[1]
    columns = right.shape[1]
    for i in range(4):
        left[:, i * tokens : (i + 1) * tokens] = planes[i][...]
        right[i * tokens : (i + 1) * tokens, :] = terms[i][:, :columns]
    side = here[3]
    _, step, _ = kept.shape
    for half in range(2):
        for owner, out_ref in ((1 - side, sent), (side, kept)):
            place = pl.multiple_of(owner * 2 * step + half * step, step)
            out_ref[half] = jnp.dot(
                left[pl.ds(place, step), :], right[...], preferred_element_type=jnp.float32
            ).astype(out_ref.dtype)


def wide_products(here, two_plane, shares, columns):
    rows, tokens = two_plane[0].shape
    outs = [
        jax.ShapeDtypeStruct((2, rows // 4, columns), jnp.bfloat16),
        jax.ShapeDtypeStruct((2, rows // 4, columns), jnp.float32),
    ]
    arrays = [*two_plane, *shares]
    return call_with_here(
        wide_product_kernel,
        here,
        (1,),
        arrays,
        [whole(a) for a in two_plane]
        + [pl.BlockSpec((tokens, columns), lambda i, here: (0, 0))] * 4,
        outs,
        [whole(o) for o in outs],
        [
            pltpu.VMEM((rows, 4 * tokens), jnp.bfloat16),
            pltpu.VMEM((4 * tokens, columns), jnp.bfloat16),
        ],
        micros=3,
    )


def down_product_kernel(here, *refs):
    planes, terms = refs[:4], (refs[4:8], refs[8:12])
    sent, kept, left, right = refs[12:]
    tokens = planes[0].shape[0]
    rows = left.shape[0]
    for i in range(4):
        right[i * tokens : (i + 1) * tokens, :] = planes[i][...]
    for chunk in range(2):
        for i in range(4):
            share = terms[chunk][i]
            at = share.shape[1] // BLK * BLK - (rows + BLK - 1) // BLK * BLK
            left[:, i * tokens : (i + 1) * tokens] = share[:, at : at + rows].T
        for half in range(2):
            product = jnp.dot(
                left[half * rows // 2 : (half + 1) * rows // 2, :],
                right[...],
                preferred_element_type=jnp.float32,
            )

            @pl.when(here[3] == chunk)
            def _(product=product, half=half):
                kept[half] = product

            @pl.when(here[3] != chunk)
            def _(product=product, half=half):
                sent[half] = product.astype(sent.dtype)


def down_products(here, d_plane, first, second, rows):
    tokens, columns = d_plane[0].shape
    outs = [
        jax.ShapeDtypeStruct((2, rows // 2, columns), jnp.bfloat16),
        jax.ShapeDtypeStruct((2, rows // 2, columns), jnp.float32),
    ]
    return call_with_here(
        down_product_kernel,
        here,
        (1,),
        [*d_plane, *first, *second],
        [whole(a) for a in (*d_plane, *first, *second)],
        outs,
        [whole(o) for o in outs],
        [
            pltpu.VMEM((rows, 4 * tokens), jnp.bfloat16),
            pltpu.VMEM((4 * tokens, columns), jnp.bfloat16),
        ],
        micros=3,
    )


GAIN_ROWS = 16


def attention_back_kernel(here, *refs):
    d_ref, q_ref, k_ref, q_scale, k_scale, q_gain, k_gain, cos_ref, sin_ref = refs[:9]
    weight, x_ref, scale_ref, gain_ref, d_h_ref, d_attn_ref = refs[9:15]
    near, far, give, give_far, d_x_ref, gains_ref = refs[15:21]
    turned, natural = refs[21:]
    f32, bf16 = jnp.float32, jnp.bfloat16
    core, y = here[1], here[2]
    cosine, sine = cos_ref[...], sin_ref[...]
    half = HD // 2
    per_group = HEADS // KV_HEADS
    tokens = x_ref.shape[0]

    def back(grad, raw, scale, gain):
        first, second = grad[:half], grad[half:]
        normed = jnp.concatenate(
            [first * cosine + second * sine, second * cosine - first * sine], axis=0
        )
        return norm_back(normed, raw, scale, gain, 0)

    q_term = jnp.zeros((HD, tokens), f32)
    k_term = jnp.zeros((HD, tokens), f32)
    for head in range(HEADS):
        at = slice(head * HD, (head + 1) * HD)
        grad, term = back(
            d_ref[head, :HD, :].astype(f32), q_ref[at, :], q_scale[head : head + 1, :], q_gain[...]
        )
        turned[at, :] = grad.astype(bf16)
        q_term = q_term + term
    for head in range(KV_HEADS):
        at = slice(head * HD, (head + 1) * HD)
        both = d_ref[head * per_group, HD:, :].astype(f32)
        for other in range(1, per_group):
            both = both + d_ref[head * per_group + other, HD:, :].astype(f32)
        grad, term = back(both[:HD], k_ref[at, :], k_scale[head : head + 1, :], k_gain[...])
        place = HEADS * HD + head * HD
        turned[place : place + HD, :] = grad.astype(bf16)
        k_term = k_term + term
        place += KV_HEADS * HD
        turned[place : place + HD, :] = both[HD:].astype(bf16)
    rows = turned.shape[0] // 4
    columns = d_attn_ref.shape[1] // 4
    shares = ((near, core, y), (far, core, 1 - y), (give, 1 - core, y), (give_far, 1 - core, 1 - y))
    for out_ref, to_core, to_y in shares:
        share = to_core * 2 + to_y
        out_ref[:rows, :] = turned[pl.ds(pl.multiple_of(share * rows, rows), rows), :]
        out_ref[rows:, :] = d_attn_ref[:, pl.ds(pl.multiple_of(share * columns, columns), columns)]
    for at in range(0, turned.shape[0], 256):
        natural[:, at : at + 256] = turned[at : at + 256, :].T
    d_normed = contract(natural[...], weight[...], (1, 1))
    x = x_ref[...].astype(f32)
    d_norm, gain_term = norm_back(d_normed, x, scale_ref[...], gain_ref[...])
    d_x_ref[...] = d_h_ref[...] + d_norm
    gains_ref[...] = jnp.zeros_like(gains_ref)
    gains_ref[0:1, :] = jnp.sum(gain_term, axis=0, keepdims=True)
    gains_ref[1:2, 0:HD] = jnp.sum(q_term.T, axis=0, keepdims=True)
    gains_ref[2:3, 0:HD] = jnp.sum(k_term.T, axis=0, keepdims=True)


def attention_back(here, arrays):
    f32, bf16 = jnp.float32, jnp.bfloat16
    shape = jax.ShapeDtypeStruct
    weight, x = arrays[9], arrays[10]
    tokens, width = x.shape
    rows = weight.shape[1] // 4 + tokens
    assert width // 4 == tokens
    outs = [
        *[shape((rows, tokens), bf16)] * 4,
        shape((tokens, width), f32),
        shape((8, width), f32),
    ]
    return call_with_here(
        attention_back_kernel, here, (1,), arrays, [whole(a) for a in arrays], outs,
        [whole(o) for o in outs],
        [pltpu.VMEM((weight.shape[1], tokens), bf16), pltpu.VMEM((tokens, weight.shape[1]), bf16)],
        micros=12,
    )


def attention_product_kernel(here, *refs):
    planes, terms, gains_ref, ffn_gain_ref = refs[:4], refs[4:8], refs[8], refs[9]
    sent, kept, left, right, left_out, right_out = refs[10:]
    tokens = planes[0].shape[2]
    cut = right.shape[1]
    for i in range(4):
        at = slice(i * tokens, (i + 1) * tokens)
        left[:, at] = planes[i][0]
        left_out[:, at] = planes[i][1]
        share = terms[i]
        right[at, :] = share[:cut].T
        right_out[at, :] = share[cut:]
    step = left.shape[0] // 4
    for owner, out_ref in ((1 - here[3], sent), (here[3], kept)):
        for half in range(2):
            at = pl.ds(pl.multiple_of(owner * 2 * step + half * step, step), step)
            out_ref[half, :step, :cut] = jnp.dot(
                left[at, :], right[...], preferred_element_type=jnp.float32
            ).astype(out_ref.dtype)
            out_ref[half, :step, cut:] = jnp.dot(
                left_out[at, :], right_out[...], preferred_element_type=jnp.float32
            ).astype(out_ref.dtype)
        rows = gains_ref.shape[1] // 2
        mine = pl.ds(pl.multiple_of(owner * rows, rows), rows)
        wide = out_ref.shape[2] - rows
        block = jnp.concatenate(
            [
                jnp.concatenate([gains_ref[0:1, mine], gains_ref[1:2, 0:wide]], axis=1),
                jnp.concatenate([ffn_gain_ref[:, mine], gains_ref[2:3, 0:wide]], axis=1),
                jnp.zeros((GAIN_ROWS - 2, out_ref.shape[2]), jnp.float32),
            ],
            axis=0,
        )
        out_ref[0, step:, :] = block.astype(out_ref.dtype)
        out_ref[1, step:, :] = jnp.zeros((GAIN_ROWS, out_ref.shape[2]), out_ref.dtype)


def attention_products(here, pair_plane, shares, gains, ffn_gain):
    _, width, tokens = pair_plane[0].shape
    cut = shares[0].shape[0] - tokens
    shape = (2, width // 4 + GAIN_ROWS, cut + tokens)
    outs = [jax.ShapeDtypeStruct(shape, jnp.bfloat16), jax.ShapeDtypeStruct(shape, jnp.float32)]
    return call_with_here(
        attention_product_kernel,
        here,
        (1,),
        [*pair_plane, *shares, gains, ffn_gain],
        [whole(a) for a in (*pair_plane, *shares, gains, ffn_gain)],
        outs,
        [whole(o) for o in outs],
        [
            pltpu.VMEM((width, 4 * tokens), jnp.bfloat16),
            pltpu.VMEM((4 * tokens, cut), jnp.bfloat16),
            pltpu.VMEM((width, 4 * tokens), jnp.bfloat16),
            pltpu.VMEM((4 * tokens, tokens), jnp.bfloat16),
        ],
        micros=3,
    )


def place_gate_up_kernel(here, *refs):
    mine, across, beside, diagonal, out_ref = *refs[:4], refs[-1]
    pieces = (mine, across, beside, diagonal)
    wide = mine.shape[2]
    for case in range(4):
        core, y = case // 2, case % 2

        @pl.when((here[1] == core) & (here[2] == y))
        def _(core=core, y=y):
            for kind in range(2):
                for column in range(2):
                    value = pieces[(y ^ column) * 2 + (core ^ kind)][0]
                    out_ref[:, kind, column * wide : (column + 1) * wide] = value.astype(
                        jnp.float32
                    )


def place_gate_up(here, chunk, pieces, before):
    _, rows, wide = pieces[0].shape
    step = 64
    blocks = rows // step

    def source(i, here):
        return ((i // blocks) ^ here[0], i % blocks, 0)

    arrays = list(pieces)
    specs = [pl.BlockSpec((1, step, wide), source)] * 4
    aliases = {}
    if before is not None:
        arrays.append(before)
        specs.append(pl.BlockSpec(memory_space=pl.ANY))
        aliases = {5: 0}
    (out,) = call_with_here(
        place_gate_up_kernel,
        here,
        (2 * blocks,),
        arrays,
        specs,
        [jax.ShapeDtypeStruct((2 * rows, 2, 2 * wide * CHUNKS), jnp.float32)],
        [pl.BlockSpec((step, 2, 2 * wide), lambda i, here: (i, 0, chunk))],
        aliases=aliases,
        micros=10,
    )
    return out


def place_down(here, pieces):
    _, rows, columns = pieces[0].shape

    def kernel(here, *refs):
        for s in range(8):

            @pl.when(pl.program_id(0) == s)
            def _(s=s):
                refs[4][...] = refs[s % 4][s // 4].astype(jnp.float32)

    def target(s, here):
        half = (s // 4) ^ here[0]
        y = ((s // 2) % 2) ^ here[2]
        core = (s % 2) ^ here[1]
        return ((core * 2 + y) * 2 + half, 0)

    (out,) = call_with_here(
        kernel,
        here,
        (8,),
        list(pieces),
        [whole(v) for v in pieces],
        [jax.ShapeDtypeStruct((rows * 8, columns), jnp.float32)],
        [pl.BlockSpec((rows, columns), target)],
    )
    return out


def place_attention(here, pieces, cut):
    _, rows, columns = pieces[0].shape
    rows -= GAIN_ROWS

    def kernel(here, *refs):
        qkv_ref, out_ref, gains_ref = refs[4:]
        for s in range(8):

            @pl.when(pl.program_id(0) == s)
            def _(s=s):
                value = refs[s % 4][s // 4]
                qkv_ref[...] = value[:rows, :cut].astype(jnp.float32)
                out_ref[...] = value[:rows, cut:].astype(jnp.float32)
                gains = value[rows:].astype(jnp.float32)
                gains_ref[...] = gains if s == 0 else gains_ref[...] + gains

    def target(s, here):
        half = (s // 4) ^ here[0]
        return (half, ((s % 2) ^ here[1]) * 2 + (((s // 2) % 2) ^ here[2]))

    shape = jax.ShapeDtypeStruct
    f32 = jnp.float32
    gain_shape = (GAIN_ROWS, columns)
    return call_with_here(
        kernel,
        here,
        (8,),
        list(pieces),
        [whole(v) for v in pieces],
        [
            shape((2 * rows, 4 * cut), f32),
            shape((2 * rows, 4 * (columns - cut)), f32),
            shape(gain_shape, f32),
        ],
        [
            pl.BlockSpec((rows, cut), target),
            pl.BlockSpec((rows, columns - cut), target),
            pl.BlockSpec(gain_shape, lambda s, here: (0, 0)),
        ],
    )


def on_block(
    tokens,
    qkv_weight,
    out_weight,
    gate_up_weight,
    down_weight,
    attn_gain,
    ffn_gain,
    query_gain,
    key_gain,
    seq_lengths,
    block_order,
    cotangent,
):
    inputs = tokens[0].astype(jnp.float32)
    rows_here = inputs.shape[0]
    ctx_size = lax.axis_size("ctx")
    ctx_index = lax.axis_index("ctx")
    per_group = HEADS // KV_HEADS
    q_width = HEADS * HD
    kv_width = KV_HEADS * HD
    order_row = block_order[0]
    lengths_row = seq_lengths[0]
    slots = jnp.arange(rows_here, dtype=jnp.int32) // BLK + ctx_index * (rows_here // BLK)
    table = slots[:, None] == jnp.arange(order_row.shape[0], dtype=jnp.int32)[None, :]
    packed = (
        jnp.sum(jnp.where(table, order_row[None, :], 0), axis=1) * BLK
        + jnp.arange(rows_here, dtype=jnp.int32) % BLK
    )
    local = packed - starts_of(packed, lengths_row)
    frequency = ROPE_BASE ** (-2.0 * jnp.arange(HD // 2, dtype=jnp.float32) / HD)
    angle = frequency[:, None] * local.astype(jnp.float32)[None, :]
    cosine = jnp.cos(angle)[None]
    sine = jnp.sin(angle)[None]
    bf16, f32 = jnp.bfloat16, jnp.float32
    parts = ctx_size // HEADS
    part = ctx_index // HEADS
    part_blocks = HEADS * rows_here // BLK
    q_order = lax.dynamic_slice_in_dim(order_row, part * part_blocks, part_blocks)
    q_slot, q_place, q_start = block_tables(q_order, lengths_row)
    q_slot = q_slot + part * part_blocks
    kv_slot, _, _ = block_tables(order_row, lengths_row)
    first = jnp.min(q_start.reshape(-1, TILE), axis=1) // TILE
    last = jnp.max(q_place.reshape(-1, TILE), axis=1) // TILE + 1
    tables = (q_slot, kv_slot, first, last)
    q_rows, kv_rows = part_blocks * BLK, order_row.shape[0] * BLK

    links = Links(ctx_size)
    here = links.here
    width = inputs.shape[1]
    rows = qkv_weight.shape[0]
    part_rows = rows // 4

    def quarter_rows(weight):
        return lax.dynamic_slice_in_dim(weight, links.quarter * part_rows, part_rows)

    qkv_piece = quarter_rows(qkv_weight)
    gains_here = jnp.concatenate([after(attn_gain, qkv_piece), ffn_gain, query_gain, key_gain])
    gains_there = links.over_x(gains_here)

    def gain_of(at, size):
        mine, other = gains_here[at : at + size], gains_there[at : at + size]
        return jnp.where(
            links.side == 0, jnp.concatenate([mine, other]), jnp.concatenate([other, mine])
        ).astype(f32)

    gain_attn = gain_of(0, rows)
    gain_ffn = gain_of(rows, rows)
    gain_query = gain_of(2 * rows, HD // 2)
    gain_key = gain_of(2 * rows + HD // 2, HD // 2)
    ff_chunk = gate_up_weight.shape[2] // CHUNKS

    def gate_up_piece(chunk):
        piece = lax.dynamic_slice(
            gate_up_weight,
            (links.quarter * part_rows, 0, chunk * ff_chunk),
            (part_rows, 2, ff_chunk),
        )
        return [piece[:, 0], piece[:, 1]]

    d_ffn = cotangent[0]
    d_beside = links.over_y(d_ffn)
    qkv_there = after(links.over_x(qkv_piece), d_beside)
    first_piece = jnp.concatenate([*gate_up_piece(0), quarter_rows(out_weight)], axis=1)
    second_piece = jnp.concatenate(gate_up_piece(1), axis=1)
    down_piece = lax.dynamic_slice_in_dim(
        down_weight, links.quarter * (width // 4), width // 4, 1
    )
    d_ffn = cotangent[0]
    tokens_here = tokens[0]
    qkv_there = after(qkv_there, first_piece)
    first_there = links.over_x(after(first_piece, qkv_there))
    gate_up = jnp.transpose(after(gate_up_weight, qkv_there), (1, 0, 2))
    qkv_beside = links.over_y(qkv_there)
    qkv_pieces = (
        qkv_there,
        links.over_core(qkv_there),
        qkv_beside,
        links.over_core(after(qkv_beside, gate_up)),
    )
    sent, w_qkv, q_raw, k_raw, q_scale, k_scale, normed, scale_one = project(
        here, tokens_here, gain_attn[None], qkv_weight, qkv_pieces,
        gain_query[:, None], gain_key[:, None], cosine[0], sine[0],
    )
    got = lax.all_to_all(sent, "ctx", 0, 0, tiled=True)
    first_there = after(first_there, sent)
    down_there = links.over_x(after(down_piece, first_there))
    first_beside = links.over_y(first_there)
    q_place, q_start = q_place[None], q_start[None]
    shape = jax.ShapeDtypeStruct
    attn_sent, *held = kernel_call(
        attend_kernel,
        tables,
        (got, q_place, q_start),
        [
            shape((ctx_size, HD, rows_here), bf16),
            shape((q_rows, HD), bf16),
            shape((HD, q_rows), bf16),
            shape((kv_rows, HD), bf16),
            shape((HD, kv_rows), bf16),
            shape((kv_rows, HD), bf16),
            shape((HD, q_rows), f32),
            shape((1, q_rows), f32),
        ],
        [pltpu.VMEM((HD, kv_rows), bf16)],
        ATTEND,
    )
    attn_in = lax.dynamic_slice_in_dim(
        lax.all_to_all(attn_sent, "ctx", 0, 0, tiled=True), part * HEADS, HEADS
    ).reshape(q_width, rows_here)
    down_there = after(down_there, attn_sent)
    second_there = links.over_x(after(second_piece, down_there))
    down_beside = links.over_y(down_there)

    def spread(there, beside, time):
        there, beside = after(there, time), after(beside, time)
        return (there, links.over_core(there), beside, links.over_core(beside))

    first_pieces = spread(first_there, first_beside, attn_sent)
    down_pieces = spread(down_there, down_beside, attn_in)
    second_beside = links.over_y(second_there)
    w_out, h_one, scale_two, two, two_t = attend_out(
        here, attn_in, tokens_here, gain_ffn[None], out_weight, first_pieces
    )
    two_beside = links.over_y(two_t)
    dealt_here, (out_sum, two_sum) = ffn(
        here, 0, two, d_ffn, gate_up, first_pieces, down_weight, down_pieces, [h_one]
    )
    second_beside = after(second_beside, out_sum)
    second_pieces = (
        second_there, links.over_core(second_there), second_beside, links.over_core(second_beside)
    )
    near, far, give, give_far = dealt_here
    got_far = links.over_core(give_far)
    first_shares = (near, links.over_core(give), links.over_y(far), links.over_y(got_far))
    out_sum = after(out_sum, got_far)
    dealt_here, (output, d_h_one, d_attn, d_heads, ffn_gain_term) = ffn(
        here, 1, two, d_ffn, gate_up, second_pieces, down_weight, down_pieces,
        [out_sum, two_sum, h_one, scale_two, w_out], gain_ffn[None],
    )
    second_shares = links.deal_plane(*dealt_here)

    def plane(value, beside, time):
        value, beside = after(value, time), after(beside, time)
        return (value, links.over_core(value), beside, links.over_core(beside))

    columns = ff_chunk // 2
    d_heads = d_heads.reshape(HEADS, HD, rows_here)
    d_got = lax.all_to_all(d_heads, "ctx", 0, 0, tiled=True)
    pair = jnp.stack([after(normed, d_heads), attn_in])
    two_plane = plane(two_t, two_beside, pair)
    first_products = wide_products(
        here, two_plane, [after(v, d_heads) for v in first_shares], columns
    )
    d_got = after(d_got, first_products[0])
    (d_sent,) = kernel_call(
        attend_back_kernel,
        tables,
        (d_got, q_place, q_start, *held),
        [shape((ctx_size, 3 * HD, rows_here), bf16)],
        [
            pltpu.VMEM((HD, q_rows), bf16),
            pltpu.VMEM((q_rows, HD), bf16),
            pltpu.VMEM((kv_rows, HD), f32),
            pltpu.VMEM((kv_rows, HD), f32),
        ],
        ATTEND_BACK,
    )
    first_got = links.over_x(first_products[0])
    d_sent = after(d_sent, first_got, *second_shares[2:])
    d_back = lax.all_to_all(d_sent, "ctx", 0, 0, tiled=True)
    d_plane = plane(d_ffn, d_beside, d_sent)
    second_products = wide_products(
        here, two_plane, [after(v, d_plane[1]) for v in second_shares], columns
    )
    down_terms = down_products(
        here, d_plane, first_shares, second_shares, columns // 2
    )
    second_got = links.over_x(after(second_products[0], first_got))
    pair_beside = links.over_y(after(pair, d_sent))
    d_back = after(d_back, down_terms[0], pair_beside, second_got)
    *d_shares, d_inputs, gain_sums = attention_back(
        here,
        [
            d_back, q_raw, k_raw, q_scale, k_scale, gain_query[:, None], gain_key[:, None],
            cosine[0], sine[0], w_qkv, tokens_here, scale_one, gain_attn[None], d_h_one, d_attn,
        ],
    )
    down_got = links.over_x(after(down_terms[0], second_got))
    near, far, give, give_far = d_shares
    second_got = after(second_got, d_shares[0])
    got, got_far = links.over_core(give), links.over_core(give_far)
    attention_shares = (near, got, links.over_y(far), links.over_y(got_far))
    pair_plane = plane(pair, pair_beside, d_sent)
    attention_terms = attention_products(
        here, pair_plane, attention_shares, gain_sums, ffn_gain_term
    )
    first_pair = links.sum_depth(first_products[1], first_got, (*attention_shares[1:], down_got, pair_plane[3]), attention_terms[0])
    second_pair = links.sum_depth(second_products[1], second_got, attention_shares[3])
    attention_pair = links.sum_depth(attention_terms[1], links.over_x(attention_terms[0]))
    first_placed = place_gate_up(here, 0, links.spread_plane(first_pair), None)
    down_pair = links.sum_depth(down_terms[1], after(down_got, got_far), first_placed)
    grad_gate_up = place_gate_up(here, 1, links.spread_plane(second_pair), first_placed)

    def spread_after(value, time):
        beside = after(links.over_y(value), time)
        return (value, links.over_core(value), beside, links.over_core(beside))

    grad_down = place_down(here, spread_after(down_pair, first_placed))
    cut = qkv_weight.shape[1] // 4
    grad_qkv, grad_out, gain_sums = place_attention(
        here, spread_after(attention_pair, grad_gate_up), cut
    )
    at = links.side * (HD // 2)
    gain_grads = [
        gain_sums[0, :rows],
        gain_sums[1, :rows],
        lax.dynamic_slice_in_dim(gain_sums[0, rows : rows + HD], at, HD // 2),
        lax.dynamic_slice_in_dim(gain_sums[1, rows : rows + HD], at, HD // 2),
    ]
    return (
        output[None],
        d_inputs[None],
        grad_qkv,
        grad_out,
        grad_gate_up,
        grad_down,
        *gain_grads,
    )


def on_device(
    tokens,
    qkv_weight,
    out_weight,
    gate_up_weight,
    down_weight,
    attn_gain,
    ffn_gain,
    query_gain,
    key_gain,
    seq_lengths,
    block_order,
    cotangent,
):
    inputs = tokens[0].astype(jnp.float32)
    rows_here = inputs.shape[0]
    ctx_size = lax.axis_size("ctx")
    ctx_index = lax.axis_index("ctx")
    per_group = HEADS // KV_HEADS
    q_width = HEADS * HD
    kv_width = KV_HEADS * HD
    order_row = block_order[0]
    lengths_row = seq_lengths[0]
    slots = jnp.arange(rows_here, dtype=jnp.int32) // BLK + ctx_index * (rows_here // BLK)
    table = slots[:, None] == jnp.arange(order_row.shape[0], dtype=jnp.int32)[None, :]
    packed = (
        jnp.sum(jnp.where(table, order_row[None, :], 0), axis=1) * BLK
        + jnp.arange(rows_here, dtype=jnp.int32) % BLK
    )
    local = packed - starts_of(packed, lengths_row)
    frequency = ROPE_BASE ** (-2.0 * jnp.arange(HD // 2, dtype=jnp.float32) / HD)
    angle = frequency[:, None] * local.astype(jnp.float32)[None, :]
    cosine = jnp.cos(angle)[None]
    sine = jnp.sin(angle)[None]
    bf16, f32 = jnp.bfloat16, jnp.float32
    parts = ctx_size // HEADS
    part = ctx_index // HEADS
    part_blocks = HEADS * rows_here // BLK
    q_order = lax.dynamic_slice_in_dim(order_row, part * part_blocks, part_blocks)
    q_slot, q_place, q_start = block_tables(q_order, lengths_row)
    q_slot = q_slot + part * part_blocks
    kv_slot, _, _ = block_tables(order_row, lengths_row)
    first = jnp.min(q_start.reshape(-1, TILE), axis=1) // TILE
    last = jnp.max(q_place.reshape(-1, TILE), axis=1) // TILE + 1
    tables = (q_slot, kv_slot, first, last)
    q_rows, kv_rows = part_blocks * BLK, order_row.shape[0] * BLK

    def fetch_attention():
        return (
            lax.all_gather(qkv_weight, "fsdp", axis=0, tiled=True),
            lax.all_gather(out_weight, "fsdp", axis=0, tiled=True),
            lax.all_gather(attn_gain, "fsdp", axis=0, tiled=True),
            lax.all_gather(ffn_gain, "fsdp", axis=0, tiled=True),
            lax.all_gather(query_gain, "fsdp", axis=0, tiled=True),
            lax.all_gather(key_gain, "fsdp", axis=0, tiled=True),
        )

    w_qkv, w_out, gain_attn, gain_ffn, gain_query, gain_key = fetch_attention()
    gain_attn = gain_attn.astype(jnp.float32)
    gain_ffn = gain_ffn.astype(jnp.float32)
    gain_query = gain_query.astype(jnp.float32)
    gain_key = gain_key.astype(jnp.float32)
    scale_one = rms_scale(inputs)
    normed = (inputs * scale_one * gain_attn).astype(jnp.bfloat16)
    projected = lax.dot_general(
        w_qkv, normed, (((0,), (1,)), ((), ())), preferred_element_type=f32
    )
    q_raw = projected[:q_width].reshape(HEADS, HD, rows_here)
    k_raw = projected[q_width : q_width + kv_width].reshape(KV_HEADS, HD, rows_here)
    values_here = projected[q_width + kv_width :].reshape(KV_HEADS, HD, rows_here).astype(bf16)
    q_scale = rms_scale(q_raw, 1)
    k_scale = rms_scale(k_raw, 1)
    column_query, column_key = gain_query[:, None], gain_key[:, None]
    queries = rope(q_raw * q_scale * column_query, cosine, sine).astype(bf16)
    keys_here = rope(k_raw * k_scale * column_key, cosine, sine).astype(bf16)
    sent = jnp.concatenate(
        [queries, jnp.repeat(keys_here, per_group, 0), jnp.repeat(values_here, per_group, 0)], axis=1
    )
    sent = jnp.concatenate([sent] * parts, axis=0)
    got = lax.all_to_all(sent, "ctx", 0, 0, tiled=True)
    q_place, q_start = q_place[None], q_start[None]
    shape = jax.ShapeDtypeStruct
    attn_sent, *held = kernel_call(
        attend_kernel,
        tables,
        (got, q_place, q_start),
        [
            shape((ctx_size, HD, rows_here), bf16),
            shape((q_rows, HD), bf16),
            shape((HD, q_rows), bf16),
            shape((kv_rows, HD), bf16),
            shape((HD, kv_rows), bf16),
            shape((kv_rows, HD), bf16),
            shape((HD, q_rows), f32),
            shape((1, q_rows), f32),
        ],
        [pltpu.VMEM((HD, kv_rows), bf16)],
        ATTEND,
    )
    attn_in = lax.dynamic_slice_in_dim(
        lax.all_to_all(attn_sent, "ctx", 0, 0, tiled=True), part * HEADS, HEADS
    ).reshape(q_width, rows_here)
    h_one = inputs + lax.dot_general(
        attn_in, w_out, (((0,), (0,)), ((), ())), preferred_element_type=f32
    )
    scale_two = rms_scale(h_one)
    normed_two = (h_one * scale_two * gain_ffn).astype(jnp.bfloat16)
    columns = normed_two
    gate_up = jnp.einsum(
        "tr,rgf->tgf",
        columns,
        lax.all_gather(gate_up_weight, "fsdp", axis=0, tiled=True),
        preferred_element_type=jnp.float32,
    )
    gate = gate_up[:, 0]
    upper = gate_up[:, 1]
    sigma = jax.nn.sigmoid(gate)
    hidden = (gate * sigma * upper).astype(jnp.bfloat16)
    columns = hidden
    ffn_out = jnp.dot(
        columns,
        lax.all_gather(down_weight, "fsdp", axis=0, tiled=True),
        preferred_element_type=jnp.float32,
    )
    output = (h_one + ffn_out).astype(jnp.bfloat16)
    d_out = cotangent[0].astype(jnp.float32)
    d_ffn = d_out.astype(jnp.bfloat16)
    d_hidden = lax.dot_general(
        d_ffn,
        lax.all_gather(down_weight, "fsdp", axis=0, tiled=True),
        (((1,), (1,)), ((), ())),
        preferred_element_type=jnp.float32,
    )
    d_gate = d_hidden * upper * sigma * (1.0 + gate * (1.0 - sigma))
    d_upper = d_hidden * gate * sigma
    d_gate_up = jnp.stack([d_gate, d_upper], axis=1).astype(jnp.bfloat16)
    d_normed_two = jnp.einsum(
        "tgf,rgf->tr",
        d_gate_up,
        lax.all_gather(gate_up_weight, "fsdp", axis=0, tiled=True),
        preferred_element_type=jnp.float32,
    )
    columns = normed_two
    grad_gate_up = lax.psum_scatter(
        jnp.einsum("tr,tgf->rgf", columns, d_gate_up, preferred_element_type=jnp.float32).astype(
            jnp.bfloat16
        ),
        "fsdp",
        scatter_dimension=0,
        tiled=True,
    )
    columns = hidden
    grad_down = lax.psum_scatter(
        lax.dot_general(
            columns, d_ffn, (((0,), (0,)), ((), ())), preferred_element_type=jnp.float32
        ).astype(jnp.bfloat16),
        "fsdp",
        scatter_dimension=0,
        tiled=True,
    )
    d_norm_two, ffn_gain_term = norm_back(d_normed_two, h_one, scale_two, gain_ffn)
    d_h_one = d_out + d_norm_two
    d_attn = d_h_one.astype(jnp.bfloat16)
    grad_out_here = jnp.dot(attn_in, d_attn, preferred_element_type=f32)
    d_heads = lax.dot_general(
        w_out, d_attn, (((1,), (1,)), ((), ())), preferred_element_type=f32
    ).astype(bf16)
    d_heads = jnp.concatenate([d_heads.reshape(HEADS, HD, rows_here)] * parts, axis=0)
    d_got = lax.all_to_all(d_heads, "ctx", 0, 0, tiled=True)
    (d_sent,) = kernel_call(
        attend_back_kernel,
        tables,
        (d_got, q_place, q_start, *held),
        [shape((ctx_size, 3 * HD, rows_here), bf16)],
        [
            pltpu.VMEM((HD, q_rows), bf16),
            pltpu.VMEM((q_rows, HD), bf16),
            pltpu.VMEM((kv_rows, HD), f32),
            pltpu.VMEM((kv_rows, HD), f32),
        ],
        ATTEND_BACK,
    )
    d_back = lax.all_to_all(d_sent, "ctx", 0, 0, tiled=True)
    d_query = lax.dynamic_slice_in_dim(d_back[:, :HD], part * HEADS, HEADS).astype(f32)
    d_key_value = jnp.sum(
        d_back[:, HD:].reshape(parts, KV_HEADS, per_group, 2 * HD, rows_here).astype(f32),
        axis=(0, 2),
    )
    dq_normed = rope_back(d_query, cosine, sine)
    dk_normed = rope_back(d_key_value[:, :HD], cosine, sine)
    dq_raw, query_term = norm_back(dq_normed, q_raw, q_scale, column_query, 1)
    dk_raw, key_term = norm_back(dk_normed, k_raw, k_scale, column_key, 1)
    d_projected = jnp.concatenate(
        [
            dq_raw.reshape(q_width, rows_here).astype(bf16),
            dk_raw.reshape(kv_width, rows_here).astype(bf16),
            d_key_value[:, HD:].reshape(kv_width, rows_here).astype(bf16),
        ],
        axis=0,
    )
    grad_qkv_here = lax.dot_general(
        normed, d_projected, (((0,), (1,)), ((), ())), preferred_element_type=f32
    )
    d_normed = lax.dot_general(
        d_projected, w_qkv, (((0,), (1,)), ((), ())), preferred_element_type=f32
    )
    d_norm_one, attn_gain_term = norm_back(d_normed, inputs, scale_one, gain_attn)
    d_inputs = d_h_one + d_norm_one
    shard_qkv, shard_out, shard_attn_gain, shard_ffn_gain, shard_query_gain, shard_key_gain = (
        lax.psum_scatter(
            grad_qkv_here.astype(jnp.bfloat16), "fsdp", scatter_dimension=0, tiled=True
        ).astype(jnp.float32),
        lax.psum_scatter(
            grad_out_here.astype(jnp.bfloat16), "fsdp", scatter_dimension=0, tiled=True
        ).astype(jnp.float32),
        lax.psum_scatter(
            jnp.sum(attn_gain_term, axis=0).astype(jnp.bfloat16),
            "fsdp",
            scatter_dimension=0,
            tiled=True,
        ).astype(jnp.float32),
        lax.psum_scatter(
            jnp.sum(ffn_gain_term, axis=0).astype(jnp.bfloat16),
            "fsdp",
            scatter_dimension=0,
            tiled=True,
        ).astype(jnp.float32),
        lax.psum_scatter(
            jnp.sum(query_term, axis=(0, 2)).astype(jnp.bfloat16),
            "fsdp",
            scatter_dimension=0,
            tiled=True,
        ).astype(jnp.float32),
        lax.psum_scatter(
            jnp.sum(key_term, axis=(0, 2)).astype(jnp.bfloat16),
            "fsdp",
            scatter_dimension=0,
            tiled=True,
        ).astype(jnp.float32),
    )
    summed_grads = (
        lax.psum(shard_qkv.astype(jnp.bfloat16), "ctx").astype(jnp.float32),
        lax.psum(shard_out.astype(jnp.bfloat16), "ctx").astype(jnp.float32),
        lax.psum(grad_gate_up, "ctx").astype(jnp.float32),
        lax.psum(grad_down, "ctx").astype(jnp.float32),
        lax.psum(shard_attn_gain.astype(jnp.bfloat16), "ctx").astype(jnp.float32),
        lax.psum(shard_ffn_gain.astype(jnp.bfloat16), "ctx").astype(jnp.float32),
        lax.psum(shard_query_gain.astype(jnp.bfloat16), "ctx").astype(jnp.float32),
        lax.psum(shard_key_gain.astype(jnp.bfloat16), "ctx").astype(jnp.float32),
    )
    return (
        output[None],
        d_inputs[None],
        summed_grads[0],
        summed_grads[1],
        summed_grads[2],
        summed_grads[3],
        summed_grads[4],
        summed_grads[5],
        summed_grads[6],
        summed_grads[7],
    )


def solution(mesh):
    block = mesh.shape["fsdp"] == 2 and mesh.shape["ctx"] == 16
    return jax.shard_map(
        on_block if block else on_device,
        mesh=mesh,
        in_specs=(
            P("fsdp", "ctx", None),
            P("fsdp", None),
            P("fsdp", None),
            P("fsdp", None, None),
            P("fsdp", None),
            P("fsdp"),
            P("fsdp"),
            P("fsdp"),
            P("fsdp"),
            P("fsdp", None),
            P("fsdp", None),
            P("fsdp", "ctx", None),
        ),
        out_specs=(
            P("fsdp", "ctx", None),
            P("fsdp", "ctx", None),
            P("fsdp", None),
            P("fsdp", None),
            P("fsdp", None, None),
            P("fsdp", None),
            P("fsdp"),
            P("fsdp"),
            P("fsdp"),
            P("fsdp"),
        ),
        check_vma=False,
    )
```

```python
import functools

import jax
import jax.numpy as jnp
from jax import lax
from jax.experimental import pallas as pl
from jax.experimental.pallas import tpu as pltpu
from jax.sharding import PartitionSpec as P

HEADS = 16
KV_HEADS = 8
HD = 64
BLK = 128
TILE = 256
CHUNKS = 2
PROJECT = 0
ATTEND = 0
OUT = 0
FFN = (0, 0)
ATTEND_BACK = 25


EPSILON = 1e-05
ROPE_BASE = 1000000.0
LOG2E = 1.4426950408889634
SCORE_SCALE = LOG2E * HD ** (-0.5)


def rms_scale(values, axis=-1):
    return lax.rsqrt(jnp.mean(values * values, axis=axis, keepdims=True) + EPSILON)


def norm_back(grad_normed, inputs, scale, gain, axis=-1):
    scaled = grad_normed * gain
    grad_in = scale * scaled - inputs * scale * scale * scale * jnp.mean(
        scaled * inputs, axis=axis, keepdims=True
    )
    return (grad_in, grad_normed * inputs * scale)


def rope(values, cosine, sine):
    half = HD // 2
    first, second = values[:, :half], values[:, half:]
    return jnp.concatenate([first * cosine - second * sine, second * cosine + first * sine], axis=1)


def rope_back(values, cosine, sine):
    half = HD // 2
    first, second = values[:, :half], values[:, half:]
    return jnp.concatenate([first * cosine + second * sine, second * cosine - first * sine], axis=1)


def starts_of(packed, lengths_row):
    ends = jnp.cumsum(lengths_row)
    past = packed[:, None] >= ends[None, :]
    return jnp.sum(jnp.where(past, lengths_row[None, :], 0), axis=1)


def block_tables(order, lengths_row):
    count = order.shape[0]
    rank = jnp.sum((order[None, :] < order[:, None]).astype(jnp.int32), axis=1)
    hit = rank[None, :] == jnp.arange(count, dtype=jnp.int32)[:, None]
    slot = jnp.sum(jnp.where(hit, jnp.arange(count, dtype=jnp.int32)[None, :], 0), axis=1)
    block = jnp.sum(jnp.where(hit, order[None, :], 0), axis=1)
    place = (block[:, None] * BLK + jnp.arange(BLK, dtype=jnp.int32)[None, :]).reshape(-1)
    return (slot, place, starts_of(place, lengths_row))


def attend_kernel(
    q_slot, kv_slot, first, last, qkv_ref, place_ref, start_ref,
    out_ref, q_ref, qt_ref, k_ref, kt_ref, v_ref, ot_ref, total_ref, vt_ref
):
    per_device = qkv_ref.shape[2] // BLK
    kv_blocks = k_ref.shape[0] // BLK
    q_blocks = q_ref.shape[0] // BLK

    def piece(slot, lower):
        return qkv_ref[
            slot // per_device,
            lower : lower + HD,
            pl.ds(pl.multiple_of((slot % per_device) * BLK, BLK), BLK),
        ]

    for i in range(kv_blocks):
        here = slice(i * BLK, (i + 1) * BLK)
        keys = piece(kv_slot[i], HD)
        kt_ref[:, here] = keys
        k_ref[here, :] = keys.T
        values = piece(kv_slot[i], 2 * HD)
        vt_ref[:, here] = values
        v_ref[here, :] = values.T
    for i in range(q_blocks):
        here = slice(i * BLK, (i + 1) * BLK)
        queries = piece(q_slot[i], 0)
        qt_ref[:, here] = queries
        q_ref[here, :] = queries.T
    if q_blocks < kv_blocks:
        out_ref[...] = jnp.zeros_like(out_ref)

    def tile(i, carry):
        rows = pl.ds(pl.multiple_of(i * TILE, TILE), TILE)
        queries = qt_ref[:, rows]
        place = place_ref[:, rows]
        start = start_ref[:, rows]

        def step(j, state):
            total, summed = state
            at = pl.multiple_of(j * TILE, TILE)
            scores = jnp.dot(
                k_ref[pl.ds(at, TILE), :], queries, preferred_element_type=jnp.float32
            )
            key_place = lax.broadcasted_iota(jnp.int32, (TILE, TILE), 0) + at
            allowed = (key_place <= place) & (key_place >= start)
            lifted = jnp.where(allowed, jnp.exp2(scores * SCORE_SCALE), 0.0)
            total = total + jnp.sum(lifted, axis=0, keepdims=True)
            summed = summed + jnp.dot(
                vt_ref[:, pl.ds(at, TILE)],
                lifted.astype(jnp.bfloat16),
                preferred_element_type=jnp.float32,
            )
            return (total, summed)

        total, summed = lax.fori_loop(
            first[i],
            last[i],
            step,
            (jnp.zeros((1, TILE), jnp.float32), jnp.zeros((HD, TILE), jnp.float32)),
        )
        attn = summed / total
        ot_ref[:, rows] = attn
        total_ref[:, rows] = jnp.log(total) * LOG2E
        rounded = attn.astype(jnp.bfloat16)
        for part in range(TILE // BLK):
            slot = q_slot[i * (TILE // BLK) + part]
            out_ref[
                slot // per_device,
                :,
                pl.ds(pl.multiple_of((slot % per_device) * BLK, BLK), BLK),
            ] = rounded[:, part * BLK : (part + 1) * BLK]
        return carry

    lax.fori_loop(0, q_blocks * BLK // TILE, tile, 0)


def attend_back_kernel(
    q_slot, kv_slot, first, last, d_ref, place_ref, start_ref,
    q_ref, qt_ref, k_ref, kt_ref, v_ref, ot_ref, total_ref,
    out_ref, dt_ref, do_ref, dk_ref, dv_ref
):
    per_device = d_ref.shape[2] // BLK
    kv_blocks = k_ref.shape[0] // BLK
    q_blocks = q_ref.shape[0] // BLK

    def lanes(slot):
        return pl.ds(pl.multiple_of((slot % per_device) * BLK, BLK), BLK)

    for i in range(q_blocks):
        here = slice(i * BLK, (i + 1) * BLK)
        slot = q_slot[i]
        grads = d_ref[slot // per_device, :, lanes(slot)]
        dt_ref[:, here] = grads
        do_ref[here, :] = grads.T
    dk_ref[...] = jnp.zeros_like(dk_ref)
    dv_ref[...] = jnp.zeros_like(dv_ref)
    if q_blocks < kv_blocks:
        out_ref[...] = jnp.zeros_like(out_ref)

    def tile(i, carry):
        rows = pl.ds(pl.multiple_of(i * TILE, TILE), TILE)
        queries = qt_ref[:, rows]
        grads = dt_ref[:, rows]
        place = place_ref[:, rows]
        start = start_ref[:, rows]
        delta = jnp.sum(grads.astype(jnp.float32) * ot_ref[:, rows], axis=0, keepdims=True)
        total = total_ref[:, rows]

        def step(j, d_query):
            at = pl.multiple_of(j * TILE, TILE)
            here = pl.ds(at, TILE)
            scores = jnp.dot(k_ref[here, :], queries, preferred_element_type=jnp.float32)
            key_place = lax.broadcasted_iota(jnp.int32, (TILE, TILE), 0) + at
            allowed = (key_place <= place) & (key_place >= start)
            shares = jnp.where(allowed, jnp.exp2(scores * SCORE_SCALE - total), 0.0)
            d_shares = jnp.dot(v_ref[here, :], grads, preferred_element_type=jnp.float32)
            d_scores = (shares * (d_shares - delta)).astype(jnp.bfloat16)
            dv_ref[here, :] += jnp.dot(
                shares.astype(jnp.bfloat16), do_ref[rows, :], preferred_element_type=jnp.float32
            )
            dk_ref[here, :] += jnp.dot(
                d_scores, q_ref[rows, :], preferred_element_type=jnp.float32
            )
            return d_query + jnp.dot(
                kt_ref[:, here], d_scores, preferred_element_type=jnp.float32
            )

        d_query = lax.fori_loop(first[i], last[i], step, jnp.zeros((HD, TILE), jnp.float32))
        rounded = (d_query * HD ** (-0.5)).astype(jnp.bfloat16)
        for part in range(TILE // BLK):
            slot = q_slot[i * (TILE // BLK) + part]
            out_ref[slot // per_device, 0:HD, lanes(slot)] = rounded[
                :, part * BLK : (part + 1) * BLK
            ]
        return carry

    lax.fori_loop(0, q_blocks * BLK // TILE, tile, 0)
    for i in range(kv_blocks):
        here = slice(i * BLK, (i + 1) * BLK)
        slot = kv_slot[i]
        out_ref[slot // per_device, HD : 2 * HD, lanes(slot)] = (
            (dk_ref[here, :] * HD ** (-0.5)).T.astype(jnp.bfloat16)
        )
        out_ref[slot // per_device, 2 * HD : 3 * HD, lanes(slot)] = (
            dv_ref[here, :].T.astype(jnp.bfloat16)
        )


def cost(micros):
    return pl.CostEstimate(
        flops=1 + micros * 1_000_000_000, bytes_accessed=1, transcendentals=0
    )


def kernel_call(kernel, tables, arrays, outs, scratch, micros):
    smem = pl.BlockSpec(memory_space=pltpu.SMEM)
    vmem = pl.BlockSpec(memory_space=pltpu.VMEM)
    return pl.pallas_call(
        kernel,
        out_shape=outs,
        in_specs=[smem] * len(tables) + [vmem] * len(arrays),
        out_specs=[vmem] * len(outs),
        scratch_shapes=scratch,
        compiler_params=pltpu.CompilerParams(vmem_limit_bytes=48 * 1024 * 1024),
        cost_estimate=cost(micros),
    )(*tables, *arrays)


class Links:
    def __init__(self, ctx_size):
        self.depth = ctx_size // 4
        index = lax.axis_index("ctx")
        self.core = index % 2
        self.y = (index // 2) % 2
        self.side = lax.axis_index("fsdp")
        self.half = index // 4 % 2
        self.quarter = index % 2 * 2 + self.y
        self.here = jnp.stack([self.half, self.core, self.y, self.side]).astype(jnp.int32)

    def route(self, place):
        pairs = []
        for z in range(self.depth):
            for y in range(2):
                for core in range(2):
                    to_z, to_y, to_core = place(z, y, core)
                    pairs.append(((z * 2 + y) * 2 + core, (to_z * 2 + to_y) * 2 + to_core))
        return pairs

    def over_core(self, value):
        return lax.ppermute(value, "ctx", self.route(lambda z, y, c: (z, y, 1 - c)))

    def over_y(self, value):
        return lax.ppermute(value, "ctx", self.route(lambda z, y, c: (z, 1 - y, c)))

    def over_z(self, value):
        return lax.ppermute(value, "ctx", self.route(lambda z, y, c: (z ^ 1, y, c)))

    def over_two_z(self, value):
        return lax.ppermute(value, "ctx", self.route(lambda z, y, c: (z ^ 2, y, c)))

    def over_x(self, value):
        return lax.ppermute(value, "fsdp", [(0, 1), (1, 0)])

    def spread_plane(self, value):
        across = self.over_core(value)
        beside = self.over_y(value)
        return (value, across, beside, self.over_core(beside))

    def deal_plane(self, near, far, give, give_far):
        got, got_far = self.over_core(give), self.over_core(give_far)
        return (near, got, self.over_y(far), self.over_y(got_far))

    def half_of(self, kept, got, own):
        index = self.half if own else 1 - self.half
        return add(pick(kept, index, 0), pick(got, index, 0))


def pick(value, index, axis):
    return lax.dynamic_index_in_dim(value, index, axis, keepdims=False)


def add(left, right):
    return (left.astype(jnp.float32) + right.astype(jnp.float32)).astype(jnp.bfloat16)


def after(value, *others):
    return lax.optimization_barrier((value, *jax.tree.leaves(others)))[0]


def contract(left, right, axes):
    return lax.dot_general(
        left, right, ((axes[:1], axes[1:]), ((), ())), preferred_element_type=jnp.float32
    )


PARAMS = pltpu.CompilerParams(vmem_limit_bytes=56 * 1024 * 1024)


def call_with_here(
    kernel, here, grid, arrays, specs, outs, out_specs, scratch=(), aliases=None, micros=0
):
    return pl.pallas_call(
        kernel,
        grid_spec=pltpu.PrefetchScalarGridSpec(
            num_scalar_prefetch=1,
            grid=grid,
            in_specs=specs,
            out_specs=out_specs,
            scratch_shapes=list(scratch),
        ),
        out_shape=outs,
        input_output_aliases=aliases or {},
        compiler_params=PARAMS,
        cost_estimate=cost(micros),
    )(here, *arrays)


def whole(array):
    rank = len(array.shape)
    return pl.BlockSpec(array.shape, lambda i, here: (0,) * rank)


def project_kernel(here, *refs):
    x_ref, gain_ref, own_ref = refs[:3]
    pieces, q_gain, k_gain, cos_ref, sin_ref = refs[3:7], refs[7], refs[8], refs[9], refs[10]
    sent, weight, q_ref, k_ref, q_scale, k_scale, normed_ref, scale_ref = refs[11:]
    core, y, side = here[1], here[2], here[3]
    rows = own_ref.shape[0]
    part = rows // 4
    f32, bf16 = jnp.float32, jnp.bfloat16
    weight[pl.ds(pl.multiple_of(side * rows, rows), rows), :] = own_ref[...]
    for p in range(4):
        at = (1 - side) * rows + (((p % 2) ^ core) * 2 + ((p // 2) ^ y)) * part
        weight[pl.ds(pl.multiple_of(at, part), part), :] = pieces[p][...]
    x = x_ref[...].astype(f32)
    scale = rms_scale(x)
    scale_ref[...] = scale
    normed = (x * scale * gain_ref[...]).astype(bf16)
    normed_ref[...] = normed.T
    cosine, sine = cos_ref[...], sin_ref[...]
    half = HD // 2

    def turned(raw, gain, raw_ref, kept_scale, head):
        raw_ref[head * HD : (head + 1) * HD, :] = raw
        scale = rms_scale(raw, 0)
        kept_scale[head : head + 1, :] = scale
        value = raw * scale * gain
        first, second = value[:half], value[half:]
        return jnp.concatenate(
            [first * cosine - second * sine, second * cosine + first * sine], axis=0
        ).astype(bf16)

    per_group = HEADS // KV_HEADS
    for at in range(0, weight.shape[1], 2 * BLK):
        block = jnp.dot(normed, weight[:, at : at + 2 * BLK], preferred_element_type=f32)
        turned_block = block.T
        for n in range(2 * BLK // HD):
            head = at // HD + n
            raw = turned_block[n * HD : (n + 1) * HD, :]
            if head < HEADS:
                sent[head, 0:HD, :] = turned(raw, q_gain[...], q_ref, q_scale, head)
                continue
            head -= HEADS
            if head < KV_HEADS:
                value, row = turned(raw, k_gain[...], k_ref, k_scale, head), HD
            else:
                value, row, head = raw.astype(bf16), 2 * HD, head - KV_HEADS
            for copy in range(per_group):
                sent[head * per_group + copy, row : row + HD, :] = value


def project(here, x, gain, own, pieces, q_gain, k_gain, cosine, sine):
    tokens, width = x.shape
    f32, bf16 = jnp.float32, jnp.bfloat16
    shape = jax.ShapeDtypeStruct
    arrays = [x, gain, own, *pieces, q_gain, k_gain, cosine, sine]
    outs = [
        shape((HEADS, 3 * HD, tokens), bf16),
        shape((width, own.shape[1]), bf16),
        shape((HEADS * HD, tokens), f32),
        shape((KV_HEADS * HD, tokens), f32),
        shape((HEADS, tokens), f32),
        shape((KV_HEADS, tokens), f32),
        shape((width, tokens), bf16),
        shape((tokens, 1), f32),
    ]
    return call_with_here(
        project_kernel, here, (1,), arrays, [whole(a) for a in arrays], outs,
        [whole(o) for o in outs], micros=PROJECT,
    )


def layer(array, index):
    return pl.BlockSpec((1, *array.shape[1:]), lambda i, here: (index, 0, 0))


def attend_out_kernel(here, *refs):
    attn_ref, x_ref, gain_ref, own_ref = refs[:4]
    pieces = refs[4:12]
    weight, h_ref, scale_ref, two_ref, two_t_ref = refs[12:]
    core, y, side = here[1], here[2], here[3]
    rows = own_ref.shape[0]
    part = rows // 4
    weight[pl.ds(pl.multiple_of(side * rows, rows), rows), :] = own_ref[...]
    for p in range(4):
        at = (1 - side) * rows + (((p % 2) ^ core) * 2 + ((p // 2) ^ y)) * part
        for n in range(2):
            piece = pieces[2 * p + n]
            wide = piece.shape[1]
            weight[pl.ds(pl.multiple_of(at, part), part), n * wide : (n + 1) * wide] = piece[...]
    attn = attn_ref[...].T
    h_one = x_ref[...].astype(jnp.float32) + jnp.dot(
        attn, weight[...], preferred_element_type=jnp.float32
    )
    scale = rms_scale(h_one)
    h_ref[...] = h_one
    scale_ref[...] = scale
    two = (h_one * scale * gain_ref[...]).astype(jnp.bfloat16)
    two_ref[...] = two
    two_t_ref[...] = two.T


def attend_out(here, attn, x, gain, own, pieces):
    tokens, width = x.shape
    f32, bf16 = jnp.float32, jnp.bfloat16
    shape = jax.ShapeDtypeStruct
    part = own.shape[0] // 4
    half = width // 2
    first = pieces[0].shape[1] // half - 2
    arrays = [attn, x, gain, own]
    specs = [whole(a) for a in arrays]
    for piece in pieces:
        for n in range(2):
            arrays.append(piece)
            specs.append(pl.BlockSpec((part, half), lambda i, here, n=n: (0, first + n)))
    outs = [
        shape((width, width), bf16),
        shape((tokens, width), f32),
        shape((tokens, 1), f32),
        shape((tokens, width), bf16),
        shape((width, tokens), bf16),
    ]
    return call_with_here(
        attend_out_kernel, here, (1,), arrays, specs, outs, [whole(o) for o in outs], micros=OUT
    )


def ffn_kernel(chunk, here, *refs):
    two_ref, d_ref, own_ref = refs[:3]
    pieces, down_ref, down_pieces = refs[3:7], refs[7], refs[8:12]
    if chunk == 0:
        before_refs, refs = refs[12:13], refs[13:]
        near, far, give, give_far, out_ref, d_two_ref = refs[:6]
        refs = refs[6:]
    else:
        before_refs, gain_ref, refs = refs[12:17], refs[17], refs[18:]
        near, far, give, give_far = refs[:4]
        out_ref, d_h_ref, d_attn_ref, heads_ref, gain_term_ref = refs[4:9]
        refs = refs[9:]
    weight, down, hidden_rows, out_sum, two_sum = refs[:5]
    held, weight_sem, down_sem, before_sem = refs[5:-3], refs[-3], refs[-2], refs[-1]
    core, y, side = here[1], here[2], here[3]
    f32, bf16 = jnp.float32, jnp.bfloat16
    own_rows, columns = own_ref.shape[1], own_ref.shape[2] // CHUNKS
    part = own_rows // 4
    tile = columns // FFN_TILES
    half = columns // 2

    def quarter(p):
        return ((p % 2) ^ core) * 2 + ((p // 2) ^ y)

    def copies(n):
        at = slice(n * tile, (n + 1) * tile)
        mine = pl.ds(pl.multiple_of(side * own_rows, own_rows), own_rows)
        found = [
            pltpu.make_async_copy(
                own_ref.at[:, :, chunk * columns + n * tile : chunk * columns + (n + 1) * tile],
                weight.at[:, mine, at],
                weight_sem.at[n, 0],
            )
        ]
        for p in range(4):
            rows = pl.ds(pl.multiple_of((1 - side) * own_rows + quarter(p) * part, part), part)
            for kind in range(2):
                begin = kind * columns + n * tile
                found.append(
                    pltpu.make_async_copy(
                        pieces[p].at[:, begin : begin + tile],
                        weight.at[kind, rows, at],
                        weight_sem.at[n, 1 + 2 * p + kind],
                    )
                )
        return found

    def own_down(n):
        at = slice(n * tile, (n + 1) * tile)
        return [pltpu.make_async_copy(down_ref.at[at, :], down.at[at, :], down_sem.at[n, 0])]

    def other_down(n):
        at = slice(n * tile, (n + 1) * tile)
        found = []
        for p in range(4):
            wide = down_pieces[p].shape[1]
            lanes = pl.ds(pl.multiple_of(quarter(p) * wide, wide), wide)
            found.append(
                pltpu.make_async_copy(
                    down_pieces[p].at[at, :], down.at[at, lanes], down_sem.at[n, p]
                )
            )
        return found

    def each(action, n):
        for copy in copies(n):
            action(copy)

        @pl.when(side == chunk)
        def _():
            for copy in own_down(n):
                action(copy)

        @pl.when(side != chunk)
        def _():
            for copy in other_down(n):
                action(copy)

    before = [
        pltpu.make_async_copy(ref, held[n], before_sem.at[n]) for n, ref in enumerate(before_refs)
    ]
    for n in range(FFN_TILES):
        each(lambda copy: copy.start(), n)
    for copy in before:
        copy.start()
    two = two_ref[...]
    d_ffn = d_ref[...]
    for n in range(FFN_TILES):
        each(lambda copy: copy.wait(), n)
        at = slice(n * tile, (n + 1) * tile)
        gate = jnp.dot(two, weight[0, :, at], preferred_element_type=f32)
        upper = jnp.dot(two, weight[1, :, at], preferred_element_type=f32)
        d_hidden = contract(d_ffn, down[at, :], (1, 1))
        sigma = jax.nn.sigmoid(gate)
        silu = gate * sigma
        hidden = (silu * upper).astype(bf16)
        d_gate = (d_hidden * upper * sigma * (1.0 + gate * (1.0 - sigma))).astype(bf16)
        d_upper = (d_hidden * silu).astype(bf16)
        out_term = jnp.dot(hidden, down[at, :], preferred_element_type=f32)
        two_term = contract(d_gate, weight[0, :, at], (1, 1)) + contract(
            d_upper, weight[1, :, at], (1, 1)
        )
        out_sum[...] = out_term if n == 0 else out_sum[...] + out_term
        two_sum[...] = two_term if n == 0 else two_sum[...] + two_term
        hidden_rows[:, at] = hidden
        mine = jnp.where(core == 0, d_gate, d_upper)
        other = jnp.where(core == 0, d_upper, d_gate)
        for column in range(2):
            begin, end = max(n * tile, column * half), min((n + 1) * tile, (column + 1) * half)
            if begin >= end:
                continue
            source = slice(begin - n * tile, end - n * tile)
            target = slice(begin - column * half, end - column * half)
            first, second = mine[:, source], other[:, source]

            @pl.when(y == column)
            def _(first=first, second=second, target=target):
                near[:, target] = first
                give[:, target] = second

            @pl.when(y != column)
            def _(first=first, second=second, target=target):
                far[:, target] = first
                give_far[:, target] = second

    share = half // 2
    target = slice(half, half + share)
    for owner in range(2):
        lower = hidden_rows[:, owner * half : owner * half + share]
        upper = hidden_rows[:, owner * half + share : (owner + 1) * half]
        close = jnp.where(y == 0, lower, upper)
        distant = jnp.where(y == 0, upper, lower)

        @pl.when(core == owner)
        def _(close=close, distant=distant):
            near[:, target] = close
            far[:, target] = distant

        @pl.when(core != owner)
        def _(close=close, distant=distant):
            give[:, target] = close
            give_far[:, target] = distant

    for copy in before:
        copy.wait()
    if chunk == 0:
        out_ref[...] = held[0][...] + out_sum[...]
        d_two_ref[...] = two_sum[...]
    else:
        out_before, two_before, h_one, scale, w_out = held
        out_ref[...] = (out_before[...] + out_sum[...]).astype(bf16)
        d_norm, gain_term = norm_back(
            two_before[...] + two_sum[...], h_one[...], scale[...], gain_ref[...]
        )
        gain_term_ref[...] = jnp.sum(gain_term, axis=0, keepdims=True)
        d_h_one = d_ffn.astype(f32) + d_norm
        d_h_ref[...] = d_h_one
        d_attn = d_h_one.astype(bf16)
        d_attn_ref[...] = d_attn
        heads_ref[...] = contract(w_out[...], d_attn, (1, 1)).astype(bf16)


FFN_TILES = 3


def ffn(here, chunk, two, d_ffn, own, pieces, down, down_pieces, before, gain=None):
    tokens, width = two.shape
    columns = own.shape[2] // CHUNKS
    padded = (columns // 2 + columns // 4 + BLK - 1) // BLK * BLK
    shape = jax.ShapeDtypeStruct
    f32, bf16 = jnp.float32, jnp.bfloat16
    outs = [shape((tokens, padded), bf16)] * 4
    if chunk == 0:
        outs += [shape((tokens, width), f32)] * 2
    else:
        outs += [
            shape((tokens, width), bf16),
            shape((tokens, width), f32),
            shape((tokens, width), bf16),
            shape((width, tokens), bf16),
            shape((1, width), f32),
        ]
    far_away = pl.BlockSpec(memory_space=pl.ANY)
    arrays = [two, d_ffn, own, *pieces, down, *down_pieces, *before]
    specs = [whole(two), whole(d_ffn)] + [far_away] * (len(arrays) - 2)
    if gain is not None:
        arrays.append(gain)
        specs.append(whole(gain))
    got = call_with_here(
        functools.partial(ffn_kernel, chunk),
        here,
        (1,),
        arrays,
        specs,
        outs,
        [whole(o) for o in outs],
        [
            pltpu.VMEM((2, width, columns), bf16),
            pltpu.VMEM((columns, width), bf16),
            pltpu.VMEM((tokens, columns), bf16),
            pltpu.VMEM((tokens, width), f32),
            pltpu.VMEM((tokens, width), f32),
        ]
        + [pltpu.VMEM(v.shape, v.dtype) for v in before]
        + [
            pltpu.SemaphoreType.DMA((FFN_TILES, 9)),
            pltpu.SemaphoreType.DMA((FFN_TILES, 4)),
            pltpu.SemaphoreType.DMA((len(before),)),
        ],
        micros=FFN[chunk],
    )
    return got[:4], got[4:]


def wide_product_kernel(here, *refs):
    planes, terms = refs[:4], refs[4:8]
    sent, kept, left, right = refs[8:]
    tokens = planes[0].shape[1]
    columns = right.shape[1]
    for i in range(4):
        left[:, i * tokens : (i + 1) * tokens] = planes[i][...]
        right[i * tokens : (i + 1) * tokens, :] = terms[i][:, :columns]
    side = here[3]
    _, step, _ = kept.shape
    for half in range(2):
        for owner, out_ref in ((1 - side, sent), (side, kept)):
            place = pl.multiple_of(owner * 2 * step + half * step, step)
            out_ref[half] = jnp.dot(
                left[pl.ds(place, step), :], right[...], preferred_element_type=jnp.float32
            ).astype(out_ref.dtype)


def wide_products(here, two_plane, shares, columns):
    rows, tokens = two_plane[0].shape
    outs = [
        jax.ShapeDtypeStruct((2, rows // 4, columns), jnp.bfloat16),
        jax.ShapeDtypeStruct((2, rows // 4, columns), jnp.float32),
    ]
    arrays = [*two_plane, *shares]
    return call_with_here(
        wide_product_kernel,
        here,
        (1,),
        arrays,
        [whole(a) for a in two_plane]
        + [pl.BlockSpec((tokens, columns), lambda i, here: (0, 0))] * 4,
        outs,
        [whole(o) for o in outs],
        [
            pltpu.VMEM((rows, 4 * tokens), jnp.bfloat16),
            pltpu.VMEM((4 * tokens, columns), jnp.bfloat16),
        ],
        micros=3,
    )


def down_product_kernel(here, *refs):
    planes, terms = refs[:4], (refs[4:8], refs[8:12])
    sent, kept, left, right = refs[12:]
    tokens = planes[0].shape[0]
    rows = left.shape[0]
    for i in range(4):
        right[i * tokens : (i + 1) * tokens, :] = planes[i][...]
    for chunk in range(2):
        for i in range(4):
            share = terms[chunk][i]
            at = share.shape[1] // BLK * BLK - (rows + BLK - 1) // BLK * BLK
            left[:, i * tokens : (i + 1) * tokens] = share[:, at : at + rows].T
        for half in range(2):
            product = jnp.dot(
                left[half * rows // 2 : (half + 1) * rows // 2, :],
                right[...],
                preferred_element_type=jnp.float32,
            )

            @pl.when(here[3] == chunk)
            def _(product=product, half=half):
                kept[half] = product

            @pl.when(here[3] != chunk)
            def _(product=product, half=half):
                sent[half] = product.astype(sent.dtype)


def down_products(here, d_plane, first, second, rows):
    tokens, columns = d_plane[0].shape
    outs = [
        jax.ShapeDtypeStruct((2, rows // 2, columns), jnp.bfloat16),
        jax.ShapeDtypeStruct((2, rows // 2, columns), jnp.float32),
    ]
    return call_with_here(
        down_product_kernel,
        here,
        (1,),
        [*d_plane, *first, *second],
        [whole(a) for a in (*d_plane, *first, *second)],
        outs,
        [whole(o) for o in outs],
        [
            pltpu.VMEM((rows, 4 * tokens), jnp.bfloat16),
            pltpu.VMEM((4 * tokens, columns), jnp.bfloat16),
        ],
        micros=3,
    )


GAIN_ROWS = 16


def attention_back_kernel(here, *refs):
    d_ref, q_ref, k_ref, q_scale, k_scale, q_gain, k_gain, cos_ref, sin_ref = refs[:9]
    weight, x_ref, scale_ref, gain_ref, d_h_ref, d_attn_ref = refs[9:15]
    near, far, give, give_far, d_x_ref, gains_ref = refs[15:21]
    turned, natural = refs[21:]
    f32, bf16 = jnp.float32, jnp.bfloat16
    core, y = here[1], here[2]
    cosine, sine = cos_ref[...], sin_ref[...]
    half = HD // 2
    per_group = HEADS // KV_HEADS
    tokens = x_ref.shape[0]

    def back(grad, raw, scale, gain):
        first, second = grad[:half], grad[half:]
        normed = jnp.concatenate(
            [first * cosine + second * sine, second * cosine - first * sine], axis=0
        )
        return norm_back(normed, raw, scale, gain, 0)

    q_term = jnp.zeros((HD, tokens), f32)
    k_term = jnp.zeros((HD, tokens), f32)
    for head in range(HEADS):
        at = slice(head * HD, (head + 1) * HD)
        grad, term = back(
            d_ref[head, :HD, :].astype(f32), q_ref[at, :], q_scale[head : head + 1, :], q_gain[...]
        )
        turned[at, :] = grad.astype(bf16)
        q_term = q_term + term
    for head in range(KV_HEADS):
        at = slice(head * HD, (head + 1) * HD)
        both = d_ref[head * per_group, HD:, :].astype(f32)
        for other in range(1, per_group):
            both = both + d_ref[head * per_group + other, HD:, :].astype(f32)
        grad, term = back(both[:HD], k_ref[at, :], k_scale[head : head + 1, :], k_gain[...])
        place = HEADS * HD + head * HD
        turned[place : place + HD, :] = grad.astype(bf16)
        k_term = k_term + term
        place += KV_HEADS * HD
        turned[place : place + HD, :] = both[HD:].astype(bf16)
    rows = turned.shape[0] // 4
    columns = d_attn_ref.shape[1] // 4
    shares = ((near, core, y), (far, core, 1 - y), (give, 1 - core, y), (give_far, 1 - core, 1 - y))
    for out_ref, to_core, to_y in shares:
        share = to_core * 2 + to_y
        out_ref[:rows, :] = turned[pl.ds(pl.multiple_of(share * rows, rows), rows), :]
        out_ref[rows:, :] = d_attn_ref[:, pl.ds(pl.multiple_of(share * columns, columns), columns)]
    for at in range(0, turned.shape[0], 256):
        natural[:, at : at + 256] = turned[at : at + 256, :].T
    d_normed = contract(natural[...], weight[...], (1, 1))
    x = x_ref[...].astype(f32)
    d_norm, gain_term = norm_back(d_normed, x, scale_ref[...], gain_ref[...])
    d_x_ref[...] = d_h_ref[...] + d_norm
    gains_ref[...] = jnp.zeros_like(gains_ref)
    gains_ref[0:1, :] = jnp.sum(gain_term, axis=0, keepdims=True)
    gains_ref[1:2, 0:HD] = jnp.sum(q_term.T, axis=0, keepdims=True)
    gains_ref[2:3, 0:HD] = jnp.sum(k_term.T, axis=0, keepdims=True)


def attention_back(here, arrays):
    f32, bf16 = jnp.float32, jnp.bfloat16
    shape = jax.ShapeDtypeStruct
    weight, x = arrays[9], arrays[10]
    tokens, width = x.shape
    rows = weight.shape[1] // 4 + tokens
    assert width // 4 == tokens
    outs = [
        *[shape((rows, tokens), bf16)] * 4,
        shape((tokens, width), f32),
        shape((8, width), f32),
    ]
    return call_with_here(
        attention_back_kernel, here, (1,), arrays, [whole(a) for a in arrays], outs,
        [whole(o) for o in outs],
        [pltpu.VMEM((weight.shape[1], tokens), bf16), pltpu.VMEM((tokens, weight.shape[1]), bf16)],
        micros=0,
    )


def attention_product_kernel(here, *refs):
    planes, terms, gains_ref, ffn_gain_ref = refs[:4], refs[4:8], refs[8], refs[9]
    sent, kept, left, right, left_out, right_out = refs[10:]
    tokens = planes[0].shape[2]
    cut = right.shape[1]
    for i in range(4):
        at = slice(i * tokens, (i + 1) * tokens)
        left[:, at] = planes[i][0]
        left_out[:, at] = planes[i][1]
        share = terms[i]
        right[at, :] = share[:cut].T
        right_out[at, :] = share[cut:]
    step = left.shape[0] // 4
    for owner, out_ref in ((1 - here[3], sent), (here[3], kept)):
        for half in range(2):
            at = pl.ds(pl.multiple_of(owner * 2 * step + half * step, step), step)
            out_ref[half, :step, :cut] = jnp.dot(
                left[at, :], right[...], preferred_element_type=jnp.float32
            ).astype(out_ref.dtype)
            out_ref[half, :step, cut:] = jnp.dot(
                left_out[at, :], right_out[...], preferred_element_type=jnp.float32
            ).astype(out_ref.dtype)
        rows = gains_ref.shape[1] // 2
        mine = pl.ds(pl.multiple_of(owner * rows, rows), rows)
        wide = out_ref.shape[2] - rows
        block = jnp.concatenate(
            [
                jnp.concatenate([gains_ref[0:1, mine], gains_ref[1:2, 0:wide]], axis=1),
                jnp.concatenate([ffn_gain_ref[:, mine], gains_ref[2:3, 0:wide]], axis=1),
                jnp.zeros((GAIN_ROWS - 2, out_ref.shape[2]), jnp.float32),
            ],
            axis=0,
        )
        out_ref[0, step:, :] = block.astype(out_ref.dtype)
        out_ref[1, step:, :] = jnp.zeros((GAIN_ROWS, out_ref.shape[2]), out_ref.dtype)


def attention_products(here, pair_plane, shares, gains, ffn_gain):
    _, width, tokens = pair_plane[0].shape
    cut = shares[0].shape[0] - tokens
    shape = (2, width // 4 + GAIN_ROWS, cut + tokens)
    outs = [jax.ShapeDtypeStruct(shape, jnp.bfloat16), jax.ShapeDtypeStruct(shape, jnp.float32)]
    return call_with_here(
        attention_product_kernel,
        here,
        (1,),
        [*pair_plane, *shares, gains, ffn_gain],
        [whole(a) for a in (*pair_plane, *shares, gains, ffn_gain)],
        outs,
        [whole(o) for o in outs],
        [
            pltpu.VMEM((width, 4 * tokens), jnp.bfloat16),
            pltpu.VMEM((4 * tokens, cut), jnp.bfloat16),
            pltpu.VMEM((width, 4 * tokens), jnp.bfloat16),
            pltpu.VMEM((4 * tokens, tokens), jnp.bfloat16),
        ],
        micros=3,
    )


def place_gate_up_kernel(here, *refs):
    mine, across, beside, diagonal, out_ref = *refs[:4], refs[-1]
    pieces = (mine, across, beside, diagonal)
    wide = mine.shape[2]
    for case in range(4):
        core, y = case // 2, case % 2

        @pl.when((here[1] == core) & (here[2] == y))
        def _(core=core, y=y):
            for kind in range(2):
                for column in range(2):
                    value = pieces[(y ^ column) * 2 + (core ^ kind)][0]
                    out_ref[:, kind, column * wide : (column + 1) * wide] = value.astype(
                        jnp.float32
                    )


def place_gate_up(here, chunk, pieces, before):
    _, rows, wide = pieces[0].shape
    step = 64
    blocks = rows // step

    def source(i, here):
        return ((i // blocks) ^ here[0], i % blocks, 0)

    arrays = list(pieces)
    specs = [pl.BlockSpec((1, step, wide), source)] * 4
    aliases = {}
    if before is not None:
        arrays.append(before)
        specs.append(pl.BlockSpec(memory_space=pl.ANY))
        aliases = {5: 0}
    (out,) = call_with_here(
        place_gate_up_kernel,
        here,
        (2 * blocks,),
        arrays,
        specs,
        [jax.ShapeDtypeStruct((2 * rows, 2, 2 * wide * CHUNKS), jnp.float32)],
        [pl.BlockSpec((step, 2, 2 * wide), lambda i, here: (i, 0, chunk))],
        aliases=aliases,
        micros=0,
    )
    return out


def place_down(here, pieces):
    _, rows, columns = pieces[0].shape

    def kernel(here, *refs):
        for s in range(8):

            @pl.when(pl.program_id(0) == s)
            def _(s=s):
                refs[4][...] = refs[s % 4][s // 4].astype(jnp.float32)

    def target(s, here):
        half = (s // 4) ^ here[0]
        y = ((s // 2) % 2) ^ here[2]
        core = (s % 2) ^ here[1]
        return ((core * 2 + y) * 2 + half, 0)

    (out,) = call_with_here(
        kernel,
        here,
        (8,),
        list(pieces),
        [whole(v) for v in pieces],
        [jax.ShapeDtypeStruct((rows * 8, columns), jnp.float32)],
        [pl.BlockSpec((rows, columns), target)],
    )
    return out


def place_attention(here, pieces, cut):
    _, rows, columns = pieces[0].shape
    rows -= GAIN_ROWS

    def kernel(here, *refs):
        qkv_ref, out_ref, gains_ref = refs[4:]
        for s in range(8):

            @pl.when(pl.program_id(0) == s)
            def _(s=s):
                value = refs[s % 4][s // 4]
                qkv_ref[...] = value[:rows, :cut].astype(jnp.float32)
                out_ref[...] = value[:rows, cut:].astype(jnp.float32)
                gains = value[rows:].astype(jnp.float32)
                gains_ref[...] = gains if s == 0 else gains_ref[...] + gains

    def target(s, here):
        half = (s // 4) ^ here[0]
        return (half, ((s % 2) ^ here[1]) * 2 + (((s // 2) % 2) ^ here[2]))

    shape = jax.ShapeDtypeStruct
    f32 = jnp.float32
    gain_shape = (GAIN_ROWS, columns)
    return call_with_here(
        kernel,
        here,
        (8,),
        list(pieces),
        [whole(v) for v in pieces],
        [
            shape((2 * rows, 4 * cut), f32),
            shape((2 * rows, 4 * (columns - cut)), f32),
            shape(gain_shape, f32),
        ],
        [
            pl.BlockSpec((rows, cut), target),
            pl.BlockSpec((rows, columns - cut), target),
            pl.BlockSpec(gain_shape, lambda s, here: (0, 0)),
        ],
    )


def on_block(
    tokens,
    qkv_weight,
    out_weight,
    gate_up_weight,
    down_weight,
    attn_gain,
    ffn_gain,
    query_gain,
    key_gain,
    seq_lengths,
    block_order,
    cotangent,
):
    inputs = tokens[0].astype(jnp.float32)
    rows_here = inputs.shape[0]
    ctx_size = lax.axis_size("ctx")
    ctx_index = lax.axis_index("ctx")
    per_group = HEADS // KV_HEADS
    q_width = HEADS * HD
    kv_width = KV_HEADS * HD
    order_row = block_order[0]
    lengths_row = seq_lengths[0]
    slots = jnp.arange(rows_here, dtype=jnp.int32) // BLK + ctx_index * (rows_here // BLK)
    table = slots[:, None] == jnp.arange(order_row.shape[0], dtype=jnp.int32)[None, :]
    packed = (
        jnp.sum(jnp.where(table, order_row[None, :], 0), axis=1) * BLK
        + jnp.arange(rows_here, dtype=jnp.int32) % BLK
    )
    local = packed - starts_of(packed, lengths_row)
    frequency = ROPE_BASE ** (-2.0 * jnp.arange(HD // 2, dtype=jnp.float32) / HD)
    angle = frequency[:, None] * local.astype(jnp.float32)[None, :]
    cosine = jnp.cos(angle)[None]
    sine = jnp.sin(angle)[None]
    bf16, f32 = jnp.bfloat16, jnp.float32
    parts = ctx_size // HEADS
    part = ctx_index // HEADS
    part_blocks = HEADS * rows_here // BLK
    q_order = lax.dynamic_slice_in_dim(order_row, part * part_blocks, part_blocks)
    q_slot, q_place, q_start = block_tables(q_order, lengths_row)
    q_slot = q_slot + part * part_blocks
    kv_slot, _, _ = block_tables(order_row, lengths_row)
    first = jnp.min(q_start.reshape(-1, TILE), axis=1) // TILE
    last = jnp.max(q_place.reshape(-1, TILE), axis=1) // TILE + 1
    tables = (q_slot, kv_slot, first, last)
    q_rows, kv_rows = part_blocks * BLK, order_row.shape[0] * BLK

    links = Links(ctx_size)
    here = links.here
    width = inputs.shape[1]
    rows = qkv_weight.shape[0]
    part_rows = rows // 4

    def quarter_rows(weight):
        return lax.dynamic_slice_in_dim(weight, links.quarter * part_rows, part_rows)

    qkv_piece = quarter_rows(qkv_weight)
    gains_here = jnp.concatenate([after(attn_gain, qkv_piece), ffn_gain, query_gain, key_gain])
    gains_there = links.over_x(gains_here)

    def gain_of(at, size):
        mine, other = gains_here[at : at + size], gains_there[at : at + size]
        return jnp.where(
            links.side == 0, jnp.concatenate([mine, other]), jnp.concatenate([other, mine])
        ).astype(f32)

    gain_attn = gain_of(0, rows)
    gain_ffn = gain_of(rows, rows)
    gain_query = gain_of(2 * rows, HD // 2)
    gain_key = gain_of(2 * rows + HD // 2, HD // 2)
    ff_chunk = gate_up_weight.shape[2] // CHUNKS

    def gate_up_piece(chunk):
        piece = lax.dynamic_slice(
            gate_up_weight,
            (links.quarter * part_rows, 0, chunk * ff_chunk),
            (part_rows, 2, ff_chunk),
        )
        return [piece[:, 0], piece[:, 1]]

    d_ffn = cotangent[0]
    d_beside = links.over_y(d_ffn)
    qkv_there = after(links.over_x(qkv_piece), d_beside)
    first_piece = jnp.concatenate([*gate_up_piece(0), quarter_rows(out_weight)], axis=1)
    second_piece = jnp.concatenate(gate_up_piece(1), axis=1)
    down_piece = lax.dynamic_slice_in_dim(
        down_weight, links.quarter * (width // 4), width // 4, 1
    )
    d_ffn = cotangent[0]
    tokens_here = tokens[0]
    qkv_there = after(qkv_there, first_piece)
    first_there = links.over_x(after(first_piece, qkv_there))
    gate_up = jnp.transpose(after(gate_up_weight, qkv_there), (1, 0, 2))
    qkv_beside = links.over_y(qkv_there)
    qkv_pieces = (
        qkv_there,
        links.over_core(qkv_there),
        qkv_beside,
        links.over_core(after(qkv_beside, gate_up)),
    )
    sent, w_qkv, q_raw, k_raw, q_scale, k_scale, normed, scale_one = project(
        here, tokens_here, gain_attn[None], qkv_weight, qkv_pieces,
        gain_query[:, None], gain_key[:, None], cosine[0], sine[0],
    )
    got = lax.all_to_all(sent, "ctx", 0, 0, tiled=True)
    first_there = after(first_there, sent)
    down_there = links.over_x(after(down_piece, first_there))
    first_beside = links.over_y(first_there)
    q_place, q_start = q_place[None], q_start[None]
    shape = jax.ShapeDtypeStruct
    attn_sent, *held = kernel_call(
        attend_kernel,
        tables,
        (got, q_place, q_start),
        [
            shape((ctx_size, HD, rows_here), bf16),
            shape((q_rows, HD), bf16),
            shape((HD, q_rows), bf16),
            shape((kv_rows, HD), bf16),
            shape((HD, kv_rows), bf16),
            shape((kv_rows, HD), bf16),
            shape((HD, q_rows), f32),
            shape((1, q_rows), f32),
        ],
        [pltpu.VMEM((HD, kv_rows), bf16)],
        ATTEND,
    )
    attn_in = lax.dynamic_slice_in_dim(
        lax.all_to_all(attn_sent, "ctx", 0, 0, tiled=True), part * HEADS, HEADS
    ).reshape(q_width, rows_here)
    down_there = after(down_there, attn_sent)
    second_there = links.over_x(after(second_piece, down_there))
    down_beside = links.over_y(down_there)

    def spread(there, beside, time):
        there, beside = after(there, time), after(beside, time)
        return (there, links.over_core(there), beside, links.over_core(beside))

    first_pieces = spread(first_there, first_beside, attn_sent)
    down_pieces = spread(down_there, down_beside, attn_in)
    second_beside = links.over_y(second_there)
    w_out, h_one, scale_two, two, two_t = attend_out(
        here, attn_in, tokens_here, gain_ffn[None], out_weight, first_pieces
    )
    two_beside = links.over_y(two_t)
    dealt_here, (out_sum, two_sum) = ffn(
        here, 0, two, d_ffn, gate_up, first_pieces, down_weight, down_pieces, [h_one]
    )
    second_beside = after(second_beside, out_sum)
    second_pieces = (
        second_there, links.over_core(second_there), second_beside, links.over_core(second_beside)
    )
    near, far, give, give_far = dealt_here
    got_far = links.over_core(give_far)
    first_shares = (near, links.over_core(give), links.over_y(far), links.over_y(got_far))
    out_sum = after(out_sum, got_far)
    dealt_here, (output, d_h_one, d_attn, d_heads, ffn_gain_term) = ffn(
        here, 1, two, d_ffn, gate_up, second_pieces, down_weight, down_pieces,
        [out_sum, two_sum, h_one, scale_two, w_out], gain_ffn[None],
    )
    second_shares = links.deal_plane(*dealt_here)

    def plane(value, beside, time):
        value, beside = after(value, time), after(beside, time)
        return (value, links.over_core(value), beside, links.over_core(beside))

    columns = ff_chunk // 2
    d_heads = d_heads.reshape(HEADS, HD, rows_here)
    d_got = lax.all_to_all(d_heads, "ctx", 0, 0, tiled=True)
    pair = jnp.stack([after(normed, d_heads), attn_in])
    two_plane = plane(two_t, two_beside, pair)
    first_products = wide_products(
        here, two_plane, [after(v, d_heads) for v in first_shares], columns
    )
    pair_across = links.over_core(pair)
    d_got = after(d_got, first_products[0], pair_across)
    (d_sent,) = kernel_call(
        attend_back_kernel,
        tables,
        (d_got, q_place, q_start, *held),
        [shape((ctx_size, 3 * HD, rows_here), bf16)],
        [
            pltpu.VMEM((HD, q_rows), bf16),
            pltpu.VMEM((q_rows, HD), bf16),
            pltpu.VMEM((kv_rows, HD), f32),
            pltpu.VMEM((kv_rows, HD), f32),
        ],
        ATTEND_BACK,
    )
    first_got = links.over_x(first_products[0])
    d_sent = after(d_sent, first_got, *second_shares[2:])
    d_back = lax.all_to_all(d_sent, "ctx", 0, 0, tiled=True)
    d_plane = plane(d_ffn, d_beside, d_sent)
    second_products = wide_products(
        here, two_plane, [after(v, d_plane[1]) for v in second_shares], columns
    )
    down_terms = down_products(
        here, d_plane, first_shares, second_shares, columns // 2
    )
    second_got = links.over_x(after(second_products[0], first_got))
    pair_beside = links.over_y(after(pair, d_sent))
    d_back = after(d_back, down_terms[0], pair_beside, second_got)
    *d_shares, d_inputs, gain_sums = attention_back(
        here,
        [
            d_back, q_raw, k_raw, q_scale, k_scale, gain_query[:, None], gain_key[:, None],
            cosine[0], sine[0], w_qkv, tokens_here, scale_one, gain_attn[None], d_h_one, d_attn,
        ],
    )
    down_got = links.over_x(after(down_terms[0], second_got))
    near, far, give, give_far = d_shares
    got, got_far = links.over_core(give), links.over_core(give_far)
    attention_shares = (near, got, links.over_y(far), links.over_y(got_far))
    pair_plane = (pair, pair_across, pair_beside, links.over_core(after(pair_beside, d_sent)))

    kept = [first_products[1], second_products[1], down_terms[1], None]
    got = [first_got, second_got, down_got, None]
    given, part, across, full, back, beside = ([None] * 4 for _ in range(6))

    def give_half(n):
        given[n] = links.over_z(links.half_of(kept[n], got[n], False))

    def sum_part(n, time):
        part[n] = add(links.half_of(kept[n], got[n], True), after(given[n], time))
        across[n] = links.over_two_z(part[n])

    def sum_full(n, time):
        full[n] = add(part[n], after(across[n], time))
        back[n] = links.over_z(full[n])

    def spread_y(n, time):
        full[n] = jnp.stack([full[n], after(back[n], time)])
        beside[n] = links.over_y(full[n])

    def spread_core(n, time):
        beside[n] = after(beside[n], time)
        return (full[n], links.over_core(full[n]), beside[n], links.over_core(beside[n]))

    give_half(0)
    given[0] = after(given[0], down_terms[0])
    sum_part(0, second_got)
    give_half(1)
    sum_part(1, got_far)
    got[2] = after(got[2], part[1], attention_shares[1], pair_plane[3])
    give_half(2)
    sum_full(0, got[2])
    attention_shares = (*attention_shares[:2], *(after(v, full[0]) for v in attention_shares[2:]))
    attention_terms = attention_products(
        here, pair_plane, attention_shares, gain_sums, ffn_gain_term
    )
    kept[3] = attention_terms[1]
    attention_got = links.over_x(attention_terms[0])
    spread_y(0, attention_terms[0])
    sum_part(2, full[0])
    sum_full(1, part[2])
    got[3] = after(attention_got, full[1])
    give_half(3)
    first_pieces = spread_core(0, got[3])
    spread_y(1, beside[0])
    sum_part(3, full[1])
    sum_full(2, part[3])
    first_placed = place_gate_up(here, 0, first_pieces, None)
    second_pieces = spread_core(1, full[2])
    spread_y(2, (first_placed, beside[1]))
    sum_full(3, full[2])
    grad_gate_up = place_gate_up(here, 1, second_pieces, first_placed)
    spread_y(3, full[2])
    grad_down = place_down(here, spread_core(2, grad_gate_up))
    cut = qkv_weight.shape[1] // 4
    grad_qkv, grad_out, gain_sums = place_attention(here, spread_core(3, grad_gate_up), cut)
    at = links.side * (HD // 2)
    gain_grads = [
        gain_sums[0, :rows],
        gain_sums[1, :rows],
        lax.dynamic_slice_in_dim(gain_sums[0, rows : rows + HD], at, HD // 2),
        lax.dynamic_slice_in_dim(gain_sums[1, rows : rows + HD], at, HD // 2),
    ]
    return (
        output[None],
        d_inputs[None],
        grad_qkv,
        grad_out,
        grad_gate_up,
        grad_down,
        *gain_grads,
    )


def on_device(
    tokens,
    qkv_weight,
    out_weight,
    gate_up_weight,
    down_weight,
    attn_gain,
    ffn_gain,
    query_gain,
    key_gain,
    seq_lengths,
    block_order,
    cotangent,
):
    inputs = tokens[0].astype(jnp.float32)
    rows_here = inputs.shape[0]
    ctx_size = lax.axis_size("ctx")
    ctx_index = lax.axis_index("ctx")
    per_group = HEADS // KV_HEADS
    q_width = HEADS * HD
    kv_width = KV_HEADS * HD
    order_row = block_order[0]
    lengths_row = seq_lengths[0]
    slots = jnp.arange(rows_here, dtype=jnp.int32) // BLK + ctx_index * (rows_here // BLK)
    table = slots[:, None] == jnp.arange(order_row.shape[0], dtype=jnp.int32)[None, :]
    packed = (
        jnp.sum(jnp.where(table, order_row[None, :], 0), axis=1) * BLK
        + jnp.arange(rows_here, dtype=jnp.int32) % BLK
    )
    local = packed - starts_of(packed, lengths_row)
    frequency = ROPE_BASE ** (-2.0 * jnp.arange(HD // 2, dtype=jnp.float32) / HD)
    angle = frequency[:, None] * local.astype(jnp.float32)[None, :]
    cosine = jnp.cos(angle)[None]
    sine = jnp.sin(angle)[None]
    bf16, f32 = jnp.bfloat16, jnp.float32
    parts = ctx_size // HEADS
    part = ctx_index // HEADS
    part_blocks = HEADS * rows_here // BLK
    q_order = lax.dynamic_slice_in_dim(order_row, part * part_blocks, part_blocks)
    q_slot, q_place, q_start = block_tables(q_order, lengths_row)
    q_slot = q_slot + part * part_blocks
    kv_slot, _, _ = block_tables(order_row, lengths_row)
    first = jnp.min(q_start.reshape(-1, TILE), axis=1) // TILE
    last = jnp.max(q_place.reshape(-1, TILE), axis=1) // TILE + 1
    tables = (q_slot, kv_slot, first, last)
    q_rows, kv_rows = part_blocks * BLK, order_row.shape[0] * BLK

    def fetch_attention():
        return (
            lax.all_gather(qkv_weight, "fsdp", axis=0, tiled=True),
            lax.all_gather(out_weight, "fsdp", axis=0, tiled=True),
            lax.all_gather(attn_gain, "fsdp", axis=0, tiled=True),
            lax.all_gather(ffn_gain, "fsdp", axis=0, tiled=True),
            lax.all_gather(query_gain, "fsdp", axis=0, tiled=True),
            lax.all_gather(key_gain, "fsdp", axis=0, tiled=True),
        )

    w_qkv, w_out, gain_attn, gain_ffn, gain_query, gain_key = fetch_attention()
    gain_attn = gain_attn.astype(jnp.float32)
    gain_ffn = gain_ffn.astype(jnp.float32)
    gain_query = gain_query.astype(jnp.float32)
    gain_key = gain_key.astype(jnp.float32)
    scale_one = rms_scale(inputs)
    normed = (inputs * scale_one * gain_attn).astype(jnp.bfloat16)
    projected = lax.dot_general(
        w_qkv, normed, (((0,), (1,)), ((), ())), preferred_element_type=f32
    )
    q_raw = projected[:q_width].reshape(HEADS, HD, rows_here)
    k_raw = projected[q_width : q_width + kv_width].reshape(KV_HEADS, HD, rows_here)
    values_here = projected[q_width + kv_width :].reshape(KV_HEADS, HD, rows_here).astype(bf16)
    q_scale = rms_scale(q_raw, 1)
    k_scale = rms_scale(k_raw, 1)
    column_query, column_key = gain_query[:, None], gain_key[:, None]
    queries = rope(q_raw * q_scale * column_query, cosine, sine).astype(bf16)
    keys_here = rope(k_raw * k_scale * column_key, cosine, sine).astype(bf16)
    sent = jnp.concatenate(
        [queries, jnp.repeat(keys_here, per_group, 0), jnp.repeat(values_here, per_group, 0)], axis=1
    )
    sent = jnp.concatenate([sent] * parts, axis=0)
    got = lax.all_to_all(sent, "ctx", 0, 0, tiled=True)
    q_place, q_start = q_place[None], q_start[None]
    shape = jax.ShapeDtypeStruct
    attn_sent, *held = kernel_call(
        attend_kernel,
        tables,
        (got, q_place, q_start),
        [
            shape((ctx_size, HD, rows_here), bf16),
            shape((q_rows, HD), bf16),
            shape((HD, q_rows), bf16),
            shape((kv_rows, HD), bf16),
            shape((HD, kv_rows), bf16),
            shape((kv_rows, HD), bf16),
            shape((HD, q_rows), f32),
            shape((1, q_rows), f32),
        ],
        [pltpu.VMEM((HD, kv_rows), bf16)],
        ATTEND,
    )
    attn_in = lax.dynamic_slice_in_dim(
        lax.all_to_all(attn_sent, "ctx", 0, 0, tiled=True), part * HEADS, HEADS
    ).reshape(q_width, rows_here)
    h_one = inputs + lax.dot_general(
        attn_in, w_out, (((0,), (0,)), ((), ())), preferred_element_type=f32
    )
    scale_two = rms_scale(h_one)
    normed_two = (h_one * scale_two * gain_ffn).astype(jnp.bfloat16)
    columns = normed_two
    gate_up = jnp.einsum(
        "tr,rgf->tgf",
        columns,
        lax.all_gather(gate_up_weight, "fsdp", axis=0, tiled=True),
        preferred_element_type=jnp.float32,
    )
    gate = gate_up[:, 0]
    upper = gate_up[:, 1]
    sigma = jax.nn.sigmoid(gate)
    hidden = (gate * sigma * upper).astype(jnp.bfloat16)
    columns = hidden
    ffn_out = jnp.dot(
        columns,
        lax.all_gather(down_weight, "fsdp", axis=0, tiled=True),
        preferred_element_type=jnp.float32,
    )
    output = (h_one + ffn_out).astype(jnp.bfloat16)
    d_out = cotangent[0].astype(jnp.float32)
    d_ffn = d_out.astype(jnp.bfloat16)
    d_hidden = lax.dot_general(
        d_ffn,
        lax.all_gather(down_weight, "fsdp", axis=0, tiled=True),
        (((1,), (1,)), ((), ())),
        preferred_element_type=jnp.float32,
    )
    d_gate = d_hidden * upper * sigma * (1.0 + gate * (1.0 - sigma))
    d_upper = d_hidden * gate * sigma
    d_gate_up = jnp.stack([d_gate, d_upper], axis=1).astype(jnp.bfloat16)
    d_normed_two = jnp.einsum(
        "tgf,rgf->tr",
        d_gate_up,
        lax.all_gather(gate_up_weight, "fsdp", axis=0, tiled=True),
        preferred_element_type=jnp.float32,
    )
    columns = normed_two
    grad_gate_up = lax.psum_scatter(
        jnp.einsum("tr,tgf->rgf", columns, d_gate_up, preferred_element_type=jnp.float32).astype(
            jnp.bfloat16
        ),
        "fsdp",
        scatter_dimension=0,
        tiled=True,
    )
    columns = hidden
    grad_down = lax.psum_scatter(
        lax.dot_general(
            columns, d_ffn, (((0,), (0,)), ((), ())), preferred_element_type=jnp.float32
        ).astype(jnp.bfloat16),
        "fsdp",
        scatter_dimension=0,
        tiled=True,
    )
    d_norm_two, ffn_gain_term = norm_back(d_normed_two, h_one, scale_two, gain_ffn)
    d_h_one = d_out + d_norm_two
    d_attn = d_h_one.astype(jnp.bfloat16)
    grad_out_here = jnp.dot(attn_in, d_attn, preferred_element_type=f32)
    d_heads = lax.dot_general(
        w_out, d_attn, (((1,), (1,)), ((), ())), preferred_element_type=f32
    ).astype(bf16)
    d_heads = jnp.concatenate([d_heads.reshape(HEADS, HD, rows_here)] * parts, axis=0)
    d_got = lax.all_to_all(d_heads, "ctx", 0, 0, tiled=True)
    (d_sent,) = kernel_call(
        attend_back_kernel,
        tables,
        (d_got, q_place, q_start, *held),
        [shape((ctx_size, 3 * HD, rows_here), bf16)],
        [
            pltpu.VMEM((HD, q_rows), bf16),
            pltpu.VMEM((q_rows, HD), bf16),
            pltpu.VMEM((kv_rows, HD), f32),
            pltpu.VMEM((kv_rows, HD), f32),
        ],
        ATTEND_BACK,
    )
    d_back = lax.all_to_all(d_sent, "ctx", 0, 0, tiled=True)
    d_query = lax.dynamic_slice_in_dim(d_back[:, :HD], part * HEADS, HEADS).astype(f32)
    d_key_value = jnp.sum(
        d_back[:, HD:].reshape(parts, KV_HEADS, per_group, 2 * HD, rows_here).astype(f32),
        axis=(0, 2),
    )
    dq_normed = rope_back(d_query, cosine, sine)
    dk_normed = rope_back(d_key_value[:, :HD], cosine, sine)
    dq_raw, query_term = norm_back(dq_normed, q_raw, q_scale, column_query, 1)
    dk_raw, key_term = norm_back(dk_normed, k_raw, k_scale, column_key, 1)
    d_projected = jnp.concatenate(
        [
            dq_raw.reshape(q_width, rows_here).astype(bf16),
            dk_raw.reshape(kv_width, rows_here).astype(bf16),
            d_key_value[:, HD:].reshape(kv_width, rows_here).astype(bf16),
        ],
        axis=0,
    )
    grad_qkv_here = lax.dot_general(
        normed, d_projected, (((0,), (1,)), ((), ())), preferred_element_type=f32
    )
    d_normed = lax.dot_general(
        d_projected, w_qkv, (((0,), (1,)), ((), ())), preferred_element_type=f32
    )
    d_norm_one, attn_gain_term = norm_back(d_normed, inputs, scale_one, gain_attn)
    d_inputs = d_h_one + d_norm_one
    shard_qkv, shard_out, shard_attn_gain, shard_ffn_gain, shard_query_gain, shard_key_gain = (
        lax.psum_scatter(
            grad_qkv_here.astype(jnp.bfloat16), "fsdp", scatter_dimension=0, tiled=True
        ).astype(jnp.float32),
        lax.psum_scatter(
            grad_out_here.astype(jnp.bfloat16), "fsdp", scatter_dimension=0, tiled=True
        ).astype(jnp.float32),
        lax.psum_scatter(
            jnp.sum(attn_gain_term, axis=0).astype(jnp.bfloat16),
            "fsdp",
            scatter_dimension=0,
            tiled=True,
        ).astype(jnp.float32),
        lax.psum_scatter(
            jnp.sum(ffn_gain_term, axis=0).astype(jnp.bfloat16),
            "fsdp",
            scatter_dimension=0,
            tiled=True,
        ).astype(jnp.float32),
        lax.psum_scatter(
            jnp.sum(query_term, axis=(0, 2)).astype(jnp.bfloat16),
            "fsdp",
            scatter_dimension=0,
            tiled=True,
        ).astype(jnp.float32),
        lax.psum_scatter(
            jnp.sum(key_term, axis=(0, 2)).astype(jnp.bfloat16),
            "fsdp",
            scatter_dimension=0,
            tiled=True,
        ).astype(jnp.float32),
    )
    summed_grads = (
        lax.psum(shard_qkv.astype(jnp.bfloat16), "ctx").astype(jnp.float32),
        lax.psum(shard_out.astype(jnp.bfloat16), "ctx").astype(jnp.float32),
        lax.psum(grad_gate_up, "ctx").astype(jnp.float32),
        lax.psum(grad_down, "ctx").astype(jnp.float32),
        lax.psum(shard_attn_gain.astype(jnp.bfloat16), "ctx").astype(jnp.float32),
        lax.psum(shard_ffn_gain.astype(jnp.bfloat16), "ctx").astype(jnp.float32),
        lax.psum(shard_query_gain.astype(jnp.bfloat16), "ctx").astype(jnp.float32),
        lax.psum(shard_key_gain.astype(jnp.bfloat16), "ctx").astype(jnp.float32),
    )
    return (
        output[None],
        d_inputs[None],
        summed_grads[0],
        summed_grads[1],
        summed_grads[2],
        summed_grads[3],
        summed_grads[4],
        summed_grads[5],
        summed_grads[6],
        summed_grads[7],
    )


def solution(mesh):
    block = mesh.shape["fsdp"] == 2 and mesh.shape["ctx"] == 16
    return jax.shard_map(
        on_block if block else on_device,
        mesh=mesh,
        in_specs=(
            P("fsdp", "ctx", None),
            P("fsdp", None),
            P("fsdp", None),
            P("fsdp", None, None),
            P("fsdp", None),
            P("fsdp"),
            P("fsdp"),
            P("fsdp"),
            P("fsdp"),
            P("fsdp", None),
            P("fsdp", None),
            P("fsdp", "ctx", None),
        ),
        out_specs=(
            P("fsdp", "ctx", None),
            P("fsdp", "ctx", None),
            P("fsdp", None),
            P("fsdp", None),
            P("fsdp", None, None),
            P("fsdp", None),
            P("fsdp"),
            P("fsdp"),
            P("fsdp"),
            P("fsdp"),
        ),
        check_vma=False,
    )
```

```python
import functools

import jax
import jax.numpy as jnp
from jax import lax
from jax.experimental import pallas as pl
from jax.experimental.pallas import tpu as pltpu
from jax.sharding import PartitionSpec as P

HEADS = 16
KV_HEADS = 8
HD = 64
BLK = 128
TILE = 512
CHUNKS = 2
PROJECT = 0
ATTEND = 0
OUT = 0
FFN = (0, 0)
ATTEND_BACK = 25


EPSILON = 1e-05
ROPE_BASE = 1000000.0
LOG2E = 1.4426950408889634
SCORE_SCALE = LOG2E * HD ** (-0.5)


def rms_scale(values, axis=-1):
    return lax.rsqrt(jnp.mean(values * values, axis=axis, keepdims=True) + EPSILON)


def norm_back(grad_normed, inputs, scale, gain, axis=-1):
    scaled = grad_normed * gain
    grad_in = scale * scaled - inputs * scale * scale * scale * jnp.mean(
        scaled * inputs, axis=axis, keepdims=True
    )
    return (grad_in, grad_normed * inputs * scale)


def rope(values, cosine, sine):
    half = HD // 2
    first, second = values[:, :half], values[:, half:]
    return jnp.concatenate([first * cosine - second * sine, second * cosine + first * sine], axis=1)


def rope_back(values, cosine, sine):
    half = HD // 2
    first, second = values[:, :half], values[:, half:]
    return jnp.concatenate([first * cosine + second * sine, second * cosine - first * sine], axis=1)


def starts_of(packed, lengths_row):
    ends = jnp.cumsum(lengths_row)
    past = packed[:, None] >= ends[None, :]
    return jnp.sum(jnp.where(past, lengths_row[None, :], 0), axis=1)


def block_tables(order, lengths_row):
    count = order.shape[0]
    rank = jnp.sum((order[None, :] < order[:, None]).astype(jnp.int32), axis=1)
    hit = rank[None, :] == jnp.arange(count, dtype=jnp.int32)[:, None]
    slot = jnp.sum(jnp.where(hit, jnp.arange(count, dtype=jnp.int32)[None, :], 0), axis=1)
    block = jnp.sum(jnp.where(hit, order[None, :], 0), axis=1)
    place = (block[:, None] * BLK + jnp.arange(BLK, dtype=jnp.int32)[None, :]).reshape(-1)
    return (slot, place, starts_of(place, lengths_row))


def attend_kernel(
    q_slot, kv_slot, first, last, qkv_ref, place_ref, start_ref,
    out_ref, q_ref, qt_ref, k_ref, kt_ref, v_ref, ot_ref, total_ref, vt_ref
):
    per_device = qkv_ref.shape[2] // BLK
    kv_blocks = k_ref.shape[0] // BLK
    q_blocks = q_ref.shape[0] // BLK

    def piece(slot, lower):
        return qkv_ref[
            slot // per_device,
            lower : lower + HD,
            pl.ds(pl.multiple_of((slot % per_device) * BLK, BLK), BLK),
        ]

    for i in range(kv_blocks):
        here = slice(i * BLK, (i + 1) * BLK)
        keys = piece(kv_slot[i], HD)
        kt_ref[:, here] = keys
        k_ref[here, :] = keys.T
        values = piece(kv_slot[i], 2 * HD)
        vt_ref[:, here] = values
        v_ref[here, :] = values.T
    for i in range(q_blocks):
        here = slice(i * BLK, (i + 1) * BLK)
        queries = piece(q_slot[i], 0)
        qt_ref[:, here] = queries
        q_ref[here, :] = queries.T
    if q_blocks < kv_blocks:
        out_ref[...] = jnp.zeros_like(out_ref)

    def tile(i, carry):
        rows = pl.ds(pl.multiple_of(i * TILE, TILE), TILE)
        queries = qt_ref[:, rows]
        place = place_ref[:, rows]
        start = start_ref[:, rows]

        def step(j, state):
            total, summed = state
            at = pl.multiple_of(j * TILE, TILE)
            scores = jnp.dot(
                k_ref[pl.ds(at, TILE), :], queries, preferred_element_type=jnp.float32
            )
            key_place = lax.broadcasted_iota(jnp.int32, (TILE, TILE), 0) + at
            allowed = (key_place <= place) & (key_place >= start)
            lifted = jnp.where(allowed, jnp.exp2(scores * SCORE_SCALE), 0.0)
            total = total + jnp.sum(lifted, axis=0, keepdims=True)
            summed = summed + jnp.dot(
                vt_ref[:, pl.ds(at, TILE)],
                lifted.astype(jnp.bfloat16),
                preferred_element_type=jnp.float32,
            )
            return (total, summed)

        total, summed = lax.fori_loop(
            first[i],
            last[i],
            step,
            (jnp.zeros((1, TILE), jnp.float32), jnp.zeros((HD, TILE), jnp.float32)),
        )
        attn = summed / total
        ot_ref[:, rows] = attn
        total_ref[:, rows] = jnp.log(total) * LOG2E
        rounded = attn.astype(jnp.bfloat16)
        for part in range(TILE // BLK):
            slot = q_slot[i * (TILE // BLK) + part]
            out_ref[
                slot // per_device,
                :,
                pl.ds(pl.multiple_of((slot % per_device) * BLK, BLK), BLK),
            ] = rounded[:, part * BLK : (part + 1) * BLK]
        return carry

    lax.fori_loop(0, q_blocks * BLK // TILE, tile, 0)


def attend_back_kernel(
    q_slot, kv_slot, first, last, d_ref, place_ref, start_ref,
    q_ref, qt_ref, k_ref, kt_ref, v_ref, ot_ref, total_ref,
    out_ref, dt_ref, do_ref, dk_ref, dv_ref
):
    per_device = d_ref.shape[2] // BLK
    kv_blocks = k_ref.shape[0] // BLK
    q_blocks = q_ref.shape[0] // BLK

    def lanes(slot):
        return pl.ds(pl.multiple_of((slot % per_device) * BLK, BLK), BLK)

    for i in range(q_blocks):
        here = slice(i * BLK, (i + 1) * BLK)
        slot = q_slot[i]
        grads = d_ref[slot // per_device, :, lanes(slot)]
        dt_ref[:, here] = grads
        do_ref[here, :] = grads.T
    dk_ref[...] = jnp.zeros_like(dk_ref)
    dv_ref[...] = jnp.zeros_like(dv_ref)
    if q_blocks < kv_blocks:
        out_ref[...] = jnp.zeros_like(out_ref)

    def tile(i, carry):
        rows = pl.ds(pl.multiple_of(i * TILE, TILE), TILE)
        queries = qt_ref[:, rows]
        grads = dt_ref[:, rows]
        place = place_ref[:, rows]
        start = start_ref[:, rows]
        delta = jnp.sum(grads.astype(jnp.float32) * ot_ref[:, rows], axis=0, keepdims=True)
        total = total_ref[:, rows]

        def step(j, d_query):
            at = pl.multiple_of(j * TILE, TILE)
            here = pl.ds(at, TILE)
            scores = jnp.dot(k_ref[here, :], queries, preferred_element_type=jnp.float32)
            key_place = lax.broadcasted_iota(jnp.int32, (TILE, TILE), 0) + at
            allowed = (key_place <= place) & (key_place >= start)
            shares = jnp.where(allowed, jnp.exp2(scores * SCORE_SCALE - total), 0.0)
            d_shares = jnp.dot(v_ref[here, :], grads, preferred_element_type=jnp.float32)
            d_scores = (shares * (d_shares - delta)).astype(jnp.bfloat16)
            dv_ref[here, :] += jnp.dot(
                shares.astype(jnp.bfloat16), do_ref[rows, :], preferred_element_type=jnp.float32
            )
            dk_ref[here, :] += jnp.dot(
                d_scores, q_ref[rows, :], preferred_element_type=jnp.float32
            )
            return d_query + jnp.dot(
                kt_ref[:, here], d_scores, preferred_element_type=jnp.float32
            )

        d_query = lax.fori_loop(first[i], last[i], step, jnp.zeros((HD, TILE), jnp.float32))
        rounded = (d_query * HD ** (-0.5)).astype(jnp.bfloat16)
        for part in range(TILE // BLK):
            slot = q_slot[i * (TILE // BLK) + part]
            out_ref[slot // per_device, 0:HD, lanes(slot)] = rounded[
                :, part * BLK : (part + 1) * BLK
            ]
        return carry

    lax.fori_loop(0, q_blocks * BLK // TILE, tile, 0)
    for i in range(kv_blocks):
        here = slice(i * BLK, (i + 1) * BLK)
        slot = kv_slot[i]
        out_ref[slot // per_device, HD : 2 * HD, lanes(slot)] = (
            (dk_ref[here, :] * HD ** (-0.5)).T.astype(jnp.bfloat16)
        )
        out_ref[slot // per_device, 2 * HD : 3 * HD, lanes(slot)] = (
            dv_ref[here, :].T.astype(jnp.bfloat16)
        )


def cost(micros):
    return pl.CostEstimate(
        flops=1 + micros * 1_000_000_000, bytes_accessed=1, transcendentals=0
    )


def kernel_call(kernel, tables, arrays, outs, scratch, micros):
    smem = pl.BlockSpec(memory_space=pltpu.SMEM)
    vmem = pl.BlockSpec(memory_space=pltpu.VMEM)
    return pl.pallas_call(
        kernel,
        out_shape=outs,
        in_specs=[smem] * len(tables) + [vmem] * len(arrays),
        out_specs=[vmem] * len(outs),
        scratch_shapes=scratch,
        compiler_params=pltpu.CompilerParams(vmem_limit_bytes=48 * 1024 * 1024),
        cost_estimate=cost(micros),
    )(*tables, *arrays)


class Links:
    def __init__(self, ctx_size):
        self.depth = ctx_size // 4
        index = lax.axis_index("ctx")
        self.core = index % 2
        self.y = (index // 2) % 2
        self.side = lax.axis_index("fsdp")
        self.half = index // 4 % 2
        self.quarter = index % 2 * 2 + self.y
        self.here = jnp.stack([self.half, self.core, self.y, self.side]).astype(jnp.int32)

    def route(self, place):
        pairs = []
        for z in range(self.depth):
            for y in range(2):
                for core in range(2):
                    to_z, to_y, to_core = place(z, y, core)
                    pairs.append(((z * 2 + y) * 2 + core, (to_z * 2 + to_y) * 2 + to_core))
        return pairs

    def over_core(self, value):
        return lax.ppermute(value, "ctx", self.route(lambda z, y, c: (z, y, 1 - c)))

    def over_y(self, value):
        return lax.ppermute(value, "ctx", self.route(lambda z, y, c: (z, 1 - y, c)))

    def over_z(self, value):
        return lax.ppermute(value, "ctx", self.route(lambda z, y, c: (z ^ 1, y, c)))

    def over_two_z(self, value):
        return lax.ppermute(value, "ctx", self.route(lambda z, y, c: (z ^ 2, y, c)))

    def over_x(self, value):
        return lax.ppermute(value, "fsdp", [(0, 1), (1, 0)])

    def spread_plane(self, value):
        across = self.over_core(value)
        beside = self.over_y(value)
        return (value, across, beside, self.over_core(beside))

    def deal_plane(self, near, far, give, give_far):
        got, got_far = self.over_core(give), self.over_core(give_far)
        return (near, got, self.over_y(far), self.over_y(got_far))

    def half_of(self, kept, got, own):
        index = self.half if own else 1 - self.half
        return add(pick(kept, index, 0), pick(got, index, 0))


def pick(value, index, axis):
    return lax.dynamic_index_in_dim(value, index, axis, keepdims=False)


def add(left, right):
    return (left.astype(jnp.float32) + right.astype(jnp.float32)).astype(jnp.bfloat16)


def after(value, *others):
    return lax.optimization_barrier((value, *jax.tree.leaves(others)))[0]


def contract(left, right, axes):
    return lax.dot_general(
        left, right, ((axes[:1], axes[1:]), ((), ())), preferred_element_type=jnp.float32
    )


PARAMS = pltpu.CompilerParams(vmem_limit_bytes=56 * 1024 * 1024)


def call_with_here(
    kernel, here, grid, arrays, specs, outs, out_specs, scratch=(), aliases=None, micros=0
):
    return pl.pallas_call(
        kernel,
        grid_spec=pltpu.PrefetchScalarGridSpec(
            num_scalar_prefetch=1,
            grid=grid,
            in_specs=specs,
            out_specs=out_specs,
            scratch_shapes=list(scratch),
        ),
        out_shape=outs,
        input_output_aliases=aliases or {},
        compiler_params=PARAMS,
        cost_estimate=cost(micros),
    )(here, *arrays)


def whole(array):
    rank = len(array.shape)
    return pl.BlockSpec(array.shape, lambda i, here: (0,) * rank)


def project_kernel(here, *refs):
    x_ref, gain_ref, own_ref = refs[:3]
    pieces, q_gain, k_gain, cos_ref, sin_ref = refs[3:7], refs[7], refs[8], refs[9], refs[10]
    sent, weight, q_ref, k_ref, q_scale, k_scale, normed_ref, scale_ref = refs[11:]
    core, y, side = here[1], here[2], here[3]
    rows = own_ref.shape[0]
    part = rows // 4
    f32, bf16 = jnp.float32, jnp.bfloat16
    weight[pl.ds(pl.multiple_of(side * rows, rows), rows), :] = own_ref[...]
    for p in range(4):
        at = (1 - side) * rows + (((p % 2) ^ core) * 2 + ((p // 2) ^ y)) * part
        weight[pl.ds(pl.multiple_of(at, part), part), :] = pieces[p][...]
    x = x_ref[...].astype(f32)
    scale = rms_scale(x)
    scale_ref[...] = scale
    normed = (x * scale * gain_ref[...]).astype(bf16)
    normed_ref[...] = normed.T
    cosine, sine = cos_ref[...], sin_ref[...]
    half = HD // 2

    def turned(raw, gain, raw_ref, kept_scale, head):
        raw_ref[head * HD : (head + 1) * HD, :] = raw
        scale = rms_scale(raw, 0)
        kept_scale[head : head + 1, :] = scale
        value = raw * scale * gain
        first, second = value[:half], value[half:]
        return jnp.concatenate(
            [first * cosine - second * sine, second * cosine + first * sine], axis=0
        ).astype(bf16)

    per_group = HEADS // KV_HEADS
    for at in range(0, weight.shape[1], 2 * BLK):
        block = jnp.dot(normed, weight[:, at : at + 2 * BLK], preferred_element_type=f32)
        turned_block = block.T
        for n in range(2 * BLK // HD):
            head = at // HD + n
            raw = turned_block[n * HD : (n + 1) * HD, :]
            if head < HEADS:
                sent[head, 0:HD, :] = turned(raw, q_gain[...], q_ref, q_scale, head)
                continue
            head -= HEADS
            if head < KV_HEADS:
                value, row = turned(raw, k_gain[...], k_ref, k_scale, head), HD
            else:
                value, row, head = raw.astype(bf16), 2 * HD, head - KV_HEADS
            for copy in range(per_group):
                sent[head * per_group + copy, row : row + HD, :] = value


def project(here, x, gain, own, pieces, q_gain, k_gain, cosine, sine):
    tokens, width = x.shape
    f32, bf16 = jnp.float32, jnp.bfloat16
    shape = jax.ShapeDtypeStruct
    arrays = [x, gain, own, *pieces, q_gain, k_gain, cosine, sine]
    outs = [
        shape((HEADS, 3 * HD, tokens), bf16),
        shape((width, own.shape[1]), bf16),
        shape((HEADS * HD, tokens), f32),
        shape((KV_HEADS * HD, tokens), f32),
        shape((HEADS, tokens), f32),
        shape((KV_HEADS, tokens), f32),
        shape((width, tokens), bf16),
        shape((tokens, 1), f32),
    ]
    return call_with_here(
        project_kernel, here, (1,), arrays, [whole(a) for a in arrays], outs,
        [whole(o) for o in outs], micros=PROJECT,
    )


def layer(array, index):
    return pl.BlockSpec((1, *array.shape[1:]), lambda i, here: (index, 0, 0))


def attend_out_kernel(here, *refs):
    attn_ref, x_ref, gain_ref, own_ref = refs[:4]
    pieces = refs[4:12]
    weight, h_ref, scale_ref, two_ref, two_t_ref = refs[12:]
    core, y, side = here[1], here[2], here[3]
    rows = own_ref.shape[0]
    part = rows // 4
    weight[pl.ds(pl.multiple_of(side * rows, rows), rows), :] = own_ref[...]
    for p in range(4):
        at = (1 - side) * rows + (((p % 2) ^ core) * 2 + ((p // 2) ^ y)) * part
        for n in range(2):
            piece = pieces[2 * p + n]
            wide = piece.shape[1]
            weight[pl.ds(pl.multiple_of(at, part), part), n * wide : (n + 1) * wide] = piece[...]
    attn = attn_ref[...].T
    h_one = x_ref[...].astype(jnp.float32) + jnp.dot(
        attn, weight[...], preferred_element_type=jnp.float32
    )
    scale = rms_scale(h_one)
    h_ref[...] = h_one
    scale_ref[...] = scale
    two = (h_one * scale * gain_ref[...]).astype(jnp.bfloat16)
    two_ref[...] = two
    two_t_ref[...] = two.T


def attend_out(here, attn, x, gain, own, pieces):
    tokens, width = x.shape
    f32, bf16 = jnp.float32, jnp.bfloat16
    shape = jax.ShapeDtypeStruct
    part = own.shape[0] // 4
    half = width // 2
    first = pieces[0].shape[1] // half - 2
    arrays = [attn, x, gain, own]
    specs = [whole(a) for a in arrays]
    for piece in pieces:
        for n in range(2):
            arrays.append(piece)
            specs.append(pl.BlockSpec((part, half), lambda i, here, n=n: (0, first + n)))
    outs = [
        shape((width, width), bf16),
        shape((tokens, width), f32),
        shape((tokens, 1), f32),
        shape((tokens, width), bf16),
        shape((width, tokens), bf16),
    ]
    return call_with_here(
        attend_out_kernel, here, (1,), arrays, specs, outs, [whole(o) for o in outs], micros=OUT
    )


def ffn_kernel(chunk, here, *refs):
    two_ref, d_ref, own_ref = refs[:3]
    pieces, down_ref, down_pieces = refs[3:7], refs[7], refs[8:12]
    if chunk == 0:
        before_refs, refs = refs[12:13], refs[13:]
        near, far, give, give_far, out_ref, d_two_ref = refs[:6]
        refs = refs[6:]
    else:
        before_refs, gain_ref, refs = refs[12:17], refs[17], refs[18:]
        near, far, give, give_far = refs[:4]
        out_ref, d_h_ref, d_attn_ref, heads_ref, gain_term_ref = refs[4:9]
        refs = refs[9:]
    weight, down, hidden_rows, out_sum, two_sum = refs[:5]
    held, weight_sem, down_sem, before_sem = refs[5:-3], refs[-3], refs[-2], refs[-1]
    core, y, side = here[1], here[2], here[3]
    f32, bf16 = jnp.float32, jnp.bfloat16
    own_rows, columns = own_ref.shape[1], own_ref.shape[2] // CHUNKS
    part = own_rows // 4
    tile = columns // FFN_TILES
    half = columns // 2

    def quarter(p):
        return ((p % 2) ^ core) * 2 + ((p // 2) ^ y)

    def copies(n):
        at = slice(n * tile, (n + 1) * tile)
        mine = pl.ds(pl.multiple_of(side * own_rows, own_rows), own_rows)
        found = [
            pltpu.make_async_copy(
                own_ref.at[:, :, chunk * columns + n * tile : chunk * columns + (n + 1) * tile],
                weight.at[:, mine, at],
                weight_sem.at[n, 0],
            )
        ]
        for p in range(4):
            rows = pl.ds(pl.multiple_of((1 - side) * own_rows + quarter(p) * part, part), part)
            for kind in range(2):
                begin = kind * columns + n * tile
                found.append(
                    pltpu.make_async_copy(
                        pieces[p].at[:, begin : begin + tile],
                        weight.at[kind, rows, at],
                        weight_sem.at[n, 1 + 2 * p + kind],
                    )
                )
        return found

    def own_down(n):
        at = slice(n * tile, (n + 1) * tile)
        return [pltpu.make_async_copy(down_ref.at[at, :], down.at[at, :], down_sem.at[n, 0])]

    def other_down(n):
        at = slice(n * tile, (n + 1) * tile)
        found = []
        for p in range(4):
            wide = down_pieces[p].shape[1]
            lanes = pl.ds(pl.multiple_of(quarter(p) * wide, wide), wide)
            found.append(
                pltpu.make_async_copy(
                    down_pieces[p].at[at, :], down.at[at, lanes], down_sem.at[n, p]
                )
            )
        return found

    def each(action, n):
        for copy in copies(n):
            action(copy)

        @pl.when(side == chunk)
        def _():
            for copy in own_down(n):
                action(copy)

        @pl.when(side != chunk)
        def _():
            for copy in other_down(n):
                action(copy)

    before = [
        pltpu.make_async_copy(ref, held[n], before_sem.at[n]) for n, ref in enumerate(before_refs)
    ]
    for n in range(FFN_TILES):
        each(lambda copy: copy.start(), n)
    for copy in before:
        copy.start()
    two = two_ref[...]
    d_ffn = d_ref[...]
    for n in range(FFN_TILES):
        each(lambda copy: copy.wait(), n)
        at = slice(n * tile, (n + 1) * tile)
        gate = jnp.dot(two, weight[0, :, at], preferred_element_type=f32)
        upper = jnp.dot(two, weight[1, :, at], preferred_element_type=f32)
        d_hidden = contract(d_ffn, down[at, :], (1, 1))
        sigma = jax.nn.sigmoid(gate)
        silu = gate * sigma
        hidden = (silu * upper).astype(bf16)
        d_gate = (d_hidden * upper * sigma * (1.0 + gate * (1.0 - sigma))).astype(bf16)
        d_upper = (d_hidden * silu).astype(bf16)
        out_term = jnp.dot(hidden, down[at, :], preferred_element_type=f32)
        two_term = contract(d_gate, weight[0, :, at], (1, 1)) + contract(
            d_upper, weight[1, :, at], (1, 1)
        )
        out_sum[...] = out_term if n == 0 else out_sum[...] + out_term
        two_sum[...] = two_term if n == 0 else two_sum[...] + two_term
        hidden_rows[:, at] = hidden
        mine = jnp.where(core == 0, d_gate, d_upper)
        other = jnp.where(core == 0, d_upper, d_gate)
        for column in range(2):
            begin, end = max(n * tile, column * half), min((n + 1) * tile, (column + 1) * half)
            if begin >= end:
                continue
            source = slice(begin - n * tile, end - n * tile)
            target = slice(begin - column * half, end - column * half)
            first, second = mine[:, source], other[:, source]

            @pl.when(y == column)
            def _(first=first, second=second, target=target):
                near[:, target] = first
                give[:, target] = second

            @pl.when(y != column)
            def _(first=first, second=second, target=target):
                far[:, target] = first
                give_far[:, target] = second

    share = half // 2
    target = slice(half, half + share)
    for owner in range(2):
        lower = hidden_rows[:, owner * half : owner * half + share]
        upper = hidden_rows[:, owner * half + share : (owner + 1) * half]
        close = jnp.where(y == 0, lower, upper)
        distant = jnp.where(y == 0, upper, lower)

        @pl.when(core == owner)
        def _(close=close, distant=distant):
            near[:, target] = close
            far[:, target] = distant

        @pl.when(core != owner)
        def _(close=close, distant=distant):
            give[:, target] = close
            give_far[:, target] = distant

    for copy in before:
        copy.wait()
    if chunk == 0:
        out_ref[...] = held[0][...] + out_sum[...]
        d_two_ref[...] = two_sum[...]
    else:
        out_before, two_before, h_one, scale, w_out = held
        out_ref[...] = (out_before[...] + out_sum[...]).astype(bf16)
        d_norm, gain_term = norm_back(
            two_before[...] + two_sum[...], h_one[...], scale[...], gain_ref[...]
        )
        gain_term_ref[...] = jnp.sum(gain_term, axis=0, keepdims=True)
        d_h_one = d_ffn.astype(f32) + d_norm
        d_h_ref[...] = d_h_one
        d_attn = d_h_one.astype(bf16)
        d_attn_ref[...] = d_attn
        heads_ref[...] = contract(w_out[...], d_attn, (1, 1)).astype(bf16)


FFN_TILES = 3


def ffn(here, chunk, two, d_ffn, own, pieces, down, down_pieces, before, gain=None):
    tokens, width = two.shape
    columns = own.shape[2] // CHUNKS
    padded = (columns // 2 + columns // 4 + BLK - 1) // BLK * BLK
    shape = jax.ShapeDtypeStruct
    f32, bf16 = jnp.float32, jnp.bfloat16
    outs = [shape((tokens, padded), bf16)] * 4
    if chunk == 0:
        outs += [shape((tokens, width), f32)] * 2
    else:
        outs += [
            shape((tokens, width), bf16),
            shape((tokens, width), f32),
            shape((tokens, width), bf16),
            shape((width, tokens), bf16),
            shape((1, width), f32),
        ]
    far_away = pl.BlockSpec(memory_space=pl.ANY)
    arrays = [two, d_ffn, own, *pieces, down, *down_pieces, *before]
    specs = [whole(two), whole(d_ffn)] + [far_away] * (len(arrays) - 2)
    if gain is not None:
        arrays.append(gain)
        specs.append(whole(gain))
    got = call_with_here(
        functools.partial(ffn_kernel, chunk),
        here,
        (1,),
        arrays,
        specs,
        outs,
        [whole(o) for o in outs],
        [
            pltpu.VMEM((2, width, columns), bf16),
            pltpu.VMEM((columns, width), bf16),
            pltpu.VMEM((tokens, columns), bf16),
            pltpu.VMEM((tokens, width), f32),
            pltpu.VMEM((tokens, width), f32),
        ]
        + [pltpu.VMEM(v.shape, v.dtype) for v in before]
        + [
            pltpu.SemaphoreType.DMA((FFN_TILES, 9)),
            pltpu.SemaphoreType.DMA((FFN_TILES, 4)),
            pltpu.SemaphoreType.DMA((len(before),)),
        ],
        micros=FFN[chunk],
    )
    return got[:4], got[4:]


def wide_product_kernel(here, *refs):
    planes, terms = refs[:4], refs[4:8]
    sent, kept, left, right = refs[8:]
    tokens = planes[0].shape[1]
    columns = right.shape[1]
    for i in range(4):
        left[:, i * tokens : (i + 1) * tokens] = planes[i][...]
        right[i * tokens : (i + 1) * tokens, :] = terms[i][:, :columns]
    side = here[3]
    _, step, _ = kept.shape
    for half in range(2):
        for owner, out_ref in ((1 - side, sent), (side, kept)):
            place = pl.multiple_of(owner * 2 * step + half * step, step)
            out_ref[half] = jnp.dot(
                left[pl.ds(place, step), :], right[...], preferred_element_type=jnp.float32
            ).astype(out_ref.dtype)


def wide_products(here, two_plane, shares, columns):
    rows, tokens = two_plane[0].shape
    outs = [
        jax.ShapeDtypeStruct((2, rows // 4, columns), jnp.bfloat16),
        jax.ShapeDtypeStruct((2, rows // 4, columns), jnp.float32),
    ]
    arrays = [*two_plane, *shares]
    return call_with_here(
        wide_product_kernel,
        here,
        (1,),
        arrays,
        [whole(a) for a in two_plane]
        + [pl.BlockSpec((tokens, columns), lambda i, here: (0, 0))] * 4,
        outs,
        [whole(o) for o in outs],
        [
            pltpu.VMEM((rows, 4 * tokens), jnp.bfloat16),
            pltpu.VMEM((4 * tokens, columns), jnp.bfloat16),
        ],
        micros=3,
    )


def down_product_kernel(here, *refs):
    planes, terms = refs[:4], (refs[4:8], refs[8:12])
    sent, kept, left, right = refs[12:]
    tokens = planes[0].shape[0]
    rows = left.shape[0]
    for i in range(4):
        right[i * tokens : (i + 1) * tokens, :] = planes[i][...]
    for chunk in range(2):
        for i in range(4):
            share = terms[chunk][i]
            at = share.shape[1] // BLK * BLK - (rows + BLK - 1) // BLK * BLK
            left[:, i * tokens : (i + 1) * tokens] = share[:, at : at + rows].T
        for half in range(2):
            product = jnp.dot(
                left[half * rows // 2 : (half + 1) * rows // 2, :],
                right[...],
                preferred_element_type=jnp.float32,
            )

            @pl.when(here[3] == chunk)
            def _(product=product, half=half):
                kept[half] = product

            @pl.when(here[3] != chunk)
            def _(product=product, half=half):
                sent[half] = product.astype(sent.dtype)


def down_products(here, d_plane, first, second, rows):
    tokens, columns = d_plane[0].shape
    outs = [
        jax.ShapeDtypeStruct((2, rows // 2, columns), jnp.bfloat16),
        jax.ShapeDtypeStruct((2, rows // 2, columns), jnp.float32),
    ]
    return call_with_here(
        down_product_kernel,
        here,
        (1,),
        [*d_plane, *first, *second],
        [whole(a) for a in (*d_plane, *first, *second)],
        outs,
        [whole(o) for o in outs],
        [
            pltpu.VMEM((rows, 4 * tokens), jnp.bfloat16),
            pltpu.VMEM((4 * tokens, columns), jnp.bfloat16),
        ],
        micros=3,
    )


GAIN_ROWS = 16


def attention_back_kernel(here, *refs):
    d_ref, q_ref, k_ref, q_scale, k_scale, q_gain, k_gain, cos_ref, sin_ref = refs[:9]
    weight, x_ref, scale_ref, gain_ref, d_h_ref, d_attn_ref = refs[9:15]
    near, far, give, give_far, d_x_ref, gains_ref = refs[15:21]
    turned, natural = refs[21:]
    f32, bf16 = jnp.float32, jnp.bfloat16
    core, y = here[1], here[2]
    cosine, sine = cos_ref[...], sin_ref[...]
    half = HD // 2
    per_group = HEADS // KV_HEADS
    tokens = x_ref.shape[0]

    def back(grad, raw, scale, gain):
        first, second = grad[:half], grad[half:]
        normed = jnp.concatenate(
            [first * cosine + second * sine, second * cosine - first * sine], axis=0
        )
        return norm_back(normed, raw, scale, gain, 0)

    q_term = jnp.zeros((HD, tokens), f32)
    k_term = jnp.zeros((HD, tokens), f32)
    for head in range(HEADS):
        at = slice(head * HD, (head + 1) * HD)
        grad, term = back(
            d_ref[head, :HD, :].astype(f32), q_ref[at, :], q_scale[head : head + 1, :], q_gain[...]
        )
        turned[at, :] = grad.astype(bf16)
        q_term = q_term + term
    for head in range(KV_HEADS):
        at = slice(head * HD, (head + 1) * HD)
        both = d_ref[head * per_group, HD:, :].astype(f32)
        for other in range(1, per_group):
            both = both + d_ref[head * per_group + other, HD:, :].astype(f32)
        grad, term = back(both[:HD], k_ref[at, :], k_scale[head : head + 1, :], k_gain[...])
        place = HEADS * HD + head * HD
        turned[place : place + HD, :] = grad.astype(bf16)
        k_term = k_term + term
        place += KV_HEADS * HD
        turned[place : place + HD, :] = both[HD:].astype(bf16)
    rows = turned.shape[0] // 4
    columns = d_attn_ref.shape[1] // 4
    shares = ((near, core, y), (far, core, 1 - y), (give, 1 - core, y), (give_far, 1 - core, 1 - y))
    for out_ref, to_core, to_y in shares:
        share = to_core * 2 + to_y
        out_ref[:rows, :] = turned[pl.ds(pl.multiple_of(share * rows, rows), rows), :]
        out_ref[rows:, :] = d_attn_ref[:, pl.ds(pl.multiple_of(share * columns, columns), columns)]
    for at in range(0, turned.shape[0], 256):
        natural[:, at : at + 256] = turned[at : at + 256, :].T
    d_normed = contract(natural[...], weight[...], (1, 1))
    x = x_ref[...].astype(f32)
    d_norm, gain_term = norm_back(d_normed, x, scale_ref[...], gain_ref[...])
    d_x_ref[...] = d_h_ref[...] + d_norm
    gains_ref[...] = jnp.zeros_like(gains_ref)
    gains_ref[0:1, :] = jnp.sum(gain_term, axis=0, keepdims=True)
    gains_ref[1:2, 0:HD] = jnp.sum(q_term.T, axis=0, keepdims=True)
    gains_ref[2:3, 0:HD] = jnp.sum(k_term.T, axis=0, keepdims=True)


def attention_back(here, arrays):
    f32, bf16 = jnp.float32, jnp.bfloat16
    shape = jax.ShapeDtypeStruct
    weight, x = arrays[9], arrays[10]
    tokens, width = x.shape
    rows = weight.shape[1] // 4 + tokens
    assert width // 4 == tokens
    outs = [
        *[shape((rows, tokens), bf16)] * 4,
        shape((tokens, width), f32),
        shape((8, width), f32),
    ]
    return call_with_here(
        attention_back_kernel, here, (1,), arrays, [whole(a) for a in arrays], outs,
        [whole(o) for o in outs],
        [pltpu.VMEM((weight.shape[1], tokens), bf16), pltpu.VMEM((tokens, weight.shape[1]), bf16)],
        micros=0,
    )


def attention_product_kernel(here, *refs):
    planes, terms, gains_ref, ffn_gain_ref = refs[:4], refs[4:8], refs[8], refs[9]
    sent, kept, left, right, left_out, right_out = refs[10:]
    tokens = planes[0].shape[2]
    cut = right.shape[1]
    for i in range(4):
        at = slice(i * tokens, (i + 1) * tokens)
        left[:, at] = planes[i][0]
        left_out[:, at] = planes[i][1]
        share = terms[i]
        right[at, :] = share[:cut].T
        right_out[at, :] = share[cut:]
    step = left.shape[0] // 4
    for owner, out_ref in ((1 - here[3], sent), (here[3], kept)):
        for half in range(2):
            at = pl.ds(pl.multiple_of(owner * 2 * step + half * step, step), step)
            out_ref[half, :step, :cut] = jnp.dot(
                left[at, :], right[...], preferred_element_type=jnp.float32
            ).astype(out_ref.dtype)
            out_ref[half, :step, cut:] = jnp.dot(
                left_out[at, :], right_out[...], preferred_element_type=jnp.float32
            ).astype(out_ref.dtype)
        rows = gains_ref.shape[1] // 2
        mine = pl.ds(pl.multiple_of(owner * rows, rows), rows)
        wide = out_ref.shape[2] - rows
        block = jnp.concatenate(
            [
                jnp.concatenate([gains_ref[0:1, mine], gains_ref[1:2, 0:wide]], axis=1),
                jnp.concatenate([ffn_gain_ref[:, mine], gains_ref[2:3, 0:wide]], axis=1),
                jnp.zeros((GAIN_ROWS - 2, out_ref.shape[2]), jnp.float32),
            ],
            axis=0,
        )
        out_ref[0, step:, :] = block.astype(out_ref.dtype)
        out_ref[1, step:, :] = jnp.zeros((GAIN_ROWS, out_ref.shape[2]), out_ref.dtype)


def attention_products(here, pair_plane, shares, gains, ffn_gain):
    _, width, tokens = pair_plane[0].shape
    cut = shares[0].shape[0] - tokens
    shape = (2, width // 4 + GAIN_ROWS, cut + tokens)
    outs = [jax.ShapeDtypeStruct(shape, jnp.bfloat16), jax.ShapeDtypeStruct(shape, jnp.float32)]
    return call_with_here(
        attention_product_kernel,
        here,
        (1,),
        [*pair_plane, *shares, gains, ffn_gain],
        [whole(a) for a in (*pair_plane, *shares, gains, ffn_gain)],
        outs,
        [whole(o) for o in outs],
        [
            pltpu.VMEM((width, 4 * tokens), jnp.bfloat16),
            pltpu.VMEM((4 * tokens, cut), jnp.bfloat16),
            pltpu.VMEM((width, 4 * tokens), jnp.bfloat16),
            pltpu.VMEM((4 * tokens, tokens), jnp.bfloat16),
        ],
        micros=3,
    )


def place_gate_up_kernel(here, *refs):
    mine, across, beside, diagonal, out_ref = *refs[:4], refs[-1]
    pieces = (mine, across, beside, diagonal)
    wide = mine.shape[2]
    for case in range(4):
        core, y = case // 2, case % 2

        @pl.when((here[1] == core) & (here[2] == y))
        def _(core=core, y=y):
            for kind in range(2):
                for column in range(2):
                    value = pieces[(y ^ column) * 2 + (core ^ kind)][0]
                    out_ref[:, kind, column * wide : (column + 1) * wide] = value.astype(
                        jnp.float32
                    )


def place_gate_up(here, chunk, pieces, before):
    _, rows, wide = pieces[0].shape
    step = 64
    blocks = rows // step

    def source(i, here):
        return ((i // blocks) ^ here[0], i % blocks, 0)

    arrays = list(pieces)
    specs = [pl.BlockSpec((1, step, wide), source)] * 4
    aliases = {}
    if before is not None:
        arrays.append(before)
        specs.append(pl.BlockSpec(memory_space=pl.ANY))
        aliases = {5: 0}
    (out,) = call_with_here(
        place_gate_up_kernel,
        here,
        (2 * blocks,),
        arrays,
        specs,
        [jax.ShapeDtypeStruct((2 * rows, 2, 2 * wide * CHUNKS), jnp.float32)],
        [pl.BlockSpec((step, 2, 2 * wide), lambda i, here: (i, 0, chunk))],
        aliases=aliases,
        micros=0,
    )
    return out


def place_down(here, pieces):
    _, rows, columns = pieces[0].shape

    def kernel(here, *refs):
        for s in range(8):

            @pl.when(pl.program_id(0) == s)
            def _(s=s):
                refs[4][...] = refs[s % 4][s // 4].astype(jnp.float32)

    def target(s, here):
        half = (s // 4) ^ here[0]
        y = ((s // 2) % 2) ^ here[2]
        core = (s % 2) ^ here[1]
        return ((core * 2 + y) * 2 + half, 0)

    (out,) = call_with_here(
        kernel,
        here,
        (8,),
        list(pieces),
        [whole(v) for v in pieces],
        [jax.ShapeDtypeStruct((rows * 8, columns), jnp.float32)],
        [pl.BlockSpec((rows, columns), target)],
    )
    return out


def place_attention(here, pieces, cut):
    _, rows, columns = pieces[0].shape
    rows -= GAIN_ROWS

    def kernel(here, *refs):
        qkv_ref, out_ref, gains_ref = refs[4:]
        for s in range(8):

            @pl.when(pl.program_id(0) == s)
            def _(s=s):
                value = refs[s % 4][s // 4]
                qkv_ref[...] = value[:rows, :cut].astype(jnp.float32)
                out_ref[...] = value[:rows, cut:].astype(jnp.float32)
                gains = value[rows:].astype(jnp.float32)
                gains_ref[...] = gains if s == 0 else gains_ref[...] + gains

    def target(s, here):
        half = (s // 4) ^ here[0]
        return (half, ((s % 2) ^ here[1]) * 2 + (((s // 2) % 2) ^ here[2]))

    shape = jax.ShapeDtypeStruct
    f32 = jnp.float32
    gain_shape = (GAIN_ROWS, columns)
    return call_with_here(
        kernel,
        here,
        (8,),
        list(pieces),
        [whole(v) for v in pieces],
        [
            shape((2 * rows, 4 * cut), f32),
            shape((2 * rows, 4 * (columns - cut)), f32),
            shape(gain_shape, f32),
        ],
        [
            pl.BlockSpec((rows, cut), target),
            pl.BlockSpec((rows, columns - cut), target),
            pl.BlockSpec(gain_shape, lambda s, here: (0, 0)),
        ],
    )


def on_block(
    tokens,
    qkv_weight,
    out_weight,
    gate_up_weight,
    down_weight,
    attn_gain,
    ffn_gain,
    query_gain,
    key_gain,
    seq_lengths,
    block_order,
    cotangent,
):
    inputs = tokens[0].astype(jnp.float32)
    rows_here = inputs.shape[0]
    ctx_size = lax.axis_size("ctx")
    ctx_index = lax.axis_index("ctx")
    per_group = HEADS // KV_HEADS
    q_width = HEADS * HD
    kv_width = KV_HEADS * HD
    order_row = block_order[0]
    lengths_row = seq_lengths[0]
    slots = jnp.arange(rows_here, dtype=jnp.int32) // BLK + ctx_index * (rows_here // BLK)
    table = slots[:, None] == jnp.arange(order_row.shape[0], dtype=jnp.int32)[None, :]
    packed = (
        jnp.sum(jnp.where(table, order_row[None, :], 0), axis=1) * BLK
        + jnp.arange(rows_here, dtype=jnp.int32) % BLK
    )
    local = packed - starts_of(packed, lengths_row)
    frequency = ROPE_BASE ** (-2.0 * jnp.arange(HD // 2, dtype=jnp.float32) / HD)
    angle = frequency[:, None] * local.astype(jnp.float32)[None, :]
    cosine = jnp.cos(angle)[None]
    sine = jnp.sin(angle)[None]
    bf16, f32 = jnp.bfloat16, jnp.float32
    parts = ctx_size // HEADS
    part = ctx_index // HEADS
    part_blocks = HEADS * rows_here // BLK
    q_order = lax.dynamic_slice_in_dim(order_row, part * part_blocks, part_blocks)
    q_slot, q_place, q_start = block_tables(q_order, lengths_row)
    q_slot = q_slot + part * part_blocks
    kv_slot, _, _ = block_tables(order_row, lengths_row)
    first = jnp.min(q_start.reshape(-1, TILE), axis=1) // TILE
    last = jnp.max(q_place.reshape(-1, TILE), axis=1) // TILE + 1
    tables = (q_slot, kv_slot, first, last)
    q_rows, kv_rows = part_blocks * BLK, order_row.shape[0] * BLK

    links = Links(ctx_size)
    here = links.here
    width = inputs.shape[1]
    rows = qkv_weight.shape[0]
    part_rows = rows // 4

    def quarter_rows(weight):
        return lax.dynamic_slice_in_dim(weight, links.quarter * part_rows, part_rows)

    qkv_piece = quarter_rows(qkv_weight)
    gains_here = jnp.concatenate([after(attn_gain, qkv_piece), ffn_gain, query_gain, key_gain])
    gains_there = links.over_x(gains_here)

    def gain_of(at, size):
        mine, other = gains_here[at : at + size], gains_there[at : at + size]
        return jnp.where(
            links.side == 0, jnp.concatenate([mine, other]), jnp.concatenate([other, mine])
        ).astype(f32)

    gain_attn = gain_of(0, rows)
    gain_ffn = gain_of(rows, rows)
    gain_query = gain_of(2 * rows, HD // 2)
    gain_key = gain_of(2 * rows + HD // 2, HD // 2)
    ff_chunk = gate_up_weight.shape[2] // CHUNKS

    def gate_up_piece(chunk):
        piece = lax.dynamic_slice(
            gate_up_weight,
            (links.quarter * part_rows, 0, chunk * ff_chunk),
            (part_rows, 2, ff_chunk),
        )
        return [piece[:, 0], piece[:, 1]]

    d_ffn = cotangent[0]
    d_beside = links.over_y(d_ffn)
    qkv_there = after(links.over_x(qkv_piece), d_beside)
    first_piece = jnp.concatenate([*gate_up_piece(0), quarter_rows(out_weight)], axis=1)
    second_piece = jnp.concatenate(gate_up_piece(1), axis=1)
    down_piece = lax.dynamic_slice_in_dim(
        down_weight, links.quarter * (width // 4), width // 4, 1
    )
    d_ffn = cotangent[0]
    tokens_here = tokens[0]
    qkv_there = after(qkv_there, first_piece)
    first_there = links.over_x(after(first_piece, qkv_there))
    gate_up = jnp.transpose(after(gate_up_weight, qkv_there), (1, 0, 2))
    qkv_beside = links.over_y(qkv_there)
    qkv_pieces = (
        qkv_there,
        links.over_core(qkv_there),
        qkv_beside,
        links.over_core(after(qkv_beside, gate_up)),
    )
    sent, w_qkv, q_raw, k_raw, q_scale, k_scale, normed, scale_one = project(
        here, tokens_here, gain_attn[None], qkv_weight, qkv_pieces,
        gain_query[:, None], gain_key[:, None], cosine[0], sine[0],
    )
    got = lax.all_to_all(sent, "ctx", 0, 0, tiled=True)
    first_there = after(first_there, sent)
    down_there = links.over_x(after(down_piece, first_there))
    first_beside = links.over_y(first_there)
    q_place, q_start = q_place[None], q_start[None]
    shape = jax.ShapeDtypeStruct
    attn_sent, *held = kernel_call(
        attend_kernel,
        tables,
        (got, q_place, q_start),
        [
            shape((ctx_size, HD, rows_here), bf16),
            shape((q_rows, HD), bf16),
            shape((HD, q_rows), bf16),
            shape((kv_rows, HD), bf16),
            shape((HD, kv_rows), bf16),
            shape((kv_rows, HD), bf16),
            shape((HD, q_rows), f32),
            shape((1, q_rows), f32),
        ],
        [pltpu.VMEM((HD, kv_rows), bf16)],
        ATTEND,
    )
    attn_in = lax.dynamic_slice_in_dim(
        lax.all_to_all(attn_sent, "ctx", 0, 0, tiled=True), part * HEADS, HEADS
    ).reshape(q_width, rows_here)
    down_there = after(down_there, attn_sent)
    second_there = links.over_x(after(second_piece, down_there))
    down_beside = links.over_y(down_there)

    def spread(there, beside, time):
        there, beside = after(there, time), after(beside, time)
        return (there, links.over_core(there), beside, links.over_core(beside))

    first_pieces = spread(first_there, first_beside, attn_sent)
    down_pieces = spread(down_there, down_beside, attn_in)
    second_beside = links.over_y(second_there)
    w_out, h_one, scale_two, two, two_t = attend_out(
        here, attn_in, tokens_here, gain_ffn[None], out_weight, first_pieces
    )
    two_beside = links.over_y(two_t)
    dealt_here, (out_sum, two_sum) = ffn(
        here, 0, two, d_ffn, gate_up, first_pieces, down_weight, down_pieces, [h_one]
    )
    second_beside = after(second_beside, out_sum)
    second_pieces = (
        second_there, links.over_core(second_there), second_beside, links.over_core(second_beside)
    )
    near, far, give, give_far = dealt_here
    got_far = links.over_core(give_far)
    first_shares = (near, links.over_core(give), links.over_y(far), links.over_y(got_far))
    out_sum = after(out_sum, got_far)
    dealt_here, (output, d_h_one, d_attn, d_heads, ffn_gain_term) = ffn(
        here, 1, two, d_ffn, gate_up, second_pieces, down_weight, down_pieces,
        [out_sum, two_sum, h_one, scale_two, w_out], gain_ffn[None],
    )
    second_shares = links.deal_plane(*dealt_here)

    def plane(value, beside, time):
        value, beside = after(value, time), after(beside, time)
        return (value, links.over_core(value), beside, links.over_core(beside))

    columns = ff_chunk // 2
    d_heads = d_heads.reshape(HEADS, HD, rows_here)
    d_got = lax.all_to_all(d_heads, "ctx", 0, 0, tiled=True)
    pair = jnp.stack([after(normed, d_heads), attn_in])
    two_plane = plane(two_t, two_beside, pair)
    first_products = wide_products(
        here, two_plane, [after(v, d_heads) for v in first_shares], columns
    )
    pair_across = links.over_core(pair)
    d_got = after(d_got, first_products[0], pair_across)
    (d_sent,) = kernel_call(
        attend_back_kernel,
        tables,
        (d_got, q_place, q_start, *held),
        [shape((ctx_size, 3 * HD, rows_here), bf16)],
        [
            pltpu.VMEM((HD, q_rows), bf16),
            pltpu.VMEM((q_rows, HD), bf16),
            pltpu.VMEM((kv_rows, HD), f32),
            pltpu.VMEM((kv_rows, HD), f32),
        ],
        ATTEND_BACK,
    )
    first_got = links.over_x(first_products[0])
    d_sent = after(d_sent, first_got, *second_shares[2:])
    d_back = lax.all_to_all(d_sent, "ctx", 0, 0, tiled=True)
    d_plane = plane(d_ffn, d_beside, d_sent)
    second_products = wide_products(
        here, two_plane, [after(v, d_plane[1]) for v in second_shares], columns
    )
    down_terms = down_products(
        here, d_plane, first_shares, second_shares, columns // 2
    )
    second_got = links.over_x(after(second_products[0], first_got))
    pair_beside = links.over_y(after(pair, d_sent))
    d_back = after(d_back, down_terms[0], pair_beside, second_got)
    *d_shares, d_inputs, gain_sums = attention_back(
        here,
        [
            d_back, q_raw, k_raw, q_scale, k_scale, gain_query[:, None], gain_key[:, None],
            cosine[0], sine[0], w_qkv, tokens_here, scale_one, gain_attn[None], d_h_one, d_attn,
        ],
    )
    down_got = links.over_x(after(down_terms[0], second_got))
    near, far, give, give_far = d_shares
    got, got_far = links.over_core(give), links.over_core(give_far)
    attention_shares = (near, got, links.over_y(far), links.over_y(got_far))
    pair_plane = (pair, pair_across, pair_beside, links.over_core(after(pair_beside, d_sent)))

    kept = [first_products[1], second_products[1], down_terms[1], None]
    got = [first_got, second_got, down_got, None]
    given, part, across, full, back, beside = ([None] * 4 for _ in range(6))

    def give_half(n):
        given[n] = links.over_z(links.half_of(kept[n], got[n], False))

    def sum_part(n, time):
        part[n] = add(links.half_of(kept[n], got[n], True), after(given[n], time))
        across[n] = links.over_two_z(part[n])

    def sum_full(n, time):
        full[n] = add(part[n], after(across[n], time))
        back[n] = links.over_z(full[n])

    def spread_y(n, time):
        full[n] = jnp.stack([full[n], after(back[n], time)])
        beside[n] = links.over_y(full[n])

    def spread_core(n, time):
        beside[n] = after(beside[n], time)
        return (full[n], links.over_core(full[n]), beside[n], links.over_core(beside[n]))

    give_half(0)
    given[0] = after(given[0], down_terms[0])
    sum_part(0, second_got)
    give_half(1)
    sum_part(1, got_far)
    got[2] = after(got[2], part[1], attention_shares[1], pair_plane[3])
    give_half(2)
    sum_full(0, got[2])
    attention_shares = (*attention_shares[:2], *(after(v, full[0]) for v in attention_shares[2:]))
    attention_terms = attention_products(
        here, pair_plane, attention_shares, gain_sums, ffn_gain_term
    )
    kept[3] = attention_terms[1]
    attention_got = links.over_x(attention_terms[0])
    spread_y(0, attention_terms[0])
    sum_part(2, full[0])
    sum_full(1, part[2])
    got[3] = after(attention_got, full[1])
    give_half(3)
    first_pieces = spread_core(0, got[3])
    spread_y(1, beside[0])
    sum_part(3, full[1])
    sum_full(2, part[3])
    first_placed = place_gate_up(here, 0, first_pieces, None)
    second_pieces = spread_core(1, full[2])
    spread_y(2, (first_placed, beside[1]))
    sum_full(3, full[2])
    grad_gate_up = place_gate_up(here, 1, second_pieces, first_placed)
    spread_y(3, full[2])
    grad_down = place_down(here, spread_core(2, grad_gate_up))
    cut = qkv_weight.shape[1] // 4
    grad_qkv, grad_out, gain_sums = place_attention(
        here, spread_core(3, (grad_gate_up, grad_down)), cut
    )
    at = links.side * (HD // 2)
    gain_grads = [
        gain_sums[0, :rows],
        gain_sums[1, :rows],
        lax.dynamic_slice_in_dim(gain_sums[0, rows : rows + HD], at, HD // 2),
        lax.dynamic_slice_in_dim(gain_sums[1, rows : rows + HD], at, HD // 2),
    ]
    return (
        output[None],
        d_inputs[None],
        grad_qkv,
        grad_out,
        grad_gate_up,
        grad_down,
        *gain_grads,
    )


def on_device(
    tokens,
    qkv_weight,
    out_weight,
    gate_up_weight,
    down_weight,
    attn_gain,
    ffn_gain,
    query_gain,
    key_gain,
    seq_lengths,
    block_order,
    cotangent,
):
    inputs = tokens[0].astype(jnp.float32)
    rows_here = inputs.shape[0]
    ctx_size = lax.axis_size("ctx")
    ctx_index = lax.axis_index("ctx")
    per_group = HEADS // KV_HEADS
    q_width = HEADS * HD
    kv_width = KV_HEADS * HD
    order_row = block_order[0]
    lengths_row = seq_lengths[0]
    slots = jnp.arange(rows_here, dtype=jnp.int32) // BLK + ctx_index * (rows_here // BLK)
    table = slots[:, None] == jnp.arange(order_row.shape[0], dtype=jnp.int32)[None, :]
    packed = (
        jnp.sum(jnp.where(table, order_row[None, :], 0), axis=1) * BLK
        + jnp.arange(rows_here, dtype=jnp.int32) % BLK
    )
    local = packed - starts_of(packed, lengths_row)
    frequency = ROPE_BASE ** (-2.0 * jnp.arange(HD // 2, dtype=jnp.float32) / HD)
    angle = frequency[:, None] * local.astype(jnp.float32)[None, :]
    cosine = jnp.cos(angle)[None]
    sine = jnp.sin(angle)[None]
    bf16, f32 = jnp.bfloat16, jnp.float32
    parts = ctx_size // HEADS
    part = ctx_index // HEADS
    part_blocks = HEADS * rows_here // BLK
    q_order = lax.dynamic_slice_in_dim(order_row, part * part_blocks, part_blocks)
    q_slot, q_place, q_start = block_tables(q_order, lengths_row)
    q_slot = q_slot + part * part_blocks
    kv_slot, _, _ = block_tables(order_row, lengths_row)
    first = jnp.min(q_start.reshape(-1, TILE), axis=1) // TILE
    last = jnp.max(q_place.reshape(-1, TILE), axis=1) // TILE + 1
    tables = (q_slot, kv_slot, first, last)
    q_rows, kv_rows = part_blocks * BLK, order_row.shape[0] * BLK

    def fetch_attention():
        return (
            lax.all_gather(qkv_weight, "fsdp", axis=0, tiled=True),
            lax.all_gather(out_weight, "fsdp", axis=0, tiled=True),
            lax.all_gather(attn_gain, "fsdp", axis=0, tiled=True),
            lax.all_gather(ffn_gain, "fsdp", axis=0, tiled=True),
            lax.all_gather(query_gain, "fsdp", axis=0, tiled=True),
            lax.all_gather(key_gain, "fsdp", axis=0, tiled=True),
        )

    w_qkv, w_out, gain_attn, gain_ffn, gain_query, gain_key = fetch_attention()
    gain_attn = gain_attn.astype(jnp.float32)
    gain_ffn = gain_ffn.astype(jnp.float32)
    gain_query = gain_query.astype(jnp.float32)
    gain_key = gain_key.astype(jnp.float32)
    scale_one = rms_scale(inputs)
    normed = (inputs * scale_one * gain_attn).astype(jnp.bfloat16)
    projected = lax.dot_general(
        w_qkv, normed, (((0,), (1,)), ((), ())), preferred_element_type=f32
    )
    q_raw = projected[:q_width].reshape(HEADS, HD, rows_here)
    k_raw = projected[q_width : q_width + kv_width].reshape(KV_HEADS, HD, rows_here)
    values_here = projected[q_width + kv_width :].reshape(KV_HEADS, HD, rows_here).astype(bf16)
    q_scale = rms_scale(q_raw, 1)
    k_scale = rms_scale(k_raw, 1)
    column_query, column_key = gain_query[:, None], gain_key[:, None]
    queries = rope(q_raw * q_scale * column_query, cosine, sine).astype(bf16)
    keys_here = rope(k_raw * k_scale * column_key, cosine, sine).astype(bf16)
    sent = jnp.concatenate(
        [queries, jnp.repeat(keys_here, per_group, 0), jnp.repeat(values_here, per_group, 0)], axis=1
    )
    sent = jnp.concatenate([sent] * parts, axis=0)
    got = lax.all_to_all(sent, "ctx", 0, 0, tiled=True)
    q_place, q_start = q_place[None], q_start[None]
    shape = jax.ShapeDtypeStruct
    attn_sent, *held = kernel_call(
        attend_kernel,
        tables,
        (got, q_place, q_start),
        [
            shape((ctx_size, HD, rows_here), bf16),
            shape((q_rows, HD), bf16),
            shape((HD, q_rows), bf16),
            shape((kv_rows, HD), bf16),
            shape((HD, kv_rows), bf16),
            shape((kv_rows, HD), bf16),
            shape((HD, q_rows), f32),
            shape((1, q_rows), f32),
        ],
        [pltpu.VMEM((HD, kv_rows), bf16)],
        ATTEND,
    )
    attn_in = lax.dynamic_slice_in_dim(
        lax.all_to_all(attn_sent, "ctx", 0, 0, tiled=True), part * HEADS, HEADS
    ).reshape(q_width, rows_here)
    h_one = inputs + lax.dot_general(
        attn_in, w_out, (((0,), (0,)), ((), ())), preferred_element_type=f32
    )
    scale_two = rms_scale(h_one)
    normed_two = (h_one * scale_two * gain_ffn).astype(jnp.bfloat16)
    columns = normed_two
    gate_up = jnp.einsum(
        "tr,rgf->tgf",
        columns,
        lax.all_gather(gate_up_weight, "fsdp", axis=0, tiled=True),
        preferred_element_type=jnp.float32,
    )
    gate = gate_up[:, 0]
    upper = gate_up[:, 1]
    sigma = jax.nn.sigmoid(gate)
    hidden = (gate * sigma * upper).astype(jnp.bfloat16)
    columns = hidden
    ffn_out = jnp.dot(
        columns,
        lax.all_gather(down_weight, "fsdp", axis=0, tiled=True),
        preferred_element_type=jnp.float32,
    )
    output = (h_one + ffn_out).astype(jnp.bfloat16)
    d_out = cotangent[0].astype(jnp.float32)
    d_ffn = d_out.astype(jnp.bfloat16)
    d_hidden = lax.dot_general(
        d_ffn,
        lax.all_gather(down_weight, "fsdp", axis=0, tiled=True),
        (((1,), (1,)), ((), ())),
        preferred_element_type=jnp.float32,
    )
    d_gate = d_hidden * upper * sigma * (1.0 + gate * (1.0 - sigma))
    d_upper = d_hidden * gate * sigma
    d_gate_up = jnp.stack([d_gate, d_upper], axis=1).astype(jnp.bfloat16)
    d_normed_two = jnp.einsum(
        "tgf,rgf->tr",
        d_gate_up,
        lax.all_gather(gate_up_weight, "fsdp", axis=0, tiled=True),
        preferred_element_type=jnp.float32,
    )
    columns = normed_two
    grad_gate_up = lax.psum_scatter(
        jnp.einsum("tr,tgf->rgf", columns, d_gate_up, preferred_element_type=jnp.float32).astype(
            jnp.bfloat16
        ),
        "fsdp",
        scatter_dimension=0,
        tiled=True,
    )
    columns = hidden
    grad_down = lax.psum_scatter(
        lax.dot_general(
            columns, d_ffn, (((0,), (0,)), ((), ())), preferred_element_type=jnp.float32
        ).astype(jnp.bfloat16),
        "fsdp",
        scatter_dimension=0,
        tiled=True,
    )
    d_norm_two, ffn_gain_term = norm_back(d_normed_two, h_one, scale_two, gain_ffn)
    d_h_one = d_out + d_norm_two
    d_attn = d_h_one.astype(jnp.bfloat16)
    grad_out_here = jnp.dot(attn_in, d_attn, preferred_element_type=f32)
    d_heads = lax.dot_general(
        w_out, d_attn, (((1,), (1,)), ((), ())), preferred_element_type=f32
    ).astype(bf16)
    d_heads = jnp.concatenate([d_heads.reshape(HEADS, HD, rows_here)] * parts, axis=0)
    d_got = lax.all_to_all(d_heads, "ctx", 0, 0, tiled=True)
    (d_sent,) = kernel_call(
        attend_back_kernel,
        tables,
        (d_got, q_place, q_start, *held),
        [shape((ctx_size, 3 * HD, rows_here), bf16)],
        [
            pltpu.VMEM((HD, q_rows), bf16),
            pltpu.VMEM((q_rows, HD), bf16),
            pltpu.VMEM((kv_rows, HD), f32),
            pltpu.VMEM((kv_rows, HD), f32),
        ],
        ATTEND_BACK,
    )
    d_back = lax.all_to_all(d_sent, "ctx", 0, 0, tiled=True)
    d_query = lax.dynamic_slice_in_dim(d_back[:, :HD], part * HEADS, HEADS).astype(f32)
    d_key_value = jnp.sum(
        d_back[:, HD:].reshape(parts, KV_HEADS, per_group, 2 * HD, rows_here).astype(f32),
        axis=(0, 2),
    )
    dq_normed = rope_back(d_query, cosine, sine)
    dk_normed = rope_back(d_key_value[:, :HD], cosine, sine)
    dq_raw, query_term = norm_back(dq_normed, q_raw, q_scale, column_query, 1)
    dk_raw, key_term = norm_back(dk_normed, k_raw, k_scale, column_key, 1)
    d_projected = jnp.concatenate(
        [
            dq_raw.reshape(q_width, rows_here).astype(bf16),
            dk_raw.reshape(kv_width, rows_here).astype(bf16),
            d_key_value[:, HD:].reshape(kv_width, rows_here).astype(bf16),
        ],
        axis=0,
    )
    grad_qkv_here = lax.dot_general(
        normed, d_projected, (((0,), (1,)), ((), ())), preferred_element_type=f32
    )
    d_normed = lax.dot_general(
        d_projected, w_qkv, (((0,), (1,)), ((), ())), preferred_element_type=f32
    )
    d_norm_one, attn_gain_term = norm_back(d_normed, inputs, scale_one, gain_attn)
    d_inputs = d_h_one + d_norm_one
    shard_qkv, shard_out, shard_attn_gain, shard_ffn_gain, shard_query_gain, shard_key_gain = (
        lax.psum_scatter(
            grad_qkv_here.astype(jnp.bfloat16), "fsdp", scatter_dimension=0, tiled=True
        ).astype(jnp.float32),
        lax.psum_scatter(
            grad_out_here.astype(jnp.bfloat16), "fsdp", scatter_dimension=0, tiled=True
        ).astype(jnp.float32),
        lax.psum_scatter(
            jnp.sum(attn_gain_term, axis=0).astype(jnp.bfloat16),
            "fsdp",
            scatter_dimension=0,
            tiled=True,
        ).astype(jnp.float32),
        lax.psum_scatter(
            jnp.sum(ffn_gain_term, axis=0).astype(jnp.bfloat16),
            "fsdp",
            scatter_dimension=0,
            tiled=True,
        ).astype(jnp.float32),
        lax.psum_scatter(
            jnp.sum(query_term, axis=(0, 2)).astype(jnp.bfloat16),
            "fsdp",
            scatter_dimension=0,
            tiled=True,
        ).astype(jnp.float32),
        lax.psum_scatter(
            jnp.sum(key_term, axis=(0, 2)).astype(jnp.bfloat16),
            "fsdp",
            scatter_dimension=0,
            tiled=True,
        ).astype(jnp.float32),
    )
    summed_grads = (
        lax.psum(shard_qkv.astype(jnp.bfloat16), "ctx").astype(jnp.float32),
        lax.psum(shard_out.astype(jnp.bfloat16), "ctx").astype(jnp.float32),
        lax.psum(grad_gate_up, "ctx").astype(jnp.float32),
        lax.psum(grad_down, "ctx").astype(jnp.float32),
        lax.psum(shard_attn_gain.astype(jnp.bfloat16), "ctx").astype(jnp.float32),
        lax.psum(shard_ffn_gain.astype(jnp.bfloat16), "ctx").astype(jnp.float32),
        lax.psum(shard_query_gain.astype(jnp.bfloat16), "ctx").astype(jnp.float32),
        lax.psum(shard_key_gain.astype(jnp.bfloat16), "ctx").astype(jnp.float32),
    )
    return (
        output[None],
        d_inputs[None],
        summed_grads[0],
        summed_grads[1],
        summed_grads[2],
        summed_grads[3],
        summed_grads[4],
        summed_grads[5],
        summed_grads[6],
        summed_grads[7],
    )


def solution(mesh):
    block = mesh.shape["fsdp"] == 2 and mesh.shape["ctx"] == 16
    return jax.shard_map(
        on_block if block else on_device,
        mesh=mesh,
        in_specs=(
            P("fsdp", "ctx", None),
            P("fsdp", None),
            P("fsdp", None),
            P("fsdp", None, None),
            P("fsdp", None),
            P("fsdp"),
            P("fsdp"),
            P("fsdp"),
            P("fsdp"),
            P("fsdp", None),
            P("fsdp", None),
            P("fsdp", "ctx", None),
        ),
        out_specs=(
            P("fsdp", "ctx", None),
            P("fsdp", "ctx", None),
            P("fsdp", None),
            P("fsdp", None),
            P("fsdp", None, None),
            P("fsdp", None),
            P("fsdp"),
            P("fsdp"),
            P("fsdp"),
            P("fsdp"),
        ),
        check_vma=False,
    )
```

```python
import functools

import jax
import jax.numpy as jnp
from jax import lax
from jax.experimental import pallas as pl
from jax.experimental.pallas import tpu as pltpu
from jax.sharding import PartitionSpec as P

HEADS = 16
KV_HEADS = 8
HD = 64
BLK = 128
TILE = 512
CHUNKS = 2
PROJECT = 0
ATTEND = 0
OUT = 0
FFN = (0, 0)
ATTEND_BACK = 25


EPSILON = 1e-05
ROPE_BASE = 1000000.0
LOG2E = 1.4426950408889634
SCORE_SCALE = LOG2E * HD ** (-0.5)


def rms_scale(values, axis=-1):
    return lax.rsqrt(jnp.mean(values * values, axis=axis, keepdims=True) + EPSILON)


def norm_back(grad_normed, inputs, scale, gain, axis=-1):
    scaled = grad_normed * gain
    grad_in = scale * scaled - inputs * scale * scale * scale * jnp.mean(
        scaled * inputs, axis=axis, keepdims=True
    )
    return (grad_in, grad_normed * inputs * scale)


def rope(values, cosine, sine):
    half = HD // 2
    first, second = values[:, :half], values[:, half:]
    return jnp.concatenate([first * cosine - second * sine, second * cosine + first * sine], axis=1)


def rope_back(values, cosine, sine):
    half = HD // 2
    first, second = values[:, :half], values[:, half:]
    return jnp.concatenate([first * cosine + second * sine, second * cosine - first * sine], axis=1)


def starts_of(packed, lengths_row):
    ends = jnp.cumsum(lengths_row)
    past = packed[:, None] >= ends[None, :]
    return jnp.sum(jnp.where(past, lengths_row[None, :], 0), axis=1)


def block_tables(order, lengths_row):
    count = order.shape[0]
    rank = jnp.sum((order[None, :] < order[:, None]).astype(jnp.int32), axis=1)
    hit = rank[None, :] == jnp.arange(count, dtype=jnp.int32)[:, None]
    slot = jnp.sum(jnp.where(hit, jnp.arange(count, dtype=jnp.int32)[None, :], 0), axis=1)
    block = jnp.sum(jnp.where(hit, order[None, :], 0), axis=1)
    place = (block[:, None] * BLK + jnp.arange(BLK, dtype=jnp.int32)[None, :]).reshape(-1)
    return (slot, place, starts_of(place, lengths_row))


def attend_kernel(
    q_slot, kv_slot, first, last, qkv_ref, place_ref, start_ref,
    out_ref, q_ref, qt_ref, k_ref, kt_ref, v_ref, ot_ref, total_ref, vt_ref
):
    per_device = qkv_ref.shape[2] // BLK
    kv_blocks = k_ref.shape[0] // BLK
    q_blocks = q_ref.shape[0] // BLK

    def piece(slot, lower):
        return qkv_ref[
            slot // per_device,
            lower : lower + HD,
            pl.ds(pl.multiple_of((slot % per_device) * BLK, BLK), BLK),
        ]

    for i in range(kv_blocks):
        here = slice(i * BLK, (i + 1) * BLK)
        keys = piece(kv_slot[i], HD)
        kt_ref[:, here] = keys
        k_ref[here, :] = keys.T
        values = piece(kv_slot[i], 2 * HD)
        vt_ref[:, here] = values
        v_ref[here, :] = values.T
    for i in range(q_blocks):
        here = slice(i * BLK, (i + 1) * BLK)
        queries = piece(q_slot[i], 0)
        qt_ref[:, here] = queries
        q_ref[here, :] = queries.T
    if q_blocks < kv_blocks:
        out_ref[...] = jnp.zeros_like(out_ref)

    def tile(i, carry):
        rows = pl.ds(pl.multiple_of(i * TILE, TILE), TILE)
        queries = qt_ref[:, rows]
        place = place_ref[:, rows]
        start = start_ref[:, rows]

        def step(j, state):
            total, summed = state
            at = pl.multiple_of(j * TILE, TILE)
            scores = jnp.dot(
                k_ref[pl.ds(at, TILE), :], queries, preferred_element_type=jnp.float32
            )
            key_place = lax.broadcasted_iota(jnp.int32, (TILE, TILE), 0) + at
            allowed = (key_place <= place) & (key_place >= start)
            lifted = jnp.where(allowed, jnp.exp2(scores * SCORE_SCALE), 0.0)
            total = total + jnp.sum(lifted, axis=0, keepdims=True)
            summed = summed + jnp.dot(
                vt_ref[:, pl.ds(at, TILE)],
                lifted.astype(jnp.bfloat16),
                preferred_element_type=jnp.float32,
            )
            return (total, summed)

        total, summed = lax.fori_loop(
            first[i],
            last[i],
            step,
            (jnp.zeros((1, TILE), jnp.float32), jnp.zeros((HD, TILE), jnp.float32)),
        )
        attn = summed / total
        ot_ref[:, rows] = attn
        total_ref[:, rows] = jnp.log(total) * LOG2E
        rounded = attn.astype(jnp.bfloat16)
        for part in range(TILE // BLK):
            slot = q_slot[i * (TILE // BLK) + part]
            out_ref[
                slot // per_device,
                :,
                pl.ds(pl.multiple_of((slot % per_device) * BLK, BLK), BLK),
            ] = rounded[:, part * BLK : (part + 1) * BLK]
        return carry

    lax.fori_loop(0, q_blocks * BLK // TILE, tile, 0)


def attend_back_kernel(
    q_slot, kv_slot, first, last, d_ref, place_ref, start_ref,
    q_ref, qt_ref, k_ref, kt_ref, v_ref, ot_ref, total_ref,
    out_ref, dt_ref, do_ref, dk_ref, dv_ref
):
    per_device = d_ref.shape[2] // BLK
    kv_blocks = k_ref.shape[0] // BLK
    q_blocks = q_ref.shape[0] // BLK

    def lanes(slot):
        return pl.ds(pl.multiple_of((slot % per_device) * BLK, BLK), BLK)

    for i in range(q_blocks):
        here = slice(i * BLK, (i + 1) * BLK)
        slot = q_slot[i]
        grads = d_ref[slot // per_device, :, lanes(slot)]
        dt_ref[:, here] = grads
        do_ref[here, :] = grads.T
    dk_ref[...] = jnp.zeros_like(dk_ref)
    dv_ref[...] = jnp.zeros_like(dv_ref)
    if q_blocks < kv_blocks:
        out_ref[...] = jnp.zeros_like(out_ref)

    def tile(i, carry):
        rows = pl.ds(pl.multiple_of(i * TILE, TILE), TILE)
        queries = qt_ref[:, rows]
        grads = dt_ref[:, rows]
        place = place_ref[:, rows]
        start = start_ref[:, rows]
        delta = jnp.sum(grads.astype(jnp.float32) * ot_ref[:, rows], axis=0, keepdims=True)
        total = total_ref[:, rows]

        def step(j, d_query):
            at = pl.multiple_of(j * TILE, TILE)
            here = pl.ds(at, TILE)
            scores = jnp.dot(k_ref[here, :], queries, preferred_element_type=jnp.float32)
            key_place = lax.broadcasted_iota(jnp.int32, (TILE, TILE), 0) + at
            allowed = (key_place <= place) & (key_place >= start)
            shares = jnp.where(allowed, jnp.exp2(scores * SCORE_SCALE - total), 0.0)
            d_shares = jnp.dot(v_ref[here, :], grads, preferred_element_type=jnp.float32)
            d_scores = (shares * (d_shares - delta)).astype(jnp.bfloat16)
            dv_ref[here, :] += jnp.dot(
                shares.astype(jnp.bfloat16), do_ref[rows, :], preferred_element_type=jnp.float32
            )
            dk_ref[here, :] += jnp.dot(
                d_scores, q_ref[rows, :], preferred_element_type=jnp.float32
            )
            return d_query + jnp.dot(
                kt_ref[:, here], d_scores, preferred_element_type=jnp.float32
            )

        d_query = lax.fori_loop(first[i], last[i], step, jnp.zeros((HD, TILE), jnp.float32))
        rounded = (d_query * HD ** (-0.5)).astype(jnp.bfloat16)
        for part in range(TILE // BLK):
            slot = q_slot[i * (TILE // BLK) + part]
            out_ref[slot // per_device, 0:HD, lanes(slot)] = rounded[
                :, part * BLK : (part + 1) * BLK
            ]
        return carry

    lax.fori_loop(0, q_blocks * BLK // TILE, tile, 0)
    for i in range(kv_blocks):
        here = slice(i * BLK, (i + 1) * BLK)
        slot = kv_slot[i]
        out_ref[slot // per_device, HD : 2 * HD, lanes(slot)] = (
            (dk_ref[here, :] * HD ** (-0.5)).T.astype(jnp.bfloat16)
        )
        out_ref[slot // per_device, 2 * HD : 3 * HD, lanes(slot)] = (
            dv_ref[here, :].T.astype(jnp.bfloat16)
        )


def cost(micros):
    return pl.CostEstimate(
        flops=1 + micros * 1_000_000_000, bytes_accessed=1, transcendentals=0
    )


def kernel_call(kernel, tables, arrays, outs, scratch, micros):
    smem = pl.BlockSpec(memory_space=pltpu.SMEM)
    vmem = pl.BlockSpec(memory_space=pltpu.VMEM)
    return pl.pallas_call(
        kernel,
        out_shape=outs,
        in_specs=[smem] * len(tables) + [vmem] * len(arrays),
        out_specs=[vmem] * len(outs),
        scratch_shapes=scratch,
        compiler_params=pltpu.CompilerParams(vmem_limit_bytes=48 * 1024 * 1024),
        cost_estimate=cost(micros),
    )(*tables, *arrays)


class Links:
    def __init__(self, ctx_size):
        self.depth = ctx_size // 4
        index = lax.axis_index("ctx")
        self.core = index % 2
        self.y = (index // 2) % 2
        self.side = lax.axis_index("fsdp")
        self.half = index // 4 % 2
        self.quarter = index % 2 * 2 + self.y
        self.here = jnp.stack([self.half, self.core, self.y, self.side]).astype(jnp.int32)

    def route(self, place):
        pairs = []
        for z in range(self.depth):
            for y in range(2):
                for core in range(2):
                    to_z, to_y, to_core = place(z, y, core)
                    pairs.append(((z * 2 + y) * 2 + core, (to_z * 2 + to_y) * 2 + to_core))
        return pairs

    def over_core(self, value):
        return lax.ppermute(value, "ctx", self.route(lambda z, y, c: (z, y, 1 - c)))

    def over_y(self, value):
        return lax.ppermute(value, "ctx", self.route(lambda z, y, c: (z, 1 - y, c)))

    def over_z(self, value):
        return lax.ppermute(value, "ctx", self.route(lambda z, y, c: (z ^ 1, y, c)))

    def over_two_z(self, value):
        return lax.ppermute(value, "ctx", self.route(lambda z, y, c: (z ^ 2, y, c)))

    def over_x(self, value):
        return lax.ppermute(value, "fsdp", [(0, 1), (1, 0)])

    def spread_plane(self, value):
        across = self.over_core(value)
        beside = self.over_y(value)
        return (value, across, beside, self.over_core(beside))

    def deal_plane(self, near, far, give, give_far):
        got, got_far = self.over_core(give), self.over_core(give_far)
        return (near, got, self.over_y(far), self.over_y(got_far))

    def half_of(self, kept, got, own):
        index = self.half if own else 1 - self.half
        return add(pick(kept, index, 0), pick(got, index, 0))


def pick(value, index, axis):
    return lax.dynamic_index_in_dim(value, index, axis, keepdims=False)


def add(left, right):
    return (left.astype(jnp.float32) + right.astype(jnp.float32)).astype(jnp.bfloat16)


def after(value, *others):
    return lax.optimization_barrier((value, *jax.tree.leaves(others)))[0]


def contract(left, right, axes):
    return lax.dot_general(
        left, right, ((axes[:1], axes[1:]), ((), ())), preferred_element_type=jnp.float32
    )


PARAMS = pltpu.CompilerParams(vmem_limit_bytes=56 * 1024 * 1024)


def call_with_here(
    kernel, here, grid, arrays, specs, outs, out_specs, scratch=(), aliases=None, micros=0
):
    return pl.pallas_call(
        kernel,
        grid_spec=pltpu.PrefetchScalarGridSpec(
            num_scalar_prefetch=1,
            grid=grid,
            in_specs=specs,
            out_specs=out_specs,
            scratch_shapes=list(scratch),
        ),
        out_shape=outs,
        input_output_aliases=aliases or {},
        compiler_params=PARAMS,
        cost_estimate=cost(micros),
    )(here, *arrays)


def whole(array):
    rank = len(array.shape)
    return pl.BlockSpec(array.shape, lambda i, here: (0,) * rank)


def project_kernel(here, *refs):
    x_ref, gain_ref, own_ref = refs[:3]
    pieces, q_gain, k_gain, cos_ref, sin_ref = refs[3:7], refs[7], refs[8], refs[9], refs[10]
    sent, weight, q_ref, k_ref, q_scale, k_scale, normed_ref, scale_ref = refs[11:]
    core, y, side = here[1], here[2], here[3]
    rows = own_ref.shape[0]
    part = rows // 4
    f32, bf16 = jnp.float32, jnp.bfloat16
    weight[pl.ds(pl.multiple_of(side * rows, rows), rows), :] = own_ref[...]
    for p in range(4):
        at = (1 - side) * rows + (((p % 2) ^ core) * 2 + ((p // 2) ^ y)) * part
        weight[pl.ds(pl.multiple_of(at, part), part), :] = pieces[p][...]
    x = x_ref[...].astype(f32)
    scale = rms_scale(x)
    scale_ref[...] = scale
    normed = (x * scale * gain_ref[...]).astype(bf16)
    normed_ref[...] = normed.T
    cosine, sine = cos_ref[...], sin_ref[...]
    half = HD // 2

    def turned(raw, gain, raw_ref, kept_scale, head):
        raw_ref[head * HD : (head + 1) * HD, :] = raw
        scale = rms_scale(raw, 0)
        kept_scale[head : head + 1, :] = scale
        value = raw * scale * gain
        first, second = value[:half], value[half:]
        return jnp.concatenate(
            [first * cosine - second * sine, second * cosine + first * sine], axis=0
        ).astype(bf16)

    per_group = HEADS // KV_HEADS
    for at in range(0, weight.shape[1], 2 * BLK):
        block = jnp.dot(normed, weight[:, at : at + 2 * BLK], preferred_element_type=f32)
        turned_block = block.T
        for n in range(2 * BLK // HD):
            head = at // HD + n
            raw = turned_block[n * HD : (n + 1) * HD, :]
            if head < HEADS:
                sent[head, 0:HD, :] = turned(raw, q_gain[...], q_ref, q_scale, head)
                continue
            head -= HEADS
            if head < KV_HEADS:
                value, row = turned(raw, k_gain[...], k_ref, k_scale, head), HD
            else:
                value, row, head = raw.astype(bf16), 2 * HD, head - KV_HEADS
            for copy in range(per_group):
                sent[head * per_group + copy, row : row + HD, :] = value


def project(here, x, gain, own, pieces, q_gain, k_gain, cosine, sine):
    tokens, width = x.shape
    f32, bf16 = jnp.float32, jnp.bfloat16
    shape = jax.ShapeDtypeStruct
    arrays = [x, gain, own, *pieces, q_gain, k_gain, cosine, sine]
    outs = [
        shape((HEADS, 3 * HD, tokens), bf16),
        shape((width, own.shape[1]), bf16),
        shape((HEADS * HD, tokens), f32),
        shape((KV_HEADS * HD, tokens), f32),
        shape((HEADS, tokens), f32),
        shape((KV_HEADS, tokens), f32),
        shape((width, tokens), bf16),
        shape((tokens, 1), f32),
    ]
    return call_with_here(
        project_kernel, here, (1,), arrays, [whole(a) for a in arrays], outs,
        [whole(o) for o in outs], micros=PROJECT,
    )


def layer(array, index):
    return pl.BlockSpec((1, *array.shape[1:]), lambda i, here: (index, 0, 0))


def attend_out_kernel(here, *refs):
    attn_ref, x_ref, gain_ref, own_ref = refs[:4]
    pieces = refs[4:20]
    weight, h_ref, scale_ref, two_ref, two_t_ref = refs[20:]
    core, y, side = here[1], here[2], here[3]
    rows = own_ref.shape[0]
    part = rows // 4
    weight[pl.ds(pl.multiple_of(side * rows, rows), rows), :] = own_ref[...]
    for p in range(4):
        at = (1 - side) * rows + (((p % 2) ^ core) * 2 + ((p // 2) ^ y)) * part
        for n in range(4):
            piece = pieces[4 * p + n]
            wide = piece.shape[1]
            weight[pl.ds(pl.multiple_of(at, part), part), n * wide : (n + 1) * wide] = piece[...]
    attn = attn_ref[...].T
    h_one = x_ref[...].astype(jnp.float32) + jnp.dot(
        attn, weight[...], preferred_element_type=jnp.float32
    )
    scale = rms_scale(h_one)
    h_ref[...] = h_one
    scale_ref[...] = scale
    two = (h_one * scale * gain_ref[...]).astype(jnp.bfloat16)
    two_ref[...] = two
    two_t_ref[...] = two.T


def attend_out(here, attn, x, gain, own, pieces):
    tokens, width = x.shape
    f32, bf16 = jnp.float32, jnp.bfloat16
    shape = jax.ShapeDtypeStruct
    part = own.shape[0] // 4
    cuts = 4
    part_width = width // cuts
    first = pieces[0].shape[1] // part_width - cuts
    arrays = [attn, x, gain, own]
    specs = [whole(a) for a in arrays]
    for piece in pieces:
        for n in range(cuts):
            arrays.append(piece)
            specs.append(pl.BlockSpec((part, part_width), lambda i, here, n=n: (0, first + n)))
    outs = [
        shape((width, width), bf16),
        shape((tokens, width), f32),
        shape((tokens, 1), f32),
        shape((tokens, width), bf16),
        shape((width, tokens), bf16),
    ]
    return call_with_here(
        attend_out_kernel, here, (1,), arrays, specs, outs, [whole(o) for o in outs], micros=OUT
    )


def ffn_kernel(chunk, here, *refs):
    two_ref, d_ref, own_ref = refs[:3]
    pieces, down_ref, down_pieces = (refs[3:7], refs[7:11]), refs[11], refs[12:16]
    refs = refs[4:]
    if chunk == 0:
        before_refs, refs = refs[12:13], refs[13:]
        near, far, give, give_far, out_ref, d_two_ref = refs[:6]
        refs = refs[6:]
    else:
        before_refs, gain_ref, refs = refs[12:17], refs[17], refs[18:]
        near, far, give, give_far = refs[:4]
        out_ref, d_h_ref, d_attn_ref, heads_ref, gain_term_ref = refs[4:9]
        refs = refs[9:]
    weight, down, hidden_rows, out_sum, two_sum = refs[:5]
    held, weight_sem, down_sem, before_sem = refs[5:-3], refs[-3], refs[-2], refs[-1]
    core, y, side = here[1], here[2], here[3]
    f32, bf16 = jnp.float32, jnp.bfloat16
    own_rows, columns = own_ref.shape[1], own_ref.shape[2] // CHUNKS
    part = own_rows // 4
    tile = columns // FFN_TILES
    half = columns // 2

    def quarter(p):
        return ((p % 2) ^ core) * 2 + ((p // 2) ^ y)

    def copies(n):
        at = slice(n * tile, (n + 1) * tile)
        mine = pl.ds(pl.multiple_of(side * own_rows, own_rows), own_rows)
        found = [
            pltpu.make_async_copy(
                own_ref.at[:, :, chunk * columns + n * tile : chunk * columns + (n + 1) * tile],
                weight.at[:, mine, at],
                weight_sem.at[n, 0],
            )
        ]
        for p in range(4):
            rows = pl.ds(pl.multiple_of((1 - side) * own_rows + quarter(p) * part, part), part)
            for kind in range(2):
                begin = n * tile + (columns if kind == 1 and chunk == 1 else 0)
                found.append(
                    pltpu.make_async_copy(
                        pieces[kind][p].at[:, begin : begin + tile],
                        weight.at[kind, rows, at],
                        weight_sem.at[n, 1 + 2 * p + kind],
                    )
                )
        return found

    def own_down(n):
        at = slice(n * tile, (n + 1) * tile)
        return [pltpu.make_async_copy(down_ref.at[at, :], down.at[at, :], down_sem.at[n, 0])]

    def other_down(n):
        at = slice(n * tile, (n + 1) * tile)
        found = []
        for p in range(4):
            wide = down_pieces[p].shape[1]
            lanes = pl.ds(pl.multiple_of(quarter(p) * wide, wide), wide)
            found.append(
                pltpu.make_async_copy(
                    down_pieces[p].at[at, :], down.at[at, lanes], down_sem.at[n, p]
                )
            )
        return found

    def each(action, n):
        for copy in copies(n):
            action(copy)

        @pl.when(side == chunk)
        def _():
            for copy in own_down(n):
                action(copy)

        @pl.when(side != chunk)
        def _():
            for copy in other_down(n):
                action(copy)

    before = [
        pltpu.make_async_copy(ref, held[n], before_sem.at[n]) for n, ref in enumerate(before_refs)
    ]
    for n in range(FFN_TILES):
        each(lambda copy: copy.start(), n)
    for copy in before:
        copy.start()
    two = two_ref[...]
    d_ffn = d_ref[...]
    for n in range(FFN_TILES):
        each(lambda copy: copy.wait(), n)
        at = slice(n * tile, (n + 1) * tile)
        gate = jnp.dot(two, weight[0, :, at], preferred_element_type=f32)
        upper = jnp.dot(two, weight[1, :, at], preferred_element_type=f32)
        d_hidden = contract(d_ffn, down[at, :], (1, 1))
        sigma = jax.nn.sigmoid(gate)
        silu = gate * sigma
        hidden = (silu * upper).astype(bf16)
        d_gate = (d_hidden * upper * sigma * (1.0 + gate * (1.0 - sigma))).astype(bf16)
        d_upper = (d_hidden * silu).astype(bf16)
        out_term = jnp.dot(hidden, down[at, :], preferred_element_type=f32)
        two_term = contract(d_gate, weight[0, :, at], (1, 1)) + contract(
            d_upper, weight[1, :, at], (1, 1)
        )
        out_sum[...] = out_term if n == 0 else out_sum[...] + out_term
        two_sum[...] = two_term if n == 0 else two_sum[...] + two_term
        hidden_rows[:, at] = hidden
        mine = jnp.where(core == 0, d_gate, d_upper)
        other = jnp.where(core == 0, d_upper, d_gate)
        for column in range(2):
            begin, end = max(n * tile, column * half), min((n + 1) * tile, (column + 1) * half)
            if begin >= end:
                continue
            source = slice(begin - n * tile, end - n * tile)
            target = slice(begin - column * half, end - column * half)
            first, second = mine[:, source], other[:, source]

            @pl.when(y == column)
            def _(first=first, second=second, target=target):
                near[:, target] = first
                give[:, target] = second

            @pl.when(y != column)
            def _(first=first, second=second, target=target):
                far[:, target] = first
                give_far[:, target] = second

    share = half // 2
    target = slice(half, half + share)
    for owner in range(2):
        lower = hidden_rows[:, owner * half : owner * half + share]
        upper = hidden_rows[:, owner * half + share : (owner + 1) * half]
        close = jnp.where(y == 0, lower, upper)
        distant = jnp.where(y == 0, upper, lower)

        @pl.when(core == owner)
        def _(close=close, distant=distant):
            near[:, target] = close
            far[:, target] = distant

        @pl.when(core != owner)
        def _(close=close, distant=distant):
            give[:, target] = close
            give_far[:, target] = distant

    for copy in before:
        copy.wait()
    if chunk == 0:
        out_ref[...] = held[0][...] + out_sum[...]
        d_two_ref[...] = two_sum[...]
    else:
        out_before, two_before, h_one, scale, w_out = held
        out_ref[...] = (out_before[...] + out_sum[...]).astype(bf16)
        d_norm, gain_term = norm_back(
            two_before[...] + two_sum[...], h_one[...], scale[...], gain_ref[...]
        )
        gain_term_ref[...] = jnp.sum(gain_term, axis=0, keepdims=True)
        d_h_one = d_ffn.astype(f32) + d_norm
        d_h_ref[...] = d_h_one
        d_attn = d_h_one.astype(bf16)
        d_attn_ref[...] = d_attn
        heads_ref[...] = contract(w_out[...], d_attn, (1, 1)).astype(bf16)


FFN_TILES = 3


def ffn(here, chunk, two, d_ffn, own, pieces, down, down_pieces, before, gain=None):
    tokens, width = two.shape
    columns = own.shape[2] // CHUNKS
    padded = (columns // 2 + columns // 4 + BLK - 1) // BLK * BLK
    shape = jax.ShapeDtypeStruct
    f32, bf16 = jnp.float32, jnp.bfloat16
    outs = [shape((tokens, padded), bf16)] * 4
    if chunk == 0:
        outs += [shape((tokens, width), f32)] * 2
    else:
        outs += [
            shape((tokens, width), bf16),
            shape((tokens, width), f32),
            shape((tokens, width), bf16),
            shape((width, tokens), bf16),
            shape((1, width), f32),
        ]
    far_away = pl.BlockSpec(memory_space=pl.ANY)
    arrays = [two, d_ffn, own, *pieces[0], *pieces[1], down, *down_pieces, *before]
    specs = [whole(two), whole(d_ffn)] + [far_away] * (len(arrays) - 2)
    if gain is not None:
        arrays.append(gain)
        specs.append(whole(gain))
    got = call_with_here(
        functools.partial(ffn_kernel, chunk),
        here,
        (1,),
        arrays,
        specs,
        outs,
        [whole(o) for o in outs],
        [
            pltpu.VMEM((2, width, columns), bf16),
            pltpu.VMEM((columns, width), bf16),
            pltpu.VMEM((tokens, columns), bf16),
            pltpu.VMEM((tokens, width), f32),
            pltpu.VMEM((tokens, width), f32),
        ]
        + [pltpu.VMEM(v.shape, v.dtype) for v in before]
        + [
            pltpu.SemaphoreType.DMA((FFN_TILES, 9)),
            pltpu.SemaphoreType.DMA((FFN_TILES, 4)),
            pltpu.SemaphoreType.DMA((len(before),)),
        ],
        micros=FFN[chunk],
    )
    return got[:4], got[4:]


def wide_product_kernel(here, *refs):
    planes, terms = refs[:4], refs[4:8]
    sent, kept, left, right = refs[8:]
    tokens = planes[0].shape[1]
    columns = right.shape[1]
    for i in range(4):
        left[:, i * tokens : (i + 1) * tokens] = planes[i][...]
        right[i * tokens : (i + 1) * tokens, :] = terms[i][:, :columns]
    side = here[3]
    _, step, _ = kept.shape
    for half in range(2):
        for owner, out_ref in ((1 - side, sent), (side, kept)):
            place = pl.multiple_of(owner * 2 * step + half * step, step)
            out_ref[half] = jnp.dot(
                left[pl.ds(place, step), :], right[...], preferred_element_type=jnp.float32
            ).astype(out_ref.dtype)


def wide_products(here, two_plane, shares, columns):
    rows, tokens = two_plane[0].shape
    outs = [
        jax.ShapeDtypeStruct((2, rows // 4, columns), jnp.bfloat16),
        jax.ShapeDtypeStruct((2, rows // 4, columns), jnp.float32),
    ]
    arrays = [*two_plane, *shares]
    return call_with_here(
        wide_product_kernel,
        here,
        (1,),
        arrays,
        [whole(a) for a in two_plane]
        + [pl.BlockSpec((tokens, columns), lambda i, here: (0, 0))] * 4,
        outs,
        [whole(o) for o in outs],
        [
            pltpu.VMEM((rows, 4 * tokens), jnp.bfloat16),
            pltpu.VMEM((4 * tokens, columns), jnp.bfloat16),
        ],
        micros=3,
    )


def down_product_kernel(here, *refs):
    planes, terms = refs[:4], (refs[4:8], refs[8:12])
    sent, kept, left, right = refs[12:]
    tokens = planes[0].shape[0]
    rows = left.shape[0]
    for i in range(4):
        right[i * tokens : (i + 1) * tokens, :] = planes[i][...]
    for chunk in range(2):
        for i in range(4):
            share = terms[chunk][i]
            at = share.shape[1] // BLK * BLK - (rows + BLK - 1) // BLK * BLK
            left[:, i * tokens : (i + 1) * tokens] = share[:, at : at + rows].T
        for half in range(2):
            product = jnp.dot(
                left[half * rows // 2 : (half + 1) * rows // 2, :],
                right[...],
                preferred_element_type=jnp.float32,
            )

            @pl.when(here[3] == chunk)
            def _(product=product, half=half):
                kept[half] = product

            @pl.when(here[3] != chunk)
            def _(product=product, half=half):
                sent[half] = product.astype(sent.dtype)


def down_products(here, d_plane, first, second, rows):
    tokens, columns = d_plane[0].shape
    outs = [
        jax.ShapeDtypeStruct((2, rows // 2, columns), jnp.bfloat16),
        jax.ShapeDtypeStruct((2, rows // 2, columns), jnp.float32),
    ]
    return call_with_here(
        down_product_kernel,
        here,
        (1,),
        [*d_plane, *first, *second],
        [whole(a) for a in (*d_plane, *first, *second)],
        outs,
        [whole(o) for o in outs],
        [
            pltpu.VMEM((rows, 4 * tokens), jnp.bfloat16),
            pltpu.VMEM((4 * tokens, columns), jnp.bfloat16),
        ],
        micros=3,
    )


GAIN_ROWS = 16


def attention_back_kernel(here, *refs):
    d_ref, q_ref, k_ref, q_scale, k_scale, q_gain, k_gain, cos_ref, sin_ref = refs[:9]
    weight, x_ref, scale_ref, gain_ref, d_h_ref, d_attn_ref = refs[9:15]
    near, far, give, give_far, d_x_ref, gains_ref = refs[15:21]
    turned, natural = refs[21:]
    f32, bf16 = jnp.float32, jnp.bfloat16
    core, y = here[1], here[2]
    cosine, sine = cos_ref[...], sin_ref[...]
    half = HD // 2
    per_group = HEADS // KV_HEADS
    tokens = x_ref.shape[0]

    def back(grad, raw, scale, gain):
        first, second = grad[:half], grad[half:]
        normed = jnp.concatenate(
            [first * cosine + second * sine, second * cosine - first * sine], axis=0
        )
        return norm_back(normed, raw, scale, gain, 0)

    q_term = jnp.zeros((HD, tokens), f32)
    k_term = jnp.zeros((HD, tokens), f32)
    for head in range(HEADS):
        at = slice(head * HD, (head + 1) * HD)
        grad, term = back(
            d_ref[head, :HD, :].astype(f32), q_ref[at, :], q_scale[head : head + 1, :], q_gain[...]
        )
        turned[at, :] = grad.astype(bf16)
        q_term = q_term + term
    for head in range(KV_HEADS):
        at = slice(head * HD, (head + 1) * HD)
        both = d_ref[head * per_group, HD:, :].astype(f32)
        for other in range(1, per_group):
            both = both + d_ref[head * per_group + other, HD:, :].astype(f32)
        grad, term = back(both[:HD], k_ref[at, :], k_scale[head : head + 1, :], k_gain[...])
        place = HEADS * HD + head * HD
        turned[place : place + HD, :] = grad.astype(bf16)
        k_term = k_term + term
        place += KV_HEADS * HD
        turned[place : place + HD, :] = both[HD:].astype(bf16)
    rows = turned.shape[0] // 4
    columns = d_attn_ref.shape[1] // 4
    shares = ((near, core, y), (far, core, 1 - y), (give, 1 - core, y), (give_far, 1 - core, 1 - y))
    for out_ref, to_core, to_y in shares:
        share = to_core * 2 + to_y
        out_ref[:rows, :] = turned[pl.ds(pl.multiple_of(share * rows, rows), rows), :]
        out_ref[rows:, :] = d_attn_ref[:, pl.ds(pl.multiple_of(share * columns, columns), columns)]
    for at in range(0, turned.shape[0], 256):
        natural[:, at : at + 256] = turned[at : at + 256, :].T
    d_normed = contract(natural[...], weight[...], (1, 1))
    x = x_ref[...].astype(f32)
    d_norm, gain_term = norm_back(d_normed, x, scale_ref[...], gain_ref[...])
    d_x_ref[...] = d_h_ref[...] + d_norm
    gains_ref[...] = jnp.zeros_like(gains_ref)
    gains_ref[0:1, :] = jnp.sum(gain_term, axis=0, keepdims=True)
    gains_ref[1:2, 0:HD] = jnp.sum(q_term.T, axis=0, keepdims=True)
    gains_ref[2:3, 0:HD] = jnp.sum(k_term.T, axis=0, keepdims=True)


def attention_back(here, arrays):
    f32, bf16 = jnp.float32, jnp.bfloat16
    shape = jax.ShapeDtypeStruct
    weight, x = arrays[9], arrays[10]
    tokens, width = x.shape
    rows = weight.shape[1] // 4 + tokens
    assert width // 4 == tokens
    outs = [
        *[shape((rows, tokens), bf16)] * 4,
        shape((tokens, width), f32),
        shape((8, width), f32),
    ]
    return call_with_here(
        attention_back_kernel, here, (1,), arrays, [whole(a) for a in arrays], outs,
        [whole(o) for o in outs],
        [pltpu.VMEM((weight.shape[1], tokens), bf16), pltpu.VMEM((tokens, weight.shape[1]), bf16)],
        micros=0,
    )


def attention_product_kernel(here, *refs):
    planes, terms, gains_ref, ffn_gain_ref = refs[:4], refs[4:8], refs[8], refs[9]
    sent, kept, left, right, left_out, right_out = refs[10:]
    tokens = planes[0].shape[2]
    cut = right.shape[1]
    for i in range(4):
        at = slice(i * tokens, (i + 1) * tokens)
        left[:, at] = planes[i][0]
        left_out[:, at] = planes[i][1]
        share = terms[i]
        right[at, :] = share[:cut].T
        right_out[at, :] = share[cut:]
    step = left.shape[0] // 4
    for owner, out_ref in ((1 - here[3], sent), (here[3], kept)):
        for half in range(2):
            at = pl.ds(pl.multiple_of(owner * 2 * step + half * step, step), step)
            out_ref[half, :step, :cut] = jnp.dot(
                left[at, :], right[...], preferred_element_type=jnp.float32
            ).astype(out_ref.dtype)
            out_ref[half, :step, cut:] = jnp.dot(
                left_out[at, :], right_out[...], preferred_element_type=jnp.float32
            ).astype(out_ref.dtype)
        rows = gains_ref.shape[1] // 2
        mine = pl.ds(pl.multiple_of(owner * rows, rows), rows)
        wide = out_ref.shape[2] - rows
        block = jnp.concatenate(
            [
                jnp.concatenate([gains_ref[0:1, mine], gains_ref[1:2, 0:wide]], axis=1),
                jnp.concatenate([ffn_gain_ref[:, mine], gains_ref[2:3, 0:wide]], axis=1),
                jnp.zeros((GAIN_ROWS - 2, out_ref.shape[2]), jnp.float32),
            ],
            axis=0,
        )
        out_ref[0, step:, :] = block.astype(out_ref.dtype)
        out_ref[1, step:, :] = jnp.zeros((GAIN_ROWS, out_ref.shape[2]), out_ref.dtype)


def attention_products(here, pair_plane, shares, gains, ffn_gain):
    _, width, tokens = pair_plane[0].shape
    cut = shares[0].shape[0] - tokens
    shape = (2, width // 4 + GAIN_ROWS, cut + tokens)
    outs = [jax.ShapeDtypeStruct(shape, jnp.bfloat16), jax.ShapeDtypeStruct(shape, jnp.float32)]
    return call_with_here(
        attention_product_kernel,
        here,
        (1,),
        [*pair_plane, *shares, gains, ffn_gain],
        [whole(a) for a in (*pair_plane, *shares, gains, ffn_gain)],
        outs,
        [whole(o) for o in outs],
        [
            pltpu.VMEM((width, 4 * tokens), jnp.bfloat16),
            pltpu.VMEM((4 * tokens, cut), jnp.bfloat16),
            pltpu.VMEM((width, 4 * tokens), jnp.bfloat16),
            pltpu.VMEM((4 * tokens, tokens), jnp.bfloat16),
        ],
        micros=3,
    )


def place_gate_up_kernel(here, *refs):
    mine, across, beside, diagonal, out_ref = *refs[:4], refs[-1]
    pieces = (mine, across, beside, diagonal)
    wide = mine.shape[2]
    for case in range(4):
        core, y = case // 2, case % 2

        @pl.when((here[1] == core) & (here[2] == y))
        def _(core=core, y=y):
            for kind in range(2):
                for column in range(2):
                    value = pieces[(y ^ column) * 2 + (core ^ kind)][0]
                    out_ref[:, kind, column * wide : (column + 1) * wide] = value.astype(
                        jnp.float32
                    )


def place_gate_up(here, chunk, pieces, before):
    _, rows, wide = pieces[0].shape
    step = 64
    blocks = rows // step

    def source(i, here):
        return ((i // blocks) ^ here[0], i % blocks, 0)

    arrays = list(pieces)
    specs = [pl.BlockSpec((1, step, wide), source)] * 4
    aliases = {}
    if before is not None:
        arrays.append(before)
        specs.append(pl.BlockSpec(memory_space=pl.ANY))
        aliases = {5: 0}
    (out,) = call_with_here(
        place_gate_up_kernel,
        here,
        (2 * blocks,),
        arrays,
        specs,
        [jax.ShapeDtypeStruct((2 * rows, 2, 2 * wide * CHUNKS), jnp.float32)],
        [pl.BlockSpec((step, 2, 2 * wide), lambda i, here: (i, 0, chunk))],
        aliases=aliases,
        micros=0,
    )
    return out


def place_down(here, pieces):
    _, rows, columns = pieces[0].shape

    def kernel(here, *refs):
        for s in range(8):

            @pl.when(pl.program_id(0) == s)
            def _(s=s):
                refs[4][...] = refs[s % 4][s // 4].astype(jnp.float32)

    def target(s, here):
        half = (s // 4) ^ here[0]
        y = ((s // 2) % 2) ^ here[2]
        core = (s % 2) ^ here[1]
        return ((core * 2 + y) * 2 + half, 0)

    (out,) = call_with_here(
        kernel,
        here,
        (8,),
        list(pieces),
        [whole(v) for v in pieces],
        [jax.ShapeDtypeStruct((rows * 8, columns), jnp.float32)],
        [pl.BlockSpec((rows, columns), target)],
    )
    return out


def place_attention(here, pieces, cut):
    _, rows, columns = pieces[0].shape
    rows -= GAIN_ROWS

    def kernel(here, *refs):
        qkv_ref, out_ref, gains_ref = refs[4:]
        for s in range(8):

            @pl.when(pl.program_id(0) == s)
            def _(s=s):
                value = refs[s % 4][s // 4]
                qkv_ref[...] = value[:rows, :cut].astype(jnp.float32)
                out_ref[...] = value[:rows, cut:].astype(jnp.float32)
                gains = value[rows:].astype(jnp.float32)
                gains_ref[...] = gains if s == 0 else gains_ref[...] + gains

    def target(s, here):
        half = (s // 4) ^ here[0]
        return (half, ((s % 2) ^ here[1]) * 2 + (((s // 2) % 2) ^ here[2]))

    shape = jax.ShapeDtypeStruct
    f32 = jnp.float32
    gain_shape = (GAIN_ROWS, columns)
    return call_with_here(
        kernel,
        here,
        (8,),
        list(pieces),
        [whole(v) for v in pieces],
        [
            shape((2 * rows, 4 * cut), f32),
            shape((2 * rows, 4 * (columns - cut)), f32),
            shape(gain_shape, f32),
        ],
        [
            pl.BlockSpec((rows, cut), target),
            pl.BlockSpec((rows, columns - cut), target),
            pl.BlockSpec(gain_shape, lambda s, here: (0, 0)),
        ],
    )


def on_block(
    tokens,
    qkv_weight,
    out_weight,
    gate_up_weight,
    down_weight,
    attn_gain,
    ffn_gain,
    query_gain,
    key_gain,
    seq_lengths,
    block_order,
    cotangent,
):
    inputs = tokens[0].astype(jnp.float32)
    rows_here = inputs.shape[0]
    ctx_size = lax.axis_size("ctx")
    ctx_index = lax.axis_index("ctx")
    per_group = HEADS // KV_HEADS
    q_width = HEADS * HD
    kv_width = KV_HEADS * HD
    order_row = block_order[0]
    lengths_row = seq_lengths[0]
    slots = jnp.arange(rows_here, dtype=jnp.int32) // BLK + ctx_index * (rows_here // BLK)
    table = slots[:, None] == jnp.arange(order_row.shape[0], dtype=jnp.int32)[None, :]
    packed = (
        jnp.sum(jnp.where(table, order_row[None, :], 0), axis=1) * BLK
        + jnp.arange(rows_here, dtype=jnp.int32) % BLK
    )
    local = packed - starts_of(packed, lengths_row)
    frequency = ROPE_BASE ** (-2.0 * jnp.arange(HD // 2, dtype=jnp.float32) / HD)
    angle = frequency[:, None] * local.astype(jnp.float32)[None, :]
    cosine = jnp.cos(angle)[None]
    sine = jnp.sin(angle)[None]
    bf16, f32 = jnp.bfloat16, jnp.float32
    parts = ctx_size // HEADS
    part = ctx_index // HEADS
    part_blocks = HEADS * rows_here // BLK
    q_order = lax.dynamic_slice_in_dim(order_row, part * part_blocks, part_blocks)
    q_slot, q_place, q_start = block_tables(q_order, lengths_row)
    q_slot = q_slot + part * part_blocks
    kv_slot, _, _ = block_tables(order_row, lengths_row)
    first = jnp.min(q_start.reshape(-1, TILE), axis=1) // TILE
    last = jnp.max(q_place.reshape(-1, TILE), axis=1) // TILE + 1
    tables = (q_slot, kv_slot, first, last)
    q_rows, kv_rows = part_blocks * BLK, order_row.shape[0] * BLK

    links = Links(ctx_size)
    here = links.here
    width = inputs.shape[1]
    rows = qkv_weight.shape[0]
    part_rows = rows // 4

    def quarter_rows(weight):
        return lax.dynamic_slice_in_dim(weight, links.quarter * part_rows, part_rows)

    qkv_piece = quarter_rows(qkv_weight)
    gains_here = jnp.concatenate([after(attn_gain, qkv_piece), ffn_gain, query_gain, key_gain])
    gains_there = links.over_x(gains_here)

    def gain_of(at, size):
        mine, other = gains_here[at : at + size], gains_there[at : at + size]
        return jnp.where(
            links.side == 0, jnp.concatenate([mine, other]), jnp.concatenate([other, mine])
        ).astype(f32)

    gain_attn = gain_of(0, rows)
    gain_ffn = gain_of(rows, rows)
    gain_query = gain_of(2 * rows, HD // 2)
    gain_key = gain_of(2 * rows + HD // 2, HD // 2)
    ff_chunk = gate_up_weight.shape[2] // CHUNKS

    def gate_up_piece(chunk):
        piece = lax.dynamic_slice(
            gate_up_weight,
            (links.quarter * part_rows, 0, chunk * ff_chunk),
            (part_rows, 2, ff_chunk),
        )
        return [piece[:, 0], piece[:, 1]]

    d_ffn = cotangent[0]
    d_beside = links.over_y(d_ffn)
    qkv_there = after(links.over_x(qkv_piece), d_beside)
    first_piece, first_up = gate_up_piece(0)
    up_piece = jnp.concatenate([first_up, quarter_rows(out_weight)], axis=1)
    second_piece = jnp.concatenate(gate_up_piece(1), axis=1)
    down_piece = lax.dynamic_slice_in_dim(
        down_weight, links.quarter * (width // 4), width // 4, 1
    )
    d_ffn = cotangent[0]
    tokens_here = tokens[0]
    qkv_there = after(qkv_there, first_piece)
    first_there = links.over_x(after(first_piece, qkv_there))
    up_there = links.over_x(after(up_piece, first_there))
    gate_up = jnp.transpose(after(gate_up_weight, qkv_there), (1, 0, 2))
    qkv_beside = links.over_y(qkv_there)
    qkv_pieces = (
        qkv_there,
        links.over_core(qkv_there),
        qkv_beside,
        links.over_core(after(qkv_beside, gate_up)),
    )
    sent, w_qkv, q_raw, k_raw, q_scale, k_scale, normed, scale_one = project(
        here, after(tokens_here, first_there), gain_attn[None], qkv_weight, qkv_pieces,
        gain_query[:, None], gain_key[:, None], cosine[0], sine[0],
    )
    got = lax.all_to_all(sent, "ctx", 0, 0, tiled=True)
    up_there = after(up_there, sent)
    down_there = links.over_x(after(down_piece, up_there))
    first_beside = links.over_y(first_there)
    up_beside = links.over_y(up_there)
    q_place, q_start = q_place[None], q_start[None]
    shape = jax.ShapeDtypeStruct
    attn_sent, *held = kernel_call(
        attend_kernel,
        tables,
        (got, q_place, q_start),
        [
            shape((ctx_size, HD, rows_here), bf16),
            shape((q_rows, HD), bf16),
            shape((HD, q_rows), bf16),
            shape((kv_rows, HD), bf16),
            shape((HD, kv_rows), bf16),
            shape((kv_rows, HD), bf16),
            shape((HD, q_rows), f32),
            shape((1, q_rows), f32),
        ],
        [pltpu.VMEM((HD, kv_rows), bf16)],
        ATTEND,
    )
    attn_sent = after(attn_sent, first_beside)
    attn_in = lax.dynamic_slice_in_dim(
        lax.all_to_all(attn_sent, "ctx", 0, 0, tiled=True), part * HEADS, HEADS
    ).reshape(q_width, rows_here)
    down_there = after(down_there, attn_sent)
    second_there = links.over_x(after(second_piece, down_there))
    down_beside = links.over_y(down_there)

    def spread(there, beside, time):
        there, beside = after(there, time), after(beside, time)
        return (there, links.over_core(there), beside, links.over_core(beside))

    first_pieces = spread(first_there, first_beside, attn_in)
    up_pieces = spread(up_there, up_beside, attn_sent)
    down_pieces = spread(down_there, down_beside, attn_in)
    second_beside = links.over_y(second_there)
    w_out, h_one, scale_two, two, two_t = attend_out(
        here, attn_in, tokens_here, gain_ffn[None], out_weight, up_pieces
    )
    two_beside = links.over_y(two_t)
    dealt_here, (out_sum, two_sum) = ffn(
        here, 0, two, d_ffn, gate_up, (first_pieces, up_pieces), down_weight, down_pieces, [h_one]
    )
    second_beside = after(second_beside, out_sum)
    second_pieces = (
        second_there, links.over_core(second_there), second_beside, links.over_core(second_beside)
    )
    near, far, give, give_far = dealt_here
    got_far = links.over_core(give_far)
    first_shares = (near, links.over_core(give), links.over_y(far), links.over_y(got_far))
    out_sum = after(out_sum, got_far)
    dealt_here, (output, d_h_one, d_attn, d_heads, ffn_gain_term) = ffn(
        here, 1, two, d_ffn, gate_up, (second_pieces, second_pieces), down_weight, down_pieces,
        [out_sum, two_sum, h_one, scale_two, w_out], gain_ffn[None],
    )
    second_shares = links.deal_plane(*dealt_here)

    def plane(value, beside, time):
        value, beside = after(value, time), after(beside, time)
        return (value, links.over_core(value), beside, links.over_core(beside))

    columns = ff_chunk // 2
    d_heads = d_heads.reshape(HEADS, HD, rows_here)
    d_got = lax.all_to_all(d_heads, "ctx", 0, 0, tiled=True)
    pair = jnp.stack([after(normed, d_heads), attn_in])
    two_plane = plane(two_t, two_beside, pair)
    first_products = wide_products(
        here, two_plane, [after(v, d_heads) for v in first_shares], columns
    )
    pair_across = links.over_core(pair)
    d_got = after(d_got, first_products[0], pair_across)
    (d_sent,) = kernel_call(
        attend_back_kernel,
        tables,
        (d_got, q_place, q_start, *held),
        [shape((ctx_size, 3 * HD, rows_here), bf16)],
        [
            pltpu.VMEM((HD, q_rows), bf16),
            pltpu.VMEM((q_rows, HD), bf16),
            pltpu.VMEM((kv_rows, HD), f32),
            pltpu.VMEM((kv_rows, HD), f32),
        ],
        ATTEND_BACK,
    )
    first_got = links.over_x(first_products[0])
    d_sent = after(d_sent, first_got, *second_shares[2:])
    d_back = lax.all_to_all(d_sent, "ctx", 0, 0, tiled=True)
    d_plane = plane(d_ffn, d_beside, d_sent)
    second_products = wide_products(
        here, two_plane, [after(v, d_plane[1]) for v in second_shares], columns
    )
    down_terms = down_products(
        here, d_plane, first_shares, second_shares, columns // 2
    )
    second_got = links.over_x(after(second_products[0], first_got))
    pair_beside = links.over_y(after(pair, d_sent))
    d_back = after(d_back, down_terms[0], pair_beside, second_got)
    *d_shares, d_inputs, gain_sums = attention_back(
        here,
        [
            d_back, q_raw, k_raw, q_scale, k_scale, gain_query[:, None], gain_key[:, None],
            cosine[0], sine[0], w_qkv, tokens_here, scale_one, gain_attn[None], d_h_one, d_attn,
        ],
    )
    down_got = links.over_x(after(down_terms[0], second_got))
    near, far, give, give_far = d_shares
    got, got_far = links.over_core(give), links.over_core(give_far)
    attention_shares = (near, got, links.over_y(far), links.over_y(got_far))
    pair_plane = (pair, pair_across, pair_beside, links.over_core(after(pair_beside, d_sent)))

    kept = [first_products[1], second_products[1], down_terms[1], None]
    got = [first_got, second_got, down_got, None]
    given, part, across, full, back, beside = ([None] * 4 for _ in range(6))

    def give_half(n):
        given[n] = links.over_z(links.half_of(kept[n], got[n], False))

    def sum_part(n, time):
        part[n] = add(links.half_of(kept[n], got[n], True), after(given[n], time))
        across[n] = links.over_two_z(part[n])

    def sum_full(n, time):
        full[n] = add(part[n], after(across[n], time))
        back[n] = links.over_z(full[n])

    def spread_y(n, time):
        full[n] = jnp.stack([full[n], after(back[n], time)])
        beside[n] = links.over_y(full[n])

    def spread_core(n, time):
        beside[n] = after(beside[n], time)
        return (full[n], links.over_core(full[n]), beside[n], links.over_core(beside[n]))

    give_half(0)
    given[0] = after(given[0], down_terms[0])
    sum_part(0, second_got)
    give_half(1)
    sum_part(1, got_far)
    got[2] = after(got[2], part[1], attention_shares[1], pair_plane[3])
    give_half(2)
    sum_full(0, got[2])
    attention_shares = (*attention_shares[:2], *(after(v, full[0]) for v in attention_shares[2:]))
    attention_terms = attention_products(
        here, pair_plane, attention_shares, gain_sums, ffn_gain_term
    )
    kept[3] = attention_terms[1]
    attention_got = links.over_x(attention_terms[0])
    spread_y(0, attention_terms[0])
    sum_part(2, full[0])
    sum_full(1, part[2])
    got[3] = after(attention_got, full[1])
    give_half(3)
    first_pieces = spread_core(0, got[3])
    spread_y(1, beside[0])
    sum_part(3, full[1])
    sum_full(2, part[3])
    first_placed = place_gate_up(here, 0, first_pieces, None)
    second_pieces = spread_core(1, full[2])
    spread_y(2, (first_placed, beside[1]))
    sum_full(3, full[2])
    grad_gate_up = place_gate_up(here, 1, second_pieces, first_placed)
    spread_y(3, full[2])
    grad_down = place_down(here, spread_core(2, grad_gate_up))
    cut = qkv_weight.shape[1] // 4
    grad_qkv, grad_out, gain_sums = place_attention(here, spread_core(3, grad_gate_up), cut)
    at = links.side * (HD // 2)
    gain_grads = [
        gain_sums[0, :rows],
        gain_sums[1, :rows],
        lax.dynamic_slice_in_dim(gain_sums[0, rows : rows + HD], at, HD // 2),
        lax.dynamic_slice_in_dim(gain_sums[1, rows : rows + HD], at, HD // 2),
    ]
    return (
        output[None],
        d_inputs[None],
        grad_qkv,
        grad_out,
        grad_gate_up,
        grad_down,
        *gain_grads,
    )


def on_device(
    tokens,
    qkv_weight,
    out_weight,
    gate_up_weight,
    down_weight,
    attn_gain,
    ffn_gain,
    query_gain,
    key_gain,
    seq_lengths,
    block_order,
    cotangent,
):
    inputs = tokens[0].astype(jnp.float32)
    rows_here = inputs.shape[0]
    ctx_size = lax.axis_size("ctx")
    ctx_index = lax.axis_index("ctx")
    per_group = HEADS // KV_HEADS
    q_width = HEADS * HD
    kv_width = KV_HEADS * HD
    order_row = block_order[0]
    lengths_row = seq_lengths[0]
    slots = jnp.arange(rows_here, dtype=jnp.int32) // BLK + ctx_index * (rows_here // BLK)
    table = slots[:, None] == jnp.arange(order_row.shape[0], dtype=jnp.int32)[None, :]
    packed = (
        jnp.sum(jnp.where(table, order_row[None, :], 0), axis=1) * BLK
        + jnp.arange(rows_here, dtype=jnp.int32) % BLK
    )
    local = packed - starts_of(packed, lengths_row)
    frequency = ROPE_BASE ** (-2.0 * jnp.arange(HD // 2, dtype=jnp.float32) / HD)
    angle = frequency[:, None] * local.astype(jnp.float32)[None, :]
    cosine = jnp.cos(angle)[None]
    sine = jnp.sin(angle)[None]
    bf16, f32 = jnp.bfloat16, jnp.float32
    parts = ctx_size // HEADS
    part = ctx_index // HEADS
    part_blocks = HEADS * rows_here // BLK
    q_order = lax.dynamic_slice_in_dim(order_row, part * part_blocks, part_blocks)
    q_slot, q_place, q_start = block_tables(q_order, lengths_row)
    q_slot = q_slot + part * part_blocks
    kv_slot, _, _ = block_tables(order_row, lengths_row)
    first = jnp.min(q_start.reshape(-1, TILE), axis=1) // TILE
    last = jnp.max(q_place.reshape(-1, TILE), axis=1) // TILE + 1
    tables = (q_slot, kv_slot, first, last)
    q_rows, kv_rows = part_blocks * BLK, order_row.shape[0] * BLK

    def fetch_attention():
        return (
            lax.all_gather(qkv_weight, "fsdp", axis=0, tiled=True),
            lax.all_gather(out_weight, "fsdp", axis=0, tiled=True),
            lax.all_gather(attn_gain, "fsdp", axis=0, tiled=True),
            lax.all_gather(ffn_gain, "fsdp", axis=0, tiled=True),
            lax.all_gather(query_gain, "fsdp", axis=0, tiled=True),
            lax.all_gather(key_gain, "fsdp", axis=0, tiled=True),
        )

    w_qkv, w_out, gain_attn, gain_ffn, gain_query, gain_key = fetch_attention()
    gain_attn = gain_attn.astype(jnp.float32)
    gain_ffn = gain_ffn.astype(jnp.float32)
    gain_query = gain_query.astype(jnp.float32)
    gain_key = gain_key.astype(jnp.float32)
    scale_one = rms_scale(inputs)
    normed = (inputs * scale_one * gain_attn).astype(jnp.bfloat16)
    projected = lax.dot_general(
        w_qkv, normed, (((0,), (1,)), ((), ())), preferred_element_type=f32
    )
    q_raw = projected[:q_width].reshape(HEADS, HD, rows_here)
    k_raw = projected[q_width : q_width + kv_width].reshape(KV_HEADS, HD, rows_here)
    values_here = projected[q_width + kv_width :].reshape(KV_HEADS, HD, rows_here).astype(bf16)
    q_scale = rms_scale(q_raw, 1)
    k_scale = rms_scale(k_raw, 1)
    column_query, column_key = gain_query[:, None], gain_key[:, None]
    queries = rope(q_raw * q_scale * column_query, cosine, sine).astype(bf16)
    keys_here = rope(k_raw * k_scale * column_key, cosine, sine).astype(bf16)
    sent = jnp.concatenate(
        [queries, jnp.repeat(keys_here, per_group, 0), jnp.repeat(values_here, per_group, 0)], axis=1
    )
    sent = jnp.concatenate([sent] * parts, axis=0)
    got = lax.all_to_all(sent, "ctx", 0, 0, tiled=True)
    q_place, q_start = q_place[None], q_start[None]
    shape = jax.ShapeDtypeStruct
    attn_sent, *held = kernel_call(
        attend_kernel,
        tables,
        (got, q_place, q_start),
        [
            shape((ctx_size, HD, rows_here), bf16),
            shape((q_rows, HD), bf16),
            shape((HD, q_rows), bf16),
            shape((kv_rows, HD), bf16),
            shape((HD, kv_rows), bf16),
            shape((kv_rows, HD), bf16),
            shape((HD, q_rows), f32),
            shape((1, q_rows), f32),
        ],
        [pltpu.VMEM((HD, kv_rows), bf16)],
        ATTEND,
    )
    attn_in = lax.dynamic_slice_in_dim(
        lax.all_to_all(attn_sent, "ctx", 0, 0, tiled=True), part * HEADS, HEADS
    ).reshape(q_width, rows_here)
    h_one = inputs + lax.dot_general(
        attn_in, w_out, (((0,), (0,)), ((), ())), preferred_element_type=f32
    )
    scale_two = rms_scale(h_one)
    normed_two = (h_one * scale_two * gain_ffn).astype(jnp.bfloat16)
    columns = normed_two
    gate_up = jnp.einsum(
        "tr,rgf->tgf",
        columns,
        lax.all_gather(gate_up_weight, "fsdp", axis=0, tiled=True),
        preferred_element_type=jnp.float32,
    )
    gate = gate_up[:, 0]
    upper = gate_up[:, 1]
    sigma = jax.nn.sigmoid(gate)
    hidden = (gate * sigma * upper).astype(jnp.bfloat16)
    columns = hidden
    ffn_out = jnp.dot(
        columns,
        lax.all_gather(down_weight, "fsdp", axis=0, tiled=True),
        preferred_element_type=jnp.float32,
    )
    output = (h_one + ffn_out).astype(jnp.bfloat16)
    d_out = cotangent[0].astype(jnp.float32)
    d_ffn = d_out.astype(jnp.bfloat16)
    d_hidden = lax.dot_general(
        d_ffn,
        lax.all_gather(down_weight, "fsdp", axis=0, tiled=True),
        (((1,), (1,)), ((), ())),
        preferred_element_type=jnp.float32,
    )
    d_gate = d_hidden * upper * sigma * (1.0 + gate * (1.0 - sigma))
    d_upper = d_hidden * gate * sigma
    d_gate_up = jnp.stack([d_gate, d_upper], axis=1).astype(jnp.bfloat16)
    d_normed_two = jnp.einsum(
        "tgf,rgf->tr",
        d_gate_up,
        lax.all_gather(gate_up_weight, "fsdp", axis=0, tiled=True),
        preferred_element_type=jnp.float32,
    )
    columns = normed_two
    grad_gate_up = lax.psum_scatter(
        jnp.einsum("tr,tgf->rgf", columns, d_gate_up, preferred_element_type=jnp.float32).astype(
            jnp.bfloat16
        ),
        "fsdp",
        scatter_dimension=0,
        tiled=True,
    )
    columns = hidden
    grad_down = lax.psum_scatter(
        lax.dot_general(
            columns, d_ffn, (((0,), (0,)), ((), ())), preferred_element_type=jnp.float32
        ).astype(jnp.bfloat16),
        "fsdp",
        scatter_dimension=0,
        tiled=True,
    )
    d_norm_two, ffn_gain_term = norm_back(d_normed_two, h_one, scale_two, gain_ffn)
    d_h_one = d_out + d_norm_two
    d_attn = d_h_one.astype(jnp.bfloat16)
    grad_out_here = jnp.dot(attn_in, d_attn, preferred_element_type=f32)
    d_heads = lax.dot_general(
        w_out, d_attn, (((1,), (1,)), ((), ())), preferred_element_type=f32
    ).astype(bf16)
    d_heads = jnp.concatenate([d_heads.reshape(HEADS, HD, rows_here)] * parts, axis=0)
    d_got = lax.all_to_all(d_heads, "ctx", 0, 0, tiled=True)
    (d_sent,) = kernel_call(
        attend_back_kernel,
        tables,
        (d_got, q_place, q_start, *held),
        [shape((ctx_size, 3 * HD, rows_here), bf16)],
        [
            pltpu.VMEM((HD, q_rows), bf16),
            pltpu.VMEM((q_rows, HD), bf16),
            pltpu.VMEM((kv_rows, HD), f32),
            pltpu.VMEM((kv_rows, HD), f32),
        ],
        ATTEND_BACK,
    )
    d_back = lax.all_to_all(d_sent, "ctx", 0, 0, tiled=True)
    d_query = lax.dynamic_slice_in_dim(d_back[:, :HD], part * HEADS, HEADS).astype(f32)
    d_key_value = jnp.sum(
        d_back[:, HD:].reshape(parts, KV_HEADS, per_group, 2 * HD, rows_here).astype(f32),
        axis=(0, 2),
    )
    dq_normed = rope_back(d_query, cosine, sine)
    dk_normed = rope_back(d_key_value[:, :HD], cosine, sine)
    dq_raw, query_term = norm_back(dq_normed, q_raw, q_scale, column_query, 1)
    dk_raw, key_term = norm_back(dk_normed, k_raw, k_scale, column_key, 1)
    d_projected = jnp.concatenate(
        [
            dq_raw.reshape(q_width, rows_here).astype(bf16),
            dk_raw.reshape(kv_width, rows_here).astype(bf16),
            d_key_value[:, HD:].reshape(kv_width, rows_here).astype(bf16),
        ],
        axis=0,
    )
    grad_qkv_here = lax.dot_general(
        normed, d_projected, (((0,), (1,)), ((), ())), preferred_element_type=f32
    )
    d_normed = lax.dot_general(
        d_projected, w_qkv, (((0,), (1,)), ((), ())), preferred_element_type=f32
    )
    d_norm_one, attn_gain_term = norm_back(d_normed, inputs, scale_one, gain_attn)
    d_inputs = d_h_one + d_norm_one
    shard_qkv, shard_out, shard_attn_gain, shard_ffn_gain, shard_query_gain, shard_key_gain = (
        lax.psum_scatter(
            grad_qkv_here.astype(jnp.bfloat16), "fsdp", scatter_dimension=0, tiled=True
        ).astype(jnp.float32),
        lax.psum_scatter(
            grad_out_here.astype(jnp.bfloat16), "fsdp", scatter_dimension=0, tiled=True
        ).astype(jnp.float32),
        lax.psum_scatter(
            jnp.sum(attn_gain_term, axis=0).astype(jnp.bfloat16),
            "fsdp",
            scatter_dimension=0,
            tiled=True,
        ).astype(jnp.float32),
        lax.psum_scatter(
            jnp.sum(ffn_gain_term, axis=0).astype(jnp.bfloat16),
            "fsdp",
            scatter_dimension=0,
            tiled=True,
        ).astype(jnp.float32),
        lax.psum_scatter(
            jnp.sum(query_term, axis=(0, 2)).astype(jnp.bfloat16),
            "fsdp",
            scatter_dimension=0,
            tiled=True,
        ).astype(jnp.float32),
        lax.psum_scatter(
            jnp.sum(key_term, axis=(0, 2)).astype(jnp.bfloat16),
            "fsdp",
            scatter_dimension=0,
            tiled=True,
        ).astype(jnp.float32),
    )
    summed_grads = (
        lax.psum(shard_qkv.astype(jnp.bfloat16), "ctx").astype(jnp.float32),
        lax.psum(shard_out.astype(jnp.bfloat16), "ctx").astype(jnp.float32),
        lax.psum(grad_gate_up, "ctx").astype(jnp.float32),
        lax.psum(grad_down, "ctx").astype(jnp.float32),
        lax.psum(shard_attn_gain.astype(jnp.bfloat16), "ctx").astype(jnp.float32),
        lax.psum(shard_ffn_gain.astype(jnp.bfloat16), "ctx").astype(jnp.float32),
        lax.psum(shard_query_gain.astype(jnp.bfloat16), "ctx").astype(jnp.float32),
        lax.psum(shard_key_gain.astype(jnp.bfloat16), "ctx").astype(jnp.float32),
    )
    return (
        output[None],
        d_inputs[None],
        summed_grads[0],
        summed_grads[1],
        summed_grads[2],
        summed_grads[3],
        summed_grads[4],
        summed_grads[5],
        summed_grads[6],
        summed_grads[7],
    )


def solution(mesh):
    block = mesh.shape["fsdp"] == 2 and mesh.shape["ctx"] == 16
    return jax.shard_map(
        on_block if block else on_device,
        mesh=mesh,
        in_specs=(
            P("fsdp", "ctx", None),
            P("fsdp", None),
            P("fsdp", None),
            P("fsdp", None, None),
            P("fsdp", None),
            P("fsdp"),
            P("fsdp"),
            P("fsdp"),
            P("fsdp"),
            P("fsdp", None),
            P("fsdp", None),
            P("fsdp", "ctx", None),
        ),
        out_specs=(
            P("fsdp", "ctx", None),
            P("fsdp", "ctx", None),
            P("fsdp", None),
            P("fsdp", None),
            P("fsdp", None, None),
            P("fsdp", None),
            P("fsdp"),
            P("fsdp"),
            P("fsdp"),
            P("fsdp"),
        ),
        check_vma=False,
    )
```

```python
import functools

import jax
import jax.numpy as jnp
from jax import lax
from jax.experimental import pallas as pl
from jax.experimental.pallas import tpu as pltpu
from jax.sharding import PartitionSpec as P

HEADS = 16
KV_HEADS = 8
HD = 64
BLK = 128
TILE = 512
CHUNKS = 2
PROJECT = 0
ATTEND = 0
OUT = 0
FFN = (0, 0)
ATTEND_BACK = 25


EPSILON = 1e-05
ROPE_BASE = 1000000.0
LOG2E = 1.4426950408889634
SCORE_SCALE = LOG2E * HD ** (-0.5)


def rms_scale(values, axis=-1):
    return lax.rsqrt(jnp.mean(values * values, axis=axis, keepdims=True) + EPSILON)


def norm_back(grad_normed, inputs, scale, gain, axis=-1):
    scaled = grad_normed * gain
    grad_in = scale * scaled - inputs * scale * scale * scale * jnp.mean(
        scaled * inputs, axis=axis, keepdims=True
    )
    return (grad_in, grad_normed * inputs * scale)


def rope(values, cosine, sine):
    half = HD // 2
    first, second = values[:, :half], values[:, half:]
    return jnp.concatenate([first * cosine - second * sine, second * cosine + first * sine], axis=1)


def rope_back(values, cosine, sine):
    half = HD // 2
    first, second = values[:, :half], values[:, half:]
    return jnp.concatenate([first * cosine + second * sine, second * cosine - first * sine], axis=1)


def starts_of(packed, lengths_row):
    ends = jnp.cumsum(lengths_row)
    past = packed[:, None] >= ends[None, :]
    return jnp.sum(jnp.where(past, lengths_row[None, :], 0), axis=1)


def block_tables(order, lengths_row):
    count = order.shape[0]
    rank = jnp.sum((order[None, :] < order[:, None]).astype(jnp.int32), axis=1)
    hit = rank[None, :] == jnp.arange(count, dtype=jnp.int32)[:, None]
    slot = jnp.sum(jnp.where(hit, jnp.arange(count, dtype=jnp.int32)[None, :], 0), axis=1)
    block = jnp.sum(jnp.where(hit, order[None, :], 0), axis=1)
    place = (block[:, None] * BLK + jnp.arange(BLK, dtype=jnp.int32)[None, :]).reshape(-1)
    return (slot, place, starts_of(place, lengths_row))


def attend_kernel(
    q_slot, kv_slot, first, last, qkv_ref, place_ref, start_ref,
    out_ref, q_ref, qt_ref, k_ref, kt_ref, v_ref, ot_ref, total_ref, vt_ref
):
    per_device = qkv_ref.shape[2] // BLK
    kv_blocks = k_ref.shape[0] // BLK
    q_blocks = q_ref.shape[0] // BLK

    def piece(slot, lower):
        return qkv_ref[
            slot // per_device,
            lower : lower + HD,
            pl.ds(pl.multiple_of((slot % per_device) * BLK, BLK), BLK),
        ]

    for i in range(kv_blocks):
        here = slice(i * BLK, (i + 1) * BLK)
        keys = piece(kv_slot[i], HD)
        kt_ref[:, here] = keys
        k_ref[here, :] = keys.T
        values = piece(kv_slot[i], 2 * HD)
        vt_ref[:, here] = values
        v_ref[here, :] = values.T
    for i in range(q_blocks):
        here = slice(i * BLK, (i + 1) * BLK)
        queries = piece(q_slot[i], 0)
        qt_ref[:, here] = queries
        q_ref[here, :] = queries.T
    if q_blocks < kv_blocks:
        out_ref[...] = jnp.zeros_like(out_ref)

    def tile(i, carry):
        rows = pl.ds(pl.multiple_of(i * TILE, TILE), TILE)
        queries = qt_ref[:, rows]
        place = place_ref[:, rows]
        start = start_ref[:, rows]

        def step(j, state):
            total, summed = state
            at = pl.multiple_of(j * TILE, TILE)
            scores = jnp.dot(
                k_ref[pl.ds(at, TILE), :], queries, preferred_element_type=jnp.float32
            )
            key_place = lax.broadcasted_iota(jnp.int32, (TILE, TILE), 0) + at
            allowed = (key_place <= place) & (key_place >= start)
            lifted = jnp.where(allowed, jnp.exp2(scores * SCORE_SCALE), 0.0)
            total = total + jnp.sum(lifted, axis=0, keepdims=True)
            summed = summed + jnp.dot(
                vt_ref[:, pl.ds(at, TILE)],
                lifted.astype(jnp.bfloat16),
                preferred_element_type=jnp.float32,
            )
            return (total, summed)

        total, summed = lax.fori_loop(
            first[i],
            last[i],
            step,
            (jnp.zeros((1, TILE), jnp.float32), jnp.zeros((HD, TILE), jnp.float32)),
        )
        attn = summed / total
        ot_ref[:, rows] = attn
        total_ref[:, rows] = jnp.log(total) * LOG2E
        rounded = attn.astype(jnp.bfloat16)
        for part in range(TILE // BLK):
            slot = q_slot[i * (TILE // BLK) + part]
            out_ref[
                slot // per_device,
                :,
                pl.ds(pl.multiple_of((slot % per_device) * BLK, BLK), BLK),
            ] = rounded[:, part * BLK : (part + 1) * BLK]
        return carry

    lax.fori_loop(0, q_blocks * BLK // TILE, tile, 0)


def attend_back_kernel(
    q_slot, kv_slot, first, last, d_ref, place_ref, start_ref,
    q_ref, qt_ref, k_ref, kt_ref, v_ref, ot_ref, total_ref,
    out_ref, dt_ref, do_ref, dk_ref, dv_ref
):
    per_device = d_ref.shape[2] // BLK
    kv_blocks = k_ref.shape[0] // BLK
    q_blocks = q_ref.shape[0] // BLK

    def lanes(slot):
        return pl.ds(pl.multiple_of((slot % per_device) * BLK, BLK), BLK)

    for i in range(q_blocks):
        here = slice(i * BLK, (i + 1) * BLK)
        slot = q_slot[i]
        grads = d_ref[slot // per_device, :, lanes(slot)]
        dt_ref[:, here] = grads
        do_ref[here, :] = grads.T
    dk_ref[...] = jnp.zeros_like(dk_ref)
    dv_ref[...] = jnp.zeros_like(dv_ref)
    if q_blocks < kv_blocks:
        out_ref[...] = jnp.zeros_like(out_ref)

    def tile(i, carry):
        rows = pl.ds(pl.multiple_of(i * TILE, TILE), TILE)
        queries = qt_ref[:, rows]
        grads = dt_ref[:, rows]
        place = place_ref[:, rows]
        start = start_ref[:, rows]
        delta = jnp.sum(grads.astype(jnp.float32) * ot_ref[:, rows], axis=0, keepdims=True)
        total = total_ref[:, rows]

        def step(j, d_query):
            at = pl.multiple_of(j * TILE, TILE)
            here = pl.ds(at, TILE)
            scores = jnp.dot(k_ref[here, :], queries, preferred_element_type=jnp.float32)
            key_place = lax.broadcasted_iota(jnp.int32, (TILE, TILE), 0) + at
            allowed = (key_place <= place) & (key_place >= start)
            shares = jnp.where(allowed, jnp.exp2(scores * SCORE_SCALE - total), 0.0)
            d_shares = jnp.dot(v_ref[here, :], grads, preferred_element_type=jnp.float32)
            d_scores = (shares * (d_shares - delta)).astype(jnp.bfloat16)
            dv_ref[here, :] += jnp.dot(
                shares.astype(jnp.bfloat16), do_ref[rows, :], preferred_element_type=jnp.float32
            )
            dk_ref[here, :] += jnp.dot(
                d_scores, q_ref[rows, :], preferred_element_type=jnp.float32
            )
            return d_query + jnp.dot(
                kt_ref[:, here], d_scores, preferred_element_type=jnp.float32
            )

        d_query = lax.fori_loop(first[i], last[i], step, jnp.zeros((HD, TILE), jnp.float32))
        rounded = (d_query * HD ** (-0.5)).astype(jnp.bfloat16)
        for part in range(TILE // BLK):
            slot = q_slot[i * (TILE // BLK) + part]
            out_ref[slot // per_device, 0:HD, lanes(slot)] = rounded[
                :, part * BLK : (part + 1) * BLK
            ]
        return carry

    lax.fori_loop(0, q_blocks * BLK // TILE, tile, 0)
    for i in range(kv_blocks):
        here = slice(i * BLK, (i + 1) * BLK)
        slot = kv_slot[i]
        out_ref[slot // per_device, HD : 2 * HD, lanes(slot)] = (
            (dk_ref[here, :] * HD ** (-0.5)).T.astype(jnp.bfloat16)
        )
        out_ref[slot // per_device, 2 * HD : 3 * HD, lanes(slot)] = (
            dv_ref[here, :].T.astype(jnp.bfloat16)
        )


def cost(micros):
    return pl.CostEstimate(
        flops=1 + micros * 1_000_000_000, bytes_accessed=1, transcendentals=0
    )


def kernel_call(kernel, tables, arrays, outs, scratch, micros):
    smem = pl.BlockSpec(memory_space=pltpu.SMEM)
    vmem = pl.BlockSpec(memory_space=pltpu.VMEM)
    return pl.pallas_call(
        kernel,
        out_shape=outs,
        in_specs=[smem] * len(tables) + [vmem] * len(arrays),
        out_specs=[vmem] * len(outs),
        scratch_shapes=scratch,
        compiler_params=pltpu.CompilerParams(vmem_limit_bytes=48 * 1024 * 1024),
        cost_estimate=cost(micros),
    )(*tables, *arrays)


class Links:
    def __init__(self, ctx_size):
        self.depth = ctx_size // 4
        index = lax.axis_index("ctx")
        self.core = index % 2
        self.y = (index // 2) % 2
        self.side = lax.axis_index("fsdp")
        self.half = index // 4 % 2
        self.quarter = index % 2 * 2 + self.y
        self.here = jnp.stack([self.half, self.core, self.y, self.side]).astype(jnp.int32)

    def route(self, place):
        pairs = []
        for z in range(self.depth):
            for y in range(2):
                for core in range(2):
                    to_z, to_y, to_core = place(z, y, core)
                    pairs.append(((z * 2 + y) * 2 + core, (to_z * 2 + to_y) * 2 + to_core))
        return pairs

    def over_core(self, value):
        return lax.ppermute(value, "ctx", self.route(lambda z, y, c: (z, y, 1 - c)))

    def over_y(self, value):
        return lax.ppermute(value, "ctx", self.route(lambda z, y, c: (z, 1 - y, c)))

    def over_z(self, value):
        return lax.ppermute(value, "ctx", self.route(lambda z, y, c: (z ^ 1, y, c)))

    def over_two_z(self, value):
        return lax.ppermute(value, "ctx", self.route(lambda z, y, c: (z ^ 2, y, c)))

    def over_x(self, value):
        return lax.ppermute(value, "fsdp", [(0, 1), (1, 0)])

    def spread_plane(self, value):
        across = self.over_core(value)
        beside = self.over_y(value)
        return (value, across, beside, self.over_core(beside))

    def deal_plane(self, near, far, give, give_far):
        got, got_far = self.over_core(give), self.over_core(give_far)
        return (near, got, self.over_y(far), self.over_y(got_far))

    def half_of(self, kept, got, own):
        index = self.half if own else 1 - self.half
        return add(pick(kept, index, 0), pick(got, index, 0))


def pick(value, index, axis):
    return lax.dynamic_index_in_dim(value, index, axis, keepdims=False)


def add(left, right):
    return (left.astype(jnp.float32) + right.astype(jnp.float32)).astype(jnp.bfloat16)


def after(value, *others):
    return lax.optimization_barrier((value, *jax.tree.leaves(others)))[0]


def contract(left, right, axes):
    return lax.dot_general(
        left, right, ((axes[:1], axes[1:]), ((), ())), preferred_element_type=jnp.float32
    )


PARAMS = pltpu.CompilerParams(vmem_limit_bytes=56 * 1024 * 1024)


def call_with_here(
    kernel, here, grid, arrays, specs, outs, out_specs, scratch=(), aliases=None, micros=0
):
    return pl.pallas_call(
        kernel,
        grid_spec=pltpu.PrefetchScalarGridSpec(
            num_scalar_prefetch=1,
            grid=grid,
            in_specs=specs,
            out_specs=out_specs,
            scratch_shapes=list(scratch),
        ),
        out_shape=outs,
        input_output_aliases=aliases or {},
        compiler_params=PARAMS,
        cost_estimate=cost(micros),
    )(here, *arrays)


def whole(array):
    rank = len(array.shape)
    return pl.BlockSpec(array.shape, lambda i, here: (0,) * rank)


def project_kernel(here, *refs):
    x_ref, gain_ref, own_ref = refs[:3]
    pieces, q_gain, k_gain, cos_ref, sin_ref = refs[3:7], refs[7], refs[8], refs[9], refs[10]
    sent, weight, q_ref, k_ref, q_scale, k_scale, normed_ref, scale_ref = refs[11:]
    core, y, side = here[1], here[2], here[3]
    rows = own_ref.shape[0]
    part = rows // 4
    f32, bf16 = jnp.float32, jnp.bfloat16
    weight[pl.ds(pl.multiple_of(side * rows, rows), rows), :] = own_ref[...]
    for p in range(4):
        at = (1 - side) * rows + (((p % 2) ^ core) * 2 + ((p // 2) ^ y)) * part
        weight[pl.ds(pl.multiple_of(at, part), part), :] = pieces[p][...]
    x = x_ref[...].astype(f32)
    scale = rms_scale(x)
    scale_ref[...] = scale
    normed = (x * scale * gain_ref[...]).astype(bf16)
    normed_ref[...] = normed.T
    cosine, sine = cos_ref[...], sin_ref[...]
    half = HD // 2

    def turned(raw, gain, raw_ref, kept_scale, head):
        raw_ref[head * HD : (head + 1) * HD, :] = raw
        scale = rms_scale(raw, 0)
        kept_scale[head : head + 1, :] = scale
        value = raw * scale * gain
        first, second = value[:half], value[half:]
        return jnp.concatenate(
            [first * cosine - second * sine, second * cosine + first * sine], axis=0
        ).astype(bf16)

    per_group = HEADS // KV_HEADS
    for at in range(0, weight.shape[1], 2 * BLK):
        block = jnp.dot(normed, weight[:, at : at + 2 * BLK], preferred_element_type=f32)
        turned_block = block.T
        for n in range(2 * BLK // HD):
            head = at // HD + n
            raw = turned_block[n * HD : (n + 1) * HD, :]
            if head < HEADS:
                sent[head, 0:HD, :] = turned(raw, q_gain[...], q_ref, q_scale, head)
                continue
            head -= HEADS
            if head < KV_HEADS:
                value, row = turned(raw, k_gain[...], k_ref, k_scale, head), HD
            else:
                value, row, head = raw.astype(bf16), 2 * HD, head - KV_HEADS
            for copy in range(per_group):
                sent[head * per_group + copy, row : row + HD, :] = value


def project(here, x, gain, own, pieces, q_gain, k_gain, cosine, sine):
    tokens, width = x.shape
    f32, bf16 = jnp.float32, jnp.bfloat16
    shape = jax.ShapeDtypeStruct
    arrays = [x, gain, own, *pieces, q_gain, k_gain, cosine, sine]
    outs = [
        shape((HEADS, 3 * HD, tokens), bf16),
        shape((width, own.shape[1]), bf16),
        shape((HEADS * HD, tokens), f32),
        shape((KV_HEADS * HD, tokens), f32),
        shape((HEADS, tokens), f32),
        shape((KV_HEADS, tokens), f32),
        shape((width, tokens), bf16),
        shape((tokens, 1), f32),
    ]
    return call_with_here(
        project_kernel, here, (1,), arrays, [whole(a) for a in arrays], outs,
        [whole(o) for o in outs], micros=PROJECT,
    )


def layer(array, index):
    return pl.BlockSpec((1, *array.shape[1:]), lambda i, here: (index, 0, 0))


def attend_out_kernel(here, *refs):
    attn_ref, x_ref, gain_ref, own_ref = refs[:4]
    pieces = refs[4:20]
    weight, h_ref, scale_ref, two_ref, two_t_ref = refs[20:]
    core, y, side = here[1], here[2], here[3]
    rows = own_ref.shape[0]
    part = rows // 4
    weight[pl.ds(pl.multiple_of(side * rows, rows), rows), :] = own_ref[...]
    for p in range(4):
        at = (1 - side) * rows + (((p % 2) ^ core) * 2 + ((p // 2) ^ y)) * part
        for n in range(4):
            piece = pieces[4 * p + n]
            wide = piece.shape[1]
            weight[pl.ds(pl.multiple_of(at, part), part), n * wide : (n + 1) * wide] = piece[...]
    attn = attn_ref[...].T
    h_one = x_ref[...].astype(jnp.float32) + jnp.dot(
        attn, weight[...], preferred_element_type=jnp.float32
    )
    scale = rms_scale(h_one)
    h_ref[...] = h_one
    scale_ref[...] = scale
    two = (h_one * scale * gain_ref[...]).astype(jnp.bfloat16)
    two_ref[...] = two
    two_t_ref[...] = two.T


def attend_out(here, attn, x, gain, own, pieces):
    tokens, width = x.shape
    f32, bf16 = jnp.float32, jnp.bfloat16
    shape = jax.ShapeDtypeStruct
    part = own.shape[0] // 4
    cuts = 4
    part_width = width // cuts
    first = pieces[0].shape[1] // part_width - cuts
    arrays = [attn, x, gain, own]
    specs = [whole(a) for a in arrays]
    for piece in pieces:
        for n in range(cuts):
            arrays.append(piece)
            specs.append(pl.BlockSpec((part, part_width), lambda i, here, n=n: (0, first + n)))
    outs = [
        shape((width, width), bf16),
        shape((tokens, width), f32),
        shape((tokens, 1), f32),
        shape((tokens, width), bf16),
        shape((width, tokens), bf16),
    ]
    return call_with_here(
        attend_out_kernel, here, (1,), arrays, specs, outs, [whole(o) for o in outs], micros=OUT
    )


def ffn_kernel(chunk, here, *refs):
    two_ref, d_ref, own_ref = refs[:3]
    pieces, down_ref, down_pieces = (refs[3:7], refs[7:11]), refs[11], refs[12:16]
    refs = refs[4:]
    if chunk == 0:
        before_refs, refs = refs[12:13], refs[13:]
        near, far, give, give_far, out_ref, d_two_ref = refs[:6]
        refs = refs[6:]
    else:
        before_refs, gain_ref, refs = refs[12:17], refs[17], refs[18:]
        near, far, give, give_far = refs[:4]
        out_ref, d_h_ref, d_attn_ref, heads_ref, gain_term_ref = refs[4:9]
        refs = refs[9:]
    weight, down, hidden_rows, out_sum, two_sum = refs[:5]
    held, weight_sem, down_sem, before_sem = refs[5:-3], refs[-3], refs[-2], refs[-1]
    core, y, side = here[1], here[2], here[3]
    f32, bf16 = jnp.float32, jnp.bfloat16
    own_rows, columns = own_ref.shape[1], own_ref.shape[2] // CHUNKS
    part = own_rows // 4
    tile = columns // FFN_TILES
    half = columns // 2

    def quarter(p):
        return ((p % 2) ^ core) * 2 + ((p // 2) ^ y)

    def copies(n):
        at = slice(n * tile, (n + 1) * tile)
        mine = pl.ds(pl.multiple_of(side * own_rows, own_rows), own_rows)
        found = [
            pltpu.make_async_copy(
                own_ref.at[:, :, chunk * columns + n * tile : chunk * columns + (n + 1) * tile],
                weight.at[:, mine, at],
                weight_sem.at[n, 0],
            )
        ]
        for p in range(4):
            rows = pl.ds(pl.multiple_of((1 - side) * own_rows + quarter(p) * part, part), part)
            for kind in range(2):
                begin = n * tile + (columns if kind == 1 and chunk == 1 else 0)
                found.append(
                    pltpu.make_async_copy(
                        pieces[kind][p].at[:, begin : begin + tile],
                        weight.at[kind, rows, at],
                        weight_sem.at[n, 1 + 2 * p + kind],
                    )
                )
        return found

    def own_down(n):
        at = slice(n * tile, (n + 1) * tile)
        return [pltpu.make_async_copy(down_ref.at[at, :], down.at[at, :], down_sem.at[n, 0])]

    def other_down(n):
        at = slice(n * tile, (n + 1) * tile)
        found = []
        for p in range(4):
            wide = down_pieces[p].shape[1]
            lanes = pl.ds(pl.multiple_of(quarter(p) * wide, wide), wide)
            found.append(
                pltpu.make_async_copy(
                    down_pieces[p].at[at, :], down.at[at, lanes], down_sem.at[n, p]
                )
            )
        return found

    def each(action, n):
        for copy in copies(n):
            action(copy)

        @pl.when(side == chunk)
        def _():
            for copy in own_down(n):
                action(copy)

        @pl.when(side != chunk)
        def _():
            for copy in other_down(n):
                action(copy)

    before = [
        pltpu.make_async_copy(ref, held[n], before_sem.at[n]) for n, ref in enumerate(before_refs)
    ]
    for n in range(FFN_TILES):
        each(lambda copy: copy.start(), n)
    for copy in before:
        copy.start()
    two = two_ref[...]
    d_ffn = d_ref[...]
    for n in range(FFN_TILES):
        each(lambda copy: copy.wait(), n)
        at = slice(n * tile, (n + 1) * tile)
        gate = jnp.dot(two, weight[0, :, at], preferred_element_type=f32)
        upper = jnp.dot(two, weight[1, :, at], preferred_element_type=f32)
        d_hidden = contract(d_ffn, down[at, :], (1, 1))
        sigma = jax.nn.sigmoid(gate)
        silu = gate * sigma
        hidden = (silu * upper).astype(bf16)
        d_gate = (d_hidden * upper * sigma * (1.0 + gate * (1.0 - sigma))).astype(bf16)
        d_upper = (d_hidden * silu).astype(bf16)
        out_term = jnp.dot(hidden, down[at, :], preferred_element_type=f32)
        two_term = contract(d_gate, weight[0, :, at], (1, 1)) + contract(
            d_upper, weight[1, :, at], (1, 1)
        )
        out_sum[...] = out_term if n == 0 else out_sum[...] + out_term
        two_sum[...] = two_term if n == 0 else two_sum[...] + two_term
        hidden_rows[:, at] = hidden
        mine = jnp.where(core == 0, d_gate, d_upper)
        other = jnp.where(core == 0, d_upper, d_gate)
        for column in range(2):
            begin, end = max(n * tile, column * half), min((n + 1) * tile, (column + 1) * half)
            if begin >= end:
                continue
            source = slice(begin - n * tile, end - n * tile)
            target = slice(begin - column * half, end - column * half)
            first, second = mine[:, source], other[:, source]

            @pl.when(y == column)
            def _(first=first, second=second, target=target):
                near[:, target] = first
                give[:, target] = second

            @pl.when(y != column)
            def _(first=first, second=second, target=target):
                far[:, target] = first
                give_far[:, target] = second

    share = half // 2
    target = slice(half, half + share)
    for owner in range(2):
        lower = hidden_rows[:, owner * half : owner * half + share]
        upper = hidden_rows[:, owner * half + share : (owner + 1) * half]
        close = jnp.where(y == 0, lower, upper)
        distant = jnp.where(y == 0, upper, lower)

        @pl.when(core == owner)
        def _(close=close, distant=distant):
            near[:, target] = close
            far[:, target] = distant

        @pl.when(core != owner)
        def _(close=close, distant=distant):
            give[:, target] = close
            give_far[:, target] = distant

    for copy in before:
        copy.wait()
    if chunk == 0:
        out_ref[...] = held[0][...] + out_sum[...]
        d_two_ref[...] = two_sum[...]
    else:
        out_before, two_before, h_one, scale, w_out = held
        out_ref[...] = (out_before[...] + out_sum[...]).astype(bf16)
        d_norm, gain_term = norm_back(
            two_before[...] + two_sum[...], h_one[...], scale[...], gain_ref[...]
        )
        gain_term_ref[...] = jnp.sum(gain_term, axis=0, keepdims=True)
        d_h_one = d_ffn.astype(f32) + d_norm
        d_h_ref[...] = d_h_one
        d_attn = d_h_one.astype(bf16)
        d_attn_ref[...] = d_attn
        heads_ref[...] = contract(w_out[...], d_attn, (1, 1)).astype(bf16)


FFN_TILES = 3


def ffn(here, chunk, two, d_ffn, own, pieces, down, down_pieces, before, gain=None):
    tokens, width = two.shape
    columns = own.shape[2] // CHUNKS
    padded = (columns // 2 + columns // 4 + BLK - 1) // BLK * BLK
    shape = jax.ShapeDtypeStruct
    f32, bf16 = jnp.float32, jnp.bfloat16
    outs = [shape((tokens, padded), bf16)] * 4
    if chunk == 0:
        outs += [shape((tokens, width), f32)] * 2
    else:
        outs += [
            shape((tokens, width), bf16),
            shape((tokens, width), f32),
            shape((tokens, width), bf16),
            shape((width, tokens), bf16),
            shape((1, width), f32),
        ]
    far_away = pl.BlockSpec(memory_space=pl.ANY)
    arrays = [two, d_ffn, own, *pieces[0], *pieces[1], down, *down_pieces, *before]
    specs = [whole(two), whole(d_ffn)] + [far_away] * (len(arrays) - 2)
    if gain is not None:
        arrays.append(gain)
        specs.append(whole(gain))
    got = call_with_here(
        functools.partial(ffn_kernel, chunk),
        here,
        (1,),
        arrays,
        specs,
        outs,
        [whole(o) for o in outs],
        [
            pltpu.VMEM((2, width, columns), bf16),
            pltpu.VMEM((columns, width), bf16),
            pltpu.VMEM((tokens, columns), bf16),
            pltpu.VMEM((tokens, width), f32),
            pltpu.VMEM((tokens, width), f32),
        ]
        + [pltpu.VMEM(v.shape, v.dtype) for v in before]
        + [
            pltpu.SemaphoreType.DMA((FFN_TILES, 9)),
            pltpu.SemaphoreType.DMA((FFN_TILES, 4)),
            pltpu.SemaphoreType.DMA((len(before),)),
        ],
        micros=FFN[chunk],
    )
    return got[:4], got[4:]


def wide_product_kernel(here, *refs):
    planes, terms = refs[:4], refs[4:8]
    sent, kept, left, right = refs[8:]
    tokens = planes[0].shape[1]
    columns = right.shape[1]
    for i in range(4):
        left[:, i * tokens : (i + 1) * tokens] = planes[i][...]
        right[i * tokens : (i + 1) * tokens, :] = terms[i][:, :columns]
    side = here[3]
    _, step, _ = kept.shape
    for half in range(2):
        for owner, out_ref in ((1 - side, sent), (side, kept)):
            place = pl.multiple_of(owner * 2 * step + half * step, step)
            out_ref[half] = jnp.dot(
                left[pl.ds(place, step), :], right[...], preferred_element_type=jnp.float32
            ).astype(out_ref.dtype)


def wide_products(here, two_plane, shares, columns):
    rows, tokens = two_plane[0].shape
    outs = [
        jax.ShapeDtypeStruct((2, rows // 4, columns), jnp.bfloat16),
        jax.ShapeDtypeStruct((2, rows // 4, columns), jnp.float32),
    ]
    arrays = [*two_plane, *shares]
    return call_with_here(
        wide_product_kernel,
        here,
        (1,),
        arrays,
        [whole(a) for a in two_plane]
        + [pl.BlockSpec((tokens, columns), lambda i, here: (0, 0))] * 4,
        outs,
        [whole(o) for o in outs],
        [
            pltpu.VMEM((rows, 4 * tokens), jnp.bfloat16),
            pltpu.VMEM((4 * tokens, columns), jnp.bfloat16),
        ],
        micros=3,
    )


def down_product_kernel(here, *refs):
    planes, terms = refs[:4], (refs[4:8], refs[8:12])
    sent, kept, left, right = refs[12:]
    tokens = planes[0].shape[0]
    rows = left.shape[0]
    for i in range(4):
        right[i * tokens : (i + 1) * tokens, :] = planes[i][...]
    for chunk in range(2):
        for i in range(4):
            share = terms[chunk][i]
            at = share.shape[1] // BLK * BLK - (rows + BLK - 1) // BLK * BLK
            left[:, i * tokens : (i + 1) * tokens] = share[:, at : at + rows].T
        for half in range(2):
            product = jnp.dot(
                left[half * rows // 2 : (half + 1) * rows // 2, :],
                right[...],
                preferred_element_type=jnp.float32,
            )

            @pl.when(here[3] == chunk)
            def _(product=product, half=half):
                kept[half] = product

            @pl.when(here[3] != chunk)
            def _(product=product, half=half):
                sent[half] = product.astype(sent.dtype)


def down_products(here, d_plane, first, second, rows):
    tokens, columns = d_plane[0].shape
    outs = [
        jax.ShapeDtypeStruct((2, rows // 2, columns), jnp.bfloat16),
        jax.ShapeDtypeStruct((2, rows // 2, columns), jnp.float32),
    ]
    return call_with_here(
        down_product_kernel,
        here,
        (1,),
        [*d_plane, *first, *second],
        [whole(a) for a in (*d_plane, *first, *second)],
        outs,
        [whole(o) for o in outs],
        [
            pltpu.VMEM((rows, 4 * tokens), jnp.bfloat16),
            pltpu.VMEM((4 * tokens, columns), jnp.bfloat16),
        ],
        micros=3,
    )


GAIN_ROWS = 16


def attention_back_kernel(here, *refs):
    d_ref, q_ref, k_ref, q_scale, k_scale, q_gain, k_gain, cos_ref, sin_ref = refs[:9]
    weight, x_ref, scale_ref, gain_ref, d_h_ref, d_attn_ref = refs[9:15]
    near, far, give, give_far, d_x_ref, gains_ref = refs[15:21]
    turned, natural = refs[21:]
    f32, bf16 = jnp.float32, jnp.bfloat16
    core, y = here[1], here[2]
    cosine, sine = cos_ref[...], sin_ref[...]
    half = HD // 2
    per_group = HEADS // KV_HEADS
    tokens = x_ref.shape[0]

    def back(grad, raw, scale, gain):
        first, second = grad[:half], grad[half:]
        normed = jnp.concatenate(
            [first * cosine + second * sine, second * cosine - first * sine], axis=0
        )
        return norm_back(normed, raw, scale, gain, 0)

    q_term = jnp.zeros((HD, tokens), f32)
    k_term = jnp.zeros((HD, tokens), f32)
    for head in range(HEADS):
        at = slice(head * HD, (head + 1) * HD)
        grad, term = back(
            d_ref[head, :HD, :].astype(f32), q_ref[at, :], q_scale[head : head + 1, :], q_gain[...]
        )
        turned[at, :] = grad.astype(bf16)
        q_term = q_term + term
    for head in range(KV_HEADS):
        at = slice(head * HD, (head + 1) * HD)
        both = d_ref[head * per_group, HD:, :].astype(f32)
        for other in range(1, per_group):
            both = both + d_ref[head * per_group + other, HD:, :].astype(f32)
        grad, term = back(both[:HD], k_ref[at, :], k_scale[head : head + 1, :], k_gain[...])
        place = HEADS * HD + head * HD
        turned[place : place + HD, :] = grad.astype(bf16)
        k_term = k_term + term
        place += KV_HEADS * HD
        turned[place : place + HD, :] = both[HD:].astype(bf16)
    rows = turned.shape[0] // 4
    columns = d_attn_ref.shape[1] // 4
    shares = ((near, core, y), (far, core, 1 - y), (give, 1 - core, y), (give_far, 1 - core, 1 - y))
    for out_ref, to_core, to_y in shares:
        share = to_core * 2 + to_y
        out_ref[:rows, :] = turned[pl.ds(pl.multiple_of(share * rows, rows), rows), :]
        out_ref[rows:, :] = d_attn_ref[:, pl.ds(pl.multiple_of(share * columns, columns), columns)]
    for at in range(0, turned.shape[0], 256):
        natural[:, at : at + 256] = turned[at : at + 256, :].T
    d_normed = contract(natural[...], weight[...], (1, 1))
    x = x_ref[...].astype(f32)
    d_norm, gain_term = norm_back(d_normed, x, scale_ref[...], gain_ref[...])
    d_x_ref[...] = d_h_ref[...] + d_norm
    gains_ref[...] = jnp.zeros_like(gains_ref)
    gains_ref[0:1, :] = jnp.sum(gain_term, axis=0, keepdims=True)
    gains_ref[1:2, 0:HD] = jnp.sum(q_term.T, axis=0, keepdims=True)
    gains_ref[2:3, 0:HD] = jnp.sum(k_term.T, axis=0, keepdims=True)


def attention_back(here, arrays):
    f32, bf16 = jnp.float32, jnp.bfloat16
    shape = jax.ShapeDtypeStruct
    weight, x = arrays[9], arrays[10]
    tokens, width = x.shape
    rows = weight.shape[1] // 4 + tokens
    assert width // 4 == tokens
    outs = [
        *[shape((rows, tokens), bf16)] * 4,
        shape((tokens, width), f32),
        shape((8, width), f32),
    ]
    return call_with_here(
        attention_back_kernel, here, (1,), arrays, [whole(a) for a in arrays], outs,
        [whole(o) for o in outs],
        [pltpu.VMEM((weight.shape[1], tokens), bf16), pltpu.VMEM((tokens, weight.shape[1]), bf16)],
        micros=0,
    )


def attention_product_kernel(here, *refs):
    planes, terms, gains_ref, ffn_gain_ref = refs[:4], refs[4:8], refs[8], refs[9]
    sent, kept, left, right, left_out, right_out = refs[10:]
    tokens = planes[0].shape[2]
    cut = right.shape[1]
    for i in range(4):
        at = slice(i * tokens, (i + 1) * tokens)
        left[:, at] = planes[i][0]
        left_out[:, at] = planes[i][1]
        share = terms[i]
        right[at, :] = share[:cut].T
        right_out[at, :] = share[cut:]
    step = left.shape[0] // 4
    for owner, out_ref in ((1 - here[3], sent), (here[3], kept)):
        for half in range(2):
            at = pl.ds(pl.multiple_of(owner * 2 * step + half * step, step), step)
            out_ref[half, :step, :cut] = jnp.dot(
                left[at, :], right[...], preferred_element_type=jnp.float32
            ).astype(out_ref.dtype)
            out_ref[half, :step, cut:] = jnp.dot(
                left_out[at, :], right_out[...], preferred_element_type=jnp.float32
            ).astype(out_ref.dtype)
        rows = gains_ref.shape[1] // 2
        mine = pl.ds(pl.multiple_of(owner * rows, rows), rows)
        wide = out_ref.shape[2] - rows
        block = jnp.concatenate(
            [
                jnp.concatenate([gains_ref[0:1, mine], gains_ref[1:2, 0:wide]], axis=1),
                jnp.concatenate([ffn_gain_ref[:, mine], gains_ref[2:3, 0:wide]], axis=1),
                jnp.zeros((GAIN_ROWS - 2, out_ref.shape[2]), jnp.float32),
            ],
            axis=0,
        )
        out_ref[0, step:, :] = block.astype(out_ref.dtype)
        out_ref[1, step:, :] = jnp.zeros((GAIN_ROWS, out_ref.shape[2]), out_ref.dtype)


def attention_products(here, pair_plane, shares, gains, ffn_gain):
    _, width, tokens = pair_plane[0].shape
    cut = shares[0].shape[0] - tokens
    shape = (2, width // 4 + GAIN_ROWS, cut + tokens)
    outs = [jax.ShapeDtypeStruct(shape, jnp.bfloat16), jax.ShapeDtypeStruct(shape, jnp.float32)]
    return call_with_here(
        attention_product_kernel,
        here,
        (1,),
        [*pair_plane, *shares, gains, ffn_gain],
        [whole(a) for a in (*pair_plane, *shares, gains, ffn_gain)],
        outs,
        [whole(o) for o in outs],
        [
            pltpu.VMEM((width, 4 * tokens), jnp.bfloat16),
            pltpu.VMEM((4 * tokens, cut), jnp.bfloat16),
            pltpu.VMEM((width, 4 * tokens), jnp.bfloat16),
            pltpu.VMEM((4 * tokens, tokens), jnp.bfloat16),
        ],
        micros=3,
    )


def place_gate_up_kernel(here, *refs):
    mine, across, beside, diagonal, out_ref = *refs[:4], refs[-1]
    pieces = (mine, across, beside, diagonal)
    wide = mine.shape[2]
    for case in range(4):
        core, y = case // 2, case % 2

        @pl.when((here[1] == core) & (here[2] == y))
        def _(core=core, y=y):
            for kind in range(2):
                for column in range(2):
                    value = pieces[(y ^ column) * 2 + (core ^ kind)][0]
                    out_ref[:, kind, column * wide : (column + 1) * wide] = value.astype(
                        jnp.float32
                    )


def place_gate_up(here, chunk, pieces, before):
    _, rows, wide = pieces[0].shape
    step = 64
    blocks = rows // step

    def source(i, here):
        return ((i // blocks) ^ here[0], i % blocks, 0)

    arrays = list(pieces)
    specs = [pl.BlockSpec((1, step, wide), source)] * 4
    aliases = {}
    if before is not None:
        arrays.append(before)
        specs.append(pl.BlockSpec(memory_space=pl.ANY))
        aliases = {5: 0}
    (out,) = call_with_here(
        place_gate_up_kernel,
        here,
        (2 * blocks,),
        arrays,
        specs,
        [jax.ShapeDtypeStruct((2 * rows, 2, 2 * wide * CHUNKS), jnp.float32)],
        [pl.BlockSpec((step, 2, 2 * wide), lambda i, here: (i, 0, chunk))],
        aliases=aliases,
        micros=0,
    )
    return out


def half_by_step(array, number):
    return pl.BlockSpec(
        (1, *array.shape[1:]), lambda s, here: (jnp.where(s > number, 1, 0), 0, 0)
    )


def place_down(here, pieces):
    _, rows, columns = pieces[0].shape

    def kernel(here, *refs):
        for s in range(8):

            @pl.when(pl.program_id(0) == s)
            def _(s=s):
                refs[4][...] = refs[s % 4][0].astype(jnp.float32)

    def target(s, here):
        half = (s // 4) ^ here[0]
        y = ((s // 2) % 2) ^ here[2]
        core = (s % 2) ^ here[1]
        return ((core * 2 + y) * 2 + half, 0)

    (out,) = call_with_here(
        kernel,
        here,
        (8,),
        list(pieces),
        [half_by_step(v, a) for a, v in enumerate(pieces)],
        [jax.ShapeDtypeStruct((rows * 8, columns), jnp.float32)],
        [pl.BlockSpec((rows, columns), target)],
    )
    return out


def place_attention(here, pieces, cut):
    _, rows, columns = pieces[0].shape
    rows -= GAIN_ROWS

    def kernel(here, *refs):
        qkv_ref, out_ref, gains_ref = refs[4:]
        for s in range(8):

            @pl.when(pl.program_id(0) == s)
            def _(s=s):
                value = refs[s % 4][0]
                qkv_ref[...] = value[:rows, :cut].astype(jnp.float32)
                out_ref[...] = value[:rows, cut:].astype(jnp.float32)
                gains = value[rows:].astype(jnp.float32)
                gains_ref[...] = gains if s == 0 else gains_ref[...] + gains

    def target(s, here):
        half = (s // 4) ^ here[0]
        return (half, ((s % 2) ^ here[1]) * 2 + (((s // 2) % 2) ^ here[2]))

    shape = jax.ShapeDtypeStruct
    f32 = jnp.float32
    gain_shape = (GAIN_ROWS, columns)
    return call_with_here(
        kernel,
        here,
        (8,),
        list(pieces),
        [half_by_step(v, a) for a, v in enumerate(pieces)],
        [
            shape((2 * rows, 4 * cut), f32),
            shape((2 * rows, 4 * (columns - cut)), f32),
            shape(gain_shape, f32),
        ],
        [
            pl.BlockSpec((rows, cut), target),
            pl.BlockSpec((rows, columns - cut), target),
            pl.BlockSpec(gain_shape, lambda s, here: (0, 0)),
        ],
    )


def on_block(
    tokens,
    qkv_weight,
    out_weight,
    gate_up_weight,
    down_weight,
    attn_gain,
    ffn_gain,
    query_gain,
    key_gain,
    seq_lengths,
    block_order,
    cotangent,
):
    inputs = tokens[0].astype(jnp.float32)
    rows_here = inputs.shape[0]
    ctx_size = lax.axis_size("ctx")
    ctx_index = lax.axis_index("ctx")
    per_group = HEADS // KV_HEADS
    q_width = HEADS * HD
    kv_width = KV_HEADS * HD
    order_row = block_order[0]
    lengths_row = seq_lengths[0]
    slots = jnp.arange(rows_here, dtype=jnp.int32) // BLK + ctx_index * (rows_here // BLK)
    table = slots[:, None] == jnp.arange(order_row.shape[0], dtype=jnp.int32)[None, :]
    packed = (
        jnp.sum(jnp.where(table, order_row[None, :], 0), axis=1) * BLK
        + jnp.arange(rows_here, dtype=jnp.int32) % BLK
    )
    local = packed - starts_of(packed, lengths_row)
    frequency = ROPE_BASE ** (-2.0 * jnp.arange(HD // 2, dtype=jnp.float32) / HD)
    angle = frequency[:, None] * local.astype(jnp.float32)[None, :]
    cosine = jnp.cos(angle)[None]
    sine = jnp.sin(angle)[None]
    bf16, f32 = jnp.bfloat16, jnp.float32
    parts = ctx_size // HEADS
    part = ctx_index // HEADS
    part_blocks = HEADS * rows_here // BLK
    q_order = lax.dynamic_slice_in_dim(order_row, part * part_blocks, part_blocks)
    q_slot, q_place, q_start = block_tables(q_order, lengths_row)
    q_slot = q_slot + part * part_blocks
    kv_slot, _, _ = block_tables(order_row, lengths_row)
    first = jnp.min(q_start.reshape(-1, TILE), axis=1) // TILE
    last = jnp.max(q_place.reshape(-1, TILE), axis=1) // TILE + 1
    tables = (q_slot, kv_slot, first, last)
    q_rows, kv_rows = part_blocks * BLK, order_row.shape[0] * BLK

    links = Links(ctx_size)
    here = links.here
    width = inputs.shape[1]
    rows = qkv_weight.shape[0]
    part_rows = rows // 4

    def quarter_rows(weight):
        return lax.dynamic_slice_in_dim(weight, links.quarter * part_rows, part_rows)

    qkv_piece = quarter_rows(qkv_weight)
    gains_here = jnp.concatenate([after(attn_gain, qkv_piece), ffn_gain, query_gain, key_gain])
    gains_there = links.over_x(gains_here)

    def gain_of(at, size):
        mine, other = gains_here[at : at + size], gains_there[at : at + size]
        return jnp.where(
            links.side == 0, jnp.concatenate([mine, other]), jnp.concatenate([other, mine])
        ).astype(f32)

    gain_attn = gain_of(0, rows)
    gain_ffn = gain_of(rows, rows)
    gain_query = gain_of(2 * rows, HD // 2)
    gain_key = gain_of(2 * rows + HD // 2, HD // 2)
    ff_chunk = gate_up_weight.shape[2] // CHUNKS

    def gate_up_piece(chunk):
        piece = lax.dynamic_slice(
            gate_up_weight,
            (links.quarter * part_rows, 0, chunk * ff_chunk),
            (part_rows, 2, ff_chunk),
        )
        return [piece[:, 0], piece[:, 1]]

    d_ffn = cotangent[0]
    d_beside = links.over_y(d_ffn)
    qkv_there = after(links.over_x(qkv_piece), d_beside)
    first_piece, first_up = gate_up_piece(0)
    up_piece = jnp.concatenate([first_up, quarter_rows(out_weight)], axis=1)
    second_piece = jnp.concatenate(gate_up_piece(1), axis=1)
    down_piece = lax.dynamic_slice_in_dim(
        down_weight, links.quarter * (width // 4), width // 4, 1
    )
    d_ffn = cotangent[0]
    tokens_here = tokens[0]
    qkv_there = after(qkv_there, first_piece)
    first_there = links.over_x(after(first_piece, qkv_there))
    up_there = links.over_x(after(up_piece, first_there))
    gate_up = jnp.transpose(after(gate_up_weight, qkv_there), (1, 0, 2))
    qkv_beside = links.over_y(qkv_there)
    qkv_pieces = (
        qkv_there,
        links.over_core(qkv_there),
        qkv_beside,
        links.over_core(after(qkv_beside, gate_up)),
    )
    sent, w_qkv, q_raw, k_raw, q_scale, k_scale, normed, scale_one = project(
        here, after(tokens_here, first_there), gain_attn[None], qkv_weight, qkv_pieces,
        gain_query[:, None], gain_key[:, None], cosine[0], sine[0],
    )
    got = lax.all_to_all(sent, "ctx", 0, 0, tiled=True)
    up_there = after(up_there, sent)
    down_there = links.over_x(after(down_piece, up_there))
    first_beside = links.over_y(first_there)
    up_beside = links.over_y(up_there)
    q_place, q_start = q_place[None], q_start[None]
    shape = jax.ShapeDtypeStruct
    attn_sent, *held = kernel_call(
        attend_kernel,
        tables,
        (got, q_place, q_start),
        [
            shape((ctx_size, HD, rows_here), bf16),
            shape((q_rows, HD), bf16),
            shape((HD, q_rows), bf16),
            shape((kv_rows, HD), bf16),
            shape((HD, kv_rows), bf16),
            shape((kv_rows, HD), bf16),
            shape((HD, q_rows), f32),
            shape((1, q_rows), f32),
        ],
        [pltpu.VMEM((HD, kv_rows), bf16)],
        ATTEND,
    )
    attn_sent = after(attn_sent, first_beside)
    attn_in = lax.dynamic_slice_in_dim(
        lax.all_to_all(attn_sent, "ctx", 0, 0, tiled=True), part * HEADS, HEADS
    ).reshape(q_width, rows_here)
    down_there = after(down_there, attn_sent)
    second_there = links.over_x(after(second_piece, down_there))
    down_beside = links.over_y(down_there)

    def spread(there, beside, time):
        there, beside = after(there, time), after(beside, time)
        return (there, links.over_core(there), beside, links.over_core(beside))

    first_pieces = spread(first_there, first_beside, attn_in)
    up_pieces = spread(up_there, up_beside, attn_sent)
    down_pieces = spread(down_there, down_beside, attn_in)
    second_beside = links.over_y(second_there)
    w_out, h_one, scale_two, two, two_t = attend_out(
        here, attn_in, tokens_here, gain_ffn[None], out_weight, up_pieces
    )
    two_beside = links.over_y(two_t)
    dealt_here, (out_sum, two_sum) = ffn(
        here, 0, two, d_ffn, gate_up, (first_pieces, up_pieces), down_weight, down_pieces, [h_one]
    )
    second_beside = after(second_beside, out_sum)
    second_pieces = (
        second_there, links.over_core(second_there), second_beside, links.over_core(second_beside)
    )
    near, far, give, give_far = dealt_here
    got_far = links.over_core(give_far)
    first_shares = (near, links.over_core(give), links.over_y(far), links.over_y(got_far))
    out_sum = after(out_sum, got_far)
    dealt_here, (output, d_h_one, d_attn, d_heads, ffn_gain_term) = ffn(
        here, 1, two, d_ffn, gate_up, (second_pieces, second_pieces), down_weight, down_pieces,
        [out_sum, two_sum, h_one, scale_two, w_out], gain_ffn[None],
    )
    second_shares = links.deal_plane(*dealt_here)

    def plane(value, beside, time):
        value, beside = after(value, time), after(beside, time)
        return (value, links.over_core(value), beside, links.over_core(beside))

    columns = ff_chunk // 2
    d_heads = d_heads.reshape(HEADS, HD, rows_here)
    d_got = lax.all_to_all(d_heads, "ctx", 0, 0, tiled=True)
    pair = jnp.stack([after(normed, d_heads), attn_in])
    two_plane = plane(two_t, two_beside, pair)
    first_products = wide_products(
        here, two_plane, [after(v, d_heads) for v in first_shares], columns
    )
    pair_across = links.over_core(pair)
    d_got = after(d_got, first_products[0], pair_across)
    (d_sent,) = kernel_call(
        attend_back_kernel,
        tables,
        (d_got, q_place, q_start, *held),
        [shape((ctx_size, 3 * HD, rows_here), bf16)],
        [
            pltpu.VMEM((HD, q_rows), bf16),
            pltpu.VMEM((q_rows, HD), bf16),
            pltpu.VMEM((kv_rows, HD), f32),
            pltpu.VMEM((kv_rows, HD), f32),
        ],
        ATTEND_BACK,
    )
    first_got = links.over_x(first_products[0])
    d_sent = after(d_sent, first_got, *second_shares[2:])
    d_back = lax.all_to_all(d_sent, "ctx", 0, 0, tiled=True)
    d_plane = plane(d_ffn, d_beside, d_sent)
    second_products = wide_products(
        here, two_plane, [after(v, d_plane[1]) for v in second_shares], columns
    )
    down_terms = down_products(
        here, d_plane, first_shares, second_shares, columns // 2
    )
    second_got = links.over_x(after(second_products[0], first_got))
    pair_beside = links.over_y(after(pair, d_sent))
    d_back = after(d_back, down_terms[0], pair_beside, second_got)
    *d_shares, d_inputs, gain_sums = attention_back(
        here,
        [
            d_back, q_raw, k_raw, q_scale, k_scale, gain_query[:, None], gain_key[:, None],
            cosine[0], sine[0], w_qkv, tokens_here, scale_one, gain_attn[None], d_h_one, d_attn,
        ],
    )
    down_got = links.over_x(after(down_terms[0], second_got))
    near, far, give, give_far = d_shares
    got, got_far = links.over_core(give), links.over_core(give_far)
    attention_shares = (near, got, links.over_y(far), links.over_y(got_far))
    pair_plane = (pair, pair_across, pair_beside, links.over_core(after(pair_beside, d_sent)))

    kept = [first_products[1], second_products[1], down_terms[1], None]
    got = [first_got, second_got, down_got, None]
    given, part, across, full, back, beside = ([None] * 4 for _ in range(6))

    def give_half(n):
        given[n] = links.over_z(links.half_of(kept[n], got[n], False))

    def sum_part(n, time):
        part[n] = add(links.half_of(kept[n], got[n], True), after(given[n], time))
        across[n] = links.over_two_z(part[n])

    def sum_full(n, time):
        full[n] = add(part[n], after(across[n], time))
        back[n] = links.over_z(full[n])

    def spread_y(n, time):
        full[n] = jnp.stack([full[n], after(back[n], time)])
        beside[n] = links.over_y(full[n])

    def spread_core(n, time):
        beside[n] = after(beside[n], time)
        return (full[n], links.over_core(full[n]), beside[n], links.over_core(beside[n]))

    give_half(0)
    given[0] = after(given[0], down_terms[0])
    sum_part(0, second_got)
    give_half(1)
    sum_part(1, got_far)
    got[2] = after(got[2], part[1], attention_shares[1], pair_plane[3])
    give_half(2)
    sum_full(0, got[2])
    attention_shares = (*attention_shares[:2], *(after(v, full[0]) for v in attention_shares[2:]))
    attention_terms = attention_products(
        here, pair_plane, attention_shares, gain_sums, ffn_gain_term
    )
    kept[3] = attention_terms[1]
    attention_got = links.over_x(attention_terms[0])
    spread_y(0, attention_terms[0])
    sum_part(2, full[0])
    sum_full(1, part[2])
    got[3] = after(attention_got, full[1])
    give_half(3)
    first_pieces = spread_core(0, got[3])
    spread_y(1, beside[0])
    sum_part(3, full[1])
    sum_full(2, part[3])
    first_placed = place_gate_up(here, 0, first_pieces, None)
    second_pieces = spread_core(1, full[2])
    spread_y(2, (first_placed, beside[1]))
    sum_full(3, full[2])
    grad_gate_up = place_gate_up(here, 1, second_pieces, first_placed)
    spread_y(3, full[2])
    grad_down = place_down(here, spread_core(2, grad_gate_up))
    cut = qkv_weight.shape[1] // 4
    last_pieces = spread_core(3, grad_gate_up)
    last_pieces = (*last_pieces[:3], after(last_pieces[3], grad_down))
    grad_qkv, grad_out, gain_sums = place_attention(here, last_pieces, cut)
    at = links.side * (HD // 2)
    gain_grads = [
        gain_sums[0, :rows],
        gain_sums[1, :rows],
        lax.dynamic_slice_in_dim(gain_sums[0, rows : rows + HD], at, HD // 2),
        lax.dynamic_slice_in_dim(gain_sums[1, rows : rows + HD], at, HD // 2),
    ]
    return (
        output[None],
        d_inputs[None],
        grad_qkv,
        grad_out,
        grad_gate_up,
        grad_down,
        *gain_grads,
    )


def on_device(
    tokens,
    qkv_weight,
    out_weight,
    gate_up_weight,
    down_weight,
    attn_gain,
    ffn_gain,
    query_gain,
    key_gain,
    seq_lengths,
    block_order,
    cotangent,
):
    inputs = tokens[0].astype(jnp.float32)
    rows_here = inputs.shape[0]
    ctx_size = lax.axis_size("ctx")
    ctx_index = lax.axis_index("ctx")
    per_group = HEADS // KV_HEADS
    q_width = HEADS * HD
    kv_width = KV_HEADS * HD
    order_row = block_order[0]
    lengths_row = seq_lengths[0]
    slots = jnp.arange(rows_here, dtype=jnp.int32) // BLK + ctx_index * (rows_here // BLK)
    table = slots[:, None] == jnp.arange(order_row.shape[0], dtype=jnp.int32)[None, :]
    packed = (
        jnp.sum(jnp.where(table, order_row[None, :], 0), axis=1) * BLK
        + jnp.arange(rows_here, dtype=jnp.int32) % BLK
    )
    local = packed - starts_of(packed, lengths_row)
    frequency = ROPE_BASE ** (-2.0 * jnp.arange(HD // 2, dtype=jnp.float32) / HD)
    angle = frequency[:, None] * local.astype(jnp.float32)[None, :]
    cosine = jnp.cos(angle)[None]
    sine = jnp.sin(angle)[None]
    bf16, f32 = jnp.bfloat16, jnp.float32
    parts = ctx_size // HEADS
    part = ctx_index // HEADS
    part_blocks = HEADS * rows_here // BLK
    q_order = lax.dynamic_slice_in_dim(order_row, part * part_blocks, part_blocks)
    q_slot, q_place, q_start = block_tables(q_order, lengths_row)
    q_slot = q_slot + part * part_blocks
    kv_slot, _, _ = block_tables(order_row, lengths_row)
    first = jnp.min(q_start.reshape(-1, TILE), axis=1) // TILE
    last = jnp.max(q_place.reshape(-1, TILE), axis=1) // TILE + 1
    tables = (q_slot, kv_slot, first, last)
    q_rows, kv_rows = part_blocks * BLK, order_row.shape[0] * BLK

    def fetch_attention():
        return (
            lax.all_gather(qkv_weight, "fsdp", axis=0, tiled=True),
            lax.all_gather(out_weight, "fsdp", axis=0, tiled=True),
            lax.all_gather(attn_gain, "fsdp", axis=0, tiled=True),
            lax.all_gather(ffn_gain, "fsdp", axis=0, tiled=True),
            lax.all_gather(query_gain, "fsdp", axis=0, tiled=True),
            lax.all_gather(key_gain, "fsdp", axis=0, tiled=True),
        )

    w_qkv, w_out, gain_attn, gain_ffn, gain_query, gain_key = fetch_attention()
    gain_attn = gain_attn.astype(jnp.float32)
    gain_ffn = gain_ffn.astype(jnp.float32)
    gain_query = gain_query.astype(jnp.float32)
    gain_key = gain_key.astype(jnp.float32)
    scale_one = rms_scale(inputs)
    normed = (inputs * scale_one * gain_attn).astype(jnp.bfloat16)
    projected = lax.dot_general(
        w_qkv, normed, (((0,), (1,)), ((), ())), preferred_element_type=f32
    )
    q_raw = projected[:q_width].reshape(HEADS, HD, rows_here)
    k_raw = projected[q_width : q_width + kv_width].reshape(KV_HEADS, HD, rows_here)
    values_here = projected[q_width + kv_width :].reshape(KV_HEADS, HD, rows_here).astype(bf16)
    q_scale = rms_scale(q_raw, 1)
    k_scale = rms_scale(k_raw, 1)
    column_query, column_key = gain_query[:, None], gain_key[:, None]
    queries = rope(q_raw * q_scale * column_query, cosine, sine).astype(bf16)
    keys_here = rope(k_raw * k_scale * column_key, cosine, sine).astype(bf16)
    sent = jnp.concatenate(
        [queries, jnp.repeat(keys_here, per_group, 0), jnp.repeat(values_here, per_group, 0)], axis=1
    )
    sent = jnp.concatenate([sent] * parts, axis=0)
    got = lax.all_to_all(sent, "ctx", 0, 0, tiled=True)
    q_place, q_start = q_place[None], q_start[None]
    shape = jax.ShapeDtypeStruct
    attn_sent, *held = kernel_call(
        attend_kernel,
        tables,
        (got, q_place, q_start),
        [
            shape((ctx_size, HD, rows_here), bf16),
            shape((q_rows, HD), bf16),
            shape((HD, q_rows), bf16),
            shape((kv_rows, HD), bf16),
            shape((HD, kv_rows), bf16),
            shape((kv_rows, HD), bf16),
            shape((HD, q_rows), f32),
            shape((1, q_rows), f32),
        ],
        [pltpu.VMEM((HD, kv_rows), bf16)],
        ATTEND,
    )
    attn_in = lax.dynamic_slice_in_dim(
        lax.all_to_all(attn_sent, "ctx", 0, 0, tiled=True), part * HEADS, HEADS
    ).reshape(q_width, rows_here)
    h_one = inputs + lax.dot_general(
        attn_in, w_out, (((0,), (0,)), ((), ())), preferred_element_type=f32
    )
    scale_two = rms_scale(h_one)
    normed_two = (h_one * scale_two * gain_ffn).astype(jnp.bfloat16)
    columns = normed_two
    gate_up = jnp.einsum(
        "tr,rgf->tgf",
        columns,
        lax.all_gather(gate_up_weight, "fsdp", axis=0, tiled=True),
        preferred_element_type=jnp.float32,
    )
    gate = gate_up[:, 0]
    upper = gate_up[:, 1]
    sigma = jax.nn.sigmoid(gate)
    hidden = (gate * sigma * upper).astype(jnp.bfloat16)
    columns = hidden
    ffn_out = jnp.dot(
        columns,
        lax.all_gather(down_weight, "fsdp", axis=0, tiled=True),
        preferred_element_type=jnp.float32,
    )
    output = (h_one + ffn_out).astype(jnp.bfloat16)
    d_out = cotangent[0].astype(jnp.float32)
    d_ffn = d_out.astype(jnp.bfloat16)
    d_hidden = lax.dot_general(
        d_ffn,
        lax.all_gather(down_weight, "fsdp", axis=0, tiled=True),
        (((1,), (1,)), ((), ())),
        preferred_element_type=jnp.float32,
    )
    d_gate = d_hidden * upper * sigma * (1.0 + gate * (1.0 - sigma))
    d_upper = d_hidden * gate * sigma
    d_gate_up = jnp.stack([d_gate, d_upper], axis=1).astype(jnp.bfloat16)
    d_normed_two = jnp.einsum(
        "tgf,rgf->tr",
        d_gate_up,
        lax.all_gather(gate_up_weight, "fsdp", axis=0, tiled=True),
        preferred_element_type=jnp.float32,
    )
    columns = normed_two
    grad_gate_up = lax.psum_scatter(
        jnp.einsum("tr,tgf->rgf", columns, d_gate_up, preferred_element_type=jnp.float32).astype(
            jnp.bfloat16
        ),
        "fsdp",
        scatter_dimension=0,
        tiled=True,
    )
    columns = hidden
    grad_down = lax.psum_scatter(
        lax.dot_general(
            columns, d_ffn, (((0,), (0,)), ((), ())), preferred_element_type=jnp.float32
        ).astype(jnp.bfloat16),
        "fsdp",
        scatter_dimension=0,
        tiled=True,
    )
    d_norm_two, ffn_gain_term = norm_back(d_normed_two, h_one, scale_two, gain_ffn)
    d_h_one = d_out + d_norm_two
    d_attn = d_h_one.astype(jnp.bfloat16)
    grad_out_here = jnp.dot(attn_in, d_attn, preferred_element_type=f32)
    d_heads = lax.dot_general(
        w_out, d_attn, (((1,), (1,)), ((), ())), preferred_element_type=f32
    ).astype(bf16)
    d_heads = jnp.concatenate([d_heads.reshape(HEADS, HD, rows_here)] * parts, axis=0)
    d_got = lax.all_to_all(d_heads, "ctx", 0, 0, tiled=True)
    (d_sent,) = kernel_call(
        attend_back_kernel,
        tables,
        (d_got, q_place, q_start, *held),
        [shape((ctx_size, 3 * HD, rows_here), bf16)],
        [
            pltpu.VMEM((HD, q_rows), bf16),
            pltpu.VMEM((q_rows, HD), bf16),
            pltpu.VMEM((kv_rows, HD), f32),
            pltpu.VMEM((kv_rows, HD), f32),
        ],
        ATTEND_BACK,
    )
    d_back = lax.all_to_all(d_sent, "ctx", 0, 0, tiled=True)
    d_query = lax.dynamic_slice_in_dim(d_back[:, :HD], part * HEADS, HEADS).astype(f32)
    d_key_value = jnp.sum(
        d_back[:, HD:].reshape(parts, KV_HEADS, per_group, 2 * HD, rows_here).astype(f32),
        axis=(0, 2),
    )
    dq_normed = rope_back(d_query, cosine, sine)
    dk_normed = rope_back(d_key_value[:, :HD], cosine, sine)
    dq_raw, query_term = norm_back(dq_normed, q_raw, q_scale, column_query, 1)
    dk_raw, key_term = norm_back(dk_normed, k_raw, k_scale, column_key, 1)
    d_projected = jnp.concatenate(
        [
            dq_raw.reshape(q_width, rows_here).astype(bf16),
            dk_raw.reshape(kv_width, rows_here).astype(bf16),
            d_key_value[:, HD:].reshape(kv_width, rows_here).astype(bf16),
        ],
        axis=0,
    )
    grad_qkv_here = lax.dot_general(
        normed, d_projected, (((0,), (1,)), ((), ())), preferred_element_type=f32
    )
    d_normed = lax.dot_general(
        d_projected, w_qkv, (((0,), (1,)), ((), ())), preferred_element_type=f32
    )
    d_norm_one, attn_gain_term = norm_back(d_normed, inputs, scale_one, gain_attn)
    d_inputs = d_h_one + d_norm_one
    shard_qkv, shard_out, shard_attn_gain, shard_ffn_gain, shard_query_gain, shard_key_gain = (
        lax.psum_scatter(
            grad_qkv_here.astype(jnp.bfloat16), "fsdp", scatter_dimension=0, tiled=True
        ).astype(jnp.float32),
        lax.psum_scatter(
            grad_out_here.astype(jnp.bfloat16), "fsdp", scatter_dimension=0, tiled=True
        ).astype(jnp.float32),
        lax.psum_scatter(
            jnp.sum(attn_gain_term, axis=0).astype(jnp.bfloat16),
            "fsdp",
            scatter_dimension=0,
            tiled=True,
        ).astype(jnp.float32),
        lax.psum_scatter(
            jnp.sum(ffn_gain_term, axis=0).astype(jnp.bfloat16),
            "fsdp",
            scatter_dimension=0,
            tiled=True,
        ).astype(jnp.float32),
        lax.psum_scatter(
            jnp.sum(query_term, axis=(0, 2)).astype(jnp.bfloat16),
            "fsdp",
            scatter_dimension=0,
            tiled=True,
        ).astype(jnp.float32),
        lax.psum_scatter(
            jnp.sum(key_term, axis=(0, 2)).astype(jnp.bfloat16),
            "fsdp",
            scatter_dimension=0,
            tiled=True,
        ).astype(jnp.float32),
    )
    summed_grads = (
        lax.psum(shard_qkv.astype(jnp.bfloat16), "ctx").astype(jnp.float32),
        lax.psum(shard_out.astype(jnp.bfloat16), "ctx").astype(jnp.float32),
        lax.psum(grad_gate_up, "ctx").astype(jnp.float32),
        lax.psum(grad_down, "ctx").astype(jnp.float32),
        lax.psum(shard_attn_gain.astype(jnp.bfloat16), "ctx").astype(jnp.float32),
        lax.psum(shard_ffn_gain.astype(jnp.bfloat16), "ctx").astype(jnp.float32),
        lax.psum(shard_query_gain.astype(jnp.bfloat16), "ctx").astype(jnp.float32),
        lax.psum(shard_key_gain.astype(jnp.bfloat16), "ctx").astype(jnp.float32),
    )
    return (
        output[None],
        d_inputs[None],
        summed_grads[0],
        summed_grads[1],
        summed_grads[2],
        summed_grads[3],
        summed_grads[4],
        summed_grads[5],
        summed_grads[6],
        summed_grads[7],
    )


def solution(mesh):
    block = mesh.shape["fsdp"] == 2 and mesh.shape["ctx"] == 16
    return jax.shard_map(
        on_block if block else on_device,
        mesh=mesh,
        in_specs=(
            P("fsdp", "ctx", None),
            P("fsdp", None),
            P("fsdp", None),
            P("fsdp", None, None),
            P("fsdp", None),
            P("fsdp"),
            P("fsdp"),
            P("fsdp"),
            P("fsdp"),
            P("fsdp", None),
            P("fsdp", None),
            P("fsdp", "ctx", None),
        ),
        out_specs=(
            P("fsdp", "ctx", None),
            P("fsdp", "ctx", None),
            P("fsdp", None),
            P("fsdp", None),
            P("fsdp", None, None),
            P("fsdp", None),
            P("fsdp"),
            P("fsdp"),
            P("fsdp"),
            P("fsdp"),
        ),
        check_vma=False,
    )
```

```python
import functools

import jax
import jax.numpy as jnp
from jax import lax
from jax.experimental import pallas as pl
from jax.experimental.pallas import tpu as pltpu
from jax.sharding import PartitionSpec as P

HEADS = 16
KV_HEADS = 8
HD = 64
BLK = 128
TILE = 512
CHUNKS = 2
PROJECT = 0
ATTEND = 0
OUT = 0
FFN = (0, 0)
ATTEND_BACK = 25


EPSILON = 1e-05
ROPE_BASE = 1000000.0
LOG2E = 1.4426950408889634
SCORE_SCALE = LOG2E * HD ** (-0.5)


def rms_scale(values, axis=-1):
    return lax.rsqrt(jnp.mean(values * values, axis=axis, keepdims=True) + EPSILON)


def norm_back(grad_normed, inputs, scale, gain, axis=-1):
    scaled = grad_normed * gain
    grad_in = scale * scaled - inputs * scale * scale * scale * jnp.mean(
        scaled * inputs, axis=axis, keepdims=True
    )
    return (grad_in, grad_normed * inputs * scale)


def rope(values, cosine, sine):
    half = HD // 2
    first, second = values[:, :half], values[:, half:]
    return jnp.concatenate([first * cosine - second * sine, second * cosine + first * sine], axis=1)


def rope_back(values, cosine, sine):
    half = HD // 2
    first, second = values[:, :half], values[:, half:]
    return jnp.concatenate([first * cosine + second * sine, second * cosine - first * sine], axis=1)


def starts_of(packed, lengths_row):
    ends = jnp.cumsum(lengths_row)
    past = packed[:, None] >= ends[None, :]
    return jnp.sum(jnp.where(past, lengths_row[None, :], 0), axis=1)


def block_tables(order, lengths_row):
    count = order.shape[0]
    rank = jnp.sum((order[None, :] < order[:, None]).astype(jnp.int32), axis=1)
    hit = rank[None, :] == jnp.arange(count, dtype=jnp.int32)[:, None]
    slot = jnp.sum(jnp.where(hit, jnp.arange(count, dtype=jnp.int32)[None, :], 0), axis=1)
    block = jnp.sum(jnp.where(hit, order[None, :], 0), axis=1)
    place = (block[:, None] * BLK + jnp.arange(BLK, dtype=jnp.int32)[None, :]).reshape(-1)
    return (slot, place, starts_of(place, lengths_row))


def attend_kernel(
    q_slot, kv_slot, first, last, qkv_ref, place_ref, start_ref,
    out_ref, q_ref, qt_ref, k_ref, kt_ref, v_ref, ot_ref, total_ref, vt_ref
):
    per_device = qkv_ref.shape[2] // BLK
    kv_blocks = k_ref.shape[0] // BLK
    q_blocks = q_ref.shape[0] // BLK

    def piece(slot, lower):
        return qkv_ref[
            slot // per_device,
            lower : lower + HD,
            pl.ds(pl.multiple_of((slot % per_device) * BLK, BLK), BLK),
        ]

    for i in range(kv_blocks):
        here = slice(i * BLK, (i + 1) * BLK)
        keys = piece(kv_slot[i], HD)
        kt_ref[:, here] = keys
        k_ref[here, :] = keys.T
        values = piece(kv_slot[i], 2 * HD)
        vt_ref[:, here] = values
        v_ref[here, :] = values.T
    for i in range(q_blocks):
        here = slice(i * BLK, (i + 1) * BLK)
        queries = piece(q_slot[i], 0)
        qt_ref[:, here] = queries
        q_ref[here, :] = queries.T
    if q_blocks < kv_blocks:
        out_ref[...] = jnp.zeros_like(out_ref)

    def tile(i, carry):
        rows = pl.ds(pl.multiple_of(i * TILE, TILE), TILE)
        queries = qt_ref[:, rows]
        place = place_ref[:, rows]
        start = start_ref[:, rows]

        def step(j, state):
            total, summed = state
            at = pl.multiple_of(j * TILE, TILE)
            scores = jnp.dot(
                k_ref[pl.ds(at, TILE), :], queries, preferred_element_type=jnp.float32
            )
            key_place = lax.broadcasted_iota(jnp.int32, (TILE, TILE), 0) + at
            allowed = (key_place <= place) & (key_place >= start)
            lifted = jnp.where(allowed, jnp.exp2(scores * SCORE_SCALE), 0.0)
            total = total + jnp.sum(lifted, axis=0, keepdims=True)
            summed = summed + jnp.dot(
                vt_ref[:, pl.ds(at, TILE)],
                lifted.astype(jnp.bfloat16),
                preferred_element_type=jnp.float32,
            )
            return (total, summed)

        total, summed = lax.fori_loop(
            first[i],
            last[i],
            step,
            (jnp.zeros((1, TILE), jnp.float32), jnp.zeros((HD, TILE), jnp.float32)),
        )
        attn = summed / total
        ot_ref[:, rows] = attn
        total_ref[:, rows] = jnp.log(total) * LOG2E
        rounded = attn.astype(jnp.bfloat16)
        for part in range(TILE // BLK):
            slot = q_slot[i * (TILE // BLK) + part]
            out_ref[
                slot // per_device,
                :,
                pl.ds(pl.multiple_of((slot % per_device) * BLK, BLK), BLK),
            ] = rounded[:, part * BLK : (part + 1) * BLK]
        return carry

    lax.fori_loop(0, q_blocks * BLK // TILE, tile, 0)


def attend_back_kernel(
    q_slot, kv_slot, first, last, d_ref, place_ref, start_ref,
    q_ref, qt_ref, k_ref, kt_ref, v_ref, ot_ref, total_ref,
    out_ref, dt_ref, do_ref, dk_ref, dv_ref
):
    per_device = d_ref.shape[2] // BLK
    kv_blocks = k_ref.shape[0] // BLK
    q_blocks = q_ref.shape[0] // BLK

    def lanes(slot):
        return pl.ds(pl.multiple_of((slot % per_device) * BLK, BLK), BLK)

    for i in range(q_blocks):
        here = slice(i * BLK, (i + 1) * BLK)
        slot = q_slot[i]
        grads = d_ref[slot // per_device, :, lanes(slot)]
        dt_ref[:, here] = grads
        do_ref[here, :] = grads.T
    dk_ref[...] = jnp.zeros_like(dk_ref)
    dv_ref[...] = jnp.zeros_like(dv_ref)
    if q_blocks < kv_blocks:
        out_ref[...] = jnp.zeros_like(out_ref)

    def tile(i, carry):
        rows = pl.ds(pl.multiple_of(i * TILE, TILE), TILE)
        queries = qt_ref[:, rows]
        grads = dt_ref[:, rows]
        place = place_ref[:, rows]
        start = start_ref[:, rows]
        delta = jnp.sum(grads.astype(jnp.float32) * ot_ref[:, rows], axis=0, keepdims=True)
        total = total_ref[:, rows]

        def step(j, d_query):
            at = pl.multiple_of(j * TILE, TILE)
            here = pl.ds(at, TILE)
            scores = jnp.dot(k_ref[here, :], queries, preferred_element_type=jnp.float32)
            key_place = lax.broadcasted_iota(jnp.int32, (TILE, TILE), 0) + at
            allowed = (key_place <= place) & (key_place >= start)
            shares = jnp.where(allowed, jnp.exp2(scores * SCORE_SCALE - total), 0.0)
            d_shares = jnp.dot(v_ref[here, :], grads, preferred_element_type=jnp.float32)
            d_scores = (shares * (d_shares - delta)).astype(jnp.bfloat16)
            dv_ref[here, :] += jnp.dot(
                shares.astype(jnp.bfloat16), do_ref[rows, :], preferred_element_type=jnp.float32
            )
            dk_ref[here, :] += jnp.dot(
                d_scores, q_ref[rows, :], preferred_element_type=jnp.float32
            )
            return d_query + jnp.dot(
                kt_ref[:, here], d_scores, preferred_element_type=jnp.float32
            )

        d_query = lax.fori_loop(first[i], last[i], step, jnp.zeros((HD, TILE), jnp.float32))
        rounded = (d_query * HD ** (-0.5)).astype(jnp.bfloat16)
        for part in range(TILE // BLK):
            slot = q_slot[i * (TILE // BLK) + part]
            out_ref[slot // per_device, 0:HD, lanes(slot)] = rounded[
                :, part * BLK : (part + 1) * BLK
            ]
        return carry

    lax.fori_loop(0, q_blocks * BLK // TILE, tile, 0)
    for i in range(kv_blocks):
        here = slice(i * BLK, (i + 1) * BLK)
        slot = kv_slot[i]
        out_ref[slot // per_device, HD : 2 * HD, lanes(slot)] = (
            (dk_ref[here, :] * HD ** (-0.5)).T.astype(jnp.bfloat16)
        )
        out_ref[slot // per_device, 2 * HD : 3 * HD, lanes(slot)] = (
            dv_ref[here, :].T.astype(jnp.bfloat16)
        )


def cost(micros):
    return pl.CostEstimate(
        flops=1 + micros * 1_000_000_000, bytes_accessed=1, transcendentals=0
    )


def kernel_call(kernel, tables, arrays, outs, scratch, micros):
    smem = pl.BlockSpec(memory_space=pltpu.SMEM)
    vmem = pl.BlockSpec(memory_space=pltpu.VMEM)
    return pl.pallas_call(
        kernel,
        out_shape=outs,
        in_specs=[smem] * len(tables) + [vmem] * len(arrays),
        out_specs=[vmem] * len(outs),
        scratch_shapes=scratch,
        compiler_params=pltpu.CompilerParams(vmem_limit_bytes=48 * 1024 * 1024),
        cost_estimate=cost(micros),
    )(*tables, *arrays)


class Links:
    def __init__(self, ctx_size):
        self.depth = ctx_size // 4
        index = lax.axis_index("ctx")
        self.core = index % 2
        self.y = (index // 2) % 2
        self.side = lax.axis_index("fsdp")
        self.half = index // 4 % 2
        self.quarter = index % 2 * 2 + self.y
        self.here = jnp.stack([self.half, self.core, self.y, self.side]).astype(jnp.int32)

    def route(self, place):
        pairs = []
        for z in range(self.depth):
            for y in range(2):
                for core in range(2):
                    to_z, to_y, to_core = place(z, y, core)
                    pairs.append(((z * 2 + y) * 2 + core, (to_z * 2 + to_y) * 2 + to_core))
        return pairs

    def over_core(self, value):
        return lax.ppermute(value, "ctx", self.route(lambda z, y, c: (z, y, 1 - c)))

    def over_y(self, value):
        return lax.ppermute(value, "ctx", self.route(lambda z, y, c: (z, 1 - y, c)))

    def over_z(self, value):
        return lax.ppermute(value, "ctx", self.route(lambda z, y, c: (z ^ 1, y, c)))

    def over_two_z(self, value):
        return lax.ppermute(value, "ctx", self.route(lambda z, y, c: (z ^ 2, y, c)))

    def over_x(self, value):
        return lax.ppermute(value, "fsdp", [(0, 1), (1, 0)])

    def spread_plane(self, value):
        across = self.over_core(value)
        beside = self.over_y(value)
        return (value, across, beside, self.over_core(beside))

    def deal_plane(self, near, far, give, give_far):
        got, got_far = self.over_core(give), self.over_core(give_far)
        return (near, got, self.over_y(far), self.over_y(got_far))

    def half_of(self, kept, got, own):
        index = self.half if own else 1 - self.half
        return add(pick(kept, index, 0), pick(got, index, 0))


def pick(value, index, axis):
    return lax.dynamic_index_in_dim(value, index, axis, keepdims=False)


def add(left, right):
    return (left.astype(jnp.float32) + right.astype(jnp.float32)).astype(jnp.bfloat16)


def after(value, *others):
    return lax.optimization_barrier((value, *jax.tree.leaves(others)))[0]


def contract(left, right, axes):
    return lax.dot_general(
        left, right, ((axes[:1], axes[1:]), ((), ())), preferred_element_type=jnp.float32
    )


PARAMS = pltpu.CompilerParams(vmem_limit_bytes=56 * 1024 * 1024)


def call_with_here(
    kernel, here, grid, arrays, specs, outs, out_specs, scratch=(), aliases=None, micros=0
):
    return pl.pallas_call(
        kernel,
        grid_spec=pltpu.PrefetchScalarGridSpec(
            num_scalar_prefetch=1,
            grid=grid,
            in_specs=specs,
            out_specs=out_specs,
            scratch_shapes=list(scratch),
        ),
        out_shape=outs,
        input_output_aliases=aliases or {},
        compiler_params=PARAMS,
        cost_estimate=cost(micros),
    )(here, *arrays)


def whole(array):
    rank = len(array.shape)
    return pl.BlockSpec(array.shape, lambda i, here: (0,) * rank)


def project_kernel(here, *refs):
    x_ref, gain_ref, own_ref = refs[:3]
    pieces, q_gain, k_gain, cos_ref, sin_ref = refs[3:7], refs[7], refs[8], refs[9], refs[10]
    sent, weight, q_ref, k_ref, q_scale, k_scale, normed_ref, scale_ref = refs[11:]
    core, y, side = here[1], here[2], here[3]
    rows = own_ref.shape[0]
    part = rows // 4
    f32, bf16 = jnp.float32, jnp.bfloat16
    weight[pl.ds(pl.multiple_of(side * rows, rows), rows), :] = own_ref[...]
    for p in range(4):
        at = (1 - side) * rows + (((p % 2) ^ core) * 2 + ((p // 2) ^ y)) * part
        weight[pl.ds(pl.multiple_of(at, part), part), :] = pieces[p][...]
    x = x_ref[...].astype(f32)
    scale = rms_scale(x)
    scale_ref[...] = scale
    normed = (x * scale * gain_ref[...]).astype(bf16)
    normed_ref[...] = normed.T
    cosine, sine = cos_ref[...], sin_ref[...]
    half = HD // 2

    def turned(raw, gain, raw_ref, kept_scale, head):
        raw_ref[head * HD : (head + 1) * HD, :] = raw
        scale = rms_scale(raw, 0)
        kept_scale[head : head + 1, :] = scale
        value = raw * scale * gain
        first, second = value[:half], value[half:]
        return jnp.concatenate(
            [first * cosine - second * sine, second * cosine + first * sine], axis=0
        ).astype(bf16)

    per_group = HEADS // KV_HEADS
    for at in range(0, weight.shape[1], 2 * BLK):
        block = jnp.dot(normed, weight[:, at : at + 2 * BLK], preferred_element_type=f32)
        turned_block = block.T
        for n in range(2 * BLK // HD):
            head = at // HD + n
            raw = turned_block[n * HD : (n + 1) * HD, :]
            if head < HEADS:
                sent[head, 0:HD, :] = turned(raw, q_gain[...], q_ref, q_scale, head)
                continue
            head -= HEADS
            if head < KV_HEADS:
                value, row = turned(raw, k_gain[...], k_ref, k_scale, head), HD
            else:
                value, row, head = raw.astype(bf16), 2 * HD, head - KV_HEADS
            for copy in range(per_group):
                sent[head * per_group + copy, row : row + HD, :] = value


def project(here, x, gain, own, pieces, q_gain, k_gain, cosine, sine):
    tokens, width = x.shape
    f32, bf16 = jnp.float32, jnp.bfloat16
    shape = jax.ShapeDtypeStruct
    arrays = [x, gain, own, *pieces, q_gain, k_gain, cosine, sine]
    outs = [
        shape((HEADS, 3 * HD, tokens), bf16),
        shape((width, own.shape[1]), bf16),
        shape((HEADS * HD, tokens), f32),
        shape((KV_HEADS * HD, tokens), f32),
        shape((HEADS, tokens), f32),
        shape((KV_HEADS, tokens), f32),
        shape((width, tokens), bf16),
        shape((tokens, 1), f32),
    ]
    return call_with_here(
        project_kernel, here, (1,), arrays, [whole(a) for a in arrays], outs,
        [whole(o) for o in outs], micros=PROJECT,
    )


def layer(array, index):
    return pl.BlockSpec((1, *array.shape[1:]), lambda i, here: (index, 0, 0))


def attend_out_kernel(here, *refs):
    attn_ref, x_ref, gain_ref, own_ref = refs[:4]
    pieces = refs[4:20]
    weight, h_ref, scale_ref, two_ref, two_t_ref = refs[20:]
    core, y, side = here[1], here[2], here[3]
    rows = own_ref.shape[0]
    part = rows // 4
    weight[pl.ds(pl.multiple_of(side * rows, rows), rows), :] = own_ref[...]
    for p in range(4):
        at = (1 - side) * rows + (((p % 2) ^ core) * 2 + ((p // 2) ^ y)) * part
        for n in range(4):
            piece = pieces[4 * p + n]
            wide = piece.shape[1]
            weight[pl.ds(pl.multiple_of(at, part), part), n * wide : (n + 1) * wide] = piece[...]
    attn = attn_ref[...].T
    h_one = x_ref[...].astype(jnp.float32) + jnp.dot(
        attn, weight[...], preferred_element_type=jnp.float32
    )
    scale = rms_scale(h_one)
    h_ref[...] = h_one
    scale_ref[...] = scale
    two = (h_one * scale * gain_ref[...]).astype(jnp.bfloat16)
    two_ref[...] = two
    two_t_ref[...] = two.T


def attend_out(here, attn, x, gain, own, pieces):
    tokens, width = x.shape
    f32, bf16 = jnp.float32, jnp.bfloat16
    shape = jax.ShapeDtypeStruct
    part = own.shape[0] // 4
    cuts = 4
    part_width = width // cuts
    first = pieces[0].shape[1] // part_width - cuts
    arrays = [attn, x, gain, own]
    specs = [whole(a) for a in arrays]
    for piece in pieces:
        for n in range(cuts):
            arrays.append(piece)
            specs.append(pl.BlockSpec((part, part_width), lambda i, here, n=n: (0, first + n)))
    outs = [
        shape((width, width), bf16),
        shape((tokens, width), f32),
        shape((tokens, 1), f32),
        shape((tokens, width), bf16),
        shape((width, tokens), bf16),
    ]
    return call_with_here(
        attend_out_kernel, here, (1,), arrays, specs, outs, [whole(o) for o in outs], micros=OUT
    )


def ffn_kernel(chunk, here, *refs):
    two_ref, d_ref, own_ref = refs[:3]
    pieces, down_ref, down_pieces = (refs[3:7], refs[7:11]), refs[11], refs[12:16]
    refs = refs[4:]
    if chunk == 0:
        before_refs, refs = refs[12:13], refs[13:]
        near, far, give, give_far, out_ref, d_two_ref = refs[:6]
        refs = refs[6:]
    else:
        before_refs, gain_ref, refs = refs[12:17], refs[17], refs[18:]
        near, far, give, give_far = refs[:4]
        out_ref, d_h_ref, d_attn_ref, heads_ref, gain_term_ref = refs[4:9]
        refs = refs[9:]
    weight, down, hidden_rows, out_sum, two_sum = refs[:5]
    held, weight_sem, down_sem, before_sem = refs[5:-3], refs[-3], refs[-2], refs[-1]
    core, y, side = here[1], here[2], here[3]
    f32, bf16 = jnp.float32, jnp.bfloat16
    own_rows, columns = own_ref.shape[1], own_ref.shape[2] // CHUNKS
    part = own_rows // 4
    tile = columns // FFN_TILES
    half = columns // 2

    def quarter(p):
        return ((p % 2) ^ core) * 2 + ((p // 2) ^ y)

    def copies(n):
        at = slice(n * tile, (n + 1) * tile)
        mine = pl.ds(pl.multiple_of(side * own_rows, own_rows), own_rows)
        found = [
            pltpu.make_async_copy(
                own_ref.at[:, :, chunk * columns + n * tile : chunk * columns + (n + 1) * tile],
                weight.at[:, mine, at],
                weight_sem.at[n, 0],
            )
        ]
        for p in range(4):
            rows = pl.ds(pl.multiple_of((1 - side) * own_rows + quarter(p) * part, part), part)
            for kind in range(2):
                begin = n * tile + (columns if kind == 1 and chunk == 1 else 0)
                found.append(
                    pltpu.make_async_copy(
                        pieces[kind][p].at[:, begin : begin + tile],
                        weight.at[kind, rows, at],
                        weight_sem.at[n, 1 + 2 * p + kind],
                    )
                )
        return found

    def own_down(n):
        at = slice(n * tile, (n + 1) * tile)
        return [pltpu.make_async_copy(down_ref.at[at, :], down.at[at, :], down_sem.at[n, 0])]

    def other_down(n):
        at = slice(n * tile, (n + 1) * tile)
        found = []
        for p in range(4):
            wide = down_pieces[p].shape[1]
            lanes = pl.ds(pl.multiple_of(quarter(p) * wide, wide), wide)
            found.append(
                pltpu.make_async_copy(
                    down_pieces[p].at[at, :], down.at[at, lanes], down_sem.at[n, p]
                )
            )
        return found

    def each(action, n):
        for copy in copies(n):
            action(copy)

        @pl.when(side == chunk)
        def _():
            for copy in own_down(n):
                action(copy)

        @pl.when(side != chunk)
        def _():
            for copy in other_down(n):
                action(copy)

    before = [
        pltpu.make_async_copy(ref, held[n], before_sem.at[n]) for n, ref in enumerate(before_refs)
    ]
    for n in range(FFN_TILES):
        each(lambda copy: copy.start(), n)
    for copy in before:
        copy.start()
    two = two_ref[...]
    d_ffn = d_ref[...]
    for n in range(FFN_TILES):
        each(lambda copy: copy.wait(), n)
        at = slice(n * tile, (n + 1) * tile)
        gate = jnp.dot(two, weight[0, :, at], preferred_element_type=f32)
        upper = jnp.dot(two, weight[1, :, at], preferred_element_type=f32)
        d_hidden = contract(d_ffn, down[at, :], (1, 1))
        sigma = jax.nn.sigmoid(gate)
        silu = gate * sigma
        hidden = (silu * upper).astype(bf16)
        d_gate = (d_hidden * upper * sigma * (1.0 + gate * (1.0 - sigma))).astype(bf16)
        d_upper = (d_hidden * silu).astype(bf16)
        out_term = jnp.dot(hidden, down[at, :], preferred_element_type=f32)
        two_term = contract(d_gate, weight[0, :, at], (1, 1)) + contract(
            d_upper, weight[1, :, at], (1, 1)
        )
        out_sum[...] = out_term if n == 0 else out_sum[...] + out_term
        two_sum[...] = two_term if n == 0 else two_sum[...] + two_term
        hidden_rows[:, at] = hidden
        mine = jnp.where(core == 0, d_gate, d_upper)
        other = jnp.where(core == 0, d_upper, d_gate)
        for column in range(2):
            begin, end = max(n * tile, column * half), min((n + 1) * tile, (column + 1) * half)
            if begin >= end:
                continue
            source = slice(begin - n * tile, end - n * tile)
            target = slice(begin - column * half, end - column * half)
            first, second = mine[:, source], other[:, source]

            @pl.when(y == column)
            def _(first=first, second=second, target=target):
                near[:, target] = first
                give[:, target] = second

            @pl.when(y != column)
            def _(first=first, second=second, target=target):
                far[:, target] = first
                give_far[:, target] = second

    share = half // 2
    target = slice(half, half + share)
    for owner in range(2):
        lower = hidden_rows[:, owner * half : owner * half + share]
        upper = hidden_rows[:, owner * half + share : (owner + 1) * half]
        close = jnp.where(y == 0, lower, upper)
        distant = jnp.where(y == 0, upper, lower)

        @pl.when(core == owner)
        def _(close=close, distant=distant):
            near[:, target] = close
            far[:, target] = distant

        @pl.when(core != owner)
        def _(close=close, distant=distant):
            give[:, target] = close
            give_far[:, target] = distant

    for copy in before:
        copy.wait()
    if chunk == 0:
        out_ref[...] = held[0][...] + out_sum[...]
        d_two_ref[...] = two_sum[...]
    else:
        out_before, two_before, h_one, scale, w_out = held
        out_ref[...] = (out_before[...] + out_sum[...]).astype(bf16)
        d_norm, gain_term = norm_back(
            two_before[...] + two_sum[...], h_one[...], scale[...], gain_ref[...]
        )
        gain_term_ref[...] = jnp.sum(gain_term, axis=0, keepdims=True)
        d_h_one = d_ffn.astype(f32) + d_norm
        d_h_ref[...] = d_h_one
        d_attn = d_h_one.astype(bf16)
        d_attn_ref[...] = d_attn
        heads_ref[...] = contract(w_out[...], d_attn, (1, 1)).astype(bf16)


FFN_TILES = 3


def ffn(here, chunk, two, d_ffn, own, pieces, down, down_pieces, before, gain=None):
    tokens, width = two.shape
    columns = own.shape[2] // CHUNKS
    padded = (columns // 2 + columns // 4 + BLK - 1) // BLK * BLK
    shape = jax.ShapeDtypeStruct
    f32, bf16 = jnp.float32, jnp.bfloat16
    outs = [shape((tokens, padded), bf16)] * 4
    if chunk == 0:
        outs += [shape((tokens, width), f32)] * 2
    else:
        outs += [
            shape((tokens, width), bf16),
            shape((tokens, width), f32),
            shape((tokens, width), bf16),
            shape((width, tokens), bf16),
            shape((1, width), f32),
        ]
    far_away = pl.BlockSpec(memory_space=pl.ANY)
    arrays = [two, d_ffn, own, *pieces[0], *pieces[1], down, *down_pieces, *before]
    specs = [whole(two), whole(d_ffn)] + [far_away] * (len(arrays) - 2)
    if gain is not None:
        arrays.append(gain)
        specs.append(whole(gain))
    got = call_with_here(
        functools.partial(ffn_kernel, chunk),
        here,
        (1,),
        arrays,
        specs,
        outs,
        [whole(o) for o in outs],
        [
            pltpu.VMEM((2, width, columns), bf16),
            pltpu.VMEM((columns, width), bf16),
            pltpu.VMEM((tokens, columns), bf16),
            pltpu.VMEM((tokens, width), f32),
            pltpu.VMEM((tokens, width), f32),
        ]
        + [pltpu.VMEM(v.shape, v.dtype) for v in before]
        + [
            pltpu.SemaphoreType.DMA((FFN_TILES, 9)),
            pltpu.SemaphoreType.DMA((FFN_TILES, 4)),
            pltpu.SemaphoreType.DMA((len(before),)),
        ],
        micros=FFN[chunk],
    )
    return got[:4], got[4:]


def wide_product_kernel(here, *refs):
    planes, terms = refs[:4], refs[4:8]
    sent, kept, left, right = refs[8:]
    tokens = planes[0].shape[1]
    columns = right.shape[1]
    for i in range(4):
        left[:, i * tokens : (i + 1) * tokens] = planes[i][...]
        right[i * tokens : (i + 1) * tokens, :] = terms[i][:, :columns]
    side = here[3]
    _, step, _ = kept.shape
    for half in range(2):
        for owner, out_ref in ((1 - side, sent), (side, kept)):
            place = pl.multiple_of(owner * 2 * step + half * step, step)
            out_ref[half] = jnp.dot(
                left[pl.ds(place, step), :], right[...], preferred_element_type=jnp.float32
            ).astype(out_ref.dtype)


def wide_products(here, two_plane, shares, columns):
    rows, tokens = two_plane[0].shape
    outs = [
        jax.ShapeDtypeStruct((2, rows // 4, columns), jnp.bfloat16),
        jax.ShapeDtypeStruct((2, rows // 4, columns), jnp.float32),
    ]
    arrays = [*two_plane, *shares]
    return call_with_here(
        wide_product_kernel,
        here,
        (1,),
        arrays,
        [whole(a) for a in two_plane]
        + [pl.BlockSpec((tokens, columns), lambda i, here: (0, 0))] * 4,
        outs,
        [whole(o) for o in outs],
        [
            pltpu.VMEM((rows, 4 * tokens), jnp.bfloat16),
            pltpu.VMEM((4 * tokens, columns), jnp.bfloat16),
        ],
        micros=3,
    )


def down_product_kernel(here, *refs):
    planes, terms = refs[:4], (refs[4:8], refs[8:12])
    sent, kept, left, right = refs[12:]
    tokens = planes[0].shape[0]
    rows = left.shape[0]
    for i in range(4):
        right[i * tokens : (i + 1) * tokens, :] = planes[i][...]
    for chunk in range(2):
        for i in range(4):
            share = terms[chunk][i]
            at = share.shape[1] // BLK * BLK - (rows + BLK - 1) // BLK * BLK
            left[:, i * tokens : (i + 1) * tokens] = share[:, at : at + rows].T
        for half in range(2):
            product = jnp.dot(
                left[half * rows // 2 : (half + 1) * rows // 2, :],
                right[...],
                preferred_element_type=jnp.float32,
            )

            @pl.when(here[3] == chunk)
            def _(product=product, half=half):
                kept[half] = product

            @pl.when(here[3] != chunk)
            def _(product=product, half=half):
                sent[half] = product.astype(sent.dtype)


def down_products(here, d_plane, first, second, rows):
    tokens, columns = d_plane[0].shape
    outs = [
        jax.ShapeDtypeStruct((2, rows // 2, columns), jnp.bfloat16),
        jax.ShapeDtypeStruct((2, rows // 2, columns), jnp.float32),
    ]
    return call_with_here(
        down_product_kernel,
        here,
        (1,),
        [*d_plane, *first, *second],
        [whole(a) for a in (*d_plane, *first, *second)],
        outs,
        [whole(o) for o in outs],
        [
            pltpu.VMEM((rows, 4 * tokens), jnp.bfloat16),
            pltpu.VMEM((4 * tokens, columns), jnp.bfloat16),
        ],
        micros=3,
    )


GAIN_ROWS = 16


def attention_back_kernel(here, *refs):
    d_ref, q_ref, k_ref, q_scale, k_scale, q_gain, k_gain, cos_ref, sin_ref = refs[:9]
    weight, x_ref, scale_ref, gain_ref, d_h_ref, d_attn_ref = refs[9:15]
    near, far, give, give_far, d_x_ref, gains_ref = refs[15:21]
    turned, natural = refs[21:]
    f32, bf16 = jnp.float32, jnp.bfloat16
    core, y = here[1], here[2]
    cosine, sine = cos_ref[...], sin_ref[...]
    half = HD // 2
    per_group = HEADS // KV_HEADS
    tokens = x_ref.shape[0]

    def back(grad, raw, scale, gain):
        first, second = grad[:half], grad[half:]
        normed = jnp.concatenate(
            [first * cosine + second * sine, second * cosine - first * sine], axis=0
        )
        return norm_back(normed, raw, scale, gain, 0)

    q_term = jnp.zeros((HD, tokens), f32)
    k_term = jnp.zeros((HD, tokens), f32)
    for head in range(HEADS):
        at = slice(head * HD, (head + 1) * HD)
        grad, term = back(
            d_ref[head, :HD, :].astype(f32), q_ref[at, :], q_scale[head : head + 1, :], q_gain[...]
        )
        turned[at, :] = grad.astype(bf16)
        q_term = q_term + term
    for head in range(KV_HEADS):
        at = slice(head * HD, (head + 1) * HD)
        both = d_ref[head * per_group, HD:, :].astype(f32)
        for other in range(1, per_group):
            both = both + d_ref[head * per_group + other, HD:, :].astype(f32)
        grad, term = back(both[:HD], k_ref[at, :], k_scale[head : head + 1, :], k_gain[...])
        place = HEADS * HD + head * HD
        turned[place : place + HD, :] = grad.astype(bf16)
        k_term = k_term + term
        place += KV_HEADS * HD
        turned[place : place + HD, :] = both[HD:].astype(bf16)
    rows = turned.shape[0] // 4
    columns = d_attn_ref.shape[1] // 4
    shares = ((near, core, y), (far, core, 1 - y), (give, 1 - core, y), (give_far, 1 - core, 1 - y))
    for out_ref, to_core, to_y in shares:
        share = to_core * 2 + to_y
        out_ref[:rows, :] = turned[pl.ds(pl.multiple_of(share * rows, rows), rows), :]
        out_ref[rows:, :] = d_attn_ref[:, pl.ds(pl.multiple_of(share * columns, columns), columns)]
    for at in range(0, turned.shape[0], 256):
        natural[:, at : at + 256] = turned[at : at + 256, :].T
    d_normed = contract(natural[...], weight[...], (1, 1))
    x = x_ref[...].astype(f32)
    d_norm, gain_term = norm_back(d_normed, x, scale_ref[...], gain_ref[...])
    d_x_ref[...] = d_h_ref[...] + d_norm
    gains_ref[...] = jnp.zeros_like(gains_ref)
    gains_ref[0:1, :] = jnp.sum(gain_term, axis=0, keepdims=True)
    gains_ref[1:2, 0:HD] = jnp.sum(q_term.T, axis=0, keepdims=True)
    gains_ref[2:3, 0:HD] = jnp.sum(k_term.T, axis=0, keepdims=True)


def attention_back(here, arrays):
    f32, bf16 = jnp.float32, jnp.bfloat16
    shape = jax.ShapeDtypeStruct
    weight, x = arrays[9], arrays[10]
    tokens, width = x.shape
    rows = weight.shape[1] // 4 + tokens
    assert width // 4 == tokens
    outs = [
        *[shape((rows, tokens), bf16)] * 4,
        shape((tokens, width), f32),
        shape((8, width), f32),
    ]
    return call_with_here(
        attention_back_kernel, here, (1,), arrays, [whole(a) for a in arrays], outs,
        [whole(o) for o in outs],
        [pltpu.VMEM((weight.shape[1], tokens), bf16), pltpu.VMEM((tokens, weight.shape[1]), bf16)],
        micros=0,
    )


def attention_product_kernel(here, *refs):
    planes, terms, gains_ref, ffn_gain_ref = refs[:4], refs[4:8], refs[8], refs[9]
    sent, kept, left, right, left_out, right_out = refs[10:]
    tokens = planes[0].shape[2]
    cut = right.shape[1]
    for i in range(4):
        at = slice(i * tokens, (i + 1) * tokens)
        left[:, at] = planes[i][0]
        left_out[:, at] = planes[i][1]
        share = terms[i]
        right[at, :] = share[:cut].T
        right_out[at, :] = share[cut:]
    step = left.shape[0] // 4
    for owner, out_ref in ((1 - here[3], sent), (here[3], kept)):
        for half in range(2):
            at = pl.ds(pl.multiple_of(owner * 2 * step + half * step, step), step)
            out_ref[half, :step, :cut] = jnp.dot(
                left[at, :], right[...], preferred_element_type=jnp.float32
            ).astype(out_ref.dtype)
            out_ref[half, :step, cut:] = jnp.dot(
                left_out[at, :], right_out[...], preferred_element_type=jnp.float32
            ).astype(out_ref.dtype)
        rows = gains_ref.shape[1] // 2
        mine = pl.ds(pl.multiple_of(owner * rows, rows), rows)
        wide = out_ref.shape[2] - rows
        block = jnp.concatenate(
            [
                jnp.concatenate([gains_ref[0:1, mine], gains_ref[1:2, 0:wide]], axis=1),
                jnp.concatenate([ffn_gain_ref[:, mine], gains_ref[2:3, 0:wide]], axis=1),
                jnp.zeros((GAIN_ROWS - 2, out_ref.shape[2]), jnp.float32),
            ],
            axis=0,
        )
        out_ref[0, step:, :] = block.astype(out_ref.dtype)
        out_ref[1, step:, :] = jnp.zeros((GAIN_ROWS, out_ref.shape[2]), out_ref.dtype)


def attention_products(here, pair_plane, shares, gains, ffn_gain):
    _, width, tokens = pair_plane[0].shape
    cut = shares[0].shape[0] - tokens
    shape = (2, width // 4 + GAIN_ROWS, cut + tokens)
    outs = [jax.ShapeDtypeStruct(shape, jnp.bfloat16), jax.ShapeDtypeStruct(shape, jnp.float32)]
    return call_with_here(
        attention_product_kernel,
        here,
        (1,),
        [*pair_plane, *shares, gains, ffn_gain],
        [whole(a) for a in (*pair_plane, *shares, gains, ffn_gain)],
        outs,
        [whole(o) for o in outs],
        [
            pltpu.VMEM((width, 4 * tokens), jnp.bfloat16),
            pltpu.VMEM((4 * tokens, cut), jnp.bfloat16),
            pltpu.VMEM((width, 4 * tokens), jnp.bfloat16),
            pltpu.VMEM((4 * tokens, tokens), jnp.bfloat16),
        ],
        micros=3,
    )


def place_gate_up_kernel(here, *refs):
    mine, across, beside, diagonal, out_ref = *refs[:4], refs[-1]
    pieces = (mine, across, beside, diagonal)
    wide = mine.shape[2]
    for case in range(4):
        core, y = case // 2, case % 2

        @pl.when((here[1] == core) & (here[2] == y))
        def _(core=core, y=y):
            for kind in range(2):
                for column in range(2):
                    value = pieces[(y ^ column) * 2 + (core ^ kind)][0]
                    out_ref[:, kind, column * wide : (column + 1) * wide] = value.astype(
                        jnp.float32
                    )


def place_gate_up(here, chunk, pieces, before):
    _, rows, wide = pieces[0].shape
    step = 128
    blocks = rows // step

    def source(i, here):
        return ((i // blocks) ^ here[0], i % blocks, 0)

    arrays = list(pieces)
    specs = [pl.BlockSpec((1, step, wide), source)] * 4
    aliases = {}
    if before is not None:
        arrays.append(before)
        specs.append(pl.BlockSpec(memory_space=pl.ANY))
        aliases = {5: 0}
    (out,) = call_with_here(
        place_gate_up_kernel,
        here,
        (2 * blocks,),
        arrays,
        specs,
        [jax.ShapeDtypeStruct((2 * rows, 2, 2 * wide * CHUNKS), jnp.float32)],
        [pl.BlockSpec((step, 2, 2 * wide), lambda i, here: (i, 0, chunk))],
        aliases=aliases,
        micros=0,
    )
    return out


def place_down(here, pieces):
    _, rows, columns = pieces[0].shape

    def kernel(here, *refs):
        for s in range(8):

            @pl.when(pl.program_id(0) == s)
            def _(s=s):
                refs[4][...] = refs[s % 4][s // 4].astype(jnp.float32)

    def target(s, here):
        half = (s // 4) ^ here[0]
        y = ((s // 2) % 2) ^ here[2]
        core = (s % 2) ^ here[1]
        return ((core * 2 + y) * 2 + half, 0)

    (out,) = call_with_here(
        kernel,
        here,
        (8,),
        list(pieces),
        [whole(v) for v in pieces],
        [jax.ShapeDtypeStruct((rows * 8, columns), jnp.float32)],
        [pl.BlockSpec((rows, columns), target)],
    )
    return out


def place_attention(here, pieces, cut):
    _, rows, columns = pieces[0].shape
    rows -= GAIN_ROWS

    def kernel(here, *refs):
        qkv_ref, out_ref, gains_ref = refs[4:]
        for s in range(8):

            @pl.when(pl.program_id(0) == s)
            def _(s=s):
                value = refs[s % 4][s // 4]
                qkv_ref[...] = value[:rows, :cut].astype(jnp.float32)
                out_ref[...] = value[:rows, cut:].astype(jnp.float32)
                gains = value[rows:].astype(jnp.float32)
                gains_ref[...] = gains if s == 0 else gains_ref[...] + gains

    def target(s, here):
        half = (s // 4) ^ here[0]
        return (half, ((s % 2) ^ here[1]) * 2 + (((s // 2) % 2) ^ here[2]))

    shape = jax.ShapeDtypeStruct
    f32 = jnp.float32
    gain_shape = (GAIN_ROWS, columns)
    return call_with_here(
        kernel,
        here,
        (8,),
        list(pieces),
        [whole(v) for v in pieces],
        [
            shape((2 * rows, 4 * cut), f32),
            shape((2 * rows, 4 * (columns - cut)), f32),
            shape(gain_shape, f32),
        ],
        [
            pl.BlockSpec((rows, cut), target),
            pl.BlockSpec((rows, columns - cut), target),
            pl.BlockSpec(gain_shape, lambda s, here: (0, 0)),
        ],
    )


def on_block(
    tokens,
    qkv_weight,
    out_weight,
    gate_up_weight,
    down_weight,
    attn_gain,
    ffn_gain,
    query_gain,
    key_gain,
    seq_lengths,
    block_order,
    cotangent,
):
    inputs = tokens[0].astype(jnp.float32)
    rows_here = inputs.shape[0]
    ctx_size = lax.axis_size("ctx")
    ctx_index = lax.axis_index("ctx")
    per_group = HEADS // KV_HEADS
    q_width = HEADS * HD
    kv_width = KV_HEADS * HD
    order_row = block_order[0]
    lengths_row = seq_lengths[0]
    slots = jnp.arange(rows_here, dtype=jnp.int32) // BLK + ctx_index * (rows_here // BLK)
    table = slots[:, None] == jnp.arange(order_row.shape[0], dtype=jnp.int32)[None, :]
    packed = (
        jnp.sum(jnp.where(table, order_row[None, :], 0), axis=1) * BLK
        + jnp.arange(rows_here, dtype=jnp.int32) % BLK
    )
    local = packed - starts_of(packed, lengths_row)
    frequency = ROPE_BASE ** (-2.0 * jnp.arange(HD // 2, dtype=jnp.float32) / HD)
    angle = frequency[:, None] * local.astype(jnp.float32)[None, :]
    cosine = jnp.cos(angle)[None]
    sine = jnp.sin(angle)[None]
    bf16, f32 = jnp.bfloat16, jnp.float32
    parts = ctx_size // HEADS
    part = ctx_index // HEADS
    part_blocks = HEADS * rows_here // BLK
    q_order = lax.dynamic_slice_in_dim(order_row, part * part_blocks, part_blocks)
    q_slot, q_place, q_start = block_tables(q_order, lengths_row)
    q_slot = q_slot + part * part_blocks
    kv_slot, _, _ = block_tables(order_row, lengths_row)
    first = jnp.min(q_start.reshape(-1, TILE), axis=1) // TILE
    last = jnp.max(q_place.reshape(-1, TILE), axis=1) // TILE + 1
    tables = (q_slot, kv_slot, first, last)
    q_rows, kv_rows = part_blocks * BLK, order_row.shape[0] * BLK

    links = Links(ctx_size)
    here = links.here
    width = inputs.shape[1]
    rows = qkv_weight.shape[0]
    part_rows = rows // 4

    def quarter_rows(weight):
        return lax.dynamic_slice_in_dim(weight, links.quarter * part_rows, part_rows)

    qkv_piece = quarter_rows(qkv_weight)
    gains_here = jnp.concatenate([after(attn_gain, qkv_piece), ffn_gain, query_gain, key_gain])
    gains_there = links.over_x(gains_here)

    def gain_of(at, size):
        mine, other = gains_here[at : at + size], gains_there[at : at + size]
        return jnp.where(
            links.side == 0, jnp.concatenate([mine, other]), jnp.concatenate([other, mine])
        ).astype(f32)

    gain_attn = gain_of(0, rows)
    gain_ffn = gain_of(rows, rows)
    gain_query = gain_of(2 * rows, HD // 2)
    gain_key = gain_of(2 * rows + HD // 2, HD // 2)
    ff_chunk = gate_up_weight.shape[2] // CHUNKS

    def gate_up_piece(chunk):
        piece = lax.dynamic_slice(
            gate_up_weight,
            (links.quarter * part_rows, 0, chunk * ff_chunk),
            (part_rows, 2, ff_chunk),
        )
        return [piece[:, 0], piece[:, 1]]

    d_ffn = cotangent[0]
    d_beside = links.over_y(d_ffn)
    qkv_there = after(links.over_x(qkv_piece), d_beside)
    first_piece, first_up = gate_up_piece(0)
    up_piece = jnp.concatenate([first_up, quarter_rows(out_weight)], axis=1)
    second_piece = jnp.concatenate(gate_up_piece(1), axis=1)
    down_piece = lax.dynamic_slice_in_dim(
        down_weight, links.quarter * (width // 4), width // 4, 1
    )
    d_ffn = cotangent[0]
    tokens_here = tokens[0]
    qkv_there = after(qkv_there, first_piece)
    first_there = links.over_x(after(first_piece, qkv_there))
    up_there = links.over_x(after(up_piece, first_there))
    gate_up = jnp.transpose(after(gate_up_weight, qkv_there), (1, 0, 2))
    qkv_beside = links.over_y(qkv_there)
    qkv_pieces = (
        qkv_there,
        links.over_core(qkv_there),
        qkv_beside,
        links.over_core(after(qkv_beside, gate_up)),
    )
    sent, w_qkv, q_raw, k_raw, q_scale, k_scale, normed, scale_one = project(
        here, after(tokens_here, first_there), gain_attn[None], qkv_weight, qkv_pieces,
        gain_query[:, None], gain_key[:, None], cosine[0], sine[0],
    )
    got = lax.all_to_all(sent, "ctx", 0, 0, tiled=True)
    up_there = after(up_there, sent)
    down_there = links.over_x(after(down_piece, up_there))
    first_beside = links.over_y(first_there)
    up_beside = links.over_y(up_there)
    q_place, q_start = q_place[None], q_start[None]
    shape = jax.ShapeDtypeStruct
    attn_sent, *held = kernel_call(
        attend_kernel,
        tables,
        (got, q_place, q_start),
        [
            shape((ctx_size, HD, rows_here), bf16),
            shape((q_rows, HD), bf16),
            shape((HD, q_rows), bf16),
            shape((kv_rows, HD), bf16),
            shape((HD, kv_rows), bf16),
            shape((kv_rows, HD), bf16),
            shape((HD, q_rows), f32),
            shape((1, q_rows), f32),
        ],
        [pltpu.VMEM((HD, kv_rows), bf16)],
        ATTEND,
    )
    attn_sent = after(attn_sent, first_beside)
    attn_in = lax.dynamic_slice_in_dim(
        lax.all_to_all(attn_sent, "ctx", 0, 0, tiled=True), part * HEADS, HEADS
    ).reshape(q_width, rows_here)
    down_there = after(down_there, attn_sent)
    second_there = links.over_x(after(second_piece, down_there))
    down_beside = links.over_y(down_there)

    def spread(there, beside, time):
        there, beside = after(there, time), after(beside, time)
        return (there, links.over_core(there), beside, links.over_core(beside))

    first_pieces = spread(first_there, first_beside, attn_in)
    up_pieces = spread(up_there, up_beside, attn_sent)
    down_pieces = spread(down_there, down_beside, attn_in)
    second_beside = links.over_y(second_there)
    w_out, h_one, scale_two, two, two_t = attend_out(
        here, attn_in, tokens_here, gain_ffn[None], out_weight, up_pieces
    )
    two_beside = links.over_y(two_t)
    dealt_here, (out_sum, two_sum) = ffn(
        here, 0, two, d_ffn, gate_up, (first_pieces, up_pieces), down_weight, down_pieces, [h_one]
    )
    second_beside = after(second_beside, out_sum)
    second_pieces = (
        second_there, links.over_core(second_there), second_beside, links.over_core(second_beside)
    )
    near, far, give, give_far = dealt_here
    got_far = links.over_core(give_far)
    first_shares = (near, links.over_core(give), links.over_y(far), links.over_y(got_far))
    out_sum = after(out_sum, got_far)
    dealt_here, (output, d_h_one, d_attn, d_heads, ffn_gain_term) = ffn(
        here, 1, two, d_ffn, gate_up, (second_pieces, second_pieces), down_weight, down_pieces,
        [out_sum, two_sum, h_one, scale_two, w_out], gain_ffn[None],
    )
    second_shares = links.deal_plane(*dealt_here)

    def plane(value, beside, time):
        value, beside = after(value, time), after(beside, time)
        return (value, links.over_core(value), beside, links.over_core(beside))

    columns = ff_chunk // 2
    d_heads = d_heads.reshape(HEADS, HD, rows_here)
    d_got = lax.all_to_all(d_heads, "ctx", 0, 0, tiled=True)
    pair = jnp.stack([after(normed, d_heads), attn_in])
    two_plane = plane(two_t, two_beside, pair)
    first_products = wide_products(
        here, two_plane, [after(v, d_heads) for v in first_shares], columns
    )
    pair_across = links.over_core(pair)
    d_got = after(d_got, first_products[0], pair_across)
    (d_sent,) = kernel_call(
        attend_back_kernel,
        tables,
        (d_got, q_place, q_start, *held),
        [shape((ctx_size, 3 * HD, rows_here), bf16)],
        [
            pltpu.VMEM((HD, q_rows), bf16),
            pltpu.VMEM((q_rows, HD), bf16),
            pltpu.VMEM((kv_rows, HD), f32),
            pltpu.VMEM((kv_rows, HD), f32),
        ],
        ATTEND_BACK,
    )
    first_got = links.over_x(first_products[0])
    d_sent = after(d_sent, first_got, *second_shares[2:])
    d_back = lax.all_to_all(d_sent, "ctx", 0, 0, tiled=True)
    d_plane = plane(d_ffn, d_beside, d_sent)
    second_products = wide_products(
        here, two_plane, [after(v, d_plane[1]) for v in second_shares], columns
    )
    down_terms = down_products(
        here, d_plane, first_shares, second_shares, columns // 2
    )
    second_got = links.over_x(after(second_products[0], first_got))
    pair_beside = links.over_y(after(pair, d_sent))
    d_back = after(d_back, down_terms[0], pair_beside, second_got)
    *d_shares, d_inputs, gain_sums = attention_back(
        here,
        [
            d_back, q_raw, k_raw, q_scale, k_scale, gain_query[:, None], gain_key[:, None],
            cosine[0], sine[0], w_qkv, tokens_here, scale_one, gain_attn[None], d_h_one, d_attn,
        ],
    )
    down_got = links.over_x(after(down_terms[0], second_got))
    near, far, give, give_far = d_shares
    got, got_far = links.over_core(give), links.over_core(give_far)
    attention_shares = (near, got, links.over_y(far), links.over_y(got_far))
    pair_plane = (pair, pair_across, pair_beside, links.over_core(after(pair_beside, d_sent)))

    kept = [first_products[1], second_products[1], down_terms[1], None]
    got = [first_got, second_got, down_got, None]
    given, part, across, full, back, beside = ([None] * 4 for _ in range(6))

    def give_half(n):
        given[n] = links.over_z(links.half_of(kept[n], got[n], False))

    def sum_part(n, time):
        part[n] = add(links.half_of(kept[n], got[n], True), after(given[n], time))
        across[n] = links.over_two_z(part[n])

    def sum_full(n, time):
        full[n] = add(part[n], after(across[n], time))
        back[n] = links.over_z(full[n])

    def spread_y(n, time):
        full[n] = jnp.stack([full[n], after(back[n], time)])
        beside[n] = links.over_y(full[n])

    def spread_core(n, time):
        beside[n] = after(beside[n], time)
        return (full[n], links.over_core(full[n]), beside[n], links.over_core(beside[n]))

    give_half(0)
    given[0] = after(given[0], down_terms[0])
    sum_part(0, second_got)
    give_half(1)
    sum_part(1, got_far)
    got[2] = after(got[2], part[1], attention_shares[1], pair_plane[3])
    give_half(2)
    sum_full(0, got[2])
    attention_shares = (*attention_shares[:2], *(after(v, full[0]) for v in attention_shares[2:]))
    attention_terms = attention_products(
        here, pair_plane, attention_shares, gain_sums, ffn_gain_term
    )
    kept[3] = attention_terms[1]
    attention_got = links.over_x(attention_terms[0])
    spread_y(0, attention_terms[0])
    sum_part(2, full[0])
    sum_full(1, part[2])
    got[3] = after(attention_got, full[1])
    give_half(3)
    first_pieces = spread_core(0, got[3])
    spread_y(1, beside[0])
    sum_part(3, full[1])
    sum_full(2, part[3])
    first_placed = place_gate_up(here, 0, first_pieces, None)
    second_pieces = spread_core(1, full[2])
    spread_y(2, (first_placed, beside[1]))
    sum_full(3, full[2])
    grad_gate_up = place_gate_up(here, 1, second_pieces, first_placed)
    spread_y(3, full[2])
    grad_down = place_down(here, spread_core(2, grad_gate_up))
    cut = qkv_weight.shape[1] // 4
    grad_qkv, grad_out, gain_sums = place_attention(here, spread_core(3, grad_gate_up), cut)
    at = links.side * (HD // 2)
    gain_grads = [
        gain_sums[0, :rows],
        gain_sums[1, :rows],
        lax.dynamic_slice_in_dim(gain_sums[0, rows : rows + HD], at, HD // 2),
        lax.dynamic_slice_in_dim(gain_sums[1, rows : rows + HD], at, HD // 2),
    ]
    return (
        output[None],
        d_inputs[None],
        grad_qkv,
        grad_out,
        grad_gate_up,
        grad_down,
        *gain_grads,
    )


def on_device(
    tokens,
    qkv_weight,
    out_weight,
    gate_up_weight,
    down_weight,
    attn_gain,
    ffn_gain,
    query_gain,
    key_gain,
    seq_lengths,
    block_order,
    cotangent,
):
    inputs = tokens[0].astype(jnp.float32)
    rows_here = inputs.shape[0]
    ctx_size = lax.axis_size("ctx")
    ctx_index = lax.axis_index("ctx")
    per_group = HEADS // KV_HEADS
    q_width = HEADS * HD
    kv_width = KV_HEADS * HD
    order_row = block_order[0]
    lengths_row = seq_lengths[0]
    slots = jnp.arange(rows_here, dtype=jnp.int32) // BLK + ctx_index * (rows_here // BLK)
    table = slots[:, None] == jnp.arange(order_row.shape[0], dtype=jnp.int32)[None, :]
    packed = (
        jnp.sum(jnp.where(table, order_row[None, :], 0), axis=1) * BLK
        + jnp.arange(rows_here, dtype=jnp.int32) % BLK
    )
    local = packed - starts_of(packed, lengths_row)
    frequency = ROPE_BASE ** (-2.0 * jnp.arange(HD // 2, dtype=jnp.float32) / HD)
    angle = frequency[:, None] * local.astype(jnp.float32)[None, :]
    cosine = jnp.cos(angle)[None]
    sine = jnp.sin(angle)[None]
    bf16, f32 = jnp.bfloat16, jnp.float32
    parts = ctx_size // HEADS
    part = ctx_index // HEADS
    part_blocks = HEADS * rows_here // BLK
    q_order = lax.dynamic_slice_in_dim(order_row, part * part_blocks, part_blocks)
    q_slot, q_place, q_start = block_tables(q_order, lengths_row)
    q_slot = q_slot + part * part_blocks
    kv_slot, _, _ = block_tables(order_row, lengths_row)
    first = jnp.min(q_start.reshape(-1, TILE), axis=1) // TILE
    last = jnp.max(q_place.reshape(-1, TILE), axis=1) // TILE + 1
    tables = (q_slot, kv_slot, first, last)
    q_rows, kv_rows = part_blocks * BLK, order_row.shape[0] * BLK

    def fetch_attention():
        return (
            lax.all_gather(qkv_weight, "fsdp", axis=0, tiled=True),
            lax.all_gather(out_weight, "fsdp", axis=0, tiled=True),
            lax.all_gather(attn_gain, "fsdp", axis=0, tiled=True),
            lax.all_gather(ffn_gain, "fsdp", axis=0, tiled=True),
            lax.all_gather(query_gain, "fsdp", axis=0, tiled=True),
            lax.all_gather(key_gain, "fsdp", axis=0, tiled=True),
        )

    w_qkv, w_out, gain_attn, gain_ffn, gain_query, gain_key = fetch_attention()
    gain_attn = gain_attn.astype(jnp.float32)
    gain_ffn = gain_ffn.astype(jnp.float32)
    gain_query = gain_query.astype(jnp.float32)
    gain_key = gain_key.astype(jnp.float32)
    scale_one = rms_scale(inputs)
    normed = (inputs * scale_one * gain_attn).astype(jnp.bfloat16)
    projected = lax.dot_general(
        w_qkv, normed, (((0,), (1,)), ((), ())), preferred_element_type=f32
    )
    q_raw = projected[:q_width].reshape(HEADS, HD, rows_here)
    k_raw = projected[q_width : q_width + kv_width].reshape(KV_HEADS, HD, rows_here)
    values_here = projected[q_width + kv_width :].reshape(KV_HEADS, HD, rows_here).astype(bf16)
    q_scale = rms_scale(q_raw, 1)
    k_scale = rms_scale(k_raw, 1)
    column_query, column_key = gain_query[:, None], gain_key[:, None]
    queries = rope(q_raw * q_scale * column_query, cosine, sine).astype(bf16)
    keys_here = rope(k_raw * k_scale * column_key, cosine, sine).astype(bf16)
    sent = jnp.concatenate(
        [queries, jnp.repeat(keys_here, per_group, 0), jnp.repeat(values_here, per_group, 0)], axis=1
    )
    sent = jnp.concatenate([sent] * parts, axis=0)
    got = lax.all_to_all(sent, "ctx", 0, 0, tiled=True)
    q_place, q_start = q_place[None], q_start[None]
    shape = jax.ShapeDtypeStruct
    attn_sent, *held = kernel_call(
        attend_kernel,
        tables,
        (got, q_place, q_start),
        [
            shape((ctx_size, HD, rows_here), bf16),
            shape((q_rows, HD), bf16),
            shape((HD, q_rows), bf16),
            shape((kv_rows, HD), bf16),
            shape((HD, kv_rows), bf16),
            shape((kv_rows, HD), bf16),
            shape((HD, q_rows), f32),
            shape((1, q_rows), f32),
        ],
        [pltpu.VMEM((HD, kv_rows), bf16)],
        ATTEND,
    )
    attn_in = lax.dynamic_slice_in_dim(
        lax.all_to_all(attn_sent, "ctx", 0, 0, tiled=True), part * HEADS, HEADS
    ).reshape(q_width, rows_here)
    h_one = inputs + lax.dot_general(
        attn_in, w_out, (((0,), (0,)), ((), ())), preferred_element_type=f32
    )
    scale_two = rms_scale(h_one)
    normed_two = (h_one * scale_two * gain_ffn).astype(jnp.bfloat16)
    columns = normed_two
    gate_up = jnp.einsum(
        "tr,rgf->tgf",
        columns,
        lax.all_gather(gate_up_weight, "fsdp", axis=0, tiled=True),
        preferred_element_type=jnp.float32,
    )
    gate = gate_up[:, 0]
    upper = gate_up[:, 1]
    sigma = jax.nn.sigmoid(gate)
    hidden = (gate * sigma * upper).astype(jnp.bfloat16)
    columns = hidden
    ffn_out = jnp.dot(
        columns,
        lax.all_gather(down_weight, "fsdp", axis=0, tiled=True),
        preferred_element_type=jnp.float32,
    )
    output = (h_one + ffn_out).astype(jnp.bfloat16)
    d_out = cotangent[0].astype(jnp.float32)
    d_ffn = d_out.astype(jnp.bfloat16)
    d_hidden = lax.dot_general(
        d_ffn,
        lax.all_gather(down_weight, "fsdp", axis=0, tiled=True),
        (((1,), (1,)), ((), ())),
        preferred_element_type=jnp.float32,
    )
    d_gate = d_hidden * upper * sigma * (1.0 + gate * (1.0 - sigma))
    d_upper = d_hidden * gate * sigma
    d_gate_up = jnp.stack([d_gate, d_upper], axis=1).astype(jnp.bfloat16)
    d_normed_two = jnp.einsum(
        "tgf,rgf->tr",
        d_gate_up,
        lax.all_gather(gate_up_weight, "fsdp", axis=0, tiled=True),
        preferred_element_type=jnp.float32,
    )
    columns = normed_two
    grad_gate_up = lax.psum_scatter(
        jnp.einsum("tr,tgf->rgf", columns, d_gate_up, preferred_element_type=jnp.float32).astype(
            jnp.bfloat16
        ),
        "fsdp",
        scatter_dimension=0,
        tiled=True,
    )
    columns = hidden
    grad_down = lax.psum_scatter(
        lax.dot_general(
            columns, d_ffn, (((0,), (0,)), ((), ())), preferred_element_type=jnp.float32
        ).astype(jnp.bfloat16),
        "fsdp",
        scatter_dimension=0,
        tiled=True,
    )
    d_norm_two, ffn_gain_term = norm_back(d_normed_two, h_one, scale_two, gain_ffn)
    d_h_one = d_out + d_norm_two
    d_attn = d_h_one.astype(jnp.bfloat16)
    grad_out_here = jnp.dot(attn_in, d_attn, preferred_element_type=f32)
    d_heads = lax.dot_general(
        w_out, d_attn, (((1,), (1,)), ((), ())), preferred_element_type=f32
    ).astype(bf16)
    d_heads = jnp.concatenate([d_heads.reshape(HEADS, HD, rows_here)] * parts, axis=0)
    d_got = lax.all_to_all(d_heads, "ctx", 0, 0, tiled=True)
    (d_sent,) = kernel_call(
        attend_back_kernel,
        tables,
        (d_got, q_place, q_start, *held),
        [shape((ctx_size, 3 * HD, rows_here), bf16)],
        [
            pltpu.VMEM((HD, q_rows), bf16),
            pltpu.VMEM((q_rows, HD), bf16),
            pltpu.VMEM((kv_rows, HD), f32),
            pltpu.VMEM((kv_rows, HD), f32),
        ],
        ATTEND_BACK,
    )
    d_back = lax.all_to_all(d_sent, "ctx", 0, 0, tiled=True)
    d_query = lax.dynamic_slice_in_dim(d_back[:, :HD], part * HEADS, HEADS).astype(f32)
    d_key_value = jnp.sum(
        d_back[:, HD:].reshape(parts, KV_HEADS, per_group, 2 * HD, rows_here).astype(f32),
        axis=(0, 2),
    )
    dq_normed = rope_back(d_query, cosine, sine)
    dk_normed = rope_back(d_key_value[:, :HD], cosine, sine)
    dq_raw, query_term = norm_back(dq_normed, q_raw, q_scale, column_query, 1)
    dk_raw, key_term = norm_back(dk_normed, k_raw, k_scale, column_key, 1)
    d_projected = jnp.concatenate(
        [
            dq_raw.reshape(q_width, rows_here).astype(bf16),
            dk_raw.reshape(kv_width, rows_here).astype(bf16),
            d_key_value[:, HD:].reshape(kv_width, rows_here).astype(bf16),
        ],
        axis=0,
    )
    grad_qkv_here = lax.dot_general(
        normed, d_projected, (((0,), (1,)), ((), ())), preferred_element_type=f32
    )
    d_normed = lax.dot_general(
        d_projected, w_qkv, (((0,), (1,)), ((), ())), preferred_element_type=f32
    )
    d_norm_one, attn_gain_term = norm_back(d_normed, inputs, scale_one, gain_attn)
    d_inputs = d_h_one + d_norm_one
    shard_qkv, shard_out, shard_attn_gain, shard_ffn_gain, shard_query_gain, shard_key_gain = (
        lax.psum_scatter(
            grad_qkv_here.astype(jnp.bfloat16), "fsdp", scatter_dimension=0, tiled=True
        ).astype(jnp.float32),
        lax.psum_scatter(
            grad_out_here.astype(jnp.bfloat16), "fsdp", scatter_dimension=0, tiled=True
        ).astype(jnp.float32),
        lax.psum_scatter(
            jnp.sum(attn_gain_term, axis=0).astype(jnp.bfloat16),
            "fsdp",
            scatter_dimension=0,
            tiled=True,
        ).astype(jnp.float32),
        lax.psum_scatter(
            jnp.sum(ffn_gain_term, axis=0).astype(jnp.bfloat16),
            "fsdp",
            scatter_dimension=0,
            tiled=True,
        ).astype(jnp.float32),
        lax.psum_scatter(
            jnp.sum(query_term, axis=(0, 2)).astype(jnp.bfloat16),
            "fsdp",
            scatter_dimension=0,
            tiled=True,
        ).astype(jnp.float32),
        lax.psum_scatter(
            jnp.sum(key_term, axis=(0, 2)).astype(jnp.bfloat16),
            "fsdp",
            scatter_dimension=0,
            tiled=True,
        ).astype(jnp.float32),
    )
    summed_grads = (
        lax.psum(shard_qkv.astype(jnp.bfloat16), "ctx").astype(jnp.float32),
        lax.psum(shard_out.astype(jnp.bfloat16), "ctx").astype(jnp.float32),
        lax.psum(grad_gate_up, "ctx").astype(jnp.float32),
        lax.psum(grad_down, "ctx").astype(jnp.float32),
        lax.psum(shard_attn_gain.astype(jnp.bfloat16), "ctx").astype(jnp.float32),
        lax.psum(shard_ffn_gain.astype(jnp.bfloat16), "ctx").astype(jnp.float32),
        lax.psum(shard_query_gain.astype(jnp.bfloat16), "ctx").astype(jnp.float32),
        lax.psum(shard_key_gain.astype(jnp.bfloat16), "ctx").astype(jnp.float32),
    )
    return (
        output[None],
        d_inputs[None],
        summed_grads[0],
        summed_grads[1],
        summed_grads[2],
        summed_grads[3],
        summed_grads[4],
        summed_grads[5],
        summed_grads[6],
        summed_grads[7],
    )


def solution(mesh):
    block = mesh.shape["fsdp"] == 2 and mesh.shape["ctx"] == 16
    return jax.shard_map(
        on_block if block else on_device,
        mesh=mesh,
        in_specs=(
            P("fsdp", "ctx", None),
            P("fsdp", None),
            P("fsdp", None),
            P("fsdp", None, None),
            P("fsdp", None),
            P("fsdp"),
            P("fsdp"),
            P("fsdp"),
            P("fsdp"),
            P("fsdp", None),
            P("fsdp", None),
            P("fsdp", "ctx", None),
        ),
        out_specs=(
            P("fsdp", "ctx", None),
            P("fsdp", "ctx", None),
            P("fsdp", None),
            P("fsdp", None),
            P("fsdp", None, None),
            P("fsdp", None),
            P("fsdp"),
            P("fsdp"),
            P("fsdp"),
            P("fsdp"),
        ),
        check_vma=False,
    )
```
